32 devices in a mesh: ctx: 4 (over z), shard: 8 (over y, x, core).
Axes of the slice: x: 2, y: 2, z: 4, core: 2. Of those that a mesh axis runs over, the one named last changes fastest.
Arguments:
- tokens: bfloat16 [8, 512, 2048], P('shard', 'ctx'), may hold values from -6 to 6
- cotangent: bfloat16 [8, 512, 2048], P('shard', 'ctx'), may hold values from -6 to 6
- block_order: int32 [8], replicated, may hold values from 0 to 7, each once
- routes: int32 [8, 512, 8], P('shard', 'ctx'), may hold values from 0 to 31, all different within a row; in each aligned block of 128 rows (0 to 127, 128 to 255, ..., all dimensions but the last counted through in order) at most 40 rows name the same one
- attn_gain: float32 [2048], replicated, may hold values from 0.1 to 1.9
- w_query: bfloat16 [2048, 4096], P('shard'), may hold values from -0.125 to 0.125
- key_weight: bfloat16 [2048, 512], P('shard'), may hold values from -0.125 to 0.125
- value_weight: bfloat16 [2048, 512], P('shard'), may hold values from -0.125 to 0.125
- query_gain: float32 [128], replicated, may hold values from 0.1 to 1.9
- key_gain: float32 [128], replicated, may hold values from 0.1 to 1.9
- w_out: bfloat16 [4096, 2048], P('shard'), may hold values from -1.5 to 1.5
- ffn_gain: float32 [2048], replicated, may hold values from 0.1 to 1.9
- w_router: bfloat16 [2048, 32], P('shard'), may hold values from -0.0625 to 0.0625
- w_gate: bfloat16 [32, 2048, 768], P(('ctx', 'shard')), may hold values from -0.125 to 0.125
- w_up: bfloat16 [32, 2048, 768], P(('ctx', 'shard')), may hold values from -0.125 to 0.125
- w_down: bfloat16 [32, 768, 2048], P(('ctx', 'shard')), may hold values from -0.625 to 0.625
Outputs:
- mixed: bfloat16 [8, 512, 2048], P('shard', 'ctx')
- grad_tokens: float32 [8, 512, 2048], P('shard', 'ctx')
- grad_attn_gain: float32 [2048], replicated
- grad_w_query: float32 [2048, 4096], P('shard')
- grad_w_key: float32 [2048, 512], P('shard')
- grad_w_value: float32 [2048, 512], P('shard')
- grad_query_gain: float32 [128], replicated
- grad_key_gain: float32 [128], replicated
- grad_w_out: float32 [4096, 2048], P('shard')
- grad_ffn_gain: float32 [2048], replicated
- grad_w_router: float32 [2048, 32], P('shard')
- grad_w_gate: float32 [32, 2048, 768], P(('ctx', 'shard'))
- grad_w_up: float32 [32, 2048, 768], P(('ctx', 'shard'))
- grad_w_down: float32 [32, 768, 2048], P(('ctx', 'shard'))
The draws below stay inside these ranges and needn't reach their ends.
Inputs may be any that keep to these rules, and one draw needn't show every extreme that they name: Slot j of every sequence's storage holds causal block block_order[j]; each of the 8 blocks once. `routes`: each token names 8 different experts; among the 128 rows of one device (aligned blocks of a sequence's storage) no expert is named by more than 40 rows, a bound that some block reaches.
All inputs are finite; a program needn't handle non-finite values.
Results may differ from the reference program's by a relative error of at most 0.028.
Values may be sent and summed in bfloat16 or wider, within the bound.
A program may use at most 384 MiB of HBM per device.

```python
import math
import jax
import jax.numpy as jnp
import numpy as np
from jax import lax

MODEL_DIM = 2048
QUERY_HEADS = 32
KEY_VALUE_HEADS = 4
HEAD_DIM = 128
F = 768
TOP = 8
TOK_DEV = 128
LENGTH = 512
SEQS = 8
EXPERTS = 32
CAP = 40
N_CTX = 4
N_SHARD = 8


def block_levels(stream_key, extent, cuts, low, high):
    level, own = 1.0, jax.random.fold_in(stream_key, 6)
    for position, blocks in cuts:
        steps = jnp.exp(jax.random.uniform(jax.random.fold_in(own, position), (blocks,), jnp.float32, low / len(cuts), high / len(cuts)))
        level = level * jnp.repeat(steps, extent[position] // blocks).reshape([-1 if axis == position else 1 for axis in range(len(extent))])
    return level


def routed_block(own_key, own, number, rows, amount, top, bound, slope):
    sequence = jax.random.permutation(own_key, amount)
    crowded, common = shares(amount, rows * top, bound, slope, True), shares(amount, rows * top, bound, slope, False)
    places = jnp.arange(amount)

    def named(lengths, rotation):
        used = int((lengths > 0).sum())
        fixed = max(1, used // 4)
        passed = fixed + (places - fixed + rotation * (used - fixed)) % max(1, amount - fixed)
        return jnp.zeros((amount,), jnp.int32).at[sequence[jnp.where(places < fixed, places, passed)]].set(jnp.asarray(lengths, jnp.int32))

    lengths = jnp.where(number % 4 == 0, named(crowded, number // 4), named(common, number - number // 4 - 1))
    mixed = jax.random.permutation(jax.random.fold_in(own, 3), amount)
    donor, taker = mixed[0:amount // 2 * 2:2], mixed[1:amount // 2 * 2:2]
    margin = jnp.minimum(lengths[donor] - 1, bound - lengths[taker]) // 2
    margin = jnp.where((donor == sequence[0]) | (taker == sequence[0]) | (lengths[taker] == 0), 0, jnp.maximum(margin, 0))
    passed = jax.random.randint(jax.random.fold_in(own, 4), (amount // 2,), 0, 1 << 20) % (margin + 1)
    lengths = lengths.at[donor].add(-passed).at[taker].add(passed)
    items = jnp.searchsorted(jnp.cumsum(lengths), jnp.arange(rows * top), side="right").astype(jnp.int32)
    grid = items.reshape(top, rows).T
    grid = grid[jax.random.permutation(jax.random.fold_in(own, 1), rows)]
    rotation = jax.random.randint(jax.random.fold_in(own, 2), (rows, 1), 0, top)
    return jnp.take_along_axis(grid, (jnp.arange(top)[None, :] + rotation) % top, axis=1)


def shares(amount, total, limit, skew, full):
    portions = [(1 << 20) // math.isqrt(standing ** skew) + 1 for standing in range(1, amount + 1)]
    largest = limit if full else min(limit, max(-(-total // amount), total * portions[0] // sum(portions)))
    least = 1 if total - largest >= amount - 1 else 0
    holding, spare = [largest] + [least] * (amount - 1), total - largest - least * (amount - 1)
    while spare > 0:
        movable = [i for i in range(1, amount) if holding[i] < largest] or [i for i in range(1, amount) if holding[i] < limit]
        mass, budget = sum([portions[i] for i in movable]), spare
        for i in movable:
            more = min(limit - holding[i], max(1, budget * portions[i] // mass), spare)
            holding[i] = holding[i] + more
            spare = spare - more
    return np.array(holding)


def scatter_about(key, shape, width, reach, pieces=(), held_as=jnp.bfloat16):
    array = jax.random.normal(key, shape, jnp.float32) * width
    if len(pieces) > 0:
        array = block_levels(key, shape, pieces, -0.22, 0.18) * array
    return jnp.clip(array, min=-reach, max=reach).astype(held_as)


def setup_inputs(seed: int = 0) -> dict:
    key_of = jax.random.split(jax.random.key(seed), 17)
    tokens = scatter_about(key_of[0], (SEQS, LENGTH, MODEL_DIM), 1.0, 6.0, ((0, 8), (1, 4)))
    cotangent = scatter_about(key_of[1], (SEQS, LENGTH, MODEL_DIM), 1.0, 6.0, ((0, 8), (1, 4)))
    block_order = jax.random.permutation(key_of[2], 2 * N_CTX).astype(jnp.int32)
    routes_keys = jax.random.split(jax.random.fold_in(key_of[3], 1), SEQS * LENGTH // TOK_DEV)
    routes_turns = jax.random.permutation(jax.random.fold_in(key_of[3], 3), SEQS * LENGTH // TOK_DEV)
    routes = jax.vmap(lambda own, number: routed_block(jax.random.fold_in(key_of[3], 2), own, number, TOK_DEV, EXPERTS, TOP, CAP, 1))(routes_keys, routes_turns).reshape((SEQS, LENGTH, TOP))
    attn_gain = jnp.clip(1.0 + 0.18 * jax.random.normal(key_of[4], (MODEL_DIM,), jnp.float32), 0.1, 1.9)
    w_query = scatter_about(key_of[5], (MODEL_DIM, QUERY_HEADS * HEAD_DIM), MODEL_DIM ** -0.5, 0.125, ((0, 8),))
    key_weight = scatter_about(key_of[6], (MODEL_DIM, KEY_VALUE_HEADS * HEAD_DIM), MODEL_DIM ** -0.5, 0.125, ((0, 8),))
    value_weight = scatter_about(key_of[7], (MODEL_DIM, KEY_VALUE_HEADS * HEAD_DIM), MODEL_DIM ** -0.5, 0.125, ((0, 8),))
    query_gain = jnp.clip(1.0 + 0.18 * jax.random.normal(key_of[8], (HEAD_DIM,), jnp.float32), 0.1, 1.9)
    key_gain = jnp.clip(1.0 + 0.18 * jax.random.normal(key_of[9], (HEAD_DIM,), jnp.float32), 0.1, 1.9)
    w_out = scatter_about(key_of[10], (QUERY_HEADS * HEAD_DIM, MODEL_DIM), (max(QUERY_HEADS * HEAD_DIM // 256, 1)) ** -0.5, 1.5, ((0, 8),))
    ffn_gain = jnp.clip(1.0 + 0.18 * jax.random.normal(key_of[11], (MODEL_DIM,), jnp.float32), 0.1, 1.9)
    w_router = scatter_about(key_of[12], (MODEL_DIM, EXPERTS), (4 * MODEL_DIM) ** -0.5, 0.0625, ((0, 8),))
    w_gate = scatter_about(key_of[13], (EXPERTS, MODEL_DIM, F), MODEL_DIM ** -0.5, 0.125, ((0, 32),))
    w_up = scatter_about(key_of[14], (EXPERTS, MODEL_DIM, F), MODEL_DIM ** -0.5, 0.125, ((0, 32),))
    w_down = scatter_about(key_of[15], (EXPERTS, F, MODEL_DIM), (F // 8) ** -0.5, 0.625, ((0, 32),))
    return {"tokens": tokens, "cotangent": cotangent, "block_order": block_order, "routes": routes, "attn_gain": attn_gain, "w_query": w_query, "key_weight": key_weight, "value_weight": value_weight, "query_gain": query_gain, "key_gain": key_gain, "w_out": w_out, "ffn_gain": ffn_gain, "w_router": w_router, "w_gate": w_gate, "w_up": w_up, "w_down": w_down}


@jax.custom_vjp
def low(v):
    return lax.optimization_barrier(v.astype(jnp.bfloat16)).astype(jnp.float32)

@jax.custom_vjp
def low_back(v):
    return v

def low_keep(v):
    return (low(v), None)

def low_pass(kept, grad):
    return (grad,)

def back_keep(v):
    return (v, None)

def back_low(kept, grad):
    return (low(grad),)
low.defvjp(low_keep, low_pass)
low_back.defvjp(back_keep, back_low)
epsilon = 1e-06
rope_base = 1000000.0

def rms_scale(hidden, gain):
    return hidden * lax.rsqrt(lax.optimization_barrier(jnp.mean(hidden * hidden, axis=-1, keepdims=True)) + epsilon) * gain

def rotate(headwise, places):
    half_size = headwise.shape[-1] // 2
    frequency = rope_base ** (-jnp.arange(half_size, dtype=jnp.float32) * 2.0 / headwise.shape[-1])
    angles = places.astype(jnp.float32)[:, None] * frequency[None, :]
    cosine = jnp.cos(angles)[:, None, :]
    sine = jnp.sin(angles)[:, None, :]
    former = headwise[..., :half_size]
    latter = headwise[..., half_size:]
    return jnp.concatenate([former * cosine - latter * sine, latter * cosine + former * sine], axis=-1)

def head_prep(pre_rows, gain, places):
    headwise = pre_rows.reshape(pre_rows.shape[0], -1, HEAD_DIM)
    return rotate(rms_scale(headwise, gain), places).reshape(pre_rows.shape)

def place_of(row_ids, order, block_rows):
    block_ids = jnp.arange(order.shape[0], dtype=jnp.int32)
    owner_block = row_ids // block_rows
    picked_block = lax.optimization_barrier(jnp.sum(jnp.where(owner_block[:, None] == block_ids[None, :], order[None, :], 0), axis=1))
    return picked_block * block_rows + row_ids % block_rows

def matmul_high(left, right):
    return jnp.dot(left, right, precision=lax.Precision.HIGHEST, preferred_element_type=jnp.float32)

def reference(tokens, cotangent, block_order, routes, attn_gain, w_query, key_weight, value_weight, query_gain, key_gain, w_out, ffn_gain, w_router, w_gate, w_up, w_down):
    seq_count, sequence_length, model_width = tokens.shape
    block_rows = sequence_length // (2 * N_CTX)
    rows_per_shard = 2 * block_rows
    query_groups = QUERY_HEADS // KEY_VALUE_HEADS
    score_scale = HEAD_DIM ** (-0.5)
    block_count = seq_count * N_CTX
    places = place_of(jnp.arange(sequence_length, dtype=jnp.int32), block_order, block_rows)
    all_places = jnp.tile(places, seq_count)
    visible = places[None, :] <= places[:, None]
    assign_per = rows_per_shard * TOP
    route_blocks = routes.reshape(block_count, assign_per)
    one_hot = (route_blocks[:, :, None] == jnp.arange(EXPERTS, dtype=jnp.int32)[None, None, :]).astype(jnp.int32)
    slot_index = lax.optimization_barrier(jnp.sum(jnp.cumsum(one_hot, axis=1) * one_hot, axis=2)) - 1
    block_ids = jnp.arange(block_count, dtype=jnp.int32)
    source_ids = block_ids % N_CTX * N_SHARD + block_ids // N_CTX
    region = block_count * CAP
    target_rows = (route_blocks * region + source_ids[:, None] * CAP + slot_index).reshape(-1)
    assign_ids = jnp.arange(block_count * assign_per, dtype=jnp.int32)
    token_ids = assign_ids // TOP
    buffer_token = jnp.zeros((EXPERTS * region,), jnp.int32).at[target_rows].set(token_ids)
    buffer_assign = jnp.zeros((EXPERTS * region,), jnp.int32).at[target_rows].set(assign_ids)
    buffer_valid = jnp.zeros((EXPERTS * region,), jnp.float32).at[target_rows].set(1.0)
    route_rows = routes.reshape(-1, TOP)

    def attend_seq(triple):
        query_sequence, key_sequence, value_sequence = triple
        headed_queries = query_sequence.reshape(sequence_length, KEY_VALUE_HEADS, query_groups, HEAD_DIM)
        headed_keys = key_sequence.reshape(sequence_length, KEY_VALUE_HEADS, HEAD_DIM)
        headed_values = value_sequence.reshape(sequence_length, KEY_VALUE_HEADS, HEAD_DIM)
        raw_scores = jnp.einsum('tkgd,pkd->kgtp', headed_queries, headed_keys, precision=lax.Precision.HIGHEST)
        scores = low_back(score_scale * raw_scores)
        scores = jnp.where(visible[None, None], scores, -1e+30)
        weights_p = low(jax.nn.softmax(scores, axis=-1))
        attended = jnp.einsum('kgtp,pkd->tkgd', weights_p, headed_values, precision=lax.Precision.HIGHEST)
        return attended.reshape(sequence_length, QUERY_HEADS * HEAD_DIM)

    def run_expert(quad):
        rows_in, gate_mat, up_mat, down_mat = quad
        gate_pre = low_back(matmul_high(rows_in, gate_mat))
        up_pre = low_back(matmul_high(rows_in, up_mat))
        hidden = low(jax.nn.silu(gate_pre) * up_pre)
        return low(low_back(matmul_high(hidden, down_mat)))

    def forward(inputs, attn_g, query_w, key_w, value_w, query_g, key_g, out_w, ffn_g, router_w, gate_w, up_w, down_w):
        normed = low(rms_scale(inputs, attn_g))
        query_pre = low_back(matmul_high(normed, query_w))
        key_pre = low_back(matmul_high(normed, key_w))
        value_all = low(low_back(matmul_high(normed, value_w)))
        query_rot = low(head_prep(query_pre, query_g, all_places))
        key_rot = low(head_prep(key_pre, key_g, all_places))
        attended = lax.map(jax.checkpoint(attend_seq), (query_rot.reshape(seq_count, sequence_length, -1), key_rot.reshape(seq_count, sequence_length, -1), value_all.reshape(seq_count, sequence_length, -1)))
        attn_rows = low(low_back(attended.reshape(-1, QUERY_HEADS * HEAD_DIM)))
        middle = inputs + low_back(matmul_high(attn_rows, out_w))
        normed_two = low(rms_scale(middle, ffn_g))
        logits = low_back(matmul_high(normed_two, router_w))
        picked_logits = jnp.take_along_axis(logits, route_rows, axis=1)
        gate_weights = jax.nn.softmax(picked_logits, axis=-1)
        rows_in = normed_two[buffer_token] * buffer_valid[:, None]
        expert_out = lax.map(jax.checkpoint(run_expert), (rows_in.reshape(EXPERTS, region, model_width), gate_w, up_w, down_w))
        expert_out = expert_out.reshape(-1, model_width)
        row_weights = gate_weights.reshape(-1)[buffer_assign] * buffer_valid
        mixture = jnp.zeros_like(inputs).at[buffer_token].add(row_weights[:, None] * expert_out)
        return middle + mixture
    floats = [argument.astype(jnp.float32) for argument in (tokens.reshape(-1, model_width), attn_gain, w_query, key_weight, value_weight, query_gain, key_gain, w_out, ffn_gain, w_router, w_gate, w_up, w_down)]
    result, backward = jax.vjp(forward, *floats)
    grads = backward(cotangent.reshape(-1, model_width).astype(jnp.float32))
    return (result.reshape(tokens.shape).astype(jnp.bfloat16), grads[0].reshape(tokens.shape), grads[1], grads[2], grads[3], grads[4], grads[5], grads[6], grads[7], grads[8], grads[9], grads[10], grads[11], grads[12])
```

```python
import jax
import jax.numpy as jnp
from jax import lax
from jax.sharding import PartitionSpec as P

QUERY_HEADS = 32
KEY_VALUE_HEADS = 4
HEAD_DIM = 128

epsilon = 1e-06
rope_base = 1000000.0
BF = jnp.bfloat16
F32 = jnp.float32


def rms_scale(hidden, gain):
    return hidden * lax.rsqrt(jnp.mean(hidden * hidden, axis=-1, keepdims=True) + epsilon) * gain


def rotate(headwise, places):
    half_size = headwise.shape[-1] // 2
    frequency = rope_base ** (-jnp.arange(half_size, dtype=F32) * 2.0 / headwise.shape[-1])
    angles = places.astype(F32)[:, None] * frequency[None, :]
    cosine = jnp.cos(angles)[:, None, :]
    sine = jnp.sin(angles)[:, None, :]
    former = headwise[..., :half_size]
    latter = headwise[..., half_size:]
    return jnp.concatenate(
        [former * cosine - latter * sine, latter * cosine + former * sine], axis=-1
    )


def place_of(row_ids, order, block_rows):
    block_ids = jnp.arange(order.shape[0], dtype=jnp.int32)
    owner_block = row_ids // block_rows
    picked_block = jnp.sum(
        jnp.where(owner_block[:, None] == block_ids[None, :], order[None, :], 0), axis=1
    )
    return picked_block * block_rows + row_ids % block_rows


def dot(left, right):
    return jnp.dot(left, right, preferred_element_type=F32)


def contract_rows(left, right):
    return lax.dot_general(left, right, (((0,), (0,)), ((), ())), preferred_element_type=F32)


def contract_cols(left, right):
    return lax.dot_general(left, right, (((1,), (1,)), ((), ())), preferred_element_type=F32)


def gather_shard(x):
    return lax.all_gather(x, "shard", axis=0, tiled=True)


def scatter_shard(x):
    return lax.psum_scatter(x, "shard", scatter_dimension=0, tiled=True)


def exchange_shard(x):
    return lax.all_to_all(x, "shard", split_axis=0, concat_axis=0, tiled=True)


def gather_ctx(x):
    return lax.all_gather(x, "ctx", axis=0, tiled=False)


def scatter_ctx(x):
    return lax.psum_scatter(x, "ctx", scatter_dimension=0, tiled=False)


def shards(
    tokens,
    cotangent,
    block_order,
    routes,
    attn_gain,
    w_query,
    key_weight,
    value_weight,
    query_gain,
    key_gain,
    w_out,
    ffn_gain,
    w_router,
    w_gate,
    w_up,
    w_down,
):
    rows = tokens.shape[1]
    width = tokens.shape[2]
    ctx_count = lax.axis_size("ctx")
    shard_count = lax.axis_size("shard")
    my_ctx = lax.axis_index("ctx")
    my_shard = lax.axis_index("shard")
    experts = ctx_count * shard_count
    block_rows = rows // 2
    heads = QUERY_HEADS // shard_count
    head_cols = heads * HEAD_DIM
    sharers = shard_count // KEY_VALUE_HEADS
    score_scale = HEAD_DIM ** (-0.5)
    top_count = routes.shape[2]
    capacity = rows * top_count // experts + max(rows * top_count // (4 * experts), 1)
    sequence = rows * ctx_count
    plane = rows * shard_count
    wrows = width // shard_count

    inputs = tokens[0].astype(F32)
    upstream_b = cotangent[0]
    upstream = upstream_b.astype(F32)

    kv_kind = [key_weight, value_weight]
    extra = [
        kv_kind[(s % sharers) % 2][:, (s // sharers) * HEAD_DIM : (s // sharers + 1) * HEAD_DIM]
        for s in range(shard_count)
    ]
    send_w = jnp.stack(
        [
            jnp.concatenate([w_query[:, s * head_cols : (s + 1) * head_cols], extra[s]], axis=1)
            for s in range(shard_count)
        ]
    )
    w_mine = exchange_shard(send_w).reshape(width, head_cols + HEAD_DIM)

    normed = rms_scale(inputs, attn_gain)
    normed_b = normed.astype(BF)
    normed_all = gather_shard(normed_b)

    routes_all = lax.all_gather(routes[0], ("ctx", "shard"), axis=0, tiled=False).reshape(
        ctx_count, shard_count, rows, top_count
    )
    named = jnp.sum(
        (routes_all[..., None] == jnp.arange(experts, dtype=jnp.int32)).astype(BF), axis=3
    )
    earlier = (
        jnp.arange(rows, dtype=jnp.int32)[:, None] > jnp.arange(rows, dtype=jnp.int32)[None, :]
    ).astype(BF)
    slots = jnp.arange(capacity, dtype=F32)

    def places_in(mask):
        rank = jnp.einsum("tu,...un->...tn", earlier, mask, preferred_element_type=F32)
        pick = jnp.where(mask > 0, rank, -1.0)
        return (jnp.swapaxes(pick, -1, -2)[..., None, :] == slots[:, None]).astype(BF)

    my_rows = lax.dynamic_index_in_dim(named, my_shard, 1, keepdims=False)
    my_rows = lax.dynamic_slice_in_dim(my_rows, my_ctx * shard_count, shard_count, 2)
    pick_send = places_in(my_rows)
    mine = lax.dynamic_slice_in_dim(named, my_ctx * shard_count + my_shard, 1, 3)
    pick_here = places_in(mine)[:, :, 0]
    chosen_here = jnp.einsum(
        "cbqt,cbte->bcqe", pick_here, named, preferred_element_type=F32
    ).reshape(-1, experts)

    def dispatch(rows_b):
        every = gather_ctx(rows_b)
        sent = jnp.einsum("bsqt,btd->sbqd", pick_send, every, preferred_element_type=F32)
        return exchange_shard(sent.astype(BF).reshape(shard_count, ctx_count * capacity, -1)).reshape(
            shard_count * ctx_count * capacity, -1
        )

    def combine(slot_rows):
        back = exchange_shard(slot_rows.reshape(shard_count, ctx_count * capacity, -1))
        back = back.reshape(shard_count, ctx_count, capacity, -1)
        part = jnp.einsum("bsqt,sbqd->btd", pick_send, back, preferred_element_type=F32)
        return scatter_ctx(part.astype(BF)).astype(F32)

    grad_expert_rows = dispatch(upstream_b)

    qkv = dot(normed_all, w_mine)
    query_pre = qkv[:, :head_cols].reshape(shard_count, rows, heads, HEAD_DIM)
    row_ids = my_ctx * rows + jnp.arange(rows, dtype=jnp.int32)
    q_places = place_of(row_ids, block_order, block_rows)
    k_places = place_of(jnp.arange(sequence, dtype=jnp.int32), block_order, block_rows)
    sees = k_places[None, :] <= q_places[:, None]

    def prep(pre, gain):
        shape = pre.shape
        flat = pre.reshape(-1, rows, shape[-2], HEAD_DIM)
        return jax.vmap(lambda v: rotate(rms_scale(v, gain), q_places))(flat).reshape(shape)

    queries = prep(query_pre, query_gain).astype(BF)
    my_place = lax.rem(my_shard, sharers)
    is_key = lax.rem(my_place, 2) == 0
    part_count = sharers // 2
    kv_pre = qkv[:, head_cols:]
    key_roped = prep(kv_pre.reshape(shard_count, rows, 1, HEAD_DIM), key_gain).reshape(plane, HEAD_DIM)
    kv_b = jnp.where(is_key, key_roped, kv_pre).astype(BF)
    groups = [
        [g * sharers + i for i in range(sharers)] for g in range(KEY_VALUE_HEADS)
    ]
    kv_pair = lax.all_gather(kv_b, "shard", axis=0, tiled=False, axis_index_groups=groups)[:2]
    kv_all = gather_ctx(kv_pair)
    kv_all = kv_all.reshape(ctx_count, 2, shard_count, rows, HEAD_DIM)
    kv_all = jnp.transpose(kv_all, (1, 2, 0, 3, 4)).reshape(2, shard_count, sequence, HEAD_DIM)
    keys, values = kv_all[0], kv_all[1]

    scores = (
        jnp.einsum("sthd,spd->shtp", queries, keys, preferred_element_type=F32) * score_scale
    )
    scores = jnp.where(sees, scores, -1e30)
    top = jnp.max(scores, axis=-1, keepdims=True)
    raised = jnp.exp(scores - top)
    total = jnp.sum(raised, axis=-1, keepdims=True)
    probs = raised / total
    probs_b = probs.astype(BF)
    attn_f32 = jnp.einsum("shtp,spd->sthd", probs_b, values, preferred_element_type=F32)
    attn_b = attn_f32.astype(BF)
    attn_rows = attn_b.reshape(plane, head_cols)
    proj = scatter_shard(dot(attn_rows, w_out).astype(BF))
    middle = inputs + proj.astype(F32)

    normed_two = rms_scale(middle, ffn_gain)
    second_b = normed_two.astype(BF)
    router_all = gather_shard(w_router)
    logits = dot(second_b, router_all)
    chosen = jnp.sum(
        (routes[0][:, :, None] == jnp.arange(experts, dtype=jnp.int32)).astype(F32), axis=1
    )

    def gates_of(log, mask):
        masked = jnp.where(mask > 0, log, -1e30)
        peak = jnp.max(masked, axis=-1, keepdims=True)
        risen = jnp.exp(masked - peak) * mask
        return risen / jnp.maximum(jnp.sum(risen, axis=-1, keepdims=True), 1e-30)

    gates = gates_of(logits, chosen)

    received = dispatch(second_b)
    my_expert = my_ctx * shard_count + my_shard
    slot_gates = lax.dynamic_slice_in_dim(
        gates_of(dot(received, router_all), chosen_here), my_expert, 1, 1
    )
    gate_pre = dot(received, w_gate[0])
    up_pre = dot(received, w_up[0])
    activated = jax.nn.silu(gate_pre)
    hidden_b = (activated * up_pre).astype(BF)
    expert_out = dot(hidden_b, w_down[0]).astype(BF)
    expert_out_f = expert_out.astype(F32)
    mixed = (middle + combine((slot_gates * expert_out_f).astype(BF))).astype(BF)
    upstream_rows = grad_expert_rows.astype(F32)
    slot_dot = jnp.sum(expert_out_f * upstream_rows, axis=1, keepdims=True)
    grad_expert = (slot_gates * upstream_rows).astype(BF)
    grad_w_down = contract_rows(hidden_b, grad_expert)
    grad_hidden = contract_cols(grad_expert, w_down[0])
    sigmoid_g = jax.nn.sigmoid(gate_pre)
    silu_slope = sigmoid_g * (1.0 + gate_pre * (1.0 - sigmoid_g))
    grad_gate_pre = (grad_hidden * up_pre * silu_slope).astype(BF)
    grad_up_pre = (grad_hidden * activated).astype(BF)
    grad_w_gate = contract_rows(received, grad_gate_pre)
    grad_w_up = contract_rows(received, grad_up_pre)
    grad_received = contract_cols(grad_gate_pre, w_gate[0]) + contract_cols(grad_up_pre, w_up[0])

    tail_cols = -(-2 * experts // 128) * 128
    coarse = slot_dot.astype(BF).astype(F32)
    fine = slot_dot - coarse
    column = jnp.arange(tail_cols, dtype=jnp.int32)[None, :]
    tail = jnp.where(column == my_expert, coarse, 0.0) + jnp.where(
        column == experts + my_expert, fine, 0.0
    )
    back = combine(jnp.concatenate([grad_received, tail], axis=1).astype(BF))
    grad_second = back[:, :width]
    grad_gates = back[:, width : width + experts] + back[:, width + experts : width + 2 * experts]
    grad_logits_b = (
        gates * (grad_gates - jnp.sum(gates * grad_gates, axis=-1, keepdims=True))
    ).astype(BF)
    grad_w_router_part = contract_rows(second_b, grad_logits_b)
    grad_second = grad_second + contract_cols(grad_logits_b, router_all)
    unused, norm_two_back = jax.vjp(rms_scale, middle, ffn_gain)
    grad_middle_part, grad_ffn_gain = norm_two_back(grad_second)
    grad_middle = upstream + grad_middle_part
    grad_proj_b = grad_middle.astype(BF)

    grad_proj_all = gather_shard(grad_proj_b)
    grad_attn = contract_cols(grad_proj_all, w_out).astype(BF)
    grad_w_out = lax.psum(contract_rows(attn_rows, grad_proj_all).astype(BF), "ctx").astype(F32)
    grad_heads = grad_attn.reshape(shard_count, rows, heads, HEAD_DIM)
    delta = jnp.transpose(jnp.sum(grad_heads.astype(F32) * attn_f32, axis=-1), (0, 2, 1))[..., None]
    grad_probs = jnp.einsum("sthd,spd->shtp", grad_heads, values, preferred_element_type=F32)
    grad_scores = (probs * (grad_probs - delta)).astype(BF)
    grad_query = score_scale * jnp.einsum(
        "shtp,spd->sthd", grad_scores, keys, preferred_element_type=F32
    )
    grad_keys = score_scale * jnp.einsum(
        "shtp,sthd->spd", grad_scores, queries, preferred_element_type=F32
    )
    grad_values = jnp.einsum("shtp,sthd->spd", probs_b, grad_heads, preferred_element_type=F32)
    grad_kv = jnp.stack([grad_keys, grad_values]).astype(BF)
    grad_kv = grad_kv.reshape(2, shard_count, ctx_count, rows, HEAD_DIM)
    grad_kv = scatter_ctx(jnp.transpose(grad_kv, (2, 0, 1, 3, 4)))
    grad_kv = grad_kv.reshape(2, part_count, plane // part_count, HEAD_DIM)
    grad_kv = jnp.transpose(grad_kv, (1, 0, 2, 3)).reshape(sharers, plane // part_count, HEAD_DIM)
    grad_kv = lax.psum_scatter(
        grad_kv, "shard", scatter_dimension=0, tiled=False, axis_index_groups=groups
    ).astype(F32)
    first = (my_place // 2) * (plane // part_count)

    unused, query_back = jax.vjp(prep, query_pre, query_gain)
    grad_query_pre, grad_query_gain = query_back(grad_query)
    parts_k = (shard_count // part_count, rows, 1, HEAD_DIM)
    kv_mine = lax.dynamic_slice_in_dim(kv_pre, first, plane // part_count, 0)
    unused, key_back = jax.vjp(prep, kv_mine.reshape(parts_k), key_gain)
    grad_key_pre, grad_key_gain = key_back(grad_kv.reshape(parts_k))
    grad_key_gain = jnp.where(is_key, grad_key_gain, 0.0)
    grad_kv_b = jnp.where(is_key, grad_key_pre.reshape(-1, HEAD_DIM), grad_kv).astype(BF)
    if part_count > 1:
        grad_kv_full = lax.dynamic_update_slice_in_dim(
            jnp.zeros((plane, HEAD_DIM), BF), grad_kv_b, first, 0
        )
    else:
        grad_kv_full = grad_kv_b
    grad_pre = jnp.concatenate(
        [grad_query_pre.reshape(plane, head_cols).astype(BF), grad_kv_full], axis=1
    )
    grad_normed = scatter_shard(contract_cols(grad_pre, w_mine).astype(BF)).astype(F32)
    unused, norm_one_back = jax.vjp(rms_scale, inputs, attn_gain)
    grad_input_part, grad_attn_gain = norm_one_back(grad_normed)
    grad_tokens = grad_middle + grad_input_part
    grad_attn_gain, grad_query_gain, grad_key_gain, grad_ffn_gain = lax.psum(
        (grad_attn_gain, grad_query_gain, grad_key_gain, grad_ffn_gain), ("ctx", "shard")
    )

    grad_w = contract_rows(normed_all, grad_pre).astype(BF)
    router_cols = -(-experts // 128) * 128
    router_part = jnp.pad(grad_w_router_part, ((0, 0), (0, router_cols - experts))).astype(BF)
    packed = jnp.concatenate([grad_w, router_part], axis=1).reshape(shard_count, wrows, -1)
    packed = exchange_shard(packed)
    queries_part = jnp.transpose(packed[:, :, :head_cols], (1, 0, 2)).reshape(wrows, -1)
    kinds = packed[:, :, head_cols : head_cols + HEAD_DIM].astype(F32)
    kinds = jnp.sum(kinds.reshape(KEY_VALUE_HEADS, part_count, 2, wrows, HEAD_DIM), axis=1)
    kinds = jnp.transpose(kinds, (2, 1, 0, 3)).reshape(wrows, -1).astype(BF)
    router_sum = jnp.sum(packed[:, :, head_cols + HEAD_DIM :].astype(F32), axis=0).astype(BF)
    summed = lax.psum(jnp.concatenate([queries_part, kinds, router_sum], axis=1), "ctx").astype(F32)
    width_q = QUERY_HEADS * HEAD_DIM
    key_width = KEY_VALUE_HEADS * HEAD_DIM
    grad_w_query = summed[:, :width_q]
    grad_w_key = summed[:, width_q : width_q + key_width]
    grad_w_value = summed[:, width_q + key_width : width_q + 2 * key_width]
    grad_w_router = summed[:, width_q + 2 * key_width : width_q + 2 * key_width + experts]
    return (
        mixed[None],
        grad_tokens[None],
        grad_attn_gain,
        grad_w_query,
        grad_w_key,
        grad_w_value,
        grad_query_gain,
        grad_key_gain,
        grad_w_out,
        grad_ffn_gain,
        grad_w_router,
        grad_w_gate[None],
        grad_w_up[None],
        grad_w_down[None],
    )


def solution(mesh):
    rows = P("shard", "ctx", None)
    matrix = P("shard", None)
    expert = P(("ctx", "shard"), None, None)
    return jax.shard_map(
        shards,
        mesh=mesh,
        in_specs=(
            rows, rows, P(), rows, P(), matrix, matrix, matrix, P(), P(), matrix, P(), matrix,
            expert, expert, expert,
        ),
        out_specs=(
            rows, rows, P(), matrix, matrix, matrix, P(), P(), matrix, P(), matrix,
            expert, expert, expert,
        ),
        check_vma=False,
    )
```

```python
import functools

import jax
import jax.numpy as jnp
from jax import lax
from jax.experimental import pallas as pl
from jax.experimental.pallas import tpu as pltpu
from jax.sharding import PartitionSpec as P

BF = jnp.bfloat16
F32 = jnp.float32
MESH = pl.DeviceIdType.MESH
ANY = pl.BlockSpec(memory_space=pl.ANY)
VMEM = pl.BlockSpec(memory_space=pltpu.VMEM)
DMA = pltpu.SemaphoreType.DMA


def push(src, dst, send_sem, recv_sem, **where):
    return pltpu.make_async_remote_copy(
        src_ref=src, dst_ref=dst, send_sem=send_sem, recv_sem=recv_sem,
        device_id=where, device_id_type=MESH,
    )


def greet(shard_peers, ctx_peers):
    barrier = pltpu.get_barrier_semaphore()
    for peer in shard_peers:
        pl.semaphore_signal(barrier, inc=1, device_id={"shard": peer}, device_id_type=MESH)
    for peer in ctx_peers:
        pl.semaphore_signal(barrier, inc=1, device_id={"ctx": peer}, device_id_type=MESH)
    pl.semaphore_wait(barrier, len(shard_peers) + len(ctx_peers))


def here(ctx_count, shard_count):
    c, s = lax.axis_index("ctx"), lax.axis_index("shard")
    parity = lax.rem(s, 2)
    sibling = s + 1 - 2 * parity
    others = [lax.rem(s + d, shard_count) for d in range(1, shard_count)]
    layers = [lax.rem(c + d, ctx_count) for d in range(1, ctx_count)]
    return c, s, parity, sibling, others, layers


def call(body, outs, in_specs, scratch, ident, args, mib=48, out_specs=None):
    return pl.pallas_call(
        body,
        out_shape=outs,
        in_specs=in_specs,
        out_specs=out_specs if out_specs is not None else [ANY] * len(outs),
        scratch_shapes=scratch,
        compiler_params=pltpu.CompilerParams(
            collective_id=ident, has_side_effects=True, vmem_limit_bytes=mib * 2**20
        ),
    )(*args)


def start_body(n_ctx, n_shard, rows, wsend, routes, router, cot,
               rows_all, w_all, routes_all, router_all, cot_all,
               local, ss_row, rs_row, ss_fwd, rs_fwd, ss_w, rs_w, ss_rt, rs_rt, ss_ro, rs_ro,
               ss_z, rs_z, ss_rz, rs_rz):
    c, s, parity, sibling, others, layers = here(n_ctx, n_shard)
    greet(others, layers)
    chips = n_shard // 2
    copies = [
        pltpu.make_async_copy(rows, rows_all.at[s], local.at[0]),
        pltpu.make_async_copy(wsend.at[s], w_all.at[s], local.at[1]),
        pltpu.make_async_copy(routes, routes_all.at[c, s], local.at[2]),
        pltpu.make_async_copy(router, router_all.at[s], local.at[3]),
        pltpu.make_async_copy(cot, cot_all.at[c], local.at[4]),
    ]
    for item in copies:
        item.start()
    waits = []
    near = []
    for i, peer in enumerate(others):
        item = push(routes, routes_all.at[c, s], ss_ro.at[i], rs_ro.at[i], shard=peer)
        item.start()
        near.append(item)
    first = []
    for d in range(1, chips):
        item = push(rows, rows_all.at[s], ss_row.at[d], rs_row.at[d], shard=lax.rem(s + 2 * d, n_shard))
        item.start()
        first.append(item)
    item = push(rows, rows_all.at[s], ss_fwd.at[0], rs_fwd.at[0], shard=sibling)
    item.start()
    waits.append(item)
    for i, layer in enumerate(layers):
        item = push(cot, cot_all.at[c], ss_z.at[i], rs_z.at[i], ctx=layer)
        item.start()
        waits.append(item)
    for i, peer in enumerate(others):
        item = push(wsend.at[peer], w_all.at[s], ss_w.at[i], rs_w.at[i], shard=peer)
        item.start()
        waits.append(item)
        item = push(router, router_all.at[s], ss_rt.at[i], rs_rt.at[i], shard=peer)
        item.start()
        waits.append(item)
    copies[2].wait()
    for item in near:
        item.wait()
    for i, layer in enumerate(layers):
        item = push(routes_all.at[c], routes_all.at[c], ss_rz.at[i], rs_rz.at[i], ctx=layer)
        item.start()
        waits.append(item)
    for d in range(1, chips):
        first[d - 1].wait()
        origin = lax.rem(s + n_shard - 2 * d, n_shard)
        item = push(rows_all.at[origin], rows_all.at[origin], ss_fwd.at[d], rs_fwd.at[d], shard=sibling)
        item.start()
        waits.append(item)
    for i in (0, 1, 3, 4):
        copies[i].wait()
    for item in waits:
        item.wait()


def start(n_ctx, n_shard, rows, wsend, routes, router, cot):
    n, z = n_shard, n_ctx
    shapes = [
        (n,) + rows.shape, wsend.shape, (z, n) + routes.shape, (n,) + router.shape, (z,) + cot.shape,
    ]
    kinds = [rows.dtype, wsend.dtype, routes.dtype, router.dtype, cot.dtype]
    sems = [DMA((5,))] + [DMA((n // 2,))] * 4 + [DMA((n - 1,))] * 6 + [DMA((z - 1,))] * 4
    return call(
        functools.partial(start_body, z, n),
        [jax.ShapeDtypeStruct(a, b) for a, b in zip(shapes, kinds)],
        [ANY] * 5, sems, 0, (rows, wsend, routes, router, cot),
    )


def spread_body(n_shard, rows, rows_all, local, ss_row, rs_row, ss_fwd, rs_fwd):
    c, s, parity, sibling, others, layers = here(1, n_shard)
    chips = n_shard // 2
    mates = [lax.rem(s + 2 * d, n_shard) for d in range(1, chips)]
    greet(mates + [sibling], [])
    mine = pltpu.make_async_copy(rows, rows_all.at[s], local)
    mine.start()
    first, waits = [], []
    for d in range(1, chips):
        item = push(rows, rows_all.at[s], ss_row.at[d], rs_row.at[d], shard=mates[d - 1])
        item.start()
        first.append(item)
    item = push(rows, rows_all.at[s], ss_fwd.at[0], rs_fwd.at[0], shard=sibling)
    item.start()
    waits.append(item)
    for d in range(1, chips):
        first[d - 1].wait()
        origin = lax.rem(s + n_shard - 2 * d, n_shard)
        item = push(rows_all.at[origin], rows_all.at[origin], ss_fwd.at[d], rs_fwd.at[d], shard=sibling)
        item.start()
        waits.append(item)
    mine.wait()
    for item in waits:
        item.wait()


def spread(n_shard, rows, ident):
    return call(
        functools.partial(spread_body, n_shard),
        [jax.ShapeDtypeStruct((n_shard,) + rows.shape, rows.dtype)],
        [ANY], [DMA] + [DMA((n_shard // 2,))] * 4, ident, (rows,),
    )[0]


def key_body(n_ctx, n_shard, mine, kv, local, ss_z, rs_z, ss_f, rs_f):
    c, s, parity, sibling, others, layers = here(n_ctx, n_shard)
    greet([sibling], layers)
    own = pltpu.make_async_copy(mine, kv.at[parity, :, c], local)
    own.start()
    far = []
    for i, layer in enumerate(layers):
        item = push(mine, kv.at[parity, :, c], ss_z.at[i], rs_z.at[i], ctx=layer)
        item.start()
        far.append(item)
    waits = []
    item = push(mine, kv.at[parity, :, c], ss_f.at[0], rs_f.at[0], shard=sibling)
    item.start()
    waits.append(item)
    for i in range(n_ctx - 1):
        far[i].wait()
        origin = lax.rem(c + n_ctx - 1 - i, n_ctx)
        item = push(kv.at[parity, :, origin], kv.at[parity, :, origin], ss_f.at[i + 1], rs_f.at[i + 1], shard=sibling)
        item.start()
        waits.append(item)
    own.wait()
    for item in waits:
        item.wait()


def key_exchange(n_ctx, n_shard, mine, ident):
    n, rows, width = mine.shape
    return call(
        functools.partial(key_body, n_ctx, n_shard),
        [jax.ShapeDtypeStruct((2, n, n_ctx, rows, width), mine.dtype)],
        [ANY], [DMA] + [DMA((n_ctx - 1,))] * 2 + [DMA((n_ctx,))] * 2, ident, (mine,),
    )[0]


def key_back_body(n_ctx, n_shard, parts, out, sib, zsend, zrecv, ss_s, rs_s, ss_z, rs_z):
    c, s, parity, sibling, others, layers = here(n_ctx, n_shard)
    greet([sibling], layers)
    waits = []
    order = layers + [c]
    near = []
    for i, layer in enumerate(order):
        item = push(parts.at[1 - parity, :, layer], sib.at[i], ss_s.at[i], rs_s.at[i], shard=sibling)
        item.start()
        near.append(item)
    far = []
    for i, layer in enumerate(layers):
        near[i].wait()
        zsend[i] = (parts[parity, :, layer].astype(F32) + sib[i].astype(F32)).astype(BF)
        item = push(zsend.at[i], zrecv.at[i], ss_z.at[i], rs_z.at[i], ctx=layer)
        item.start()
        far.append(item)
    near[n_ctx - 1].wait()
    total = parts[parity, :, c].astype(F32) + sib[n_ctx - 1].astype(F32)
    for i in range(n_ctx - 1):
        far[i].wait()
        total = total + zrecv[i].astype(F32)
    out[...] = total


def key_back(n_ctx, n_shard, parts, ident):
    block = (parts.shape[1], parts.shape[3], parts.shape[4])
    return call(
        functools.partial(key_back_body, n_ctx, n_shard),
        [jax.ShapeDtypeStruct(block, F32)],
        [VMEM],
        [
            pltpu.VMEM((n_ctx,) + block, BF), pltpu.VMEM((n_ctx - 1,) + block, BF),
            pltpu.VMEM((n_ctx - 1,) + block, BF),
        ] + [DMA((n_ctx,))] * 2 + [DMA((n_ctx - 1,))] * 2,
        ident, (parts,), out_specs=[VMEM],
    )[0]


def product_body(n_shard, tile, flip, left, right, out, part, to_sib, sib, to_chip, got,
                 ss_s, rs_s, ss_c, rs_c):
    c, s, parity, sibling, others, layers = here(1, n_shard)
    chips = n_shard // 2
    chip = lax.div(s, 2)
    mates = [lax.rem(s + 2 * d, n_shard) for d in range(1, chips)]
    greet(mates + [sibling], [])
    rows, width = out.shape
    order = list(range(1, chips)) + [0]
    near = [None] * chips
    for d in order:
        first = pl.multiple_of(lax.rem(chip + d, chips) * (2 * rows), 2 * rows)

        @pl.loop(0, width // tile)
        def _(j):
            cols = pl.ds(pl.multiple_of(j * tile, tile), tile)
            if flip:
                value = lax.dot_general(left[pl.ds(first, 2 * rows), :], right[cols, :],
                                        (((1,), (1,)), ((), ())), preferred_element_type=F32)
            else:
                value = jnp.dot(left[pl.ds(first, 2 * rows), :], right[:, cols],
                                preferred_element_type=F32)
            part[d, :, :, cols] = value.reshape(2, rows, tile)

        to_sib[d] = part[d, 1 - parity].astype(BF)
        near[d] = push(to_sib.at[d], sib.at[d], ss_s.at[d], rs_s.at[d], shard=sibling)
        near[d].start()
    far = []
    for d in range(1, chips):
        near[d].wait()
        to_chip[d - 1] = (part[d, parity] + sib[d].astype(F32)).astype(BF)
        item = push(to_chip.at[d - 1], got.at[d - 1], ss_c.at[d - 1], rs_c.at[d - 1], shard=mates[d - 1])
        item.start()
        far.append(item)
    near[0].wait()
    out[...] = part[0, parity] + sib[0].astype(F32)
    for d in range(1, chips):
        far[d - 1].wait()
        out[...] += got[d - 1].astype(F32)


def product_scatter(n_shard, left, right, flip, ident):
    rows = left.shape[0] // n_shard
    width = right.shape[0] if flip else right.shape[1]
    chips = n_shard // 2
    return call(
        functools.partial(product_body, n_shard, 512, flip),
        [jax.ShapeDtypeStruct((rows, width), F32)],
        [VMEM, VMEM],
        [
            pltpu.VMEM((chips, 2, rows, width), F32), pltpu.VMEM((chips, rows, width), BF),
            pltpu.VMEM((chips, rows, width), BF), pltpu.VMEM((chips - 1, rows, width), BF),
            pltpu.VMEM((chips - 1, rows, width), BF),
        ] + [DMA((chips,))] * 2 + [DMA((chips - 1,))] * 2,
        ident, (left, right), mib=56, out_specs=[VMEM],
    )[0]


def finish_body(n_ctx, n_shard, q_cols, weights, router, gains, q_out, kv_out, router_out, gains_out,
                pieces, landing, acc, total, router_in, router_mid, router_far, gains_in, gains_mid, gains_far, local,
                ss_w, rs_w, ss_i, rs_i, ss_o, rs_o, ss_q, ss_k, ss_r, rs_r, ss_g, rs_g, ss_h, rs_h, ss_t, rs_t):
    c, s, parity, sibling, others, layers = here(n_ctx, n_shard)
    half = n_ctx // 2
    left = c < half
    depth = jnp.where(left, c, n_ctx - 1 - c)
    inner = jnp.where(left, c + 1, c - 1)
    outer = jnp.clip(jnp.where(left, c - 1, c + 1), 0, n_ctx - 1)
    middle = depth == half - 1
    inside = depth > 0
    greet(others, layers)
    waits = []
    sends = [None]
    mine = pltpu.make_async_copy(gains, gains_in.at[s], local)
    mine.start()
    for i, peer in enumerate(others):
        item = push(weights.at[peer], pieces.at[i + 1], ss_w.at[i], rs_w.at[i], shard=peer)
        item.start()
        sends.append(item)
        item = push(router.at[peer], router_in.at[i], ss_r.at[i], rs_r.at[i], shard=peer)
        item.start()
        waits.append(item)
        item = push(gains, gains_in.at[s], ss_g.at[i], rs_g.at[i], shard=peer)
        item.start()
        waits.append(item)

    def inward(j):
        at = jnp.where(middle, 1, 0)
        return push(acc.at[j], landing.at[at, j], ss_i.at[j], rs_i.at[at, j], ctx=inner)

    def outward(j):
        return push(total.at[j], landing.at[1, j], ss_o.at[j], rs_i.at[1, j], ctx=outer)

    def arrived(which, j):
        push(acc.at[j], landing.at[which, j], ss_i.at[j], rs_i.at[which, j], ctx=inner).wait_recv()

    def out_copies(j):
        source = lax.rem(s + n_shard - j, n_shard)
        cols = pl.ds(pl.multiple_of(source * q_cols, q_cols), q_cols)
        return (
            pltpu.make_async_copy(total.at[j, :, pl.ds(0, q_cols)], q_out.at[:, cols], ss_q.at[j]),
            pltpu.make_async_copy(total.at[j, :, pl.ds(q_cols, 128)], kv_out.at[source], ss_k.at[j]),
        )

    def first_half(j):
        if j == 0:
            own = weights[s]
        else:
            sends[j].wait()
            own = pieces[j]

        @pl.when(inside)
        def _():
            arrived(0, j)
            acc[j] = (own.astype(F32) + landing[0, j].astype(F32)).astype(BF)

        @pl.when(jnp.logical_not(inside))
        def _():
            acc[j] = own

        inward(j).start()

    def second_half(j):
        arrived(1, j)

        @pl.when(middle)
        def _():
            total[j] = (acc[j].astype(F32) + landing[1, j].astype(F32)).astype(BF)

        @pl.when(jnp.logical_not(middle))
        def _():
            total[j] = landing[1, j]

        @pl.when(inside)
        def _():
            outward(j).start()

        for item in out_copies(j):
            item.start()

    lag = 2
    for j in range(n_shard + lag):
        if j < n_shard:
            first_half(j)
        if j >= lag:
            second_half(j - lag)
        if j == lag:
            for item in waits:
                item.wait()
            mine.wait()
            gains_mid[...] = gains_in[0]
            for i in range(1, n_shard):
                gains_mid[...] += gains_in[i]
            router_mid[...] = router[s].astype(F32)
            for i in range(n_shard - 1):
                router_mid[...] += router_in[i].astype(F32)
            for i, layer in enumerate(layers):
                push(gains_mid, gains_far.at[c], ss_h.at[i], rs_h.at[i], ctx=layer).start()
                push(router_mid, router_far.at[c], ss_t.at[i], rs_t.at[i], ctx=layer).start()
            mine = pltpu.make_async_copy(gains_mid, gains_far.at[c], local)
            mine.start()
    mine.wait()
    mine = pltpu.make_async_copy(router_mid, router_far.at[c], local)
    mine.start()
    for i, layer in enumerate(layers):
        push(gains_mid, gains_far.at[c], ss_h.at[i], rs_h.at[i], ctx=layer).wait()
        push(router_mid, router_far.at[c], ss_t.at[i], rs_t.at[i], ctx=layer).wait()
    mine.wait()
    gains_out[...] = gains_far[0]
    router_out[...] = router_far[0]
    for i in range(1, n_ctx):
        gains_out[...] += gains_far[i]
        router_out[...] += router_far[i]
    for j in range(n_shard):
        inward(j).wait_send()

        @pl.when(inside)
        def _():
            outward(j).wait_send()

        for item in out_copies(j):
            item.wait()


def finish(n_ctx, n_shard, q_cols, weights, router, gains, ident):
    n, rows, cols = weights.shape
    gain_rows = gains.shape[0]
    router_shape = router.shape[1:]
    return call(
        functools.partial(finish_body, n_ctx, n, q_cols),
        [
            jax.ShapeDtypeStruct((rows, n * q_cols), BF), jax.ShapeDtypeStruct((n, rows, 128), BF),
            jax.ShapeDtypeStruct(router_shape, F32), jax.ShapeDtypeStruct(gains.shape, F32),
        ],
        [VMEM] * 3,
        [
            pltpu.VMEM((n, rows, cols), BF), pltpu.VMEM((2, n, rows, cols), BF),
            pltpu.VMEM((n, rows, cols), BF), pltpu.VMEM((n, rows, cols), BF),
            pltpu.VMEM((n - 1,) + router_shape, BF), pltpu.VMEM(router_shape, F32),
            pltpu.VMEM((n_ctx,) + router_shape, F32), pltpu.VMEM((n, gain_rows, 128), F32),
            pltpu.VMEM((gain_rows, 128), F32), pltpu.VMEM((n_ctx, gain_rows, 128), F32), DMA,
            DMA((n - 1,)), DMA((n - 1,)), DMA((n,)), DMA((2, n)), DMA((n,)), DMA((1,)),
            DMA((n,)), DMA((n,)), DMA((n - 1,)), DMA((n - 1,)), DMA((n - 1,)), DMA((n - 1,)),
            DMA((n_ctx - 1,)), DMA((n_ctx - 1,)), DMA((n_ctx - 1,)), DMA((n_ctx - 1,)),
        ],
        ident, (weights, router, gains), mib=56, out_specs=[ANY, ANY, VMEM, VMEM],
    )


def flip_bits(index, mask):
    result = index
    bit = 1
    while bit <= mask:
        if mask & bit:
            result = result + bit - 2 * bit * lax.rem(lax.div(index, bit), 2)
        bit *= 2
    return result


def dispatch_body(n_ctx, n_shard, group, tile, rows, picks, recv, zrows, ready, local,
                  ss_z, rs_z, ss_x, rs_x):
    c, s, parity, sibling, others, layers = here(n_ctx, n_shard)
    greet(others, layers)
    count, width = rows.shape
    groups = n_ctx // group
    own = pltpu.make_async_copy(rows, zrows.at[c], local.at[0])
    own.start()
    far = []
    for d in range(1, n_ctx):
        item = push(rows, zrows.at[c], ss_z.at[d], rs_z.at[d], ctx=flip_bits(c, d))
        item.start()
        far.append(item)
    waits = []
    for k in range(groups):
        at = flip_bits(lax.div(c, group), k)
        if k == 0:
            own.wait()
        for d in range(max(k * group, 1), (k + 1) * group):
            far[d - 1].wait()
        first = pl.multiple_of(at * group, group)

        @pl.loop(0, width // tile)
        def _(j):
            cols = pl.ds(pl.multiple_of(j * tile, tile), tile)
            block = zrows[pl.ds(first, group), :, cols].reshape(group * count, tile)
            value = jnp.dot(picks[at], block, preferred_element_type=F32).astype(BF)
            ready[k, :, :, cols] = value.reshape(n_shard, -1, tile)

        for i, peer in enumerate(others):
            item = push(ready.at[k, peer], recv.at[s, at], ss_x.at[k, i], rs_x.at[k, i], shard=peer)
            item.start()
            waits.append(item)
        item = pltpu.make_async_copy(ready.at[k, s], recv.at[s, at], local.at[k + 1])
        item.start()
        waits.append(item)
    for item in waits:
        item.wait()


def dispatch_rows(n_ctx, n_shard, group, rows, picks, ident):
    groups, slots = picks.shape[0], picks.shape[1] // n_shard
    count, width = rows.shape
    return call(
        functools.partial(dispatch_body, n_ctx, n_shard, group, 512),
        [jax.ShapeDtypeStruct((n_shard, groups, slots, width), BF)],
        [VMEM, VMEM],
        [
            pltpu.VMEM((n_ctx, count, width), BF), pltpu.VMEM((groups, n_shard, slots, width), BF),
            DMA((groups + 1,)), DMA((n_ctx,)), DMA((n_ctx,)),
            DMA((groups, n_shard - 1)), DMA((groups, n_shard - 1)),
        ],
        ident, (rows, picks), mib=56,
    )[0]


def combine_body(n_ctx, n_shard, group, tile, rows, picks, out, land, value, zsend, zrecv, local,
                 ss_x, rs_x, ss_z, rs_z):
    c, s, parity, sibling, others, layers = here(n_ctx, n_shard)
    greet(others, layers)
    count, width = out.shape
    groups = n_ctx // group
    near = {}
    for k in reversed(range(groups)):
        at = flip_bits(lax.div(c, group), k)
        near[k] = []
        for i, peer in enumerate(others):
            item = push(rows.at[peer, at], land.at[k, s], ss_x.at[k, i], rs_x.at[k, i], shard=peer)
            item.start()
            near[k].append(item)
        item = pltpu.make_async_copy(rows.at[s, at], land.at[k, s], local.at[k])
        item.start()
        near[k].append(item)
    far = []
    for k in reversed(range(groups)):
        at = flip_bits(lax.div(c, group), k)
        for item in near[k]:
            item.wait()

        @pl.loop(0, width // tile)
        def _(j):
            cols = pl.ds(pl.multiple_of(j * tile, tile), tile)
            block = land[k, :, :, cols].reshape(-1, tile)
            value[:, cols] = jnp.dot(picks[at], block, preferred_element_type=F32)

        for d in range(k * group, (k + 1) * group):
            place = lax.rem(flip_bits(c, d), group)
            block = value[pl.ds(pl.multiple_of(place * count, count), count), :]
            if d == 0:
                out[...] = block
            else:
                zsend[d - 1] = block.astype(BF)
                item = push(zsend.at[d - 1], zrecv.at[d - 1], ss_z.at[d], rs_z.at[d], ctx=flip_bits(c, d))
                item.start()
                far.append((d, item))
    for d, item in far:
        item.wait()
        out[...] += zrecv[d - 1].astype(F32)


def combine_rows(n_ctx, n_shard, group, rows, picks, ident):
    groups, slots, width = rows.shape[1:]
    count = picks.shape[1] // group
    tile = 128 * max(t for t in range(1, 9) if (width // 128) % t == 0)
    return call(
        functools.partial(combine_body, n_ctx, n_shard, group, tile),
        [jax.ShapeDtypeStruct((count, width), F32)],
        [VMEM, VMEM],
        [
            pltpu.VMEM((groups, n_shard, slots, width), BF), pltpu.VMEM((group * count, width), F32),
            pltpu.VMEM((n_ctx - 1, count, width), BF), pltpu.VMEM((n_ctx - 1, count, width), BF),
            DMA((groups,)), DMA((groups, n_shard - 1)), DMA((groups, n_shard - 1)),
            DMA((n_ctx,)), DMA((n_ctx,)),
        ],
        ident, (rows, picks), mib=56, out_specs=[VMEM],
    )[0]


QUERY_HEADS = 32
KEY_VALUE_HEADS = 4
HEAD_DIM = 128

epsilon = 1e-06
rope_base = 1000000.0


def rms_scale(hidden, gain):
    return hidden * lax.rsqrt(jnp.mean(hidden * hidden, axis=-1, keepdims=True) + epsilon) * gain


def rotate(headwise, places):
    half_size = headwise.shape[-1] // 2
    frequency = rope_base ** (-jnp.arange(half_size, dtype=F32) * 2.0 / headwise.shape[-1])
    angles = places.astype(F32)[:, None] * frequency[None, :]
    cosine = jnp.cos(angles)[:, None, :]
    sine = jnp.sin(angles)[:, None, :]
    former = headwise[..., :half_size]
    latter = headwise[..., half_size:]
    return jnp.concatenate(
        [former * cosine - latter * sine, latter * cosine + former * sine], axis=-1
    )


def place_of(row_ids, order, block_rows):
    block_ids = jnp.arange(order.shape[0], dtype=jnp.int32)
    owner_block = row_ids // block_rows
    picked_block = jnp.sum(
        jnp.where(owner_block[:, None] == block_ids[None, :], order[None, :], 0), axis=1
    )
    return picked_block * block_rows + row_ids % block_rows


def dot(left, right):
    return jnp.dot(left, right, preferred_element_type=F32)


def contract_rows(left, right):
    return lax.dot_general(left, right, (((0,), (0,)), ((), ())), preferred_element_type=F32)


def contract_cols(left, right):
    return lax.dot_general(left, right, (((1,), (1,)), ((), ())), preferred_element_type=F32)


def exchange_shard(x):
    return lax.all_to_all(x, "shard", split_axis=0, concat_axis=0, tiled=True)


def gather_ctx(x):
    return lax.all_gather(x, "ctx", axis=0, tiled=False)


def scatter_ctx(x):
    return lax.psum_scatter(x, "ctx", scatter_dimension=0, tiled=False)


def shards(
    tokens,
    cotangent,
    block_order,
    routes,
    attn_gain,
    w_query,
    key_weight,
    value_weight,
    query_gain,
    key_gain,
    w_out,
    ffn_gain,
    w_router,
    w_gate,
    w_up,
    w_down,
):
    rows = tokens.shape[1]
    width = tokens.shape[2]
    ctx_count = lax.axis_size("ctx")
    shard_count = lax.axis_size("shard")
    my_ctx = lax.axis_index("ctx")
    my_shard = lax.axis_index("shard")
    experts = ctx_count * shard_count
    block_rows = rows // 2
    heads = QUERY_HEADS // shard_count
    head_cols = heads * HEAD_DIM
    sharers = shard_count // KEY_VALUE_HEADS
    score_scale = HEAD_DIM ** (-0.5)
    top_count = routes.shape[2]
    capacity = rows * top_count // experts + max(rows * top_count // (4 * experts), 1)
    sequence = rows * ctx_count
    plane = rows * shard_count
    wrows = width // shard_count

    inputs = tokens[0].astype(F32)
    upstream_b = cotangent[0]
    upstream = upstream_b.astype(F32)

    kv_kind = [key_weight, value_weight]
    extra = [
        kv_kind[(s % sharers) % 2][:, (s // sharers) * HEAD_DIM : (s // sharers + 1) * HEAD_DIM]
        for s in range(shard_count)
    ]
    send_w = jnp.stack(
        [
            jnp.concatenate([w_query[:, s * head_cols : (s + 1) * head_cols], extra[s]], axis=1)
            for s in range(shard_count)
        ]
    )
    normed = rms_scale(inputs, attn_gain)
    normed_b = normed.astype(BF)
    normed_all, w_mine, routes_all, router_all, upstream_z = start(
        ctx_count, shard_count, normed_b, send_w, routes[0].T, w_router.T, upstream_b
    )
    normed_all = normed_all.reshape(plane, width)
    w_mine = w_mine.reshape(width, head_cols + HEAD_DIM)
    routes_all = jnp.swapaxes(routes_all, 2, 3)
    router_all = jnp.swapaxes(router_all, 1, 2).reshape(width, experts)

    named = jnp.sum(
        (routes_all[..., None] == jnp.arange(experts, dtype=jnp.int32)).astype(BF), axis=3
    )
    earlier = (
        jnp.arange(rows, dtype=jnp.int32)[:, None] > jnp.arange(rows, dtype=jnp.int32)[None, :]
    ).astype(BF)
    slots = jnp.arange(capacity, dtype=F32)

    def places_in(mask):
        rank = jnp.einsum("tu,...un->...tn", earlier, mask, preferred_element_type=F32)
        pick = jnp.where(mask > 0, rank, -1.0)
        return (jnp.swapaxes(pick, -1, -2)[..., None, :] == slots[:, None]).astype(BF)

    my_rows = lax.dynamic_index_in_dim(named, my_shard, 1, keepdims=False)
    my_rows = lax.dynamic_slice_in_dim(my_rows, my_ctx * shard_count, shard_count, 2)
    pick_send = places_in(my_rows)
    mine = lax.dynamic_slice_in_dim(named, my_ctx * shard_count + my_shard, 1, 3)
    pick_here = places_in(mine)[:, :, 0]
    chosen_here = jnp.einsum(
        "cbqt,cbte->bcqe", pick_here, named, preferred_element_type=F32
    ).reshape(-1, experts)

    group = 1
    while group * capacity % 16:
        group *= 2
    groups = ctx_count // group
    by_group = jnp.swapaxes(pick_send.reshape(groups, group, shard_count, capacity, rows), 1, 2)
    same = jnp.eye(group, dtype=BF)
    picks = (by_group[:, :, :, :, None, :] * same[None, None, :, None, :, None]).reshape(
        groups, shard_count * group * capacity, group * rows
    )
    picks_t = jnp.swapaxes(picks, 1, 2)
    slot_rows = shard_count * ctx_count * capacity
    block_shape = (shard_count, groups, group * capacity)

    sent_up = jnp.einsum(
        "nkr,nrd->nkd", picks, upstream_z.reshape(groups, group * rows, width), preferred_element_type=F32
    ).astype(BF)
    sent_up = jnp.swapaxes(sent_up.reshape((groups, shard_count, group * capacity, width)), 0, 1)
    upstream_rows = exchange_shard(sent_up).reshape(slot_rows, width).astype(F32)

    qkv = dot(normed_all, w_mine)
    query_pre = qkv[:, :head_cols].reshape(shard_count, rows, heads, HEAD_DIM)
    row_ids = my_ctx * rows + jnp.arange(rows, dtype=jnp.int32)
    q_places = place_of(row_ids, block_order, block_rows)
    k_places = place_of(jnp.arange(sequence, dtype=jnp.int32), block_order, block_rows)
    sees = k_places[None, :] <= q_places[:, None]

    def prep(pre, gain):
        shape = pre.shape
        flat = pre.reshape(-1, rows, shape[-2], HEAD_DIM)
        return jax.vmap(lambda v: rotate(rms_scale(v, gain), q_places))(flat).reshape(shape)

    queries = prep(query_pre, query_gain).astype(BF)
    my_place = lax.rem(my_shard, sharers)
    is_key = lax.rem(my_place, 2) == 0
    part_count = sharers // 2
    kv_pre = qkv[:, head_cols:]
    key_roped = prep(kv_pre.reshape(shard_count, rows, 1, HEAD_DIM), key_gain).reshape(plane, HEAD_DIM)
    kv_b = jnp.where(is_key, key_roped, kv_pre).astype(BF)
    kv_all = key_exchange(ctx_count, shard_count, kv_b.reshape(shard_count, rows, HEAD_DIM), 1)
    kv_all = kv_all.reshape(2, shard_count, sequence, HEAD_DIM)
    keys, values = kv_all[0], kv_all[1]

    scores = (
        jnp.einsum("sthd,spd->shtp", queries, keys, preferred_element_type=F32) * score_scale
    )
    scores = jnp.where(sees, scores, -1e30)
    top = jnp.max(scores, axis=-1, keepdims=True)
    raised = jnp.exp(scores - top)
    total = jnp.sum(raised, axis=-1, keepdims=True)
    probs = raised / total
    probs_b = probs.astype(BF)
    attn_f32 = jnp.einsum("shtp,spd->sthd", probs_b, values, preferred_element_type=F32)
    attn_b = attn_f32.astype(BF)
    attn_rows = attn_b.reshape(plane, head_cols)
    middle = inputs + product_scatter(shard_count, attn_rows, w_out, False, 2)

    normed_two = rms_scale(middle, ffn_gain)
    second_b = normed_two.astype(BF)
    logits = dot(second_b, router_all)
    chosen = jnp.sum(
        (routes[0][:, :, None] == jnp.arange(experts, dtype=jnp.int32)).astype(F32), axis=1
    )

    def gates_of(log, mask):
        masked = jnp.where(mask > 0, log, -1e30)
        peak = jnp.max(masked, axis=-1, keepdims=True)
        risen = jnp.exp(masked - peak) * mask
        return risen / jnp.maximum(jnp.sum(risen, axis=-1, keepdims=True), 1e-30)

    gates = gates_of(logits, chosen)

    received = dispatch_rows(ctx_count, shard_count, group, second_b, picks, 3).reshape(slot_rows, width)
    my_expert = my_ctx * shard_count + my_shard
    slot_gates = lax.dynamic_slice_in_dim(
        gates_of(dot(received, router_all), chosen_here), my_expert, 1, 1
    )
    gate_pre = dot(received, w_gate[0])
    up_pre = dot(received, w_up[0])
    activated = jax.nn.silu(gate_pre)
    hidden_b = (activated * up_pre).astype(BF)
    expert_out = dot(hidden_b, w_down[0]).astype(BF)
    expert_out_f = expert_out.astype(F32)
    mix_back = exchange_shard((slot_gates * expert_out_f).astype(BF).reshape(block_shape + (width,)))
    mix_part = jnp.einsum(
        "nrsk,snkd->nrd",
        picks_t.reshape(groups, group * rows, shard_count, group * capacity),
        mix_back,
        preferred_element_type=F32,
    ).astype(BF)
    mixture = scatter_ctx(mix_part.reshape(ctx_count, rows, width)).astype(F32)
    mixed = (middle + mixture).astype(BF)
    slot_dot = jnp.sum(expert_out_f * upstream_rows, axis=1, keepdims=True)
    grad_expert = (slot_gates * upstream_rows).astype(BF)
    grad_w_down = contract_rows(hidden_b, grad_expert)
    grad_hidden = contract_cols(grad_expert, w_down[0])
    sigmoid_g = jax.nn.sigmoid(gate_pre)
    silu_slope = sigmoid_g * (1.0 + gate_pre * (1.0 - sigmoid_g))
    grad_gate_pre = (grad_hidden * up_pre * silu_slope).astype(BF)
    grad_up_pre = (grad_hidden * activated).astype(BF)
    grad_w_gate = contract_rows(received, grad_gate_pre)
    grad_w_up = contract_rows(received, grad_up_pre)
    grad_received = contract_cols(grad_gate_pre, w_gate[0]) + contract_cols(grad_up_pre, w_up[0])

    tail_cols = -(-2 * experts // 128) * 128
    coarse = slot_dot.astype(BF).astype(F32)
    fine = slot_dot - coarse
    column = jnp.arange(tail_cols, dtype=jnp.int32)[None, :]
    tail = jnp.where(column == my_expert, coarse, 0.0) + jnp.where(
        column == experts + my_expert, fine, 0.0
    )
    back_rows = jnp.concatenate([grad_received, tail], axis=1).astype(BF)
    back = combine_rows(
        ctx_count, shard_count, group, back_rows.reshape(block_shape + (width + tail_cols,)), picks_t, 4
    )
    grad_second = back[:, :width]
    grad_gates = back[:, width : width + experts] + back[:, width + experts : width + 2 * experts]
    grad_logits_b = (
        gates * (grad_gates - jnp.sum(gates * grad_gates, axis=-1, keepdims=True))
    ).astype(BF)
    router_part = contract_rows(grad_logits_b, second_b).astype(BF)
    grad_second = grad_second + contract_cols(grad_logits_b, router_all)
    unused, norm_two_back = jax.vjp(rms_scale, middle, ffn_gain)
    grad_middle_part, grad_ffn_gain = norm_two_back(grad_second)
    grad_middle = upstream + grad_middle_part
    grad_proj_b = grad_middle.astype(BF)

    grad_proj_all = spread(shard_count, grad_proj_b, 5).reshape(plane, width)
    grad_attn = contract_cols(grad_proj_all, w_out).astype(BF)
    grad_w_out = lax.psum(contract_rows(attn_rows, grad_proj_all).astype(BF), "ctx").astype(F32)
    grad_heads = grad_attn.reshape(shard_count, rows, heads, HEAD_DIM)
    delta = jnp.transpose(jnp.sum(grad_heads.astype(F32) * attn_f32, axis=-1), (0, 2, 1))[..., None]
    grad_probs = jnp.einsum("sthd,spd->shtp", grad_heads, values, preferred_element_type=F32)
    grad_scores = (probs * (grad_probs - delta)).astype(BF)
    grad_query = score_scale * jnp.einsum(
        "shtp,spd->sthd", grad_scores, keys, preferred_element_type=F32
    )
    grad_keys = score_scale * jnp.einsum(
        "shtp,sthd->spd", grad_scores, queries, preferred_element_type=F32
    )
    grad_values = jnp.einsum("shtp,sthd->spd", probs_b, grad_heads, preferred_element_type=F32)
    grad_kv = jnp.stack([grad_keys, grad_values]).astype(BF)
    grad_kv = key_back(
        ctx_count, shard_count, grad_kv.reshape(2, shard_count, ctx_count, rows, HEAD_DIM), 6
    )
    unused, query_back = jax.vjp(prep, query_pre, query_gain)
    grad_query_pre, grad_query_gain = query_back(grad_query)
    kv_shape = (shard_count, rows, 1, HEAD_DIM)
    unused, key_prep_back = jax.vjp(prep, kv_pre.reshape(kv_shape), key_gain)
    grad_key_pre, grad_key_gain = key_prep_back(grad_kv.reshape(kv_shape))
    grad_key_gain = jnp.where(is_key, grad_key_gain, 0.0)
    grad_kv_full = jnp.where(
        is_key, grad_key_pre.reshape(plane, HEAD_DIM), grad_kv.reshape(plane, HEAD_DIM)
    ).astype(BF)
    grad_pre = jnp.concatenate(
        [grad_query_pre.reshape(plane, head_cols).astype(BF), grad_kv_full], axis=1
    )
    grad_normed = product_scatter(shard_count, grad_pre, w_mine, True, 7)
    unused, norm_one_back = jax.vjp(rms_scale, inputs, attn_gain)
    grad_input_part, grad_attn_gain = norm_one_back(grad_normed)
    grad_tokens = grad_middle + grad_input_part
    gains = jnp.concatenate([grad_attn_gain, grad_ffn_gain, grad_query_gain, grad_key_gain])
    gain_rows = -(-gains.shape[0] // 1024) * 8
    gains = jnp.pad(gains, (0, gain_rows * 128 - gains.shape[0])).reshape(gain_rows, 128)

    grad_w = contract_rows(normed_all, grad_pre).astype(BF).reshape(shard_count, wrows, -1)
    router_parts = jnp.swapaxes(router_part.reshape(experts, shard_count, wrows), 0, 1)
    q_sum, kv_sum, router_sum, gains = finish(
        ctx_count, shard_count, head_cols, grad_w, router_parts, gains, 8
    )
    gains = gains.reshape(-1)
    grad_attn_gain, grad_ffn_gain = gains[:width], gains[width : 2 * width]
    grad_query_gain = gains[2 * width : 2 * width + HEAD_DIM]
    grad_key_gain = gains[2 * width + HEAD_DIM : 2 * width + 2 * HEAD_DIM]
    grad_w_query = q_sum.astype(F32)
    kinds = kv_sum.astype(F32).reshape(KEY_VALUE_HEADS, part_count, 2, wrows, HEAD_DIM)
    kinds = jnp.transpose(jnp.sum(kinds, axis=1), (1, 2, 0, 3)).reshape(2, wrows, -1)
    grad_w_key, grad_w_value = kinds[0], kinds[1]
    grad_w_router = router_sum.T
    return (
        mixed[None],
        grad_tokens[None],
        grad_attn_gain,
        grad_w_query,
        grad_w_key,
        grad_w_value,
        grad_query_gain,
        grad_key_gain,
        grad_w_out,
        grad_ffn_gain,
        grad_w_router,
        grad_w_gate[None],
        grad_w_up[None],
        grad_w_down[None],
    )


def solution(mesh):
    rows = P("shard", "ctx", None)
    matrix = P("shard", None)
    expert = P(("ctx", "shard"), None, None)
    return jax.shard_map(
        shards,
        mesh=mesh,
        in_specs=(
            rows, rows, P(), rows, P(), matrix, matrix, matrix, P(), P(), matrix, P(), matrix,
            expert, expert, expert,
        ),
        out_specs=(
            rows, rows, P(), matrix, matrix, matrix, P(), P(), matrix, P(), matrix,
            expert, expert, expert,
        ),
        check_vma=False,
    )
```

```python
import functools

import jax
import jax.numpy as jnp
from jax import lax
from jax.experimental import pallas as pl
from jax.experimental.pallas import tpu as pltpu
from jax.sharding import PartitionSpec as P

BF = jnp.bfloat16
F32 = jnp.float32
MESH = pl.DeviceIdType.MESH
ANY = pl.BlockSpec(memory_space=pl.ANY)
VMEM = pl.BlockSpec(memory_space=pltpu.VMEM)
DMA = pltpu.SemaphoreType.DMA
epsilon = 1e-06


def push(src, dst, send_sem, recv_sem, **where):
    return pltpu.make_async_remote_copy(
        src_ref=src, dst_ref=dst, send_sem=send_sem, recv_sem=recv_sem,
        device_id=where, device_id_type=MESH,
    )


def greet(shard_peers, ctx_peers):
    barrier = pltpu.get_barrier_semaphore()
    for peer in shard_peers:
        pl.semaphore_signal(barrier, inc=1, device_id={"shard": peer}, device_id_type=MESH)
    for peer in ctx_peers:
        pl.semaphore_signal(barrier, inc=1, device_id={"ctx": peer}, device_id_type=MESH)
    pl.semaphore_wait(barrier, len(shard_peers) + len(ctx_peers))


def here(ctx_count, shard_count):
    c, s = lax.axis_index("ctx"), lax.axis_index("shard")
    parity = lax.rem(s, 2)
    sibling = s + 1 - 2 * parity
    others = [lax.rem(s + d, shard_count) for d in range(1, shard_count)]
    layers = [lax.rem(c + d, ctx_count) for d in range(1, ctx_count)]
    return c, s, parity, sibling, others, layers


def flip_bits(index, mask):
    result = index
    bit = 1
    while bit <= mask:
        if mask & bit:
            result = result + bit - 2 * bit * lax.rem(lax.div(index, bit), 2)
        bit *= 2
    return result


def lowest(d):
    return d & -d


class Fan:
    def __init__(self, n_ctx, c, block, ss, rs, near_first):
        self.n_ctx, self.c, self.block, self.ss, self.rs, self.near_first = n_ctx, c, block, ss, rs, near_first
        self.items = {}

    def send(self, d, src):
        bits = [b for b in (1, 2, 4, 8, 16) if b < (lowest(d) or self.n_ctx)]
        for b in bits if self.near_first else reversed(bits):
            item = push(src, self.block(d), self.ss.at[d | b], self.rs.at[d | b], ctx=flip_bits(self.c, b))
            item.start()
            self.items[d | b] = item

    def arrival(self, d):
        self.items[d].wait_recv()
        if lowest(d) > 1:
            self.send(d, self.block(d))

    def order(self):
        return sorted(range(1, self.n_ctx), key=lambda d: (bin(d).count("1"), d if self.near_first else -d))

    def drain(self):
        for d in range(1, self.n_ctx):
            self.items[d].wait_send()


class Fold:
    def __init__(self, c, sent, received, ss, rs):
        self.c, self.sent, self.received, self.ss, self.rs = c, sent, received, ss, rs
        self.items = {}

    def take(self, d, value):
        for b in (1, 2, 4, 8, 16):
            if b < lowest(d) or (d == 0 and b in self.items):
                self.items[d | b].wait_recv()
                value = value + self.received[(d | b) - 1].astype(F32)
        return value

    def give(self, d, value):
        self.sent[d - 1] = value.astype(BF)
        item = push(self.sent.at[d - 1], self.received.at[d - 1], self.ss.at[d], self.rs.at[d],
                    ctx=flip_bits(self.c, lowest(d)))
        item.start()
        self.items[d] = item

    def drain(self):
        for item in self.items.values():
            item.wait_send()


def call(body, outs, in_specs, scratch, ident, args, mib=48, out_specs=None):
    return pl.pallas_call(
        body,
        out_shape=outs,
        in_specs=in_specs,
        out_specs=out_specs if out_specs is not None else [ANY] * len(outs),
        scratch_shapes=scratch,
        compiler_params=pltpu.CompilerParams(
            collective_id=ident, has_side_effects=True, vmem_limit_bytes=mib * 2**20
        ),
    )(*args)


def start_body(n_ctx, n_shard, rows, wsend, routes, router, cot,
               rows_all, w_all, routes_all, router_all, cot_all,
               local, ss_row, rs_row, ss_fwd, rs_fwd, ss_w, rs_w, ss_rt, rs_rt, ss_ro, rs_ro,
               ss_z, rs_z, ss_rz, rs_rz):
    c, s, parity, sibling, others, layers = here(n_ctx, n_shard)
    greet(others, layers)
    chips = n_shard // 2
    copies = [
        pltpu.make_async_copy(rows, rows_all.at[s], local.at[0]),
        pltpu.make_async_copy(wsend.at[s], w_all.at[s], local.at[1]),
        pltpu.make_async_copy(routes, routes_all.at[c, s], local.at[2]),
        pltpu.make_async_copy(router, router_all.at[s], local.at[3]),
        pltpu.make_async_copy(cot, cot_all.at[c], local.at[4]),
    ]
    for item in copies:
        item.start()
    waits = []
    near = []
    for i, peer in enumerate(others):
        item = push(routes, routes_all.at[c, s], ss_ro.at[i], rs_ro.at[i], shard=peer)
        item.start()
        near.append(item)
    first = []
    for d in range(1, chips):
        item = push(rows, rows_all.at[s], ss_row.at[d], rs_row.at[d], shard=lax.rem(s + 2 * d, n_shard))
        item.start()
        first.append(item)
    item = push(rows, rows_all.at[s], ss_fwd.at[0], rs_fwd.at[0], shard=sibling)
    item.start()
    waits.append(item)
    fan = Fan(n_ctx, c, lambda d: cot_all.at[flip_bits(c, d)], ss_z, rs_z, False)
    fan.send(0, cot)
    for i, peer in enumerate(others):
        item = push(wsend.at[peer], w_all.at[s], ss_w.at[i], rs_w.at[i], shard=peer)
        item.start()
        waits.append(item)
        item = push(router, router_all.at[s], ss_rt.at[i], rs_rt.at[i], shard=peer)
        item.start()
        waits.append(item)
    copies[2].wait()
    for item in near:
        item.wait()
    for i, layer in enumerate(layers):
        item = push(routes_all.at[c], routes_all.at[c], ss_rz.at[i], rs_rz.at[i], ctx=layer)
        item.start()
        waits.append(item)
    for d in range(1, chips):
        first[d - 1].wait()
        origin = lax.rem(s + n_shard - 2 * d, n_shard)
        item = push(rows_all.at[origin], rows_all.at[origin], ss_fwd.at[d], rs_fwd.at[d], shard=sibling)
        item.start()
        waits.append(item)
    for d in fan.order():
        fan.arrival(d)
    fan.drain()
    for i in (0, 1, 3, 4):
        copies[i].wait()
    for item in waits:
        item.wait()


def start(n_ctx, n_shard, rows, wsend, routes, router, cot):
    n, z = n_shard, n_ctx
    shapes = [
        (n,) + rows.shape, wsend.shape, (z, n) + routes.shape, (n,) + router.shape, (z,) + cot.shape,
    ]
    kinds = [rows.dtype, wsend.dtype, routes.dtype, router.dtype, cot.dtype]
    sems = [DMA((5,))] + [DMA((n // 2,))] * 4 + [DMA((n - 1,))] * 6 + [DMA((z,))] * 4
    return call(
        functools.partial(start_body, z, n),
        [jax.ShapeDtypeStruct(a, b) for a, b in zip(shapes, kinds)],
        [ANY] * 5, sems, 0, (rows, wsend, routes, router, cot),
    )


def spread_body(n_shard, rows, rows_all, local, ss_row, rs_row, ss_fwd, rs_fwd):
    c, s, parity, sibling, others, layers = here(1, n_shard)
    chips = n_shard // 2
    mates = [lax.rem(s + 2 * d, n_shard) for d in range(1, chips)]
    greet(mates + [sibling], [])
    mine = pltpu.make_async_copy(rows, rows_all.at[s], local)
    mine.start()
    first, waits = [], []
    for d in range(1, chips):
        item = push(rows, rows_all.at[s], ss_row.at[d], rs_row.at[d], shard=mates[d - 1])
        item.start()
        first.append(item)
    item = push(rows, rows_all.at[s], ss_fwd.at[0], rs_fwd.at[0], shard=sibling)
    item.start()
    waits.append(item)
    for d in range(1, chips):
        first[d - 1].wait()
        origin = lax.rem(s + n_shard - 2 * d, n_shard)
        item = push(rows_all.at[origin], rows_all.at[origin], ss_fwd.at[d], rs_fwd.at[d], shard=sibling)
        item.start()
        waits.append(item)
    mine.wait()
    for item in waits:
        item.wait()


def spread(n_shard, rows, ident):
    return call(
        functools.partial(spread_body, n_shard),
        [jax.ShapeDtypeStruct((n_shard,) + rows.shape, rows.dtype)],
        [ANY], [DMA] + [DMA((n_shard // 2,))] * 4, ident, (rows,),
    )[0]


def key_body(n_ctx, n_shard, mine, kv, local, ss_z, rs_z, ss_f, rs_f):
    c, s, parity, sibling, others, layers = here(n_ctx, n_shard)
    greet([sibling], layers)
    own = pltpu.make_async_copy(mine, kv.at[parity, :, c], local)
    own.start()
    fan = Fan(n_ctx, c, lambda d: kv.at[parity, :, flip_bits(c, d)], ss_z, rs_z, False)
    fan.send(0, mine)
    waits = []
    item = push(mine, kv.at[parity, :, c], ss_f.at[0], rs_f.at[0], shard=sibling)
    item.start()
    waits.append(item)
    for d in fan.order():
        fan.arrival(d)
        block = kv.at[parity, :, flip_bits(c, d)]
        item = push(block, block, ss_f.at[d], rs_f.at[d], shard=sibling)
        item.start()
        waits.append(item)
    fan.drain()
    own.wait()
    for item in waits:
        item.wait()


def key_exchange(n_ctx, n_shard, mine, ident):
    n, rows, width = mine.shape
    return call(
        functools.partial(key_body, n_ctx, n_shard),
        [jax.ShapeDtypeStruct((2, n, n_ctx, rows, width), mine.dtype)],
        [ANY], [DMA] + [DMA((n_ctx,))] * 4, ident, (mine,),
    )[0]


def key_back_body(n_ctx, n_shard, parts, out, sib, zsend, zrecv, ss_s, rs_s, ss_z, rs_z):
    c, s, parity, sibling, others, layers = here(n_ctx, n_shard)
    greet([sibling], layers)
    order = list(range(1, n_ctx)) + [0]
    near = {}
    for d in order:
        block = parts.at[1 - parity, :, lax.rem(c + d, n_ctx)]
        near[d] = push(block, sib.at[d], ss_s.at[d], rs_s.at[d], shard=sibling)
        near[d].start()
    far = {}
    for d in order:
        near[d].wait()
        layer = lax.rem(c + d, n_ctx)
        value = parts[parity, :, layer].astype(F32) + sib[d].astype(F32)
        if d:
            zsend[d - 1] = value.astype(BF)
            far[d] = push(zsend.at[d - 1], zrecv.at[d - 1], ss_z.at[d], rs_z.at[d], ctx=layer)
            far[d].start()
    for d in range(1, n_ctx):
        far[d].wait()
        value = value + zrecv[d - 1].astype(F32)
    out[...] = value


def key_back(n_ctx, n_shard, parts, ident):
    block = (parts.shape[1], parts.shape[3], parts.shape[4])
    return call(
        functools.partial(key_back_body, n_ctx, n_shard),
        [jax.ShapeDtypeStruct(block, F32)],
        [VMEM],
        [
            pltpu.VMEM((n_ctx,) + block, BF), pltpu.VMEM((n_ctx - 1,) + block, BF),
            pltpu.VMEM((n_ctx - 1,) + block, BF),
        ] + [DMA((n_ctx,))] * 4,
        ident, (parts,), out_specs=[VMEM],
    )[0]


def product_body(n_shard, tile, flip, left, right, out, part, to_sib, sib, to_chip, got,
                 ss_s, rs_s, ss_c, rs_c):
    c, s, parity, sibling, others, layers = here(1, n_shard)
    chips = n_shard // 2
    chip = lax.div(s, 2)
    mates = [lax.rem(s + 2 * d, n_shard) for d in range(1, chips)]
    greet(mates + [sibling], [])
    rows, width = out.shape
    order = list(range(1, chips)) + [0]
    near = [None] * chips
    for d in order:
        first = pl.multiple_of(lax.rem(chip + d, chips) * (2 * rows), 2 * rows)

        @pl.loop(0, width // tile)
        def _(j):
            cols = pl.ds(pl.multiple_of(j * tile, tile), tile)
            if flip:
                value = lax.dot_general(left[pl.ds(first, 2 * rows), :], right[cols, :],
                                        (((1,), (1,)), ((), ())), preferred_element_type=F32)
            else:
                value = jnp.dot(left[pl.ds(first, 2 * rows), :], right[:, cols],
                                preferred_element_type=F32)
            part[d, :, :, cols] = value.reshape(2, rows, tile)

        to_sib[d] = part[d, 1 - parity].astype(BF)
        near[d] = push(to_sib.at[d], sib.at[d], ss_s.at[d], rs_s.at[d], shard=sibling)
        near[d].start()
    far = []
    for d in range(1, chips):
        near[d].wait()
        to_chip[d - 1] = (part[d, parity] + sib[d].astype(F32)).astype(BF)
        item = push(to_chip.at[d - 1], got.at[d - 1], ss_c.at[d - 1], rs_c.at[d - 1], shard=mates[d - 1])
        item.start()
        far.append(item)
    near[0].wait()
    out[...] = part[0, parity] + sib[0].astype(F32)
    for d in range(1, chips):
        far[d - 1].wait()
        out[...] += got[d - 1].astype(F32)


def product_scatter(n_shard, left, right, flip, ident):
    rows = left.shape[0] // n_shard
    width = right.shape[0] if flip else right.shape[1]
    chips = n_shard // 2
    return call(
        functools.partial(product_body, n_shard, 512, flip),
        [jax.ShapeDtypeStruct((rows, width), F32)],
        [VMEM, VMEM],
        [
            pltpu.VMEM((chips, 2, rows, width), F32), pltpu.VMEM((chips, rows, width), BF),
            pltpu.VMEM((chips, rows, width), BF), pltpu.VMEM((chips - 1, rows, width), BF),
            pltpu.VMEM((chips - 1, rows, width), BF),
        ] + [DMA((chips,))] * 2 + [DMA((chips - 1,))] * 2,
        ident, (left, right), mib=56, out_specs=[VMEM],
    )[0]


def finish_body(n_ctx, n_shard, q_cols, tile,
                weights, wide, router, gains, left, right, tokens, gain,
                q_out, kv_out, wide_out, router_out, gains_out, rows_out,
                wide_landing, wide_acc, wide_total, ss_wi, rs_wi, ss_wo, ss_wc, pieces, landing, acc, total, router_in, router_mid, router_far,
                gains_own, gains_in, gains_mid, gains_far, pair, own_part, to_sib, sib, to_chip, got,
                local, ss_w, rs_w, ss_i, rs_i, ss_o, ss_q, ss_k, ss_r, rs_r, ss_g, rs_g, ss_h, rs_h,
                ss_t, rs_t, ss_s, rs_s, ss_c, rs_c):
    c, s, parity, sibling, others, layers = here(n_ctx, n_shard)
    half = n_ctx // 2
    chips = n_shard // 2
    chip = lax.div(s, 2)
    mates = [lax.rem(s + 2 * d, n_shard) for d in range(1, chips)]
    left_side = c < half
    depth = jnp.where(left_side, c, n_ctx - 1 - c)
    inner = jnp.where(left_side, c + 1, c - 1)
    outer = jnp.clip(jnp.where(left_side, c - 1, c + 1), 0, n_ctx - 1)
    middle = depth == half - 1
    inside = depth > 0
    rows, width = rows_out.shape
    greet(others, layers)
    sends, small = [None], []
    for i, peer in enumerate(others):
        item = push(weights.at[peer], pieces.at[i + 1], ss_w.at[i], rs_w.at[i], shard=peer)
        item.start()
        sends.append(item)
    for i, peer in enumerate(others):
        item = push(router.at[peer], router_in.at[i], ss_r.at[i], rs_r.at[i], shard=peer)
        item.start()
        small.append(item)

    def out_copies(j, ref):
        source = lax.rem(s + n_shard - j, n_shard)
        cols = pl.ds(pl.multiple_of(source * q_cols, q_cols), q_cols)
        return (
            pltpu.make_async_copy(ref.at[:, pl.ds(0, q_cols)], q_out.at[:, cols], ss_q.at[j]),
            pltpu.make_async_copy(ref.at[:, pl.ds(q_cols, 128)], kv_out.at[source], ss_k.at[j]),
        )

    def wide_copies(j, ref):
        return (pltpu.make_async_copy(ref, wide_out.at[j], ss_wc.at[j]),)

    class Line:
        def __init__(self, ready, own, acc, landing, total, ss_i, rs_i, ss_o, copies):
            self.ready, self.own, self.acc, self.landing, self.total = ready, own, acc, landing, total
            self.ss_i, self.rs_i, self.ss_o, self.copies = ss_i, rs_i, ss_o, copies

        def inward(self, j, ref):
            at = jnp.where(middle, 1, 0)
            return push(ref, self.landing.at[at, j], self.ss_i.at[j], self.rs_i.at[at, j], ctx=inner)

        def outward(self, j):
            return push(self.total.at[j], self.landing.at[1, j], self.ss_o.at[j], self.rs_i.at[1, j], ctx=outer)

        def arrived(self, which, j):
            push(self.acc.at[j], self.landing.at[which, j], self.ss_i.at[j], self.rs_i.at[which, j],
                 ctx=inner).wait_recv()

        def outermost(self, j):
            @pl.when(jnp.logical_not(inside))
            def _():
                self.ready(j)
                self.inward(j, self.own(j)).start()

        def first_half(self, j):
            @pl.when(inside)
            def _():
                self.ready(j)
                self.arrived(0, j)
                self.acc[j] = (self.own(j)[...].astype(F32) + self.landing[0, j].astype(F32)).astype(BF)
                self.inward(j, self.acc.at[j]).start()

        def second_half(self, j):
            self.arrived(1, j)

            @pl.when(middle)
            def _():
                self.total[j] = (self.acc[j].astype(F32) + self.landing[1, j].astype(F32)).astype(BF)

            @pl.when(jnp.logical_not(middle))
            def _():
                self.total[j] = self.landing[1, j]

            @pl.when(inside)
            def _():
                self.outward(j).start()

            for item in self.copies(j, self.total.at[j]):
                item.start()

        def drain(self, j):
            self.inward(j, self.acc.at[j]).wait_send()

            @pl.when(inside)
            def _():
                self.outward(j).wait_send()

            for item in self.copies(j, self.total.at[j]):
                item.wait()

    line = Line(lambda j: sends[j].wait() if j else None, lambda j: pieces.at[j] if j else weights.at[s],
                acc, landing, total, ss_i, rs_i, ss_o, out_copies)
    wide_line = Line(lambda j: None, lambda j: wide.at[j], wide_acc, wide_landing, wide_total,
                     ss_wi, rs_wi, ss_wo, wide_copies)
    wides = wide.shape[0]
    steps = [(wide_line, j) for j in range(wides)] + [(line, j) for j in range(n_shard)]

    near, far = {}, {}

    def product(d):
        first = pl.multiple_of(lax.rem(chip + d, chips) * (2 * rows), 2 * rows)

        @pl.loop(0, width // tile)
        def _(j):
            cols = pl.ds(pl.multiple_of(j * tile, tile), tile)
            value = lax.dot_general(left[pl.ds(first, 2 * rows), :], right[cols, :],
                                    (((1,), (1,)), ((), ())), preferred_element_type=F32)
            pair[...] = value.reshape(2, rows, tile)
            own_part[d, :, cols] = pair[parity]
            to_sib[d, :, cols] = pair[1 - parity].astype(BF)

        near[d] = push(to_sib.at[d], sib.at[d], ss_s.at[d], rs_s.at[d], shard=sibling)
        near[d].start()

    def chip_sum(d):
        near[d].wait()
        to_chip[d - 1] = (own_part[d] + sib[d].astype(F32)).astype(BF)
        far[d] = push(to_chip.at[d - 1], got.at[d - 1], ss_c.at[d - 1], rs_c.at[d - 1], shard=mates[d - 1])
        far[d].start()

    gain_sends = []

    def last_sum():
        near[0].wait()
        grad = own_part[0] + sib[0].astype(F32)
        for d in range(1, chips):
            far[d].wait()
            grad = grad + got[d - 1].astype(F32)
        x = tokens[...].astype(F32)
        scale = lax.rsqrt(jnp.mean(x * x, axis=-1, keepdims=True) + epsilon)
        unit = x * scale
        scaled = grad * gain[...]
        rows_out[...] = scale * (scaled - unit * jnp.mean(scaled * unit, axis=-1, keepdims=True))
        gains_own[...] = gains[...]
        gains_own[0:1] = jnp.sum(grad * unit, axis=0, keepdims=True)
        mine = pltpu.make_async_copy(gains_own, gains_in.at[s], local.at[0])
        mine.start()
        gain_sends.append(mine)
        for i, peer in enumerate(others):
            item = push(gains_own, gains_in.at[s], ss_g.at[i], rs_g.at[i], shard=peer)
            item.start()
            gain_sends.append(item)

    def small_plane():
        for item in small + gain_sends:
            item.wait()
        gains_mid[...] = gains_in[0]
        for i in range(1, n_shard):
            gains_mid[...] += gains_in[i]
        router_mid[...] = router[s].astype(F32)
        for i in range(n_shard - 1):
            router_mid[...] += router_in[i].astype(F32)
        for i, layer in enumerate(layers):
            push(gains_mid, gains_far.at[c], ss_h.at[i], rs_h.at[i], ctx=layer).start()
            push(router_mid, router_far.at[c], ss_t.at[i], rs_t.at[i], ctx=layer).start()
        pltpu.make_async_copy(gains_mid, gains_far.at[c], local.at[1]).start()
        pltpu.make_async_copy(router_mid, router_far.at[c], local.at[2]).start()

    def small_all():
        pltpu.make_async_copy(gains_mid, gains_far.at[c], local.at[1]).wait()
        pltpu.make_async_copy(router_mid, router_far.at[c], local.at[2]).wait()
        for i, layer in enumerate(layers):
            push(gains_mid, gains_far.at[c], ss_h.at[i], rs_h.at[i], ctx=layer).wait()
            push(router_mid, router_far.at[c], ss_t.at[i], rs_t.at[i], ctx=layer).wait()
        gains_out[...] = gains_far[0]
        router_out[...] = router_far[0]
        for i in range(1, n_ctx):
            gains_out[...] += gains_far[i]
            router_out[...] += router_far[i]

    lag, ahead = 2, 6
    for which, j in steps[:ahead]:
        which.outermost(j)
    for d in list(range(1, chips)) + [0]:
        product(d)
    side = [functools.partial(chip_sum, d) for d in range(1, chips)] + [last_sum, small_plane]
    for n in range(len(steps) + lag):
        if n + ahead < len(steps):
            steps[n + ahead][0].outermost(steps[n + ahead][1])
        if n < len(steps):
            steps[n][0].first_half(steps[n][1])
        if n >= lag:
            steps[n - lag][0].second_half(steps[n - lag][1])
        if n >= 2 and side:
            side.pop(0)()
    for job in side:
        job()
    small_all()
    for which, j in steps:
        which.drain(j)


def finish(n_ctx, n_shard, q_cols, weights, wide, router, gains, left, right, tokens, gain, ident):
    n, rows, cols = weights.shape
    router_shape = router.shape[1:]
    count, width = tokens.shape
    chips = n // 2
    tile = 512
    wides = wide.shape[0]
    return call(
        functools.partial(finish_body, n_ctx, n, q_cols, tile),
        [
            jax.ShapeDtypeStruct((rows, n * q_cols), BF), jax.ShapeDtypeStruct((n, rows, 128), BF),
            jax.ShapeDtypeStruct(wide.shape, BF),
            jax.ShapeDtypeStruct(router_shape, F32), jax.ShapeDtypeStruct(gains.shape, F32),
            jax.ShapeDtypeStruct((count, width), F32),
        ],
        [VMEM] * 8,
        [
            pltpu.VMEM((2,) + wide.shape, BF), pltpu.VMEM(wide.shape, BF), pltpu.VMEM(wide.shape, BF),
            DMA((wides,)), DMA((2, wides)), DMA((wides,)), DMA((wides,)),
            pltpu.VMEM((n, rows, cols), BF), pltpu.VMEM((2, n, rows, cols), BF),
            pltpu.VMEM((n, rows, cols), BF), pltpu.VMEM((n, rows, cols), BF),
            pltpu.VMEM((n - 1,) + router_shape, BF), pltpu.VMEM(router_shape, F32),
            pltpu.VMEM((n_ctx,) + router_shape, F32),
            pltpu.VMEM(gains.shape, F32), pltpu.VMEM((n,) + gains.shape, F32),
            pltpu.VMEM(gains.shape, F32), pltpu.VMEM((n_ctx,) + gains.shape, F32),
            pltpu.VMEM((2, count, tile), F32), pltpu.VMEM((chips, count, width), F32),
            pltpu.VMEM((chips, count, width), BF), pltpu.VMEM((chips, count, width), BF),
            pltpu.VMEM((chips - 1, count, width), BF), pltpu.VMEM((chips - 1, count, width), BF),
            DMA((3,)), DMA((n - 1,)), DMA((n - 1,)), DMA((n,)), DMA((2, n)), DMA((n,)),
            DMA((n,)), DMA((n,)), DMA((n - 1,)), DMA((n - 1,)), DMA((n - 1,)), DMA((n - 1,)),
            DMA((n_ctx - 1,)), DMA((n_ctx - 1,)), DMA((n_ctx - 1,)), DMA((n_ctx - 1,)),
            DMA((chips,)), DMA((chips,)), DMA((chips - 1,)), DMA((chips - 1,)),
        ],
        ident, (weights, wide, router, gains, left, right, tokens, gain), mib=60,
        out_specs=[ANY, ANY, ANY, VMEM, VMEM, VMEM],
    )


def dispatch_body(n_ctx, n_shard, group, tile, rows, picks, recv, zrows, ready, local,
                  ss_z, rs_z, ss_x, rs_x):
    c, s, parity, sibling, others, layers = here(n_ctx, n_shard)
    greet(others, layers)
    count, width = rows.shape
    groups = n_ctx // group
    own = pltpu.make_async_copy(rows, zrows.at[c], local.at[0])
    own.start()
    fan = Fan(n_ctx, c, lambda d: zrows.at[flip_bits(c, d)], ss_z, rs_z, True)
    fan.send(0, rows)
    waits = []
    seen = set()
    for k in range(groups):
        at = flip_bits(lax.div(c, group), k)
        if k == 0:
            own.wait()
        for d in fan.order():
            if d < (k + 1) * group and d not in seen:
                fan.arrival(d)
                seen.add(d)
        first = pl.multiple_of(at * group, group)

        @pl.loop(0, width // tile)
        def _(j):
            cols = pl.ds(pl.multiple_of(j * tile, tile), tile)
            block = zrows[pl.ds(first, group), :, cols].reshape(group * count, tile)
            value = jnp.dot(picks[at], block, preferred_element_type=F32).astype(BF)
            ready[k, :, :, cols] = value.reshape(n_shard, -1, tile)

        for i, peer in enumerate(others):
            item = push(ready.at[k, peer], recv.at[s, at], ss_x.at[k, i], rs_x.at[k, i], shard=peer)
            item.start()
            waits.append(item)
        item = pltpu.make_async_copy(ready.at[k, s], recv.at[s, at], local.at[k + 1])
        item.start()
        waits.append(item)
    fan.drain()
    for item in waits:
        item.wait()


def dispatch_rows(n_ctx, n_shard, group, rows, picks, ident):
    groups, slots = picks.shape[0], picks.shape[1] // n_shard
    count, width = rows.shape
    return call(
        functools.partial(dispatch_body, n_ctx, n_shard, group, 512),
        [jax.ShapeDtypeStruct((n_shard, groups, slots, width), BF)],
        [VMEM, VMEM],
        [
            pltpu.VMEM((n_ctx, count, width), BF), pltpu.VMEM((groups, n_shard, slots, width), BF),
            DMA((groups + 1,)), DMA((n_ctx,)), DMA((n_ctx,)),
            DMA((groups, n_shard - 1)), DMA((groups, n_shard - 1)),
        ],
        ident, (rows, picks), mib=56,
    )[0]


def combine_body(n_ctx, n_shard, group, tile, rows, mix, picks, out, mix_out, land, value, zsend, zrecv,
                 msend, mrecv, mix_kept, local, ss_x, rs_x, ss_z, rs_z, ss_m, rs_m):
    c, s, parity, sibling, others, layers = here(n_ctx, n_shard)
    greet(others, layers)
    count, width = out.shape
    mix_width = mix_out.shape[1]
    groups = n_ctx // group
    near = {}
    for k in reversed(range(groups)):
        at = flip_bits(lax.div(c, group), k)
        near[k] = []
        for i, peer in enumerate(others):
            item = push(rows.at[peer, at], land.at[k, s], ss_x.at[k, i], rs_x.at[k, i], shard=peer)
            item.start()
            near[k].append(item)
        item = pltpu.make_async_copy(rows.at[s, at], land.at[k, s], local.at[k])
        item.start()
        near[k].append(item)

    def local_sums(k, block_of, step, last):
        at = flip_bits(lax.div(c, group), k)

        @pl.loop(0, last // step)
        def _(j):
            cols = pl.ds(pl.multiple_of(j * step, step), step)
            value[:, cols] = jnp.dot(picks[at], block_of(at, cols), preferred_element_type=F32)

    def part(d, last):
        place = lax.rem(flip_bits(c, d), group)
        return value[pl.ds(pl.multiple_of(place * count, count), count), pl.ds(0, last)]

    def in_group(k):
        return sorted(range(k * group, (k + 1) * group), key=lambda d: (lowest(d) or n_ctx, d))

    mix_fold = Fold(c, msend, mrecv, ss_m, rs_m)
    for k in reversed(range(groups)):
        local_sums(k, lambda at, cols: mix[:, at, :, cols].reshape(picks.shape[2], -1), 512, mix_width)
        for d in in_group(k):
            if lowest(d) == 1:
                mix_fold.give(d, part(d, mix_width))
            else:
                mix_kept[d // 2] = part(d, mix_width)
    fold = Fold(c, zsend, zrecv, ss_z, rs_z)
    for k in reversed(range(groups)):
        for item in near[k]:
            item.wait()
        local_sums(k, lambda at, cols: land[k, :, :, cols].reshape(picks.shape[2], -1), tile, width)
        for d in in_group(k):
            if lowest(d) == 1:
                fold.give(d, part(d, width))
        for d in in_group(k):
            if lowest(d) != 1:
                if d:
                    mix_fold.give(d, mix_fold.take(d, mix_kept[d // 2]))
                    fold.give(d, fold.take(d, part(d, width)))
                else:
                    mix_out[...] = mix_fold.take(0, mix_kept[0])
                    out[...] = fold.take(0, part(0, width))
    mix_fold.drain()
    fold.drain()


def combine_rows(n_ctx, n_shard, group, rows, mix, picks, ident):
    groups, slots, width = rows.shape[1:]
    mix_width = mix.shape[3]
    count = picks.shape[1] // group
    tile = 128 * max(t for t in range(1, 9) if (width // 128) % t == 0)
    return call(
        functools.partial(combine_body, n_ctx, n_shard, group, tile),
        [jax.ShapeDtypeStruct((count, width), F32), jax.ShapeDtypeStruct((count, mix_width), F32)],
        [VMEM, VMEM, VMEM],
        [
            pltpu.VMEM((groups, n_shard, slots, width), BF), pltpu.VMEM((group * count, width), F32),
            pltpu.VMEM((n_ctx - 1, count, width), BF), pltpu.VMEM((n_ctx - 1, count, width), BF),
            pltpu.VMEM((n_ctx - 1, count, mix_width), BF), pltpu.VMEM((n_ctx - 1, count, mix_width), BF),
            pltpu.VMEM((n_ctx // 2, count, mix_width), F32), DMA((groups,)), DMA((groups, n_shard - 1)), DMA((groups, n_shard - 1)),
            DMA((n_ctx,)), DMA((n_ctx,)), DMA((n_ctx,)), DMA((n_ctx,)),
        ],
        ident, (rows, mix, picks), mib=60, out_specs=[VMEM, VMEM],
    )


QUERY_HEADS = 32
KEY_VALUE_HEADS = 4
HEAD_DIM = 128

epsilon = 1e-06
rope_base = 1000000.0


def rms_scale(hidden, gain):
    return hidden * lax.rsqrt(jnp.mean(hidden * hidden, axis=-1, keepdims=True) + epsilon) * gain


def rotate(headwise, places):
    half_size = headwise.shape[-1] // 2
    frequency = rope_base ** (-jnp.arange(half_size, dtype=F32) * 2.0 / headwise.shape[-1])
    angles = places.astype(F32)[:, None] * frequency[None, :]
    cosine = jnp.cos(angles)[:, None, :]
    sine = jnp.sin(angles)[:, None, :]
    former = headwise[..., :half_size]
    latter = headwise[..., half_size:]
    return jnp.concatenate(
        [former * cosine - latter * sine, latter * cosine + former * sine], axis=-1
    )


def place_of(row_ids, order, block_rows):
    block_ids = jnp.arange(order.shape[0], dtype=jnp.int32)
    owner_block = row_ids // block_rows
    picked_block = jnp.sum(
        jnp.where(owner_block[:, None] == block_ids[None, :], order[None, :], 0), axis=1
    )
    return picked_block * block_rows + row_ids % block_rows


def dot(left, right):
    return jnp.dot(left, right, preferred_element_type=F32)


def contract_rows(left, right):
    return lax.dot_general(left, right, (((0,), (0,)), ((), ())), preferred_element_type=F32)


def contract_cols(left, right):
    return lax.dot_general(left, right, (((1,), (1,)), ((), ())), preferred_element_type=F32)


def exchange_shard(x):
    return lax.all_to_all(x, "shard", split_axis=0, concat_axis=0, tiled=True)


def gather_ctx(x):
    return lax.all_gather(x, "ctx", axis=0, tiled=False)


def shards(
    tokens,
    cotangent,
    block_order,
    routes,
    attn_gain,
    w_query,
    key_weight,
    value_weight,
    query_gain,
    key_gain,
    w_out,
    ffn_gain,
    w_router,
    w_gate,
    w_up,
    w_down,
):
    rows = tokens.shape[1]
    width = tokens.shape[2]
    ctx_count = lax.axis_size("ctx")
    shard_count = lax.axis_size("shard")
    my_ctx = lax.axis_index("ctx")
    my_shard = lax.axis_index("shard")
    experts = ctx_count * shard_count
    block_rows = rows // 2
    heads = QUERY_HEADS // shard_count
    head_cols = heads * HEAD_DIM
    sharers = shard_count // KEY_VALUE_HEADS
    score_scale = HEAD_DIM ** (-0.5)
    top_count = routes.shape[2]
    capacity = rows * top_count // experts + max(rows * top_count // (4 * experts), 1)
    sequence = rows * ctx_count
    plane = rows * shard_count
    wrows = width // shard_count

    inputs = tokens[0].astype(F32)
    upstream_b = cotangent[0]
    upstream = upstream_b.astype(F32)

    kv_kind = [key_weight, value_weight]
    extra = [
        kv_kind[(s % sharers) % 2][:, (s // sharers) * HEAD_DIM : (s // sharers + 1) * HEAD_DIM]
        for s in range(shard_count)
    ]
    send_w = jnp.stack(
        [
            jnp.concatenate([w_query[:, s * head_cols : (s + 1) * head_cols], extra[s]], axis=1)
            for s in range(shard_count)
        ]
    )
    normed = rms_scale(inputs, attn_gain)
    normed_b = normed.astype(BF)
    normed_all, w_mine, routes_all, router_all, upstream_z = start(
        ctx_count, shard_count, normed_b, send_w, routes[0].T, w_router.T, upstream_b
    )
    normed_all = normed_all.reshape(plane, width)
    w_mine = w_mine.reshape(width, head_cols + HEAD_DIM)
    routes_all = jnp.swapaxes(routes_all, 2, 3)
    router_all = jnp.swapaxes(router_all, 1, 2).reshape(width, experts)

    named = jnp.sum(
        (routes_all[..., None] == jnp.arange(experts, dtype=jnp.int32)).astype(BF), axis=3
    )
    earlier = (
        jnp.arange(rows, dtype=jnp.int32)[:, None] > jnp.arange(rows, dtype=jnp.int32)[None, :]
    ).astype(BF)
    slots = jnp.arange(capacity, dtype=F32)

    def places_in(mask):
        rank = jnp.einsum("tu,...un->...tn", earlier, mask, preferred_element_type=F32)
        pick = jnp.where(mask > 0, rank, -1.0)
        return (jnp.swapaxes(pick, -1, -2)[..., None, :] == slots[:, None]).astype(BF)

    my_rows = lax.dynamic_index_in_dim(named, my_shard, 1, keepdims=False)
    my_rows = lax.dynamic_slice_in_dim(my_rows, my_ctx * shard_count, shard_count, 2)
    pick_send = places_in(my_rows)
    mine = lax.dynamic_slice_in_dim(named, my_ctx * shard_count + my_shard, 1, 3)
    pick_here = places_in(mine)[:, :, 0]
    chosen_here = jnp.einsum(
        "cbqt,cbte->bcqe", pick_here, named, preferred_element_type=F32
    ).reshape(-1, experts)

    group = 1
    while group * capacity % 16:
        group *= 2
    groups = ctx_count // group
    by_group = jnp.swapaxes(pick_send.reshape(groups, group, shard_count, capacity, rows), 1, 2)
    same = jnp.eye(group, dtype=BF)
    picks = (by_group[:, :, :, :, None, :] * same[None, None, :, None, :, None]).reshape(
        groups, shard_count * group * capacity, group * rows
    )
    picks_t = jnp.swapaxes(picks, 1, 2)
    slot_rows = shard_count * ctx_count * capacity
    block_shape = (shard_count, groups, group * capacity)

    sent_up = jnp.einsum(
        "nkr,nrd->nkd", picks, upstream_z.reshape(groups, group * rows, width), preferred_element_type=F32
    ).astype(BF)
    sent_up = jnp.swapaxes(sent_up.reshape((groups, shard_count, group * capacity, width)), 0, 1)
    upstream_rows = exchange_shard(sent_up).reshape(slot_rows, width)

    qkv = dot(normed_all, w_mine)
    query_pre = qkv[:, :head_cols].reshape(shard_count, rows, heads, HEAD_DIM)
    row_ids = my_ctx * rows + jnp.arange(rows, dtype=jnp.int32)
    q_places = place_of(row_ids, block_order, block_rows)
    k_places = place_of(jnp.arange(sequence, dtype=jnp.int32), block_order, block_rows)
    sees = k_places[None, :] <= q_places[:, None]

    def prep(pre, gain):
        shape = pre.shape
        flat = pre.reshape(-1, rows, shape[-2], HEAD_DIM)
        return jax.vmap(lambda v: rotate(rms_scale(v, gain), q_places))(flat).reshape(shape)

    queries = prep(query_pre, query_gain).astype(BF)
    my_place = lax.rem(my_shard, sharers)
    is_key = lax.rem(my_place, 2) == 0
    part_count = sharers // 2
    kv_pre = qkv[:, head_cols:]
    key_roped = prep(kv_pre.reshape(shard_count, rows, 1, HEAD_DIM), key_gain).reshape(plane, HEAD_DIM)
    kv_b = jnp.where(is_key, key_roped, kv_pre).astype(BF)
    kv_all = key_exchange(ctx_count, shard_count, kv_b.reshape(shard_count, rows, HEAD_DIM), 1)
    kv_all = kv_all.reshape(2, shard_count, sequence, HEAD_DIM)
    keys, values = kv_all[0], kv_all[1]

    scores = (
        jnp.einsum("sthd,spd->shtp", queries, keys, preferred_element_type=F32) * score_scale
    )
    scores = jnp.where(sees, scores, -1e30)
    top = jnp.max(scores, axis=-1, keepdims=True)
    raised = jnp.exp(scores - top)
    total = jnp.sum(raised, axis=-1, keepdims=True)
    probs = raised / total
    probs_b = probs.astype(BF)
    attn_f32 = jnp.einsum("shtp,spd->sthd", probs_b, values, preferred_element_type=F32)
    attn_b = attn_f32.astype(BF)
    attn_rows = attn_b.reshape(plane, head_cols)
    middle = inputs + product_scatter(shard_count, attn_rows, w_out, False, 2)

    normed_two = rms_scale(middle, ffn_gain)
    second_b = normed_two.astype(BF)
    logits = dot(second_b, router_all)
    chosen = jnp.sum(
        (routes[0][:, :, None] == jnp.arange(experts, dtype=jnp.int32)).astype(F32), axis=1
    )

    def gates_of(log, mask):
        masked = jnp.where(mask > 0, log, -1e30)
        peak = jnp.max(masked, axis=-1, keepdims=True)
        risen = jnp.exp(masked - peak) * mask
        return risen / jnp.maximum(jnp.sum(risen, axis=-1, keepdims=True), 1e-30)

    gates = gates_of(logits, chosen)

    received = dispatch_rows(ctx_count, shard_count, group, second_b, picks, 3).reshape(slot_rows, width)
    my_expert = my_ctx * shard_count + my_shard
    slot_gates = lax.dynamic_slice_in_dim(
        gates_of(dot(received, router_all), chosen_here), my_expert, 1, 1
    )
    gate_pre = dot(received, w_gate[0])
    up_pre = dot(received, w_up[0])
    activated = jax.nn.silu(gate_pre)
    hidden_b = (activated * up_pre).astype(BF)
    expert_out = dot(hidden_b, w_down[0]).astype(BF)
    expert_out_f = expert_out.astype(F32)
    mix_sent = (slot_gates * expert_out_f).astype(BF)
    mix_sent, upstream_rows, expert_out = lax.optimization_barrier((mix_sent, upstream_rows, expert_out))
    expert_out_f = expert_out.astype(F32)
    mix_back = exchange_shard(mix_sent.reshape(block_shape + (width,)))
    upstream_rows = upstream_rows.astype(F32)
    slot_dot = jnp.sum(expert_out_f * upstream_rows, axis=1, keepdims=True)
    grad_expert = (slot_gates * upstream_rows).astype(BF)
    grad_w_down = contract_rows(hidden_b, grad_expert)
    grad_hidden = contract_cols(grad_expert, w_down[0])
    sigmoid_g = jax.nn.sigmoid(gate_pre)
    silu_slope = sigmoid_g * (1.0 + gate_pre * (1.0 - sigmoid_g))
    grad_gate_pre = (grad_hidden * up_pre * silu_slope).astype(BF)
    grad_up_pre = (grad_hidden * activated).astype(BF)
    grad_w_gate = contract_rows(received, grad_gate_pre)
    grad_w_up = contract_rows(received, grad_up_pre)
    grad_received = contract_cols(grad_gate_pre, w_gate[0]) + contract_cols(grad_up_pre, w_up[0])

    tail_cols = -(-2 * experts // 128) * 128
    coarse = slot_dot.astype(BF).astype(F32)
    fine = slot_dot - coarse
    column = jnp.arange(tail_cols, dtype=jnp.int32)[None, :]
    tail = jnp.where(column == my_expert, coarse, 0.0) + jnp.where(
        column == experts + my_expert, fine, 0.0
    )
    back_rows = jnp.concatenate([grad_received, tail], axis=1).astype(BF)
    back, mixture = combine_rows(
        ctx_count, shard_count, group, back_rows.reshape(block_shape + (width + tail_cols,)), mix_back,
        picks_t, 4,
    )
    mixed = (middle + mixture).astype(BF)
    grad_second = back[:, :width]
    grad_gates = back[:, width : width + experts] + back[:, width + experts : width + 2 * experts]
    grad_logits_b = (
        gates * (grad_gates - jnp.sum(gates * grad_gates, axis=-1, keepdims=True))
    ).astype(BF)
    router_part = contract_rows(grad_logits_b, second_b).astype(BF)
    grad_second = grad_second + contract_cols(grad_logits_b, router_all)
    unused, norm_two_back = jax.vjp(rms_scale, middle, ffn_gain)
    grad_middle_part, grad_ffn_gain = norm_two_back(grad_second)
    grad_middle = upstream + grad_middle_part
    grad_proj_b = grad_middle.astype(BF)

    grad_proj_all = spread(shard_count, grad_proj_b, 5).reshape(plane, width)
    out_part = contract_rows(attn_rows, grad_proj_all).astype(BF)
    out_part, grad_proj_all = lax.optimization_barrier((out_part, grad_proj_all))
    grad_attn = contract_cols(grad_proj_all, w_out).astype(BF)
    grad_heads = grad_attn.reshape(shard_count, rows, heads, HEAD_DIM)
    delta = jnp.transpose(jnp.sum(grad_heads.astype(F32) * attn_f32, axis=-1), (0, 2, 1))[..., None]
    grad_probs = jnp.einsum("sthd,spd->shtp", grad_heads, values, preferred_element_type=F32)
    grad_scores = (probs * (grad_probs - delta)).astype(BF)
    grad_query = score_scale * jnp.einsum(
        "shtp,spd->sthd", grad_scores, keys, preferred_element_type=F32
    )
    grad_keys = score_scale * jnp.einsum(
        "shtp,sthd->spd", grad_scores, queries, preferred_element_type=F32
    )
    grad_values = jnp.einsum("shtp,sthd->spd", probs_b, grad_heads, preferred_element_type=F32)
    grad_kv = jnp.stack([grad_keys, grad_values]).astype(BF)
    grad_kv = key_back(
        ctx_count, shard_count, grad_kv.reshape(2, shard_count, ctx_count, rows, HEAD_DIM), 6
    )
    unused, query_back = jax.vjp(prep, query_pre, query_gain)
    grad_query_pre, grad_query_gain = query_back(grad_query)
    kv_shape = (shard_count, rows, 1, HEAD_DIM)
    unused, key_prep_back = jax.vjp(prep, kv_pre.reshape(kv_shape), key_gain)
    grad_key_pre, grad_key_gain = key_prep_back(grad_kv.reshape(kv_shape))
    grad_key_gain = jnp.where(is_key, grad_key_gain, 0.0)
    grad_kv_full = jnp.where(
        is_key, grad_key_pre.reshape(plane, HEAD_DIM), grad_kv.reshape(plane, HEAD_DIM)
    ).astype(BF)
    grad_pre = jnp.concatenate(
        [grad_query_pre.reshape(plane, head_cols).astype(BF), grad_kv_full], axis=1
    )
    gains = jnp.concatenate(
        [
            jnp.zeros((1, width), F32),
            grad_ffn_gain[None],
            jnp.pad(
                jnp.concatenate([grad_query_gain, grad_key_gain])[None],
                ((0, 6 - 1), (0, width - 2 * HEAD_DIM)),
            ),
        ]
    )
    grad_w = contract_rows(normed_all, grad_pre).astype(BF).reshape(shard_count, wrows, -1)
    router_parts = jnp.swapaxes(router_part.reshape(experts, shard_count, wrows), 0, 1)
    q_sum, kv_sum, out_sum, router_sum, gains, grad_input_part = finish(
        ctx_count, shard_count, head_cols, grad_w, out_part.reshape(8, -1, width), router_parts, gains, grad_pre, w_mine,
        tokens[0], attn_gain[None], 8,
    )
    grad_tokens = grad_middle + grad_input_part
    grad_attn_gain, grad_ffn_gain = gains[0], gains[1]
    grad_query_gain, grad_key_gain = gains[2, :HEAD_DIM], gains[2, HEAD_DIM : 2 * HEAD_DIM]
    grad_w_query = q_sum.astype(F32)
    grad_w_out = out_sum.reshape(head_cols, width).astype(F32)
    kinds = kv_sum.astype(F32).reshape(KEY_VALUE_HEADS, part_count, 2, wrows, HEAD_DIM)
    kinds = jnp.transpose(jnp.sum(kinds, axis=1), (1, 2, 0, 3)).reshape(2, wrows, -1)
    grad_w_key, grad_w_value = kinds[0], kinds[1]
    grad_w_router = router_sum.T
    return (
        mixed[None],
        grad_tokens[None],
        grad_attn_gain,
        grad_w_query,
        grad_w_key,
        grad_w_value,
        grad_query_gain,
        grad_key_gain,
        grad_w_out,
        grad_ffn_gain,
        grad_w_router,
        grad_w_gate[None],
        grad_w_up[None],
        grad_w_down[None],
    )


def solution(mesh):
    rows = P("shard", "ctx", None)
    matrix = P("shard", None)
    expert = P(("ctx", "shard"), None, None)
    return jax.shard_map(
        shards,
        mesh=mesh,
        in_specs=(
            rows, rows, P(), rows, P(), matrix, matrix, matrix, P(), P(), matrix, P(), matrix,
            expert, expert, expert,
        ),
        out_specs=(
            rows, rows, P(), matrix, matrix, matrix, P(), P(), matrix, P(), matrix,
            expert, expert, expert,
        ),
        check_vma=False,
    )
```

```python
import functools

import jax
import jax.numpy as jnp
from jax import lax
from jax.experimental import pallas as pl
from jax.experimental.pallas import tpu as pltpu
from jax.sharding import PartitionSpec as P

BF = jnp.bfloat16
F32 = jnp.float32
MESH = pl.DeviceIdType.MESH
ANY = pl.BlockSpec(memory_space=pl.ANY)
VMEM = pl.BlockSpec(memory_space=pltpu.VMEM)
DMA = pltpu.SemaphoreType.DMA
epsilon = 1e-06
rope_base = 1000000.0
QUERY_HEADS = 32
KEY_VALUE_HEADS = 4
HEAD_DIM = 128


def push(src, dst, send_sem, recv_sem, **where):
    return pltpu.make_async_remote_copy(
        src_ref=src, dst_ref=dst, send_sem=send_sem, recv_sem=recv_sem,
        device_id=where, device_id_type=MESH,
    )


def greet(shard_peers, ctx_peers):
    barrier = pltpu.get_barrier_semaphore()
    for peer in shard_peers:
        pl.semaphore_signal(barrier, inc=1, device_id={"shard": peer}, device_id_type=MESH)
    for peer in ctx_peers:
        pl.semaphore_signal(barrier, inc=1, device_id={"ctx": peer}, device_id_type=MESH)
    pl.semaphore_wait(barrier, len(shard_peers) + len(ctx_peers))


def here(ctx_count, shard_count):
    c, s = lax.axis_index("ctx"), lax.axis_index("shard")
    parity = lax.rem(s, 2)
    sibling = s + 1 - 2 * parity
    others = [lax.rem(s + d, shard_count) for d in range(1, shard_count)]
    layers = [lax.rem(c + d, ctx_count) for d in range(1, ctx_count)]
    return c, s, parity, sibling, others, layers


def flip_bits(index, mask):
    result = index
    bit = 1
    while bit <= mask:
        if mask & bit:
            result = result + bit - 2 * bit * lax.rem(lax.div(index, bit), 2)
        bit *= 2
    return result


def lowest(d):
    return d & -d


class Fan:
    def __init__(self, n_ctx, c, block, ss, rs, near_first):
        self.n_ctx, self.c, self.block, self.ss, self.rs, self.near_first = n_ctx, c, block, ss, rs, near_first
        self.items = {}

    def send(self, d, src):
        bits = [b for b in (1, 2, 4, 8, 16) if b < (lowest(d) or self.n_ctx)]
        for b in bits if self.near_first else reversed(bits):
            item = push(src, self.block(d), self.ss.at[d | b], self.rs.at[d | b], ctx=flip_bits(self.c, b))
            item.start()
            self.items[d | b] = item

    def arrival(self, d):
        self.items[d].wait_recv()
        if lowest(d) > 1:
            self.send(d, self.block(d))

    def order(self):
        return sorted(range(1, self.n_ctx), key=lambda d: (bin(d).count("1"), d if self.near_first else -d))

    def drain(self):
        for d in range(1, self.n_ctx):
            self.items[d].wait_send()


class Fold:
    def __init__(self, c, sent, received, ss, rs):
        self.c, self.sent, self.received, self.ss, self.rs = c, sent, received, ss, rs
        self.items = {}

    def take(self, d, value):
        for b in (1, 2, 4, 8, 16):
            if b < lowest(d) or (d == 0 and b in self.items):
                self.items[d | b].wait_recv()
                value = value + self.received[(d | b) - 1].astype(F32)
        return value

    def give(self, d, value):
        self.sent[d - 1] = value.astype(BF)
        item = push(self.sent.at[d - 1], self.received.at[d - 1], self.ss.at[d], self.rs.at[d],
                    ctx=flip_bits(self.c, lowest(d)))
        item.start()
        self.items[d] = item

    def drain(self):
        for item in self.items.values():
            item.wait_send()


def call(body, outs, in_specs, scratch, ident, args, mib=48, out_specs=None):
    return pl.pallas_call(
        body,
        out_shape=outs,
        in_specs=in_specs,
        out_specs=out_specs if out_specs is not None else [ANY] * len(outs),
        scratch_shapes=scratch,
        compiler_params=pltpu.CompilerParams(
            collective_id=ident, has_side_effects=True, vmem_limit_bytes=mib * 2**20
        ),
    )(*args)


def slot_table(code, slots):
    places = lax.broadcasted_iota(jnp.int32, (slots, code.shape[1]), 0).astype(F32)
    return jnp.concatenate(
        [(places == code[e : e + 1, :]).astype(BF) for e in range(code.shape[0])], axis=0
    )


def turn(value, cosine, sine):
    return value * cosine + pltpu.roll(value, HEAD_DIM // 2, 1) * sine


def unit_rows(value):
    scale = lax.rsqrt(jnp.mean(value * value, axis=-1, keepdims=True) + epsilon)
    return value * scale, scale


def front_body(n_ctx, n_shard, group, capacity, heads, kv_heads, tile,
               tokens, gain, w_query, key_w, value_w, routes, router, cot, cosine, sine, bias, q_gain, k_gain, w_out,
               rows_out, w_all_out, router_all, code, cot_rows, qpre_out, kvpre, q_out, kv_out, attn_out, mid,
               own_rows, rows_all, w_all, zroutes, zcot, ready, qpre, q, kv, attn,
               own_part, pair, to_sib, sib, to_chip, got,
               local, ss_row, rs_row, ss_fwd, rs_fwd, ss_w, rs_w, ss_k, rs_k, ss_rt, rs_rt, ss_ro, rs_ro, ss_z, rs_z,
               ss_x, rs_x, ss_kz, rs_kz, ss_kf, rs_kf, ss_s, rs_s, ss_c, rs_c, out_sem):
    c, s, parity, sibling, others, layers = here(n_ctx, n_shard)
    chips = n_shard // 2
    chip = lax.div(s, 2)
    count, width = tokens.shape
    wr = w_query.shape[0]
    cols = heads * HEAD_DIM
    sharers = n_shard // kv_heads
    groups = n_ctx // group
    slots = group * capacity
    keys = n_ctx * count
    mates = [lax.rem(s + 2 * d, n_shard) for d in range(1, chips)]
    x = tokens[...].astype(F32)
    unit, unused = unit_rows(x)
    own_rows[...] = (unit * gain[...]).astype(BF)
    greet(others, layers)

    route_fan = Fan(n_ctx, c, lambda d: zroutes.at[flip_bits(c, d)], ss_ro, rs_ro, False)
    route_fan.send(0, routes)
    cot_fan = Fan(n_ctx, c, lambda d: zcot.at[flip_bits(c, d)], ss_z, rs_z, False)
    cot_fan.send(0, cot)
    first, waits = [], []
    for d in range(1, chips):
        item = push(own_rows, rows_all.at[s], ss_row.at[d], rs_row.at[d], shard=mates[d - 1])
        item.start()
        first.append(item)
    item = push(own_rows, rows_all.at[s], ss_fwd.at[0], rs_fwd.at[0], shard=sibling)
    item.start()
    waits.append(item)
    w_waits = []
    for i, peer in enumerate(others):
        from_q = w_query.at[:, pl.ds(pl.multiple_of(peer * cols, cols), cols)]
        item = push(from_q, w_all.at[s, :, pl.ds(0, cols)], ss_w.at[i], rs_w.at[i], shard=peer)
        item.start()
        w_waits.append(item)
        head = pl.ds(pl.multiple_of(lax.div(peer, sharers) * HEAD_DIM, HEAD_DIM), HEAD_DIM)
        for kind, ref in enumerate((key_w, value_w)):
            item = push(ref.at[:, head], w_all.at[s, :, pl.ds(cols, HEAD_DIM)], ss_k.at[i], rs_k.at[i], shard=peer)

            @pl.when(lax.rem(peer, 2) == kind)
            def _(item=item):
                item.start()

        w_waits.append(item)
        item = push(router, router_all.at[:, pl.ds(pl.multiple_of(s * wr, wr), wr)], ss_rt.at[i], rs_rt.at[i], shard=peer)
        item.start()
        waits.append(item)
    copies = [
        pltpu.make_async_copy(own_rows, rows_all.at[s], local.at[0]),
        pltpu.make_async_copy(w_query.at[:, pl.ds(pl.multiple_of(s * cols, cols), cols)],
                              w_all.at[s, :, pl.ds(0, cols)], local.at[1]),
        pltpu.make_async_copy(routes, zroutes.at[c], local.at[2]),
        pltpu.make_async_copy(router, router_all.at[:, pl.ds(pl.multiple_of(s * wr, wr), wr)], local.at[3]),
        pltpu.make_async_copy(cot, zcot.at[c], local.at[4]),
    ]
    for item in copies:
        item.start()
    head = pl.ds(pl.multiple_of(lax.div(s, sharers) * HEAD_DIM, HEAD_DIM), HEAD_DIM)
    for kind, ref in enumerate((key_w, value_w)):
        own_head = pltpu.make_async_copy(ref.at[:, head], w_all.at[s, :, pl.ds(cols, HEAD_DIM)], local.at[5])

        @pl.when(parity == kind)
        def _(own_head=own_head):
            own_head.start()

    copies[2].wait()
    for d in route_fan.order():
        route_fan.arrival(d)
    before = (
        lax.broadcasted_iota(jnp.int32, (count, count), 0) < lax.broadcasted_iota(jnp.int32, (count, count), 1)
    ).astype(BF)
    for layer in range(n_ctx):
        named = zroutes[layer]
        mask = jnp.concatenate(
            [jnp.max((named == c * n_shard + e).astype(F32), axis=0, keepdims=True) for e in range(n_shard)], axis=0
        )
        rank = jnp.dot(mask.astype(BF), before, preferred_element_type=F32)
        at = layer % group
        code[layer // group, :, at * count : (at + 1) * count] = jnp.where(
            mask > 0, rank + float(at * capacity), -1.0
        )

    for d in range(1, chips):
        first[d - 1].wait()
        origin = lax.rem(s + n_shard - 2 * d, n_shard)
        item = push(rows_all.at[origin], rows_all.at[origin], ss_fwd.at[d], rs_fwd.at[d], shard=sibling)
        item.start()
        waits.append(item)
    for d in cot_fan.order():
        cot_fan.arrival(d)
    copies[4].wait()
    for k in range(groups):
        table = slot_table(code[k], slots)

        @pl.loop(0, width // tile)
        def _(j):
            part = pl.ds(pl.multiple_of(j * tile, tile), tile)
            block = zcot[k * group : (k + 1) * group, :, part].reshape(group * count, tile)
            value = jnp.dot(table, block, preferred_element_type=F32).astype(BF)
            ready[k, :, :, part] = value.reshape(n_shard, slots, tile)

    for item in waits + w_waits:
        item.wait()
    copies[0].wait()
    copies[1].wait()
    copies[3].wait()
    own_head.wait()
    outs = [
        pltpu.make_async_copy(rows_all, rows_out, out_sem.at[0]),
        pltpu.make_async_copy(w_all, w_all_out, out_sem.at[1]),
    ]
    outs[0].start()
    outs[1].start()

    right = w_all[:, :, pl.ds(cols, HEAD_DIM)].reshape(width, HEAD_DIM)

    @pl.loop(0, n_shard)
    def _(b):
        pre = jnp.dot(rows_all[b], right, preferred_element_type=F32)
        kvpre[b] = pre
        keyed, unused = unit_rows(pre)
        keyed = turn(keyed * k_gain[...], cosine[...], sine[...])
        kv[parity, b, c] = jnp.where(parity == 0, keyed, pre).astype(BF)

    fan = Fan(n_ctx, c, lambda d: kv.at[parity, :, flip_bits(c, d)], ss_kz, rs_kz, False)
    fan.send(0, kv.at[parity, :, c])
    kv_waits = []
    item = push(kv.at[parity, :, c], kv.at[parity, :, c], ss_kf.at[0], rs_kf.at[0], shard=sibling)
    item.start()
    kv_waits.append(item)

    cot_waits = []
    for k in range(groups):
        for i, peer in enumerate(others):
            item = push(ready.at[k, peer], cot_rows.at[s, k], ss_x.at[k, i], rs_x.at[k, i], shard=peer)
            item.start()
            cot_waits.append(item)
        item = pltpu.make_async_copy(ready.at[k, s], cot_rows.at[s, k], local.at[6 + k])
        item.start()
        cot_waits.append(item)

    @pl.loop(0, n_shard // 2)
    def _(b):
        left = rows_all[pl.ds(b * 2, 2)].reshape(2 * count, width)
        pre = jnp.dot(left, w_all[:, :, pl.ds(0, cols)].reshape(width, cols), preferred_element_type=F32)
        qpre[pl.ds(b * 2, 2)] = pre.reshape(2, count, cols)
        for i in range(2):
            for h in range(heads):
                part = pre[i * count : (i + 1) * count, h * HEAD_DIM : (h + 1) * HEAD_DIM]
                unit, unused = unit_rows(part)
                q[b * 2 + i, :, h * HEAD_DIM : (h + 1) * HEAD_DIM] = turn(
                    unit * q_gain[...], cosine[...], sine[...]
                ).astype(BF)

    for d in fan.order():
        fan.arrival(d)
        block = kv.at[parity, :, flip_bits(c, d)]
        item = push(block, block, ss_kf.at[d], rs_kf.at[d], shard=sibling)
        item.start()
        kv_waits.append(item)
    outs += [pltpu.make_async_copy(qpre, qpre_out, out_sem.at[2]), pltpu.make_async_copy(q, q_out, out_sem.at[3])]
    outs[2].start()
    outs[3].start()
    for item in kv_waits:
        item.wait()
    fan.drain()
    outs.append(pltpu.make_async_copy(kv, kv_out, out_sem.at[4]))
    outs[4].start()

    near, far = {}, {}
    order = list(range(1, chips)) + [0]

    def product(at):
        d = order[at]
        first_seq = 2 * lax.rem(chip + d, chips)

        @pl.loop(0, 2)
        def _(i):
            b = first_seq + i
            k_all = kv[0, b].reshape(keys, HEAD_DIM)
            v_all = kv[1, b].reshape(keys, HEAD_DIM)
            for h in range(heads):
                hs = slice(h * HEAD_DIM, (h + 1) * HEAD_DIM)
                scores = lax.dot_general(q[b, :, hs], k_all, (((1,), (1,)), ((), ())), preferred_element_type=F32)
                scores = scores * (HEAD_DIM ** -0.5) + bias[...]
                raised = jnp.exp(scores - jnp.max(scores, axis=-1, keepdims=True))
                probs = raised / jnp.sum(raised, axis=-1, keepdims=True)
                attn[b, :, hs] = jnp.dot(probs.astype(BF), v_all, preferred_element_type=F32).astype(BF)

        left = attn[pl.ds(first_seq, 2)].reshape(2 * count, cols)

        @pl.loop(0, width // tile)
        def _(j):
            part = pl.ds(pl.multiple_of(j * tile, tile), tile)
            value = jnp.dot(left, w_out[:, part], preferred_element_type=F32)
            pair[...] = value.reshape(2, count, tile)
            own_part[at % 2, :, part] = pair[parity]
            to_sib[at, :, part] = pair[1 - parity].astype(BF)

        near[at] = push(to_sib.at[at], sib.at[at], ss_s.at[at], rs_s.at[at], shard=sibling)
        near[at].start()

    def chip_sum(at):
        near[at].wait()
        to_chip[at] = (own_part[at % 2] + sib[at].astype(F32)).astype(BF)
        far[at] = push(to_chip.at[at], got.at[at], ss_c.at[at], rs_c.at[at], shard=mates[order[at] - 1])
        far[at].start()

    for at in range(chips):
        product(at)
        if at:
            chip_sum(at - 1)
    outs.append(pltpu.make_async_copy(attn, attn_out, out_sem.at[5]))
    outs[5].start()
    near[chips - 1].wait()
    mid[...] = tokens[...].astype(F32) + own_part[(chips - 1) % 2] + sib[chips - 1].astype(F32)
    for at in range(chips - 1):
        far[at].wait()
        mid[...] += got[at].astype(F32)
    cot_fan.drain()
    route_fan.drain()
    for item in cot_waits + outs:
        item.wait()


def front(n_ctx, n_shard, group, capacity, kv_heads, args, ident):
    tokens, gain, w_query, key_w, value_w, routes, router, cot = args[:8]
    n, z = n_shard, n_ctx
    count, width = tokens.shape
    wr, chips, groups, slots = w_query.shape[0], n_shard // 2, n_ctx // group, group * capacity
    cols = w_query.shape[1] // n
    heads = cols // HEAD_DIM
    sds = jax.ShapeDtypeStruct
    dma = lambda *shape: DMA(shape)
    return call(
        functools.partial(front_body, z, n, group, capacity, heads, kv_heads, 512),
        [
            sds((n, count, width), BF), sds((n, wr, cols + HEAD_DIM), BF), sds((router.shape[0], width), BF),
            sds((groups, n, group * count), F32), sds((n, groups, slots, width), BF), sds((n, count, cols), F32),
            sds((n, count, HEAD_DIM), F32), sds((n, count, cols), BF), sds((2, n, z, count, HEAD_DIM), BF),
            sds((n, count, cols), BF), sds((count, width), F32),
        ],
        [VMEM, VMEM, ANY, ANY, ANY, VMEM, ANY, ANY] + [VMEM] * 6,
        [
            pltpu.VMEM((count, width), BF), pltpu.VMEM((n, count, width), BF), pltpu.VMEM((n, wr, cols + HEAD_DIM), BF),
            pltpu.VMEM((z,) + routes.shape, jnp.int32), pltpu.VMEM((z, count, width), BF),
            pltpu.VMEM((groups, n, slots, width), BF), pltpu.VMEM((n, count, cols), F32),
            pltpu.VMEM((n, count, cols), BF), pltpu.VMEM((2, n, z, count, HEAD_DIM), BF),
            pltpu.VMEM((n, count, cols), BF), pltpu.VMEM((2, count, width), F32), pltpu.VMEM((2, count, 512), F32),
            pltpu.VMEM((chips, count, width), BF), pltpu.VMEM((chips, count, width), BF),
            pltpu.VMEM((chips - 1, count, width), BF), pltpu.VMEM((chips - 1, count, width), BF),
            dma(6 + groups), dma(chips), dma(chips), dma(chips), dma(chips), dma(n - 1), dma(n - 1), dma(n - 1), dma(n - 1),
            dma(n - 1), dma(n - 1), dma(z), dma(z), dma(z), dma(z), dma(groups, n - 1), dma(groups, n - 1),
            dma(z), dma(z), dma(z), dma(z), dma(chips), dma(chips), dma(chips - 1), dma(chips - 1), dma(6),
        ],
        ident, args, mib=60,
        out_specs=[ANY, ANY, ANY, VMEM, ANY, ANY, VMEM, ANY, ANY, ANY, VMEM],
    )


def spread_body(n_shard, rows, rows_all, local, ss_row, rs_row, ss_fwd, rs_fwd):
    c, s, parity, sibling, others, layers = here(1, n_shard)
    chips = n_shard // 2
    mates = [lax.rem(s + 2 * d, n_shard) for d in range(1, chips)]
    greet(mates + [sibling], [])
    mine = pltpu.make_async_copy(rows, rows_all.at[s], local)
    mine.start()
    first, waits = [], []
    for d in range(1, chips):
        item = push(rows, rows_all.at[s], ss_row.at[d], rs_row.at[d], shard=mates[d - 1])
        item.start()
        first.append(item)
    item = push(rows, rows_all.at[s], ss_fwd.at[0], rs_fwd.at[0], shard=sibling)
    item.start()
    waits.append(item)
    for d in range(1, chips):
        first[d - 1].wait()
        origin = lax.rem(s + n_shard - 2 * d, n_shard)
        item = push(rows_all.at[origin], rows_all.at[origin], ss_fwd.at[d], rs_fwd.at[d], shard=sibling)
        item.start()
        waits.append(item)
    mine.wait()
    for item in waits:
        item.wait()


def spread(n_shard, rows, ident):
    return call(
        functools.partial(spread_body, n_shard),
        [jax.ShapeDtypeStruct((n_shard,) + rows.shape, rows.dtype)],
        [ANY], [DMA] + [DMA((n_shard // 2,))] * 4, ident, (rows,),
    )[0]


def key_back_body(n_ctx, n_shard, parts, out, sib, zsend, zrecv, ss_s, rs_s, ss_z, rs_z):
    c, s, parity, sibling, others, layers = here(n_ctx, n_shard)
    greet([sibling], layers)
    order = list(range(1, n_ctx)) + [0]
    near = {}
    for d in order:
        block = parts.at[1 - parity, :, lax.rem(c + d, n_ctx)]
        near[d] = push(block, sib.at[d], ss_s.at[d], rs_s.at[d], shard=sibling)
        near[d].start()
    far = {}
    for d in order:
        near[d].wait()
        layer = lax.rem(c + d, n_ctx)
        value = parts[parity, :, layer].astype(F32) + sib[d].astype(F32)
        if d:
            zsend[d - 1] = value.astype(BF)
            far[d] = push(zsend.at[d - 1], zrecv.at[d - 1], ss_z.at[d], rs_z.at[d], ctx=layer)
            far[d].start()
    for d in range(1, n_ctx):
        far[d].wait()
        value = value + zrecv[d - 1].astype(F32)
    out[...] = value


def key_back(n_ctx, n_shard, parts, ident):
    block = (parts.shape[1], parts.shape[3], parts.shape[4])
    return call(
        functools.partial(key_back_body, n_ctx, n_shard),
        [jax.ShapeDtypeStruct(block, F32)],
        [VMEM],
        [
            pltpu.VMEM((n_ctx,) + block, BF), pltpu.VMEM((n_ctx - 1,) + block, BF),
            pltpu.VMEM((n_ctx - 1,) + block, BF),
        ] + [DMA((n_ctx,))] * 4,
        ident, (parts,), out_specs=[VMEM],
    )[0]


def finish_body(n_ctx, n_shard, q_cols, tile,
                weights, wide, router, gains, left, right, tokens, gain,
                q_out, kv_out, wide_out, router_out, gains_out, rows_out,
                wide_landing, wide_acc, wide_total, ss_wi, rs_wi, ss_wo, ss_wc, pieces, landing, acc, total, router_in, router_mid, router_far,
                gains_own, gains_in, gains_mid, gains_far, pair, own_part, to_sib, sib, to_chip, got,
                local, ss_w, rs_w, ss_i, rs_i, ss_o, ss_q, ss_k, ss_r, rs_r, ss_g, rs_g, ss_h, rs_h,
                ss_t, rs_t, ss_s, rs_s, ss_c, rs_c):
    c, s, parity, sibling, others, layers = here(n_ctx, n_shard)
    half = n_ctx // 2
    chips = n_shard // 2
    chip = lax.div(s, 2)
    mates = [lax.rem(s + 2 * d, n_shard) for d in range(1, chips)]
    left_side = c < half
    depth = jnp.where(left_side, c, n_ctx - 1 - c)
    inner = jnp.where(left_side, c + 1, c - 1)
    outer = jnp.clip(jnp.where(left_side, c - 1, c + 1), 0, n_ctx - 1)
    middle = depth == half - 1
    inside = depth > 0
    rows, width = rows_out.shape
    greet(others, layers)
    sends, small = [None], []
    for i, peer in enumerate(others):
        item = push(weights.at[peer], pieces.at[i + 1], ss_w.at[i], rs_w.at[i], shard=peer)
        item.start()
        sends.append(item)
    for i, peer in enumerate(others):
        item = push(router.at[peer], router_in.at[i], ss_r.at[i], rs_r.at[i], shard=peer)
        item.start()
        small.append(item)

    def out_copies(j, ref):
        source = lax.rem(s + n_shard - j, n_shard)
        cols = pl.ds(pl.multiple_of(source * q_cols, q_cols), q_cols)
        return (
            pltpu.make_async_copy(ref.at[:, pl.ds(0, q_cols)], q_out.at[:, cols], ss_q.at[j]),
            pltpu.make_async_copy(ref.at[:, pl.ds(q_cols, 128)], kv_out.at[source], ss_k.at[j]),
        )

    def wide_copies(j, ref):
        return (pltpu.make_async_copy(ref, wide_out.at[j], ss_wc.at[j]),)

    class Line:
        def __init__(self, ready, own, acc, landing, total, ss_i, rs_i, ss_o, copies):
            self.ready, self.own, self.acc, self.landing, self.total = ready, own, acc, landing, total
            self.ss_i, self.rs_i, self.ss_o, self.copies = ss_i, rs_i, ss_o, copies

        def inward(self, j, ref):
            at = jnp.where(middle, 1, 0)
            return push(ref, self.landing.at[at, j], self.ss_i.at[j], self.rs_i.at[at, j], ctx=inner)

        def outward(self, j):
            return push(self.total.at[j], self.landing.at[1, j], self.ss_o.at[j], self.rs_i.at[1, j], ctx=outer)

        def arrived(self, which, j):
            push(self.acc.at[j], self.landing.at[which, j], self.ss_i.at[j], self.rs_i.at[which, j],
                 ctx=inner).wait_recv()

        def outermost(self, j):
            @pl.when(jnp.logical_not(inside))
            def _():
                self.ready(j)
                self.inward(j, self.own(j)).start()

        def first_half(self, j):
            @pl.when(inside)
            def _():
                self.ready(j)
                self.arrived(0, j)
                self.acc[j] = (self.own(j)[...].astype(F32) + self.landing[0, j].astype(F32)).astype(BF)
                self.inward(j, self.acc.at[j]).start()

        def second_half(self, j):
            self.arrived(1, j)

            @pl.when(middle)
            def _():
                self.total[j] = (self.acc[j].astype(F32) + self.landing[1, j].astype(F32)).astype(BF)

            @pl.when(jnp.logical_not(middle))
            def _():
                self.total[j] = self.landing[1, j]

            @pl.when(inside)
            def _():
                self.outward(j).start()

            for item in self.copies(j, self.total.at[j]):
                item.start()

        def drain(self, j):
            self.inward(j, self.acc.at[j]).wait_send()

            @pl.when(inside)
            def _():
                self.outward(j).wait_send()

            for item in self.copies(j, self.total.at[j]):
                item.wait()

    line = Line(lambda j: sends[j].wait() if j else None, lambda j: pieces.at[j] if j else weights.at[s],
                acc, landing, total, ss_i, rs_i, ss_o, out_copies)
    wide_line = Line(lambda j: None, lambda j: wide.at[j], wide_acc, wide_landing, wide_total,
                     ss_wi, rs_wi, ss_wo, wide_copies)
    wides = wide.shape[0]
    steps = [(wide_line, j) for j in range(wides)] + [(line, j) for j in range(n_shard)]

    near, far = {}, {}

    def product(d):
        first = pl.multiple_of(lax.rem(chip + d, chips) * (2 * rows), 2 * rows)

        @pl.loop(0, width // tile)
        def _(j):
            cols = pl.ds(pl.multiple_of(j * tile, tile), tile)
            value = lax.dot_general(left[pl.ds(first, 2 * rows), :], right[cols, :],
                                    (((1,), (1,)), ((), ())), preferred_element_type=F32)
            pair[...] = value.reshape(2, rows, tile)
            own_part[d, :, cols] = pair[parity]
            to_sib[d, :, cols] = pair[1 - parity].astype(BF)

        near[d] = push(to_sib.at[d], sib.at[d], ss_s.at[d], rs_s.at[d], shard=sibling)
        near[d].start()

    def chip_sum(d):
        near[d].wait()
        to_chip[d - 1] = (own_part[d] + sib[d].astype(F32)).astype(BF)
        far[d] = push(to_chip.at[d - 1], got.at[d - 1], ss_c.at[d - 1], rs_c.at[d - 1], shard=mates[d - 1])
        far[d].start()

    gain_sends = []

    def last_sum():
        near[0].wait()
        grad = own_part[0] + sib[0].astype(F32)
        for d in range(1, chips):
            far[d].wait()
            grad = grad + got[d - 1].astype(F32)
        x = tokens[...].astype(F32)
        scale = lax.rsqrt(jnp.mean(x * x, axis=-1, keepdims=True) + epsilon)
        unit = x * scale
        scaled = grad * gain[...]
        rows_out[...] = scale * (scaled - unit * jnp.mean(scaled * unit, axis=-1, keepdims=True))
        gains_own[...] = gains[...]
        gains_own[0:1] = jnp.sum(grad * unit, axis=0, keepdims=True)
        mine = pltpu.make_async_copy(gains_own, gains_in.at[s], local.at[0])
        mine.start()
        gain_sends.append(mine)
        for i, peer in enumerate(others):
            item = push(gains_own, gains_in.at[s], ss_g.at[i], rs_g.at[i], shard=peer)
            item.start()
            gain_sends.append(item)

    def small_plane():
        for item in small + gain_sends:
            item.wait()
        gains_mid[...] = gains_in[0]
        for i in range(1, n_shard):
            gains_mid[...] += gains_in[i]
        router_mid[...] = router[s].astype(F32)
        for i in range(n_shard - 1):
            router_mid[...] += router_in[i].astype(F32)
        for i, layer in enumerate(layers):
            push(gains_mid, gains_far.at[c], ss_h.at[i], rs_h.at[i], ctx=layer).start()
            push(router_mid, router_far.at[c], ss_t.at[i], rs_t.at[i], ctx=layer).start()
        pltpu.make_async_copy(gains_mid, gains_far.at[c], local.at[1]).start()
        pltpu.make_async_copy(router_mid, router_far.at[c], local.at[2]).start()

    def small_all():
        pltpu.make_async_copy(gains_mid, gains_far.at[c], local.at[1]).wait()
        pltpu.make_async_copy(router_mid, router_far.at[c], local.at[2]).wait()
        for i, layer in enumerate(layers):
            push(gains_mid, gains_far.at[c], ss_h.at[i], rs_h.at[i], ctx=layer).wait()
            push(router_mid, router_far.at[c], ss_t.at[i], rs_t.at[i], ctx=layer).wait()
        gains_out[...] = gains_far[0]
        router_out[...] = router_far[0]
        for i in range(1, n_ctx):
            gains_out[...] += gains_far[i]
            router_out[...] += router_far[i]

    lag, ahead = 2, 6
    for which, j in steps[:ahead]:
        which.outermost(j)
    for d in list(range(1, chips)) + [0]:
        product(d)
    side = [functools.partial(chip_sum, d) for d in range(1, chips)] + [last_sum, small_plane]
    for n in range(len(steps) + lag):
        if n + ahead < len(steps):
            steps[n + ahead][0].outermost(steps[n + ahead][1])
        if n < len(steps):
            steps[n][0].first_half(steps[n][1])
        if n >= lag:
            steps[n - lag][0].second_half(steps[n - lag][1])
        if n >= 2 and side:
            side.pop(0)()
    for job in side:
        job()
    small_all()
    for which, j in steps:
        which.drain(j)


def finish(n_ctx, n_shard, q_cols, weights, wide, router, gains, left, right, tokens, gain, ident):
    n, rows, cols = weights.shape
    router_shape = router.shape[1:]
    count, width = tokens.shape
    chips = n // 2
    tile = 512
    wides = wide.shape[0]
    return call(
        functools.partial(finish_body, n_ctx, n, q_cols, tile),
        [
            jax.ShapeDtypeStruct((rows, n * q_cols), BF), jax.ShapeDtypeStruct((n, rows, 128), BF),
            jax.ShapeDtypeStruct(wide.shape, BF),
            jax.ShapeDtypeStruct(router_shape, F32), jax.ShapeDtypeStruct(gains.shape, F32),
            jax.ShapeDtypeStruct((count, width), F32),
        ],
        [VMEM] * 8,
        [
            pltpu.VMEM((2,) + wide.shape, BF), pltpu.VMEM(wide.shape, BF), pltpu.VMEM(wide.shape, BF),
            DMA((wides,)), DMA((2, wides)), DMA((wides,)), DMA((wides,)),
            pltpu.VMEM((n, rows, cols), BF), pltpu.VMEM((2, n, rows, cols), BF),
            pltpu.VMEM((n, rows, cols), BF), pltpu.VMEM((n, rows, cols), BF),
            pltpu.VMEM((n - 1,) + router_shape, BF), pltpu.VMEM(router_shape, F32),
            pltpu.VMEM((n_ctx,) + router_shape, F32),
            pltpu.VMEM(gains.shape, F32), pltpu.VMEM((n,) + gains.shape, F32),
            pltpu.VMEM(gains.shape, F32), pltpu.VMEM((n_ctx,) + gains.shape, F32),
            pltpu.VMEM((2, count, tile), F32), pltpu.VMEM((chips, count, width), F32),
            pltpu.VMEM((chips, count, width), BF), pltpu.VMEM((chips, count, width), BF),
            pltpu.VMEM((chips - 1, count, width), BF), pltpu.VMEM((chips - 1, count, width), BF),
            DMA((3,)), DMA((n - 1,)), DMA((n - 1,)), DMA((n,)), DMA((2, n)), DMA((n,)),
            DMA((n,)), DMA((n,)), DMA((n - 1,)), DMA((n - 1,)), DMA((n - 1,)), DMA((n - 1,)),
            DMA((n_ctx - 1,)), DMA((n_ctx - 1,)), DMA((n_ctx - 1,)), DMA((n_ctx - 1,)),
            DMA((chips,)), DMA((chips,)), DMA((chips - 1,)), DMA((chips - 1,)),
        ],
        ident, (weights, wide, router, gains, left, right, tokens, gain), mib=60,
        out_specs=[ANY, ANY, ANY, VMEM, VMEM, VMEM],
    )


def dispatch_body(n_ctx, n_shard, group, tile, rows, tail, code, recv, tail_recv,
                  zrows, ztail, ready, tail_ready, local, ss_z, rs_z, ss_t, rs_t, ss_x, rs_x, ss_y, rs_y):
    c, s, parity, sibling, others, layers = here(n_ctx, n_shard)
    greet(others, layers)
    count, width = rows.shape
    groups = n_ctx // group
    slots = recv.shape[2]
    own = [pltpu.make_async_copy(rows, zrows.at[c], local.at[0]), pltpu.make_async_copy(tail, ztail.at[c], local.at[1])]
    fans = [
        Fan(n_ctx, c, lambda d: ztail.at[flip_bits(c, d)], ss_t, rs_t, True),
        Fan(n_ctx, c, lambda d: zrows.at[flip_bits(c, d)], ss_z, rs_z, True),
    ]
    fans[0].send(0, tail)
    fans[1].send(0, rows)
    for item in own:
        item.start()
    waits = []
    seen = set()
    for k in range(groups):
        at = flip_bits(lax.div(c, group), k)
        if k == 0:
            for item in own:
                item.wait()
        table = slot_table(code[at], slots)
        for d in fans[0].order():
            if d < (k + 1) * group and d not in seen:
                fans[0].arrival(d)
                fans[1].arrival(d)
                seen.add(d)
        first = pl.multiple_of(at * group, group)
        block = ztail[pl.ds(first, group)].reshape(group * count, -1)
        tail_ready[k] = jnp.dot(table, block, preferred_element_type=F32).astype(BF).reshape(n_shard, slots, -1)

        @pl.loop(0, width // tile)
        def _(j):
            cols = pl.ds(pl.multiple_of(j * tile, tile), tile)
            block = zrows[pl.ds(first, group), :, cols].reshape(group * count, tile)
            value = jnp.dot(table, block, preferred_element_type=F32).astype(BF)
            ready[k, :, :, cols] = value.reshape(n_shard, slots, tile)

        for i, peer in enumerate(others):
            item = push(ready.at[k, peer], recv.at[s, at], ss_x.at[k, i], rs_x.at[k, i], shard=peer)
            item.start()
            waits.append(item)
            item = push(tail_ready.at[k, peer], tail_recv.at[s, at], ss_y.at[k, i], rs_y.at[k, i], shard=peer)
            item.start()
            waits.append(item)
        item = pltpu.make_async_copy(ready.at[k, s], recv.at[s, at], local.at[2 * k + 2])
        item.start()
        waits.append(item)
        item = pltpu.make_async_copy(tail_ready.at[k, s], tail_recv.at[s, at], local.at[2 * k + 3])
        item.start()
        waits.append(item)
    for fan in fans:
        fan.drain()
    for item in waits:
        item.wait()


def dispatch_rows(n_ctx, n_shard, group, capacity, rows, tail, code, ident):
    groups, slots = code.shape[0], group * capacity
    count, width = rows.shape
    few = tail.shape[1]
    return call(
        functools.partial(dispatch_body, n_ctx, n_shard, group, 512),
        [
            jax.ShapeDtypeStruct((n_shard, groups, slots, width), BF),
            jax.ShapeDtypeStruct((n_shard, groups, slots, few), BF),
        ],
        [VMEM, VMEM, VMEM],
        [
            pltpu.VMEM((n_ctx, count, width), BF), pltpu.VMEM((n_ctx, count, few), BF),
            pltpu.VMEM((groups, n_shard, slots, width), BF), pltpu.VMEM((groups, n_shard, slots, few), BF),
            DMA((2 * groups + 2,)), DMA((n_ctx,)), DMA((n_ctx,)), DMA((n_ctx,)), DMA((n_ctx,)),
        ] + [DMA((groups, n_shard - 1))] * 4,
        ident, (rows, tail, code), mib=56,
    )


def combine_body(n_ctx, n_shard, group, tile, rows, tail, mix, code, out, tail_out, mix_out,
                 land, tail_land, value, tail_value, zsend, zrecv, tsend, trecv, msend, mrecv, mix_kept, table, local,
                 ss_x, rs_x, ss_y, rs_y, ss_z, rs_z, ss_t, rs_t, ss_m, rs_m):
    c, s, parity, sibling, others, layers = here(n_ctx, n_shard)
    greet(others, layers)
    count, width = out.shape
    groups = n_ctx // group
    slots = rows.shape[2]
    near = {}
    for k in reversed(range(groups)):
        at = flip_bits(lax.div(c, group), k)
        near[k] = []
        for i, peer in enumerate(others):
            item = push(rows.at[peer, at], land.at[k, s], ss_x.at[k, i], rs_x.at[k, i], shard=peer)
            item.start()
            near[k].append(item)
            item = push(tail.at[peer, at], tail_land.at[k, s], ss_y.at[k, i], rs_y.at[k, i], shard=peer)
            item.start()
            near[k].append(item)
        item = pltpu.make_async_copy(rows.at[s, at], land.at[k, s], local.at[k, 0])
        item.start()
        near[k].append(item)
        item = pltpu.make_async_copy(tail.at[s, at], tail_land.at[k, s], local.at[k, 1])
        item.start()
        near[k].append(item)
    for k in range(groups):
        table[k] = slot_table(code[flip_bits(lax.div(c, group), k)], slots).T

    def local_sums(k, block_of):
        @pl.loop(0, width // tile)
        def _(j):
            cols = pl.ds(pl.multiple_of(j * tile, tile), tile)
            value[:, cols] = jnp.dot(table[k], block_of(cols), preferred_element_type=F32)

    def part(ref, d):
        place = lax.rem(flip_bits(c, d), group)
        return ref[pl.ds(pl.multiple_of(place * count, count), count), :]

    def in_group(k):
        return sorted(range(k * group, (k + 1) * group), key=lambda d: (lowest(d) or n_ctx, d))

    mix_fold = Fold(c, msend, mrecv, ss_m, rs_m)
    for k in reversed(range(groups)):
        at = flip_bits(lax.div(c, group), k)
        local_sums(k, lambda cols: mix[:, at, :, cols].reshape(n_shard * slots, tile))
        for d in in_group(k):
            if lowest(d) == 1:
                mix_fold.give(d, part(value, d))
            else:
                mix_kept[d // 2] = part(value, d)
    fold = Fold(c, zsend, zrecv, ss_z, rs_z)
    tail_fold = Fold(c, tsend, trecv, ss_t, rs_t)
    for k in reversed(range(groups)):
        for item in near[k]:
            item.wait()
        local_sums(k, lambda cols: land[k, :, :, cols].reshape(n_shard * slots, tile))
        tail_value[...] = jnp.dot(
            table[k], tail_land[k].reshape(n_shard * slots, -1), preferred_element_type=F32
        )
        for d in in_group(k):
            if lowest(d) == 1:
                fold.give(d, part(value, d))
                tail_fold.give(d, part(tail_value, d))
        for d in in_group(k):
            if lowest(d) != 1:
                if d:
                    mix_fold.give(d, mix_fold.take(d, mix_kept[d // 2]))
                    fold.give(d, fold.take(d, part(value, d)))
                    tail_fold.give(d, tail_fold.take(d, part(tail_value, d)))
                else:
                    mix_out[...] = mix_fold.take(0, mix_kept[0])
                    out[...] = fold.take(0, part(value, 0))
                    tail_out[...] = tail_fold.take(0, part(tail_value, 0))
    for item in (mix_fold, fold, tail_fold):
        item.drain()


def combine_rows(n_ctx, n_shard, group, rows, tail, mix, code, ident):
    groups, slots, width = rows.shape[1:]
    few = tail.shape[3]
    count = code.shape[2] // group
    sds = jax.ShapeDtypeStruct
    return call(
        functools.partial(combine_body, n_ctx, n_shard, group, 512),
        [sds((count, width), F32), sds((count, few), F32), sds((count, width), F32)],
        [VMEM] * 4,
        [
            pltpu.VMEM((groups, n_shard, slots, width), BF), pltpu.VMEM((groups, n_shard, slots, few), BF),
            pltpu.VMEM((group * count, width), F32), pltpu.VMEM((group * count, few), F32),
            pltpu.VMEM((n_ctx - 1, count, width), BF), pltpu.VMEM((n_ctx - 1, count, width), BF),
            pltpu.VMEM((n_ctx - 1, count, few), BF), pltpu.VMEM((n_ctx - 1, count, few), BF),
            pltpu.VMEM((n_ctx - 1, count, width), BF), pltpu.VMEM((n_ctx - 1, count, width), BF),
            pltpu.VMEM((n_ctx // 2, count, width), F32), pltpu.VMEM((groups, group * count, n_shard * slots), BF),
            DMA((groups, 2)),
        ] + [DMA((groups, n_shard - 1))] * 4 + [DMA((n_ctx,))] * 6,
        ident, (rows, tail, mix, code), mib=60, out_specs=[VMEM] * 3,
    )


def rms_scale(hidden, gain):
    return hidden * lax.rsqrt(jnp.mean(hidden * hidden, axis=-1, keepdims=True) + epsilon) * gain


def rotate(headwise, places):
    half_size = headwise.shape[-1] // 2
    frequency = rope_base ** (-jnp.arange(half_size, dtype=F32) * 2.0 / headwise.shape[-1])
    angles = places.astype(F32)[:, None] * frequency[None, :]
    cosine = jnp.cos(angles)[:, None, :]
    sine = jnp.sin(angles)[:, None, :]
    former = headwise[..., :half_size]
    latter = headwise[..., half_size:]
    return jnp.concatenate(
        [former * cosine - latter * sine, latter * cosine + former * sine], axis=-1
    )


def place_of(row_ids, order, block_rows):
    block_ids = jnp.arange(order.shape[0], dtype=jnp.int32)
    owner_block = row_ids // block_rows
    picked_block = jnp.sum(
        jnp.where(owner_block[:, None] == block_ids[None, :], order[None, :], 0), axis=1
    )
    return picked_block * block_rows + row_ids % block_rows


def dot(left, right):
    return jnp.dot(left, right, preferred_element_type=F32)


def contract_rows(left, right):
    return lax.dot_general(left, right, (((0,), (0,)), ((), ())), preferred_element_type=F32)


def contract_cols(left, right):
    return lax.dot_general(left, right, (((1,), (1,)), ((), ())), preferred_element_type=F32)


def exchange_shard(x):
    return lax.all_to_all(x, "shard", split_axis=0, concat_axis=0, tiled=True)


def gather_ctx(x):
    return lax.all_gather(x, "ctx", axis=0, tiled=False)


def shards(
    tokens,
    cotangent,
    block_order,
    routes,
    attn_gain,
    w_query,
    key_weight,
    value_weight,
    query_gain,
    key_gain,
    w_out,
    ffn_gain,
    w_router,
    w_gate,
    w_up,
    w_down,
):
    rows = tokens.shape[1]
    width = tokens.shape[2]
    ctx_count = lax.axis_size("ctx")
    shard_count = lax.axis_size("shard")
    my_ctx = lax.axis_index("ctx")
    my_shard = lax.axis_index("shard")
    experts = ctx_count * shard_count
    block_rows = rows // 2
    heads = QUERY_HEADS // shard_count
    head_cols = heads * HEAD_DIM
    sharers = shard_count // KEY_VALUE_HEADS
    score_scale = HEAD_DIM ** (-0.5)
    top_count = routes.shape[2]
    capacity = rows * top_count // experts + max(rows * top_count // (4 * experts), 1)
    sequence = rows * ctx_count
    plane = rows * shard_count
    wrows = width // shard_count

    inputs = tokens[0].astype(F32)
    upstream_b = cotangent[0]
    upstream = upstream_b.astype(F32)

    group = 1
    while group * capacity % 16:
        group *= 2
    groups = ctx_count // group
    slot_rows = shard_count * ctx_count * capacity
    block_shape = (shard_count, groups, group * capacity)
    row_ids = my_ctx * rows + jnp.arange(rows, dtype=jnp.int32)
    q_places = place_of(row_ids, block_order, block_rows)
    k_places = place_of(jnp.arange(sequence, dtype=jnp.int32), block_order, block_rows)
    bias = jnp.where(k_places[None, :] <= q_places[:, None], 0.0, -1e30).astype(F32)
    frequency = rope_base ** (-jnp.arange(HEAD_DIM // 2, dtype=F32) * 2.0 / HEAD_DIM)
    angles = q_places.astype(F32)[:, None] * frequency[None, :]
    cosine = jnp.concatenate([jnp.cos(angles)] * 2, axis=1)
    sine = jnp.concatenate([-jnp.sin(angles), jnp.sin(angles)], axis=1)
    (
        normed_all, w_mine, router_all, code, upstream_rows, query_pre, kv_pre, queries, kv_all, attn_rows, middle,
    ) = front(
        ctx_count, shard_count, group, capacity, KEY_VALUE_HEADS,
        (
            tokens[0], attn_gain[None], w_query, key_weight, value_weight, routes[0].T, w_router.T, upstream_b,
            cosine, sine, bias, query_gain[None], key_gain[None], w_out,
        ),
        0,
    )
    normed_all = normed_all.reshape(plane, width)
    w_mine = w_mine.reshape(width, head_cols + HEAD_DIM)
    upstream_rows = upstream_rows.reshape(slot_rows, width)
    query_pre = query_pre.reshape(shard_count, rows, heads, HEAD_DIM)
    kv_pre = kv_pre.reshape(plane, HEAD_DIM)
    queries = queries.reshape(shard_count, rows, heads, HEAD_DIM)
    kv_all = kv_all.reshape(2, shard_count, sequence, HEAD_DIM)
    keys, values = kv_all[0], kv_all[1]
    attn_rows = attn_rows.reshape(plane, head_cols)
    is_key = lax.rem(my_shard, 2) == 0
    part_count = sharers // 2

    def prep(pre, gain):
        shape = pre.shape
        flat = pre.reshape(-1, rows, shape[-2], HEAD_DIM)
        return jax.vmap(lambda v: rotate(rms_scale(v, gain), q_places))(flat).reshape(shape)

    normed_two = rms_scale(middle, ffn_gain)
    second_b = normed_two.astype(BF)
    logits = contract_cols(second_b, router_all)
    chosen = jnp.sum(
        (routes[0][:, :, None] == jnp.arange(experts, dtype=jnp.int32)).astype(F32), axis=1
    )

    def gates_of(log, mask):
        masked = jnp.where(mask > 0, log, -1e30)
        peak = jnp.max(masked, axis=-1, keepdims=True)
        risen = jnp.exp(masked - peak) * mask
        return risen / jnp.maximum(jnp.sum(risen, axis=-1, keepdims=True), 1e-30)

    gates = gates_of(logits, chosen)

    tail_cols = -(-2 * experts // 128) * 128

    def two_parts(value):
        coarse = value.astype(BF).astype(F32)
        return coarse.astype(BF), (value - coarse).astype(BF)

    gates_two = jnp.concatenate(two_parts(gates), axis=1)
    gates_two = jnp.pad(gates_two, ((0, 0), (0, tail_cols - 2 * experts)))
    received, gate_tail = dispatch_rows(ctx_count, shard_count, group, capacity, second_b, gates_two, code, 3)
    received = received.reshape(slot_rows, width)
    my_expert = my_ctx * shard_count + my_shard
    column = jnp.arange(tail_cols, dtype=jnp.int32)[None, :]
    mine_column = (column == my_expert) | (column == experts + my_expert)
    gate_tail = gate_tail.reshape(slot_rows, tail_cols).astype(F32)
    slot_gates = jnp.sum(jnp.where(mine_column, gate_tail, 0.0), axis=1, keepdims=True)
    gate_pre = dot(received, w_gate[0])
    up_pre = dot(received, w_up[0])
    activated = jax.nn.silu(gate_pre)
    hidden_b = (activated * up_pre).astype(BF)
    expert_out = dot(hidden_b, w_down[0]).astype(BF)
    expert_out_f = expert_out.astype(F32)
    mix_sent = (slot_gates * expert_out_f).astype(BF)
    mix_sent, upstream_rows, expert_out = lax.optimization_barrier((mix_sent, upstream_rows, expert_out))
    expert_out_f = expert_out.astype(F32)
    mix_back = exchange_shard(mix_sent.reshape(block_shape + (width,)))
    upstream_rows = upstream_rows.astype(F32)
    slot_dot = jnp.sum(expert_out_f * upstream_rows, axis=1, keepdims=True)
    grad_expert = (slot_gates * upstream_rows).astype(BF)
    grad_w_down = contract_rows(hidden_b, grad_expert)
    grad_hidden = contract_cols(grad_expert, w_down[0])
    sigmoid_g = jax.nn.sigmoid(gate_pre)
    silu_slope = sigmoid_g * (1.0 + gate_pre * (1.0 - sigmoid_g))
    grad_gate_pre = (grad_hidden * up_pre * silu_slope).astype(BF)
    grad_up_pre = (grad_hidden * activated).astype(BF)
    grad_w_gate = contract_rows(received, grad_gate_pre)
    grad_w_up = contract_rows(received, grad_up_pre)
    grad_received = contract_cols(grad_gate_pre, w_gate[0]) + contract_cols(grad_up_pre, w_up[0])

    coarse, fine = two_parts(slot_dot)
    tail = jnp.where(column == my_expert, coarse, jnp.where(column == experts + my_expert, fine, jnp.zeros((), BF)))
    grad_second, back_tail, mixture = combine_rows(
        ctx_count, shard_count, group, grad_received.astype(BF).reshape(block_shape + (width,)),
        tail.reshape(block_shape + (tail_cols,)), mix_back, code, 4,
    )
    mixed = (middle + mixture).astype(BF)
    grad_gates = back_tail[:, :experts] + back_tail[:, experts : 2 * experts]
    grad_logits_b = (
        gates * (grad_gates - jnp.sum(gates * grad_gates, axis=-1, keepdims=True))
    ).astype(BF)
    router_part = contract_rows(grad_logits_b, second_b).astype(BF)
    grad_second = grad_second + dot(grad_logits_b, router_all)
    unused, norm_two_back = jax.vjp(rms_scale, middle, ffn_gain)
    grad_middle_part, grad_ffn_gain = norm_two_back(grad_second)
    grad_middle = upstream + grad_middle_part
    grad_proj_b = grad_middle.astype(BF)

    grad_proj_all = spread(shard_count, grad_proj_b, 5).reshape(plane, width)
    out_part = contract_rows(attn_rows, grad_proj_all).astype(BF)
    out_part, grad_proj_all = lax.optimization_barrier((out_part, grad_proj_all))
    grad_attn = contract_cols(grad_proj_all, w_out).astype(BF)
    grad_heads = grad_attn.reshape(shard_count, rows, heads, HEAD_DIM)
    scores = (
        jnp.einsum("sthd,spd->shtp", queries, keys, preferred_element_type=F32) * score_scale
    )
    scores = scores + bias
    raised = jnp.exp(scores - jnp.max(scores, axis=-1, keepdims=True))
    probs = raised / jnp.sum(raised, axis=-1, keepdims=True)
    probs_b = probs.astype(BF)
    grad_probs = jnp.einsum("sthd,spd->shtp", grad_heads, values, preferred_element_type=F32)
    delta = jnp.sum(probs * grad_probs, axis=-1, keepdims=True)
    grad_scores = (probs * (grad_probs - delta)).astype(BF)
    grad_query = score_scale * jnp.einsum(
        "shtp,spd->sthd", grad_scores, keys, preferred_element_type=F32
    )
    grad_keys = score_scale * jnp.einsum(
        "shtp,sthd->spd", grad_scores, queries, preferred_element_type=F32
    )
    grad_values = jnp.einsum("shtp,sthd->spd", probs_b, grad_heads, preferred_element_type=F32)
    grad_kv = jnp.stack([grad_keys, grad_values]).astype(BF)
    grad_kv = key_back(
        ctx_count, shard_count, grad_kv.reshape(2, shard_count, ctx_count, rows, HEAD_DIM), 6
    )
    unused, query_back = jax.vjp(prep, query_pre, query_gain)
    grad_query_pre, grad_query_gain = query_back(grad_query)
    kv_shape = (shard_count, rows, 1, HEAD_DIM)
    unused, key_prep_back = jax.vjp(prep, kv_pre.reshape(kv_shape), key_gain)
    grad_key_pre, grad_key_gain = key_prep_back(grad_kv.reshape(kv_shape))
    grad_key_gain = jnp.where(is_key, grad_key_gain, 0.0)
    grad_kv_full = jnp.where(
        is_key, grad_key_pre.reshape(plane, HEAD_DIM), grad_kv.reshape(plane, HEAD_DIM)
    ).astype(BF)
    grad_pre = jnp.concatenate(
        [grad_query_pre.reshape(plane, head_cols).astype(BF), grad_kv_full], axis=1
    )
    gains = jnp.concatenate(
        [
            jnp.zeros((1, width), F32),
            grad_ffn_gain[None],
            jnp.pad(
                jnp.concatenate([grad_query_gain, grad_key_gain])[None],
                ((0, 6 - 1), (0, width - 2 * HEAD_DIM)),
            ),
        ]
    )
    grad_w = contract_rows(normed_all, grad_pre).astype(BF).reshape(shard_count, wrows, -1)
    router_parts = jnp.swapaxes(router_part.reshape(experts, shard_count, wrows), 0, 1)
    q_sum, kv_sum, out_sum, router_sum, gains, grad_input_part = finish(
        ctx_count, shard_count, head_cols, grad_w, out_part.reshape(8, -1, width), router_parts, gains, grad_pre, w_mine,
        tokens[0], attn_gain[None], 8,
    )
    grad_tokens = grad_middle + grad_input_part
    grad_attn_gain, grad_ffn_gain = gains[0], gains[1]
    grad_query_gain, grad_key_gain = gains[2, :HEAD_DIM], gains[2, HEAD_DIM : 2 * HEAD_DIM]
    grad_w_query = q_sum.astype(F32)
    grad_w_out = out_sum.reshape(head_cols, width).astype(F32)
    kinds = kv_sum.astype(F32).reshape(KEY_VALUE_HEADS, part_count, 2, wrows, HEAD_DIM)
    kinds = jnp.transpose(jnp.sum(kinds, axis=1), (1, 2, 0, 3)).reshape(2, wrows, -1)
    grad_w_key, grad_w_value = kinds[0], kinds[1]
    grad_w_router = router_sum.T
    return (
        mixed[None],
        grad_tokens[None],
        grad_attn_gain,
        grad_w_query,
        grad_w_key,
        grad_w_value,
        grad_query_gain,
        grad_key_gain,
        grad_w_out,
        grad_ffn_gain,
        grad_w_router,
        grad_w_gate[None],
        grad_w_up[None],
        grad_w_down[None],
    )


def solution(mesh):
    rows = P("shard", "ctx", None)
    matrix = P("shard", None)
    expert = P(("ctx", "shard"), None, None)
    return jax.shard_map(
        shards,
        mesh=mesh,
        in_specs=(
            rows, rows, P(), rows, P(), matrix, matrix, matrix, P(), P(), matrix, P(), matrix,
            expert, expert, expert,
        ),
        out_specs=(
            rows, rows, P(), matrix, matrix, matrix, P(), P(), matrix, P(), matrix,
            expert, expert, expert,
        ),
        check_vma=False,
    )
```

```python
import functools

import jax
import jax.numpy as jnp
from jax import lax
from jax.experimental import pallas as pl
from jax.experimental.pallas import tpu as pltpu
from jax.sharding import PartitionSpec as P

BF = jnp.bfloat16
F32 = jnp.float32
MESH = pl.DeviceIdType.MESH
ANY = pl.BlockSpec(memory_space=pl.ANY)
VMEM = pl.BlockSpec(memory_space=pltpu.VMEM)
DMA = pltpu.SemaphoreType.DMA
epsilon = 1e-06
rope_base = 1000000.0
QUERY_HEADS = 32
KEY_VALUE_HEADS = 4
HEAD_DIM = 128


def push(src, dst, send_sem, recv_sem, **where):
    return pltpu.make_async_remote_copy(
        src_ref=src, dst_ref=dst, send_sem=send_sem, recv_sem=recv_sem,
        device_id=where, device_id_type=MESH,
    )


def greet(shard_peers, ctx_peers):
    barrier = pltpu.get_barrier_semaphore()
    for peer in shard_peers:
        pl.semaphore_signal(barrier, inc=1, device_id={"shard": peer}, device_id_type=MESH)
    for peer in ctx_peers:
        pl.semaphore_signal(barrier, inc=1, device_id={"ctx": peer}, device_id_type=MESH)
    pl.semaphore_wait(barrier, len(shard_peers) + len(ctx_peers))


def here(ctx_count, shard_count):
    c, s = lax.axis_index("ctx"), lax.axis_index("shard")
    parity = lax.rem(s, 2)
    sibling = s + 1 - 2 * parity
    others = [lax.rem(s + d, shard_count) for d in range(1, shard_count)]
    layers = [lax.rem(c + d, ctx_count) for d in range(1, ctx_count)]
    return c, s, parity, sibling, others, layers


def flip_bits(index, mask):
    result = index
    bit = 1
    while bit <= mask:
        if mask & bit:
            result = result + bit - 2 * bit * lax.rem(lax.div(index, bit), 2)
        bit *= 2
    return result


def lowest(d):
    return d & -d


class Fan:
    def __init__(self, n_ctx, c, block, ss, rs, near_first):
        self.n_ctx, self.c, self.block, self.ss, self.rs, self.near_first = n_ctx, c, block, ss, rs, near_first
        self.items = {}

    def send(self, d, src):
        bits = [b for b in (1, 2, 4, 8, 16) if b < (lowest(d) or self.n_ctx)]
        for b in bits if self.near_first else reversed(bits):
            item = push(src, self.block(d), self.ss.at[d | b], self.rs.at[d | b], ctx=flip_bits(self.c, b))
            item.start()
            self.items[d | b] = item

    def arrival(self, d):
        self.items[d].wait_recv()
        if lowest(d) > 1:
            self.send(d, self.block(d))

    def order(self):
        return sorted(range(1, self.n_ctx), key=lambda d: (bin(d).count("1"), d if self.near_first else -d))

    def drain(self):
        for d in range(1, self.n_ctx):
            self.items[d].wait_send()


class Fold:
    def __init__(self, c, sent, received, ss, rs):
        self.c, self.sent, self.received, self.ss, self.rs = c, sent, received, ss, rs
        self.items = {}

    def take(self, d, value):
        for b in (1, 2, 4, 8, 16):
            if b < lowest(d) or (d == 0 and b in self.items):
                self.items[d | b].wait_recv()
                value = value + self.received[(d | b) - 1].astype(F32)
        return value

    def give(self, d, value):
        self.sent[d - 1] = value.astype(BF)
        item = push(self.sent.at[d - 1], self.received.at[d - 1], self.ss.at[d], self.rs.at[d],
                    ctx=flip_bits(self.c, lowest(d)))
        item.start()
        self.items[d] = item

    def drain(self):
        for item in self.items.values():
            item.wait_send()


def call(body, outs, in_specs, scratch, ident, args, mib=48, out_specs=None):
    return pl.pallas_call(
        body,
        out_shape=outs,
        in_specs=in_specs,
        out_specs=out_specs if out_specs is not None else [ANY] * len(outs),
        scratch_shapes=scratch,
        compiler_params=pltpu.CompilerParams(
            collective_id=ident, has_side_effects=True, vmem_limit_bytes=mib * 2**20
        ),
    )(*args)


def slot_table(code, slots):
    places = lax.broadcasted_iota(jnp.int32, (slots, code.shape[1]), 0).astype(F32)
    return jnp.concatenate(
        [(places == code[e : e + 1, :]).astype(BF) for e in range(code.shape[0])], axis=0
    )


def turn(value, cosine, sine):
    return value * cosine + pltpu.roll(value, HEAD_DIM // 2, 1) * sine


def unit_rows(value):
    scale = lax.rsqrt(jnp.mean(value * value, axis=-1, keepdims=True) + epsilon)
    return value * scale, scale


def front_body(n_ctx, n_shard, group, capacity, heads, kv_heads, tile,
               tokens, gain, w_query, key_w, value_w, routes, router, cot, cosine, sine, bias, q_gain, k_gain, w_out,
               rows_out, w_all_out, router_all, code, cot_rows, qpre_out, kvpre, q_out, kv_out, attn_out, mid,
               own_rows, rows_all, w_all, zroutes, zcot, ready, qpre, q, kv, attn,
               own_part, pair, to_sib, sib, to_chip, got,
               local, ss_row, rs_row, ss_fwd, rs_fwd, ss_w, rs_w, ss_k, rs_k, ss_rt, rs_rt, ss_ro, rs_ro, ss_z, rs_z,
               ss_x, rs_x, ss_kz, rs_kz, ss_kf, rs_kf, ss_s, rs_s, ss_c, rs_c, out_sem):
    c, s, parity, sibling, others, layers = here(n_ctx, n_shard)
    chips = n_shard // 2
    chip = lax.div(s, 2)
    count, width = tokens.shape
    wr = w_query.shape[0]
    cols = heads * HEAD_DIM
    sharers = n_shard // kv_heads
    groups = n_ctx // group
    slots = group * capacity
    keys = n_ctx * count
    mates = [lax.rem(s + 2 * d, n_shard) for d in range(1, chips)]
    x = tokens[...].astype(F32)
    unit, unused = unit_rows(x)
    own_rows[...] = (unit * gain[...]).astype(BF)
    greet(others, layers)

    route_fan = Fan(n_ctx, c, lambda d: zroutes.at[flip_bits(c, d)], ss_ro, rs_ro, False)
    route_fan.send(0, routes)
    cot_fan = Fan(n_ctx, c, lambda d: zcot.at[flip_bits(c, d)], ss_z, rs_z, False)
    cot_fan.send(0, cot)
    first, waits = [], []
    for d in range(1, chips):
        item = push(own_rows, rows_all.at[s], ss_row.at[d], rs_row.at[d], shard=mates[d - 1])
        item.start()
        first.append(item)
    item = push(own_rows, rows_all.at[s], ss_fwd.at[0], rs_fwd.at[0], shard=sibling)
    item.start()
    waits.append(item)
    w_waits = []
    for i, peer in enumerate(others):
        from_q = w_query.at[:, pl.ds(pl.multiple_of(peer * cols, cols), cols)]
        item = push(from_q, w_all.at[s, :, pl.ds(0, cols)], ss_w.at[i], rs_w.at[i], shard=peer)
        item.start()
        w_waits.append(item)
        head = pl.ds(pl.multiple_of(lax.div(peer, sharers) * HEAD_DIM, HEAD_DIM), HEAD_DIM)
        for kind, ref in enumerate((key_w, value_w)):
            item = push(ref.at[:, head], w_all.at[s, :, pl.ds(cols, HEAD_DIM)], ss_k.at[i], rs_k.at[i], shard=peer)

            @pl.when(lax.rem(peer, 2) == kind)
            def _(item=item):
                item.start()

        w_waits.append(item)
        item = push(router, router_all.at[:, pl.ds(pl.multiple_of(s * wr, wr), wr)], ss_rt.at[i], rs_rt.at[i], shard=peer)
        item.start()
        waits.append(item)
    copies = [
        pltpu.make_async_copy(own_rows, rows_all.at[s], local.at[0]),
        pltpu.make_async_copy(w_query.at[:, pl.ds(pl.multiple_of(s * cols, cols), cols)],
                              w_all.at[s, :, pl.ds(0, cols)], local.at[1]),
        pltpu.make_async_copy(routes, zroutes.at[c], local.at[2]),
        pltpu.make_async_copy(router, router_all.at[:, pl.ds(pl.multiple_of(s * wr, wr), wr)], local.at[3]),
        pltpu.make_async_copy(cot, zcot.at[c], local.at[4]),
    ]
    for item in copies:
        item.start()
    head = pl.ds(pl.multiple_of(lax.div(s, sharers) * HEAD_DIM, HEAD_DIM), HEAD_DIM)
    for kind, ref in enumerate((key_w, value_w)):
        own_head = pltpu.make_async_copy(ref.at[:, head], w_all.at[s, :, pl.ds(cols, HEAD_DIM)], local.at[5])

        @pl.when(parity == kind)
        def _(own_head=own_head):
            own_head.start()

    copies[2].wait()
    for d in route_fan.order():
        route_fan.arrival(d)
    before = (
        lax.broadcasted_iota(jnp.int32, (count, count), 0) < lax.broadcasted_iota(jnp.int32, (count, count), 1)
    ).astype(BF)
    for layer in range(n_ctx):
        named = zroutes[layer]
        mask = jnp.concatenate(
            [jnp.max((named == c * n_shard + e).astype(F32), axis=0, keepdims=True) for e in range(n_shard)], axis=0
        )
        rank = jnp.dot(mask.astype(BF), before, preferred_element_type=F32)
        at = layer % group
        code[layer // group, :, at * count : (at + 1) * count] = jnp.where(
            mask > 0, rank + float(at * capacity), -1.0
        )

    for d in range(1, chips):
        first[d - 1].wait()
        origin = lax.rem(s + n_shard - 2 * d, n_shard)
        item = push(rows_all.at[origin], rows_all.at[origin], ss_fwd.at[d], rs_fwd.at[d], shard=sibling)
        item.start()
        waits.append(item)
    for d in cot_fan.order():
        cot_fan.arrival(d)
    copies[4].wait()
    for k in range(groups):
        table = slot_table(code[k], slots)

        @pl.loop(0, width // tile)
        def _(j):
            part = pl.ds(pl.multiple_of(j * tile, tile), tile)
            block = zcot[k * group : (k + 1) * group, :, part].reshape(group * count, tile)
            value = jnp.dot(table, block, preferred_element_type=F32).astype(BF)
            ready[k, :, :, part] = value.reshape(n_shard, slots, tile)

    for item in waits + w_waits:
        item.wait()
    copies[0].wait()
    copies[1].wait()
    copies[3].wait()
    own_head.wait()
    outs = [
        pltpu.make_async_copy(rows_all, rows_out, out_sem.at[0]),
        pltpu.make_async_copy(w_all, w_all_out, out_sem.at[1]),
    ]
    outs[0].start()
    outs[1].start()

    right = w_all[:, :, pl.ds(cols, HEAD_DIM)].reshape(width, HEAD_DIM)

    @pl.loop(0, n_shard)
    def _(b):
        pre = jnp.dot(rows_all[b], right, preferred_element_type=F32)
        kvpre[b] = pre
        keyed, unused = unit_rows(pre)
        keyed = turn(keyed * k_gain[...], cosine[...], sine[...])
        kv[parity, b, c] = jnp.where(parity == 0, keyed, pre).astype(BF)

    fan = Fan(n_ctx, c, lambda d: kv.at[parity, :, flip_bits(c, d)], ss_kz, rs_kz, False)
    fan.send(0, kv.at[parity, :, c])
    kv_waits = []
    item = push(kv.at[parity, :, c], kv.at[parity, :, c], ss_kf.at[0], rs_kf.at[0], shard=sibling)
    item.start()
    kv_waits.append(item)

    cot_waits = []
    for k in range(groups):
        for i, peer in enumerate(others):
            item = push(ready.at[k, peer], cot_rows.at[s, k], ss_x.at[k, i], rs_x.at[k, i], shard=peer)
            item.start()
            cot_waits.append(item)
        item = pltpu.make_async_copy(ready.at[k, s], cot_rows.at[s, k], local.at[6 + k])
        item.start()
        cot_waits.append(item)

    @pl.loop(0, n_shard // 2)
    def _(b):
        left = rows_all[pl.ds(b * 2, 2)].reshape(2 * count, width)
        pre = jnp.dot(left, w_all[:, :, pl.ds(0, cols)].reshape(width, cols), preferred_element_type=F32)
        qpre[pl.ds(b * 2, 2)] = pre.reshape(2, count, cols)
        for i in range(2):
            for h in range(heads):
                part = pre[i * count : (i + 1) * count, h * HEAD_DIM : (h + 1) * HEAD_DIM]
                unit, unused = unit_rows(part)
                q[b * 2 + i, :, h * HEAD_DIM : (h + 1) * HEAD_DIM] = turn(
                    unit * q_gain[...], cosine[...], sine[...]
                ).astype(BF)

    for d in fan.order():
        fan.arrival(d)
        block = kv.at[parity, :, flip_bits(c, d)]
        item = push(block, block, ss_kf.at[d], rs_kf.at[d], shard=sibling)
        item.start()
        kv_waits.append(item)
    outs += [pltpu.make_async_copy(qpre, qpre_out, out_sem.at[2]), pltpu.make_async_copy(q, q_out, out_sem.at[3])]
    outs[2].start()
    outs[3].start()
    for item in kv_waits:
        item.wait()
    fan.drain()
    outs.append(pltpu.make_async_copy(kv, kv_out, out_sem.at[4]))
    outs[4].start()

    near, far = {}, {}
    order = list(range(1, chips)) + [0]

    def product(at):
        d = order[at]
        first_seq = 2 * lax.rem(chip + d, chips)

        @pl.loop(0, 2)
        def _(i):
            b = first_seq + i
            k_all = kv[0, b].reshape(keys, HEAD_DIM)
            v_all = kv[1, b].reshape(keys, HEAD_DIM)
            for h in range(heads):
                hs = slice(h * HEAD_DIM, (h + 1) * HEAD_DIM)
                scores = lax.dot_general(q[b, :, hs], k_all, (((1,), (1,)), ((), ())), preferred_element_type=F32)
                scores = scores * (HEAD_DIM ** -0.5) + bias[...]
                raised = jnp.exp(scores - jnp.max(scores, axis=-1, keepdims=True))
                probs = raised / jnp.sum(raised, axis=-1, keepdims=True)
                attn[b, :, hs] = jnp.dot(probs.astype(BF), v_all, preferred_element_type=F32).astype(BF)

        left = attn[pl.ds(first_seq, 2)].reshape(2 * count, cols)

        @pl.loop(0, width // tile)
        def _(j):
            part = pl.ds(pl.multiple_of(j * tile, tile), tile)
            value = jnp.dot(left, w_out[:, part], preferred_element_type=F32)
            pair[...] = value.reshape(2, count, tile)
            own_part[at % 2, :, part] = pair[parity]
            to_sib[at, :, part] = pair[1 - parity].astype(BF)

        near[at] = push(to_sib.at[at], sib.at[at], ss_s.at[at], rs_s.at[at], shard=sibling)
        near[at].start()

    def chip_sum(at):
        near[at].wait()
        to_chip[at] = (own_part[at % 2] + sib[at].astype(F32)).astype(BF)
        far[at] = push(to_chip.at[at], got.at[at], ss_c.at[at], rs_c.at[at], shard=mates[order[at] - 1])
        far[at].start()

    for at in range(chips):
        product(at)
        if at:
            chip_sum(at - 1)
    outs.append(pltpu.make_async_copy(attn, attn_out, out_sem.at[5]))
    outs[5].start()
    near[chips - 1].wait()
    mid[...] = tokens[...].astype(F32) + own_part[(chips - 1) % 2] + sib[chips - 1].astype(F32)
    for at in range(chips - 1):
        far[at].wait()
        mid[...] += got[at].astype(F32)
    cot_fan.drain()
    route_fan.drain()
    for item in cot_waits + outs:
        item.wait()


def front(n_ctx, n_shard, group, capacity, kv_heads, args, ident):
    tokens, gain, w_query, key_w, value_w, routes, router, cot = args[:8]
    n, z = n_shard, n_ctx
    count, width = tokens.shape
    wr, chips, groups, slots = w_query.shape[0], n_shard // 2, n_ctx // group, group * capacity
    cols = w_query.shape[1] // n
    heads = cols // HEAD_DIM
    sds = jax.ShapeDtypeStruct
    dma = lambda *shape: DMA(shape)
    return call(
        functools.partial(front_body, z, n, group, capacity, heads, kv_heads, 512),
        [
            sds((n, count, width), BF), sds((n, wr, cols + HEAD_DIM), BF), sds((router.shape[0], width), BF),
            sds((groups, n, group * count), F32), sds((n, groups, slots, width), BF), sds((n, count, cols), F32),
            sds((n, count, HEAD_DIM), F32), sds((n, count, cols), BF), sds((2, n, z, count, HEAD_DIM), BF),
            sds((n, count, cols), BF), sds((count, width), F32),
        ],
        [VMEM, VMEM, ANY, ANY, ANY, VMEM, ANY, ANY] + [VMEM] * 6,
        [
            pltpu.VMEM((count, width), BF), pltpu.VMEM((n, count, width), BF), pltpu.VMEM((n, wr, cols + HEAD_DIM), BF),
            pltpu.VMEM((z,) + routes.shape, jnp.int32), pltpu.VMEM((z, count, width), BF),
            pltpu.VMEM((groups, n, slots, width), BF), pltpu.VMEM((n, count, cols), F32),
            pltpu.VMEM((n, count, cols), BF), pltpu.VMEM((2, n, z, count, HEAD_DIM), BF),
            pltpu.VMEM((n, count, cols), BF), pltpu.VMEM((2, count, width), F32), pltpu.VMEM((2, count, 512), F32),
            pltpu.VMEM((chips, count, width), BF), pltpu.VMEM((chips, count, width), BF),
            pltpu.VMEM((chips - 1, count, width), BF), pltpu.VMEM((chips - 1, count, width), BF),
            dma(6 + groups), dma(chips), dma(chips), dma(chips), dma(chips), dma(n - 1), dma(n - 1), dma(n - 1), dma(n - 1),
            dma(n - 1), dma(n - 1), dma(z), dma(z), dma(z), dma(z), dma(groups, n - 1), dma(groups, n - 1),
            dma(z), dma(z), dma(z), dma(z), dma(chips), dma(chips), dma(chips - 1), dma(chips - 1), dma(6),
        ],
        ident, args, mib=60,
        out_specs=[ANY, ANY, ANY, VMEM, ANY, ANY, VMEM, ANY, ANY, ANY, VMEM],
    )


def spread_body(n_shard, rows, rows_all, local, ss_row, rs_row, ss_fwd, rs_fwd):
    c, s, parity, sibling, others, layers = here(1, n_shard)
    chips = n_shard // 2
    mates = [lax.rem(s + 2 * d, n_shard) for d in range(1, chips)]
    greet(mates + [sibling], [])
    mine = pltpu.make_async_copy(rows, rows_all.at[s], local)
    mine.start()
    first, waits = [], []
    for d in range(1, chips):
        item = push(rows, rows_all.at[s], ss_row.at[d], rs_row.at[d], shard=mates[d - 1])
        item.start()
        first.append(item)
    item = push(rows, rows_all.at[s], ss_fwd.at[0], rs_fwd.at[0], shard=sibling)
    item.start()
    waits.append(item)
    for d in range(1, chips):
        first[d - 1].wait()
        origin = lax.rem(s + n_shard - 2 * d, n_shard)
        item = push(rows_all.at[origin], rows_all.at[origin], ss_fwd.at[d], rs_fwd.at[d], shard=sibling)
        item.start()
        waits.append(item)
    mine.wait()
    for item in waits:
        item.wait()


def spread(n_shard, rows, ident):
    return call(
        functools.partial(spread_body, n_shard),
        [jax.ShapeDtypeStruct((n_shard,) + rows.shape, rows.dtype)],
        [ANY], [DMA] + [DMA((n_shard // 2,))] * 4, ident, (rows,),
    )[0]


def key_back_body(n_ctx, n_shard, parts, out, sib, zsend, zrecv, ss_s, rs_s, ss_z, rs_z):
    c, s, parity, sibling, others, layers = here(n_ctx, n_shard)
    greet([sibling], layers)
    order = list(range(1, n_ctx)) + [0]
    near = {}
    for d in order:
        block = parts.at[1 - parity, :, lax.rem(c + d, n_ctx)]
        near[d] = push(block, sib.at[d], ss_s.at[d], rs_s.at[d], shard=sibling)
        near[d].start()
    far = {}
    for d in order:
        near[d].wait()
        layer = lax.rem(c + d, n_ctx)
        value = parts[parity, :, layer].astype(F32) + sib[d].astype(F32)
        if d:
            zsend[d - 1] = value.astype(BF)
            far[d] = push(zsend.at[d - 1], zrecv.at[d - 1], ss_z.at[d], rs_z.at[d], ctx=layer)
            far[d].start()
    for d in range(1, n_ctx):
        far[d].wait()
        value = value + zrecv[d - 1].astype(F32)
    out[...] = value


def key_back(n_ctx, n_shard, parts, ident):
    block = (parts.shape[1], parts.shape[3], parts.shape[4])
    return call(
        functools.partial(key_back_body, n_ctx, n_shard),
        [jax.ShapeDtypeStruct(block, F32)],
        [VMEM],
        [
            pltpu.VMEM((n_ctx,) + block, BF), pltpu.VMEM((n_ctx - 1,) + block, BF),
            pltpu.VMEM((n_ctx - 1,) + block, BF),
        ] + [DMA((n_ctx,))] * 4,
        ident, (parts,), out_specs=[VMEM],
    )[0]


def finish_body(n_ctx, n_shard, q_cols, tile,
                weights, wide, router, gains, left, right, tokens, gain,
                q_out, kv_out, wide_out, router_out, gains_out, rows_out,
                wide_landing, wide_acc, wide_total, ss_wi, rs_wi, ss_wo, ss_wc, pieces, landing, acc, total, router_in, router_mid, router_far,
                gains_own, gains_in, gains_mid, gains_far, pair, own_part, to_sib, sib, to_chip, got,
                local, ss_w, rs_w, ss_i, rs_i, ss_o, ss_q, ss_k, ss_r, rs_r, ss_g, rs_g, ss_h, rs_h,
                ss_t, rs_t, ss_s, rs_s, ss_c, rs_c):
    c, s, parity, sibling, others, layers = here(n_ctx, n_shard)
    half = n_ctx // 2
    chips = n_shard // 2
    chip = lax.div(s, 2)
    mates = [lax.rem(s + 2 * d, n_shard) for d in range(1, chips)]
    left_side = c < half
    depth = jnp.where(left_side, c, n_ctx - 1 - c)
    inner = jnp.where(left_side, c + 1, c - 1)
    outer = jnp.clip(jnp.where(left_side, c - 1, c + 1), 0, n_ctx - 1)
    middle = depth == half - 1
    inside = depth > 0
    rows, width = rows_out.shape
    greet(others, layers)
    sends, small = [None], []
    for i, peer in enumerate(others):
        item = push(weights.at[peer], pieces.at[i + 1], ss_w.at[i], rs_w.at[i], shard=peer)
        item.start()
        sends.append(item)
    for i, peer in enumerate(others):
        item = push(router.at[peer], router_in.at[i], ss_r.at[i], rs_r.at[i], shard=peer)
        item.start()
        small.append(item)

    def out_copies(j, ref):
        source = lax.rem(s + n_shard - j, n_shard)
        cols = pl.ds(pl.multiple_of(source * q_cols, q_cols), q_cols)
        return (
            pltpu.make_async_copy(ref.at[:, pl.ds(0, q_cols)], q_out.at[:, cols], ss_q.at[j]),
            pltpu.make_async_copy(ref.at[:, pl.ds(q_cols, 128)], kv_out.at[source], ss_k.at[j]),
        )

    def wide_copies(j, ref):
        return (pltpu.make_async_copy(ref, wide_out.at[j], ss_wc.at[j]),)

    class Line:
        def __init__(self, ready, own, acc, landing, total, ss_i, rs_i, ss_o, copies):
            self.ready, self.own, self.acc, self.landing, self.total = ready, own, acc, landing, total
            self.ss_i, self.rs_i, self.ss_o, self.copies = ss_i, rs_i, ss_o, copies

        def inward(self, j, ref):
            at = jnp.where(middle, 1, 0)
            return push(ref, self.landing.at[at, j], self.ss_i.at[j], self.rs_i.at[at, j], ctx=inner)

        def outward(self, j):
            return push(self.total.at[j], self.landing.at[1, j], self.ss_o.at[j], self.rs_i.at[1, j], ctx=outer)

        def arrived(self, which, j):
            push(self.acc.at[j], self.landing.at[which, j], self.ss_i.at[j], self.rs_i.at[which, j],
                 ctx=inner).wait_recv()

        def outermost(self, j):
            @pl.when(jnp.logical_not(inside))
            def _():
                self.ready(j)
                self.inward(j, self.own(j)).start()

        def first_half(self, j):
            @pl.when(inside)
            def _():
                self.ready(j)
                self.arrived(0, j)
                self.acc[j] = (self.own(j)[...].astype(F32) + self.landing[0, j].astype(F32)).astype(BF)
                self.inward(j, self.acc.at[j]).start()

        def second_half(self, j):
            self.arrived(1, j)

            @pl.when(middle)
            def _():
                self.total[j] = (self.acc[j].astype(F32) + self.landing[1, j].astype(F32)).astype(BF)

            @pl.when(jnp.logical_not(middle))
            def _():
                self.total[j] = self.landing[1, j]

            @pl.when(inside)
            def _():
                self.outward(j).start()

            for item in self.copies(j, self.total.at[j]):
                item.start()

        def drain(self, j):
            self.inward(j, self.acc.at[j]).wait_send()

            @pl.when(inside)
            def _():
                self.outward(j).wait_send()

            for item in self.copies(j, self.total.at[j]):
                item.wait()

    line = Line(lambda j: sends[j].wait() if j else None, lambda j: pieces.at[j] if j else weights.at[s],
                acc, landing, total, ss_i, rs_i, ss_o, out_copies)
    wide_line = Line(lambda j: None, lambda j: wide.at[j], wide_acc, wide_landing, wide_total,
                     ss_wi, rs_wi, ss_wo, wide_copies)
    wides = wide.shape[0]
    steps = [(wide_line, j) for j in range(wides)] + [(line, j) for j in range(n_shard)]

    near, far = {}, {}

    def product(d):
        first = pl.multiple_of(lax.rem(chip + d, chips) * (2 * rows), 2 * rows)

        @pl.loop(0, width // tile)
        def _(j):
            cols = pl.ds(pl.multiple_of(j * tile, tile), tile)
            value = lax.dot_general(left[pl.ds(first, 2 * rows), :], right[cols, :],
                                    (((1,), (1,)), ((), ())), preferred_element_type=F32)
            pair[...] = value.reshape(2, rows, tile)
            own_part[d, :, cols] = pair[parity]
            to_sib[d, :, cols] = pair[1 - parity].astype(BF)

        near[d] = push(to_sib.at[d], sib.at[d], ss_s.at[d], rs_s.at[d], shard=sibling)
        near[d].start()

    def chip_sum(d):
        near[d].wait()
        to_chip[d - 1] = (own_part[d] + sib[d].astype(F32)).astype(BF)
        far[d] = push(to_chip.at[d - 1], got.at[d - 1], ss_c.at[d - 1], rs_c.at[d - 1], shard=mates[d - 1])
        far[d].start()

    gain_sends = []

    def last_sum():
        near[0].wait()
        grad = own_part[0] + sib[0].astype(F32)
        for d in range(1, chips):
            far[d].wait()
            grad = grad + got[d - 1].astype(F32)
        x = tokens[...].astype(F32)
        scale = lax.rsqrt(jnp.mean(x * x, axis=-1, keepdims=True) + epsilon)
        unit = x * scale
        scaled = grad * gain[...]
        rows_out[...] = scale * (scaled - unit * jnp.mean(scaled * unit, axis=-1, keepdims=True))
        gains_own[...] = gains[...]
        gains_own[0:1] = jnp.sum(grad * unit, axis=0, keepdims=True)
        mine = pltpu.make_async_copy(gains_own, gains_in.at[s], local.at[0])
        mine.start()
        gain_sends.append(mine)
        for i, peer in enumerate(others):
            item = push(gains_own, gains_in.at[s], ss_g.at[i], rs_g.at[i], shard=peer)
            item.start()
            gain_sends.append(item)

    def small_plane():
        for item in small + gain_sends:
            item.wait()
        gains_mid[...] = gains_in[0]
        for i in range(1, n_shard):
            gains_mid[...] += gains_in[i]
        router_mid[...] = router[s].astype(F32)
        for i in range(n_shard - 1):
            router_mid[...] += router_in[i].astype(F32)
        for i, layer in enumerate(layers):
            push(gains_mid, gains_far.at[c], ss_h.at[i], rs_h.at[i], ctx=layer).start()
            push(router_mid, router_far.at[c], ss_t.at[i], rs_t.at[i], ctx=layer).start()
        pltpu.make_async_copy(gains_mid, gains_far.at[c], local.at[1]).start()
        pltpu.make_async_copy(router_mid, router_far.at[c], local.at[2]).start()

    def small_all():
        pltpu.make_async_copy(gains_mid, gains_far.at[c], local.at[1]).wait()
        pltpu.make_async_copy(router_mid, router_far.at[c], local.at[2]).wait()
        for i, layer in enumerate(layers):
            push(gains_mid, gains_far.at[c], ss_h.at[i], rs_h.at[i], ctx=layer).wait()
            push(router_mid, router_far.at[c], ss_t.at[i], rs_t.at[i], ctx=layer).wait()
        gains_out[...] = gains_far[0]
        router_out[...] = router_far[0]
        for i in range(1, n_ctx):
            gains_out[...] += gains_far[i]
            router_out[...] += router_far[i]

    lag, ahead = 2, 6
    for which, j in steps[:ahead]:
        which.outermost(j)
    for d in list(range(1, chips)) + [0]:
        product(d)
    side = [functools.partial(chip_sum, d) for d in range(1, chips)] + [last_sum, small_plane]
    for n in range(len(steps) + lag):
        if n + ahead < len(steps):
            steps[n + ahead][0].outermost(steps[n + ahead][1])
        if n < len(steps):
            steps[n][0].first_half(steps[n][1])
        if n >= lag:
            steps[n - lag][0].second_half(steps[n - lag][1])
        if n >= 2 and side:
            side.pop(0)()
    for job in side:
        job()
    small_all()
    for which, j in steps:
        which.drain(j)


def finish(n_ctx, n_shard, q_cols, weights, wide, router, gains, left, right, tokens, gain, ident):
    n, rows, cols = weights.shape
    router_shape = router.shape[1:]
    count, width = tokens.shape
    chips = n // 2
    tile = 512
    wides = wide.shape[0]
    return call(
        functools.partial(finish_body, n_ctx, n, q_cols, tile),
        [
            jax.ShapeDtypeStruct((rows, n * q_cols), BF), jax.ShapeDtypeStruct((n, rows, 128), BF),
            jax.ShapeDtypeStruct(wide.shape, BF),
            jax.ShapeDtypeStruct(router_shape, F32), jax.ShapeDtypeStruct(gains.shape, F32),
            jax.ShapeDtypeStruct((count, width), F32),
        ],
        [VMEM] * 8,
        [
            pltpu.VMEM((2,) + wide.shape, BF), pltpu.VMEM(wide.shape, BF), pltpu.VMEM(wide.shape, BF),
            DMA((wides,)), DMA((2, wides)), DMA((wides,)), DMA((wides,)),
            pltpu.VMEM((n, rows, cols), BF), pltpu.VMEM((2, n, rows, cols), BF),
            pltpu.VMEM((n, rows, cols), BF), pltpu.VMEM((n, rows, cols), BF),
            pltpu.VMEM((n - 1,) + router_shape, BF), pltpu.VMEM(router_shape, F32),
            pltpu.VMEM((n_ctx,) + router_shape, F32),
            pltpu.VMEM(gains.shape, F32), pltpu.VMEM((n,) + gains.shape, F32),
            pltpu.VMEM(gains.shape, F32), pltpu.VMEM((n_ctx,) + gains.shape, F32),
            pltpu.VMEM((2, count, tile), F32), pltpu.VMEM((chips, count, width), F32),
            pltpu.VMEM((chips, count, width), BF), pltpu.VMEM((chips, count, width), BF),
            pltpu.VMEM((chips - 1, count, width), BF), pltpu.VMEM((chips - 1, count, width), BF),
            DMA((3,)), DMA((n - 1,)), DMA((n - 1,)), DMA((n,)), DMA((2, n)), DMA((n,)),
            DMA((n,)), DMA((n,)), DMA((n - 1,)), DMA((n - 1,)), DMA((n - 1,)), DMA((n - 1,)),
            DMA((n_ctx - 1,)), DMA((n_ctx - 1,)), DMA((n_ctx - 1,)), DMA((n_ctx - 1,)),
            DMA((chips,)), DMA((chips,)), DMA((chips - 1,)), DMA((chips - 1,)),
        ],
        ident, (weights, wide, router, gains, left, right, tokens, gain), mib=60,
        out_specs=[ANY, ANY, ANY, VMEM, VMEM, VMEM],
    )


def back_body(n_ctx, n_shard, heads, wides,
              grad_out, q, kv, attn, qpre, kvpre, w_out, rows_in, w_all, cosine, sine, bias, q_gain, k_gain,
              tokens, gain, gains, router,
              q_out, kv_out, wide_out, router_out, gains_out, rows_out,
              grads, rows_all, attn_t, grad_heads, ds_all, p_all, parts, pre, q_sum, k_sum, wide, weights,
              sibk, zsend, zrecv, wide_landing, pieces, landing,
              own_part, pair, to_sib, sib, to_chip, got, router_in, router_mid, router_far,
              gains_own, gains_in, gains_mid, gains_far, local,
              ss_row, rs_row, ss_fwd, rs_fwd, ss_sk, rs_sk, ss_zk, rs_zk,
              ss_wi, rs_wi, ss_wo, ss_wc, ss_w, rs_w, ss_i, rs_i, ss_o, ss_q, ss_k,
              ss_r, rs_r, ss_g, rs_g, ss_h, rs_h, ss_t, rs_t, ss_s, rs_s, ss_c, rs_c):
    c, s, parity, sibling, others, layers = here(n_ctx, n_shard)
    half = n_ctx // 2
    chips = n_shard // 2
    chip = lax.div(s, 2)
    mates = [lax.rem(s + 2 * d, n_shard) for d in range(1, chips)]
    left_side = c < half
    depth = jnp.where(left_side, c, n_ctx - 1 - c)
    inner = jnp.where(left_side, c + 1, c - 1)
    outer = jnp.clip(jnp.where(left_side, c - 1, c + 1), 0, n_ctx - 1)
    middle = depth == half - 1
    inside = depth > 0
    count, width = tokens.shape
    wr = w_all.shape[1]
    cols = heads * HEAD_DIM
    keys = n_ctx * count
    scaling = HEAD_DIM ** -0.5
    own_copies = [
        pltpu.make_async_copy(grad_out, grads.at[s], local.at[0]),
        pltpu.make_async_copy(rows_in, rows_all, local.at[1]),
    ]
    for item in own_copies:
        item.start()
    greet(others, layers)

    first, forwards = {}, {}
    for d in range(1, chips):
        first[d] = push(grad_out, grads.at[s], ss_row.at[d], rs_row.at[d], shard=mates[d - 1])
        first[d].start()
    forwards[0] = push(grad_out, grads.at[s], ss_fwd.at[0], rs_fwd.at[0], shard=sibling)
    forwards[0].start()
    small = []
    for i, peer in enumerate(others):
        item = push(router.at[peer], router_in.at[i], ss_r.at[i], rs_r.at[i], shard=peer)
        item.start()
        small.append(item)
    q_sum[...] = jnp.zeros_like(q_sum)
    k_sum[...] = jnp.zeros_like(k_sum)

    def norm_back(grad, value, norm_gain, total):
        unit, scale = unit_rows(value)
        grad = grad * cosine[...] + pltpu.roll(grad * sine[...], HEAD_DIM // 2, 1)
        total[...] += jnp.sum(grad * unit, axis=0, keepdims=True)
        scaled = grad * norm_gain[...]
        return scale * (scaled - unit * jnp.mean(scaled * unit, axis=-1, keepdims=True))

    near, far = {}, {}

    def seqs_of(d):
        return 2 * lax.rem(chip + chips - d, chips)

    def attention_back(d):
        fs = seqs_of(d)
        grad = lax.dot_general(grads[pl.ds(fs, 2)].reshape(2 * count, width), w_out[...],
                               (((1,), (1,)), ((), ())), preferred_element_type=F32)
        grad_heads[...] = grad.reshape(2, count, cols).astype(BF)

        @pl.loop(0, 2)
        def _(i):
            b = fs + i
            k_all = kv[0, b].reshape(keys, HEAD_DIM)
            v_all = kv[1, b].reshape(keys, HEAD_DIM)
            for h in range(heads):
                hs = slice(h * HEAD_DIM, (h + 1) * HEAD_DIM)
                rs = slice(h * count, (h + 1) * count)
                scores = lax.dot_general(q[b, :, hs], k_all, (((1,), (1,)), ((), ())), preferred_element_type=F32)
                scores = scores * scaling + bias[...]
                raised = jnp.exp(scores - jnp.max(scores, axis=-1, keepdims=True))
                probs = raised / jnp.sum(raised, axis=-1, keepdims=True)
                grad_p = lax.dot_general(grad_heads[i, :, hs], v_all, (((1,), (1,)), ((), ())),
                                         preferred_element_type=F32)
                delta = jnp.sum(probs * grad_p, axis=-1, keepdims=True)
                ds = (probs * (grad_p - delta)).astype(BF)
                ds_all[rs, :] = ds
                p_all[rs, :] = probs.astype(BF)
                grad_q = jnp.dot(ds, k_all, preferred_element_type=F32) * scaling
                pre[b, :, hs] = norm_back(grad_q, qpre[b, :, hs], q_gain, q_sum).astype(BF)
            grad_k, grad_v = jnp.zeros((keys, HEAD_DIM), F32), jnp.zeros((keys, HEAD_DIM), F32)
            stacked_q = jnp.concatenate([q[b, :, h * HEAD_DIM : (h + 1) * HEAD_DIM] for h in range(heads)], axis=0)
            stacked_g = jnp.concatenate(
                [grad_heads[i, :, h * HEAD_DIM : (h + 1) * HEAD_DIM] for h in range(heads)], axis=0
            )
            grad_k = lax.dot_general(ds_all[...], stacked_q, (((0,), (0,)), ((), ())), preferred_element_type=F32)
            grad_v = lax.dot_general(p_all[...], stacked_g, (((0,), (0,)), ((), ())), preferred_element_type=F32)
            parts[0, b] = (grad_k * scaling).astype(BF).reshape(n_ctx, count, HEAD_DIM)
            parts[1, b] = grad_v.astype(BF).reshape(n_ctx, count, HEAD_DIM)

        near[d] = push(parts.at[1 - parity, pl.ds(fs, 2)], sibk.at[d], ss_sk.at[d], rs_sk.at[d], shard=sibling)
        near[d].start()

    def key_sum(d):
        fs = seqs_of(d)
        near[d].wait()
        for i, layer in enumerate(layers):
            zsend[d, i] = (
                parts[parity, pl.ds(fs, 2), layer].astype(F32) + sibk[d, :, layer].astype(F32)
            ).astype(BF)
            far[d, i] = push(zsend.at[d, i], zrecv.at[d, i], ss_zk.at[d, i], rs_zk.at[d, i], ctx=layer)
            far[d, i].start()

    for d in range(chips):
        if d:
            first[d].wait()
            origin = lax.rem(s + n_shard - 2 * d, n_shard)
            forwards[d] = push(grads.at[origin], grads.at[origin], ss_fwd.at[d], rs_fwd.at[d], shard=sibling)
            forwards[d].start()
        else:
            own_copies[0].wait()
        forwards[d].wait()
        attention_back(d)
        if d:
            key_sum(d - 1)
    key_sum(chips - 1)

    def out_copies(j, ref):
        source = lax.rem(s + n_shard - j, n_shard)
        to = pl.ds(pl.multiple_of(source * cols, cols), cols)
        return (
            pltpu.make_async_copy(ref.at[:, pl.ds(0, cols)], q_out.at[:, to], ss_q.at[j]),
            pltpu.make_async_copy(ref.at[:, pl.ds(cols, HEAD_DIM)], kv_out.at[source], ss_k.at[j]),
        )

    def wide_copies(j, ref):
        step = wide.shape[2]
        return (pltpu.make_async_copy(ref, wide_out.at[:, pl.ds(j * step, step)], ss_wc.at[j]),)

    class Line:
        def __init__(self, ready, own, landing, ss_i, rs_i, ss_o, copies):
            self.ready, self.own, self.landing = ready, own, landing
            self.ss_i, self.rs_i, self.ss_o, self.copies = ss_i, rs_i, ss_o, copies

        def inward(self, j, ref):
            at = jnp.where(middle, 1, 0)
            return push(ref, self.landing.at[at, j], self.ss_i.at[j], self.rs_i.at[at, j], ctx=inner)

        def outward(self, j):
            return push(self.landing.at[1, j], self.landing.at[1, j], self.ss_o.at[j], self.rs_i.at[1, j], ctx=outer)

        def arrived(self, which, j):
            push(self.landing.at[0, j], self.landing.at[which, j], self.ss_i.at[j], self.rs_i.at[which, j],
                 ctx=inner).wait_recv()

        def outermost(self, j):
            @pl.when(jnp.logical_not(inside))
            def _():
                self.ready(j)
                self.inward(j, self.own(j)).start()

        def first_half(self, j):
            @pl.when(inside)
            def _():
                self.ready(j)
                self.arrived(0, j)
                self.landing[0, j] = (self.own(j)[...].astype(F32) + self.landing[0, j].astype(F32)).astype(BF)
                self.inward(j, self.landing.at[0, j]).start()

        def second_half(self, j):
            self.arrived(1, j)

            @pl.when(middle)
            def _():
                self.landing[1, j] = (self.landing[0, j].astype(F32) + self.landing[1, j].astype(F32)).astype(BF)

            @pl.when(inside)
            def _():
                self.outward(j).start()

            for item in self.copies(j, self.landing.at[1, j]):
                item.start()

        def drain(self, j):
            self.inward(j, self.landing.at[0, j]).wait_send()

            @pl.when(inside)
            def _():
                self.outward(j).wait_send()

            for item in self.copies(j, self.landing.at[1, j]):
                item.wait()

    sends = [None]
    line = Line(lambda j: sends[j].wait() if j else None, lambda j: pieces.at[j] if j else weights.at[s],
                landing, ss_i, rs_i, ss_o, out_copies)
    wide_line = Line(lambda j: None, lambda j: wide.at[j], wide_landing, ss_wi, rs_wi, ss_wo, wide_copies)
    steps = [(wide_line, j) for j in range(wides)] + [(line, j) for j in range(n_shard)]
    lag, ahead = 2, 6

    attn_t[...] = attn[...].reshape(n_shard * count, cols).T
    step = width // wides
    for j in range(wides):
        block = grads[:, :, j * step : (j + 1) * step].reshape(n_shard * count, step)
        wide[j] = jnp.dot(attn_t[...], block, preferred_element_type=F32).astype(BF)
        if j < ahead:
            wide_line.outermost(j)

    own_copies[1].wait()

    @pl.loop(0, n_shard)
    def _(e):
        block = rows_all[:, :, pl.ds(pl.multiple_of(e * wr, wr), wr)].reshape(n_shard * count, wr)
        right = pre[:, :, pl.ds(0, cols)].reshape(n_shard * count, cols)
        weights[e, :, pl.ds(0, cols)] = lax.dot_general(
            block, right, (((0,), (0,)), ((), ())), preferred_element_type=F32).astype(BF)

    wide_line.first_half(0)
    for d in range(chips):
        fs = seqs_of(d)
        total = parts[parity, pl.ds(fs, 2), c].astype(F32) + sibk[d, :, c].astype(F32)
        for i in range(n_ctx - 1):
            far[d, i].wait()
            total = total + zrecv[d, i].astype(F32)
        for i in range(2):
            keyed = norm_back(total[i], kvpre[fs + i], k_gain, k_sum)
            pre[fs + i, :, pl.ds(cols, HEAD_DIM)] = jnp.where(parity == 0, keyed, total[i]).astype(BF)

    @pl.loop(0, n_shard)
    def _(e):
        block = rows_all[:, :, pl.ds(pl.multiple_of(e * wr, wr), wr)].reshape(n_shard * count, wr)
        right = pre[:, :, pl.ds(cols, HEAD_DIM)].reshape(n_shard * count, HEAD_DIM)
        weights[e, :, pl.ds(cols, HEAD_DIM)] = lax.dot_general(
            block, right, (((0,), (0,)), ((), ())), preferred_element_type=F32).astype(BF)

    for i, peer in enumerate(others):
        item = push(weights.at[peer], pieces.at[i + 1], ss_w.at[i], rs_w.at[i], shard=peer)
        item.start()
        sends.append(item)

    order = list(range(1, chips)) + [0]
    to_sibling, to_mate = {}, {}

    def product(at):
        fs = 2 * lax.rem(chip + order[at], chips)
        left = pre[pl.ds(fs, 2)].reshape(2 * count, cols + HEAD_DIM)

        @pl.loop(0, n_shard)
        def _(j):
            part = pl.ds(pl.multiple_of(j * wr, wr), wr)
            value = lax.dot_general(left, w_all[j], (((1,), (1,)), ((), ())), preferred_element_type=F32)
            pair[...] = value.reshape(2, count, wr)
            own_part[at % 2, :, part] = pair[parity]
            to_sib[at, :, part] = pair[1 - parity].astype(BF)

        to_sibling[at] = push(to_sib.at[at], sib.at[at], ss_s.at[at], rs_s.at[at], shard=sibling)
        to_sibling[at].start()

    def chip_sum(at):
        to_sibling[at].wait()
        to_chip[at] = (own_part[at % 2] + sib[at].astype(F32)).astype(BF)
        to_mate[at] = push(to_chip.at[at], got.at[at], ss_c.at[at], rs_c.at[at], shard=mates[order[at] - 1])
        to_mate[at].start()

    gain_sends = []

    def last_sum():
        to_sibling[chips - 1].wait()
        grad = own_part[(chips - 1) % 2] + sib[chips - 1].astype(F32)
        for at in range(chips - 1):
            to_mate[at].wait()
            grad = grad + got[at].astype(F32)
        unit, scale = unit_rows(tokens[...].astype(F32))
        scaled = grad * gain[...]
        rows_out[...] = scale * (scaled - unit * jnp.mean(scaled * unit, axis=-1, keepdims=True))
        gains_own[...] = gains[...]
        gains_own[0:1] = jnp.sum(grad * unit, axis=0, keepdims=True)
        gains_own[2:3, 0:HEAD_DIM] = q_sum[...]
        gains_own[2:3, HEAD_DIM : 2 * HEAD_DIM] = jnp.where(parity == 0, k_sum[...], jnp.zeros_like(k_sum))
        mine = pltpu.make_async_copy(gains_own, gains_in.at[s], local.at[2])
        mine.start()
        gain_sends.append(mine)
        for i, peer in enumerate(others):
            item = push(gains_own, gains_in.at[s], ss_g.at[i], rs_g.at[i], shard=peer)
            item.start()
            gain_sends.append(item)

    def small_plane():
        for item in small + gain_sends:
            item.wait()
        gains_mid[...] = gains_in[0]
        for i in range(1, n_shard):
            gains_mid[...] += gains_in[i]
        router_mid[...] = router[s].astype(F32)
        for i in range(n_shard - 1):
            router_mid[...] += router_in[i].astype(F32)
        for i, layer in enumerate(layers):
            push(gains_mid, gains_far.at[c], ss_h.at[i], rs_h.at[i], ctx=layer).start()
            push(router_mid, router_far.at[c], ss_t.at[i], rs_t.at[i], ctx=layer).start()
        pltpu.make_async_copy(gains_mid, gains_far.at[c], local.at[3]).start()
        pltpu.make_async_copy(router_mid, router_far.at[c], local.at[4]).start()

    def small_all():
        pltpu.make_async_copy(gains_mid, gains_far.at[c], local.at[3]).wait()
        pltpu.make_async_copy(router_mid, router_far.at[c], local.at[4]).wait()
        for i, layer in enumerate(layers):
            push(gains_mid, gains_far.at[c], ss_h.at[i], rs_h.at[i], ctx=layer).wait()
            push(router_mid, router_far.at[c], ss_t.at[i], rs_t.at[i], ctx=layer).wait()
        gains_out[...] = gains_far[0]
        router_out[...] = router_far[0]
        for i in range(1, n_ctx):
            gains_out[...] += gains_far[i]
            router_out[...] += router_far[i]

    side = []
    for at in range(chips):
        side.append(functools.partial(product, at))
        if at:
            side.append(functools.partial(chip_sum, at - 1))
    side += [last_sum, small_plane]
    for n in range(1, len(steps) + lag):
        if n + ahead - 1 < len(steps):
            steps[n + ahead - 1][0].outermost(steps[n + ahead - 1][1])
        if n < len(steps):
            steps[n][0].first_half(steps[n][1])
        if n >= lag:
            steps[n - lag][0].second_half(steps[n - lag][1])
        if side:
            side.pop(0)()
    for job in side:
        job()
    small_all()
    for which, j in steps:
        which.drain(j)


def back(n_ctx, n_shard, heads, args, ident):
    count, width = args[0].shape
    rows_in, w_all, router, gains = args[7], args[8], args[17], args[16]
    n, z, chips, wides = n_shard, n_ctx, n_shard // 2, 8
    wr, cols = w_all.shape[1], heads * HEAD_DIM
    keys = z * count
    sds, scratch = jax.ShapeDtypeStruct, pltpu.VMEM
    router_shape = router.shape[1:]
    dma = lambda *shape: DMA(shape)
    wide_block, block = (cols, width // wides), (wr, cols + HEAD_DIM)
    return call(
        functools.partial(back_body, z, n, heads, wides),
        [
            sds((wr, n * cols), BF), sds((n, wr, HEAD_DIM), BF), sds((cols, width), BF), sds(router_shape, F32),
            sds(gains.shape, F32), sds((count, width), F32),
        ],
        [VMEM] * 7 + [ANY] + [VMEM] * 10,
        [
            scratch((n, count, width), BF), scratch((n, count, width), BF), scratch((cols, n * count), BF),
            scratch((2, count, cols), BF), scratch((heads * count, keys), BF), scratch((heads * count, keys), BF),
            scratch((2, n, z, count, HEAD_DIM), BF), scratch((n, count, cols + HEAD_DIM), BF),
            scratch((1, HEAD_DIM), F32), scratch((1, HEAD_DIM), F32),
            scratch((wides,) + wide_block, BF), scratch((n,) + block, BF),
            scratch((chips, 2, z, count, HEAD_DIM), BF), scratch((chips, z - 1, 2, count, HEAD_DIM), BF),
            scratch((chips, z - 1, 2, count, HEAD_DIM), BF), scratch((2, wides) + wide_block, BF),
            scratch((n,) + block, BF), scratch((2, n) + block, BF),
            scratch((2, count, width), F32), scratch((2, count, wr), F32), scratch((chips, count, width), BF),
            scratch((chips, count, width), BF), scratch((chips - 1, count, width), BF),
            scratch((chips - 1, count, width), BF),
            scratch((n - 1,) + router_shape, BF), scratch(router_shape, F32), scratch((z,) + router_shape, F32),
            scratch(gains.shape, F32), scratch((n,) + gains.shape, F32), scratch(gains.shape, F32),
            scratch((z,) + gains.shape, F32), dma(5),
            dma(chips), dma(chips), dma(chips), dma(chips), dma(chips), dma(chips), dma(chips, z - 1), dma(chips, z - 1),
            dma(wides), dma(2, wides), dma(wides), dma(wides), dma(n - 1), dma(n - 1), dma(n), dma(2, n), dma(n), dma(n),
            dma(n), dma(n - 1), dma(n - 1), dma(n - 1), dma(n - 1), dma(z - 1), dma(z - 1), dma(z - 1), dma(z - 1),
            dma(chips), dma(chips), dma(chips - 1), dma(chips - 1),
        ],
        ident, args, mib=62, out_specs=[ANY, ANY, ANY, VMEM, VMEM, VMEM],
    )


def dispatch_body(n_ctx, n_shard, group, tile, rows, tail, code, recv, tail_recv,
                  zrows, ztail, ready, tail_ready, local, ss_z, rs_z, ss_t, rs_t, ss_x, rs_x, ss_y, rs_y):
    c, s, parity, sibling, others, layers = here(n_ctx, n_shard)
    greet(others, layers)
    count, width = rows.shape
    groups = n_ctx // group
    slots = recv.shape[2]
    own = [pltpu.make_async_copy(rows, zrows.at[c], local.at[0]), pltpu.make_async_copy(tail, ztail.at[c], local.at[1])]
    fans = [
        Fan(n_ctx, c, lambda d: ztail.at[flip_bits(c, d)], ss_t, rs_t, True),
        Fan(n_ctx, c, lambda d: zrows.at[flip_bits(c, d)], ss_z, rs_z, True),
    ]
    fans[0].send(0, tail)
    fans[1].send(0, rows)
    for item in own:
        item.start()
    waits = []
    seen = set()
    for k in range(groups):
        at = flip_bits(lax.div(c, group), k)
        if k == 0:
            for item in own:
                item.wait()
        table = slot_table(code[at], slots)
        for d in fans[0].order():
            if d < (k + 1) * group and d not in seen:
                fans[0].arrival(d)
                fans[1].arrival(d)
                seen.add(d)
        first = pl.multiple_of(at * group, group)
        block = ztail[pl.ds(first, group)].reshape(group * count, -1)
        tail_ready[k] = jnp.dot(table, block, preferred_element_type=F32).astype(BF).reshape(n_shard, slots, -1)

        @pl.loop(0, width // tile)
        def _(j):
            cols = pl.ds(pl.multiple_of(j * tile, tile), tile)
            block = zrows[pl.ds(first, group), :, cols].reshape(group * count, tile)
            value = jnp.dot(table, block, preferred_element_type=F32).astype(BF)
            ready[k, :, :, cols] = value.reshape(n_shard, slots, tile)

        for i, peer in enumerate(others):
            item = push(ready.at[k, peer], recv.at[s, at], ss_x.at[k, i], rs_x.at[k, i], shard=peer)
            item.start()
            waits.append(item)
            item = push(tail_ready.at[k, peer], tail_recv.at[s, at], ss_y.at[k, i], rs_y.at[k, i], shard=peer)
            item.start()
            waits.append(item)
        item = pltpu.make_async_copy(ready.at[k, s], recv.at[s, at], local.at[2 * k + 2])
        item.start()
        waits.append(item)
        item = pltpu.make_async_copy(tail_ready.at[k, s], tail_recv.at[s, at], local.at[2 * k + 3])
        item.start()
        waits.append(item)
    for fan in fans:
        fan.drain()
    for item in waits:
        item.wait()


def dispatch_rows(n_ctx, n_shard, group, capacity, rows, tail, code, ident):
    groups, slots = code.shape[0], group * capacity
    count, width = rows.shape
    few = tail.shape[1]
    return call(
        functools.partial(dispatch_body, n_ctx, n_shard, group, 512),
        [
            jax.ShapeDtypeStruct((n_shard, groups, slots, width), BF),
            jax.ShapeDtypeStruct((n_shard, groups, slots, few), BF),
        ],
        [VMEM, VMEM, VMEM],
        [
            pltpu.VMEM((n_ctx, count, width), BF), pltpu.VMEM((n_ctx, count, few), BF),
            pltpu.VMEM((groups, n_shard, slots, width), BF), pltpu.VMEM((groups, n_shard, slots, few), BF),
            DMA((2 * groups + 2,)), DMA((n_ctx,)), DMA((n_ctx,)), DMA((n_ctx,)), DMA((n_ctx,)),
        ] + [DMA((groups, n_shard - 1))] * 4,
        ident, (rows, tail, code), mib=56,
    )


def combine_body(n_ctx, n_shard, group, tile, rows, tail, mix, code, out, tail_out, mix_out,
                 land, tail_land, value, tail_value, zsend, zrecv, tsend, trecv, msend, mrecv, mix_kept, table, local,
                 ss_x, rs_x, ss_y, rs_y, ss_z, rs_z, ss_t, rs_t, ss_m, rs_m):
    c, s, parity, sibling, others, layers = here(n_ctx, n_shard)
    greet(others, layers)
    count, width = out.shape
    groups = n_ctx // group
    slots = rows.shape[2]
    near = {}
    for k in reversed(range(groups)):
        at = flip_bits(lax.div(c, group), k)
        near[k] = []
        for i, peer in enumerate(others):
            item = push(rows.at[peer, at], land.at[k, s], ss_x.at[k, i], rs_x.at[k, i], shard=peer)
            item.start()
            near[k].append(item)
            item = push(tail.at[peer, at], tail_land.at[k, s], ss_y.at[k, i], rs_y.at[k, i], shard=peer)
            item.start()
            near[k].append(item)
        item = pltpu.make_async_copy(rows.at[s, at], land.at[k, s], local.at[k, 0])
        item.start()
        near[k].append(item)
        item = pltpu.make_async_copy(tail.at[s, at], tail_land.at[k, s], local.at[k, 1])
        item.start()
        near[k].append(item)
    for k in range(groups):
        table[k] = slot_table(code[flip_bits(lax.div(c, group), k)], slots).T

    def local_sums(k, block_of):
        @pl.loop(0, width // tile)
        def _(j):
            cols = pl.ds(pl.multiple_of(j * tile, tile), tile)
            value[:, cols] = jnp.dot(table[k], block_of(cols), preferred_element_type=F32)

    def part(ref, d):
        place = lax.rem(flip_bits(c, d), group)
        return ref[pl.ds(pl.multiple_of(place * count, count), count), :]

    def in_group(k):
        return sorted(range(k * group, (k + 1) * group), key=lambda d: (lowest(d) or n_ctx, d))

    mix_fold = Fold(c, msend, mrecv, ss_m, rs_m)
    for k in reversed(range(groups)):
        at = flip_bits(lax.div(c, group), k)
        local_sums(k, lambda cols: mix[:, at, :, cols].reshape(n_shard * slots, tile))
        for d in in_group(k):
            if lowest(d) == 1:
                mix_fold.give(d, part(value, d))
            else:
                mix_kept[d // 2] = part(value, d)
    fold = Fold(c, zsend, zrecv, ss_z, rs_z)
    tail_fold = Fold(c, tsend, trecv, ss_t, rs_t)
    for k in reversed(range(groups)):
        for item in near[k]:
            item.wait()
        local_sums(k, lambda cols: land[k, :, :, cols].reshape(n_shard * slots, tile))
        tail_value[...] = jnp.dot(
            table[k], tail_land[k].reshape(n_shard * slots, -1), preferred_element_type=F32
        )
        for d in in_group(k):
            if lowest(d) == 1:
                fold.give(d, part(value, d))
                tail_fold.give(d, part(tail_value, d))
        for d in in_group(k):
            if lowest(d) != 1:
                if d:
                    mix_fold.give(d, mix_fold.take(d, mix_kept[d // 2]))
                    fold.give(d, fold.take(d, part(value, d)))
                    tail_fold.give(d, tail_fold.take(d, part(tail_value, d)))
                else:
                    mix_out[...] = mix_fold.take(0, mix_kept[0])
                    out[...] = fold.take(0, part(value, 0))
                    tail_out[...] = tail_fold.take(0, part(tail_value, 0))
    for item in (mix_fold, fold, tail_fold):
        item.drain()


def combine_rows(n_ctx, n_shard, group, rows, tail, mix, code, ident):
    groups, slots, width = rows.shape[1:]
    few = tail.shape[3]
    count = code.shape[2] // group
    sds = jax.ShapeDtypeStruct
    return call(
        functools.partial(combine_body, n_ctx, n_shard, group, 512),
        [sds((count, width), F32), sds((count, few), F32), sds((count, width), F32)],
        [VMEM] * 4,
        [
            pltpu.VMEM((groups, n_shard, slots, width), BF), pltpu.VMEM((groups, n_shard, slots, few), BF),
            pltpu.VMEM((group * count, width), F32), pltpu.VMEM((group * count, few), F32),
            pltpu.VMEM((n_ctx - 1, count, width), BF), pltpu.VMEM((n_ctx - 1, count, width), BF),
            pltpu.VMEM((n_ctx - 1, count, few), BF), pltpu.VMEM((n_ctx - 1, count, few), BF),
            pltpu.VMEM((n_ctx - 1, count, width), BF), pltpu.VMEM((n_ctx - 1, count, width), BF),
            pltpu.VMEM((n_ctx // 2, count, width), F32), pltpu.VMEM((groups, group * count, n_shard * slots), BF),
            DMA((groups, 2)),
        ] + [DMA((groups, n_shard - 1))] * 4 + [DMA((n_ctx,))] * 6,
        ident, (rows, tail, mix, code), mib=60, out_specs=[VMEM] * 3,
    )


def rms_scale(hidden, gain):
    return hidden * lax.rsqrt(jnp.mean(hidden * hidden, axis=-1, keepdims=True) + epsilon) * gain


def rotate(headwise, places):
    half_size = headwise.shape[-1] // 2
    frequency = rope_base ** (-jnp.arange(half_size, dtype=F32) * 2.0 / headwise.shape[-1])
    angles = places.astype(F32)[:, None] * frequency[None, :]
    cosine = jnp.cos(angles)[:, None, :]
    sine = jnp.sin(angles)[:, None, :]
    former = headwise[..., :half_size]
    latter = headwise[..., half_size:]
    return jnp.concatenate(
        [former * cosine - latter * sine, latter * cosine + former * sine], axis=-1
    )


def place_of(row_ids, order, block_rows):
    block_ids = jnp.arange(order.shape[0], dtype=jnp.int32)
    owner_block = row_ids // block_rows
    picked_block = jnp.sum(
        jnp.where(owner_block[:, None] == block_ids[None, :], order[None, :], 0), axis=1
    )
    return picked_block * block_rows + row_ids % block_rows


def dot(left, right):
    return jnp.dot(left, right, preferred_element_type=F32)


def contract_rows(left, right):
    return lax.dot_general(left, right, (((0,), (0,)), ((), ())), preferred_element_type=F32)


def contract_cols(left, right):
    return lax.dot_general(left, right, (((1,), (1,)), ((), ())), preferred_element_type=F32)


def exchange_shard(x):
    return lax.all_to_all(x, "shard", split_axis=0, concat_axis=0, tiled=True)


def gather_ctx(x):
    return lax.all_gather(x, "ctx", axis=0, tiled=False)


def shards(
    tokens,
    cotangent,
    block_order,
    routes,
    attn_gain,
    w_query,
    key_weight,
    value_weight,
    query_gain,
    key_gain,
    w_out,
    ffn_gain,
    w_router,
    w_gate,
    w_up,
    w_down,
):
    rows = tokens.shape[1]
    width = tokens.shape[2]
    ctx_count = lax.axis_size("ctx")
    shard_count = lax.axis_size("shard")
    my_ctx = lax.axis_index("ctx")
    my_shard = lax.axis_index("shard")
    experts = ctx_count * shard_count
    block_rows = rows // 2
    heads = QUERY_HEADS // shard_count
    head_cols = heads * HEAD_DIM
    sharers = shard_count // KEY_VALUE_HEADS
    score_scale = HEAD_DIM ** (-0.5)
    top_count = routes.shape[2]
    capacity = rows * top_count // experts + max(rows * top_count // (4 * experts), 1)
    sequence = rows * ctx_count
    plane = rows * shard_count
    wrows = width // shard_count

    inputs = tokens[0].astype(F32)
    upstream_b = cotangent[0]
    upstream = upstream_b.astype(F32)

    group = 1
    while group * capacity % 16:
        group *= 2
    groups = ctx_count // group
    slot_rows = shard_count * ctx_count * capacity
    block_shape = (shard_count, groups, group * capacity)
    row_ids = my_ctx * rows + jnp.arange(rows, dtype=jnp.int32)
    q_places = place_of(row_ids, block_order, block_rows)
    k_places = place_of(jnp.arange(sequence, dtype=jnp.int32), block_order, block_rows)
    bias = jnp.where(k_places[None, :] <= q_places[:, None], 0.0, -1e30).astype(F32)
    frequency = rope_base ** (-jnp.arange(HEAD_DIM // 2, dtype=F32) * 2.0 / HEAD_DIM)
    angles = q_places.astype(F32)[:, None] * frequency[None, :]
    cosine = jnp.concatenate([jnp.cos(angles)] * 2, axis=1)
    sine = jnp.concatenate([-jnp.sin(angles), jnp.sin(angles)], axis=1)
    (
        normed_all, w_mine, router_all, code, upstream_rows, query_pre, kv_pre, queries, kv_all, attn_rows, middle,
    ) = front(
        ctx_count, shard_count, group, capacity, KEY_VALUE_HEADS,
        (
            tokens[0], attn_gain[None], w_query, key_weight, value_weight, routes[0].T, w_router.T, upstream_b,
            cosine, sine, bias, query_gain[None], key_gain[None], w_out,
        ),
        0,
    )
    upstream_rows = upstream_rows.reshape(slot_rows, width)
    is_key = lax.rem(my_shard, 2) == 0
    part_count = sharers // 2

    def prep(pre, gain):
        shape = pre.shape
        flat = pre.reshape(-1, rows, shape[-2], HEAD_DIM)
        return jax.vmap(lambda v: rotate(rms_scale(v, gain), q_places))(flat).reshape(shape)

    normed_two = rms_scale(middle, ffn_gain)
    second_b = normed_two.astype(BF)
    logits = contract_cols(second_b, router_all)
    chosen = jnp.sum(
        (routes[0][:, :, None] == jnp.arange(experts, dtype=jnp.int32)).astype(F32), axis=1
    )

    def gates_of(log, mask):
        masked = jnp.where(mask > 0, log, -1e30)
        peak = jnp.max(masked, axis=-1, keepdims=True)
        risen = jnp.exp(masked - peak) * mask
        return risen / jnp.maximum(jnp.sum(risen, axis=-1, keepdims=True), 1e-30)

    gates = gates_of(logits, chosen)

    tail_cols = -(-2 * experts // 128) * 128

    def two_parts(value):
        coarse = value.astype(BF).astype(F32)
        return coarse.astype(BF), (value - coarse).astype(BF)

    gates_two = jnp.concatenate(two_parts(gates), axis=1)
    gates_two = jnp.pad(gates_two, ((0, 0), (0, tail_cols - 2 * experts)))
    received, gate_tail = dispatch_rows(ctx_count, shard_count, group, capacity, second_b, gates_two, code, 3)
    received = received.reshape(slot_rows, width)
    my_expert = my_ctx * shard_count + my_shard
    column = jnp.arange(tail_cols, dtype=jnp.int32)[None, :]
    mine_column = (column == my_expert) | (column == experts + my_expert)
    gate_tail = gate_tail.reshape(slot_rows, tail_cols).astype(F32)
    slot_gates = jnp.sum(jnp.where(mine_column, gate_tail, 0.0), axis=1, keepdims=True)
    gate_pre = dot(received, w_gate[0])
    up_pre = dot(received, w_up[0])
    activated = jax.nn.silu(gate_pre)
    hidden_b = (activated * up_pre).astype(BF)
    expert_out = dot(hidden_b, w_down[0]).astype(BF)
    expert_out_f = expert_out.astype(F32)
    mix_sent = (slot_gates * expert_out_f).astype(BF)
    mix_sent, upstream_rows, expert_out = lax.optimization_barrier((mix_sent, upstream_rows, expert_out))
    expert_out_f = expert_out.astype(F32)
    mix_back = exchange_shard(mix_sent.reshape(block_shape + (width,)))
    upstream_rows = upstream_rows.astype(F32)
    slot_dot = jnp.sum(expert_out_f * upstream_rows, axis=1, keepdims=True)
    grad_expert = (slot_gates * upstream_rows).astype(BF)
    grad_w_down = contract_rows(hidden_b, grad_expert)
    grad_hidden = contract_cols(grad_expert, w_down[0])
    sigmoid_g = jax.nn.sigmoid(gate_pre)
    silu_slope = sigmoid_g * (1.0 + gate_pre * (1.0 - sigmoid_g))
    grad_gate_pre = (grad_hidden * up_pre * silu_slope).astype(BF)
    grad_up_pre = (grad_hidden * activated).astype(BF)
    grad_w_gate = contract_rows(received, grad_gate_pre)
    grad_w_up = contract_rows(received, grad_up_pre)
    grad_received = contract_cols(grad_gate_pre, w_gate[0]) + contract_cols(grad_up_pre, w_up[0])

    coarse, fine = two_parts(slot_dot)
    tail = jnp.where(column == my_expert, coarse, jnp.where(column == experts + my_expert, fine, jnp.zeros((), BF)))
    grad_second, back_tail, mixture = combine_rows(
        ctx_count, shard_count, group, grad_received.astype(BF).reshape(block_shape + (width,)),
        tail.reshape(block_shape + (tail_cols,)), mix_back, code, 4,
    )
    mixed = (middle + mixture).astype(BF)
    grad_gates = back_tail[:, :experts] + back_tail[:, experts : 2 * experts]
    grad_logits_b = (
        gates * (grad_gates - jnp.sum(gates * grad_gates, axis=-1, keepdims=True))
    ).astype(BF)
    router_part = contract_rows(grad_logits_b, second_b).astype(BF)
    grad_second = grad_second + dot(grad_logits_b, router_all)
    unused, norm_two_back = jax.vjp(rms_scale, middle, ffn_gain)
    grad_middle_part, grad_ffn_gain = norm_two_back(grad_second)
    grad_middle = upstream + grad_middle_part
    grad_proj_b = grad_middle.astype(BF)

    router_parts = jnp.swapaxes(router_part.reshape(experts, shard_count, wrows), 0, 1)
    if plane * width <= 2**21:
        gains = jnp.concatenate([jnp.zeros((1, width), F32), grad_ffn_gain[None], jnp.zeros((6, width), F32)])
        q_sum, kv_sum, out_sum, router_sum, gains, grad_input_part = back(
            ctx_count, shard_count, heads,
            (
                grad_proj_b, queries, kv_all, attn_rows, query_pre, kv_pre, w_out, normed_all, w_mine,
                cosine, sine, bias, query_gain[None], key_gain[None], tokens[0], attn_gain[None], gains, router_parts,
            ),
            5,
        )
    else:
        normed_all = normed_all.reshape(plane, width)
        w_mine = w_mine.reshape(width, head_cols + HEAD_DIM)
        query_pre = query_pre.reshape(shard_count, rows, heads, HEAD_DIM)
        kv_pre = kv_pre.reshape(plane, HEAD_DIM)
        queries = queries.reshape(shard_count, rows, heads, HEAD_DIM)
        kv_all = kv_all.reshape(2, shard_count, sequence, HEAD_DIM)
        keys, values = kv_all[0], kv_all[1]
        attn_rows = attn_rows.reshape(plane, head_cols)
        grad_proj_all = spread(shard_count, grad_proj_b, 5).reshape(plane, width)
        out_part = contract_rows(attn_rows, grad_proj_all).astype(BF)
        out_part, grad_proj_all = lax.optimization_barrier((out_part, grad_proj_all))
        grad_attn = contract_cols(grad_proj_all, w_out).astype(BF)
        grad_heads = grad_attn.reshape(shard_count, rows, heads, HEAD_DIM)
        scores = (
            jnp.einsum("sthd,spd->shtp", queries, keys, preferred_element_type=F32) * score_scale
        )
        scores = scores + bias
        raised = jnp.exp(scores - jnp.max(scores, axis=-1, keepdims=True))
        probs = raised / jnp.sum(raised, axis=-1, keepdims=True)
        probs_b = probs.astype(BF)
        grad_probs = jnp.einsum("sthd,spd->shtp", grad_heads, values, preferred_element_type=F32)
        delta = jnp.sum(probs * grad_probs, axis=-1, keepdims=True)
        grad_scores = (probs * (grad_probs - delta)).astype(BF)
        grad_query = score_scale * jnp.einsum(
            "shtp,spd->sthd", grad_scores, keys, preferred_element_type=F32
        )
        grad_keys = score_scale * jnp.einsum(
            "shtp,sthd->spd", grad_scores, queries, preferred_element_type=F32
        )
        grad_values = jnp.einsum("shtp,sthd->spd", probs_b, grad_heads, preferred_element_type=F32)
        grad_kv = jnp.stack([grad_keys, grad_values]).astype(BF)
        grad_kv = key_back(
            ctx_count, shard_count, grad_kv.reshape(2, shard_count, ctx_count, rows, HEAD_DIM), 6
        )
        unused, query_back = jax.vjp(prep, query_pre, query_gain)
        grad_query_pre, grad_query_gain = query_back(grad_query)
        kv_shape = (shard_count, rows, 1, HEAD_DIM)
        unused, key_prep_back = jax.vjp(prep, kv_pre.reshape(kv_shape), key_gain)
        grad_key_pre, grad_key_gain = key_prep_back(grad_kv.reshape(kv_shape))
        grad_key_gain = jnp.where(is_key, grad_key_gain, 0.0)
        grad_kv_full = jnp.where(
            is_key, grad_key_pre.reshape(plane, HEAD_DIM), grad_kv.reshape(plane, HEAD_DIM)
        ).astype(BF)
        grad_pre = jnp.concatenate(
            [grad_query_pre.reshape(plane, head_cols).astype(BF), grad_kv_full], axis=1
        )
        gains = jnp.concatenate(
            [
                jnp.zeros((1, width), F32),
                grad_ffn_gain[None],
                jnp.pad(
                    jnp.concatenate([grad_query_gain, grad_key_gain])[None],
                    ((0, 6 - 1), (0, width - 2 * HEAD_DIM)),
                ),
            ]
        )
        grad_w = contract_rows(normed_all, grad_pre).astype(BF).reshape(shard_count, wrows, -1)
        q_sum, kv_sum, out_sum, router_sum, gains, grad_input_part = finish(
            ctx_count, shard_count, head_cols, grad_w, out_part.reshape(8, -1, width), router_parts, gains, grad_pre, w_mine,
            tokens[0], attn_gain[None], 8,
        )
    grad_tokens = grad_middle + grad_input_part
    grad_attn_gain, grad_ffn_gain = gains[0], gains[1]
    grad_query_gain, grad_key_gain = gains[2, :HEAD_DIM], gains[2, HEAD_DIM : 2 * HEAD_DIM]
    grad_w_query = q_sum.astype(F32)
    grad_w_out = out_sum.reshape(head_cols, width).astype(F32)
    kinds = kv_sum.astype(F32).reshape(KEY_VALUE_HEADS, part_count, 2, wrows, HEAD_DIM)
    kinds = jnp.transpose(jnp.sum(kinds, axis=1), (1, 2, 0, 3)).reshape(2, wrows, -1)
    grad_w_key, grad_w_value = kinds[0], kinds[1]
    grad_w_router = router_sum.T
    return (
        mixed[None],
        grad_tokens[None],
        grad_attn_gain,
        grad_w_query,
        grad_w_key,
        grad_w_value,
        grad_query_gain,
        grad_key_gain,
        grad_w_out,
        grad_ffn_gain,
        grad_w_router,
        grad_w_gate[None],
        grad_w_up[None],
        grad_w_down[None],
    )


def solution(mesh):
    rows = P("shard", "ctx", None)
    matrix = P("shard", None)
    expert = P(("ctx", "shard"), None, None)
    return jax.shard_map(
        shards,
        mesh=mesh,
        in_specs=(
            rows, rows, P(), rows, P(), matrix, matrix, matrix, P(), P(), matrix, P(), matrix,
            expert, expert, expert,
        ),
        out_specs=(
            rows, rows, P(), matrix, matrix, matrix, P(), P(), matrix, P(), matrix,
            expert, expert, expert,
        ),
        check_vma=False,
    )
```

```python
import functools

import jax
import jax.numpy as jnp
from jax import lax
from jax.experimental import pallas as pl
from jax.experimental.pallas import tpu as pltpu
from jax.sharding import PartitionSpec as P

BF = jnp.bfloat16
F32 = jnp.float32
MESH = pl.DeviceIdType.MESH
ANY = pl.BlockSpec(memory_space=pl.ANY)
VMEM = pl.BlockSpec(memory_space=pltpu.VMEM)
DMA = pltpu.SemaphoreType.DMA
epsilon = 1e-06
rope_base = 1000000.0
QUERY_HEADS = 32
KEY_VALUE_HEADS = 4
HEAD_DIM = 128


def push(src, dst, send_sem, recv_sem, **where):
    return pltpu.make_async_remote_copy(
        src_ref=src, dst_ref=dst, send_sem=send_sem, recv_sem=recv_sem,
        device_id=where, device_id_type=MESH,
    )


def greet(shard_peers, ctx_peers):
    barrier = pltpu.get_barrier_semaphore()
    for peer in shard_peers:
        pl.semaphore_signal(barrier, inc=1, device_id={"shard": peer}, device_id_type=MESH)
    for peer in ctx_peers:
        pl.semaphore_signal(barrier, inc=1, device_id={"ctx": peer}, device_id_type=MESH)
    pl.semaphore_wait(barrier, len(shard_peers) + len(ctx_peers))


def here(ctx_count, shard_count):
    c, s = lax.axis_index("ctx"), lax.axis_index("shard")
    parity = lax.rem(s, 2)
    sibling = s + 1 - 2 * parity
    others = [lax.rem(s + d, shard_count) for d in range(1, shard_count)]
    layers = [lax.rem(c + d, ctx_count) for d in range(1, ctx_count)]
    return c, s, parity, sibling, others, layers


def flip_bits(index, mask):
    result = index
    bit = 1
    while bit <= mask:
        if mask & bit:
            result = result + bit - 2 * bit * lax.rem(lax.div(index, bit), 2)
        bit *= 2
    return result


def lowest(d):
    return d & -d


class Fan:
    def __init__(self, n_ctx, c, block, ss, rs, near_first):
        self.n_ctx, self.c, self.block, self.ss, self.rs, self.near_first = n_ctx, c, block, ss, rs, near_first
        self.items = {}

    def send(self, d, src):
        bits = [b for b in (1, 2, 4, 8, 16) if b < (lowest(d) or self.n_ctx)]
        for b in bits if self.near_first else reversed(bits):
            item = push(src, self.block(d), self.ss.at[d | b], self.rs.at[d | b], ctx=flip_bits(self.c, b))
            item.start()
            self.items[d | b] = item

    def arrival(self, d):
        self.items[d].wait_recv()
        if lowest(d) > 1:
            self.send(d, self.block(d))

    def order(self):
        return sorted(range(1, self.n_ctx), key=lambda d: (bin(d).count("1"), d if self.near_first else -d))

    def drain(self):
        for d in range(1, self.n_ctx):
            self.items[d].wait_send()


class Fold:
    def __init__(self, c, sent, received, ss, rs, slots=None, after=None):
        self.c, self.sent, self.received, self.ss, self.rs = c, sent, received, ss, rs
        self.slots, self.after = slots or {}, after or {}
        self.items, self.left = {}, set()

    def take(self, d, value):
        for b in (1, 2, 4, 8, 16):
            if b < lowest(d) or (d == 0 and b in self.items):
                self.items[d | b].wait_recv()
                value = value + self.received[(d | b) - 1].astype(F32)
        return value

    def give(self, d, value):
        slot = self.slots.get(d, d - 1)
        if d in self.after:
            other, which = self.after[d]
            other.items[which].wait_send()
            other.left.add(which)
        self.sent[slot] = value.astype(BF)
        item = push(self.sent.at[slot], self.received.at[d - 1], self.ss.at[d], self.rs.at[d],
                    ctx=flip_bits(self.c, lowest(d)))
        item.start()
        self.items[d] = item

    def drain(self):
        for d, item in self.items.items():
            if d not in self.left:
                item.wait_send()


def call(body, outs, in_specs, scratch, ident, args, mib=48, out_specs=None):
    return pl.pallas_call(
        body,
        out_shape=outs,
        in_specs=in_specs,
        out_specs=out_specs if out_specs is not None else [ANY] * len(outs),
        scratch_shapes=scratch,
        compiler_params=pltpu.CompilerParams(
            collective_id=ident, has_side_effects=True, vmem_limit_bytes=mib * 2**20
        ),
    )(*args)


def slot_table(code, slots):
    places = lax.broadcasted_iota(jnp.int32, (slots, code.shape[1]), 0).astype(F32)
    return jnp.concatenate(
        [(places == code[e : e + 1, :]).astype(BF) for e in range(code.shape[0])], axis=0
    )


def turn(value, cosine, sine):
    return value * cosine + pltpu.roll(value, HEAD_DIM // 2, 1) * sine


def unit_rows(value):
    scale = lax.rsqrt(jnp.mean(value * value, axis=-1, keepdims=True) + epsilon)
    return value * scale, scale


def front_body(n_ctx, n_shard, group, capacity, heads, kv_heads, tile,
               tokens, gain, w_query, key_w, value_w, routes, router, cot, cosine, sine, bias, q_gain, k_gain, w_out,
               rows_out, w_all_out, router_all, code, cot_rows, qpre_out, kvpre, q_out, kv_out, attn_out, mid,
               own_rows, rows_all, w_all, zroutes, zcot, ready, qpre, q, kv, attn,
               own_part, pair, to_sib, sib, to_chip, got,
               local, ss_row, rs_row, ss_fwd, rs_fwd, ss_w, rs_w, ss_k, rs_k, ss_rt, rs_rt, ss_ro, rs_ro, ss_z, rs_z,
               ss_x, rs_x, ss_kz, rs_kz, ss_kf, rs_kf, ss_s, rs_s, ss_c, rs_c, out_sem):
    c, s, parity, sibling, others, layers = here(n_ctx, n_shard)
    chips = n_shard // 2
    chip = lax.div(s, 2)
    count, width = tokens.shape
    wr = w_query.shape[0]
    cols = heads * HEAD_DIM
    sharers = n_shard // kv_heads
    groups = n_ctx // group
    slots = group * capacity
    keys = n_ctx * count
    mates = [lax.rem(s + 2 * d, n_shard) for d in range(1, chips)]
    x = tokens[...].astype(F32)
    unit, unused = unit_rows(x)
    own_rows[...] = (unit * gain[...]).astype(BF)
    greet(others, layers)

    route_fan = Fan(n_ctx, c, lambda d: zroutes.at[flip_bits(c, d)], ss_ro, rs_ro, False)
    route_fan.send(0, routes)
    cot_fan = Fan(n_ctx, c, lambda d: zcot.at[flip_bits(c, d)], ss_z, rs_z, False)
    cot_fan.send(0, cot)
    first, waits = [], []
    for d in range(1, chips):
        item = push(own_rows, rows_all.at[s], ss_row.at[d], rs_row.at[d], shard=mates[d - 1])
        item.start()
        first.append(item)
    item = push(own_rows, rows_all.at[s], ss_fwd.at[0], rs_fwd.at[0], shard=sibling)
    item.start()
    waits.append(item)
    w_waits = []
    for i, peer in enumerate(others):
        from_q = w_query.at[:, pl.ds(pl.multiple_of(peer * cols, cols), cols)]
        item = push(from_q, w_all.at[s, :, pl.ds(0, cols)], ss_w.at[i], rs_w.at[i], shard=peer)
        item.start()
        w_waits.append(item)
        head = pl.ds(pl.multiple_of(lax.div(peer, sharers) * HEAD_DIM, HEAD_DIM), HEAD_DIM)
        for kind, ref in enumerate((key_w, value_w)):
            item = push(ref.at[:, head], w_all.at[s, :, pl.ds(cols, HEAD_DIM)], ss_k.at[i], rs_k.at[i], shard=peer)

            @pl.when(lax.rem(peer, 2) == kind)
            def _(item=item):
                item.start()

        w_waits.append(item)
        item = push(router, router_all.at[:, pl.ds(pl.multiple_of(s * wr, wr), wr)], ss_rt.at[i], rs_rt.at[i], shard=peer)
        item.start()
        waits.append(item)
    copies = [
        pltpu.make_async_copy(own_rows, rows_all.at[s], local.at[0]),
        pltpu.make_async_copy(w_query.at[:, pl.ds(pl.multiple_of(s * cols, cols), cols)],
                              w_all.at[s, :, pl.ds(0, cols)], local.at[1]),
        pltpu.make_async_copy(routes, zroutes.at[c], local.at[2]),
        pltpu.make_async_copy(router, router_all.at[:, pl.ds(pl.multiple_of(s * wr, wr), wr)], local.at[3]),
        pltpu.make_async_copy(cot, zcot.at[c], local.at[4]),
    ]
    for item in copies:
        item.start()
    head = pl.ds(pl.multiple_of(lax.div(s, sharers) * HEAD_DIM, HEAD_DIM), HEAD_DIM)
    for kind, ref in enumerate((key_w, value_w)):
        own_head = pltpu.make_async_copy(ref.at[:, head], w_all.at[s, :, pl.ds(cols, HEAD_DIM)], local.at[5])

        @pl.when(parity == kind)
        def _(own_head=own_head):
            own_head.start()

    copies[2].wait()
    for d in route_fan.order():
        route_fan.arrival(d)
    before = (
        lax.broadcasted_iota(jnp.int32, (count, count), 0) < lax.broadcasted_iota(jnp.int32, (count, count), 1)
    ).astype(BF)
    for layer in range(n_ctx):
        named = zroutes[layer]
        mask = jnp.concatenate(
            [jnp.max((named == c * n_shard + e).astype(F32), axis=0, keepdims=True) for e in range(n_shard)], axis=0
        )
        rank = jnp.dot(mask.astype(BF), before, preferred_element_type=F32)
        at = layer % group
        code[layer // group, :, at * count : (at + 1) * count] = jnp.where(
            mask > 0, rank + float(at * capacity), -1.0
        )

    for d in range(1, chips):
        first[d - 1].wait()
        origin = lax.rem(s + n_shard - 2 * d, n_shard)
        item = push(rows_all.at[origin], rows_all.at[origin], ss_fwd.at[d], rs_fwd.at[d], shard=sibling)
        item.start()
        waits.append(item)
    for d in cot_fan.order():
        cot_fan.arrival(d)
    copies[4].wait()
    for k in range(groups):
        table = slot_table(code[k], slots)

        @pl.loop(0, width // tile)
        def _(j):
            part = pl.ds(pl.multiple_of(j * tile, tile), tile)
            block = zcot[k * group : (k + 1) * group, :, part].reshape(group * count, tile)
            value = jnp.dot(table, block, preferred_element_type=F32).astype(BF)
            ready[k, :, :, part] = value.reshape(n_shard, slots, tile)

    for item in waits + w_waits:
        item.wait()
    copies[0].wait()
    copies[1].wait()
    copies[3].wait()
    own_head.wait()
    outs = [
        pltpu.make_async_copy(rows_all, rows_out, out_sem.at[0]),
        pltpu.make_async_copy(w_all, w_all_out, out_sem.at[1]),
    ]
    outs[0].start()
    outs[1].start()

    right = w_all[:, :, pl.ds(cols, HEAD_DIM)].reshape(width, HEAD_DIM)

    @pl.loop(0, n_shard)
    def _(b):
        pre = jnp.dot(rows_all[b], right, preferred_element_type=F32)
        kvpre[b] = pre
        keyed, unused = unit_rows(pre)
        keyed = turn(keyed * k_gain[...], cosine[...], sine[...])
        kv[parity, b, c] = jnp.where(parity == 0, keyed, pre).astype(BF)

    fan = Fan(n_ctx, c, lambda d: kv.at[parity, :, flip_bits(c, d)], ss_kz, rs_kz, False)
    fan.send(0, kv.at[parity, :, c])
    kv_waits = []
    item = push(kv.at[parity, :, c], kv.at[parity, :, c], ss_kf.at[0], rs_kf.at[0], shard=sibling)
    item.start()
    kv_waits.append(item)

    cot_waits = []
    for k in range(groups):
        for i, peer in enumerate(others):
            item = push(ready.at[k, peer], cot_rows.at[k, s], ss_x.at[k, i], rs_x.at[k, i], shard=peer)
            item.start()
            cot_waits.append(item)
        item = pltpu.make_async_copy(ready.at[k, s], cot_rows.at[k, s], local.at[6 + k])
        item.start()
        cot_waits.append(item)

    @pl.loop(0, n_shard // 2)
    def _(b):
        left = rows_all[pl.ds(b * 2, 2)].reshape(2 * count, width)
        pre = jnp.dot(left, w_all[:, :, pl.ds(0, cols)].reshape(width, cols), preferred_element_type=F32)
        qpre[pl.ds(b * 2, 2)] = pre.reshape(2, count, cols)
        for i in range(2):
            for h in range(heads):
                part = pre[i * count : (i + 1) * count, h * HEAD_DIM : (h + 1) * HEAD_DIM]
                unit, unused = unit_rows(part)
                q[b * 2 + i, :, h * HEAD_DIM : (h + 1) * HEAD_DIM] = turn(
                    unit * q_gain[...], cosine[...], sine[...]
                ).astype(BF)

    for d in fan.order():
        fan.arrival(d)
        block = kv.at[parity, :, flip_bits(c, d)]
        item = push(block, block, ss_kf.at[d], rs_kf.at[d], shard=sibling)
        item.start()
        kv_waits.append(item)
    outs += [pltpu.make_async_copy(qpre, qpre_out, out_sem.at[2]), pltpu.make_async_copy(q, q_out, out_sem.at[3])]
    outs[2].start()
    outs[3].start()
    for item in kv_waits:
        item.wait()
    fan.drain()
    outs.append(pltpu.make_async_copy(kv, kv_out, out_sem.at[4]))
    outs[4].start()

    near, far = {}, {}
    order = list(range(1, chips)) + [0]

    def product(at):
        d = order[at]
        first_seq = 2 * lax.rem(chip + d, chips)

        @pl.loop(0, 2)
        def _(i):
            b = first_seq + i
            k_all = kv[0, b].reshape(keys, HEAD_DIM)
            v_all = kv[1, b].reshape(keys, HEAD_DIM)
            for h in range(heads):
                hs = slice(h * HEAD_DIM, (h + 1) * HEAD_DIM)
                scores = lax.dot_general(q[b, :, hs], k_all, (((1,), (1,)), ((), ())), preferred_element_type=F32)
                scores = scores * (HEAD_DIM ** -0.5) + bias[...]
                raised = jnp.exp(scores - jnp.max(scores, axis=-1, keepdims=True))
                probs = raised / jnp.sum(raised, axis=-1, keepdims=True)
                attn[b, :, hs] = jnp.dot(probs.astype(BF), v_all, preferred_element_type=F32).astype(BF)

        left = attn[pl.ds(first_seq, 2)].reshape(2 * count, cols)

        @pl.loop(0, width // tile)
        def _(j):
            part = pl.ds(pl.multiple_of(j * tile, tile), tile)
            value = jnp.dot(left, w_out[:, part], preferred_element_type=F32)
            pair[...] = value.reshape(2, count, tile)
            own_part[at % 2, :, part] = pair[parity]
            to_sib[at, :, part] = pair[1 - parity].astype(BF)

        near[at] = push(to_sib.at[at], sib.at[at], ss_s.at[at], rs_s.at[at], shard=sibling)
        near[at].start()

    def chip_sum(at):
        near[at].wait()
        to_chip[at] = (own_part[at % 2] + sib[at].astype(F32)).astype(BF)
        far[at] = push(to_chip.at[at], got.at[at], ss_c.at[at], rs_c.at[at], shard=mates[order[at] - 1])
        far[at].start()

    for at in range(chips):
        product(at)
        if at:
            chip_sum(at - 1)
    outs.append(pltpu.make_async_copy(attn, attn_out, out_sem.at[5]))
    outs[5].start()
    near[chips - 1].wait()
    mid[...] = tokens[...].astype(F32) + own_part[(chips - 1) % 2] + sib[chips - 1].astype(F32)
    for at in range(chips - 1):
        far[at].wait()
        mid[...] += got[at].astype(F32)
    cot_fan.drain()
    route_fan.drain()
    for item in cot_waits + outs:
        item.wait()


def front(n_ctx, n_shard, group, capacity, kv_heads, args, ident):
    tokens, gain, w_query, key_w, value_w, routes, router, cot = args[:8]
    n, z = n_shard, n_ctx
    count, width = tokens.shape
    wr, chips, groups, slots = w_query.shape[0], n_shard // 2, n_ctx // group, group * capacity
    cols = w_query.shape[1] // n
    heads = cols // HEAD_DIM
    sds = jax.ShapeDtypeStruct
    dma = lambda *shape: DMA(shape)
    return call(
        functools.partial(front_body, z, n, group, capacity, heads, kv_heads, 512),
        [
            sds((n, count, width), BF), sds((n, wr, cols + HEAD_DIM), BF), sds((router.shape[0], width), BF),
            sds((groups, n, group * count), F32), sds((groups, n, slots, width), BF), sds((n, count, cols), F32),
            sds((n, count, HEAD_DIM), F32), sds((n, count, cols), BF), sds((2, n, z, count, HEAD_DIM), BF),
            sds((n, count, cols), BF), sds((count, width), F32),
        ],
        [VMEM, VMEM, ANY, ANY, ANY, VMEM, ANY, ANY] + [VMEM] * 6,
        [
            pltpu.VMEM((count, width), BF), pltpu.VMEM((n, count, width), BF), pltpu.VMEM((n, wr, cols + HEAD_DIM), BF),
            pltpu.VMEM((z,) + routes.shape, jnp.int32), pltpu.VMEM((z, count, width), BF),
            pltpu.VMEM((groups, n, slots, width), BF), pltpu.VMEM((n, count, cols), F32),
            pltpu.VMEM((n, count, cols), BF), pltpu.VMEM((2, n, z, count, HEAD_DIM), BF),
            pltpu.VMEM((n, count, cols), BF), pltpu.VMEM((2, count, width), F32), pltpu.VMEM((2, count, 512), F32),
            pltpu.VMEM((chips, count, width), BF), pltpu.VMEM((chips, count, width), BF),
            pltpu.VMEM((chips - 1, count, width), BF), pltpu.VMEM((chips - 1, count, width), BF),
            dma(6 + groups), dma(chips), dma(chips), dma(chips), dma(chips), dma(n - 1), dma(n - 1), dma(n - 1), dma(n - 1),
            dma(n - 1), dma(n - 1), dma(z), dma(z), dma(z), dma(z), dma(groups, n - 1), dma(groups, n - 1),
            dma(z), dma(z), dma(z), dma(z), dma(chips), dma(chips), dma(chips - 1), dma(chips - 1), dma(6),
        ],
        ident, args, mib=60,
        out_specs=[ANY, ANY, ANY, VMEM, ANY, ANY, VMEM, ANY, ANY, ANY, VMEM],
    )


def spread_body(n_shard, rows, rows_all, local, ss_row, rs_row, ss_fwd, rs_fwd):
    c, s, parity, sibling, others, layers = here(1, n_shard)
    chips = n_shard // 2
    mates = [lax.rem(s + 2 * d, n_shard) for d in range(1, chips)]
    greet(mates + [sibling], [])
    mine = pltpu.make_async_copy(rows, rows_all.at[s], local)
    mine.start()
    first, waits = [], []
    for d in range(1, chips):
        item = push(rows, rows_all.at[s], ss_row.at[d], rs_row.at[d], shard=mates[d - 1])
        item.start()
        first.append(item)
    item = push(rows, rows_all.at[s], ss_fwd.at[0], rs_fwd.at[0], shard=sibling)
    item.start()
    waits.append(item)
    for d in range(1, chips):
        first[d - 1].wait()
        origin = lax.rem(s + n_shard - 2 * d, n_shard)
        item = push(rows_all.at[origin], rows_all.at[origin], ss_fwd.at[d], rs_fwd.at[d], shard=sibling)
        item.start()
        waits.append(item)
    mine.wait()
    for item in waits:
        item.wait()


def spread(n_shard, rows, ident):
    return call(
        functools.partial(spread_body, n_shard),
        [jax.ShapeDtypeStruct((n_shard,) + rows.shape, rows.dtype)],
        [ANY], [DMA] + [DMA((n_shard // 2,))] * 4, ident, (rows,),
    )[0]


def key_back_body(n_ctx, n_shard, parts, out, sib, zsend, zrecv, ss_s, rs_s, ss_z, rs_z):
    c, s, parity, sibling, others, layers = here(n_ctx, n_shard)
    greet([sibling], layers)
    order = list(range(1, n_ctx)) + [0]
    near = {}
    for d in order:
        block = parts.at[1 - parity, :, lax.rem(c + d, n_ctx)]
        near[d] = push(block, sib.at[d], ss_s.at[d], rs_s.at[d], shard=sibling)
        near[d].start()
    far = {}
    for d in order:
        near[d].wait()
        layer = lax.rem(c + d, n_ctx)
        value = parts[parity, :, layer].astype(F32) + sib[d].astype(F32)
        if d:
            zsend[d - 1] = value.astype(BF)
            far[d] = push(zsend.at[d - 1], zrecv.at[d - 1], ss_z.at[d], rs_z.at[d], ctx=layer)
            far[d].start()
    for d in range(1, n_ctx):
        far[d].wait()
        value = value + zrecv[d - 1].astype(F32)
    out[...] = value


def key_back(n_ctx, n_shard, parts, ident):
    block = (parts.shape[1], parts.shape[3], parts.shape[4])
    return call(
        functools.partial(key_back_body, n_ctx, n_shard),
        [jax.ShapeDtypeStruct(block, F32)],
        [VMEM],
        [
            pltpu.VMEM((n_ctx,) + block, BF), pltpu.VMEM((n_ctx - 1,) + block, BF),
            pltpu.VMEM((n_ctx - 1,) + block, BF),
        ] + [DMA((n_ctx,))] * 4,
        ident, (parts,), out_specs=[VMEM],
    )[0]


def finish_body(n_ctx, n_shard, q_cols, tile,
                weights, wide, router, gains, left, right, tokens, gain,
                q_out, kv_out, wide_out, router_out, gains_out, rows_out,
                wide_landing, wide_acc, wide_total, ss_wi, rs_wi, ss_wo, ss_wc, pieces, landing, acc, total, router_in, router_mid, router_far,
                gains_own, gains_in, gains_mid, gains_far, pair, own_part, to_sib, sib, to_chip, got,
                local, ss_w, rs_w, ss_i, rs_i, ss_o, ss_q, ss_k, ss_r, rs_r, ss_g, rs_g, ss_h, rs_h,
                ss_t, rs_t, ss_s, rs_s, ss_c, rs_c):
    c, s, parity, sibling, others, layers = here(n_ctx, n_shard)
    half = n_ctx // 2
    chips = n_shard // 2
    chip = lax.div(s, 2)
    mates = [lax.rem(s + 2 * d, n_shard) for d in range(1, chips)]
    left_side = c < half
    depth = jnp.where(left_side, c, n_ctx - 1 - c)
    inner = jnp.where(left_side, c + 1, c - 1)
    outer = jnp.clip(jnp.where(left_side, c - 1, c + 1), 0, n_ctx - 1)
    middle = depth == half - 1
    inside = depth > 0
    rows, width = rows_out.shape
    greet(others, layers)
    sends, small = [None], []
    for i, peer in enumerate(others):
        item = push(weights.at[peer], pieces.at[i + 1], ss_w.at[i], rs_w.at[i], shard=peer)
        item.start()
        sends.append(item)
    for i, peer in enumerate(others):
        item = push(router.at[peer], router_in.at[i], ss_r.at[i], rs_r.at[i], shard=peer)
        item.start()
        small.append(item)

    def out_copies(j, ref):
        source = lax.rem(s + n_shard - j, n_shard)
        cols = pl.ds(pl.multiple_of(source * q_cols, q_cols), q_cols)
        return (
            pltpu.make_async_copy(ref.at[:, pl.ds(0, q_cols)], q_out.at[:, cols], ss_q.at[j]),
            pltpu.make_async_copy(ref.at[:, pl.ds(q_cols, 128)], kv_out.at[source], ss_k.at[j]),
        )

    def wide_copies(j, ref):
        return (pltpu.make_async_copy(ref, wide_out.at[j], ss_wc.at[j]),)

    class Line:
        def __init__(self, ready, own, acc, landing, total, ss_i, rs_i, ss_o, copies):
            self.ready, self.own, self.acc, self.landing, self.total = ready, own, acc, landing, total
            self.ss_i, self.rs_i, self.ss_o, self.copies = ss_i, rs_i, ss_o, copies

        def inward(self, j, ref):
            at = jnp.where(middle, 1, 0)
            return push(ref, self.landing.at[at, j], self.ss_i.at[j], self.rs_i.at[at, j], ctx=inner)

        def outward(self, j):
            return push(self.total.at[j], self.landing.at[1, j], self.ss_o.at[j], self.rs_i.at[1, j], ctx=outer)

        def arrived(self, which, j):
            push(self.acc.at[j], self.landing.at[which, j], self.ss_i.at[j], self.rs_i.at[which, j],
                 ctx=inner).wait_recv()

        def outermost(self, j):
            @pl.when(jnp.logical_not(inside))
            def _():
                self.ready(j)
                self.inward(j, self.own(j)).start()

        def first_half(self, j):
            @pl.when(inside)
            def _():
                self.ready(j)
                self.arrived(0, j)
                self.acc[j] = (self.own(j)[...].astype(F32) + self.landing[0, j].astype(F32)).astype(BF)
                self.inward(j, self.acc.at[j]).start()

        def second_half(self, j):
            self.arrived(1, j)

            @pl.when(middle)
            def _():
                self.total[j] = (self.acc[j].astype(F32) + self.landing[1, j].astype(F32)).astype(BF)

            @pl.when(jnp.logical_not(middle))
            def _():
                self.total[j] = self.landing[1, j]

            @pl.when(inside)
            def _():
                self.outward(j).start()

            for item in self.copies(j, self.total.at[j]):
                item.start()

        def drain(self, j):
            self.inward(j, self.acc.at[j]).wait_send()

            @pl.when(inside)
            def _():
                self.outward(j).wait_send()

            for item in self.copies(j, self.total.at[j]):
                item.wait()

    line = Line(lambda j: sends[j].wait() if j else None, lambda j: pieces.at[j] if j else weights.at[s],
                acc, landing, total, ss_i, rs_i, ss_o, out_copies)
    wide_line = Line(lambda j: None, lambda j: wide.at[j], wide_acc, wide_landing, wide_total,
                     ss_wi, rs_wi, ss_wo, wide_copies)
    wides = wide.shape[0]
    steps = [(wide_line, j) for j in range(wides)] + [(line, j) for j in range(n_shard)]

    near, far = {}, {}

    def product(d):
        first = pl.multiple_of(lax.rem(chip + d, chips) * (2 * rows), 2 * rows)

        @pl.loop(0, width // tile)
        def _(j):
            cols = pl.ds(pl.multiple_of(j * tile, tile), tile)
            value = lax.dot_general(left[pl.ds(first, 2 * rows), :], right[cols, :],
                                    (((1,), (1,)), ((), ())), preferred_element_type=F32)
            pair[...] = value.reshape(2, rows, tile)
            own_part[d, :, cols] = pair[parity]
            to_sib[d, :, cols] = pair[1 - parity].astype(BF)

        near[d] = push(to_sib.at[d], sib.at[d], ss_s.at[d], rs_s.at[d], shard=sibling)
        near[d].start()

    def chip_sum(d):
        near[d].wait()
        to_chip[d - 1] = (own_part[d] + sib[d].astype(F32)).astype(BF)
        far[d] = push(to_chip.at[d - 1], got.at[d - 1], ss_c.at[d - 1], rs_c.at[d - 1], shard=mates[d - 1])
        far[d].start()

    gain_sends = []

    def last_sum():
        near[0].wait()
        grad = own_part[0] + sib[0].astype(F32)
        for d in range(1, chips):
            far[d].wait()
            grad = grad + got[d - 1].astype(F32)
        x = tokens[...].astype(F32)
        scale = lax.rsqrt(jnp.mean(x * x, axis=-1, keepdims=True) + epsilon)
        unit = x * scale
        scaled = grad * gain[...]
        rows_out[...] = scale * (scaled - unit * jnp.mean(scaled * unit, axis=-1, keepdims=True))
        gains_own[...] = gains[...]
        gains_own[0:1] = jnp.sum(grad * unit, axis=0, keepdims=True)
        mine = pltpu.make_async_copy(gains_own, gains_in.at[s], local.at[0])
        mine.start()
        gain_sends.append(mine)
        for i, peer in enumerate(others):
            item = push(gains_own, gains_in.at[s], ss_g.at[i], rs_g.at[i], shard=peer)
            item.start()
            gain_sends.append(item)

    def small_plane():
        for item in small + gain_sends:
            item.wait()
        gains_mid[...] = gains_in[0]
        for i in range(1, n_shard):
            gains_mid[...] += gains_in[i]
        router_mid[...] = router[s].astype(F32)
        for i in range(n_shard - 1):
            router_mid[...] += router_in[i].astype(F32)
        for i, layer in enumerate(layers):
            push(gains_mid, gains_far.at[c], ss_h.at[i], rs_h.at[i], ctx=layer).start()
            push(router_mid, router_far.at[c], ss_t.at[i], rs_t.at[i], ctx=layer).start()
        pltpu.make_async_copy(gains_mid, gains_far.at[c], local.at[1]).start()
        pltpu.make_async_copy(router_mid, router_far.at[c], local.at[2]).start()

    def small_all():
        pltpu.make_async_copy(gains_mid, gains_far.at[c], local.at[1]).wait()
        pltpu.make_async_copy(router_mid, router_far.at[c], local.at[2]).wait()
        for i, layer in enumerate(layers):
            push(gains_mid, gains_far.at[c], ss_h.at[i], rs_h.at[i], ctx=layer).wait()
            push(router_mid, router_far.at[c], ss_t.at[i], rs_t.at[i], ctx=layer).wait()
        gains_out[...] = gains_far[0]
        router_out[...] = router_far[0]
        for i in range(1, n_ctx):
            gains_out[...] += gains_far[i]
            router_out[...] += router_far[i]

    lag, ahead = 2, 6
    for which, j in steps[:ahead]:
        which.outermost(j)
    for d in list(range(1, chips)) + [0]:
        product(d)
    side = [functools.partial(chip_sum, d) for d in range(1, chips)] + [last_sum, small_plane]
    for n in range(len(steps) + lag):
        if n + ahead < len(steps):
            steps[n + ahead][0].outermost(steps[n + ahead][1])
        if n < len(steps):
            steps[n][0].first_half(steps[n][1])
        if n >= lag:
            steps[n - lag][0].second_half(steps[n - lag][1])
        if n >= 2 and side:
            side.pop(0)()
    for job in side:
        job()
    small_all()
    for which, j in steps:
        which.drain(j)


def finish(n_ctx, n_shard, q_cols, weights, wide, router, gains, left, right, tokens, gain, ident):
    n, rows, cols = weights.shape
    router_shape = router.shape[1:]
    count, width = tokens.shape
    chips = n // 2
    tile = 512
    wides = wide.shape[0]
    return call(
        functools.partial(finish_body, n_ctx, n, q_cols, tile),
        [
            jax.ShapeDtypeStruct((rows, n * q_cols), BF), jax.ShapeDtypeStruct((n, rows, 128), BF),
            jax.ShapeDtypeStruct(wide.shape, BF),
            jax.ShapeDtypeStruct(router_shape, F32), jax.ShapeDtypeStruct(gains.shape, F32),
            jax.ShapeDtypeStruct((count, width), F32),
        ],
        [VMEM] * 8,
        [
            pltpu.VMEM((2,) + wide.shape, BF), pltpu.VMEM(wide.shape, BF), pltpu.VMEM(wide.shape, BF),
            DMA((wides,)), DMA((2, wides)), DMA((wides,)), DMA((wides,)),
            pltpu.VMEM((n, rows, cols), BF), pltpu.VMEM((2, n, rows, cols), BF),
            pltpu.VMEM((n, rows, cols), BF), pltpu.VMEM((n, rows, cols), BF),
            pltpu.VMEM((n - 1,) + router_shape, BF), pltpu.VMEM(router_shape, F32),
            pltpu.VMEM((n_ctx,) + router_shape, F32),
            pltpu.VMEM(gains.shape, F32), pltpu.VMEM((n,) + gains.shape, F32),
            pltpu.VMEM(gains.shape, F32), pltpu.VMEM((n_ctx,) + gains.shape, F32),
            pltpu.VMEM((2, count, tile), F32), pltpu.VMEM((chips, count, width), F32),
            pltpu.VMEM((chips, count, width), BF), pltpu.VMEM((chips, count, width), BF),
            pltpu.VMEM((chips - 1, count, width), BF), pltpu.VMEM((chips - 1, count, width), BF),
            DMA((3,)), DMA((n - 1,)), DMA((n - 1,)), DMA((n,)), DMA((2, n)), DMA((n,)),
            DMA((n,)), DMA((n,)), DMA((n - 1,)), DMA((n - 1,)), DMA((n - 1,)), DMA((n - 1,)),
            DMA((n_ctx - 1,)), DMA((n_ctx - 1,)), DMA((n_ctx - 1,)), DMA((n_ctx - 1,)),
            DMA((chips,)), DMA((chips,)), DMA((chips - 1,)), DMA((chips - 1,)),
        ],
        ident, (weights, wide, router, gains, left, right, tokens, gain), mib=60,
        out_specs=[ANY, ANY, ANY, VMEM, VMEM, VMEM],
    )


def back_body(n_ctx, n_shard, heads, wides,
              grad_out, q, kv, attn, qpre, kvpre, w_out, rows_in, w_all, cosine, sine, bias, q_gain, k_gain,
              tokens, gain, gains, router,
              q_out, kv_out, wide_out, router_out, gains_out, rows_out,
              grads, rows_all, attn_t, grad_heads, ds_all, p_all, parts, pre, q_sum, k_sum, wide, weights,
              sibk, zsend, zrecv, wide_landing, pieces, landing,
              own_part, pair, to_sib, sib, to_chip, got, router_in, router_mid, router_far,
              gains_own, gains_in, gains_mid, gains_far, local,
              ss_row, rs_row, ss_fwd, rs_fwd, ss_sk, rs_sk, ss_zk, rs_zk,
              ss_wi, rs_wi, ss_wo, ss_wc, ss_w, rs_w, ss_i, rs_i, ss_o, ss_q, ss_k,
              ss_r, rs_r, ss_g, rs_g, ss_h, rs_h, ss_t, rs_t, ss_s, rs_s, ss_c, rs_c):
    c, s, parity, sibling, others, layers = here(n_ctx, n_shard)
    half = n_ctx // 2
    chips = n_shard // 2
    chip = lax.div(s, 2)
    mates = [lax.rem(s + 2 * d, n_shard) for d in range(1, chips)]
    left_side = c < half
    depth = jnp.where(left_side, c, n_ctx - 1 - c)
    inner = jnp.where(left_side, c + 1, c - 1)
    outer = jnp.clip(jnp.where(left_side, c - 1, c + 1), 0, n_ctx - 1)
    middle = depth == half - 1
    inside = depth > 0
    count, width = tokens.shape
    wr = w_all.shape[1]
    cols = heads * HEAD_DIM
    keys = n_ctx * count
    scaling = HEAD_DIM ** -0.5
    own_copies = [
        pltpu.make_async_copy(grad_out, grads.at[s], local.at[0]),
        pltpu.make_async_copy(rows_in, rows_all, local.at[1]),
    ]
    for item in own_copies:
        item.start()
    greet(others, layers)

    first, forwards = {}, {}
    for d in range(1, chips):
        first[d] = push(grad_out, grads.at[s], ss_row.at[d], rs_row.at[d], shard=mates[d - 1])
        first[d].start()
    forwards[0] = push(grad_out, grads.at[s], ss_fwd.at[0], rs_fwd.at[0], shard=sibling)
    forwards[0].start()
    small = []
    for i, peer in enumerate(others):
        item = push(router.at[peer], router_in.at[i], ss_r.at[i], rs_r.at[i], shard=peer)
        item.start()
        small.append(item)
    q_sum[...] = jnp.zeros_like(q_sum)
    k_sum[...] = jnp.zeros_like(k_sum)

    def norm_back(grad, value, norm_gain, total):
        unit, scale = unit_rows(value)
        grad = grad * cosine[...] + pltpu.roll(grad * sine[...], HEAD_DIM // 2, 1)
        total[...] += jnp.sum(grad * unit, axis=0, keepdims=True)
        scaled = grad * norm_gain[...]
        return scale * (scaled - unit * jnp.mean(scaled * unit, axis=-1, keepdims=True))

    near, far = {}, {}

    def seqs_of(d):
        return 2 * lax.rem(chip + chips - d, chips)

    def attention_back(d):
        fs = seqs_of(d)
        grad = lax.dot_general(grads[pl.ds(fs, 2)].reshape(2 * count, width), w_out[...],
                               (((1,), (1,)), ((), ())), preferred_element_type=F32)
        grad_heads[...] = grad.reshape(2, count, cols).astype(BF)

        @pl.loop(0, 2)
        def _(i):
            b = fs + i
            k_all = kv[0, b].reshape(keys, HEAD_DIM)
            v_all = kv[1, b].reshape(keys, HEAD_DIM)
            for h in range(heads):
                hs = slice(h * HEAD_DIM, (h + 1) * HEAD_DIM)
                rs = slice(h * count, (h + 1) * count)
                scores = lax.dot_general(q[b, :, hs], k_all, (((1,), (1,)), ((), ())), preferred_element_type=F32)
                scores = scores * scaling + bias[...]
                raised = jnp.exp(scores - jnp.max(scores, axis=-1, keepdims=True))
                probs = raised / jnp.sum(raised, axis=-1, keepdims=True)
                grad_p = lax.dot_general(grad_heads[i, :, hs], v_all, (((1,), (1,)), ((), ())),
                                         preferred_element_type=F32)
                delta = jnp.sum(probs * grad_p, axis=-1, keepdims=True)
                ds = (probs * (grad_p - delta)).astype(BF)
                ds_all[rs, :] = ds
                p_all[rs, :] = probs.astype(BF)
                grad_q = jnp.dot(ds, k_all, preferred_element_type=F32) * scaling
                pre[b, :, hs] = norm_back(grad_q, qpre[b, :, hs], q_gain, q_sum).astype(BF)
            grad_k, grad_v = jnp.zeros((keys, HEAD_DIM), F32), jnp.zeros((keys, HEAD_DIM), F32)
            stacked_q = jnp.concatenate([q[b, :, h * HEAD_DIM : (h + 1) * HEAD_DIM] for h in range(heads)], axis=0)
            stacked_g = jnp.concatenate(
                [grad_heads[i, :, h * HEAD_DIM : (h + 1) * HEAD_DIM] for h in range(heads)], axis=0
            )
            grad_k = lax.dot_general(ds_all[...], stacked_q, (((0,), (0,)), ((), ())), preferred_element_type=F32)
            grad_v = lax.dot_general(p_all[...], stacked_g, (((0,), (0,)), ((), ())), preferred_element_type=F32)
            parts[0, b] = (grad_k * scaling).astype(BF).reshape(n_ctx, count, HEAD_DIM)
            parts[1, b] = grad_v.astype(BF).reshape(n_ctx, count, HEAD_DIM)

        near[d] = push(parts.at[1 - parity, pl.ds(fs, 2)], sibk.at[d], ss_sk.at[d], rs_sk.at[d], shard=sibling)
        near[d].start()

    def key_sum(d):
        fs = seqs_of(d)
        near[d].wait()
        for i, layer in enumerate(layers):
            zsend[d, i] = (
                parts[parity, pl.ds(fs, 2), layer].astype(F32) + sibk[d, :, layer].astype(F32)
            ).astype(BF)
            far[d, i] = push(zsend.at[d, i], zrecv.at[d, i], ss_zk.at[d, i], rs_zk.at[d, i], ctx=layer)
            far[d, i].start()

    for d in range(chips):
        if d:
            first[d].wait()
            origin = lax.rem(s + n_shard - 2 * d, n_shard)
            forwards[d] = push(grads.at[origin], grads.at[origin], ss_fwd.at[d], rs_fwd.at[d], shard=sibling)
            forwards[d].start()
        else:
            own_copies[0].wait()
        forwards[d].wait()
        attention_back(d)
        if d:
            key_sum(d - 1)
    key_sum(chips - 1)

    def out_copies(j, ref):
        source = lax.rem(s + n_shard - j, n_shard)
        to = pl.ds(pl.multiple_of(source * cols, cols), cols)
        return (
            pltpu.make_async_copy(ref.at[:, pl.ds(0, cols)], q_out.at[:, to], ss_q.at[j]),
            pltpu.make_async_copy(ref.at[:, pl.ds(cols, HEAD_DIM)], kv_out.at[source], ss_k.at[j]),
        )

    def wide_copies(j, ref):
        step = wide.shape[2]
        return (pltpu.make_async_copy(ref, wide_out.at[:, pl.ds(j * step, step)], ss_wc.at[j]),)

    class Line:
        def __init__(self, ready, own, landing, ss_i, rs_i, ss_o, copies):
            self.ready, self.own, self.landing = ready, own, landing
            self.ss_i, self.rs_i, self.ss_o, self.copies = ss_i, rs_i, ss_o, copies

        def inward(self, j, ref):
            at = jnp.where(middle, 1, 0)
            return push(ref, self.landing.at[at, j], self.ss_i.at[j], self.rs_i.at[at, j], ctx=inner)

        def outward(self, j):
            return push(self.landing.at[1, j], self.landing.at[1, j], self.ss_o.at[j], self.rs_i.at[1, j], ctx=outer)

        def arrived(self, which, j):
            push(self.landing.at[0, j], self.landing.at[which, j], self.ss_i.at[j], self.rs_i.at[which, j],
                 ctx=inner).wait_recv()

        def outermost(self, j):
            @pl.when(jnp.logical_not(inside))
            def _():
                self.ready(j)
                self.inward(j, self.own(j)).start()

        def first_half(self, j):
            @pl.when(inside)
            def _():
                self.ready(j)
                self.arrived(0, j)
                self.landing[0, j] = (self.own(j)[...].astype(F32) + self.landing[0, j].astype(F32)).astype(BF)
                self.inward(j, self.landing.at[0, j]).start()

        def second_half(self, j):
            self.arrived(1, j)

            @pl.when(middle)
            def _():
                self.landing[1, j] = (self.landing[0, j].astype(F32) + self.landing[1, j].astype(F32)).astype(BF)

            @pl.when(inside)
            def _():
                self.outward(j).start()

            for item in self.copies(j, self.landing.at[1, j]):
                item.start()

        def drain(self, j):
            self.inward(j, self.landing.at[0, j]).wait_send()

            @pl.when(inside)
            def _():
                self.outward(j).wait_send()

            for item in self.copies(j, self.landing.at[1, j]):
                item.wait()

    sends = [None]
    line = Line(lambda j: sends[j].wait() if j else None, lambda j: pieces.at[j] if j else weights.at[s],
                landing, ss_i, rs_i, ss_o, out_copies)
    wide_line = Line(lambda j: None, lambda j: wide.at[j], wide_landing, ss_wi, rs_wi, ss_wo, wide_copies)
    steps = [(wide_line, j) for j in range(wides)] + [(line, j) for j in range(n_shard)]
    lag, ahead = 2, 6

    attn_t[...] = attn[...].reshape(n_shard * count, cols).T
    step = width // wides
    for j in range(wides):
        block = grads[:, :, j * step : (j + 1) * step].reshape(n_shard * count, step)
        wide[j] = jnp.dot(attn_t[...], block, preferred_element_type=F32).astype(BF)
        if j < ahead:
            wide_line.outermost(j)

    own_copies[1].wait()

    @pl.loop(0, n_shard)
    def _(e):
        block = rows_all[:, :, pl.ds(pl.multiple_of(e * wr, wr), wr)].reshape(n_shard * count, wr)
        right = pre[:, :, pl.ds(0, cols)].reshape(n_shard * count, cols)
        weights[e, :, pl.ds(0, cols)] = lax.dot_general(
            block, right, (((0,), (0,)), ((), ())), preferred_element_type=F32).astype(BF)

    wide_line.first_half(0)
    for d in range(chips):
        fs = seqs_of(d)
        total = parts[parity, pl.ds(fs, 2), c].astype(F32) + sibk[d, :, c].astype(F32)
        for i in range(n_ctx - 1):
            far[d, i].wait()
            total = total + zrecv[d, i].astype(F32)
        for i in range(2):
            keyed = norm_back(total[i], kvpre[fs + i], k_gain, k_sum)
            pre[fs + i, :, pl.ds(cols, HEAD_DIM)] = jnp.where(parity == 0, keyed, total[i]).astype(BF)

    @pl.loop(0, n_shard)
    def _(e):
        block = rows_all[:, :, pl.ds(pl.multiple_of(e * wr, wr), wr)].reshape(n_shard * count, wr)
        right = pre[:, :, pl.ds(cols, HEAD_DIM)].reshape(n_shard * count, HEAD_DIM)
        weights[e, :, pl.ds(cols, HEAD_DIM)] = lax.dot_general(
            block, right, (((0,), (0,)), ((), ())), preferred_element_type=F32).astype(BF)

    for i, peer in enumerate(others):
        item = push(weights.at[peer], pieces.at[i + 1], ss_w.at[i], rs_w.at[i], shard=peer)
        item.start()
        sends.append(item)

    order = list(range(1, chips)) + [0]
    to_sibling, to_mate = {}, {}

    def product(at):
        fs = 2 * lax.rem(chip + order[at], chips)
        left = pre[pl.ds(fs, 2)].reshape(2 * count, cols + HEAD_DIM)

        @pl.loop(0, n_shard)
        def _(j):
            part = pl.ds(pl.multiple_of(j * wr, wr), wr)
            value = lax.dot_general(left, w_all[j], (((1,), (1,)), ((), ())), preferred_element_type=F32)
            pair[...] = value.reshape(2, count, wr)
            own_part[at % 2, :, part] = pair[parity]
            to_sib[at, :, part] = pair[1 - parity].astype(BF)

        to_sibling[at] = push(to_sib.at[at], sib.at[at], ss_s.at[at], rs_s.at[at], shard=sibling)
        to_sibling[at].start()

    def chip_sum(at):
        to_sibling[at].wait()
        to_chip[at] = (own_part[at % 2] + sib[at].astype(F32)).astype(BF)
        to_mate[at] = push(to_chip.at[at], got.at[at], ss_c.at[at], rs_c.at[at], shard=mates[order[at] - 1])
        to_mate[at].start()

    gain_sends = []

    def last_sum():
        to_sibling[chips - 1].wait()
        grad = own_part[(chips - 1) % 2] + sib[chips - 1].astype(F32)
        for at in range(chips - 1):
            to_mate[at].wait()
            grad = grad + got[at].astype(F32)
        unit, scale = unit_rows(tokens[...].astype(F32))
        scaled = grad * gain[...]
        rows_out[...] = scale * (scaled - unit * jnp.mean(scaled * unit, axis=-1, keepdims=True))
        gains_own[...] = gains[...]
        gains_own[0:1] = jnp.sum(grad * unit, axis=0, keepdims=True)
        gains_own[2:3, 0:HEAD_DIM] = q_sum[...]
        gains_own[2:3, HEAD_DIM : 2 * HEAD_DIM] = jnp.where(parity == 0, k_sum[...], jnp.zeros_like(k_sum))
        mine = pltpu.make_async_copy(gains_own, gains_in.at[s], local.at[2])
        mine.start()
        gain_sends.append(mine)
        for i, peer in enumerate(others):
            item = push(gains_own, gains_in.at[s], ss_g.at[i], rs_g.at[i], shard=peer)
            item.start()
            gain_sends.append(item)

    def small_plane():
        for item in small + gain_sends:
            item.wait()
        gains_mid[...] = gains_in[0]
        for i in range(1, n_shard):
            gains_mid[...] += gains_in[i]
        router_mid[...] = router[s].astype(F32)
        for i in range(n_shard - 1):
            router_mid[...] += router_in[i].astype(F32)
        for i, layer in enumerate(layers):
            push(gains_mid, gains_far.at[c], ss_h.at[i], rs_h.at[i], ctx=layer).start()
            push(router_mid, router_far.at[c], ss_t.at[i], rs_t.at[i], ctx=layer).start()
        pltpu.make_async_copy(gains_mid, gains_far.at[c], local.at[3]).start()
        pltpu.make_async_copy(router_mid, router_far.at[c], local.at[4]).start()

    def small_all():
        pltpu.make_async_copy(gains_mid, gains_far.at[c], local.at[3]).wait()
        pltpu.make_async_copy(router_mid, router_far.at[c], local.at[4]).wait()
        for i, layer in enumerate(layers):
            push(gains_mid, gains_far.at[c], ss_h.at[i], rs_h.at[i], ctx=layer).wait()
            push(router_mid, router_far.at[c], ss_t.at[i], rs_t.at[i], ctx=layer).wait()
        gains_out[...] = gains_far[0]
        router_out[...] = router_far[0]
        for i in range(1, n_ctx):
            gains_out[...] += gains_far[i]
            router_out[...] += router_far[i]

    side = []
    for at in range(chips):
        side.append(functools.partial(product, at))
        if at:
            side.append(functools.partial(chip_sum, at - 1))
    side += [last_sum, small_plane]
    for n in range(1, len(steps) + lag):
        if n + ahead - 1 < len(steps):
            steps[n + ahead - 1][0].outermost(steps[n + ahead - 1][1])
        if n < len(steps):
            steps[n][0].first_half(steps[n][1])
        if n >= lag:
            steps[n - lag][0].second_half(steps[n - lag][1])
        if side:
            side.pop(0)()
    for job in side:
        job()
    small_all()
    for which, j in steps:
        which.drain(j)


def back(n_ctx, n_shard, heads, args, ident):
    count, width = args[0].shape
    rows_in, w_all, router, gains = args[7], args[8], args[17], args[16]
    n, z, chips, wides = n_shard, n_ctx, n_shard // 2, 8
    wr, cols = w_all.shape[1], heads * HEAD_DIM
    keys = z * count
    sds, scratch = jax.ShapeDtypeStruct, pltpu.VMEM
    router_shape = router.shape[1:]
    dma = lambda *shape: DMA(shape)
    wide_block, block = (cols, width // wides), (wr, cols + HEAD_DIM)
    return call(
        functools.partial(back_body, z, n, heads, wides),
        [
            sds((wr, n * cols), BF), sds((n, wr, HEAD_DIM), BF), sds((cols, width), BF), sds(router_shape, F32),
            sds(gains.shape, F32), sds((count, width), F32),
        ],
        [VMEM] * 7 + [ANY] + [VMEM] * 10,
        [
            scratch((n, count, width), BF), scratch((n, count, width), BF), scratch((cols, n * count), BF),
            scratch((2, count, cols), BF), scratch((heads * count, keys), BF), scratch((heads * count, keys), BF),
            scratch((2, n, z, count, HEAD_DIM), BF), scratch((n, count, cols + HEAD_DIM), BF),
            scratch((1, HEAD_DIM), F32), scratch((1, HEAD_DIM), F32),
            scratch((wides,) + wide_block, BF), scratch((n,) + block, BF),
            scratch((chips, 2, z, count, HEAD_DIM), BF), scratch((chips, z - 1, 2, count, HEAD_DIM), BF),
            scratch((chips, z - 1, 2, count, HEAD_DIM), BF), scratch((2, wides) + wide_block, BF),
            scratch((n,) + block, BF), scratch((2, n) + block, BF),
            scratch((2, count, width), F32), scratch((2, count, wr), F32), scratch((chips, count, width), BF),
            scratch((chips, count, width), BF), scratch((chips - 1, count, width), BF),
            scratch((chips - 1, count, width), BF),
            scratch((n - 1,) + router_shape, BF), scratch(router_shape, F32), scratch((z,) + router_shape, F32),
            scratch(gains.shape, F32), scratch((n,) + gains.shape, F32), scratch(gains.shape, F32),
            scratch((z,) + gains.shape, F32), dma(5),
            dma(chips), dma(chips), dma(chips), dma(chips), dma(chips), dma(chips), dma(chips, z - 1), dma(chips, z - 1),
            dma(wides), dma(2, wides), dma(wides), dma(wides), dma(n - 1), dma(n - 1), dma(n), dma(2, n), dma(n), dma(n),
            dma(n), dma(n - 1), dma(n - 1), dma(n - 1), dma(n - 1), dma(z - 1), dma(z - 1), dma(z - 1), dma(z - 1),
            dma(chips), dma(chips), dma(chips - 1), dma(chips - 1),
        ],
        ident, args, mib=62, out_specs=[ANY, ANY, ANY, VMEM, VMEM, VMEM],
    )


def dispatch_body(n_ctx, n_shard, group, tile, rows, tail, code, recv, tail_recv,
                  zrows, ztail, ready, tail_ready, local, ss_z, rs_z, ss_t, rs_t, ss_x, rs_x, ss_y, rs_y):
    c, s, parity, sibling, others, layers = here(n_ctx, n_shard)
    greet(others, layers)
    count, width = rows.shape
    groups = n_ctx // group
    slots = recv.shape[2]
    own = [pltpu.make_async_copy(rows, zrows.at[c], local.at[0]), pltpu.make_async_copy(tail, ztail.at[c], local.at[1])]
    fans = [
        Fan(n_ctx, c, lambda d: ztail.at[flip_bits(c, d)], ss_t, rs_t, True),
        Fan(n_ctx, c, lambda d: zrows.at[flip_bits(c, d)], ss_z, rs_z, True),
    ]
    fans[0].send(0, tail)
    fans[1].send(0, rows)
    for item in own:
        item.start()
    waits = []
    seen = set()
    for k in range(groups):
        at = flip_bits(lax.div(c, group), k)
        if k == 0:
            for item in own:
                item.wait()
        table = slot_table(code[at], slots)
        for d in fans[0].order():
            if d < (k + 1) * group and d not in seen:
                fans[0].arrival(d)
                fans[1].arrival(d)
                seen.add(d)
        first = pl.multiple_of(at * group, group)
        block = ztail[pl.ds(first, group)].reshape(group * count, -1)
        tail_ready[k] = jnp.dot(table, block, preferred_element_type=F32).astype(BF).reshape(n_shard, slots, -1)

        @pl.loop(0, width // tile)
        def _(j):
            cols = pl.ds(pl.multiple_of(j * tile, tile), tile)
            block = zrows[pl.ds(first, group), :, cols].reshape(group * count, tile)
            value = jnp.dot(table, block, preferred_element_type=F32).astype(BF)
            ready[k, :, :, cols] = value.reshape(n_shard, slots, tile)

        for i, peer in enumerate(others):
            item = push(ready.at[k, peer], recv.at[s, at], ss_x.at[k, i], rs_x.at[k, i], shard=peer)
            item.start()
            waits.append(item)
            item = push(tail_ready.at[k, peer], tail_recv.at[s, at], ss_y.at[k, i], rs_y.at[k, i], shard=peer)
            item.start()
            waits.append(item)
        item = pltpu.make_async_copy(ready.at[k, s], recv.at[s, at], local.at[2 * k + 2])
        item.start()
        waits.append(item)
        item = pltpu.make_async_copy(tail_ready.at[k, s], tail_recv.at[s, at], local.at[2 * k + 3])
        item.start()
        waits.append(item)
    for fan in fans:
        fan.drain()
    for item in waits:
        item.wait()


def dispatch_rows(n_ctx, n_shard, group, capacity, rows, tail, code, ident):
    groups, slots = code.shape[0], group * capacity
    count, width = rows.shape
    few = tail.shape[1]
    return call(
        functools.partial(dispatch_body, n_ctx, n_shard, group, 512),
        [
            jax.ShapeDtypeStruct((n_shard, groups, slots, width), BF),
            jax.ShapeDtypeStruct((n_shard, groups, slots, few), BF),
        ],
        [VMEM, VMEM, VMEM],
        [
            pltpu.VMEM((n_ctx, count, width), BF), pltpu.VMEM((n_ctx, count, few), BF),
            pltpu.VMEM((groups, n_shard, slots, width), BF), pltpu.VMEM((groups, n_shard, slots, few), BF),
            DMA((2 * groups + 2,)), DMA((n_ctx,)), DMA((n_ctx,)), DMA((n_ctx,)), DMA((n_ctx,)),
        ] + [DMA((groups, n_shard - 1))] * 4,
        ident, (rows, tail, code), mib=56,
    )


def combine_body(n_ctx, n_shard, group, tile, rows, tail, mix, code, out, tail_out, mix_out,
                 land, tail_land, value, tail_value, zsend, zrecv, tsend, trecv, msend, mrecv, mix_kept, table, local,
                 ss_x, rs_x, ss_y, rs_y, ss_z, rs_z, ss_t, rs_t, ss_m, rs_m):
    c, s, parity, sibling, others, layers = here(n_ctx, n_shard)
    greet(others, layers)
    count, width = out.shape
    groups = n_ctx // group
    slots = rows.shape[2]
    near = {}
    for k in reversed(range(groups)):
        at = flip_bits(lax.div(c, group), k)
        near[k] = []
        for i, peer in enumerate(others):
            item = push(rows.at[peer, at], land.at[k, s], ss_x.at[k, i], rs_x.at[k, i], shard=peer)
            item.start()
            near[k].append(item)
            item = push(tail.at[peer, at], tail_land.at[k, s], ss_y.at[k, i], rs_y.at[k, i], shard=peer)
            item.start()
            near[k].append(item)
        item = pltpu.make_async_copy(rows.at[s, at], land.at[k, s], local.at[k, 0])
        item.start()
        near[k].append(item)
        item = pltpu.make_async_copy(tail.at[s, at], tail_land.at[k, s], local.at[k, 1])
        item.start()
        near[k].append(item)
    for k in range(groups):
        table[k] = slot_table(code[flip_bits(lax.div(c, group), k)], slots).T

    def local_sums(k, block_of):
        @pl.loop(0, width // tile)
        def _(j):
            cols = pl.ds(pl.multiple_of(j * tile, tile), tile)
            value[:, cols] = jnp.dot(table[k], block_of(cols), preferred_element_type=F32)

    def part(ref, d):
        place = lax.rem(flip_bits(c, d), group)
        return ref[pl.ds(pl.multiple_of(place * count, count), count), :]

    def in_group(k):
        return sorted(range(k * group, (k + 1) * group), key=lambda d: (lowest(d) or n_ctx, d))

    mix_fold = Fold(c, msend, mrecv, ss_m, rs_m)
    for k in reversed(range(groups)):
        at = flip_bits(lax.div(c, group), k)
        local_sums(k, lambda cols: mix[:, at, :, cols].reshape(n_shard * slots, tile))
        for d in in_group(k):
            if lowest(d) == 1:
                mix_fold.give(d, part(value, d))
            else:
                mix_kept[d // 2] = part(value, d)
    fold = Fold(c, zsend, zrecv, ss_z, rs_z)
    tail_fold = Fold(c, tsend, trecv, ss_t, rs_t)
    for k in reversed(range(groups)):
        for item in near[k]:
            item.wait()
        local_sums(k, lambda cols: land[k, :, :, cols].reshape(n_shard * slots, tile))
        tail_value[...] = jnp.dot(
            table[k], tail_land[k].reshape(n_shard * slots, -1), preferred_element_type=F32
        )
        for d in in_group(k):
            if lowest(d) == 1:
                fold.give(d, part(value, d))
                tail_fold.give(d, part(tail_value, d))
        for d in in_group(k):
            if lowest(d) != 1:
                if d:
                    mix_fold.give(d, mix_fold.take(d, mix_kept[d // 2]))
                    fold.give(d, fold.take(d, part(value, d)))
                    tail_fold.give(d, tail_fold.take(d, part(tail_value, d)))
                else:
                    mix_out[...] = mix_fold.take(0, mix_kept[0])
                    out[...] = fold.take(0, part(value, 0))
                    tail_out[...] = tail_fold.take(0, part(tail_value, 0))
    for item in (mix_fold, fold, tail_fold):
        item.drain()


def combine_rows(n_ctx, n_shard, group, rows, tail, mix, code, ident):
    groups, slots, width = rows.shape[1:]
    few = tail.shape[3]
    count = code.shape[2] // group
    sds = jax.ShapeDtypeStruct
    return call(
        functools.partial(combine_body, n_ctx, n_shard, group, 512),
        [sds((count, width), F32), sds((count, few), F32), sds((count, width), F32)],
        [VMEM] * 4,
        [
            pltpu.VMEM((groups, n_shard, slots, width), BF), pltpu.VMEM((groups, n_shard, slots, few), BF),
            pltpu.VMEM((group * count, width), F32), pltpu.VMEM((group * count, few), F32),
            pltpu.VMEM((n_ctx - 1, count, width), BF), pltpu.VMEM((n_ctx - 1, count, width), BF),
            pltpu.VMEM((n_ctx - 1, count, few), BF), pltpu.VMEM((n_ctx - 1, count, few), BF),
            pltpu.VMEM((n_ctx - 1, count, width), BF), pltpu.VMEM((n_ctx - 1, count, width), BF),
            pltpu.VMEM((n_ctx // 2, count, width), F32), pltpu.VMEM((groups, group * count, n_shard * slots), BF),
            DMA((groups, 2)),
        ] + [DMA((groups, n_shard - 1))] * 4 + [DMA((n_ctx,))] * 6,
        ident, (rows, tail, mix, code), mib=60, out_specs=[VMEM] * 3,
    )


def expert_body(n_ctx, n_shard, group, half, tile,
                rows, tail, code, w_gate, w_up, w_down, cot_in,
                out, tail_out, mix_out, g_gate, g_up, g_down,
                zrows, ztail, ready, tail_ready, recv, tail_recv, cot, back_rows, back_tail, land, tail_land, mix_land,
                hidden, grad_gate, grad_up, work, slot_dot, table, tail_value,
                zrecv, tsend, trecv, mrecv, stage, stage_d, local,
                ss_z, rs_z, ss_t, rs_t, ss_x, rs_x, ss_y, rs_y, ss_d, rs_d, ss_e, rs_e, ss_m, rs_m,
                ss_fz, rs_fz, ss_ft, rs_ft, ss_fm, rs_fm, ss_st, ss_sd):
    c, s, parity, sibling, others, layers = here(n_ctx, n_shard)
    count, width = rows.shape
    few = tail.shape[1]
    inner = w_gate.shape[1]
    groups = n_ctx // group
    slots = recv.shape[2]
    chunk = half * slots
    experts = n_ctx * n_shard
    expert = c * n_shard + s
    loads = [
        pltpu.make_async_copy(rows, zrows.at[c], local.at[0]),
        pltpu.make_async_copy(tail, ztail.at[c], local.at[1]),
    ] + [
        pltpu.make_async_copy(cot_in.at[flip_bits(lax.div(c, group), k)], cot.at[k], local.at[2 + 2 * groups + k])
        for k in range(groups)
    ]
    for item in loads:
        item.start()
    greet(others, layers)
    fans = [
        Fan(n_ctx, c, lambda d: ztail.at[flip_bits(c, d)], ss_t, rs_t, True),
        Fan(n_ctx, c, lambda d: zrows.at[flip_bits(c, d)], ss_z, rs_z, True),
    ]
    fans[0].send(0, tail)
    fans[1].send(0, rows)

    sent = {}
    seen = set()
    loads[0].wait()
    loads[1].wait()
    for k in range(groups):
        at = flip_bits(lax.div(c, group), k)
        picks = slot_table(code[at], slots)
        table[k] = picks.T
        for d in fans[0].order():
            if d < (k + 1) * group and d not in seen:
                fans[0].arrival(d)
                fans[1].arrival(d)
                seen.add(d)
        first = pl.multiple_of(at * group, group)
        block = ztail[pl.ds(first, group)].reshape(group * count, few)
        tail_ready[k] = jnp.dot(picks, block, preferred_element_type=F32).astype(BF).reshape(n_shard, slots, few)

        @pl.loop(0, width // tile)
        def _(j):
            cols = pl.ds(pl.multiple_of(j * tile, tile), tile)
            block = zrows[pl.ds(first, group), :, cols].reshape(group * count, tile)
            moved = jnp.dot(picks, block, preferred_element_type=F32).astype(BF)
            ready[k, :, :, cols] = moved.reshape(n_shard, slots, tile)

        sent[k] = []
        for i, peer in enumerate(others):
            sent[k].append(push(ready.at[k, peer], recv.at[k, s], ss_x.at[k, i], rs_x.at[k, i], shard=peer))
            sent[k].append(push(tail_ready.at[k, peer], tail_recv.at[k, s], ss_y.at[k, i], rs_y.at[k, i], shard=peer))
        sent[k].append(pltpu.make_async_copy(ready.at[k, s], recv.at[k, s], local.at[2 + 2 * k]))
        sent[k].append(pltpu.make_async_copy(tail_ready.at[k, s], tail_recv.at[k, s], local.at[3 + 2 * k]))
        for item in sent[k]:
            item.start()
    for fan in fans:
        fan.drain()
    for item in loads[2:]:
        item.wait()

    gate_pre, up_pre = work.at[0:chunk, 0:inner], work.at[0:chunk, inner : 2 * inner]
    value = work.at[0 : group * count, 0:width]
    column = lax.broadcasted_iota(jnp.int32, (1, few), 1)
    is_coarse, is_fine = column == expert, column == experts + expert

    def send_back(src, dst, k, e, ss, rs):
        @pl.when(s != e)
        def _():
            push(src.at[k, e], dst.at[k, s], ss.at[k, e], rs.at[k, s], shard=e).start()

        @pl.when(s == e)
        def _():
            pltpu.make_async_copy(src.at[k, e], dst.at[k, e], rs.at[k, e]).start()

    def wait_back(src, dst, k, ss, rs):
        for e in range(n_shard):
            @pl.when(s != e)
            def _():
                push(src.at[k, e], dst.at[k, e], ss.at[k, e], rs.at[k, e], shard=e).wait()

            @pl.when(s == e)
            def _():
                pltpu.make_async_copy(src.at[k, e], dst.at[k, e], rs.at[k, e]).wait()

    def experts_part(k, h):
        of = slice(h * half, (h + 1) * half)
        r = pl.ds((k * n_shard + h * half) * slots, chunk)
        gates = jnp.sum(
            jnp.where(is_coarse | is_fine, tail_recv[k, of].reshape(chunk, few).astype(F32), 0.0), axis=1, keepdims=True
        )

        @pl.loop(0, inner // 256)
        def _(j):
            cols = pl.ds(pl.multiple_of(j * 256, 256), 256)
            x = recv[k, of].reshape(chunk, width)
            g = jnp.dot(x, w_gate[:, cols], preferred_element_type=F32)
            u = jnp.dot(x, w_up[:, cols], preferred_element_type=F32)
            gate_pre[:, cols] = g
            up_pre[:, cols] = u
            hidden[r, cols] = (g * jax.nn.sigmoid(g) * u).astype(BF)

        slot_dot[...] = jnp.zeros_like(slot_dot)

        @pl.loop(0, width // tile)
        def _(j):
            cols = pl.ds(pl.multiple_of(j * tile, tile), tile)
            o = jnp.dot(hidden[r, :], w_down[:, cols], preferred_element_type=F32).astype(BF).astype(F32)
            up_row = cot[k, of, :, cols].reshape(chunk, tile).astype(F32)
            slot_dot[...] += jnp.sum(o * up_row, axis=1, keepdims=True)
            ready[k, of, :, cols] = (gates * o).astype(BF).reshape(half, slots, tile)
            cot[k, of, :, cols] = (gates * up_row).astype(BF).reshape(half, slots, tile)

        coarse = slot_dot[...].astype(BF).astype(F32)
        fine = slot_dot[...] - coarse
        back_tail[k, of] = jnp.where(is_coarse, coarse, jnp.where(is_fine, fine, 0.0)).astype(BF).reshape(half, slots, few)

        @pl.loop(0, inner // 256)
        def _(j):
            cols = pl.ds(pl.multiple_of(j * 256, 256), 256)
            gh = lax.dot_general(cot[k, of].reshape(chunk, width), w_down[cols, :], (((1,), (1,)), ((), ())),
                                 preferred_element_type=F32)
            g, u = gate_pre[:, cols], up_pre[:, cols]
            sig = jax.nn.sigmoid(g)
            grad_gate[r, cols] = (gh * u * (sig * (1.0 + g * (1.0 - sig)))).astype(BF)
            grad_up[r, cols] = (gh * (g * sig)).astype(BF)

        @pl.loop(0, width // tile)
        def _(j):
            cols = pl.ds(pl.multiple_of(j * tile, tile), tile)
            gx = lax.dot_general(grad_gate[r, :], w_gate[cols, :], (((1,), (1,)), ((), ())), preferred_element_type=F32)
            gx += lax.dot_general(grad_up[r, :], w_up[cols, :], (((1,), (1,)), ((), ())), preferred_element_type=F32)
            back_rows[k, of, :, cols] = gx.astype(BF).reshape(half, slots, tile)

        for e in range(h * half, (h + 1) * half):
            send_back(back_rows, land, k, e, ss_d, rs_d)
            send_back(back_tail, tail_land, k, e, ss_e, rs_e)

    for k in range(groups):
        for item in sent[k]:
            item.wait()
        for h in range(n_shard // half):
            experts_part(k, h)
    for k in reversed(range(groups)):
        for e in range(n_shard):
            send_back(ready, mix_land, k, e, ss_m, rs_m)

    everything = groups * n_shard * slots

    def stage_out(j, which):
        at = pl.ds(pl.multiple_of(j * 256, 256), 256)
        return pltpu.make_async_copy(stage.at[which], (g_gate, g_up)[which].at[at], ss_st.at[which])

    @pl.loop(0, width // 256)
    def _(j):
        x = recv[:, :, :, pl.ds(pl.multiple_of(j * 256, 256), 256)].reshape(everything, 256)
        for which, grad in enumerate((grad_gate, grad_up)):
            total = lax.dot_general(x, grad[...], (((0,), (0,)), ((), ())), preferred_element_type=F32).astype(BF)

            @pl.when(j >= 1)
            def _():
                stage_out(j - 1, which).wait()

            stage[which] = total
            stage_out(j, which).start()

    def down_out(j):
        return pltpu.make_async_copy(stage_d, g_down.at[:, pl.ds(pl.multiple_of(j * 256, 256), 256)], ss_sd)

    @pl.loop(0, width // 256)
    def _(j):
        grad = cot[:, :, :, pl.ds(pl.multiple_of(j * 256, 256), 256)].reshape(everything, 256)
        total = lax.dot_general(
            hidden[...], grad, (((0,), (0,)), ((), ())), preferred_element_type=F32).astype(BF)

        @pl.when(j >= 1)
        def _():
            down_out(j - 1).wait()

        stage_d[...] = total
        down_out(j).start()

    last = width // 256 - 1
    stage_out(last, 0).wait()
    stage_out(last, 1).wait()
    down_out(last).wait()

    def local_sums(k, ref):
        @pl.loop(0, width // tile)
        def _(j):
            cols = pl.ds(pl.multiple_of(j * tile, tile), tile)
            block = ref[k, :, :, cols].reshape(n_shard * slots, tile)
            value[:, cols] = jnp.dot(table[k], block, preferred_element_type=F32)

    def part(ref, d):
        place = lax.rem(flip_bits(c, d), group)
        return ref[pl.ds(pl.multiple_of(place * count, count), count), :]

    def fold_group(k, fold, ref, into):
        for d in sorted(range(k * group, (k + 1) * group), key=lambda d: (lowest(d) or n_ctx, d)):
            if d:
                fold.give(d, fold.take(d, part(ref, d)) if lowest(d) > 1 else part(ref, d))
            else:
                into[...] = part(ref, 0)

    fold = Fold(c, zrows, zrecv, ss_fz, rs_fz)
    tail_fold = Fold(c, tsend, trecv, ss_ft, rs_ft)
    mix_fold = Fold(c, zrows, mrecv, ss_fm, rs_fm, {3: 3, 2: 0, 1: 2}, {2: (fold, 1), 1: (fold, 3)})
    for k in range(groups):
        wait_back(back_rows, land, k, ss_d, rs_d)
        wait_back(back_tail, tail_land, k, ss_e, rs_e)
        local_sums(k, land)
        tail_value[...] = jnp.dot(table[k], tail_land[k].reshape(n_shard * slots, few), preferred_element_type=F32)
        fold_group(k, tail_fold, tail_value, tail_out)
        fold_group(k, fold, value, out)
    for k in reversed(range(groups)):
        wait_back(ready, mix_land, k, ss_m, rs_m)
        local_sums(k, mix_land)
        fold_group(k, mix_fold, value, mix_out)
    out[...] = fold.take(0, out[...])
    tail_out[...] = tail_fold.take(0, tail_out[...])
    mix_out[...] = mix_fold.take(0, mix_out[...])
    for item in (fold, tail_fold, mix_fold):
        item.drain()


def run_experts(n_ctx, n_shard, group, capacity, rows, tail, code, w_gate, w_up, w_down, cot_rows, ident):
    n, z, groups, slots = n_shard, n_ctx, code.shape[0], group * capacity
    count, width = rows.shape
    few, inner, half = tail.shape[1], w_gate.shape[1], n_shard // 2
    everything, chunk = groups * n * slots, half * slots
    sds, scratch = jax.ShapeDtypeStruct, pltpu.VMEM
    dma = lambda *shape: DMA(shape)
    wide, thin = (groups, n, slots, width), (groups, n, slots, few)
    return call(
        functools.partial(expert_body, z, n, group, half, 512),
        [
            sds((count, width), F32), sds((count, few), F32), sds((count, width), F32),
            sds((width, inner), BF), sds((width, inner), BF), sds((inner, width), BF),
        ],
        [VMEM] * 6 + [ANY],
        [
            scratch((z, count, width), BF), scratch((z, count, few), BF), scratch(wide, BF), scratch(thin, BF),
            scratch(wide, BF), scratch(thin, BF), scratch(wide, BF), scratch(wide, BF), scratch(thin, BF),
            scratch(wide, BF), scratch(thin, BF), scratch(wide, BF),
            scratch((everything, inner), BF), scratch((everything, inner), BF), scratch((everything, inner), BF),
            scratch((max(chunk, group * count), max(2 * inner, width)), F32), scratch((chunk, 1), F32),
            scratch((groups, group * count, n * slots), BF),
            scratch((group * count, few), F32), scratch((z - 1, count, width), BF),
            scratch((z - 1, count, few), BF), scratch((z - 1, count, few), BF), scratch((z - 1, count, width), BF),
            scratch((2, 256, inner), BF), scratch((inner, 256), BF), dma(2 + 3 * groups),
        ] + [dma(z)] * 4 + [dma(groups, n - 1)] * 4 + [dma(groups, n)] * 6 + [dma(z)] * 6 + [dma(2), DMA],
        ident, (rows, tail, code, w_gate, w_up, w_down, cot_rows), mib=63, out_specs=[VMEM] * 3 + [ANY] * 3,
    )


def rms_scale(hidden, gain):
    return hidden * lax.rsqrt(jnp.mean(hidden * hidden, axis=-1, keepdims=True) + epsilon) * gain


def rotate(headwise, places):
    half_size = headwise.shape[-1] // 2
    frequency = rope_base ** (-jnp.arange(half_size, dtype=F32) * 2.0 / headwise.shape[-1])
    angles = places.astype(F32)[:, None] * frequency[None, :]
    cosine = jnp.cos(angles)[:, None, :]
    sine = jnp.sin(angles)[:, None, :]
    former = headwise[..., :half_size]
    latter = headwise[..., half_size:]
    return jnp.concatenate(
        [former * cosine - latter * sine, latter * cosine + former * sine], axis=-1
    )


def place_of(row_ids, order, block_rows):
    block_ids = jnp.arange(order.shape[0], dtype=jnp.int32)
    owner_block = row_ids // block_rows
    picked_block = jnp.sum(
        jnp.where(owner_block[:, None] == block_ids[None, :], order[None, :], 0), axis=1
    )
    return picked_block * block_rows + row_ids % block_rows


def dot(left, right):
    return jnp.dot(left, right, preferred_element_type=F32)


def contract_rows(left, right):
    return lax.dot_general(left, right, (((0,), (0,)), ((), ())), preferred_element_type=F32)


def contract_cols(left, right):
    return lax.dot_general(left, right, (((1,), (1,)), ((), ())), preferred_element_type=F32)


def exchange_shard(x):
    return lax.all_to_all(x, "shard", split_axis=0, concat_axis=0, tiled=True)


def gather_ctx(x):
    return lax.all_gather(x, "ctx", axis=0, tiled=False)


def shards(
    tokens,
    cotangent,
    block_order,
    routes,
    attn_gain,
    w_query,
    key_weight,
    value_weight,
    query_gain,
    key_gain,
    w_out,
    ffn_gain,
    w_router,
    w_gate,
    w_up,
    w_down,
):
    rows = tokens.shape[1]
    width = tokens.shape[2]
    ctx_count = lax.axis_size("ctx")
    shard_count = lax.axis_size("shard")
    my_ctx = lax.axis_index("ctx")
    my_shard = lax.axis_index("shard")
    experts = ctx_count * shard_count
    block_rows = rows // 2
    heads = QUERY_HEADS // shard_count
    head_cols = heads * HEAD_DIM
    sharers = shard_count // KEY_VALUE_HEADS
    score_scale = HEAD_DIM ** (-0.5)
    top_count = routes.shape[2]
    capacity = rows * top_count // experts + max(rows * top_count // (4 * experts), 1)
    sequence = rows * ctx_count
    plane = rows * shard_count
    wrows = width // shard_count

    inputs = tokens[0].astype(F32)
    upstream_b = cotangent[0]
    upstream = upstream_b.astype(F32)

    group = 1
    while group * capacity % 16:
        group *= 2
    groups = ctx_count // group
    slot_rows = shard_count * ctx_count * capacity
    block_shape = (shard_count, groups, group * capacity)
    row_ids = my_ctx * rows + jnp.arange(rows, dtype=jnp.int32)
    q_places = place_of(row_ids, block_order, block_rows)
    k_places = place_of(jnp.arange(sequence, dtype=jnp.int32), block_order, block_rows)
    bias = jnp.where(k_places[None, :] <= q_places[:, None], 0.0, -1e30).astype(F32)
    frequency = rope_base ** (-jnp.arange(HEAD_DIM // 2, dtype=F32) * 2.0 / HEAD_DIM)
    angles = q_places.astype(F32)[:, None] * frequency[None, :]
    cosine = jnp.concatenate([jnp.cos(angles)] * 2, axis=1)
    sine = jnp.concatenate([-jnp.sin(angles), jnp.sin(angles)], axis=1)
    (
        normed_all, w_mine, router_all, code, upstream_rows, query_pre, kv_pre, queries, kv_all, attn_rows, middle,
    ) = front(
        ctx_count, shard_count, group, capacity, KEY_VALUE_HEADS,
        (
            tokens[0], attn_gain[None], w_query, key_weight, value_weight, routes[0].T, w_router.T, upstream_b,
            cosine, sine, bias, query_gain[None], key_gain[None], w_out,
        ),
        0,
    )
    is_key = lax.rem(my_shard, 2) == 0
    part_count = sharers // 2

    def prep(pre, gain):
        shape = pre.shape
        flat = pre.reshape(-1, rows, shape[-2], HEAD_DIM)
        return jax.vmap(lambda v: rotate(rms_scale(v, gain), q_places))(flat).reshape(shape)

    normed_two = rms_scale(middle, ffn_gain)
    second_b = normed_two.astype(BF)
    logits = contract_cols(second_b, router_all)
    chosen = jnp.sum(
        (routes[0][:, :, None] == jnp.arange(experts, dtype=jnp.int32)).astype(F32), axis=1
    )

    def gates_of(log, mask):
        masked = jnp.where(mask > 0, log, -1e30)
        peak = jnp.max(masked, axis=-1, keepdims=True)
        risen = jnp.exp(masked - peak) * mask
        return risen / jnp.maximum(jnp.sum(risen, axis=-1, keepdims=True), 1e-30)

    gates = gates_of(logits, chosen)

    tail_cols = -(-2 * experts // 128) * 128

    def two_parts(value):
        coarse = value.astype(BF).astype(F32)
        return coarse.astype(BF), (value - coarse).astype(BF)

    gates_two = jnp.concatenate(two_parts(gates), axis=1)
    gates_two = jnp.pad(gates_two, ((0, 0), (0, tail_cols - 2 * experts)))
    small = plane * width <= 2**21 and ctx_count == 4
    if small:
        grad_second, back_tail, mixture, grad_w_gate, grad_w_up, grad_w_down = run_experts(
            ctx_count, shard_count, group, capacity, second_b, gates_two, code, w_gate[0], w_up[0], w_down[0],
            upstream_rows, 3,
        )
        grad_w_gate, grad_w_up, grad_w_down = (
            grad_w_gate.astype(F32), grad_w_up.astype(F32), grad_w_down.astype(F32),
        )
    else:
        received, gate_tail = dispatch_rows(ctx_count, shard_count, group, capacity, second_b, gates_two, code, 3)
        received = received.reshape(slot_rows, width)
        my_expert = my_ctx * shard_count + my_shard
        upstream_rows = jnp.swapaxes(upstream_rows, 0, 1).reshape(slot_rows, width)
        column = jnp.arange(tail_cols, dtype=jnp.int32)[None, :]
        mine_column = (column == my_expert) | (column == experts + my_expert)
        gate_tail = gate_tail.reshape(slot_rows, tail_cols).astype(F32)
        slot_gates = jnp.sum(jnp.where(mine_column, gate_tail, 0.0), axis=1, keepdims=True)
        gate_pre = dot(received, w_gate[0])
        up_pre = dot(received, w_up[0])
        activated = jax.nn.silu(gate_pre)
        hidden_b = (activated * up_pre).astype(BF)
        expert_out = dot(hidden_b, w_down[0]).astype(BF)
        expert_out_f = expert_out.astype(F32)
        mix_sent = (slot_gates * expert_out_f).astype(BF)
        mix_sent, upstream_rows, expert_out = lax.optimization_barrier((mix_sent, upstream_rows, expert_out))
        expert_out_f = expert_out.astype(F32)
        mix_back = exchange_shard(mix_sent.reshape(block_shape + (width,)))
        upstream_rows = upstream_rows.astype(F32)
        slot_dot = jnp.sum(expert_out_f * upstream_rows, axis=1, keepdims=True)
        grad_expert = (slot_gates * upstream_rows).astype(BF)
        grad_w_down = contract_rows(hidden_b, grad_expert)
        grad_hidden = contract_cols(grad_expert, w_down[0])
        sigmoid_g = jax.nn.sigmoid(gate_pre)
        silu_slope = sigmoid_g * (1.0 + gate_pre * (1.0 - sigmoid_g))
        grad_gate_pre = (grad_hidden * up_pre * silu_slope).astype(BF)
        grad_up_pre = (grad_hidden * activated).astype(BF)
        grad_w_gate = contract_rows(received, grad_gate_pre)
        grad_w_up = contract_rows(received, grad_up_pre)
        grad_received = contract_cols(grad_gate_pre, w_gate[0]) + contract_cols(grad_up_pre, w_up[0])

        coarse, fine = two_parts(slot_dot)
        tail = jnp.where(column == my_expert, coarse, jnp.where(column == experts + my_expert, fine, jnp.zeros((), BF)))
        grad_second, back_tail, mixture = combine_rows(
            ctx_count, shard_count, group, grad_received.astype(BF).reshape(block_shape + (width,)),
            tail.reshape(block_shape + (tail_cols,)), mix_back, code, 4,
        )
    mixed = (middle + mixture).astype(BF)
    grad_gates = back_tail[:, :experts] + back_tail[:, experts : 2 * experts]
    grad_logits_b = (
        gates * (grad_gates - jnp.sum(gates * grad_gates, axis=-1, keepdims=True))
    ).astype(BF)
    router_part = contract_rows(grad_logits_b, second_b).astype(BF)
    grad_second = grad_second + dot(grad_logits_b, router_all)
    unused, norm_two_back = jax.vjp(rms_scale, middle, ffn_gain)
    grad_middle_part, grad_ffn_gain = norm_two_back(grad_second)
    grad_middle = upstream + grad_middle_part
    grad_proj_b = grad_middle.astype(BF)

    router_parts = jnp.swapaxes(router_part.reshape(experts, shard_count, wrows), 0, 1)
    if small:
        gains = jnp.concatenate([jnp.zeros((1, width), F32), grad_ffn_gain[None], jnp.zeros((6, width), F32)])
        q_sum, kv_sum, out_sum, router_sum, gains, grad_input_part = back(
            ctx_count, shard_count, heads,
            (
                grad_proj_b, queries, kv_all, attn_rows, query_pre, kv_pre, w_out, normed_all, w_mine,
                cosine, sine, bias, query_gain[None], key_gain[None], tokens[0], attn_gain[None], gains, router_parts,
            ),
            5,
        )
    else:
        normed_all = normed_all.reshape(plane, width)
        w_mine = w_mine.reshape(width, head_cols + HEAD_DIM)
        query_pre = query_pre.reshape(shard_count, rows, heads, HEAD_DIM)
        kv_pre = kv_pre.reshape(plane, HEAD_DIM)
        queries = queries.reshape(shard_count, rows, heads, HEAD_DIM)
        kv_all = kv_all.reshape(2, shard_count, sequence, HEAD_DIM)
        keys, values = kv_all[0], kv_all[1]
        attn_rows = attn_rows.reshape(plane, head_cols)
        grad_proj_all = spread(shard_count, grad_proj_b, 5).reshape(plane, width)
        out_part = contract_rows(attn_rows, grad_proj_all).astype(BF)
        out_part, grad_proj_all = lax.optimization_barrier((out_part, grad_proj_all))
        grad_attn = contract_cols(grad_proj_all, w_out).astype(BF)
        grad_heads = grad_attn.reshape(shard_count, rows, heads, HEAD_DIM)
        scores = (
            jnp.einsum("sthd,spd->shtp", queries, keys, preferred_element_type=F32) * score_scale
        )
        scores = scores + bias
        raised = jnp.exp(scores - jnp.max(scores, axis=-1, keepdims=True))
        probs = raised / jnp.sum(raised, axis=-1, keepdims=True)
        probs_b = probs.astype(BF)
        grad_probs = jnp.einsum("sthd,spd->shtp", grad_heads, values, preferred_element_type=F32)
        delta = jnp.sum(probs * grad_probs, axis=-1, keepdims=True)
        grad_scores = (probs * (grad_probs - delta)).astype(BF)
        grad_query = score_scale * jnp.einsum(
            "shtp,spd->sthd", grad_scores, keys, preferred_element_type=F32
        )
        grad_keys = score_scale * jnp.einsum(
            "shtp,sthd->spd", grad_scores, queries, preferred_element_type=F32
        )
        grad_values = jnp.einsum("shtp,sthd->spd", probs_b, grad_heads, preferred_element_type=F32)
        grad_kv = jnp.stack([grad_keys, grad_values]).astype(BF)
        grad_kv = key_back(
            ctx_count, shard_count, grad_kv.reshape(2, shard_count, ctx_count, rows, HEAD_DIM), 6
        )
        unused, query_back = jax.vjp(prep, query_pre, query_gain)
        grad_query_pre, grad_query_gain = query_back(grad_query)
        kv_shape = (shard_count, rows, 1, HEAD_DIM)
        unused, key_prep_back = jax.vjp(prep, kv_pre.reshape(kv_shape), key_gain)
        grad_key_pre, grad_key_gain = key_prep_back(grad_kv.reshape(kv_shape))
        grad_key_gain = jnp.where(is_key, grad_key_gain, 0.0)
        grad_kv_full = jnp.where(
            is_key, grad_key_pre.reshape(plane, HEAD_DIM), grad_kv.reshape(plane, HEAD_DIM)
        ).astype(BF)
        grad_pre = jnp.concatenate(
            [grad_query_pre.reshape(plane, head_cols).astype(BF), grad_kv_full], axis=1
        )
        gains = jnp.concatenate(
            [
                jnp.zeros((1, width), F32),
                grad_ffn_gain[None],
                jnp.pad(
                    jnp.concatenate([grad_query_gain, grad_key_gain])[None],
                    ((0, 6 - 1), (0, width - 2 * HEAD_DIM)),
                ),
            ]
        )
        grad_w = contract_rows(normed_all, grad_pre).astype(BF).reshape(shard_count, wrows, -1)
        q_sum, kv_sum, out_sum, router_sum, gains, grad_input_part = finish(
            ctx_count, shard_count, head_cols, grad_w, out_part.reshape(8, -1, width), router_parts, gains, grad_pre, w_mine,
            tokens[0], attn_gain[None], 8,
        )
    grad_tokens = grad_middle + grad_input_part
    grad_attn_gain, grad_ffn_gain = gains[0], gains[1]
    grad_query_gain, grad_key_gain = gains[2, :HEAD_DIM], gains[2, HEAD_DIM : 2 * HEAD_DIM]
    grad_w_query = q_sum.astype(F32)
    grad_w_out = out_sum.reshape(head_cols, width).astype(F32)
    kinds = kv_sum.astype(F32).reshape(KEY_VALUE_HEADS, part_count, 2, wrows, HEAD_DIM)
    kinds = jnp.transpose(jnp.sum(kinds, axis=1), (1, 2, 0, 3)).reshape(2, wrows, -1)
    grad_w_key, grad_w_value = kinds[0], kinds[1]
    grad_w_router = router_sum.T
    return (
        mixed[None],
        grad_tokens[None],
        grad_attn_gain,
        grad_w_query,
        grad_w_key,
        grad_w_value,
        grad_query_gain,
        grad_key_gain,
        grad_w_out,
        grad_ffn_gain,
        grad_w_router,
        grad_w_gate[None],
        grad_w_up[None],
        grad_w_down[None],
    )


def solution(mesh):
    rows = P("shard", "ctx", None)
    matrix = P("shard", None)
    expert = P(("ctx", "shard"), None, None)
    return jax.shard_map(
        shards,
        mesh=mesh,
        in_specs=(
            rows, rows, P(), rows, P(), matrix, matrix, matrix, P(), P(), matrix, P(), matrix,
            expert, expert, expert,
        ),
        out_specs=(
            rows, rows, P(), matrix, matrix, matrix, P(), P(), matrix, P(), matrix,
            expert, expert, expert,
        ),
        check_vma=False,
    )
```

```python
import functools

import jax
import jax.numpy as jnp
from jax import lax
from jax.experimental import pallas as pl
from jax.experimental.pallas import tpu as pltpu
from jax.sharding import PartitionSpec as P

BF = jnp.bfloat16
F32 = jnp.float32
MESH = pl.DeviceIdType.MESH
ANY = pl.BlockSpec(memory_space=pl.ANY)
VMEM = pl.BlockSpec(memory_space=pltpu.VMEM)
DMA = pltpu.SemaphoreType.DMA
epsilon = 1e-06
rope_base = 1000000.0
QUERY_HEADS = 32
KEY_VALUE_HEADS = 4
HEAD_DIM = 128


def push(src, dst, send_sem, recv_sem, **where):
    return pltpu.make_async_remote_copy(
        src_ref=src, dst_ref=dst, send_sem=send_sem, recv_sem=recv_sem,
        device_id=where, device_id_type=MESH,
    )


def greet(shard_peers, ctx_peers):
    barrier = pltpu.get_barrier_semaphore()
    for peer in shard_peers:
        pl.semaphore_signal(barrier, inc=1, device_id={"shard": peer}, device_id_type=MESH)
    for peer in ctx_peers:
        pl.semaphore_signal(barrier, inc=1, device_id={"ctx": peer}, device_id_type=MESH)
    pl.semaphore_wait(barrier, len(shard_peers) + len(ctx_peers))


def here(ctx_count, shard_count):
    c, s = lax.axis_index("ctx"), lax.axis_index("shard")
    parity = lax.rem(s, 2)
    sibling = s + 1 - 2 * parity
    others = [lax.rem(s + d, shard_count) for d in range(1, shard_count)]
    layers = [lax.rem(c + d, ctx_count) for d in range(1, ctx_count)]
    return c, s, parity, sibling, others, layers


def flip_bits(index, mask):
    result = index
    bit = 1
    while bit <= mask:
        if mask & bit:
            result = result + bit - 2 * bit * lax.rem(lax.div(index, bit), 2)
        bit *= 2
    return result


def lowest(d):
    return d & -d


class Fan:
    def __init__(self, n_ctx, c, block, ss, rs, near_first):
        self.n_ctx, self.c, self.block, self.ss, self.rs, self.near_first = n_ctx, c, block, ss, rs, near_first
        self.items = {}

    def send(self, d, src):
        bits = [b for b in (1, 2, 4, 8, 16) if b < (lowest(d) or self.n_ctx)]
        for b in bits if self.near_first else reversed(bits):
            item = push(src, self.block(d), self.ss.at[d | b], self.rs.at[d | b], ctx=flip_bits(self.c, b))
            item.start()
            self.items[d | b] = item

    def arrival(self, d):
        self.items[d].wait_recv()
        if lowest(d) > 1:
            self.send(d, self.block(d))

    def order(self):
        return sorted(range(1, self.n_ctx), key=lambda d: (bin(d).count("1"), d if self.near_first else -d))

    def drain(self):
        for d in range(1, self.n_ctx):
            self.items[d].wait_send()


class Fold:
    def __init__(self, c, sent, received, ss, rs, slots=None, after=None):
        self.c, self.sent, self.received, self.ss, self.rs = c, sent, received, ss, rs
        self.slots, self.after = slots or {}, after or {}
        self.items, self.left = {}, set()

    def take(self, d, value):
        for b in (1, 2, 4, 8, 16):
            if b < lowest(d) or (d == 0 and b in self.items):
                self.items[d | b].wait_recv()
                value = value + self.received[(d | b) - 1].astype(F32)
        return value

    def give(self, d, value):
        slot = self.slots.get(d, d - 1)
        if d in self.after:
            other, which = self.after[d]
            other.items[which].wait_send()
            other.left.add(which)
        self.sent[slot] = value.astype(BF)
        item = push(self.sent.at[slot], self.received.at[d - 1], self.ss.at[d], self.rs.at[d],
                    ctx=flip_bits(self.c, lowest(d)))
        item.start()
        self.items[d] = item

    def drain(self):
        for d, item in self.items.items():
            if d not in self.left:
                item.wait_send()


def call(body, outs, in_specs, scratch, ident, args, mib=48, out_specs=None):
    return pl.pallas_call(
        body,
        out_shape=outs,
        in_specs=in_specs,
        out_specs=out_specs if out_specs is not None else [ANY] * len(outs),
        scratch_shapes=scratch,
        compiler_params=pltpu.CompilerParams(
            collective_id=ident, has_side_effects=True, vmem_limit_bytes=mib * 2**20
        ),
    )(*args)


def slot_table(code, slots):
    places = lax.broadcasted_iota(jnp.int32, (slots, code.shape[1]), 0).astype(F32)
    return jnp.concatenate(
        [(places == code[e : e + 1, :]).astype(BF) for e in range(code.shape[0])], axis=0
    )


def turn(value, cosine, sine):
    return value * cosine + pltpu.roll(value, HEAD_DIM // 2, 1) * sine


def unit_rows(value):
    scale = lax.rsqrt(jnp.mean(value * value, axis=-1, keepdims=True) + epsilon)
    return value * scale, scale


def front_body(n_ctx, n_shard, group, capacity, heads, kv_heads, tile,
               tokens, gain, w_query, key_w, value_w, routes, router, cot, cosine, sine, bias, q_gain, k_gain, w_out,
               rows_out, w_all_out, router_all, code, cot_rows, qpre_out, kvpre, q_out, kv_out, attn_out, mid,
               own_rows, rows_all, w_all, zroutes, zcot, ready, qpre, q, kv, attn,
               own_part, pair, to_sib, sib, to_chip, got,
               local, ss_row, rs_row, ss_fwd, rs_fwd, ss_w, rs_w, ss_k, rs_k, ss_rt, rs_rt, ss_ro, rs_ro, ss_z, rs_z,
               ss_x, rs_x, ss_kz, rs_kz, ss_kf, rs_kf, ss_s, rs_s, ss_c, rs_c, out_sem):
    c, s, parity, sibling, others, layers = here(n_ctx, n_shard)
    chips = n_shard // 2
    chip = lax.div(s, 2)
    count, width = tokens.shape
    wr = w_query.shape[0]
    cols = heads * HEAD_DIM
    sharers = n_shard // kv_heads
    groups = n_ctx // group
    slots = group * capacity
    keys = n_ctx * count
    mates = [lax.rem(s + 2 * d, n_shard) for d in range(1, chips)]
    x = tokens[...].astype(F32)
    unit, unused = unit_rows(x)
    own_rows[...] = (unit * gain[...]).astype(BF)
    greet(others, layers)

    route_fan = Fan(n_ctx, c, lambda d: zroutes.at[flip_bits(c, d)], ss_ro, rs_ro, False)
    route_fan.send(0, routes)
    cot_fan = Fan(n_ctx, c, lambda d: zcot.at[flip_bits(c, d)], ss_z, rs_z, False)
    cot_fan.send(0, cot)
    first, waits = [], []
    for d in range(1, chips):
        item = push(own_rows, rows_all.at[s], ss_row.at[d], rs_row.at[d], shard=mates[d - 1])
        item.start()
        first.append(item)
    item = push(own_rows, rows_all.at[s], ss_fwd.at[0], rs_fwd.at[0], shard=sibling)
    item.start()
    waits.append(item)
    w_waits = []
    for i, peer in enumerate(others):
        from_q = w_query.at[:, pl.ds(pl.multiple_of(peer * cols, cols), cols)]
        item = push(from_q, w_all.at[s, :, pl.ds(0, cols)], ss_w.at[i], rs_w.at[i], shard=peer)
        item.start()
        w_waits.append(item)
        head = pl.ds(pl.multiple_of(lax.div(peer, sharers) * HEAD_DIM, HEAD_DIM), HEAD_DIM)
        for kind, ref in enumerate((key_w, value_w)):
            item = push(ref.at[:, head], w_all.at[s, :, pl.ds(cols, HEAD_DIM)], ss_k.at[i], rs_k.at[i], shard=peer)

            @pl.when(lax.rem(peer, 2) == kind)
            def _(item=item):
                item.start()

        w_waits.append(item)
        item = push(router, router_all.at[:, pl.ds(pl.multiple_of(s * wr, wr), wr)], ss_rt.at[i], rs_rt.at[i], shard=peer)
        item.start()
        waits.append(item)
    copies = [
        pltpu.make_async_copy(own_rows, rows_all.at[s], local.at[0]),
        pltpu.make_async_copy(w_query.at[:, pl.ds(pl.multiple_of(s * cols, cols), cols)],
                              w_all.at[s, :, pl.ds(0, cols)], local.at[1]),
        pltpu.make_async_copy(routes, zroutes.at[c], local.at[2]),
        pltpu.make_async_copy(router, router_all.at[:, pl.ds(pl.multiple_of(s * wr, wr), wr)], local.at[3]),
        pltpu.make_async_copy(cot, zcot.at[c], local.at[4]),
    ]
    for item in copies:
        item.start()
    head = pl.ds(pl.multiple_of(lax.div(s, sharers) * HEAD_DIM, HEAD_DIM), HEAD_DIM)
    for kind, ref in enumerate((key_w, value_w)):
        own_head = pltpu.make_async_copy(ref.at[:, head], w_all.at[s, :, pl.ds(cols, HEAD_DIM)], local.at[5])

        @pl.when(parity == kind)
        def _(own_head=own_head):
            own_head.start()

    copies[2].wait()
    for d in route_fan.order():
        route_fan.arrival(d)
    before = (
        lax.broadcasted_iota(jnp.int32, (count, count), 0) < lax.broadcasted_iota(jnp.int32, (count, count), 1)
    ).astype(BF)
    for layer in range(n_ctx):
        named = zroutes[layer]
        mask = jnp.concatenate(
            [jnp.max((named == c * n_shard + e).astype(F32), axis=0, keepdims=True) for e in range(n_shard)], axis=0
        )
        rank = jnp.dot(mask.astype(BF), before, preferred_element_type=F32)
        at = layer % group
        code[layer // group, :, at * count : (at + 1) * count] = jnp.where(
            mask > 0, rank + float(at * capacity), -1.0
        )

    for d in range(1, chips):
        first[d - 1].wait()
        origin = lax.rem(s + n_shard - 2 * d, n_shard)
        item = push(rows_all.at[origin], rows_all.at[origin], ss_fwd.at[d], rs_fwd.at[d], shard=sibling)
        item.start()
        waits.append(item)
    for d in cot_fan.order():
        cot_fan.arrival(d)
    copies[4].wait()
    for k in range(groups):
        table = slot_table(code[k], slots)

        @pl.loop(0, width // tile)
        def _(j):
            part = pl.ds(pl.multiple_of(j * tile, tile), tile)
            block = zcot[k * group : (k + 1) * group, :, part].reshape(group * count, tile)
            value = jnp.dot(table, block, preferred_element_type=F32).astype(BF)
            ready[k, :, :, part] = value.reshape(n_shard, slots, tile)

    cot_waits = []
    for k in range(groups):
        for i, peer in enumerate(others):
            item = push(ready.at[k, peer], cot_rows.at[k, s], ss_x.at[k, i], rs_x.at[k, i], shard=peer)
            item.start()
            cot_waits.append(item)
        item = pltpu.make_async_copy(ready.at[k, s], cot_rows.at[k, s], local.at[6 + k])
        item.start()
        cot_waits.append(item)

    for item in waits + w_waits:
        item.wait()
    copies[0].wait()
    copies[1].wait()
    copies[3].wait()
    own_head.wait()
    outs = [
        pltpu.make_async_copy(rows_all, rows_out, out_sem.at[0]),
        pltpu.make_async_copy(w_all, w_all_out, out_sem.at[1]),
    ]
    outs[0].start()
    outs[1].start()

    right = w_all[:, :, pl.ds(cols, HEAD_DIM)].reshape(width, HEAD_DIM)

    @pl.loop(0, n_shard)
    def _(b):
        pre = jnp.dot(rows_all[b], right, preferred_element_type=F32)
        kvpre[b] = pre
        keyed, unused = unit_rows(pre)
        keyed = turn(keyed * k_gain[...], cosine[...], sine[...])
        kv[parity, b, c] = jnp.where(parity == 0, keyed, pre).astype(BF)

    fan = Fan(n_ctx, c, lambda d: kv.at[parity, :, flip_bits(c, d)], ss_kz, rs_kz, False)
    fan.send(0, kv.at[parity, :, c])
    kv_waits = []
    item = push(kv.at[parity, :, c], kv.at[parity, :, c], ss_kf.at[0], rs_kf.at[0], shard=sibling)
    item.start()
    kv_waits.append(item)

    @pl.loop(0, n_shard // 2)
    def _(b):
        left = rows_all[pl.ds(b * 2, 2)].reshape(2 * count, width)
        pre = jnp.dot(left, w_all[:, :, pl.ds(0, cols)].reshape(width, cols), preferred_element_type=F32)
        qpre[pl.ds(b * 2, 2)] = pre.reshape(2, count, cols)
        for i in range(2):
            for h in range(heads):
                part = pre[i * count : (i + 1) * count, h * HEAD_DIM : (h + 1) * HEAD_DIM]
                unit, unused = unit_rows(part)
                q[b * 2 + i, :, h * HEAD_DIM : (h + 1) * HEAD_DIM] = turn(
                    unit * q_gain[...], cosine[...], sine[...]
                ).astype(BF)

    for d in fan.order():
        fan.arrival(d)
        block = kv.at[parity, :, flip_bits(c, d)]
        item = push(block, block, ss_kf.at[d], rs_kf.at[d], shard=sibling)
        item.start()
        kv_waits.append(item)
    outs += [pltpu.make_async_copy(qpre, qpre_out, out_sem.at[2]), pltpu.make_async_copy(q, q_out, out_sem.at[3])]
    outs[2].start()
    outs[3].start()
    for item in kv_waits:
        item.wait()
    fan.drain()
    outs.append(pltpu.make_async_copy(kv, kv_out, out_sem.at[4]))
    outs[4].start()

    near, far = {}, {}
    order = list(range(1, chips)) + [0]

    def product(at):
        d = order[at]
        first_seq = 2 * lax.rem(chip + d, chips)

        @pl.loop(0, 2)
        def _(i):
            b = first_seq + i
            k_all = kv[0, b].reshape(keys, HEAD_DIM)
            v_all = kv[1, b].reshape(keys, HEAD_DIM)
            for h in range(heads):
                hs = slice(h * HEAD_DIM, (h + 1) * HEAD_DIM)
                scores = lax.dot_general(q[b, :, hs], k_all, (((1,), (1,)), ((), ())), preferred_element_type=F32)
                scores = scores * (HEAD_DIM ** -0.5) + bias[...]
                raised = jnp.exp(scores - jnp.max(scores, axis=-1, keepdims=True))
                probs = raised / jnp.sum(raised, axis=-1, keepdims=True)
                attn[b, :, hs] = jnp.dot(probs.astype(BF), v_all, preferred_element_type=F32).astype(BF)

        left = attn[pl.ds(first_seq, 2)].reshape(2 * count, cols)

        @pl.loop(0, width // tile)
        def _(j):
            part = pl.ds(pl.multiple_of(j * tile, tile), tile)
            value = jnp.dot(left, w_out[:, part], preferred_element_type=F32)
            pair[...] = value.reshape(2, count, tile)
            own_part[at % 2, :, part] = pair[parity]
            to_sib[at, :, part] = pair[1 - parity].astype(BF)

        near[at] = push(to_sib.at[at], sib.at[at], ss_s.at[at], rs_s.at[at], shard=sibling)
        near[at].start()

    def chip_sum(at):
        near[at].wait()
        to_chip[at] = (own_part[at % 2] + sib[at].astype(F32)).astype(BF)
        far[at] = push(to_chip.at[at], got.at[at], ss_c.at[at], rs_c.at[at], shard=mates[order[at] - 1])
        far[at].start()

    for at in range(chips):
        product(at)
        if at:
            chip_sum(at - 1)
    outs.append(pltpu.make_async_copy(attn, attn_out, out_sem.at[5]))
    outs[5].start()
    near[chips - 1].wait()
    mid[...] = tokens[...].astype(F32) + own_part[(chips - 1) % 2] + sib[chips - 1].astype(F32)
    for at in range(chips - 1):
        far[at].wait()
        mid[...] += got[at].astype(F32)
    cot_fan.drain()
    route_fan.drain()
    for item in cot_waits + outs:
        item.wait()


def front(n_ctx, n_shard, group, capacity, kv_heads, args, ident):
    tokens, gain, w_query, key_w, value_w, routes, router, cot = args[:8]
    n, z = n_shard, n_ctx
    count, width = tokens.shape
    wr, chips, groups, slots = w_query.shape[0], n_shard // 2, n_ctx // group, group * capacity
    cols = w_query.shape[1] // n
    heads = cols // HEAD_DIM
    sds = jax.ShapeDtypeStruct
    dma = lambda *shape: DMA(shape)
    return call(
        functools.partial(front_body, z, n, group, capacity, heads, kv_heads, 512),
        [
            sds((n, count, width), BF), sds((n, wr, cols + HEAD_DIM), BF), sds((router.shape[0], width), BF),
            sds((groups, n, group * count), F32), sds((groups, n, slots, width), BF), sds((n, count, cols), F32),
            sds((n, count, HEAD_DIM), F32), sds((n, count, cols), BF), sds((2, n, z, count, HEAD_DIM), BF),
            sds((n, count, cols), BF), sds((count, width), F32),
        ],
        [VMEM, VMEM, ANY, ANY, ANY, VMEM, ANY, ANY] + [VMEM] * 6,
        [
            pltpu.VMEM((count, width), BF), pltpu.VMEM((n, count, width), BF), pltpu.VMEM((n, wr, cols + HEAD_DIM), BF),
            pltpu.VMEM((z,) + routes.shape, jnp.int32), pltpu.VMEM((z, count, width), BF),
            pltpu.VMEM((groups, n, slots, width), BF), pltpu.VMEM((n, count, cols), F32),
            pltpu.VMEM((n, count, cols), BF), pltpu.VMEM((2, n, z, count, HEAD_DIM), BF),
            pltpu.VMEM((n, count, cols), BF), pltpu.VMEM((2, count, width), F32), pltpu.VMEM((2, count, 512), F32),
            pltpu.VMEM((chips, count, width), BF), pltpu.VMEM((chips, count, width), BF),
            pltpu.VMEM((chips - 1, count, width), BF), pltpu.VMEM((chips - 1, count, width), BF),
            dma(6 + groups), dma(chips), dma(chips), dma(chips), dma(chips), dma(n - 1), dma(n - 1), dma(n - 1), dma(n - 1),
            dma(n - 1), dma(n - 1), dma(z), dma(z), dma(z), dma(z), dma(groups, n - 1), dma(groups, n - 1),
            dma(z), dma(z), dma(z), dma(z), dma(chips), dma(chips), dma(chips - 1), dma(chips - 1), dma(6),
        ],
        ident, args, mib=60,
        out_specs=[ANY, ANY, ANY, VMEM, ANY, ANY, VMEM, ANY, ANY, ANY, VMEM],
    )


def spread_body(n_shard, rows, rows_all, local, ss_row, rs_row, ss_fwd, rs_fwd):
    c, s, parity, sibling, others, layers = here(1, n_shard)
    chips = n_shard // 2
    mates = [lax.rem(s + 2 * d, n_shard) for d in range(1, chips)]
    greet(mates + [sibling], [])
    mine = pltpu.make_async_copy(rows, rows_all.at[s], local)
    mine.start()
    first, waits = [], []
    for d in range(1, chips):
        item = push(rows, rows_all.at[s], ss_row.at[d], rs_row.at[d], shard=mates[d - 1])
        item.start()
        first.append(item)
    item = push(rows, rows_all.at[s], ss_fwd.at[0], rs_fwd.at[0], shard=sibling)
    item.start()
    waits.append(item)
    for d in range(1, chips):
        first[d - 1].wait()
        origin = lax.rem(s + n_shard - 2 * d, n_shard)
        item = push(rows_all.at[origin], rows_all.at[origin], ss_fwd.at[d], rs_fwd.at[d], shard=sibling)
        item.start()
        waits.append(item)
    mine.wait()
    for item in waits:
        item.wait()


def spread(n_shard, rows, ident):
    return call(
        functools.partial(spread_body, n_shard),
        [jax.ShapeDtypeStruct((n_shard,) + rows.shape, rows.dtype)],
        [ANY], [DMA] + [DMA((n_shard // 2,))] * 4, ident, (rows,),
    )[0]


def key_back_body(n_ctx, n_shard, parts, out, sib, zsend, zrecv, ss_s, rs_s, ss_z, rs_z):
    c, s, parity, sibling, others, layers = here(n_ctx, n_shard)
    greet([sibling], layers)
    order = list(range(1, n_ctx)) + [0]
    near = {}
    for d in order:
        block = parts.at[1 - parity, :, lax.rem(c + d, n_ctx)]
        near[d] = push(block, sib.at[d], ss_s.at[d], rs_s.at[d], shard=sibling)
        near[d].start()
    far = {}
    for d in order:
        near[d].wait()
        layer = lax.rem(c + d, n_ctx)
        value = parts[parity, :, layer].astype(F32) + sib[d].astype(F32)
        if d:
            zsend[d - 1] = value.astype(BF)
            far[d] = push(zsend.at[d - 1], zrecv.at[d - 1], ss_z.at[d], rs_z.at[d], ctx=layer)
            far[d].start()
    for d in range(1, n_ctx):
        far[d].wait()
        value = value + zrecv[d - 1].astype(F32)
    out[...] = value


def key_back(n_ctx, n_shard, parts, ident):
    block = (parts.shape[1], parts.shape[3], parts.shape[4])
    return call(
        functools.partial(key_back_body, n_ctx, n_shard),
        [jax.ShapeDtypeStruct(block, F32)],
        [VMEM],
        [
            pltpu.VMEM((n_ctx,) + block, BF), pltpu.VMEM((n_ctx - 1,) + block, BF),
            pltpu.VMEM((n_ctx - 1,) + block, BF),
        ] + [DMA((n_ctx,))] * 4,
        ident, (parts,), out_specs=[VMEM],
    )[0]


def finish_body(n_ctx, n_shard, q_cols, tile,
                weights, wide, router, gains, left, right, tokens, gain,
                q_out, kv_out, wide_out, router_out, gains_out, rows_out,
                wide_landing, wide_acc, wide_total, ss_wi, rs_wi, ss_wo, ss_wc, pieces, landing, acc, total, router_in, router_mid, router_far,
                gains_own, gains_in, gains_mid, gains_far, pair, own_part, to_sib, sib, to_chip, got,
                local, ss_w, rs_w, ss_i, rs_i, ss_o, ss_q, ss_k, ss_r, rs_r, ss_g, rs_g, ss_h, rs_h,
                ss_t, rs_t, ss_s, rs_s, ss_c, rs_c):
    c, s, parity, sibling, others, layers = here(n_ctx, n_shard)
    half = n_ctx // 2
    chips = n_shard // 2
    chip = lax.div(s, 2)
    mates = [lax.rem(s + 2 * d, n_shard) for d in range(1, chips)]
    left_side = c < half
    depth = jnp.where(left_side, c, n_ctx - 1 - c)
    inner = jnp.where(left_side, c + 1, c - 1)
    outer = jnp.clip(jnp.where(left_side, c - 1, c + 1), 0, n_ctx - 1)
    middle = depth == half - 1
    inside = depth > 0
    rows, width = rows_out.shape
    greet(others, layers)
    sends, small = [None], []
    for i, peer in enumerate(others):
        item = push(weights.at[peer], pieces.at[i + 1], ss_w.at[i], rs_w.at[i], shard=peer)
        item.start()
        sends.append(item)
    for i, peer in enumerate(others):
        item = push(router.at[peer], router_in.at[i], ss_r.at[i], rs_r.at[i], shard=peer)
        item.start()
        small.append(item)

    def out_copies(j, ref):
        source = lax.rem(s + n_shard - j, n_shard)
        cols = pl.ds(pl.multiple_of(source * q_cols, q_cols), q_cols)
        return (
            pltpu.make_async_copy(ref.at[:, pl.ds(0, q_cols)], q_out.at[:, cols], ss_q.at[j]),
            pltpu.make_async_copy(ref.at[:, pl.ds(q_cols, 128)], kv_out.at[source], ss_k.at[j]),
        )

    def wide_copies(j, ref):
        return (pltpu.make_async_copy(ref, wide_out.at[j], ss_wc.at[j]),)

    class Line:
        def __init__(self, ready, own, acc, landing, total, ss_i, rs_i, ss_o, copies):
            self.ready, self.own, self.acc, self.landing, self.total = ready, own, acc, landing, total
            self.ss_i, self.rs_i, self.ss_o, self.copies = ss_i, rs_i, ss_o, copies

        def inward(self, j, ref):
            at = jnp.where(middle, 1, 0)
            return push(ref, self.landing.at[at, j], self.ss_i.at[j], self.rs_i.at[at, j], ctx=inner)

        def outward(self, j):
            return push(self.total.at[j], self.landing.at[1, j], self.ss_o.at[j], self.rs_i.at[1, j], ctx=outer)

        def arrived(self, which, j):
            push(self.acc.at[j], self.landing.at[which, j], self.ss_i.at[j], self.rs_i.at[which, j],
                 ctx=inner).wait_recv()

        def outermost(self, j):
            @pl.when(jnp.logical_not(inside))
            def _():
                self.ready(j)
                self.inward(j, self.own(j)).start()

        def first_half(self, j):
            @pl.when(inside)
            def _():
                self.ready(j)
                self.arrived(0, j)
                self.acc[j] = (self.own(j)[...].astype(F32) + self.landing[0, j].astype(F32)).astype(BF)
                self.inward(j, self.acc.at[j]).start()

        def second_half(self, j):
            self.arrived(1, j)

            @pl.when(middle)
            def _():
                self.total[j] = (self.acc[j].astype(F32) + self.landing[1, j].astype(F32)).astype(BF)

            @pl.when(jnp.logical_not(middle))
            def _():
                self.total[j] = self.landing[1, j]

            @pl.when(inside)
            def _():
                self.outward(j).start()

            for item in self.copies(j, self.total.at[j]):
                item.start()

        def drain(self, j):
            self.inward(j, self.acc.at[j]).wait_send()

            @pl.when(inside)
            def _():
                self.outward(j).wait_send()

            for item in self.copies(j, self.total.at[j]):
                item.wait()

    line = Line(lambda j: sends[j].wait() if j else None, lambda j: pieces.at[j] if j else weights.at[s],
                acc, landing, total, ss_i, rs_i, ss_o, out_copies)
    wide_line = Line(lambda j: None, lambda j: wide.at[j], wide_acc, wide_landing, wide_total,
                     ss_wi, rs_wi, ss_wo, wide_copies)
    wides = wide.shape[0]
    steps = [(wide_line, j) for j in range(wides)] + [(line, j) for j in range(n_shard)]

    near, far = {}, {}

    def product(d):
        first = pl.multiple_of(lax.rem(chip + d, chips) * (2 * rows), 2 * rows)

        @pl.loop(0, width // tile)
        def _(j):
            cols = pl.ds(pl.multiple_of(j * tile, tile), tile)
            value = lax.dot_general(left[pl.ds(first, 2 * rows), :], right[cols, :],
                                    (((1,), (1,)), ((), ())), preferred_element_type=F32)
            pair[...] = value.reshape(2, rows, tile)
            own_part[d, :, cols] = pair[parity]
            to_sib[d, :, cols] = pair[1 - parity].astype(BF)

        near[d] = push(to_sib.at[d], sib.at[d], ss_s.at[d], rs_s.at[d], shard=sibling)
        near[d].start()

    def chip_sum(d):
        near[d].wait()
        to_chip[d - 1] = (own_part[d] + sib[d].astype(F32)).astype(BF)
        far[d] = push(to_chip.at[d - 1], got.at[d - 1], ss_c.at[d - 1], rs_c.at[d - 1], shard=mates[d - 1])
        far[d].start()

    gain_sends = []

    def last_sum():
        near[0].wait()
        grad = own_part[0] + sib[0].astype(F32)
        for d in range(1, chips):
            far[d].wait()
            grad = grad + got[d - 1].astype(F32)
        x = tokens[...].astype(F32)
        scale = lax.rsqrt(jnp.mean(x * x, axis=-1, keepdims=True) + epsilon)
        unit = x * scale
        scaled = grad * gain[...]
        rows_out[...] = scale * (scaled - unit * jnp.mean(scaled * unit, axis=-1, keepdims=True))
        gains_own[...] = gains[...]
        gains_own[0:1] = jnp.sum(grad * unit, axis=0, keepdims=True)
        mine = pltpu.make_async_copy(gains_own, gains_in.at[s], local.at[0])
        mine.start()
        gain_sends.append(mine)
        for i, peer in enumerate(others):
            item = push(gains_own, gains_in.at[s], ss_g.at[i], rs_g.at[i], shard=peer)
            item.start()
            gain_sends.append(item)

    def small_plane():
        for item in small + gain_sends:
            item.wait()
        gains_mid[...] = gains_in[0]
        for i in range(1, n_shard):
            gains_mid[...] += gains_in[i]
        router_mid[...] = router[s].astype(F32)
        for i in range(n_shard - 1):
            router_mid[...] += router_in[i].astype(F32)
        for i, layer in enumerate(layers):
            push(gains_mid, gains_far.at[c], ss_h.at[i], rs_h.at[i], ctx=layer).start()
            push(router_mid, router_far.at[c], ss_t.at[i], rs_t.at[i], ctx=layer).start()
        pltpu.make_async_copy(gains_mid, gains_far.at[c], local.at[1]).start()
        pltpu.make_async_copy(router_mid, router_far.at[c], local.at[2]).start()

    def small_all():
        pltpu.make_async_copy(gains_mid, gains_far.at[c], local.at[1]).wait()
        pltpu.make_async_copy(router_mid, router_far.at[c], local.at[2]).wait()
        for i, layer in enumerate(layers):
            push(gains_mid, gains_far.at[c], ss_h.at[i], rs_h.at[i], ctx=layer).wait()
            push(router_mid, router_far.at[c], ss_t.at[i], rs_t.at[i], ctx=layer).wait()
        gains_out[...] = gains_far[0]
        router_out[...] = router_far[0]
        for i in range(1, n_ctx):
            gains_out[...] += gains_far[i]
            router_out[...] += router_far[i]

    lag, ahead = 2, 6
    for which, j in steps[:ahead]:
        which.outermost(j)
    for d in list(range(1, chips)) + [0]:
        product(d)
    side = [functools.partial(chip_sum, d) for d in range(1, chips)] + [last_sum, small_plane]
    for n in range(len(steps) + lag):
        if n + ahead < len(steps):
            steps[n + ahead][0].outermost(steps[n + ahead][1])
        if n < len(steps):
            steps[n][0].first_half(steps[n][1])
        if n >= lag:
            steps[n - lag][0].second_half(steps[n - lag][1])
        if n >= 2 and side:
            side.pop(0)()
    for job in side:
        job()
    small_all()
    for which, j in steps:
        which.drain(j)


def finish(n_ctx, n_shard, q_cols, weights, wide, router, gains, left, right, tokens, gain, ident):
    n, rows, cols = weights.shape
    router_shape = router.shape[1:]
    count, width = tokens.shape
    chips = n // 2
    tile = 512
    wides = wide.shape[0]
    return call(
        functools.partial(finish_body, n_ctx, n, q_cols, tile),
        [
            jax.ShapeDtypeStruct((rows, n * q_cols), BF), jax.ShapeDtypeStruct((n, rows, 128), BF),
            jax.ShapeDtypeStruct(wide.shape, BF),
            jax.ShapeDtypeStruct(router_shape, F32), jax.ShapeDtypeStruct(gains.shape, F32),
            jax.ShapeDtypeStruct((count, width), F32),
        ],
        [VMEM] * 8,
        [
            pltpu.VMEM((2,) + wide.shape, BF), pltpu.VMEM(wide.shape, BF), pltpu.VMEM(wide.shape, BF),
            DMA((wides,)), DMA((2, wides)), DMA((wides,)), DMA((wides,)),
            pltpu.VMEM((n, rows, cols), BF), pltpu.VMEM((2, n, rows, cols), BF),
            pltpu.VMEM((n, rows, cols), BF), pltpu.VMEM((n, rows, cols), BF),
            pltpu.VMEM((n - 1,) + router_shape, BF), pltpu.VMEM(router_shape, F32),
            pltpu.VMEM((n_ctx,) + router_shape, F32),
            pltpu.VMEM(gains.shape, F32), pltpu.VMEM((n,) + gains.shape, F32),
            pltpu.VMEM(gains.shape, F32), pltpu.VMEM((n_ctx,) + gains.shape, F32),
            pltpu.VMEM((2, count, tile), F32), pltpu.VMEM((chips, count, width), F32),
            pltpu.VMEM((chips, count, width), BF), pltpu.VMEM((chips, count, width), BF),
            pltpu.VMEM((chips - 1, count, width), BF), pltpu.VMEM((chips - 1, count, width), BF),
            DMA((3,)), DMA((n - 1,)), DMA((n - 1,)), DMA((n,)), DMA((2, n)), DMA((n,)),
            DMA((n,)), DMA((n,)), DMA((n - 1,)), DMA((n - 1,)), DMA((n - 1,)), DMA((n - 1,)),
            DMA((n_ctx - 1,)), DMA((n_ctx - 1,)), DMA((n_ctx - 1,)), DMA((n_ctx - 1,)),
            DMA((chips,)), DMA((chips,)), DMA((chips - 1,)), DMA((chips - 1,)),
        ],
        ident, (weights, wide, router, gains, left, right, tokens, gain), mib=60,
        out_specs=[ANY, ANY, ANY, VMEM, VMEM, VMEM],
    )


def back_body(n_ctx, n_shard, group, heads, wides,
              grad_out, q, kv, attn, qpre, kvpre, w_out, rows_in, w_all, cosine, sine, bias, q_gain, k_gain,
              tokens, gain, gains, router, mix_near, mix_far, code,
              q_out, kv_out, wide_out, router_out, gains_out, rows_out, mix_out, mix_land,
              grads, attn_t, grad_heads, ds_all, p_all, parts, pre, q_sum, k_sum, wide, weights,
              sibk, zsend, zrecv, wide_landing, pieces, landing,
              own_part, pair, to_sib, sib, to_chip, got, router_in, router_mid, router_far,
              gains_own, gains_in, gains_mid, gains_far, mix_rows, mix_sent, mix_recv, local,
              ss_row, rs_row, ss_fwd, rs_fwd, ss_sk, rs_sk, ss_zk, rs_zk,
              ss_wi, rs_wi, ss_wo, ss_wc, ss_w, rs_w, ss_i, rs_i, ss_o, ss_q, ss_k,
              ss_r, rs_r, ss_g, rs_g, ss_h, rs_h, ss_t, rs_t, ss_s, rs_s, ss_c, rs_c, ss_m, rs_m, ss_f, rs_f, ss_v, rs_v):
    c, s, parity, sibling, others, layers = here(n_ctx, n_shard)
    half = n_ctx // 2
    chips = n_shard // 2
    chip = lax.div(s, 2)
    mates = [lax.rem(s + 2 * d, n_shard) for d in range(1, chips)]
    left_side = c < half
    depth = jnp.where(left_side, c, n_ctx - 1 - c)
    inner = jnp.where(left_side, c + 1, c - 1)
    outer = jnp.clip(jnp.where(left_side, c - 1, c + 1), 0, n_ctx - 1)
    middle = depth == half - 1
    inside = depth > 0
    count, width = tokens.shape
    wr = w_all.shape[1]
    cols = heads * HEAD_DIM
    keys = n_ctx * count
    scaling = HEAD_DIM ** -0.5
    own_copies = [
        pltpu.make_async_copy(grad_out, grads.at[s], local.at[0]),
        pltpu.make_async_copy(rows_in, grads, local.at[1]),
    ]
    own_copies[0].start()
    greet(others, layers)

    first, forwards = {}, {}
    for d in range(1, chips):
        first[d] = push(grad_out, grads.at[s], ss_row.at[d], rs_row.at[d], shard=mates[d - 1])
        first[d].start()
    forwards[0] = push(grad_out, grads.at[s], ss_fwd.at[0], rs_fwd.at[0], shard=sibling)
    forwards[0].start()
    small = []
    for i, peer in enumerate(others):
        item = push(router.at[peer], router_in.at[i], ss_r.at[i], rs_r.at[i], shard=peer)
        item.start()
        small.append(item)
    q_sum[...] = jnp.zeros_like(q_sum)
    k_sum[...] = jnp.zeros_like(k_sum)

    def norm_back(grad, value, norm_gain, total):
        unit, scale = unit_rows(value)
        grad = grad * cosine[...] + pltpu.roll(grad * sine[...], HEAD_DIM // 2, 1)
        total[...] += jnp.sum(grad * unit, axis=0, keepdims=True)
        scaled = grad * norm_gain[...]
        return scale * (scaled - unit * jnp.mean(scaled * unit, axis=-1, keepdims=True))

    slots = mix_near.shape[1]
    mix_fold = Fold(c, mix_sent, mix_recv, ss_f, rs_f)
    tile = mix_rows.shape[2]

    def mix_sums(k, ref):
        table = slot_table(code[flip_bits(lax.div(c, group), k)], slots).T

        @pl.loop(0, width // tile)
        def _(j):
            part = pl.ds(pl.multiple_of(j * tile, tile), tile)
            item = pltpu.make_async_copy(ref.at[:, :, part], mix_rows, local.at[5])
            item.start()
            item.wait()
            value = jnp.dot(table, mix_rows[...].reshape(n_shard * slots, tile), preferred_element_type=F32)
            own_part[:, :, part] = value.reshape(2, count, tile)

    def mix_part(d):
        return own_part[lax.rem(flip_bits(c, d), group)]

    def mix_send():
        for i, peer in enumerate(others):
            push(mix_near.at[peer], mix_land.at[s], ss_m.at[i], rs_m.at[i], shard=peer).start()
        pltpu.make_async_copy(mix_near.at[s], mix_land.at[s], local.at[6]).start()

    def mix_last():
        for i, peer in enumerate(others):
            push(mix_near.at[peer], mix_land.at[s], ss_m.at[i], rs_m.at[i], shard=peer).wait()
        pltpu.make_async_copy(mix_near.at[s], mix_land.at[s], local.at[6]).wait()
        mix_sums(0, mix_land)
        mix_fold.give(1, mix_part(1))
        mix_out[...] = mix_part(0)

    mix_sums(1, mix_far)
    mix_fold.give(3, mix_part(3))
    near, far = {}, {}

    def seqs_of(d):
        return 2 * lax.rem(chip + chips - d, chips)

    def attention_back(d):
        fs = seqs_of(d)
        grad = lax.dot_general(grads[pl.ds(fs, 2)].reshape(2 * count, width), w_out[...],
                               (((1,), (1,)), ((), ())), preferred_element_type=F32)
        grad_heads[...] = grad.reshape(2, count, cols).astype(BF)

        @pl.loop(0, 2)
        def _(i):
            b = fs + i
            k_all = kv[0, b].reshape(keys, HEAD_DIM)
            v_all = kv[1, b].reshape(keys, HEAD_DIM)
            for h in range(heads):
                hs = slice(h * HEAD_DIM, (h + 1) * HEAD_DIM)
                rs = slice(h * count, (h + 1) * count)
                scores = lax.dot_general(q[b, :, hs], k_all, (((1,), (1,)), ((), ())), preferred_element_type=F32)
                scores = scores * scaling + bias[...]
                raised = jnp.exp(scores - jnp.max(scores, axis=-1, keepdims=True))
                probs = raised / jnp.sum(raised, axis=-1, keepdims=True)
                grad_p = lax.dot_general(grad_heads[i, :, hs], v_all, (((1,), (1,)), ((), ())),
                                         preferred_element_type=F32)
                delta = jnp.sum(probs * grad_p, axis=-1, keepdims=True)
                ds = (probs * (grad_p - delta)).astype(BF)
                ds_all[rs, :] = ds
                p_all[rs, :] = probs.astype(BF)
                grad_q = jnp.dot(ds, k_all, preferred_element_type=F32) * scaling
                pre[b, :, hs] = norm_back(grad_q, qpre[b, :, hs], q_gain, q_sum).astype(BF)
            grad_k, grad_v = jnp.zeros((keys, HEAD_DIM), F32), jnp.zeros((keys, HEAD_DIM), F32)
            stacked_q = jnp.concatenate([q[b, :, h * HEAD_DIM : (h + 1) * HEAD_DIM] for h in range(heads)], axis=0)
            stacked_g = jnp.concatenate(
                [grad_heads[i, :, h * HEAD_DIM : (h + 1) * HEAD_DIM] for h in range(heads)], axis=0
            )
            grad_k = lax.dot_general(ds_all[...], stacked_q, (((0,), (0,)), ((), ())), preferred_element_type=F32)
            grad_v = lax.dot_general(p_all[...], stacked_g, (((0,), (0,)), ((), ())), preferred_element_type=F32)
            parts[0, b] = (grad_k * scaling).astype(BF).reshape(n_ctx, count, HEAD_DIM)
            parts[1, b] = grad_v.astype(BF).reshape(n_ctx, count, HEAD_DIM)

        near[d] = push(parts.at[1 - parity, pl.ds(fs, 2)], sibk.at[d], ss_sk.at[d], rs_sk.at[d], shard=sibling)
        near[d].start()

    def key_sum(d):
        fs = seqs_of(d)
        near[d].wait()
        for i, layer in enumerate(layers):
            zsend[d, i] = (
                parts[parity, pl.ds(fs, 2), layer].astype(F32) + sibk[d, :, layer].astype(F32)
            ).astype(BF)
            far[d, i] = push(zsend.at[d, i], zrecv.at[d, i], ss_zk.at[d, i], rs_zk.at[d, i], ctx=layer)
            far[d, i].start()

    def half_rows(j):
        return pl.ds((j % 2) * (wr // 2), wr // 2)

    def out_copies(j, ref):
        source = lax.rem(s + n_shard - j // 2, n_shard)
        to = pl.ds(pl.multiple_of(source * cols, cols), cols)
        return (
            pltpu.make_async_copy(ref.at[:, pl.ds(0, cols)], q_out.at[half_rows(j), to], ss_q.at[j]),
            pltpu.make_async_copy(ref.at[:, pl.ds(cols, HEAD_DIM)], kv_out.at[source, half_rows(j)], ss_k.at[j]),
        )

    def wide_copies(j, ref):
        step = wide.shape[2]
        return (pltpu.make_async_copy(ref, wide_out.at[:, pl.ds(j * step, step)], ss_wc.at[j]),)

    class Line:
        def __init__(self, ready, own, landing, ss_i, rs_i, ss_o, copies):
            self.ready, self.own, self.landing = ready, own, landing
            self.ss_i, self.rs_i, self.ss_o, self.copies = ss_i, rs_i, ss_o, copies

        def inward(self, j, ref):
            at = jnp.where(middle, 1, 0)
            return push(ref, self.landing.at[at, j], self.ss_i.at[j], self.rs_i.at[at, j], ctx=inner)

        def outward(self, j):
            return push(self.landing.at[1, j], self.landing.at[1, j], self.ss_o.at[j], self.rs_i.at[1, j], ctx=outer)

        def arrived(self, which, j):
            push(self.landing.at[0, j], self.landing.at[which, j], self.ss_i.at[j], self.rs_i.at[which, j],
                 ctx=inner).wait_recv()

        def outermost(self, j):
            @pl.when(jnp.logical_not(inside))
            def _():
                self.ready(j)
                self.inward(j, self.own(j)).start()

        def first_half(self, j):
            @pl.when(inside)
            def _():
                self.ready(j)
                self.arrived(0, j)
                self.landing[0, j] = (self.own(j)[...].astype(F32) + self.landing[0, j].astype(F32)).astype(BF)
                self.inward(j, self.landing.at[0, j]).start()

        def second_half(self, j):
            self.arrived(1, j)

            @pl.when(middle)
            def _():
                self.landing[1, j] = (self.landing[0, j].astype(F32) + self.landing[1, j].astype(F32)).astype(BF)

            @pl.when(inside)
            def _():
                self.outward(j).start()

            for item in self.copies(j, self.landing.at[1, j]):
                item.start()

        def drain(self, j):
            self.inward(j, self.landing.at[0, j]).wait_send()

            @pl.when(inside)
            def _():
                self.outward(j).wait_send()

            for item in self.copies(j, self.landing.at[1, j]):
                item.wait()

    sends = [[] for j in range(n_shard)]
    line = Line(lambda j: [item.wait() for item in sends[j // 2]] if j % 2 == 0 else None,
                lambda j: pieces.at[j // 2, half_rows(j)] if j >= 2 else weights.at[s, half_rows(j)],
                landing, ss_i, rs_i, ss_o, out_copies)
    wide_line = Line(lambda j: None, lambda j: wide.at[j], wide_landing, ss_wi, rs_wi, ss_wo, wide_copies)
    steps = [(wide_line, j) for j in range(wides)] + [(line, j) for j in range(2 * n_shard)]
    lag, ahead = 2, 6

    def advance(n):
        if n + ahead < len(steps):
            steps[n + ahead][0].outermost(steps[n + ahead][1])
        if n < len(steps):
            steps[n][0].first_half(steps[n][1])
        if n >= lag:
            steps[n - lag][0].second_half(steps[n - lag][1])

    attn_t[...] = attn[...].reshape(n_shard * count, cols).T
    step = width // wides
    for d in range(chips):
        if d:
            first[d].wait()
            origin = lax.rem(s + n_shard - 2 * d, n_shard)
            forwards[d] = push(grads.at[origin], grads.at[origin], ss_fwd.at[d], rs_fwd.at[d], shard=sibling)
            forwards[d].start()
        else:
            own_copies[0].wait()
        forwards[d].wait()
        if d + 1 == chips:
            mix_send()
            for j in range(wides):
                block = grads[:, :, j * step : (j + 1) * step].reshape(n_shard * count, step)
                wide[j] = jnp.dot(attn_t[...], block, preferred_element_type=F32).astype(BF)
                if j < ahead:
                    wide_line.outermost(j)
        attention_back(d)
        if d == 0:
            mix_fold.give(2, mix_fold.take(2, mix_part(2)))
        if d:
            key_sum(d - 1)

    rows_all = grads
    own_copies[1].start()
    key_sum(chips - 1)
    advance(0)
    own_copies[1].wait()

    @pl.loop(0, n_shard)
    def _(e):
        block = rows_all[:, :, pl.ds(pl.multiple_of(e * wr, wr), wr)].reshape(n_shard * count, wr)
        right = pre[:, :, pl.ds(0, cols)].reshape(n_shard * count, cols)
        weights[e, :, pl.ds(0, cols)] = lax.dot_general(
            block, right, (((0,), (0,)), ((), ())), preferred_element_type=F32).astype(BF)

    for i, peer in enumerate(others):
        item = push(weights.at[peer, :, pl.ds(0, cols)], pieces.at[i + 1, :, pl.ds(0, cols)],
                    ss_w.at[i], rs_w.at[i], shard=peer)
        item.start()
        sends[i + 1].append(item)
    advance(1)
    for d in range(chips):
        fs = seqs_of(d)
        total = parts[parity, pl.ds(fs, 2), c].astype(F32) + sibk[d, :, c].astype(F32)
        for i in range(n_ctx - 1):
            far[d, i].wait()
            total = total + zrecv[d, i].astype(F32)
        for i in range(2):
            keyed = norm_back(total[i], kvpre[fs + i], k_gain, k_sum)
            pre[fs + i, :, pl.ds(cols, HEAD_DIM)] = jnp.where(parity == 0, keyed, total[i]).astype(BF)

    @pl.loop(0, n_shard)
    def _(e):
        block = rows_all[:, :, pl.ds(pl.multiple_of(e * wr, wr), wr)].reshape(n_shard * count, wr)
        right = pre[:, :, pl.ds(cols, HEAD_DIM)].reshape(n_shard * count, HEAD_DIM)
        weights[e, :, pl.ds(cols, HEAD_DIM)] = lax.dot_general(
            block, right, (((0,), (0,)), ((), ())), preferred_element_type=F32).astype(BF)

    for i, peer in enumerate(others):
        item = push(weights.at[peer, :, pl.ds(cols, HEAD_DIM)], pieces.at[i + 1, :, pl.ds(cols, HEAD_DIM)],
                    ss_v.at[i], rs_v.at[i], shard=peer)
        item.start()
        sends[i + 1].append(item)
    advance(2)

    order = list(range(1, chips)) + [0]
    to_sibling, to_mate = {}, {}

    def product(at):
        fs = 2 * lax.rem(chip + order[at], chips)
        left = pre[pl.ds(fs, 2)].reshape(2 * count, cols + HEAD_DIM)

        @pl.loop(0, n_shard)
        def _(j):
            part = pl.ds(pl.multiple_of(j * wr, wr), wr)
            value = lax.dot_general(left, w_all[j], (((1,), (1,)), ((), ())), preferred_element_type=F32)
            pair[...] = value.reshape(2, count, wr)
            own_part[at % 2, :, part] = pair[parity]
            to_sib[at, :, part] = pair[1 - parity].astype(BF)

        to_sibling[at] = push(to_sib.at[at], sib.at[at], ss_s.at[at], rs_s.at[at], shard=sibling)
        to_sibling[at].start()

    def chip_sum(at):
        to_sibling[at].wait()
        to_chip[at] = (own_part[at % 2] + sib[at].astype(F32)).astype(BF)
        to_mate[at] = push(to_chip.at[at], got.at[at], ss_c.at[at], rs_c.at[at], shard=mates[order[at] - 1])
        to_mate[at].start()

    gain_sends = []

    def last_sum():
        to_sibling[chips - 1].wait()
        grad = own_part[(chips - 1) % 2] + sib[chips - 1].astype(F32)
        for at in range(chips - 1):
            to_mate[at].wait()
            grad = grad + got[at].astype(F32)
        unit, scale = unit_rows(tokens[...].astype(F32))
        scaled = grad * gain[...]
        rows_out[...] = scale * (scaled - unit * jnp.mean(scaled * unit, axis=-1, keepdims=True))
        gains_own[...] = gains[...]
        gains_own[0:1] = jnp.sum(grad * unit, axis=0, keepdims=True)
        gains_own[2:3, 0:HEAD_DIM] = q_sum[...]
        gains_own[2:3, HEAD_DIM : 2 * HEAD_DIM] = jnp.where(parity == 0, k_sum[...], jnp.zeros_like(k_sum))
        mine = pltpu.make_async_copy(gains_own, gains_in.at[s], local.at[2])
        mine.start()
        gain_sends.append(mine)
        for i, peer in enumerate(others):
            item = push(gains_own, gains_in.at[s], ss_g.at[i], rs_g.at[i], shard=peer)
            item.start()
            gain_sends.append(item)

    def small_plane():
        for item in small + gain_sends:
            item.wait()
        gains_mid[...] = gains_in[0]
        for i in range(1, n_shard):
            gains_mid[...] += gains_in[i]
        router_mid[...] = router[s].astype(F32)
        for i in range(n_shard - 1):
            router_mid[...] += router_in[i].astype(F32)
        for i, layer in enumerate(layers):
            push(gains_mid, gains_far.at[c], ss_h.at[i], rs_h.at[i], ctx=layer).start()
            push(router_mid, router_far.at[c], ss_t.at[i], rs_t.at[i], ctx=layer).start()
        pltpu.make_async_copy(gains_mid, gains_far.at[c], local.at[3]).start()
        pltpu.make_async_copy(router_mid, router_far.at[c], local.at[4]).start()

    def small_all():
        pltpu.make_async_copy(gains_mid, gains_far.at[c], local.at[3]).wait()
        pltpu.make_async_copy(router_mid, router_far.at[c], local.at[4]).wait()
        for i, layer in enumerate(layers):
            push(gains_mid, gains_far.at[c], ss_h.at[i], rs_h.at[i], ctx=layer).wait()
            push(router_mid, router_far.at[c], ss_t.at[i], rs_t.at[i], ctx=layer).wait()
        gains_out[...] = gains_far[0]
        router_out[...] = router_far[0]
        for i in range(1, n_ctx):
            gains_out[...] += gains_far[i]
            router_out[...] += router_far[i]

    side = []
    for at in range(chips):
        side.append(functools.partial(product, at))
        if at:
            side.append(functools.partial(chip_sum, at - 1))
    count_steps = len(steps) + lag
    late = {16: last_sum, 18: mix_last, 21: small_plane}
    for n in range(3, count_steps):
        advance(n)
        if side:
            side.pop(0)()
        if n in late:
            late[n]()
    for job in side:
        job()
    small_all()
    mix_out[...] = mix_fold.take(0, mix_out[...])
    mix_fold.drain()
    for which, j in steps:
        which.drain(j)


def back(n_ctx, n_shard, group, heads, args, ident):
    count, width = args[0].shape
    rows_in, w_all, router, gains, mix_near = args[7], args[8], args[17], args[16], args[18]
    n, z, chips, wides = n_shard, n_ctx, n_shard // 2, 16
    wr, cols = w_all.shape[1], heads * HEAD_DIM
    keys = z * count
    sds, scratch = jax.ShapeDtypeStruct, pltpu.VMEM
    router_shape = router.shape[1:]
    dma = lambda *shape: DMA(shape)
    wide_block, block = (cols, width // wides), (wr, cols + HEAD_DIM)
    return call(
        functools.partial(back_body, z, n, group, heads, wides),
        [
            sds((wr, n * cols), BF), sds((n, wr, HEAD_DIM), BF), sds((cols, width), BF), sds(router_shape, F32),
            sds(gains.shape, F32), sds((count, width), F32), sds((count, width), F32), sds(mix_near.shape, BF),
        ],
        [VMEM] * 7 + [ANY] + [VMEM] * 10 + [ANY, ANY, VMEM],
        [
            scratch((n, count, width), BF), scratch((cols, n * count), BF),
            scratch((2, count, cols), BF), scratch((heads * count, keys), BF), scratch((heads * count, keys), BF),
            scratch((2, n, z, count, HEAD_DIM), BF), scratch((n, count, cols + HEAD_DIM), BF),
            scratch((1, HEAD_DIM), F32), scratch((1, HEAD_DIM), F32),
            scratch((wides,) + wide_block, BF), scratch((n,) + block, BF),
            scratch((chips, 2, z, count, HEAD_DIM), BF), scratch((chips, z - 1, 2, count, HEAD_DIM), BF),
            scratch((chips, z - 1, 2, count, HEAD_DIM), BF), scratch((2, wides) + wide_block, BF),
            scratch((n,) + block, BF), scratch((2, 2 * n, wr // 2, cols + HEAD_DIM), BF),
            scratch((2, count, width), F32), scratch((2, count, wr), F32), scratch((chips, count, width), BF),
            scratch((chips, count, width), BF), scratch((chips - 1, count, width), BF),
            scratch((chips - 1, count, width), BF),
            scratch((n - 1,) + router_shape, BF), scratch(router_shape, F32), scratch((z,) + router_shape, F32),
            scratch(gains.shape, F32), scratch((n,) + gains.shape, F32), scratch(gains.shape, F32),
            scratch((z,) + gains.shape, F32), scratch((n, mix_near.shape[1], 512), BF),
            scratch((z - 1, count, width), BF), scratch((z - 1, count, width), BF), dma(7),
            dma(chips), dma(chips), dma(chips), dma(chips), dma(chips), dma(chips), dma(chips, z - 1), dma(chips, z - 1),
            dma(wides), dma(2, wides), dma(wides), dma(wides), dma(n - 1), dma(n - 1), dma(2 * n), dma(2, 2 * n), dma(2 * n),
            dma(2 * n), dma(2 * n), dma(n - 1), dma(n - 1), dma(n - 1), dma(n - 1), dma(z - 1), dma(z - 1), dma(z - 1), dma(z - 1),
            dma(chips), dma(chips), dma(chips - 1), dma(chips - 1), dma(n - 1), dma(n - 1), dma(z), dma(z), dma(n - 1), dma(n - 1),
        ],
        ident, args, mib=62, out_specs=[ANY, ANY, ANY, VMEM, VMEM, VMEM, VMEM, ANY],
    )


def dispatch_body(n_ctx, n_shard, group, tile, rows, tail, code, recv, tail_recv,
                  zrows, ztail, ready, tail_ready, local, ss_z, rs_z, ss_t, rs_t, ss_x, rs_x, ss_y, rs_y):
    c, s, parity, sibling, others, layers = here(n_ctx, n_shard)
    greet(others, layers)
    count, width = rows.shape
    groups = n_ctx // group
    slots = recv.shape[2]
    own = [pltpu.make_async_copy(rows, zrows.at[c], local.at[0]), pltpu.make_async_copy(tail, ztail.at[c], local.at[1])]
    fans = [
        Fan(n_ctx, c, lambda d: ztail.at[flip_bits(c, d)], ss_t, rs_t, True),
        Fan(n_ctx, c, lambda d: zrows.at[flip_bits(c, d)], ss_z, rs_z, True),
    ]
    fans[0].send(0, tail)
    fans[1].send(0, rows)
    for item in own:
        item.start()
    waits = []
    seen = set()
    for k in range(groups):
        at = flip_bits(lax.div(c, group), k)
        if k == 0:
            for item in own:
                item.wait()
        table = slot_table(code[at], slots)
        for d in fans[0].order():
            if d < (k + 1) * group and d not in seen:
                fans[0].arrival(d)
                fans[1].arrival(d)
                seen.add(d)
        first = pl.multiple_of(at * group, group)
        block = ztail[pl.ds(first, group)].reshape(group * count, -1)
        tail_ready[k] = jnp.dot(table, block, preferred_element_type=F32).astype(BF).reshape(n_shard, slots, -1)

        @pl.loop(0, width // tile)
        def _(j):
            cols = pl.ds(pl.multiple_of(j * tile, tile), tile)
            block = zrows[pl.ds(first, group), :, cols].reshape(group * count, tile)
            value = jnp.dot(table, block, preferred_element_type=F32).astype(BF)
            ready[k, :, :, cols] = value.reshape(n_shard, slots, tile)

        for i, peer in enumerate(others):
            item = push(ready.at[k, peer], recv.at[s, at], ss_x.at[k, i], rs_x.at[k, i], shard=peer)
            item.start()
            waits.append(item)
            item = push(tail_ready.at[k, peer], tail_recv.at[s, at], ss_y.at[k, i], rs_y.at[k, i], shard=peer)
            item.start()
            waits.append(item)
        item = pltpu.make_async_copy(ready.at[k, s], recv.at[s, at], local.at[2 * k + 2])
        item.start()
        waits.append(item)
        item = pltpu.make_async_copy(tail_ready.at[k, s], tail_recv.at[s, at], local.at[2 * k + 3])
        item.start()
        waits.append(item)
    for fan in fans:
        fan.drain()
    for item in waits:
        item.wait()


def dispatch_rows(n_ctx, n_shard, group, capacity, rows, tail, code, ident):
    groups, slots = code.shape[0], group * capacity
    count, width = rows.shape
    few = tail.shape[1]
    return call(
        functools.partial(dispatch_body, n_ctx, n_shard, group, 512),
        [
            jax.ShapeDtypeStruct((n_shard, groups, slots, width), BF),
            jax.ShapeDtypeStruct((n_shard, groups, slots, few), BF),
        ],
        [VMEM, VMEM, VMEM],
        [
            pltpu.VMEM((n_ctx, count, width), BF), pltpu.VMEM((n_ctx, count, few), BF),
            pltpu.VMEM((groups, n_shard, slots, width), BF), pltpu.VMEM((groups, n_shard, slots, few), BF),
            DMA((2 * groups + 2,)), DMA((n_ctx,)), DMA((n_ctx,)), DMA((n_ctx,)), DMA((n_ctx,)),
        ] + [DMA((groups, n_shard - 1))] * 4,
        ident, (rows, tail, code), mib=56,
    )


def combine_body(n_ctx, n_shard, group, tile, rows, tail, mix, code, out, tail_out, mix_out,
                 land, tail_land, value, tail_value, zsend, zrecv, tsend, trecv, msend, mrecv, mix_kept, table, local,
                 ss_x, rs_x, ss_y, rs_y, ss_z, rs_z, ss_t, rs_t, ss_m, rs_m):
    c, s, parity, sibling, others, layers = here(n_ctx, n_shard)
    greet(others, layers)
    count, width = out.shape
    groups = n_ctx // group
    slots = rows.shape[2]
    near = {}
    for k in reversed(range(groups)):
        at = flip_bits(lax.div(c, group), k)
        near[k] = []
        for i, peer in enumerate(others):
            item = push(rows.at[peer, at], land.at[k, s], ss_x.at[k, i], rs_x.at[k, i], shard=peer)
            item.start()
            near[k].append(item)
            item = push(tail.at[peer, at], tail_land.at[k, s], ss_y.at[k, i], rs_y.at[k, i], shard=peer)
            item.start()
            near[k].append(item)
        item = pltpu.make_async_copy(rows.at[s, at], land.at[k, s], local.at[k, 0])
        item.start()
        near[k].append(item)
        item = pltpu.make_async_copy(tail.at[s, at], tail_land.at[k, s], local.at[k, 1])
        item.start()
        near[k].append(item)
    for k in range(groups):
        table[k] = slot_table(code[flip_bits(lax.div(c, group), k)], slots).T

    def local_sums(k, block_of):
        @pl.loop(0, width // tile)
        def _(j):
            cols = pl.ds(pl.multiple_of(j * tile, tile), tile)
            value[:, cols] = jnp.dot(table[k], block_of(cols), preferred_element_type=F32)

    def part(ref, d):
        place = lax.rem(flip_bits(c, d), group)
        return ref[pl.ds(pl.multiple_of(place * count, count), count), :]

    def in_group(k):
        return sorted(range(k * group, (k + 1) * group), key=lambda d: (lowest(d) or n_ctx, d))

    mix_fold = Fold(c, msend, mrecv, ss_m, rs_m)
    for k in reversed(range(groups)):
        at = flip_bits(lax.div(c, group), k)
        local_sums(k, lambda cols: mix[:, at, :, cols].reshape(n_shard * slots, tile))
        for d in in_group(k):
            if lowest(d) == 1:
                mix_fold.give(d, part(value, d))
            else:
                mix_kept[d // 2] = part(value, d)
    fold = Fold(c, zsend, zrecv, ss_z, rs_z)
    tail_fold = Fold(c, tsend, trecv, ss_t, rs_t)
    for k in reversed(range(groups)):
        for item in near[k]:
            item.wait()
        local_sums(k, lambda cols: land[k, :, :, cols].reshape(n_shard * slots, tile))
        tail_value[...] = jnp.dot(
            table[k], tail_land[k].reshape(n_shard * slots, -1), preferred_element_type=F32
        )
        for d in in_group(k):
            if lowest(d) == 1:
                fold.give(d, part(value, d))
                tail_fold.give(d, part(tail_value, d))
        for d in in_group(k):
            if lowest(d) != 1:
                if d:
                    mix_fold.give(d, mix_fold.take(d, mix_kept[d // 2]))
                    fold.give(d, fold.take(d, part(value, d)))
                    tail_fold.give(d, tail_fold.take(d, part(tail_value, d)))
                else:
                    mix_out[...] = mix_fold.take(0, mix_kept[0])
                    out[...] = fold.take(0, part(value, 0))
                    tail_out[...] = tail_fold.take(0, part(tail_value, 0))
    for item in (mix_fold, fold, tail_fold):
        item.drain()


def combine_rows(n_ctx, n_shard, group, rows, tail, mix, code, ident):
    groups, slots, width = rows.shape[1:]
    few = tail.shape[3]
    count = code.shape[2] // group
    sds = jax.ShapeDtypeStruct
    return call(
        functools.partial(combine_body, n_ctx, n_shard, group, 512),
        [sds((count, width), F32), sds((count, few), F32), sds((count, width), F32)],
        [VMEM] * 4,
        [
            pltpu.VMEM((groups, n_shard, slots, width), BF), pltpu.VMEM((groups, n_shard, slots, few), BF),
            pltpu.VMEM((group * count, width), F32), pltpu.VMEM((group * count, few), F32),
            pltpu.VMEM((n_ctx - 1, count, width), BF), pltpu.VMEM((n_ctx - 1, count, width), BF),
            pltpu.VMEM((n_ctx - 1, count, few), BF), pltpu.VMEM((n_ctx - 1, count, few), BF),
            pltpu.VMEM((n_ctx - 1, count, width), BF), pltpu.VMEM((n_ctx - 1, count, width), BF),
            pltpu.VMEM((n_ctx // 2, count, width), F32), pltpu.VMEM((groups, group * count, n_shard * slots), BF),
            DMA((groups, 2)),
        ] + [DMA((groups, n_shard - 1))] * 4 + [DMA((n_ctx,))] * 6,
        ident, (rows, tail, mix, code), mib=60, out_specs=[VMEM] * 3,
    )


def expert_body(n_ctx, n_shard, group, half, tile,
                rows, tail, code, w_gate, w_up, w_down, cot_in,
                out, tail_out, mix_near, mix_far, g_gate, g_up, g_down,
                zrows, ztail, ready, tail_ready, recv, tail_recv, cot, back_rows, back_tail, land, tail_land,
                hidden, grad_gate, grad_up, work, slot_dot, table, tail_value,
                zrecv, tsend, trecv, stage, stage_d, local, ss_a, rs_a,
                ss_z, rs_z, ss_t, rs_t, ss_x, rs_x, ss_y, rs_y, ss_d, rs_d, ss_e, rs_e, ss_m, rs_m,
                ss_fz, rs_fz, ss_ft, rs_ft, ss_st, ss_sd):
    c, s, parity, sibling, others, layers = here(n_ctx, n_shard)
    count, width = rows.shape
    few = tail.shape[1]
    inner = w_gate.shape[1]
    groups = n_ctx // group
    slots = recv.shape[2]
    chunk = half * slots
    experts = n_ctx * n_shard
    expert = c * n_shard + s
    loads = [
        pltpu.make_async_copy(rows, zrows.at[c], local.at[0]),
        pltpu.make_async_copy(tail, ztail.at[c], local.at[1]),
    ] + [
        pltpu.make_async_copy(cot_in.at[flip_bits(lax.div(c, group), k)], cot.at[k], local.at[2 + 2 * groups + k])
        for k in range(groups)
    ]
    for item in loads:
        item.start()
    greet(others, layers)
    fan = Fan(n_ctx, c, lambda d: ztail.at[flip_bits(c, d)], ss_t, rs_t, True)
    fan.send(0, tail)
    near_layer, far_layer = flip_bits(c, 1), flip_bits(c, 2)
    sides = [slice(0, width // 2), slice(width // 2, width)]
    near = push(rows, zrows.at[c], ss_z.at[0], rs_z.at[0], ctx=near_layer)
    near.start()
    away = [push(rows.at[:, side], zrows.at[c, :, side], ss_z.at[1 + n], rs_z.at[1 + n], ctx=far_layer)
            for n, side in enumerate(sides)]
    passed = [push(zrows.at[far_layer, :, side], zrows.at[far_layer, :, side], ss_z.at[3 + n], rs_z.at[3 + n],
                   ctx=near_layer) for n, side in enumerate(sides)]

    sent = {0: [], 1: []}
    early = (slots // group) // 16 * 16
    place = lax.rem(c, group)
    early_at = pl.multiple_of(place * (slots - early), 16)
    late_at = pl.multiple_of((1 - place) * early, 16)

    def some_slots(rows_code, first, amount):
        places = (lax.broadcasted_iota(jnp.int32, (amount, rows_code.shape[1]), 0) + first).astype(F32)
        return jnp.concatenate(
            [(places == rows_code[e : e + 1, :]).astype(BF) for e in range(n_shard)], axis=0
        )

    own_code = code[lax.div(c, group), :, pl.ds(pl.multiple_of(place * count, count), count)]
    early_picks = some_slots(own_code, early_at, early)

    @pl.loop(0, width // tile)
    def _(j):
        cols = pl.ds(pl.multiple_of(j * tile, tile), tile)
        moved = jnp.dot(early_picks, rows[:, cols], preferred_element_type=F32).astype(BF)
        ready[0, :, pl.ds(early_at, early), cols] = moved.reshape(n_shard, early, tile)

    for i, peer in enumerate(others):
        sent[0].append(push(ready.at[0, peer, pl.ds(early_at, early)], recv.at[0, s, pl.ds(early_at, early)],
                            ss_a.at[i], rs_a.at[i], shard=peer))
        sent[0][-1].start()
    loads[0].wait()
    loads[1].wait()
    near.wait_send()
    away[0].start()
    near.wait_recv()
    for k in range(groups):
        at = flip_bits(lax.div(c, group), k)
        whole = slot_table(code[at], slots)
        table[k] = whole.T
        for d in (2, 3) if k else (1,):
            fan.arrival(d)
        first = pl.multiple_of(at * group, group)
        block = ztail[pl.ds(first, group)].reshape(group * count, few)
        tail_ready[k] = jnp.dot(whole, block, preferred_element_type=F32).astype(BF).reshape(n_shard, slots, few)
        amount = slots if k else slots - early
        begin = 0 if k else late_at
        span = pl.ds(begin, amount)
        picks = some_slots(code[at], begin, amount)
        for n, side in enumerate(sides if k else [slice(0, width)]):
            if k:
                if n == 0:
                    away[0].wait_send()
                    away[1].start()
                away[n].wait_recv()
                passed[n].start()
                passed[n].wait_recv()

            @pl.loop(side.start // tile, side.stop // tile)
            def _(j):
                cols = pl.ds(pl.multiple_of(j * tile, tile), tile)
                block = zrows[pl.ds(first, group), :, cols].reshape(group * count, tile)
                moved = jnp.dot(picks, block, preferred_element_type=F32).astype(BF)
                ready[k, :, span, cols] = moved.reshape(n_shard, amount, tile)

            fresh = []
            for i, peer in enumerate(others):
                fresh.append(push(ready.at[k, peer, span, side], recv.at[k, s, span, side],
                                  ss_x.at[k + n, i], rs_x.at[k + n, i], shard=peer))
            if n == 0:
                for i, peer in enumerate(others):
                    fresh.append(push(tail_ready.at[k, peer], tail_recv.at[k, s], ss_y.at[k, i], rs_y.at[k, i], shard=peer))
                fresh.append(pltpu.make_async_copy(tail_ready.at[k, s], tail_recv.at[k, s], local.at[3 + 2 * k]))
            if n == k:
                fresh.append(pltpu.make_async_copy(ready.at[k, s], recv.at[k, s], local.at[2 + 2 * k]))
            for item in fresh:
                item.start()
            sent[k] += fresh
    fan.drain()
    away[1].wait_send()
    for item in passed:
        item.wait_send()
    for item in loads[2:]:
        item.wait()

    gate_pre, up_pre = work.at[0:chunk, 0:inner], work.at[0:chunk, inner : 2 * inner]
    value = work.at[0 : group * count, 0:width]
    column = lax.broadcasted_iota(jnp.int32, (1, few), 1)
    is_coarse, is_fine = column == expert, column == experts + expert

    def send_back(src, dst, e, ss, rs):
        @pl.when(s != e)
        def _():
            push(src.at[e], dst.at[s], ss.at[e], rs.at[s], shard=e).start()

        @pl.when(s == e)
        def _():
            pltpu.make_async_copy(src.at[e], dst.at[e], rs.at[e]).start()

    def wait_back(src, dst, ss, rs):
        for e in range(n_shard):
            @pl.when(s != e)
            def _():
                push(src.at[e], dst.at[e], ss.at[e], rs.at[e], shard=e).wait()

            @pl.when(s == e)
            def _():
                pltpu.make_async_copy(src.at[e], dst.at[e], rs.at[e]).wait()

    def experts_part(k, h):
        of = slice(h * half, (h + 1) * half)
        r = pl.ds((k * n_shard + h * half) * slots, chunk)
        gates = jnp.sum(
            jnp.where(is_coarse | is_fine, tail_recv[k, of].reshape(chunk, few).astype(F32), 0.0), axis=1, keepdims=True
        )

        @pl.loop(0, inner // 256)
        def _(j):
            cols = pl.ds(pl.multiple_of(j * 256, 256), 256)
            x = recv[k, of].reshape(chunk, width)
            g = jnp.dot(x, w_gate[:, cols], preferred_element_type=F32)
            u = jnp.dot(x, w_up[:, cols], preferred_element_type=F32)
            gate_pre[:, cols] = g
            up_pre[:, cols] = u
            hidden[r, cols] = (g * jax.nn.sigmoid(g) * u).astype(BF)

        slot_dot[...] = jnp.zeros_like(slot_dot)

        @pl.loop(0, width // tile)
        def _(j):
            cols = pl.ds(pl.multiple_of(j * tile, tile), tile)
            o = jnp.dot(hidden[r, :], w_down[:, cols], preferred_element_type=F32).astype(BF).astype(F32)
            up_row = cot[k, of, :, cols].reshape(chunk, tile).astype(F32)
            slot_dot[...] += jnp.sum(o * up_row, axis=1, keepdims=True)
            ready[k, of, :, cols] = (gates * o).astype(BF).reshape(half, slots, tile)
            cot[k, of, :, cols] = (gates * up_row).astype(BF).reshape(half, slots, tile)

        coarse = slot_dot[...].astype(BF).astype(F32)
        fine = slot_dot[...] - coarse
        back_tail[k, of] = jnp.where(is_coarse, coarse, jnp.where(is_fine, fine, 0.0)).astype(BF).reshape(half, slots, few)

        @pl.loop(0, inner // 256)
        def _(j):
            cols = pl.ds(pl.multiple_of(j * 256, 256), 256)
            gh = lax.dot_general(cot[k, of].reshape(chunk, width), w_down[cols, :], (((1,), (1,)), ((), ())),
                                 preferred_element_type=F32)
            g, u = gate_pre[:, cols], up_pre[:, cols]
            sig = jax.nn.sigmoid(g)
            grad_gate[r, cols] = (gh * u * (sig * (1.0 + g * (1.0 - sig)))).astype(BF)
            grad_up[r, cols] = (gh * (g * sig)).astype(BF)

        @pl.loop(0, width // tile)
        def _(j):
            cols = pl.ds(pl.multiple_of(j * tile, tile), tile)
            gx = lax.dot_general(grad_gate[r, :], w_gate[cols, :], (((1,), (1,)), ((), ())), preferred_element_type=F32)
            gx += lax.dot_general(grad_up[r, :], w_up[cols, :], (((1,), (1,)), ((), ())), preferred_element_type=F32)
            back_rows[k, of, :, cols] = gx.astype(BF).reshape(half, slots, tile)

    def send_part(k, h):
        for e in range(h * half, (h + 1) * half):
            send_back(back_rows.at[k], land.at[k], e, ss_d.at[k], rs_d.at[k])
            send_back(back_tail.at[k], tail_land.at[k], e, ss_e.at[k], rs_e.at[k])

    halves = n_shard // half
    for k in range(groups):
        for item in sent[k]:
            item.wait()
        for h in range(halves):
            experts_part(k, h)
            if k or h + 1 < halves:
                send_part(k, h)
    send_part(0, halves - 1)
    for e in range(n_shard):
        send_back(ready.at[groups - 1], mix_far, e, ss_m, rs_m)
    keep = pltpu.make_async_copy(ready.at[0], mix_near, local.at[0])
    keep.start()

    everything = groups * n_shard * slots

    def stage_out(j, which):
        at = pl.ds(pl.multiple_of(j * 256, 256), 256)
        return pltpu.make_async_copy(stage.at[which], (g_gate, g_up)[which].at[at], ss_st.at[which])

    @pl.loop(0, width // 256)
    def _(j):
        x = recv[:, :, :, pl.ds(pl.multiple_of(j * 256, 256), 256)].reshape(everything, 256)
        for which, grad in enumerate((grad_gate, grad_up)):
            total = lax.dot_general(x, grad[...], (((0,), (0,)), ((), ())), preferred_element_type=F32).astype(BF)

            @pl.when(j >= 1)
            def _():
                stage_out(j - 1, which).wait()

            stage[which] = total
            stage_out(j, which).start()

    def down_out(j):
        return pltpu.make_async_copy(stage_d, g_down.at[:, pl.ds(pl.multiple_of(j * 256, 256), 256)], ss_sd)

    @pl.loop(0, width // 256)
    def _(j):
        grad = cot[:, :, :, pl.ds(pl.multiple_of(j * 256, 256), 256)].reshape(everything, 256)
        total = lax.dot_general(
            hidden[...], grad, (((0,), (0,)), ((), ())), preferred_element_type=F32).astype(BF)

        @pl.when(j >= 1)
        def _():
            down_out(j - 1).wait()

        stage_d[...] = total
        down_out(j).start()

    last = width // 256 - 1
    stage_out(last, 0).wait()
    stage_out(last, 1).wait()
    down_out(last).wait()

    def local_sums(k, ref):
        @pl.loop(0, width // tile)
        def _(j):
            cols = pl.ds(pl.multiple_of(j * tile, tile), tile)
            block = ref[k, :, :, cols].reshape(n_shard * slots, tile)
            value[:, cols] = jnp.dot(table[k], block, preferred_element_type=F32)

    def part(ref, d):
        place = lax.rem(flip_bits(c, d), group)
        return ref[pl.ds(pl.multiple_of(place * count, count), count), :]

    folds = [Fold(c, zrows.at[:, :, side], zrecv.at[:, :, side], ss_fz.at[n], rs_fz.at[n]) for n, side in enumerate(sides)]
    tail_fold = Fold(c, tsend, trecv, ss_ft, rs_ft)
    for k in reversed(range(groups)):
        wait_back(back_rows.at[k], land.at[k], ss_d.at[k], rs_d.at[k])
        wait_back(back_tail.at[k], tail_land.at[k], ss_e.at[k], rs_e.at[k])
        local_sums(k, land)
        tail_value[...] = jnp.dot(table[k], tail_land[k].reshape(n_shard * slots, few), preferred_element_type=F32)
        if k:
            tail_fold.give(3, part(tail_value, 3))
            folds[0].give(3, part(value, 3)[:, sides[0]])
            folds[0].items[3].wait_send()
            folds[0].left.add(3)
            folds[1].give(3, part(value, 3)[:, sides[1]])
            for fold, side in zip(folds, sides):
                fold.give(2, fold.take(2, part(value, 2)[:, side]))
            tail_fold.give(2, tail_fold.take(2, part(tail_value, 2)))
        else:
            tail_fold.give(1, part(tail_value, 1))
            for fold, side in zip(folds, sides):
                fold.give(1, part(value, 1)[:, side])
    for fold, side in zip(folds, sides):
        out[:, side] = fold.take(0, part(value, 0)[:, side])
    tail_out[...] = tail_fold.take(0, part(tail_value, 0))
    for fold in folds + [tail_fold]:
        fold.drain()
    wait_back(ready.at[groups - 1], mix_far, ss_m, rs_m)
    keep.wait()


def run_experts(n_ctx, n_shard, group, capacity, rows, tail, code, w_gate, w_up, w_down, cot_rows, ident):
    n, z, groups, slots = n_shard, n_ctx, code.shape[0], group * capacity
    count, width = rows.shape
    few, inner, half = tail.shape[1], w_gate.shape[1], n_shard // 2
    everything, chunk = groups * n * slots, half * slots
    sds, scratch = jax.ShapeDtypeStruct, pltpu.VMEM
    dma = lambda *shape: DMA(shape)
    wide, thin = (groups, n, slots, width), (groups, n, slots, few)
    return call(
        functools.partial(expert_body, z, n, group, half, 512),
        [
            sds((count, width), F32), sds((count, few), F32), sds((n, slots, width), BF), sds((n, slots, width), BF),
            sds((width, inner), BF), sds((width, inner), BF), sds((inner, width), BF),
        ],
        [VMEM] * 6 + [ANY],
        [
            scratch((z, count, width), BF), scratch((z, count, few), BF), scratch(wide, BF), scratch(thin, BF),
            scratch(wide, BF), scratch(thin, BF), scratch(wide, BF), scratch(wide, BF), scratch(thin, BF),
            scratch(wide, BF), scratch(thin, BF),
            scratch((everything, inner), BF), scratch((everything, inner), BF), scratch((everything, inner), BF),
            scratch((max(chunk, group * count), max(2 * inner, width)), F32), scratch((chunk, 1), F32),
            scratch((groups, group * count, n * slots), BF),
            scratch((group * count, few), F32), scratch((z - 1, count, width), BF),
            scratch((z - 1, count, few), BF), scratch((z - 1, count, few), BF),
            scratch((2, 256, inner), BF), scratch((inner, 256), BF), dma(2 + 3 * groups), dma(n - 1), dma(n - 1),
        ] + [dma(5)] * 2 + [dma(z)] * 2 + [dma(groups + 1, n - 1)] * 2 + [dma(groups, n - 1)] * 2 + [dma(groups, n)] * 4
        + [dma(n)] * 2 + [dma(2, z)] * 2 + [dma(z)] * 2 + [dma(2), DMA],
        ident, (rows, tail, code, w_gate, w_up, w_down, cot_rows), mib=62, out_specs=[VMEM] * 2 + [ANY] * 5,
    )


def rms_scale(hidden, gain):
    return hidden * lax.rsqrt(jnp.mean(hidden * hidden, axis=-1, keepdims=True) + epsilon) * gain


def rotate(headwise, places):
    half_size = headwise.shape[-1] // 2
    frequency = rope_base ** (-jnp.arange(half_size, dtype=F32) * 2.0 / headwise.shape[-1])
    angles = places.astype(F32)[:, None] * frequency[None, :]
    cosine = jnp.cos(angles)[:, None, :]
    sine = jnp.sin(angles)[:, None, :]
    former = headwise[..., :half_size]
    latter = headwise[..., half_size:]
    return jnp.concatenate(
        [former * cosine - latter * sine, latter * cosine + former * sine], axis=-1
    )


def place_of(row_ids, order, block_rows):
    block_ids = jnp.arange(order.shape[0], dtype=jnp.int32)
    owner_block = row_ids // block_rows
    picked_block = jnp.sum(
        jnp.where(owner_block[:, None] == block_ids[None, :], order[None, :], 0), axis=1
    )
    return picked_block * block_rows + row_ids % block_rows


def dot(left, right):
    return jnp.dot(left, right, preferred_element_type=F32)


def contract_rows(left, right):
    return lax.dot_general(left, right, (((0,), (0,)), ((), ())), preferred_element_type=F32)


def contract_cols(left, right):
    return lax.dot_general(left, right, (((1,), (1,)), ((), ())), preferred_element_type=F32)


def exchange_shard(x):
    return lax.all_to_all(x, "shard", split_axis=0, concat_axis=0, tiled=True)


def gather_ctx(x):
    return lax.all_gather(x, "ctx", axis=0, tiled=False)


def shards(
    tokens,
    cotangent,
    block_order,
    routes,
    attn_gain,
    w_query,
    key_weight,
    value_weight,
    query_gain,
    key_gain,
    w_out,
    ffn_gain,
    w_router,
    w_gate,
    w_up,
    w_down,
):
    rows = tokens.shape[1]
    width = tokens.shape[2]
    ctx_count = lax.axis_size("ctx")
    shard_count = lax.axis_size("shard")
    my_ctx = lax.axis_index("ctx")
    my_shard = lax.axis_index("shard")
    experts = ctx_count * shard_count
    block_rows = rows // 2
    heads = QUERY_HEADS // shard_count
    head_cols = heads * HEAD_DIM
    sharers = shard_count // KEY_VALUE_HEADS
    score_scale = HEAD_DIM ** (-0.5)
    top_count = routes.shape[2]
    capacity = rows * top_count // experts + max(rows * top_count // (4 * experts), 1)
    sequence = rows * ctx_count
    plane = rows * shard_count
    wrows = width // shard_count

    inputs = tokens[0].astype(F32)
    upstream_b = cotangent[0]
    upstream = upstream_b.astype(F32)

    group = 1
    while group * capacity % 16:
        group *= 2
    groups = ctx_count // group
    slot_rows = shard_count * ctx_count * capacity
    block_shape = (shard_count, groups, group * capacity)
    row_ids = my_ctx * rows + jnp.arange(rows, dtype=jnp.int32)
    q_places = place_of(row_ids, block_order, block_rows)
    k_places = place_of(jnp.arange(sequence, dtype=jnp.int32), block_order, block_rows)
    bias = jnp.where(k_places[None, :] <= q_places[:, None], 0.0, -1e30).astype(F32)
    frequency = rope_base ** (-jnp.arange(HEAD_DIM // 2, dtype=F32) * 2.0 / HEAD_DIM)
    angles = q_places.astype(F32)[:, None] * frequency[None, :]
    cosine = jnp.concatenate([jnp.cos(angles)] * 2, axis=1)
    sine = jnp.concatenate([-jnp.sin(angles), jnp.sin(angles)], axis=1)
    (
        normed_all, w_mine, router_all, code, upstream_rows, query_pre, kv_pre, queries, kv_all, attn_rows, middle,
    ) = front(
        ctx_count, shard_count, group, capacity, KEY_VALUE_HEADS,
        (
            tokens[0], attn_gain[None], w_query, key_weight, value_weight, routes[0].T, w_router.T, upstream_b,
            cosine, sine, bias, query_gain[None], key_gain[None], w_out,
        ),
        0,
    )
    is_key = lax.rem(my_shard, 2) == 0
    part_count = sharers // 2

    def prep(pre, gain):
        shape = pre.shape
        flat = pre.reshape(-1, rows, shape[-2], HEAD_DIM)
        return jax.vmap(lambda v: rotate(rms_scale(v, gain), q_places))(flat).reshape(shape)

    normed_two = rms_scale(middle, ffn_gain)
    second_b = normed_two.astype(BF)
    logits = contract_cols(second_b, router_all)
    chosen = jnp.sum(
        (routes[0][:, :, None] == jnp.arange(experts, dtype=jnp.int32)).astype(F32), axis=1
    )

    def gates_of(log, mask):
        masked = jnp.where(mask > 0, log, -1e30)
        peak = jnp.max(masked, axis=-1, keepdims=True)
        risen = jnp.exp(masked - peak) * mask
        return risen / jnp.maximum(jnp.sum(risen, axis=-1, keepdims=True), 1e-30)

    gates = gates_of(logits, chosen)

    tail_cols = -(-2 * experts // 128) * 128

    def two_parts(value):
        coarse = value.astype(BF).astype(F32)
        return coarse.astype(BF), (value - coarse).astype(BF)

    gates_two = jnp.concatenate(two_parts(gates), axis=1)
    gates_two = jnp.pad(gates_two, ((0, 0), (0, tail_cols - 2 * experts)))
    small = plane * width <= 2**21 and ctx_count == 4 and group == 2
    if small:
        grad_second, back_tail, mix_near, mix_far, grad_w_gate, grad_w_up, grad_w_down = run_experts(
            ctx_count, shard_count, group, capacity, second_b, gates_two, code, w_gate[0], w_up[0], w_down[0],
            upstream_rows, 3,
        )
        grad_w_gate, grad_w_up, grad_w_down = (
            grad_w_gate.astype(F32), grad_w_up.astype(F32), grad_w_down.astype(F32),
        )
    else:
        received, gate_tail = dispatch_rows(ctx_count, shard_count, group, capacity, second_b, gates_two, code, 3)
        received = received.reshape(slot_rows, width)
        my_expert = my_ctx * shard_count + my_shard
        upstream_rows = jnp.swapaxes(upstream_rows, 0, 1).reshape(slot_rows, width)
        column = jnp.arange(tail_cols, dtype=jnp.int32)[None, :]
        mine_column = (column == my_expert) | (column == experts + my_expert)
        gate_tail = gate_tail.reshape(slot_rows, tail_cols).astype(F32)
        slot_gates = jnp.sum(jnp.where(mine_column, gate_tail, 0.0), axis=1, keepdims=True)
        gate_pre = dot(received, w_gate[0])
        up_pre = dot(received, w_up[0])
        activated = jax.nn.silu(gate_pre)
        hidden_b = (activated * up_pre).astype(BF)
        expert_out = dot(hidden_b, w_down[0]).astype(BF)
        expert_out_f = expert_out.astype(F32)
        mix_sent = (slot_gates * expert_out_f).astype(BF)
        mix_sent, upstream_rows, expert_out = lax.optimization_barrier((mix_sent, upstream_rows, expert_out))
        expert_out_f = expert_out.astype(F32)
        mix_back = exchange_shard(mix_sent.reshape(block_shape + (width,)))
        upstream_rows = upstream_rows.astype(F32)
        slot_dot = jnp.sum(expert_out_f * upstream_rows, axis=1, keepdims=True)
        grad_expert = (slot_gates * upstream_rows).astype(BF)
        grad_w_down = contract_rows(hidden_b, grad_expert)
        grad_hidden = contract_cols(grad_expert, w_down[0])
        sigmoid_g = jax.nn.sigmoid(gate_pre)
        silu_slope = sigmoid_g * (1.0 + gate_pre * (1.0 - sigmoid_g))
        grad_gate_pre = (grad_hidden * up_pre * silu_slope).astype(BF)
        grad_up_pre = (grad_hidden * activated).astype(BF)
        grad_w_gate = contract_rows(received, grad_gate_pre)
        grad_w_up = contract_rows(received, grad_up_pre)
        grad_received = contract_cols(grad_gate_pre, w_gate[0]) + contract_cols(grad_up_pre, w_up[0])

        coarse, fine = two_parts(slot_dot)
        tail = jnp.where(column == my_expert, coarse, jnp.where(column == experts + my_expert, fine, jnp.zeros((), BF)))
        grad_second, back_tail, mixture = combine_rows(
            ctx_count, shard_count, group, grad_received.astype(BF).reshape(block_shape + (width,)),
            tail.reshape(block_shape + (tail_cols,)), mix_back, code, 4,
        )
    grad_gates = back_tail[:, :experts] + back_tail[:, experts : 2 * experts]
    grad_logits_b = (
        gates * (grad_gates - jnp.sum(gates * grad_gates, axis=-1, keepdims=True))
    ).astype(BF)
    router_part = contract_rows(grad_logits_b, second_b).astype(BF)
    grad_second = grad_second + dot(grad_logits_b, router_all)
    unused, norm_two_back = jax.vjp(rms_scale, middle, ffn_gain)
    grad_middle_part, grad_ffn_gain = norm_two_back(grad_second)
    grad_middle = upstream + grad_middle_part
    grad_proj_b = grad_middle.astype(BF)

    router_parts = jnp.swapaxes(router_part.reshape(experts, shard_count, wrows), 0, 1)
    if small:
        gains = jnp.concatenate([jnp.zeros((1, width), F32), grad_ffn_gain[None], jnp.zeros((6, width), F32)])
        q_sum, kv_sum, out_sum, router_sum, gains, grad_input_part, mixture, unused = back(
            ctx_count, shard_count, group, heads,
            (
                grad_proj_b, queries, kv_all, attn_rows, query_pre, kv_pre, w_out, normed_all, w_mine,
                cosine, sine, bias, query_gain[None], key_gain[None], tokens[0], attn_gain[None], gains, router_parts,
                mix_near, mix_far, code,
            ),
            5,
        )
    else:
        normed_all = normed_all.reshape(plane, width)
        w_mine = w_mine.reshape(width, head_cols + HEAD_DIM)
        query_pre = query_pre.reshape(shard_count, rows, heads, HEAD_DIM)
        kv_pre = kv_pre.reshape(plane, HEAD_DIM)
        queries = queries.reshape(shard_count, rows, heads, HEAD_DIM)
        kv_all = kv_all.reshape(2, shard_count, sequence, HEAD_DIM)
        keys, values = kv_all[0], kv_all[1]
        attn_rows = attn_rows.reshape(plane, head_cols)
        grad_proj_all = spread(shard_count, grad_proj_b, 5).reshape(plane, width)
        out_part = contract_rows(attn_rows, grad_proj_all).astype(BF)
        out_part, grad_proj_all = lax.optimization_barrier((out_part, grad_proj_all))
        grad_attn = contract_cols(grad_proj_all, w_out).astype(BF)
        grad_heads = grad_attn.reshape(shard_count, rows, heads, HEAD_DIM)
        scores = (
            jnp.einsum("sthd,spd->shtp", queries, keys, preferred_element_type=F32) * score_scale
        )
        scores = scores + bias
        raised = jnp.exp(scores - jnp.max(scores, axis=-1, keepdims=True))
        probs = raised / jnp.sum(raised, axis=-1, keepdims=True)
        probs_b = probs.astype(BF)
        grad_probs = jnp.einsum("sthd,spd->shtp", grad_heads, values, preferred_element_type=F32)
        delta = jnp.sum(probs * grad_probs, axis=-1, keepdims=True)
        grad_scores = (probs * (grad_probs - delta)).astype(BF)
        grad_query = score_scale * jnp.einsum(
            "shtp,spd->sthd", grad_scores, keys, preferred_element_type=F32
        )
        grad_keys = score_scale * jnp.einsum(
            "shtp,sthd->spd", grad_scores, queries, preferred_element_type=F32
        )
        grad_values = jnp.einsum("shtp,sthd->spd", probs_b, grad_heads, preferred_element_type=F32)
        grad_kv = jnp.stack([grad_keys, grad_values]).astype(BF)
        grad_kv = key_back(
            ctx_count, shard_count, grad_kv.reshape(2, shard_count, ctx_count, rows, HEAD_DIM), 6
        )
        unused, query_back = jax.vjp(prep, query_pre, query_gain)
        grad_query_pre, grad_query_gain = query_back(grad_query)
        kv_shape = (shard_count, rows, 1, HEAD_DIM)
        unused, key_prep_back = jax.vjp(prep, kv_pre.reshape(kv_shape), key_gain)
        grad_key_pre, grad_key_gain = key_prep_back(grad_kv.reshape(kv_shape))
        grad_key_gain = jnp.where(is_key, grad_key_gain, 0.0)
        grad_kv_full = jnp.where(
            is_key, grad_key_pre.reshape(plane, HEAD_DIM), grad_kv.reshape(plane, HEAD_DIM)
        ).astype(BF)
        grad_pre = jnp.concatenate(
            [grad_query_pre.reshape(plane, head_cols).astype(BF), grad_kv_full], axis=1
        )
        gains = jnp.concatenate(
            [
                jnp.zeros((1, width), F32),
                grad_ffn_gain[None],
                jnp.pad(
                    jnp.concatenate([grad_query_gain, grad_key_gain])[None],
                    ((0, 6 - 1), (0, width - 2 * HEAD_DIM)),
                ),
            ]
        )
        grad_w = contract_rows(normed_all, grad_pre).astype(BF).reshape(shard_count, wrows, -1)
        q_sum, kv_sum, out_sum, router_sum, gains, grad_input_part = finish(
            ctx_count, shard_count, head_cols, grad_w, out_part.reshape(8, -1, width), router_parts, gains, grad_pre, w_mine,
            tokens[0], attn_gain[None], 8,
        )
    mixed = (middle + mixture).astype(BF)
    grad_tokens = grad_middle + grad_input_part
    grad_attn_gain, grad_ffn_gain = gains[0], gains[1]
    grad_query_gain, grad_key_gain = gains[2, :HEAD_DIM], gains[2, HEAD_DIM : 2 * HEAD_DIM]
    grad_w_query = q_sum.astype(F32)
    grad_w_out = out_sum.reshape(head_cols, width).astype(F32)
    kinds = kv_sum.astype(F32).reshape(KEY_VALUE_HEADS, part_count, 2, wrows, HEAD_DIM)
    kinds = jnp.transpose(jnp.sum(kinds, axis=1), (1, 2, 0, 3)).reshape(2, wrows, -1)
    grad_w_key, grad_w_value = kinds[0], kinds[1]
    grad_w_router = router_sum.T
    return (
        mixed[None],
        grad_tokens[None],
        grad_attn_gain,
        grad_w_query,
        grad_w_key,
        grad_w_value,
        grad_query_gain,
        grad_key_gain,
        grad_w_out,
        grad_ffn_gain,
        grad_w_router,
        grad_w_gate[None],
        grad_w_up[None],
        grad_w_down[None],
    )


def solution(mesh):
    rows = P("shard", "ctx", None)
    matrix = P("shard", None)
    expert = P(("ctx", "shard"), None, None)
    return jax.shard_map(
        shards,
        mesh=mesh,
        in_specs=(
            rows, rows, P(), rows, P(), matrix, matrix, matrix, P(), P(), matrix, P(), matrix,
            expert, expert, expert,
        ),
        out_specs=(
            rows, rows, P(), matrix, matrix, matrix, P(), P(), matrix, P(), matrix,
            expert, expert, expert,
        ),
        check_vma=False,
    )
```

```python
import functools

import jax
import jax.numpy as jnp
from jax import lax
from jax.experimental import pallas as pl
from jax.experimental.pallas import tpu as pltpu
from jax.sharding import PartitionSpec as P

BF = jnp.bfloat16
F32 = jnp.float32
MESH = pl.DeviceIdType.MESH
ANY = pl.BlockSpec(memory_space=pl.ANY)
VMEM = pl.BlockSpec(memory_space=pltpu.VMEM)
DMA = pltpu.SemaphoreType.DMA
epsilon = 1e-06
rope_base = 1000000.0
QUERY_HEADS = 32
KEY_VALUE_HEADS = 4
HEAD_DIM = 128


def push(src, dst, send_sem, recv_sem, **where):
    return pltpu.make_async_remote_copy(
        src_ref=src, dst_ref=dst, send_sem=send_sem, recv_sem=recv_sem,
        device_id=where, device_id_type=MESH,
    )


def greet(shard_peers, ctx_peers):
    barrier = pltpu.get_barrier_semaphore()
    for peer in shard_peers:
        pl.semaphore_signal(barrier, inc=1, device_id={"shard": peer}, device_id_type=MESH)
    for peer in ctx_peers:
        pl.semaphore_signal(barrier, inc=1, device_id={"ctx": peer}, device_id_type=MESH)
    pl.semaphore_wait(barrier, len(shard_peers) + len(ctx_peers))


def here(ctx_count, shard_count):
    c, s = lax.axis_index("ctx"), lax.axis_index("shard")
    parity = lax.rem(s, 2)
    sibling = s + 1 - 2 * parity
    others = [lax.rem(s + d, shard_count) for d in range(1, shard_count)]
    layers = [lax.rem(c + d, ctx_count) for d in range(1, ctx_count)]
    return c, s, parity, sibling, others, layers


def flip_bits(index, mask):
    result = index
    bit = 1
    while bit <= mask:
        if mask & bit:
            result = result + bit - 2 * bit * lax.rem(lax.div(index, bit), 2)
        bit *= 2
    return result


def lowest(d):
    return d & -d


class Fan:
    def __init__(self, n_ctx, c, block, ss, rs, near_first):
        self.n_ctx, self.c, self.block, self.ss, self.rs, self.near_first = n_ctx, c, block, ss, rs, near_first
        self.items = {}

    def send(self, d, src):
        bits = [b for b in (1, 2, 4, 8, 16) if b < (lowest(d) or self.n_ctx)]
        for b in bits if self.near_first else reversed(bits):
            item = push(src, self.block(d), self.ss.at[d | b], self.rs.at[d | b], ctx=flip_bits(self.c, b))
            item.start()
            self.items[d | b] = item

    def arrival(self, d):
        self.items[d].wait_recv()
        if lowest(d) > 1:
            self.send(d, self.block(d))

    def order(self):
        return sorted(range(1, self.n_ctx), key=lambda d: (bin(d).count("1"), d if self.near_first else -d))

    def drain(self):
        for d in range(1, self.n_ctx):
            self.items[d].wait_send()


class Fold:
    def __init__(self, c, sent, received, ss, rs, slots=None, after=None):
        self.c, self.sent, self.received, self.ss, self.rs = c, sent, received, ss, rs
        self.slots, self.after = slots or {}, after or {}
        self.items, self.left = {}, set()

    def take(self, d, value):
        for b in (1, 2, 4, 8, 16):
            if b < lowest(d) or (d == 0 and b in self.items):
                self.items[d | b].wait_recv()
                value = value + self.received[(d | b) - 1].astype(F32)
        return value

    def give(self, d, value):
        slot = self.slots.get(d, d - 1)
        if d in self.after:
            other, which = self.after[d]
            other.items[which].wait_send()
            other.left.add(which)
        self.sent[slot] = value.astype(BF)
        item = push(self.sent.at[slot], self.received.at[d - 1], self.ss.at[d], self.rs.at[d],
                    ctx=flip_bits(self.c, lowest(d)))
        item.start()
        self.items[d] = item

    def give_as_is(self, d, ref):
        self.items[d] = push(ref, self.received.at[d - 1], self.ss.at[d], self.rs.at[d],
                             ctx=flip_bits(self.c, lowest(d)))
        self.items[d].start()

    def drain(self):
        for d, item in self.items.items():
            if d not in self.left:
                item.wait_send()


def call(body, outs, in_specs, scratch, ident, args, mib=48, out_specs=None):
    return pl.pallas_call(
        body,
        out_shape=outs,
        in_specs=in_specs,
        out_specs=out_specs if out_specs is not None else [ANY] * len(outs),
        scratch_shapes=scratch,
        compiler_params=pltpu.CompilerParams(
            collective_id=ident, has_side_effects=True, vmem_limit_bytes=mib * 2**20
        ),
    )(*args)


def by_core(s, n_shard):
    return lax.rem(s, 2) * (n_shard // 2) + lax.div(s, 2)


def from_core(place, n_shard):
    return place % (n_shard // 2) * 2 + place // (n_shard // 2)


def slot_table(code, slots):
    places = lax.broadcasted_iota(jnp.int32, (slots, code.shape[1]), 0).astype(F32)
    return jnp.concatenate(
        [(places == code[e : e + 1, :]).astype(BF) for e in range(code.shape[0])], axis=0
    )


def turn(value, cosine, sine):
    return value * cosine + pltpu.roll(value, HEAD_DIM // 2, 1) * sine


def unit_rows(value):
    scale = lax.rsqrt(jnp.mean(value * value, axis=-1, keepdims=True) + epsilon)
    return value * scale, scale


def front_body(n_ctx, n_shard, group, capacity, heads, kv_heads, paired, tile,
               tokens, gain, w_query, key_w, value_w, routes, router, cot, cosine, sine, bias, q_gain, k_gain, w_out,
               rows_out, w_all_out, router_all, code, cot_rows, qpre_out, kvpre, q_out, kv_out, attn_out, mid,
               own_rows, rows_all, w_all, zroutes, zcot, ready, qpre, q, kv, attn,
               own_part, pair, to_sib, sib, to_chip, got,
               local, ss_row, rs_row, ss_fwd, rs_fwd, ss_w, rs_w, ss_k, rs_k, ss_rt, rs_rt, ss_ro, rs_ro, ss_z, rs_z,
               ss_x, rs_x, ss_kz, rs_kz, ss_kf, rs_kf, ss_s, rs_s, ss_c, rs_c, out_sem):
    c, s, parity, sibling, others, layers = here(n_ctx, n_shard)
    chips = n_shard // 2
    chip = lax.div(s, 2)
    count, width = tokens.shape
    wr = w_query.shape[0]
    cols = heads * HEAD_DIM
    sharers = n_shard // kv_heads
    groups = n_ctx // group
    slots = group * capacity
    keys = n_ctx * count
    mates = [lax.rem(s + 2 * d, n_shard) for d in range(1, chips)]
    x = tokens[...].astype(F32)
    unit, unused = unit_rows(x)
    own_rows[...] = (unit * gain[...]).astype(BF)
    greet(others, layers)

    route_fan = Fan(n_ctx, c, lambda d: zroutes.at[flip_bits(c, d)], ss_ro, rs_ro, False)
    route_fan.send(0, routes)
    cot_fan = Fan(n_ctx, c, lambda d: zcot.at[flip_bits(c, d)], ss_z, rs_z, False)
    cot_fan.send(0, cot)
    first, waits = [], []
    for d in range(1, chips):
        item = push(own_rows, rows_all.at[s], ss_row.at[d], rs_row.at[d], shard=mates[d - 1])
        item.start()
        first.append(item)
    item = push(own_rows, rows_all.at[s], ss_fwd.at[0], rs_fwd.at[0], shard=sibling)
    item.start()
    waits.append(item)
    w_waits = []
    for i, peer in enumerate(others):
        from_q = w_query.at[:, pl.ds(pl.multiple_of(peer * cols, cols), cols)]
        item = push(from_q, w_all.at[s, :, pl.ds(0, cols)], ss_w.at[i], rs_w.at[i], shard=peer)
        item.start()
        w_waits.append(item)
        head = pl.ds(pl.multiple_of(lax.div(peer, sharers) * HEAD_DIM, HEAD_DIM), HEAD_DIM)
        for kind, ref in enumerate((key_w, value_w)):
            item = push(ref.at[:, head], w_all.at[s, :, pl.ds(cols, HEAD_DIM)], ss_k.at[i], rs_k.at[i], shard=peer)

            @pl.when(lax.rem(peer, 2) == kind)
            def _(item=item):
                item.start()

        w_waits.append(item)
        item = push(router, router_all.at[:, pl.ds(pl.multiple_of(s * wr, wr), wr)], ss_rt.at[i], rs_rt.at[i], shard=peer)
        item.start()
        waits.append(item)
    copies = [
        pltpu.make_async_copy(own_rows, rows_all.at[s], local.at[0]),
        pltpu.make_async_copy(w_query.at[:, pl.ds(pl.multiple_of(s * cols, cols), cols)],
                              w_all.at[s, :, pl.ds(0, cols)], local.at[1]),
        pltpu.make_async_copy(routes, zroutes.at[c], local.at[2]),
        pltpu.make_async_copy(router, router_all.at[:, pl.ds(pl.multiple_of(s * wr, wr), wr)], local.at[3]),
        pltpu.make_async_copy(cot, zcot.at[c], local.at[4]),
    ]
    for item in copies:
        item.start()
    head = pl.ds(pl.multiple_of(lax.div(s, sharers) * HEAD_DIM, HEAD_DIM), HEAD_DIM)
    for kind, ref in enumerate((key_w, value_w)):
        own_head = pltpu.make_async_copy(ref.at[:, head], w_all.at[s, :, pl.ds(cols, HEAD_DIM)], local.at[5])

        @pl.when(parity == kind)
        def _(own_head=own_head):
            own_head.start()

    copies[2].wait()
    for d in route_fan.order():
        route_fan.arrival(d)
    before = (
        lax.broadcasted_iota(jnp.int32, (count, count), 0) < lax.broadcasted_iota(jnp.int32, (count, count), 1)
    ).astype(BF)
    for layer in range(n_ctx):
        named = zroutes[layer]
        mask = jnp.concatenate(
            [jnp.max((named == c * n_shard + e).astype(F32), axis=0, keepdims=True) for e in range(n_shard)], axis=0
        )
        rank = jnp.dot(mask.astype(BF), before, preferred_element_type=F32)
        at = layer % group
        code[layer // group, :, at * count : (at + 1) * count] = jnp.where(
            mask > 0, rank + float(at * capacity), -1.0
        )

    for d in range(1, chips):
        first[d - 1].wait()
        origin = lax.rem(s + n_shard - 2 * d, n_shard)
        item = push(rows_all.at[origin], rows_all.at[origin], ss_fwd.at[d], rs_fwd.at[d], shard=sibling)
        item.start()
        waits.append(item)
    for d in cot_fan.order():
        cot_fan.arrival(d)
    copies[4].wait()
    for k in range(groups):
        table = slot_table(code[k], slots)

        @pl.loop(0, width // tile)
        def _(j):
            part = pl.ds(pl.multiple_of(j * tile, tile), tile)
            block = zcot[k * group : (k + 1) * group, :, part].reshape(group * count, tile)
            value = jnp.dot(table, block, preferred_element_type=F32).astype(BF)
            ready[k, :, :, part] = value.reshape(n_shard, slots, tile)

    place = by_core(s, n_shard) if paired else s
    cot_waits = []
    for k in range(groups):
        for i, peer in enumerate(others):
            item = push(ready.at[k, peer], cot_rows.at[k, place], ss_x.at[k, i], rs_x.at[k, i], shard=peer)
            item.start()
            cot_waits.append(item)
        item = pltpu.make_async_copy(ready.at[k, s], cot_rows.at[k, place], local.at[6 + k])
        item.start()
        cot_waits.append(item)

    for item in waits + w_waits:
        item.wait()
    copies[0].wait()
    copies[1].wait()
    copies[3].wait()
    own_head.wait()
    outs = [
        pltpu.make_async_copy(rows_all, rows_out, out_sem.at[0]),
        pltpu.make_async_copy(w_all, w_all_out, out_sem.at[1]),
    ]
    outs[0].start()
    outs[1].start()

    right = w_all[:, :, pl.ds(cols, HEAD_DIM)].reshape(width, HEAD_DIM)

    @pl.loop(0, n_shard)
    def _(b):
        pre = jnp.dot(rows_all[b], right, preferred_element_type=F32)
        kvpre[b] = pre
        keyed, unused = unit_rows(pre)
        keyed = turn(keyed * k_gain[...], cosine[...], sine[...])
        kv[parity, b, c] = jnp.where(parity == 0, keyed, pre).astype(BF)

    fan = Fan(n_ctx, c, lambda d: kv.at[parity, :, flip_bits(c, d)], ss_kz, rs_kz, False)
    fan.send(0, kv.at[parity, :, c])
    kv_waits = []
    item = push(kv.at[parity, :, c], kv.at[parity, :, c], ss_kf.at[0], rs_kf.at[0], shard=sibling)
    item.start()
    kv_waits.append(item)

    @pl.loop(0, n_shard // 2)
    def _(b):
        left = rows_all[pl.ds(b * 2, 2)].reshape(2 * count, width)
        pre = jnp.dot(left, w_all[:, :, pl.ds(0, cols)].reshape(width, cols), preferred_element_type=F32)
        qpre[pl.ds(b * 2, 2)] = pre.reshape(2, count, cols)
        for i in range(2):
            for h in range(heads):
                part = pre[i * count : (i + 1) * count, h * HEAD_DIM : (h + 1) * HEAD_DIM]
                unit, unused = unit_rows(part)
                q[b * 2 + i, :, h * HEAD_DIM : (h + 1) * HEAD_DIM] = turn(
                    unit * q_gain[...], cosine[...], sine[...]
                ).astype(BF)

    for d in fan.order():
        fan.arrival(d)
        block = kv.at[parity, :, flip_bits(c, d)]
        item = push(block, block, ss_kf.at[d], rs_kf.at[d], shard=sibling)
        item.start()
        kv_waits.append(item)
    outs += [pltpu.make_async_copy(qpre, qpre_out, out_sem.at[2]), pltpu.make_async_copy(q, q_out, out_sem.at[3])]
    outs[2].start()
    outs[3].start()
    for item in kv_waits:
        item.wait()
    fan.drain()
    outs.append(pltpu.make_async_copy(kv, kv_out, out_sem.at[4]))
    outs[4].start()

    near, far = {}, {}
    order = list(range(1, chips)) + [0]

    def product(at):
        d = order[at]
        first_seq = 2 * lax.rem(chip + d, chips)

        @pl.loop(0, 2)
        def _(i):
            b = first_seq + i
            k_all = kv[0, b].reshape(keys, HEAD_DIM)
            v_all = kv[1, b].reshape(keys, HEAD_DIM)
            for h in range(heads):
                hs = slice(h * HEAD_DIM, (h + 1) * HEAD_DIM)
                scores = lax.dot_general(q[b, :, hs], k_all, (((1,), (1,)), ((), ())), preferred_element_type=F32)
                scores = scores * (HEAD_DIM ** -0.5) + bias[...]
                raised = jnp.exp(scores - jnp.max(scores, axis=-1, keepdims=True))
                probs = raised / jnp.sum(raised, axis=-1, keepdims=True)
                attn[b, :, hs] = jnp.dot(probs.astype(BF), v_all, preferred_element_type=F32).astype(BF)

        left = attn[pl.ds(first_seq, 2)].reshape(2 * count, cols)

        @pl.loop(0, width // tile)
        def _(j):
            part = pl.ds(pl.multiple_of(j * tile, tile), tile)
            value = jnp.dot(left, w_out[:, part], preferred_element_type=F32)
            pair[...] = value.reshape(2, count, tile)
            own_part[at % 2, :, part] = pair[parity]
            to_sib[at, :, part] = pair[1 - parity].astype(BF)

        near[at] = push(to_sib.at[at], sib.at[at], ss_s.at[at], rs_s.at[at], shard=sibling)
        near[at].start()

    def chip_sum(at):
        near[at].wait()
        to_chip[at] = (own_part[at % 2] + sib[at].astype(F32)).astype(BF)
        far[at] = push(to_chip.at[at], got.at[at], ss_c.at[at], rs_c.at[at], shard=mates[order[at] - 1])
        far[at].start()

    for at in range(chips):
        product(at)
        if at:
            chip_sum(at - 1)
    outs.append(pltpu.make_async_copy(attn, attn_out, out_sem.at[5]))
    outs[5].start()
    near[chips - 1].wait()
    mid[...] = tokens[...].astype(F32) + own_part[(chips - 1) % 2] + sib[chips - 1].astype(F32)
    for at in range(chips - 1):
        far[at].wait()
        mid[...] += got[at].astype(F32)
    cot_fan.drain()
    route_fan.drain()
    for item in cot_waits + outs:
        item.wait()


def front(n_ctx, n_shard, group, capacity, kv_heads, paired, args, ident):
    tokens, gain, w_query, key_w, value_w, routes, router, cot = args[:8]
    n, z = n_shard, n_ctx
    count, width = tokens.shape
    wr, chips, groups, slots = w_query.shape[0], n_shard // 2, n_ctx // group, group * capacity
    cols = w_query.shape[1] // n
    heads = cols // HEAD_DIM
    sds = jax.ShapeDtypeStruct
    dma = lambda *shape: DMA(shape)
    return call(
        functools.partial(front_body, z, n, group, capacity, heads, kv_heads, paired, 512),
        [
            sds((n, count, width), BF), sds((n, wr, cols + HEAD_DIM), BF), sds((router.shape[0], width), BF),
            sds((groups, n, group * count), F32), sds((groups, n, slots, width), BF), sds((n, count, cols), F32),
            sds((n, count, HEAD_DIM), F32), sds((n, count, cols), BF), sds((2, n, z, count, HEAD_DIM), BF),
            sds((n, count, cols), BF), sds((count, width), F32),
        ],
        [VMEM, VMEM, ANY, ANY, ANY, VMEM, ANY, ANY] + [VMEM] * 6,
        [
            pltpu.VMEM((count, width), BF), pltpu.VMEM((n, count, width), BF), pltpu.VMEM((n, wr, cols + HEAD_DIM), BF),
            pltpu.VMEM((z,) + routes.shape, jnp.int32), pltpu.VMEM((z, count, width), BF),
            pltpu.VMEM((groups, n, slots, width), BF), pltpu.VMEM((n, count, cols), F32),
            pltpu.VMEM((n, count, cols), BF), pltpu.VMEM((2, n, z, count, HEAD_DIM), BF),
            pltpu.VMEM((n, count, cols), BF), pltpu.VMEM((2, count, width), F32), pltpu.VMEM((2, count, 512), F32),
            pltpu.VMEM((chips, count, width), BF), pltpu.VMEM((chips, count, width), BF),
            pltpu.VMEM((chips - 1, count, width), BF), pltpu.VMEM((chips - 1, count, width), BF),
            dma(6 + groups), dma(chips), dma(chips), dma(chips), dma(chips), dma(n - 1), dma(n - 1), dma(n - 1), dma(n - 1),
            dma(n - 1), dma(n - 1), dma(z), dma(z), dma(z), dma(z), dma(groups, n - 1), dma(groups, n - 1),
            dma(z), dma(z), dma(z), dma(z), dma(chips), dma(chips), dma(chips - 1), dma(chips - 1), dma(6),
        ],
        ident, args, mib=60,
        out_specs=[ANY, ANY, ANY, VMEM, ANY, ANY, VMEM, ANY, ANY, ANY, VMEM],
    )


def spread_body(n_shard, rows, rows_all, local, ss_row, rs_row, ss_fwd, rs_fwd):
    c, s, parity, sibling, others, layers = here(1, n_shard)
    chips = n_shard // 2
    mates = [lax.rem(s + 2 * d, n_shard) for d in range(1, chips)]
    greet(mates + [sibling], [])
    mine = pltpu.make_async_copy(rows, rows_all.at[s], local)
    mine.start()
    first, waits = [], []
    for d in range(1, chips):
        item = push(rows, rows_all.at[s], ss_row.at[d], rs_row.at[d], shard=mates[d - 1])
        item.start()
        first.append(item)
    item = push(rows, rows_all.at[s], ss_fwd.at[0], rs_fwd.at[0], shard=sibling)
    item.start()
    waits.append(item)
    for d in range(1, chips):
        first[d - 1].wait()
        origin = lax.rem(s + n_shard - 2 * d, n_shard)
        item = push(rows_all.at[origin], rows_all.at[origin], ss_fwd.at[d], rs_fwd.at[d], shard=sibling)
        item.start()
        waits.append(item)
    mine.wait()
    for item in waits:
        item.wait()


def spread(n_shard, rows, ident):
    return call(
        functools.partial(spread_body, n_shard),
        [jax.ShapeDtypeStruct((n_shard,) + rows.shape, rows.dtype)],
        [ANY], [DMA] + [DMA((n_shard // 2,))] * 4, ident, (rows,),
    )[0]


def key_back_body(n_ctx, n_shard, parts, out, sib, zsend, zrecv, ss_s, rs_s, ss_z, rs_z):
    c, s, parity, sibling, others, layers = here(n_ctx, n_shard)
    greet([sibling], layers)
    order = list(range(1, n_ctx)) + [0]
    near = {}
    for d in order:
        block = parts.at[1 - parity, :, lax.rem(c + d, n_ctx)]
        near[d] = push(block, sib.at[d], ss_s.at[d], rs_s.at[d], shard=sibling)
        near[d].start()
    far = {}
    for d in order:
        near[d].wait()
        layer = lax.rem(c + d, n_ctx)
        value = parts[parity, :, layer].astype(F32) + sib[d].astype(F32)
        if d:
            zsend[d - 1] = value.astype(BF)
            far[d] = push(zsend.at[d - 1], zrecv.at[d - 1], ss_z.at[d], rs_z.at[d], ctx=layer)
            far[d].start()
    for d in range(1, n_ctx):
        far[d].wait()
        value = value + zrecv[d - 1].astype(F32)
    out[...] = value


def key_back(n_ctx, n_shard, parts, ident):
    block = (parts.shape[1], parts.shape[3], parts.shape[4])
    return call(
        functools.partial(key_back_body, n_ctx, n_shard),
        [jax.ShapeDtypeStruct(block, F32)],
        [VMEM],
        [
            pltpu.VMEM((n_ctx,) + block, BF), pltpu.VMEM((n_ctx - 1,) + block, BF),
            pltpu.VMEM((n_ctx - 1,) + block, BF),
        ] + [DMA((n_ctx,))] * 4,
        ident, (parts,), out_specs=[VMEM],
    )[0]


def finish_body(n_ctx, n_shard, q_cols, tile,
                weights, wide, router, gains, left, right, tokens, gain,
                q_out, kv_out, wide_out, router_out, gains_out, rows_out,
                wide_landing, wide_acc, wide_total, ss_wi, rs_wi, ss_wo, ss_wc, pieces, landing, acc, total, router_in, router_mid, router_far,
                gains_own, gains_in, gains_mid, gains_far, pair, own_part, to_sib, sib, to_chip, got,
                local, ss_w, rs_w, ss_i, rs_i, ss_o, ss_q, ss_k, ss_r, rs_r, ss_g, rs_g, ss_h, rs_h,
                ss_t, rs_t, ss_s, rs_s, ss_c, rs_c):
    c, s, parity, sibling, others, layers = here(n_ctx, n_shard)
    half = n_ctx // 2
    chips = n_shard // 2
    chip = lax.div(s, 2)
    mates = [lax.rem(s + 2 * d, n_shard) for d in range(1, chips)]
    left_side = c < half
    depth = jnp.where(left_side, c, n_ctx - 1 - c)
    inner = jnp.where(left_side, c + 1, c - 1)
    outer = jnp.clip(jnp.where(left_side, c - 1, c + 1), 0, n_ctx - 1)
    middle = depth == half - 1
    inside = depth > 0
    rows, width = rows_out.shape
    greet(others, layers)
    sends, small = [None], []
    for i, peer in enumerate(others):
        item = push(weights.at[peer], pieces.at[i + 1], ss_w.at[i], rs_w.at[i], shard=peer)
        item.start()
        sends.append(item)
    for i, peer in enumerate(others):
        item = push(router.at[peer], router_in.at[i], ss_r.at[i], rs_r.at[i], shard=peer)
        item.start()
        small.append(item)

    def out_copies(j, ref):
        source = lax.rem(s + n_shard - j, n_shard)
        cols = pl.ds(pl.multiple_of(source * q_cols, q_cols), q_cols)
        return (
            pltpu.make_async_copy(ref.at[:, pl.ds(0, q_cols)], q_out.at[:, cols], ss_q.at[j]),
            pltpu.make_async_copy(ref.at[:, pl.ds(q_cols, 128)], kv_out.at[source], ss_k.at[j]),
        )

    def wide_copies(j, ref):
        return (pltpu.make_async_copy(ref, wide_out.at[j], ss_wc.at[j]),)

    class Line:
        def __init__(self, ready, own, acc, landing, total, ss_i, rs_i, ss_o, copies):
            self.ready, self.own, self.acc, self.landing, self.total = ready, own, acc, landing, total
            self.ss_i, self.rs_i, self.ss_o, self.copies = ss_i, rs_i, ss_o, copies

        def inward(self, j, ref):
            at = jnp.where(middle, 1, 0)
            return push(ref, self.landing.at[at, j], self.ss_i.at[j], self.rs_i.at[at, j], ctx=inner)

        def outward(self, j):
            return push(self.total.at[j], self.landing.at[1, j], self.ss_o.at[j], self.rs_i.at[1, j], ctx=outer)

        def arrived(self, which, j):
            push(self.acc.at[j], self.landing.at[which, j], self.ss_i.at[j], self.rs_i.at[which, j],
                 ctx=inner).wait_recv()

        def outermost(self, j):
            @pl.when(jnp.logical_not(inside))
            def _():
                self.ready(j)
                self.inward(j, self.own(j)).start()

        def first_half(self, j):
            @pl.when(inside)
            def _():
                self.ready(j)
                self.arrived(0, j)
                self.acc[j] = (self.own(j)[...].astype(F32) + self.landing[0, j].astype(F32)).astype(BF)
                self.inward(j, self.acc.at[j]).start()

        def second_half(self, j):
            self.arrived(1, j)

            @pl.when(middle)
            def _():
                self.total[j] = (self.acc[j].astype(F32) + self.landing[1, j].astype(F32)).astype(BF)

            @pl.when(jnp.logical_not(middle))
            def _():
                self.total[j] = self.landing[1, j]

            @pl.when(inside)
            def _():
                self.outward(j).start()

            for item in self.copies(j, self.total.at[j]):
                item.start()

        def drain(self, j):
            self.inward(j, self.acc.at[j]).wait_send()

            @pl.when(inside)
            def _():
                self.outward(j).wait_send()

            for item in self.copies(j, self.total.at[j]):
                item.wait()

    line = Line(lambda j: sends[j].wait() if j else None, lambda j: pieces.at[j] if j else weights.at[s],
                acc, landing, total, ss_i, rs_i, ss_o, out_copies)
    wide_line = Line(lambda j: None, lambda j: wide.at[j], wide_acc, wide_landing, wide_total,
                     ss_wi, rs_wi, ss_wo, wide_copies)
    wides = wide.shape[0]
    steps = [(wide_line, j) for j in range(wides)] + [(line, j) for j in range(n_shard)]

    near, far = {}, {}

    def product(d):
        first = pl.multiple_of(lax.rem(chip + d, chips) * (2 * rows), 2 * rows)

        @pl.loop(0, width // tile)
        def _(j):
            cols = pl.ds(pl.multiple_of(j * tile, tile), tile)
            value = lax.dot_general(left[pl.ds(first, 2 * rows), :], right[cols, :],
                                    (((1,), (1,)), ((), ())), preferred_element_type=F32)
            pair[...] = value.reshape(2, rows, tile)
            own_part[d, :, cols] = pair[parity]
            to_sib[d, :, cols] = pair[1 - parity].astype(BF)

        near[d] = push(to_sib.at[d], sib.at[d], ss_s.at[d], rs_s.at[d], shard=sibling)
        near[d].start()

    def chip_sum(d):
        near[d].wait()
        to_chip[d - 1] = (own_part[d] + sib[d].astype(F32)).astype(BF)
        far[d] = push(to_chip.at[d - 1], got.at[d - 1], ss_c.at[d - 1], rs_c.at[d - 1], shard=mates[d - 1])
        far[d].start()

    gain_sends = []

    def last_sum():
        near[0].wait()
        grad = own_part[0] + sib[0].astype(F32)
        for d in range(1, chips):
            far[d].wait()
            grad = grad + got[d - 1].astype(F32)
        x = tokens[...].astype(F32)
        scale = lax.rsqrt(jnp.mean(x * x, axis=-1, keepdims=True) + epsilon)
        unit = x * scale
        scaled = grad * gain[...]
        rows_out[...] = scale * (scaled - unit * jnp.mean(scaled * unit, axis=-1, keepdims=True))
        gains_own[...] = gains[...]
        gains_own[0:1] = jnp.sum(grad * unit, axis=0, keepdims=True)
        mine = pltpu.make_async_copy(gains_own, gains_in.at[s], local.at[0])
        mine.start()
        gain_sends.append(mine)
        for i, peer in enumerate(others):
            item = push(gains_own, gains_in.at[s], ss_g.at[i], rs_g.at[i], shard=peer)
            item.start()
            gain_sends.append(item)

    def small_plane():
        for item in small + gain_sends:
            item.wait()
        gains_mid[...] = gains_in[0]
        for i in range(1, n_shard):
            gains_mid[...] += gains_in[i]
        router_mid[...] = router[s].astype(F32)
        for i in range(n_shard - 1):
            router_mid[...] += router_in[i].astype(F32)
        for i, layer in enumerate(layers):
            push(gains_mid, gains_far.at[c], ss_h.at[i], rs_h.at[i], ctx=layer).start()
            push(router_mid, router_far.at[c], ss_t.at[i], rs_t.at[i], ctx=layer).start()
        pltpu.make_async_copy(gains_mid, gains_far.at[c], local.at[1]).start()
        pltpu.make_async_copy(router_mid, router_far.at[c], local.at[2]).start()

    def small_all():
        pltpu.make_async_copy(gains_mid, gains_far.at[c], local.at[1]).wait()
        pltpu.make_async_copy(router_mid, router_far.at[c], local.at[2]).wait()
        for i, layer in enumerate(layers):
            push(gains_mid, gains_far.at[c], ss_h.at[i], rs_h.at[i], ctx=layer).wait()
            push(router_mid, router_far.at[c], ss_t.at[i], rs_t.at[i], ctx=layer).wait()
        gains_out[...] = gains_far[0]
        router_out[...] = router_far[0]
        for i in range(1, n_ctx):
            gains_out[...] += gains_far[i]
            router_out[...] += router_far[i]

    lag, ahead = 2, 6
    for which, j in steps[:ahead]:
        which.outermost(j)
    for d in list(range(1, chips)) + [0]:
        product(d)
    side = [functools.partial(chip_sum, d) for d in range(1, chips)] + [last_sum, small_plane]
    for n in range(len(steps) + lag):
        if n + ahead < len(steps):
            steps[n + ahead][0].outermost(steps[n + ahead][1])
        if n < len(steps):
            steps[n][0].first_half(steps[n][1])
        if n >= lag:
            steps[n - lag][0].second_half(steps[n - lag][1])
        if n >= 2 and side:
            side.pop(0)()
    for job in side:
        job()
    small_all()
    for which, j in steps:
        which.drain(j)


def finish(n_ctx, n_shard, q_cols, weights, wide, router, gains, left, right, tokens, gain, ident):
    n, rows, cols = weights.shape
    router_shape = router.shape[1:]
    count, width = tokens.shape
    chips = n // 2
    tile = 512
    wides = wide.shape[0]
    return call(
        functools.partial(finish_body, n_ctx, n, q_cols, tile),
        [
            jax.ShapeDtypeStruct((rows, n * q_cols), BF), jax.ShapeDtypeStruct((n, rows, 128), BF),
            jax.ShapeDtypeStruct(wide.shape, BF),
            jax.ShapeDtypeStruct(router_shape, F32), jax.ShapeDtypeStruct(gains.shape, F32),
            jax.ShapeDtypeStruct((count, width), F32),
        ],
        [VMEM] * 8,
        [
            pltpu.VMEM((2,) + wide.shape, BF), pltpu.VMEM(wide.shape, BF), pltpu.VMEM(wide.shape, BF),
            DMA((wides,)), DMA((2, wides)), DMA((wides,)), DMA((wides,)),
            pltpu.VMEM((n, rows, cols), BF), pltpu.VMEM((2, n, rows, cols), BF),
            pltpu.VMEM((n, rows, cols), BF), pltpu.VMEM((n, rows, cols), BF),
            pltpu.VMEM((n - 1,) + router_shape, BF), pltpu.VMEM(router_shape, F32),
            pltpu.VMEM((n_ctx,) + router_shape, F32),
            pltpu.VMEM(gains.shape, F32), pltpu.VMEM((n,) + gains.shape, F32),
            pltpu.VMEM(gains.shape, F32), pltpu.VMEM((n_ctx,) + gains.shape, F32),
            pltpu.VMEM((2, count, tile), F32), pltpu.VMEM((chips, count, width), F32),
            pltpu.VMEM((chips, count, width), BF), pltpu.VMEM((chips, count, width), BF),
            pltpu.VMEM((chips - 1, count, width), BF), pltpu.VMEM((chips - 1, count, width), BF),
            DMA((3,)), DMA((n - 1,)), DMA((n - 1,)), DMA((n,)), DMA((2, n)), DMA((n,)),
            DMA((n,)), DMA((n,)), DMA((n - 1,)), DMA((n - 1,)), DMA((n - 1,)), DMA((n - 1,)),
            DMA((n_ctx - 1,)), DMA((n_ctx - 1,)), DMA((n_ctx - 1,)), DMA((n_ctx - 1,)),
            DMA((chips,)), DMA((chips,)), DMA((chips - 1,)), DMA((chips - 1,)),
        ],
        ident, (weights, wide, router, gains, left, right, tokens, gain), mib=60,
        out_specs=[ANY, ANY, ANY, VMEM, VMEM, VMEM],
    )


def back_body(n_ctx, n_shard, group, heads, wides,
              grad_out, q_in, kv_in, attn_in, qpre_in, kvpre_in, w_out_in, rows_in, w_all_in, cosine, sine, bias, q_gain, k_gain,
              tokens, gain, gains, router, mix_near, mix_part, code,
              q_out, kv_out, wide_out, router_out, gains_out, rows_out, mix_out, mix_land,
              q, kv, attn, qpre, kvpre, w_out, w_all, loads, grads, attn_t, grad_heads, ds_all, p_all, parts, pre, q_sum, k_sum, wide, weights,
              sibk, zsend, zrecv, wide_landing, pieces, landing,
              own_part, pair, to_sib, sib, to_chip, got, router_in, router_mid, router_far,
              gains_own, gains_in, gains_mid, gains_far, mix_rows, mix_sent, mix_recv, local,
              ss_row, rs_row, ss_fwd, rs_fwd, ss_sk, rs_sk, ss_zk, rs_zk,
              ss_wi, rs_wi, ss_wo, ss_wc, ss_w, rs_w, ss_i, rs_i, ss_o, ss_q, ss_k,
              ss_r, rs_r, ss_g, rs_g, ss_h, rs_h, ss_t, rs_t, ss_s, rs_s, ss_c, rs_c, ss_m, rs_m, ss_f, rs_f, ss_v, rs_v):
    c, s, parity, sibling, others, layers = here(n_ctx, n_shard)
    half = n_ctx // 2
    chips = n_shard // 2
    chip = lax.div(s, 2)
    mates = [lax.rem(s + 2 * d, n_shard) for d in range(1, chips)]
    left_side = c < half
    depth = jnp.where(left_side, c, n_ctx - 1 - c)
    inner = jnp.where(left_side, c + 1, c - 1)
    outer = jnp.clip(jnp.where(left_side, c - 1, c + 1), 0, n_ctx - 1)
    middle = depth == half - 1
    inside = depth > 0
    count, width = tokens.shape
    wr = w_all.shape[1]
    cols = heads * HEAD_DIM
    keys = n_ctx * count
    scaling = HEAD_DIM ** -0.5
    own_copies = [
        pltpu.make_async_copy(grad_out, grads.at[s], local.at[0]),
        pltpu.make_async_copy(rows_in, grads, local.at[1]),
    ]
    own_copies[0].start()
    load = [
        pltpu.make_async_copy(a, b, loads.at[n])
        for n, (a, b) in enumerate(((q_in, q), (kv_in, kv), (w_out_in, w_out), (qpre_in, qpre), (attn_in, attn),
                                    (kvpre_in, kvpre), (w_all_in, w_all)))
    ]
    greet(others, layers)

    first, forwards = {}, {}
    for d in range(1, chips):
        first[d] = push(grad_out, grads.at[s], ss_row.at[d], rs_row.at[d], shard=mates[d - 1])
        first[d].start()
    forwards[0] = push(grad_out, grads.at[s], ss_fwd.at[0], rs_fwd.at[0], shard=sibling)
    forwards[0].start()
    for item in load:
        item.start()
    small = []
    for i, peer in enumerate(others):
        item = push(router.at[peer], router_in.at[i], ss_r.at[i], rs_r.at[i], shard=peer)
        item.start()
        small.append(item)
    q_sum[...] = jnp.zeros_like(q_sum)
    k_sum[...] = jnp.zeros_like(k_sum)

    def norm_back(grad, value, norm_gain, total):
        unit, scale = unit_rows(value)
        grad = grad * cosine[...] + pltpu.roll(grad * sine[...], HEAD_DIM // 2, 1)
        total[...] += jnp.sum(grad * unit, axis=0, keepdims=True)
        scaled = grad * norm_gain[...]
        return scale * (scaled - unit * jnp.mean(scaled * unit, axis=-1, keepdims=True))

    slots = mix_near.shape[1]
    mix_fold = Fold(c, mix_sent, mix_recv, ss_f, rs_f)
    tile = mix_rows.shape[2]

    def mix_sums(k, ref):
        table = slot_table(code[flip_bits(lax.div(c, group), k)], slots).T

        @pl.loop(0, width // tile)
        def _(j):
            part = pl.ds(pl.multiple_of(j * tile, tile), tile)
            item = pltpu.make_async_copy(ref.at[:, :, part], mix_rows, local.at[5])
            item.start()
            item.wait()
            value = jnp.dot(table, mix_rows[...].reshape(n_shard * slots, tile), preferred_element_type=F32)
            own_part[:, :, part] = value.reshape(2, count, tile)

    def near_part(d):
        return own_part[lax.rem(flip_bits(c, d), group)]

    def mix_send():
        for i, peer in enumerate(others):
            push(mix_near.at[by_core(peer, n_shard)], mix_land.at[s], ss_m.at[i], rs_m.at[i], shard=peer).start()
        pltpu.make_async_copy(mix_near.at[by_core(s, n_shard)], mix_land.at[s], local.at[6]).start()

    def mix_last():
        for i, peer in enumerate(others):
            push(mix_near.at[by_core(peer, n_shard)], mix_land.at[s], ss_m.at[i], rs_m.at[i], shard=peer).wait()
        pltpu.make_async_copy(mix_near.at[by_core(s, n_shard)], mix_land.at[s], local.at[6]).wait()
        mix_sums(0, mix_land)
        mix_fold.give(1, near_part(1))
        mix_out[...] = near_part(0)

    mix_fold.give_as_is(3, mix_part.at[1])
    near, far = {}, {}

    def seqs_of(d):
        return 2 * lax.rem(chip + chips - d, chips)

    def attention_back(d):
        fs = seqs_of(d)
        grad = lax.dot_general(grads[pl.ds(fs, 2)].reshape(2 * count, width), w_out[...],
                               (((1,), (1,)), ((), ())), preferred_element_type=F32)
        grad_heads[...] = grad.reshape(2, count, cols).astype(BF)

        @pl.loop(0, 2)
        def _(i):
            b = fs + i
            k_all = kv[0, b].reshape(keys, HEAD_DIM)
            v_all = kv[1, b].reshape(keys, HEAD_DIM)
            for h in range(heads):
                hs = slice(h * HEAD_DIM, (h + 1) * HEAD_DIM)
                rs = slice(h * count, (h + 1) * count)
                scores = lax.dot_general(q[b, :, hs], k_all, (((1,), (1,)), ((), ())), preferred_element_type=F32)
                scores = scores * scaling + bias[...]
                raised = jnp.exp(scores - jnp.max(scores, axis=-1, keepdims=True))
                probs = raised / jnp.sum(raised, axis=-1, keepdims=True)
                grad_p = lax.dot_general(grad_heads[i, :, hs], v_all, (((1,), (1,)), ((), ())),
                                         preferred_element_type=F32)
                delta = jnp.sum(probs * grad_p, axis=-1, keepdims=True)
                ds = (probs * (grad_p - delta)).astype(BF)
                ds_all[rs, :] = ds
                p_all[rs, :] = probs.astype(BF)
                grad_q = jnp.dot(ds, k_all, preferred_element_type=F32) * scaling
                pre[b, :, hs] = norm_back(grad_q, qpre[b, :, hs], q_gain, q_sum).astype(BF)
            grad_k, grad_v = jnp.zeros((keys, HEAD_DIM), F32), jnp.zeros((keys, HEAD_DIM), F32)
            stacked_q = jnp.concatenate([q[b, :, h * HEAD_DIM : (h + 1) * HEAD_DIM] for h in range(heads)], axis=0)
            stacked_g = jnp.concatenate(
                [grad_heads[i, :, h * HEAD_DIM : (h + 1) * HEAD_DIM] for h in range(heads)], axis=0
            )
            grad_k = lax.dot_general(ds_all[...], stacked_q, (((0,), (0,)), ((), ())), preferred_element_type=F32)
            grad_v = lax.dot_general(p_all[...], stacked_g, (((0,), (0,)), ((), ())), preferred_element_type=F32)
            parts[0, b] = (grad_k * scaling).astype(BF).reshape(n_ctx, count, HEAD_DIM)
            parts[1, b] = grad_v.astype(BF).reshape(n_ctx, count, HEAD_DIM)

        near[d] = push(parts.at[1 - parity, pl.ds(fs, 2)], sibk.at[d], ss_sk.at[d], rs_sk.at[d], shard=sibling)
        near[d].start()

    def key_sum(d):
        fs = seqs_of(d)
        near[d].wait()
        for i, layer in enumerate(layers):
            zsend[d, i] = (
                parts[parity, pl.ds(fs, 2), layer].astype(F32) + sibk[d, :, layer].astype(F32)
            ).astype(BF)
            far[d, i] = push(zsend.at[d, i], zrecv.at[d, i], ss_zk.at[d, i], rs_zk.at[d, i], ctx=layer)
            far[d, i].start()

    def half_rows(j):
        return pl.ds((j % 2) * (wr // 2), wr // 2)

    def out_copies(j, ref):
        source = lax.rem(s + n_shard - j // 2, n_shard)
        to = pl.ds(pl.multiple_of(source * cols, cols), cols)
        return (
            pltpu.make_async_copy(ref.at[:, pl.ds(0, cols)], q_out.at[half_rows(j), to], ss_q.at[j]),
            pltpu.make_async_copy(ref.at[:, pl.ds(cols, HEAD_DIM)], kv_out.at[source, half_rows(j)], ss_k.at[j]),
        )

    def wide_copies(j, ref):
        step = wide.shape[2]
        return (pltpu.make_async_copy(ref, wide_out.at[:, pl.ds(j * step, step)], ss_wc.at[j]),)

    class Line:
        def __init__(self, ready, own, landing, ss_i, rs_i, ss_o, copies):
            self.ready, self.own, self.landing = ready, own, landing
            self.ss_i, self.rs_i, self.ss_o, self.copies = ss_i, rs_i, ss_o, copies

        def inward(self, j, ref):
            at = jnp.where(middle, 1, 0)
            return push(ref, self.landing.at[at, j], self.ss_i.at[j], self.rs_i.at[at, j], ctx=inner)

        def outward(self, j):
            return push(self.landing.at[1, j], self.landing.at[1, j], self.ss_o.at[j], self.rs_i.at[1, j], ctx=outer)

        def arrived(self, which, j):
            push(self.landing.at[0, j], self.landing.at[which, j], self.ss_i.at[j], self.rs_i.at[which, j],
                 ctx=inner).wait_recv()

        def outermost(self, j):
            @pl.when(jnp.logical_not(inside))
            def _():
                self.ready(j)
                self.inward(j, self.own(j)).start()

        def first_half(self, j):
            @pl.when(inside)
            def _():
                self.ready(j)
                self.arrived(0, j)
                self.landing[0, j] = (self.own(j)[...].astype(F32) + self.landing[0, j].astype(F32)).astype(BF)
                self.inward(j, self.landing.at[0, j]).start()

        def second_half(self, j):
            self.arrived(1, j)

            @pl.when(middle)
            def _():
                self.landing[1, j] = (self.landing[0, j].astype(F32) + self.landing[1, j].astype(F32)).astype(BF)

            @pl.when(inside)
            def _():
                self.outward(j).start()

            for item in self.copies(j, self.landing.at[1, j]):
                item.start()

        def drain(self, j):
            self.inward(j, self.landing.at[0, j]).wait_send()

            @pl.when(inside)
            def _():
                self.outward(j).wait_send()

            for item in self.copies(j, self.landing.at[1, j]):
                item.wait()

    sends = [[] for j in range(n_shard)]
    line = Line(lambda j: [item.wait() for item in sends[j // 2]] if j % 2 == 0 else None,
                lambda j: pieces.at[j // 2, half_rows(j)] if j >= 2 else weights.at[s, half_rows(j)],
                landing, ss_i, rs_i, ss_o, out_copies)
    wide_line = Line(lambda j: None, lambda j: wide.at[j], wide_landing, ss_wi, rs_wi, ss_wo, wide_copies)
    steps = [(wide_line, j) for j in range(wides)] + [(line, j) for j in range(2 * n_shard)]
    lag, ahead = 2, 6

    def advance(n):
        if n + ahead < len(steps):
            steps[n + ahead][0].outermost(steps[n + ahead][1])
        if n < len(steps):
            steps[n][0].first_half(steps[n][1])
        if n >= lag:
            steps[n - lag][0].second_half(steps[n - lag][1])

    step = width // wides
    for item in load[:4]:
        item.wait()
    for d in range(chips):
        if d:
            first[d].wait()
            origin = lax.rem(s + n_shard - 2 * d, n_shard)
            forwards[d] = push(grads.at[origin], grads.at[origin], ss_fwd.at[d], rs_fwd.at[d], shard=sibling)
            forwards[d].start()
        else:
            own_copies[0].wait()
        forwards[d].wait()
        if d + 1 == chips:
            mix_send()
            for item in load[4:]:
                item.wait()
            attn_t[...] = attn[...].reshape(n_shard * count, cols).T
            for j in range(wides):
                block = grads[:, :, j * step : (j + 1) * step].reshape(n_shard * count, step)
                wide[j] = jnp.dot(attn_t[...], block, preferred_element_type=F32).astype(BF)
                if j < ahead:
                    wide_line.outermost(j)
        attention_back(d)
        if d == 0:
            mix_fold.give(2, mix_fold.take(2, mix_part[0].astype(F32)))
        if d:
            key_sum(d - 1)

    rows_all = grads
    own_copies[1].start()
    key_sum(chips - 1)
    advance(0)
    own_copies[1].wait()

    @pl.loop(0, n_shard)
    def _(e):
        block = rows_all[:, :, pl.ds(pl.multiple_of(e * wr, wr), wr)].reshape(n_shard * count, wr)
        right = pre[:, :, pl.ds(0, cols)].reshape(n_shard * count, cols)
        weights[e, :, pl.ds(0, cols)] = lax.dot_general(
            block, right, (((0,), (0,)), ((), ())), preferred_element_type=F32).astype(BF)

    for i, peer in enumerate(others):
        item = push(weights.at[peer, :, pl.ds(0, cols)], pieces.at[i + 1, :, pl.ds(0, cols)],
                    ss_w.at[i], rs_w.at[i], shard=peer)
        item.start()
        sends[i + 1].append(item)
    advance(1)
    for d in range(chips):
        fs = seqs_of(d)
        total = parts[parity, pl.ds(fs, 2), c].astype(F32) + sibk[d, :, c].astype(F32)
        for i in range(n_ctx - 1):
            far[d, i].wait()
            total = total + zrecv[d, i].astype(F32)
        for i in range(2):
            keyed = norm_back(total[i], kvpre[fs + i], k_gain, k_sum)
            pre[fs + i, :, pl.ds(cols, HEAD_DIM)] = jnp.where(parity == 0, keyed, total[i]).astype(BF)

    @pl.loop(0, n_shard)
    def _(e):
        block = rows_all[:, :, pl.ds(pl.multiple_of(e * wr, wr), wr)].reshape(n_shard * count, wr)
        right = pre[:, :, pl.ds(cols, HEAD_DIM)].reshape(n_shard * count, HEAD_DIM)
        weights[e, :, pl.ds(cols, HEAD_DIM)] = lax.dot_general(
            block, right, (((0,), (0,)), ((), ())), preferred_element_type=F32).astype(BF)

    for i, peer in enumerate(others):
        item = push(weights.at[peer, :, pl.ds(cols, HEAD_DIM)], pieces.at[i + 1, :, pl.ds(cols, HEAD_DIM)],
                    ss_v.at[i], rs_v.at[i], shard=peer)
        item.start()
        sends[i + 1].append(item)
    advance(2)

    order = list(range(1, chips)) + [0]
    to_sibling, to_mate = {}, {}

    def product(at):
        fs = 2 * lax.rem(chip + order[at], chips)
        left = pre[pl.ds(fs, 2)].reshape(2 * count, cols + HEAD_DIM)

        @pl.loop(0, n_shard)
        def _(j):
            part = pl.ds(pl.multiple_of(j * wr, wr), wr)
            value = lax.dot_general(left, w_all[j], (((1,), (1,)), ((), ())), preferred_element_type=F32)
            pair[...] = value.reshape(2, count, wr)
            own_part[at % 2, :, part] = pair[parity]
            to_sib[at, :, part] = pair[1 - parity].astype(BF)

        to_sibling[at] = push(to_sib.at[at], sib.at[at], ss_s.at[at], rs_s.at[at], shard=sibling)
        to_sibling[at].start()

    def chip_sum(at):
        to_sibling[at].wait()
        to_chip[at] = (own_part[at % 2] + sib[at].astype(F32)).astype(BF)
        to_mate[at] = push(to_chip.at[at], got.at[at], ss_c.at[at], rs_c.at[at], shard=mates[order[at] - 1])
        to_mate[at].start()

    gain_sends = []

    def last_sum():
        to_sibling[chips - 1].wait()
        grad = own_part[(chips - 1) % 2] + sib[chips - 1].astype(F32)
        for at in range(chips - 1):
            to_mate[at].wait()
            grad = grad + got[at].astype(F32)
        unit, scale = unit_rows(tokens[...].astype(F32))
        scaled = grad * gain[...]
        rows_out[...] = scale * (scaled - unit * jnp.mean(scaled * unit, axis=-1, keepdims=True))
        gains_own[...] = gains[...]
        summed = jnp.sum(grad * unit, axis=0, keepdims=True)
        lanes = gains.shape[1]
        for n in range(width // lanes):
            gains_own[n : n + 1] = summed[:, n * lanes : (n + 1) * lanes]
        n = 2 * width // lanes
        gains_own[n : n + 1] = q_sum[...]
        gains_own[n + 1 : n + 2] = jnp.where(parity == 0, k_sum[...], jnp.zeros_like(k_sum))
        mine = pltpu.make_async_copy(gains_own, gains_in.at[s], local.at[2])
        mine.start()
        gain_sends.append(mine)
        for i, peer in enumerate(others):
            item = push(gains_own, gains_in.at[s], ss_g.at[i], rs_g.at[i], shard=peer)
            item.start()
            gain_sends.append(item)

    def small_plane():
        for item in small + gain_sends:
            item.wait()
        gains_mid[...] = gains_in[0]
        for i in range(1, n_shard):
            gains_mid[...] += gains_in[i]
        total = router[s].astype(F32)
        for i in range(n_shard - 1):
            total = total + router_in[i].astype(F32)
        router_mid[...] = total.astype(BF)
        for i, layer in enumerate(layers):
            push(gains_mid, gains_far.at[c], ss_h.at[i], rs_h.at[i], ctx=layer).start()
            push(router_mid, router_far.at[c], ss_t.at[i], rs_t.at[i], ctx=layer).start()
        pltpu.make_async_copy(gains_mid, gains_far.at[c], local.at[3]).start()
        pltpu.make_async_copy(router_mid, router_far.at[c], local.at[4]).start()

    def small_all():
        pltpu.make_async_copy(gains_mid, gains_far.at[c], local.at[3]).wait()
        pltpu.make_async_copy(router_mid, router_far.at[c], local.at[4]).wait()
        for i, layer in enumerate(layers):
            push(gains_mid, gains_far.at[c], ss_h.at[i], rs_h.at[i], ctx=layer).wait()
            push(router_mid, router_far.at[c], ss_t.at[i], rs_t.at[i], ctx=layer).wait()
        gains_out[...] = gains_far[0]
        router_out[...] = router_far[0].astype(F32)
        for i in range(1, n_ctx):
            gains_out[...] += gains_far[i]
            router_out[...] += router_far[i].astype(F32)

    side = []
    for at in range(chips):
        side.append(functools.partial(product, at))
        if at:
            side.append(functools.partial(chip_sum, at - 1))
    count_steps = len(steps) + lag
    late = {21: last_sum, 23: mix_last, 26: small_plane}
    for n in range(3, count_steps):
        advance(n)
        if side:
            side.pop(0)()
        if n in late:
            late[n]()
    for job in side:
        job()
    small_all()
    mix_out[...] = mix_fold.take(0, mix_out[...])
    mix_fold.drain()
    for which, j in steps:
        which.drain(j)


def back(n_ctx, n_shard, group, heads, args, ident):
    count, width = args[0].shape
    rows_in, w_all, router, gains, mix_near = args[7], args[8], args[17], args[16], args[18]
    n, z, chips, wides = n_shard, n_ctx, n_shard // 2, 16
    wr, cols = w_all.shape[1], heads * HEAD_DIM
    keys = z * count
    sds, scratch = jax.ShapeDtypeStruct, pltpu.VMEM
    router_shape = router.shape[1:]
    dma = lambda *shape: DMA(shape)
    wide_block, block = (cols, width // wides), (wr, cols + HEAD_DIM)
    return call(
        functools.partial(back_body, z, n, group, heads, wides),
        [
            sds((wr, n * cols), BF), sds((n, wr, HEAD_DIM), BF), sds((cols, width), BF), sds(router_shape, F32),
            sds(gains.shape, F32), sds((count, width), F32), sds((count, width), F32), sds(mix_near.shape, BF),
        ],
        [VMEM] + [ANY] * 8 + [VMEM] * 9 + [ANY, VMEM, VMEM],
        [scratch(item.shape, item.dtype) for item in args[1:7] + args[8:9]] + [dma(7)] + [
            scratch((n, count, width), BF), scratch((cols, n * count), BF),
            scratch((2, count, cols), BF), scratch((heads * count, keys), BF), scratch((heads * count, keys), BF),
            scratch((2, n, z, count, HEAD_DIM), BF), scratch((n, count, cols + HEAD_DIM), BF),
            scratch((1, HEAD_DIM), F32), scratch((1, HEAD_DIM), F32),
            scratch((wides,) + wide_block, BF), scratch((n,) + block, BF),
            scratch((chips, 2, z, count, HEAD_DIM), BF), scratch((chips, z - 1, 2, count, HEAD_DIM), BF),
            scratch((chips, z - 1, 2, count, HEAD_DIM), BF), scratch((2, wides) + wide_block, BF),
            scratch((n,) + block, BF), scratch((2, 2 * n, wr // 2, cols + HEAD_DIM), BF),
            scratch((2, count, width), F32), scratch((2, count, wr), F32), scratch((chips, count, width), BF),
            scratch((chips, count, width), BF), scratch((chips - 1, count, width), BF),
            scratch((chips - 1, count, width), BF),
            scratch((n - 1,) + router_shape, BF), scratch(router_shape, BF), scratch((z,) + router_shape, BF),
            scratch(gains.shape, F32), scratch((n,) + gains.shape, F32), scratch(gains.shape, F32),
            scratch((z,) + gains.shape, F32), scratch((n, mix_near.shape[1], 512), BF),
            scratch((z - 1, count, width), BF), scratch((z - 1, count, width), BF), dma(7),
            dma(chips), dma(chips), dma(chips), dma(chips), dma(chips), dma(chips), dma(chips, z - 1), dma(chips, z - 1),
            dma(wides), dma(2, wides), dma(wides), dma(wides), dma(n - 1), dma(n - 1), dma(2 * n), dma(2, 2 * n), dma(2 * n),
            dma(2 * n), dma(2 * n), dma(n - 1), dma(n - 1), dma(n - 1), dma(n - 1), dma(z - 1), dma(z - 1), dma(z - 1), dma(z - 1),
            dma(chips), dma(chips), dma(chips - 1), dma(chips - 1), dma(n - 1), dma(n - 1), dma(z), dma(z), dma(n - 1), dma(n - 1),
        ],
        ident, args, mib=62, out_specs=[ANY, ANY, ANY, VMEM, VMEM, VMEM, VMEM, ANY],
    )


def dispatch_body(n_ctx, n_shard, group, tile, rows, tail, code, recv, tail_recv,
                  zrows, ztail, ready, tail_ready, local, ss_z, rs_z, ss_t, rs_t, ss_x, rs_x, ss_y, rs_y):
    c, s, parity, sibling, others, layers = here(n_ctx, n_shard)
    greet(others, layers)
    count, width = rows.shape
    groups = n_ctx // group
    slots = recv.shape[2]
    own = [pltpu.make_async_copy(rows, zrows.at[c], local.at[0]), pltpu.make_async_copy(tail, ztail.at[c], local.at[1])]
    fans = [
        Fan(n_ctx, c, lambda d: ztail.at[flip_bits(c, d)], ss_t, rs_t, True),
        Fan(n_ctx, c, lambda d: zrows.at[flip_bits(c, d)], ss_z, rs_z, True),
    ]
    fans[0].send(0, tail)
    fans[1].send(0, rows)
    for item in own:
        item.start()
    waits = []
    seen = set()
    for k in range(groups):
        at = flip_bits(lax.div(c, group), k)
        if k == 0:
            for item in own:
                item.wait()
        table = slot_table(code[at], slots)
        for d in fans[0].order():
            if d < (k + 1) * group and d not in seen:
                fans[0].arrival(d)
                fans[1].arrival(d)
                seen.add(d)
        first = pl.multiple_of(at * group, group)
        block = ztail[pl.ds(first, group)].reshape(group * count, -1)
        tail_ready[k] = jnp.dot(table, block, preferred_element_type=F32).astype(BF).reshape(n_shard, slots, -1)

        @pl.loop(0, width // tile)
        def _(j):
            cols = pl.ds(pl.multiple_of(j * tile, tile), tile)
            block = zrows[pl.ds(first, group), :, cols].reshape(group * count, tile)
            value = jnp.dot(table, block, preferred_element_type=F32).astype(BF)
            ready[k, :, :, cols] = value.reshape(n_shard, slots, tile)

        for i, peer in enumerate(others):
            item = push(ready.at[k, peer], recv.at[s, at], ss_x.at[k, i], rs_x.at[k, i], shard=peer)
            item.start()
            waits.append(item)
            item = push(tail_ready.at[k, peer], tail_recv.at[s, at], ss_y.at[k, i], rs_y.at[k, i], shard=peer)
            item.start()
            waits.append(item)
        item = pltpu.make_async_copy(ready.at[k, s], recv.at[s, at], local.at[2 * k + 2])
        item.start()
        waits.append(item)
        item = pltpu.make_async_copy(tail_ready.at[k, s], tail_recv.at[s, at], local.at[2 * k + 3])
        item.start()
        waits.append(item)
    for fan in fans:
        fan.drain()
    for item in waits:
        item.wait()


def dispatch_rows(n_ctx, n_shard, group, capacity, rows, tail, code, ident):
    groups, slots = code.shape[0], group * capacity
    count, width = rows.shape
    few = tail.shape[1]
    return call(
        functools.partial(dispatch_body, n_ctx, n_shard, group, 512),
        [
            jax.ShapeDtypeStruct((n_shard, groups, slots, width), BF),
            jax.ShapeDtypeStruct((n_shard, groups, slots, few), BF),
        ],
        [VMEM, VMEM, VMEM],
        [
            pltpu.VMEM((n_ctx, count, width), BF), pltpu.VMEM((n_ctx, count, few), BF),
            pltpu.VMEM((groups, n_shard, slots, width), BF), pltpu.VMEM((groups, n_shard, slots, few), BF),
            DMA((2 * groups + 2,)), DMA((n_ctx,)), DMA((n_ctx,)), DMA((n_ctx,)), DMA((n_ctx,)),
        ] + [DMA((groups, n_shard - 1))] * 4,
        ident, (rows, tail, code), mib=56,
    )


def combine_body(n_ctx, n_shard, group, tile, rows, tail, mix, code, out, tail_out, mix_out,
                 land, tail_land, value, tail_value, zsend, zrecv, tsend, trecv, msend, mrecv, mix_kept, table, local,
                 ss_x, rs_x, ss_y, rs_y, ss_z, rs_z, ss_t, rs_t, ss_m, rs_m):
    c, s, parity, sibling, others, layers = here(n_ctx, n_shard)
    greet(others, layers)
    count, width = out.shape
    groups = n_ctx // group
    slots = rows.shape[2]
    near = {}
    for k in reversed(range(groups)):
        at = flip_bits(lax.div(c, group), k)
        near[k] = []
        for i, peer in enumerate(others):
            item = push(rows.at[peer, at], land.at[k, s], ss_x.at[k, i], rs_x.at[k, i], shard=peer)
            item.start()
            near[k].append(item)
            item = push(tail.at[peer, at], tail_land.at[k, s], ss_y.at[k, i], rs_y.at[k, i], shard=peer)
            item.start()
            near[k].append(item)
        item = pltpu.make_async_copy(rows.at[s, at], land.at[k, s], local.at[k, 0])
        item.start()
        near[k].append(item)
        item = pltpu.make_async_copy(tail.at[s, at], tail_land.at[k, s], local.at[k, 1])
        item.start()
        near[k].append(item)
    for k in range(groups):
        table[k] = slot_table(code[flip_bits(lax.div(c, group), k)], slots).T

    def local_sums(k, block_of):
        @pl.loop(0, width // tile)
        def _(j):
            cols = pl.ds(pl.multiple_of(j * tile, tile), tile)
            value[:, cols] = jnp.dot(table[k], block_of(cols), preferred_element_type=F32)

    def part(ref, d):
        place = lax.rem(flip_bits(c, d), group)
        return ref[pl.ds(pl.multiple_of(place * count, count), count), :]

    def in_group(k):
        return sorted(range(k * group, (k + 1) * group), key=lambda d: (lowest(d) or n_ctx, d))

    mix_fold = Fold(c, msend, mrecv, ss_m, rs_m)
    for k in reversed(range(groups)):
        at = flip_bits(lax.div(c, group), k)
        local_sums(k, lambda cols: mix[:, at, :, cols].reshape(n_shard * slots, tile))
        for d in in_group(k):
            if lowest(d) == 1:
                mix_fold.give(d, part(value, d))
            else:
                mix_kept[d // 2] = part(value, d)
    fold = Fold(c, zsend, zrecv, ss_z, rs_z)
    tail_fold = Fold(c, tsend, trecv, ss_t, rs_t)
    for k in reversed(range(groups)):
        for item in near[k]:
            item.wait()
        local_sums(k, lambda cols: land[k, :, :, cols].reshape(n_shard * slots, tile))
        tail_value[...] = jnp.dot(
            table[k], tail_land[k].reshape(n_shard * slots, -1), preferred_element_type=F32
        )
        for d in in_group(k):
            if lowest(d) == 1:
                fold.give(d, part(value, d))
                tail_fold.give(d, part(tail_value, d))
        for d in in_group(k):
            if lowest(d) != 1:
                if d:
                    mix_fold.give(d, mix_fold.take(d, mix_kept[d // 2]))
                    fold.give(d, fold.take(d, part(value, d)))
                    tail_fold.give(d, tail_fold.take(d, part(tail_value, d)))
                else:
                    mix_out[...] = mix_fold.take(0, mix_kept[0])
                    out[...] = fold.take(0, part(value, 0))
                    tail_out[...] = tail_fold.take(0, part(tail_value, 0))
    for item in (mix_fold, fold, tail_fold):
        item.drain()


def combine_rows(n_ctx, n_shard, group, rows, tail, mix, code, ident):
    groups, slots, width = rows.shape[1:]
    few = tail.shape[3]
    count = code.shape[2] // group
    sds = jax.ShapeDtypeStruct
    return call(
        functools.partial(combine_body, n_ctx, n_shard, group, 512),
        [sds((count, width), F32), sds((count, few), F32), sds((count, width), F32)],
        [VMEM] * 4,
        [
            pltpu.VMEM((groups, n_shard, slots, width), BF), pltpu.VMEM((groups, n_shard, slots, few), BF),
            pltpu.VMEM((group * count, width), F32), pltpu.VMEM((group * count, few), F32),
            pltpu.VMEM((n_ctx - 1, count, width), BF), pltpu.VMEM((n_ctx - 1, count, width), BF),
            pltpu.VMEM((n_ctx - 1, count, few), BF), pltpu.VMEM((n_ctx - 1, count, few), BF),
            pltpu.VMEM((n_ctx - 1, count, width), BF), pltpu.VMEM((n_ctx - 1, count, width), BF),
            pltpu.VMEM((n_ctx // 2, count, width), F32), pltpu.VMEM((groups, group * count, n_shard * slots), BF),
            DMA((groups, 2)),
        ] + [DMA((groups, n_shard - 1))] * 4 + [DMA((n_ctx,))] * 6,
        ident, (rows, tail, mix, code), mib=60, out_specs=[VMEM] * 3,
    )


def expert_body(n_ctx, n_shard, group, half, tile,
                rows, tail, code, gate_in, up_in, down_in, cot_in,
                out, tail_out, mix_near, mix_far, mix_part, g_gate, g_up, g_down,
                w_gate, w_up, w_down, loaded, zrows, ztail, ready, tail_ready, recv, tail_recv, cot, back_rows, back_tail, land, tail_land,
                hidden, grad_gate, grad_up, work, slot_dot, table, tail_value,
                zrecv, tsend, trecv, stage, stage_d, local, ss_a, rs_a,
                ss_z, rs_z, ss_t, rs_t, ss_x, rs_x, ss_y, rs_y, ss_d, rs_d, ss_e, rs_e, ss_m, rs_m,
                ss_fz, rs_fz, ss_ft, rs_ft, ss_st, ss_sd):
    c, s, parity, sibling, others, layers = here(n_ctx, n_shard)
    count, width = rows.shape
    few = tail.shape[1]
    inner = w_gate.shape[1]
    groups = n_ctx // group
    slots = recv.shape[2]
    chunk = half * slots
    experts = n_ctx * n_shard
    expert = c * n_shard + s
    mine = by_core(s, n_shard)
    loads = [
        pltpu.make_async_copy(rows, zrows.at[c], local.at[0]),
        pltpu.make_async_copy(tail, ztail.at[c], local.at[1]),
    ] + [
        pltpu.make_async_copy(cot_in.at[flip_bits(lax.div(c, group), k)], cot.at[k], local.at[2 + 2 * groups + k])
        for k in range(groups)
    ]
    greet(others, layers)
    fan = Fan(n_ctx, c, lambda d: ztail.at[flip_bits(c, d)], ss_t, rs_t, True)
    fan.send(0, tail)
    near_layer, far_layer = flip_bits(c, 1), flip_bits(c, 2)
    sides = [slice(0, width // 2), slice(width // 2, width)]
    near = push(rows, zrows.at[c], ss_z.at[0], rs_z.at[0], ctx=near_layer)
    near.start()
    edge = jnp.logical_or(c == 0, c == n_ctx - 1)
    away = [push(rows.at[:, side], zrows.at[c, :, side], ss_z.at[1 + n], rs_z.at[1 + n], ctx=far_layer)
            for n, side in enumerate(sides)]
    passed = [push(zrows.at[far_layer, :, side], zrows.at[far_layer, :, side], ss_z.at[3 + n], rs_z.at[3 + n],
                   ctx=near_layer) for n, side in enumerate(sides)]

    @pl.when(jnp.logical_not(edge))
    def _():
        for item in away:
            item.start()

    loads += [
        pltpu.make_async_copy(a, b, loaded.at[n])
        for n, (a, b) in enumerate(((gate_in, w_gate), (up_in, w_up), (down_in, w_down)))
    ]
    loads[0].start()
    loads[1].start()

    sent = {0: [], 1: []}
    early = (slots // group) // 16 * 16
    place = lax.rem(c, group)
    early_at = pl.multiple_of(place * (slots - early), 16)
    late_at = pl.multiple_of((1 - place) * early, 16)

    def some_slots(rows_code, first, amount):
        places = (lax.broadcasted_iota(jnp.int32, (amount, rows_code.shape[1]), 0) + first).astype(F32)
        return jnp.concatenate(
            [(places == rows_code[e : e + 1, :]).astype(BF) for e in range(n_shard)], axis=0
        )

    own_code = code[lax.div(c, group), :, pl.ds(pl.multiple_of(place * count, count), count)]
    early_picks = some_slots(own_code, early_at, early)

    @pl.loop(0, width // tile)
    def _(j):
        cols = pl.ds(pl.multiple_of(j * tile, tile), tile)
        moved = jnp.dot(early_picks, rows[:, cols], preferred_element_type=F32).astype(BF)
        ready[0, :, pl.ds(early_at, early), cols] = moved.reshape(n_shard, early, tile)

    for i, peer in enumerate(others):
        sent[0].append(push(ready.at[0, peer, pl.ds(early_at, early)], recv.at[0, mine, pl.ds(early_at, early)],
                            ss_a.at[i], rs_a.at[i], shard=peer))
        sent[0][-1].start()
    for item in loads[2:]:
        item.start()
    loads[0].wait()
    loads[1].wait()
    near.wait_send()

    @pl.when(edge)
    def _():
        for item in away:
            item.start()

    near.wait_recv()
    for k in range(groups):
        at = flip_bits(lax.div(c, group), k)
        whole = slot_table(code[at], slots)
        table[k] = whole.T
        for d in (2, 3) if k else (1,):
            fan.arrival(d)
        first = pl.multiple_of(at * group, group)
        block = ztail[pl.ds(first, group)].reshape(group * count, few)
        tail_ready[k] = jnp.dot(whole, block, preferred_element_type=F32).astype(BF).reshape(n_shard, slots, few)
        amount = slots if k else slots - early
        begin = 0 if k else late_at
        span = pl.ds(begin, amount)
        picks = some_slots(code[at], begin, amount)
        for n, side in enumerate(sides if k else [slice(0, width)]):
            if k:
                if n == 0:
                    for m in range(2):
                        away[m].wait_recv()
                        passed[m].start()
                passed[n].wait_recv()

            @pl.loop(side.start // tile, side.stop // tile)
            def _(j):
                cols = pl.ds(pl.multiple_of(j * tile, tile), tile)
                block = zrows[pl.ds(first, group), :, cols].reshape(group * count, tile)
                moved = jnp.dot(picks, block, preferred_element_type=F32).astype(BF)
                ready[k, :, span, cols] = moved.reshape(n_shard, amount, tile)

            fresh = []
            for i, peer in enumerate(others):
                fresh.append(push(ready.at[k, peer, span, side], recv.at[k, mine, span, side],
                                  ss_x.at[k + n, i], rs_x.at[k + n, i], shard=peer))
            if n == 0:
                for i, peer in enumerate(others):
                    fresh.append(push(tail_ready.at[k, peer], tail_recv.at[k, mine], ss_y.at[k, i], rs_y.at[k, i], shard=peer))
                fresh.append(pltpu.make_async_copy(tail_ready.at[k, s], tail_recv.at[k, mine], local.at[3 + 2 * k]))
            if n == k:
                fresh.append(pltpu.make_async_copy(ready.at[k, s], recv.at[k, mine], local.at[2 + 2 * k]))
            for item in fresh:
                item.start()
            sent[k] += fresh
    fan.drain()
    for item in away + passed:
        item.wait_send()
    for item in loads[2:]:
        item.wait()

    gate_pre, up_pre = work.at[0:chunk, 0:inner], work.at[0:chunk, inner : 2 * inner]
    value = work.at[0 : group * count, 0:width]
    column = lax.broadcasted_iota(jnp.int32, (1, few), 1)
    is_coarse, is_fine = column == expert, column == experts + expert

    def send_back(src, dst, p, ss, rs):
        e = from_core(p, n_shard)

        @pl.when(s != e)
        def _():
            push(src.at[p], dst.at[s], ss.at[e], rs.at[s], shard=e).start()

        @pl.when(s == e)
        def _():
            pltpu.make_async_copy(src.at[p], dst.at[e], rs.at[e]).start()

    def wait_back(src, dst, ss, rs):
        for p in range(n_shard):
            e = from_core(p, n_shard)

            @pl.when(s != e)
            def _():
                push(src.at[p], dst.at[e], ss.at[e], rs.at[e], shard=e).wait()

            @pl.when(s == e)
            def _():
                pltpu.make_async_copy(src.at[p], dst.at[e], rs.at[e]).wait()

    def experts_part(k, h):
        of = slice(h * half, (h + 1) * half)
        r = pl.ds((k * n_shard + h * half) * slots, chunk)
        gates = jnp.sum(
            jnp.where(is_coarse | is_fine, tail_recv[k, of].reshape(chunk, few).astype(F32), 0.0), axis=1, keepdims=True
        )

        @pl.loop(0, inner // 256)
        def _(j):
            cols = pl.ds(pl.multiple_of(j * 256, 256), 256)
            x = recv[k, of].reshape(chunk, width)
            g = jnp.dot(x, w_gate[:, cols], preferred_element_type=F32)
            u = jnp.dot(x, w_up[:, cols], preferred_element_type=F32)
            gate_pre[:, cols] = g
            up_pre[:, cols] = u
            hidden[r, cols] = (g * jax.nn.sigmoid(g) * u).astype(BF)

        slot_dot[...] = jnp.zeros_like(slot_dot)

        @pl.loop(0, width // tile)
        def _(j):
            cols = pl.ds(pl.multiple_of(j * tile, tile), tile)
            o = jnp.dot(hidden[r, :], w_down[:, cols], preferred_element_type=F32).astype(BF).astype(F32)
            up_row = cot[k, of, :, cols].reshape(chunk, tile).astype(F32)
            slot_dot[...] += jnp.sum(o * up_row, axis=1, keepdims=True)
            ready[k, of, :, cols] = (gates * o).astype(BF).reshape(half, slots, tile)
            cot[k, of, :, cols] = (gates * up_row).astype(BF).reshape(half, slots, tile)

        coarse = slot_dot[...].astype(BF).astype(F32)
        fine = slot_dot[...] - coarse
        back_tail[k, of] = jnp.where(is_coarse, coarse, jnp.where(is_fine, fine, 0.0)).astype(BF).reshape(half, slots, few)

        @pl.loop(0, inner // 256)
        def _(j):
            cols = pl.ds(pl.multiple_of(j * 256, 256), 256)
            gh = lax.dot_general(cot[k, of].reshape(chunk, width), w_down[cols, :], (((1,), (1,)), ((), ())),
                                 preferred_element_type=F32)
            g, u = gate_pre[:, cols], up_pre[:, cols]
            sig = jax.nn.sigmoid(g)
            grad_gate[r, cols] = (gh * u * (sig * (1.0 + g * (1.0 - sig)))).astype(BF)
            grad_up[r, cols] = (gh * (g * sig)).astype(BF)

        @pl.loop(0, width // tile)
        def _(j):
            cols = pl.ds(pl.multiple_of(j * tile, tile), tile)
            gx = lax.dot_general(grad_gate[r, :], w_gate[cols, :], (((1,), (1,)), ((), ())), preferred_element_type=F32)
            gx += lax.dot_general(grad_up[r, :], w_up[cols, :], (((1,), (1,)), ((), ())), preferred_element_type=F32)
            back_rows[k, of, :, cols] = gx.astype(BF).reshape(half, slots, tile)

    def send_part(k, h):
        for p in range(h * half, (h + 1) * half):
            send_back(back_rows.at[k], land.at[k], p, ss_d.at[k], rs_d.at[k])
            send_back(back_tail.at[k], tail_land.at[k], p, ss_e.at[k], rs_e.at[k])

    halves = n_shard // half
    for k in range(groups):
        for item in sent[k]:
            item.wait()
        for h in range(halves):
            experts_part(k, h)
            if k or h + 1 < halves:
                send_part(k, h)
    send_part(0, halves - 1)
    for p in range(n_shard):
        send_back(ready.at[groups - 1], mix_far, p, ss_m, rs_m)
    keep = pltpu.make_async_copy(ready.at[0], mix_near, local.at[0])
    keep.start()

    everything = groups * n_shard * slots

    def stage_out(j, which):
        at = pl.ds(pl.multiple_of(j * 256, 256), 256)
        return pltpu.make_async_copy(stage.at[which], (g_gate, g_up)[which].at[at], ss_st.at[which])

    @pl.loop(0, width // 256)
    def _(j):
        x = recv[:, :, :, pl.ds(pl.multiple_of(j * 256, 256), 256)].reshape(everything, 256)
        for which, grad in enumerate((grad_gate, grad_up)):
            total = lax.dot_general(x, grad[...], (((0,), (0,)), ((), ())), preferred_element_type=F32).astype(BF)

            @pl.when(j >= 1)
            def _():
                stage_out(j - 1, which).wait()

            stage[which] = total
            stage_out(j, which).start()

    def down_out(j):
        return pltpu.make_async_copy(stage_d, g_down.at[:, pl.ds(pl.multiple_of(j * 256, 256), 256)], ss_sd)

    @pl.loop(0, width // 256)
    def _(j):
        grad = cot[:, :, :, pl.ds(pl.multiple_of(j * 256, 256), 256)].reshape(everything, 256)
        total = lax.dot_general(
            hidden[...], grad, (((0,), (0,)), ((), ())), preferred_element_type=F32).astype(BF)

        @pl.when(j >= 1)
        def _():
            down_out(j - 1).wait()

        stage_d[...] = total
        down_out(j).start()

    last = width // 256 - 1
    stage_out(last, 0).wait()
    stage_out(last, 1).wait()
    down_out(last).wait()

    def local_sums(k, ref):
        @pl.loop(0, width // tile)
        def _(j):
            cols = pl.ds(pl.multiple_of(j * tile, tile), tile)
            block = ref[k, :, :, cols].reshape(n_shard * slots, tile)
            value[:, cols] = jnp.dot(table[k], block, preferred_element_type=F32)

    def part(ref, d):
        place = lax.rem(flip_bits(c, d), group)
        return ref[pl.ds(pl.multiple_of(place * count, count), count), :]

    folds = [Fold(c, zrows.at[:, :, side], zrecv.at[:, :, side], ss_fz.at[n], rs_fz.at[n]) for n, side in enumerate(sides)]
    tail_fold = Fold(c, tsend, trecv, ss_ft, rs_ft)
    for k in reversed(range(groups)):
        wait_back(back_rows.at[k], land.at[k], ss_d.at[k], rs_d.at[k])
        wait_back(back_tail.at[k], tail_land.at[k], ss_e.at[k], rs_e.at[k])
        local_sums(k, land)
        tail_value[...] = jnp.dot(table[k], tail_land[k].reshape(n_shard * slots, few), preferred_element_type=F32)
        if k:
            tail_fold.give(3, part(tail_value, 3))
            folds[0].give(3, part(value, 3)[:, sides[0]])
            folds[0].items[3].wait_send()
            folds[0].left.add(3)
            folds[1].give(3, part(value, 3)[:, sides[1]])
            for fold, side in zip(folds, sides):
                fold.give(2, fold.take(2, part(value, 2)[:, side]))
            tail_fold.give(2, tail_fold.take(2, part(tail_value, 2)))
        else:
            tail_fold.give(1, part(tail_value, 1))
            for fold, side in zip(folds, sides):
                fold.give(1, part(value, 1)[:, side])
    out[...] = part(value, 0)
    wait_back(ready.at[groups - 1], mix_far, ss_m, rs_m)
    keep.wait()
    again = pltpu.make_async_copy(mix_far, ready.at[0], local.at[0])
    again.start()
    again.wait()

    @pl.loop(0, width // tile)
    def _(j):
        cols = pl.ds(pl.multiple_of(j * tile, tile), tile)
        block = ready[0, :, :, cols].reshape(n_shard * slots, tile)
        value[:, cols] = jnp.dot(table[1], block, preferred_element_type=F32)

    for d in (2, 3):
        mix_part[d - 2] = part(value, d).astype(BF)
    for fold, side in zip(folds, sides):
        out[:, side] = fold.take(0, out[:, side])
    tail_out[...] = tail_fold.take(0, part(tail_value, 0))
    for fold in folds + [tail_fold]:
        fold.drain()


def run_experts(n_ctx, n_shard, group, capacity, rows, tail, code, w_gate, w_up, w_down, cot_rows, ident):
    n, z, groups, slots = n_shard, n_ctx, code.shape[0], group * capacity
    count, width = rows.shape
    few, inner, half = tail.shape[1], w_gate.shape[1], n_shard // 2
    everything, chunk = groups * n * slots, half * slots
    sds, scratch = jax.ShapeDtypeStruct, pltpu.VMEM
    dma = lambda *shape: DMA(shape)
    wide, thin = (groups, n, slots, width), (groups, n, slots, few)
    return call(
        functools.partial(expert_body, z, n, group, half, 512),
        [
            sds((count, width), F32), sds((count, few), F32), sds((n, slots, width), BF), sds((n, slots, width), BF),
            sds((2, count, width), BF), sds((width, inner), BF), sds((width, inner), BF), sds((inner, width), BF),
        ],
        [VMEM] * 3 + [ANY] * 4,
        [scratch(item.shape, BF) for item in (w_gate, w_up, w_down)] + [
            dma(3),
            scratch((z, count, width), BF), scratch((z, count, few), BF), scratch(wide, BF), scratch(thin, BF),
            scratch(wide, BF), scratch(thin, BF), scratch(wide, BF), scratch(wide, BF), scratch(thin, BF),
            scratch(wide, BF), scratch(thin, BF),
            scratch((everything, inner), BF), scratch((everything, inner), BF), scratch((everything, inner), BF),
            scratch((max(chunk, group * count), max(2 * inner, width)), F32), scratch((chunk, 1), F32),
            scratch((groups, group * count, n * slots), BF),
            scratch((group * count, few), F32), scratch((z - 1, count, width), BF),
            scratch((z - 1, count, few), BF), scratch((z - 1, count, few), BF),
            scratch((2, 256, inner), BF), scratch((inner, 256), BF), dma(2 + 3 * groups), dma(n - 1), dma(n - 1),
        ] + [dma(5)] * 2 + [dma(z)] * 2 + [dma(groups + 1, n - 1)] * 2 + [dma(groups, n - 1)] * 2 + [dma(groups, n)] * 4
        + [dma(n)] * 2 + [dma(2, z)] * 2 + [dma(z)] * 2 + [dma(2), DMA],
        ident, (rows, tail, code, w_gate, w_up, w_down, cot_rows), mib=62, out_specs=[VMEM] * 2 + [ANY] * 2 + [VMEM] + [ANY] * 3,
    )


def rms_scale(hidden, gain):
    return hidden * lax.rsqrt(jnp.mean(hidden * hidden, axis=-1, keepdims=True) + epsilon) * gain


def rotate(headwise, places):
    half_size = headwise.shape[-1] // 2
    frequency = rope_base ** (-jnp.arange(half_size, dtype=F32) * 2.0 / headwise.shape[-1])
    angles = places.astype(F32)[:, None] * frequency[None, :]
    cosine = jnp.cos(angles)[:, None, :]
    sine = jnp.sin(angles)[:, None, :]
    former = headwise[..., :half_size]
    latter = headwise[..., half_size:]
    return jnp.concatenate(
        [former * cosine - latter * sine, latter * cosine + former * sine], axis=-1
    )


def place_of(row_ids, order, block_rows):
    block_ids = jnp.arange(order.shape[0], dtype=jnp.int32)
    owner_block = row_ids // block_rows
    picked_block = jnp.sum(
        jnp.where(owner_block[:, None] == block_ids[None, :], order[None, :], 0), axis=1
    )
    return picked_block * block_rows + row_ids % block_rows


def dot(left, right):
    return jnp.dot(left, right, preferred_element_type=F32)


def contract_rows(left, right):
    return lax.dot_general(left, right, (((0,), (0,)), ((), ())), preferred_element_type=F32)


def contract_cols(left, right):
    return lax.dot_general(left, right, (((1,), (1,)), ((), ())), preferred_element_type=F32)


def exchange_shard(x):
    return lax.all_to_all(x, "shard", split_axis=0, concat_axis=0, tiled=True)


def gather_ctx(x):
    return lax.all_gather(x, "ctx", axis=0, tiled=False)


def shards(
    tokens,
    cotangent,
    block_order,
    routes,
    attn_gain,
    w_query,
    key_weight,
    value_weight,
    query_gain,
    key_gain,
    w_out,
    ffn_gain,
    w_router,
    w_gate,
    w_up,
    w_down,
):
    rows = tokens.shape[1]
    width = tokens.shape[2]
    ctx_count = lax.axis_size("ctx")
    shard_count = lax.axis_size("shard")
    my_ctx = lax.axis_index("ctx")
    my_shard = lax.axis_index("shard")
    experts = ctx_count * shard_count
    block_rows = rows // 2
    heads = QUERY_HEADS // shard_count
    head_cols = heads * HEAD_DIM
    sharers = shard_count // KEY_VALUE_HEADS
    score_scale = HEAD_DIM ** (-0.5)
    top_count = routes.shape[2]
    capacity = rows * top_count // experts + max(rows * top_count // (4 * experts), 1)
    sequence = rows * ctx_count
    plane = rows * shard_count
    wrows = width // shard_count

    inputs = tokens[0].astype(F32)
    upstream_b = cotangent[0]
    upstream = upstream_b.astype(F32)

    group = 1
    while group * capacity % 16:
        group *= 2
    groups = ctx_count // group
    small = plane * width <= 2**21 and ctx_count == 4 and group == 2
    slot_rows = shard_count * ctx_count * capacity
    block_shape = (shard_count, groups, group * capacity)
    row_ids = my_ctx * rows + jnp.arange(rows, dtype=jnp.int32)
    q_places = place_of(row_ids, block_order, block_rows)
    k_places = place_of(jnp.arange(sequence, dtype=jnp.int32), block_order, block_rows)
    bias = jnp.where(k_places[None, :] <= q_places[:, None], 0.0, -1e30).astype(F32)
    frequency = rope_base ** (-jnp.arange(HEAD_DIM // 2, dtype=F32) * 2.0 / HEAD_DIM)
    angles = q_places.astype(F32)[:, None] * frequency[None, :]
    cosine = jnp.concatenate([jnp.cos(angles)] * 2, axis=1)
    sine = jnp.concatenate([-jnp.sin(angles), jnp.sin(angles)], axis=1)
    (
        normed_all, w_mine, router_all, code, upstream_rows, query_pre, kv_pre, queries, kv_all, attn_rows, middle,
    ) = front(
        ctx_count, shard_count, group, capacity, KEY_VALUE_HEADS, small,
        (
            tokens[0], attn_gain[None], w_query, key_weight, value_weight, routes[0].T, w_router.T, upstream_b,
            cosine, sine, bias, query_gain[None], key_gain[None], w_out,
        ),
        0,
    )
    is_key = lax.rem(my_shard, 2) == 0
    part_count = sharers // 2

    def prep(pre, gain):
        shape = pre.shape
        flat = pre.reshape(-1, rows, shape[-2], HEAD_DIM)
        return jax.vmap(lambda v: rotate(rms_scale(v, gain), q_places))(flat).reshape(shape)

    normed_two = rms_scale(middle, ffn_gain)
    second_b = normed_two.astype(BF)
    logits = contract_cols(second_b, router_all)
    chosen = jnp.sum(
        (routes[0][:, :, None] == jnp.arange(experts, dtype=jnp.int32)).astype(F32), axis=1
    )

    def gates_of(log, mask):
        masked = jnp.where(mask > 0, log, -1e30)
        peak = jnp.max(masked, axis=-1, keepdims=True)
        risen = jnp.exp(masked - peak) * mask
        return risen / jnp.maximum(jnp.sum(risen, axis=-1, keepdims=True), 1e-30)

    gates = gates_of(logits, chosen)

    tail_cols = -(-2 * experts // 128) * 128

    def two_parts(value):
        coarse = value.astype(BF).astype(F32)
        return coarse.astype(BF), (value - coarse).astype(BF)

    gates_two = jnp.concatenate(two_parts(gates), axis=1)
    gates_two = jnp.pad(gates_two, ((0, 0), (0, tail_cols - 2 * experts)))
    if small:
        grad_second, back_tail, mix_near, unused, mix_part, grad_w_gate, grad_w_up, grad_w_down = run_experts(
            ctx_count, shard_count, group, capacity, second_b, gates_two, code, w_gate[0], w_up[0], w_down[0],
            upstream_rows, 3,
        )
        grad_w_gate, grad_w_up, grad_w_down = (
            grad_w_gate.astype(F32), grad_w_up.astype(F32), grad_w_down.astype(F32),
        )
    else:
        received, gate_tail = dispatch_rows(ctx_count, shard_count, group, capacity, second_b, gates_two, code, 3)
        received = received.reshape(slot_rows, width)
        my_expert = my_ctx * shard_count + my_shard
        upstream_rows = jnp.swapaxes(upstream_rows, 0, 1).reshape(slot_rows, width)
        column = jnp.arange(tail_cols, dtype=jnp.int32)[None, :]
        mine_column = (column == my_expert) | (column == experts + my_expert)
        gate_tail = gate_tail.reshape(slot_rows, tail_cols).astype(F32)
        slot_gates = jnp.sum(jnp.where(mine_column, gate_tail, 0.0), axis=1, keepdims=True)
        gate_pre = dot(received, w_gate[0])
        up_pre = dot(received, w_up[0])
        activated = jax.nn.silu(gate_pre)
        hidden_b = (activated * up_pre).astype(BF)
        expert_out = dot(hidden_b, w_down[0]).astype(BF)
        expert_out_f = expert_out.astype(F32)
        mix_sent = (slot_gates * expert_out_f).astype(BF)
        mix_sent, upstream_rows, expert_out = lax.optimization_barrier((mix_sent, upstream_rows, expert_out))
        expert_out_f = expert_out.astype(F32)
        mix_back = exchange_shard(mix_sent.reshape(block_shape + (width,)))
        upstream_rows = upstream_rows.astype(F32)
        slot_dot = jnp.sum(expert_out_f * upstream_rows, axis=1, keepdims=True)
        grad_expert = (slot_gates * upstream_rows).astype(BF)
        grad_w_down = contract_rows(hidden_b, grad_expert)
        grad_hidden = contract_cols(grad_expert, w_down[0])
        sigmoid_g = jax.nn.sigmoid(gate_pre)
        silu_slope = sigmoid_g * (1.0 + gate_pre * (1.0 - sigmoid_g))
        grad_gate_pre = (grad_hidden * up_pre * silu_slope).astype(BF)
        grad_up_pre = (grad_hidden * activated).astype(BF)
        grad_w_gate = contract_rows(received, grad_gate_pre)
        grad_w_up = contract_rows(received, grad_up_pre)
        grad_received = contract_cols(grad_gate_pre, w_gate[0]) + contract_cols(grad_up_pre, w_up[0])

        coarse, fine = two_parts(slot_dot)
        tail = jnp.where(column == my_expert, coarse, jnp.where(column == experts + my_expert, fine, jnp.zeros((), BF)))
        grad_second, back_tail, mixture = combine_rows(
            ctx_count, shard_count, group, grad_received.astype(BF).reshape(block_shape + (width,)),
            tail.reshape(block_shape + (tail_cols,)), mix_back, code, 4,
        )
    grad_gates = back_tail[:, :experts] + back_tail[:, experts : 2 * experts]
    grad_logits_b = (
        gates * (grad_gates - jnp.sum(gates * grad_gates, axis=-1, keepdims=True))
    ).astype(BF)
    router_part = contract_rows(grad_logits_b, second_b).astype(BF)
    grad_second = grad_second + dot(grad_logits_b, router_all)
    unused, norm_two_back = jax.vjp(rms_scale, middle, ffn_gain)
    grad_middle_part, grad_ffn_gain = norm_two_back(grad_second)
    grad_middle = upstream + grad_middle_part
    grad_proj_b = grad_middle.astype(BF)

    router_parts = jnp.swapaxes(router_part.reshape(experts, shard_count, wrows), 0, 1)
    if small:
        gains = jnp.concatenate([jnp.zeros((width,), F32), grad_ffn_gain, jnp.zeros((8 * HEAD_DIM,), F32)])
        gains = gains.reshape(-1, HEAD_DIM)
        q_sum, kv_sum, out_sum, router_sum, gains, grad_input_part, mixture, unused = back(
            ctx_count, shard_count, group, heads,
            (
                grad_proj_b, queries, kv_all, attn_rows, query_pre, kv_pre, w_out, normed_all, w_mine,
                cosine, sine, bias, query_gain[None], key_gain[None], tokens[0], attn_gain[None], gains, router_parts,
                mix_near, mix_part, code,
            ),
            5,
        )
    else:
        normed_all = normed_all.reshape(plane, width)
        w_mine = w_mine.reshape(width, head_cols + HEAD_DIM)
        query_pre = query_pre.reshape(shard_count, rows, heads, HEAD_DIM)
        kv_pre = kv_pre.reshape(plane, HEAD_DIM)
        queries = queries.reshape(shard_count, rows, heads, HEAD_DIM)
        kv_all = kv_all.reshape(2, shard_count, sequence, HEAD_DIM)
        keys, values = kv_all[0], kv_all[1]
        attn_rows = attn_rows.reshape(plane, head_cols)
        grad_proj_all = spread(shard_count, grad_proj_b, 5).reshape(plane, width)
        out_part = contract_rows(attn_rows, grad_proj_all).astype(BF)
        out_part, grad_proj_all = lax.optimization_barrier((out_part, grad_proj_all))
        grad_attn = contract_cols(grad_proj_all, w_out).astype(BF)
        grad_heads = grad_attn.reshape(shard_count, rows, heads, HEAD_DIM)
        scores = (
            jnp.einsum("sthd,spd->shtp", queries, keys, preferred_element_type=F32) * score_scale
        )
        scores = scores + bias
        raised = jnp.exp(scores - jnp.max(scores, axis=-1, keepdims=True))
        probs = raised / jnp.sum(raised, axis=-1, keepdims=True)
        probs_b = probs.astype(BF)
        grad_probs = jnp.einsum("sthd,spd->shtp", grad_heads, values, preferred_element_type=F32)
        delta = jnp.sum(probs * grad_probs, axis=-1, keepdims=True)
        grad_scores = (probs * (grad_probs - delta)).astype(BF)
        grad_query = score_scale * jnp.einsum(
            "shtp,spd->sthd", grad_scores, keys, preferred_element_type=F32
        )
        grad_keys = score_scale * jnp.einsum(
            "shtp,sthd->spd", grad_scores, queries, preferred_element_type=F32
        )
        grad_values = jnp.einsum("shtp,sthd->spd", probs_b, grad_heads, preferred_element_type=F32)
        grad_kv = jnp.stack([grad_keys, grad_values]).astype(BF)
        grad_kv = key_back(
            ctx_count, shard_count, grad_kv.reshape(2, shard_count, ctx_count, rows, HEAD_DIM), 6
        )
        unused, query_back = jax.vjp(prep, query_pre, query_gain)
        grad_query_pre, grad_query_gain = query_back(grad_query)
        kv_shape = (shard_count, rows, 1, HEAD_DIM)
        unused, key_prep_back = jax.vjp(prep, kv_pre.reshape(kv_shape), key_gain)
        grad_key_pre, grad_key_gain = key_prep_back(grad_kv.reshape(kv_shape))
        grad_key_gain = jnp.where(is_key, grad_key_gain, 0.0)
        grad_kv_full = jnp.where(
            is_key, grad_key_pre.reshape(plane, HEAD_DIM), grad_kv.reshape(plane, HEAD_DIM)
        ).astype(BF)
        grad_pre = jnp.concatenate(
            [grad_query_pre.reshape(plane, head_cols).astype(BF), grad_kv_full], axis=1
        )
        gains = jnp.concatenate(
            [
                jnp.zeros((1, width), F32),
                grad_ffn_gain[None],
                jnp.pad(
                    jnp.concatenate([grad_query_gain, grad_key_gain])[None],
                    ((0, 6 - 1), (0, width - 2 * HEAD_DIM)),
                ),
            ]
        )
        grad_w = contract_rows(normed_all, grad_pre).astype(BF).reshape(shard_count, wrows, -1)
        q_sum, kv_sum, out_sum, router_sum, gains, grad_input_part = finish(
            ctx_count, shard_count, head_cols, grad_w, out_part.reshape(8, -1, width), router_parts, gains, grad_pre, w_mine,
            tokens[0], attn_gain[None], 8,
        )
    mixed = (middle + mixture).astype(BF)
    grad_tokens = grad_middle + grad_input_part
    gains = gains.reshape(-1)
    grad_attn_gain, grad_ffn_gain = gains[:width], gains[width : 2 * width]
    grad_query_gain = gains[2 * width : 2 * width + HEAD_DIM]
    grad_key_gain = gains[2 * width + HEAD_DIM : 2 * width + 2 * HEAD_DIM]
    grad_w_query = q_sum.astype(F32)
    grad_w_out = out_sum.reshape(head_cols, width).astype(F32)
    kinds = kv_sum.astype(F32).reshape(KEY_VALUE_HEADS, part_count, 2, wrows, HEAD_DIM)
    kinds = jnp.transpose(jnp.sum(kinds, axis=1), (1, 2, 0, 3)).reshape(2, wrows, -1)
    grad_w_key, grad_w_value = kinds[0], kinds[1]
    grad_w_router = router_sum.T
    return (
        mixed[None],
        grad_tokens[None],
        grad_attn_gain,
        grad_w_query,
        grad_w_key,
        grad_w_value,
        grad_query_gain,
        grad_key_gain,
        grad_w_out,
        grad_ffn_gain,
        grad_w_router,
        grad_w_gate[None],
        grad_w_up[None],
        grad_w_down[None],
    )


def solution(mesh):
    rows = P("shard", "ctx", None)
    matrix = P("shard", None)
    expert = P(("ctx", "shard"), None, None)
    return jax.shard_map(
        shards,
        mesh=mesh,
        in_specs=(
            rows, rows, P(), rows, P(), matrix, matrix, matrix, P(), P(), matrix, P(), matrix,
            expert, expert, expert,
        ),
        out_specs=(
            rows, rows, P(), matrix, matrix, matrix, P(), P(), matrix, P(), matrix,
            expert, expert, expert,
        ),
        check_vma=False,
    )
```

```python
import functools

import jax
import jax.numpy as jnp
from jax import lax
from jax.experimental import pallas as pl
from jax.experimental.pallas import tpu as pltpu
from jax.sharding import PartitionSpec as P

BF = jnp.bfloat16
F32 = jnp.float32
MESH = pl.DeviceIdType.MESH
ANY = pl.BlockSpec(memory_space=pl.ANY)
VMEM = pl.BlockSpec(memory_space=pltpu.VMEM)
DMA = pltpu.SemaphoreType.DMA
epsilon = 1e-06
rope_base = 1000000.0
QUERY_HEADS = 32
KEY_VALUE_HEADS = 4
HEAD_DIM = 128


def push(src, dst, send_sem, recv_sem, **where):
    return pltpu.make_async_remote_copy(
        src_ref=src, dst_ref=dst, send_sem=send_sem, recv_sem=recv_sem,
        device_id=where, device_id_type=MESH,
    )


def greet(shard_peers, ctx_peers):
    barrier = pltpu.get_barrier_semaphore()
    for peer in shard_peers:
        pl.semaphore_signal(barrier, inc=1, device_id={"shard": peer}, device_id_type=MESH)
    for peer in ctx_peers:
        pl.semaphore_signal(barrier, inc=1, device_id={"ctx": peer}, device_id_type=MESH)
    pl.semaphore_wait(barrier, len(shard_peers) + len(ctx_peers))


def here(ctx_count, shard_count):
    c, s = lax.axis_index("ctx"), lax.axis_index("shard")
    parity = lax.rem(s, 2)
    sibling = s + 1 - 2 * parity
    others = [lax.rem(s + d, shard_count) for d in range(1, shard_count)]
    layers = [lax.rem(c + d, ctx_count) for d in range(1, ctx_count)]
    return c, s, parity, sibling, others, layers


def flip_bits(index, mask):
    result = index
    bit = 1
    while bit <= mask:
        if mask & bit:
            result = result + bit - 2 * bit * lax.rem(lax.div(index, bit), 2)
        bit *= 2
    return result


def lowest(d):
    return d & -d


class Fan:
    def __init__(self, n_ctx, c, block, ss, rs, near_first):
        self.n_ctx, self.c, self.block, self.ss, self.rs, self.near_first = n_ctx, c, block, ss, rs, near_first
        self.items = {}

    def send(self, d, src):
        bits = [b for b in (1, 2, 4, 8, 16) if b < (lowest(d) or self.n_ctx)]
        for b in bits if self.near_first else reversed(bits):
            item = push(src, self.block(d), self.ss.at[d | b], self.rs.at[d | b], ctx=flip_bits(self.c, b))
            item.start()
            self.items[d | b] = item

    def arrival(self, d):
        self.items[d].wait_recv()
        if lowest(d) > 1:
            self.send(d, self.block(d))

    def order(self):
        return sorted(range(1, self.n_ctx), key=lambda d: (bin(d).count("1"), d if self.near_first else -d))

    def drain(self):
        for d in range(1, self.n_ctx):
            self.items[d].wait_send()


class Fold:
    def __init__(self, c, sent, received, ss, rs, slots=None, after=None):
        self.c, self.sent, self.received, self.ss, self.rs = c, sent, received, ss, rs
        self.slots, self.after = slots or {}, after or {}
        self.items, self.left = {}, set()

    def take(self, d, value):
        for b in (1, 2, 4, 8, 16):
            if b < lowest(d) or (d == 0 and b in self.items):
                self.items[d | b].wait_recv()
                value = value + self.received[(d | b) - 1].astype(F32)
        return value

    def give(self, d, value):
        slot = self.slots.get(d, d - 1)
        if d in self.after:
            other, which = self.after[d]
            other.items[which].wait_send()
            other.left.add(which)
        self.sent[slot] = value.astype(BF)
        item = push(self.sent.at[slot], self.received.at[d - 1], self.ss.at[d], self.rs.at[d],
                    ctx=flip_bits(self.c, lowest(d)))
        item.start()
        self.items[d] = item

    def give_as_is(self, d, ref):
        self.items[d] = push(ref, self.received.at[d - 1], self.ss.at[d], self.rs.at[d],
                             ctx=flip_bits(self.c, lowest(d)))
        self.items[d].start()

    def drain(self):
        for d, item in self.items.items():
            if d not in self.left:
                item.wait_send()


def call(body, outs, in_specs, scratch, ident, args, mib=48, out_specs=None):
    return pl.pallas_call(
        body,
        out_shape=outs,
        in_specs=in_specs,
        out_specs=out_specs if out_specs is not None else [ANY] * len(outs),
        scratch_shapes=scratch,
        compiler_params=pltpu.CompilerParams(
            collective_id=ident, has_side_effects=True, vmem_limit_bytes=mib * 2**20
        ),
    )(*args)


def by_core(s, n_shard):
    return lax.rem(s, 2) * (n_shard // 2) + lax.div(s, 2)


def from_core(place, n_shard):
    return place % (n_shard // 2) * 2 + place // (n_shard // 2)


def slot_table(code, slots):
    places = lax.broadcasted_iota(jnp.int32, (slots, code.shape[1]), 0).astype(F32)
    return jnp.concatenate(
        [(places == code[e : e + 1, :]).astype(BF) for e in range(code.shape[0])], axis=0
    )


def turn(value, cosine, sine):
    return value * cosine + pltpu.roll(value, HEAD_DIM // 2, 1) * sine


def unit_rows(value):
    scale = lax.rsqrt(jnp.mean(value * value, axis=-1, keepdims=True) + epsilon)
    return value * scale, scale


def front_body(n_ctx, n_shard, group, capacity, heads, kv_heads, paired, tile,
               tokens, gain, w_query, key_w, value_w, routes, router, cot, cosine, sine, bias, q_gain, k_gain, w_out,
               rows_out, w_all_out, router_all, code, cot_rows, qpre_out, kvpre, q_out, kv_out, attn_out, mid,
               own_rows, rows_all, w_all, zroutes, zcot, ready, qpre, q, kv, attn,
               own_part, pair, to_sib, sib, to_chip, got,
               local, ss_row, rs_row, ss_fwd, rs_fwd, ss_w, rs_w, ss_k, rs_k, ss_rt, rs_rt, ss_ro, rs_ro, ss_z, rs_z,
               ss_x, rs_x, ss_kz, rs_kz, ss_kf, rs_kf, ss_s, rs_s, ss_c, rs_c, out_sem):
    c, s, parity, sibling, others, layers = here(n_ctx, n_shard)
    chips = n_shard // 2
    chip = lax.div(s, 2)
    count, width = tokens.shape
    wr = w_query.shape[0]
    cols = heads * HEAD_DIM
    sharers = n_shard // kv_heads
    groups = n_ctx // group
    slots = group * capacity
    keys = n_ctx * count
    mates = [lax.rem(s + 2 * d, n_shard) for d in range(1, chips)]
    x = tokens[...].astype(F32)
    unit, unused = unit_rows(x)
    own_rows[...] = (unit * gain[...]).astype(BF)
    greet(others, layers)

    route_fan = Fan(n_ctx, c, lambda d: zroutes.at[flip_bits(c, d)], ss_ro, rs_ro, False)
    route_fan.send(0, routes)
    cot_fan = Fan(n_ctx, c, lambda d: zcot.at[flip_bits(c, d)], ss_z, rs_z, False)
    cot_fan.send(0, cot)
    first, waits = [], []
    for d in range(1, chips):
        item = push(own_rows, rows_all.at[s], ss_row.at[d], rs_row.at[d], shard=mates[d - 1])
        item.start()
        first.append(item)
    item = push(own_rows, rows_all.at[s], ss_fwd.at[0], rs_fwd.at[0], shard=sibling)
    item.start()
    waits.append(item)
    w_waits = []
    for i, peer in enumerate(others):
        from_q = w_query.at[:, pl.ds(pl.multiple_of(peer * cols, cols), cols)]
        item = push(from_q, w_all.at[s, :, pl.ds(0, cols)], ss_w.at[i], rs_w.at[i], shard=peer)
        item.start()
        w_waits.append(item)
        head = pl.ds(pl.multiple_of(lax.div(peer, sharers) * HEAD_DIM, HEAD_DIM), HEAD_DIM)
        for kind, ref in enumerate((key_w, value_w)):
            item = push(ref.at[:, head], w_all.at[s, :, pl.ds(cols, HEAD_DIM)], ss_k.at[i], rs_k.at[i], shard=peer)

            @pl.when(lax.rem(peer, 2) == kind)
            def _(item=item):
                item.start()

        w_waits.append(item)
        item = push(router, router_all.at[:, pl.ds(pl.multiple_of(s * wr, wr), wr)], ss_rt.at[i], rs_rt.at[i], shard=peer)
        item.start()
        waits.append(item)
    copies = [
        pltpu.make_async_copy(own_rows, rows_all.at[s], local.at[0]),
        pltpu.make_async_copy(w_query.at[:, pl.ds(pl.multiple_of(s * cols, cols), cols)],
                              w_all.at[s, :, pl.ds(0, cols)], local.at[1]),
        pltpu.make_async_copy(routes, zroutes.at[c], local.at[2]),
        pltpu.make_async_copy(router, router_all.at[:, pl.ds(pl.multiple_of(s * wr, wr), wr)], local.at[3]),
        pltpu.make_async_copy(cot, zcot.at[c], local.at[4]),
    ]
    for item in copies:
        item.start()
    head = pl.ds(pl.multiple_of(lax.div(s, sharers) * HEAD_DIM, HEAD_DIM), HEAD_DIM)
    for kind, ref in enumerate((key_w, value_w)):
        own_head = pltpu.make_async_copy(ref.at[:, head], w_all.at[s, :, pl.ds(cols, HEAD_DIM)], local.at[5])

        @pl.when(parity == kind)
        def _(own_head=own_head):
            own_head.start()

    copies[2].wait()
    for d in route_fan.order():
        route_fan.arrival(d)
    before = (
        lax.broadcasted_iota(jnp.int32, (count, count), 0) < lax.broadcasted_iota(jnp.int32, (count, count), 1)
    ).astype(BF)
    for layer in range(n_ctx):
        named = zroutes[layer]
        mask = jnp.concatenate(
            [jnp.max((named == c * n_shard + e).astype(F32), axis=0, keepdims=True) for e in range(n_shard)], axis=0
        )
        rank = jnp.dot(mask.astype(BF), before, preferred_element_type=F32)
        at = layer % group
        code[layer // group, :, at * count : (at + 1) * count] = jnp.where(
            mask > 0, rank + float(at * capacity), -1.0
        )

    for d in range(1, chips):
        first[d - 1].wait()
        origin = lax.rem(s + n_shard - 2 * d, n_shard)
        item = push(rows_all.at[origin], rows_all.at[origin], ss_fwd.at[d], rs_fwd.at[d], shard=sibling)
        item.start()
        waits.append(item)
    for d in cot_fan.order():
        cot_fan.arrival(d)
    copies[4].wait()
    for k in range(groups):
        table = slot_table(code[k], slots)

        @pl.loop(0, width // tile)
        def _(j):
            part = pl.ds(pl.multiple_of(j * tile, tile), tile)
            block = zcot[k * group : (k + 1) * group, :, part].reshape(group * count, tile)
            value = jnp.dot(table, block, preferred_element_type=F32).astype(BF)
            ready[k, :, :, part] = value.reshape(n_shard, slots, tile)

    place = by_core(s, n_shard) if paired else s
    cot_waits = []
    for k in range(groups):
        for i, peer in enumerate(others):
            item = push(ready.at[k, peer], cot_rows.at[k, place], ss_x.at[k, i], rs_x.at[k, i], shard=peer)
            item.start()
            cot_waits.append(item)
        item = pltpu.make_async_copy(ready.at[k, s], cot_rows.at[k, place], local.at[6 + k])
        item.start()
        cot_waits.append(item)

    for item in waits + w_waits:
        item.wait()
    copies[0].wait()
    copies[1].wait()
    copies[3].wait()
    own_head.wait()
    outs = [
        pltpu.make_async_copy(rows_all, rows_out, out_sem.at[0]),
        pltpu.make_async_copy(w_all, w_all_out, out_sem.at[1]),
    ]
    outs[0].start()
    outs[1].start()

    right = w_all[:, :, pl.ds(cols, HEAD_DIM)].reshape(width, HEAD_DIM)

    @pl.loop(0, n_shard)
    def _(b):
        pre = jnp.dot(rows_all[b], right, preferred_element_type=F32)
        kvpre[b] = pre
        keyed, unused = unit_rows(pre)
        keyed = turn(keyed * k_gain[...], cosine[...], sine[...])
        kv[parity, b, c] = jnp.where(parity == 0, keyed, pre).astype(BF)

    fan = Fan(n_ctx, c, lambda d: kv.at[parity, :, flip_bits(c, d)], ss_kz, rs_kz, False)
    fan.send(0, kv.at[parity, :, c])
    kv_waits = []
    item = push(kv.at[parity, :, c], kv.at[parity, :, c], ss_kf.at[0], rs_kf.at[0], shard=sibling)
    item.start()
    kv_waits.append(item)

    @pl.loop(0, n_shard // 2)
    def _(b):
        left = rows_all[pl.ds(b * 2, 2)].reshape(2 * count, width)
        pre = jnp.dot(left, w_all[:, :, pl.ds(0, cols)].reshape(width, cols), preferred_element_type=F32)
        qpre[pl.ds(b * 2, 2)] = pre.reshape(2, count, cols)
        for i in range(2):
            for h in range(heads):
                part = pre[i * count : (i + 1) * count, h * HEAD_DIM : (h + 1) * HEAD_DIM]
                unit, unused = unit_rows(part)
                q[b * 2 + i, :, h * HEAD_DIM : (h + 1) * HEAD_DIM] = turn(
                    unit * q_gain[...], cosine[...], sine[...]
                ).astype(BF)

    for d in fan.order():
        fan.arrival(d)
        block = kv.at[parity, :, flip_bits(c, d)]
        item = push(block, block, ss_kf.at[d], rs_kf.at[d], shard=sibling)
        item.start()
        kv_waits.append(item)
    outs += [pltpu.make_async_copy(qpre, qpre_out, out_sem.at[2]), pltpu.make_async_copy(q, q_out, out_sem.at[3])]
    outs[2].start()
    outs[3].start()
    for item in kv_waits:
        item.wait()
    fan.drain()
    outs.append(pltpu.make_async_copy(kv, kv_out, out_sem.at[4]))
    outs[4].start()

    near, far = {}, {}
    order = list(range(1, chips)) + [0]

    def product(at):
        d = order[at]
        first_seq = 2 * lax.rem(chip + d, chips)

        @pl.loop(0, 2)
        def _(i):
            b = first_seq + i
            k_all = kv[0, b].reshape(keys, HEAD_DIM)
            v_all = kv[1, b].reshape(keys, HEAD_DIM)
            for h in range(heads):
                hs = slice(h * HEAD_DIM, (h + 1) * HEAD_DIM)
                scores = lax.dot_general(q[b, :, hs], k_all, (((1,), (1,)), ((), ())), preferred_element_type=F32)
                scores = scores * (HEAD_DIM ** -0.5) + bias[...]
                raised = jnp.exp(scores - jnp.max(scores, axis=-1, keepdims=True))
                probs = raised / jnp.sum(raised, axis=-1, keepdims=True)
                attn[b, :, hs] = jnp.dot(probs.astype(BF), v_all, preferred_element_type=F32).astype(BF)

        left = attn[pl.ds(first_seq, 2)].reshape(2 * count, cols)

        @pl.loop(0, width // tile)
        def _(j):
            part = pl.ds(pl.multiple_of(j * tile, tile), tile)
            value = jnp.dot(left, w_out[:, part], preferred_element_type=F32)
            pair[...] = value.reshape(2, count, tile)
            own_part[at % 2, :, part] = pair[parity]
            to_sib[at, :, part] = pair[1 - parity].astype(BF)

        near[at] = push(to_sib.at[at], sib.at[at], ss_s.at[at], rs_s.at[at], shard=sibling)
        near[at].start()

    def chip_sum(at):
        near[at].wait()
        to_chip[at] = (own_part[at % 2] + sib[at].astype(F32)).astype(BF)
        far[at] = push(to_chip.at[at], got.at[at], ss_c.at[at], rs_c.at[at], shard=mates[order[at] - 1])
        far[at].start()

    for at in range(chips):
        product(at)
        if at:
            chip_sum(at - 1)
    outs.append(pltpu.make_async_copy(attn, attn_out, out_sem.at[5]))
    outs[5].start()
    near[chips - 1].wait()
    mid[...] = tokens[...].astype(F32) + own_part[(chips - 1) % 2] + sib[chips - 1].astype(F32)
    for at in range(chips - 1):
        far[at].wait()
        mid[...] += got[at].astype(F32)
    cot_fan.drain()
    route_fan.drain()
    for item in cot_waits + outs:
        item.wait()


def front(n_ctx, n_shard, group, capacity, kv_heads, paired, args, ident):
    tokens, gain, w_query, key_w, value_w, routes, router, cot = args[:8]
    n, z = n_shard, n_ctx
    count, width = tokens.shape
    wr, chips, groups, slots = w_query.shape[0], n_shard // 2, n_ctx // group, group * capacity
    cols = w_query.shape[1] // n
    heads = cols // HEAD_DIM
    sds = jax.ShapeDtypeStruct
    dma = lambda *shape: DMA(shape)
    return call(
        functools.partial(front_body, z, n, group, capacity, heads, kv_heads, paired, 512),
        [
            sds((n, count, width), BF), sds((n, wr, cols + HEAD_DIM), BF), sds((router.shape[0], width), BF),
            sds((groups, n, group * count), F32), sds((groups, n, slots, width), BF), sds((n, count, cols), F32),
            sds((n, count, HEAD_DIM), F32), sds((n, count, cols), BF), sds((2, n, z, count, HEAD_DIM), BF),
            sds((n, count, cols), BF), sds((count, width), F32),
        ],
        [VMEM, VMEM, ANY, ANY, ANY, VMEM, ANY, ANY] + [VMEM] * 6,
        [
            pltpu.VMEM((count, width), BF), pltpu.VMEM((n, count, width), BF), pltpu.VMEM((n, wr, cols + HEAD_DIM), BF),
            pltpu.VMEM((z,) + routes.shape, jnp.int32), pltpu.VMEM((z, count, width), BF),
            pltpu.VMEM((groups, n, slots, width), BF), pltpu.VMEM((n, count, cols), F32),
            pltpu.VMEM((n, count, cols), BF), pltpu.VMEM((2, n, z, count, HEAD_DIM), BF),
            pltpu.VMEM((n, count, cols), BF), pltpu.VMEM((2, count, width), F32), pltpu.VMEM((2, count, 512), F32),
            pltpu.VMEM((chips, count, width), BF), pltpu.VMEM((chips, count, width), BF),
            pltpu.VMEM((chips - 1, count, width), BF), pltpu.VMEM((chips - 1, count, width), BF),
            dma(6 + groups), dma(chips), dma(chips), dma(chips), dma(chips), dma(n - 1), dma(n - 1), dma(n - 1), dma(n - 1),
            dma(n - 1), dma(n - 1), dma(z), dma(z), dma(z), dma(z), dma(groups, n - 1), dma(groups, n - 1),
            dma(z), dma(z), dma(z), dma(z), dma(chips), dma(chips), dma(chips - 1), dma(chips - 1), dma(6),
        ],
        ident, args, mib=60,
        out_specs=[ANY, ANY, ANY, VMEM, ANY, ANY, VMEM, ANY, ANY, ANY, VMEM],
    )


def spread_body(n_shard, rows, rows_all, local, ss_row, rs_row, ss_fwd, rs_fwd):
    c, s, parity, sibling, others, layers = here(1, n_shard)
    chips = n_shard // 2
    mates = [lax.rem(s + 2 * d, n_shard) for d in range(1, chips)]
    greet(mates + [sibling], [])
    mine = pltpu.make_async_copy(rows, rows_all.at[s], local)
    mine.start()
    first, waits = [], []
    for d in range(1, chips):
        item = push(rows, rows_all.at[s], ss_row.at[d], rs_row.at[d], shard=mates[d - 1])
        item.start()
        first.append(item)
    item = push(rows, rows_all.at[s], ss_fwd.at[0], rs_fwd.at[0], shard=sibling)
    item.start()
    waits.append(item)
    for d in range(1, chips):
        first[d - 1].wait()
        origin = lax.rem(s + n_shard - 2 * d, n_shard)
        item = push(rows_all.at[origin], rows_all.at[origin], ss_fwd.at[d], rs_fwd.at[d], shard=sibling)
        item.start()
        waits.append(item)
    mine.wait()
    for item in waits:
        item.wait()


def spread(n_shard, rows, ident):
    return call(
        functools.partial(spread_body, n_shard),
        [jax.ShapeDtypeStruct((n_shard,) + rows.shape, rows.dtype)],
        [ANY], [DMA] + [DMA((n_shard // 2,))] * 4, ident, (rows,),
    )[0]


def key_back_body(n_ctx, n_shard, parts, out, sib, zsend, zrecv, ss_s, rs_s, ss_z, rs_z):
    c, s, parity, sibling, others, layers = here(n_ctx, n_shard)
    greet([sibling], layers)
    order = list(range(1, n_ctx)) + [0]
    near = {}
    for d in order:
        block = parts.at[1 - parity, :, lax.rem(c + d, n_ctx)]
        near[d] = push(block, sib.at[d], ss_s.at[d], rs_s.at[d], shard=sibling)
        near[d].start()
    far = {}
    for d in order:
        near[d].wait()
        layer = lax.rem(c + d, n_ctx)
        value = parts[parity, :, layer].astype(F32) + sib[d].astype(F32)
        if d:
            zsend[d - 1] = value.astype(BF)
            far[d] = push(zsend.at[d - 1], zrecv.at[d - 1], ss_z.at[d], rs_z.at[d], ctx=layer)
            far[d].start()
    for d in range(1, n_ctx):
        far[d].wait()
        value = value + zrecv[d - 1].astype(F32)
    out[...] = value


def key_back(n_ctx, n_shard, parts, ident):
    block = (parts.shape[1], parts.shape[3], parts.shape[4])
    return call(
        functools.partial(key_back_body, n_ctx, n_shard),
        [jax.ShapeDtypeStruct(block, F32)],
        [VMEM],
        [
            pltpu.VMEM((n_ctx,) + block, BF), pltpu.VMEM((n_ctx - 1,) + block, BF),
            pltpu.VMEM((n_ctx - 1,) + block, BF),
        ] + [DMA((n_ctx,))] * 4,
        ident, (parts,), out_specs=[VMEM],
    )[0]


def finish_body(n_ctx, n_shard, q_cols, tile,
                weights, wide, router, gains, left, right, tokens, gain,
                q_out, kv_out, wide_out, router_out, gains_out, rows_out,
                wide_landing, wide_acc, wide_total, ss_wi, rs_wi, ss_wo, ss_wc, pieces, landing, acc, total, router_in, router_mid, router_far,
                gains_own, gains_in, gains_mid, gains_far, pair, own_part, to_sib, sib, to_chip, got,
                local, ss_w, rs_w, ss_i, rs_i, ss_o, ss_q, ss_k, ss_r, rs_r, ss_g, rs_g, ss_h, rs_h,
                ss_t, rs_t, ss_s, rs_s, ss_c, rs_c):
    c, s, parity, sibling, others, layers = here(n_ctx, n_shard)
    half = n_ctx // 2
    chips = n_shard // 2
    chip = lax.div(s, 2)
    mates = [lax.rem(s + 2 * d, n_shard) for d in range(1, chips)]
    left_side = c < half
    depth = jnp.where(left_side, c, n_ctx - 1 - c)
    inner = jnp.where(left_side, c + 1, c - 1)
    outer = jnp.clip(jnp.where(left_side, c - 1, c + 1), 0, n_ctx - 1)
    middle = depth == half - 1
    inside = depth > 0
    rows, width = rows_out.shape
    greet(others, layers)
    sends, small = [None], []
    for i, peer in enumerate(others):
        item = push(weights.at[peer], pieces.at[i + 1], ss_w.at[i], rs_w.at[i], shard=peer)
        item.start()
        sends.append(item)
    for i, peer in enumerate(others):
        item = push(router.at[peer], router_in.at[i], ss_r.at[i], rs_r.at[i], shard=peer)
        item.start()
        small.append(item)

    def out_copies(j, ref):
        source = lax.rem(s + n_shard - j, n_shard)
        cols = pl.ds(pl.multiple_of(source * q_cols, q_cols), q_cols)
        return (
            pltpu.make_async_copy(ref.at[:, pl.ds(0, q_cols)], q_out.at[:, cols], ss_q.at[j]),
            pltpu.make_async_copy(ref.at[:, pl.ds(q_cols, 128)], kv_out.at[source], ss_k.at[j]),
        )

    def wide_copies(j, ref):
        return (pltpu.make_async_copy(ref, wide_out.at[j], ss_wc.at[j]),)

    class Line:
        def __init__(self, ready, own, acc, landing, total, ss_i, rs_i, ss_o, copies):
            self.ready, self.own, self.acc, self.landing, self.total = ready, own, acc, landing, total
            self.ss_i, self.rs_i, self.ss_o, self.copies = ss_i, rs_i, ss_o, copies

        def inward(self, j, ref):
            at = jnp.where(middle, 1, 0)
            return push(ref, self.landing.at[at, j], self.ss_i.at[j], self.rs_i.at[at, j], ctx=inner)

        def outward(self, j):
            return push(self.total.at[j], self.landing.at[1, j], self.ss_o.at[j], self.rs_i.at[1, j], ctx=outer)

        def arrived(self, which, j):
            push(self.acc.at[j], self.landing.at[which, j], self.ss_i.at[j], self.rs_i.at[which, j],
                 ctx=inner).wait_recv()

        def outermost(self, j):
            @pl.when(jnp.logical_not(inside))
            def _():
                self.ready(j)
                self.inward(j, self.own(j)).start()

        def first_half(self, j):
            @pl.when(inside)
            def _():
                self.ready(j)
                self.arrived(0, j)
                self.acc[j] = (self.own(j)[...].astype(F32) + self.landing[0, j].astype(F32)).astype(BF)
                self.inward(j, self.acc.at[j]).start()

        def second_half(self, j):
            self.arrived(1, j)

            @pl.when(middle)
            def _():
                self.total[j] = (self.acc[j].astype(F32) + self.landing[1, j].astype(F32)).astype(BF)

            @pl.when(jnp.logical_not(middle))
            def _():
                self.total[j] = self.landing[1, j]

            @pl.when(inside)
            def _():
                self.outward(j).start()

            for item in self.copies(j, self.total.at[j]):
                item.start()

        def drain(self, j):
            self.inward(j, self.acc.at[j]).wait_send()

            @pl.when(inside)
            def _():
                self.outward(j).wait_send()

            for item in self.copies(j, self.total.at[j]):
                item.wait()

    line = Line(lambda j: sends[j].wait() if j else None, lambda j: pieces.at[j] if j else weights.at[s],
                acc, landing, total, ss_i, rs_i, ss_o, out_copies)
    wide_line = Line(lambda j: None, lambda j: wide.at[j], wide_acc, wide_landing, wide_total,
                     ss_wi, rs_wi, ss_wo, wide_copies)
    wides = wide.shape[0]
    steps = [(wide_line, j) for j in range(wides)] + [(line, j) for j in range(n_shard)]

    near, far = {}, {}

    def product(d):
        first = pl.multiple_of(lax.rem(chip + d, chips) * (2 * rows), 2 * rows)

        @pl.loop(0, width // tile)
        def _(j):
            cols = pl.ds(pl.multiple_of(j * tile, tile), tile)
            value = lax.dot_general(left[pl.ds(first, 2 * rows), :], right[cols, :],
                                    (((1,), (1,)), ((), ())), preferred_element_type=F32)
            pair[...] = value.reshape(2, rows, tile)
            own_part[d, :, cols] = pair[parity]
            to_sib[d, :, cols] = pair[1 - parity].astype(BF)

        near[d] = push(to_sib.at[d], sib.at[d], ss_s.at[d], rs_s.at[d], shard=sibling)
        near[d].start()

    def chip_sum(d):
        near[d].wait()
        to_chip[d - 1] = (own_part[d] + sib[d].astype(F32)).astype(BF)
        far[d] = push(to_chip.at[d - 1], got.at[d - 1], ss_c.at[d - 1], rs_c.at[d - 1], shard=mates[d - 1])
        far[d].start()

    gain_sends = []

    def last_sum():
        near[0].wait()
        grad = own_part[0] + sib[0].astype(F32)
        for d in range(1, chips):
            far[d].wait()
            grad = grad + got[d - 1].astype(F32)
        x = tokens[...].astype(F32)
        scale = lax.rsqrt(jnp.mean(x * x, axis=-1, keepdims=True) + epsilon)
        unit = x * scale
        scaled = grad * gain[...]
        rows_out[...] = scale * (scaled - unit * jnp.mean(scaled * unit, axis=-1, keepdims=True))
        gains_own[...] = gains[...]
        gains_own[0:1] = jnp.sum(grad * unit, axis=0, keepdims=True)
        mine = pltpu.make_async_copy(gains_own, gains_in.at[s], local.at[0])
        mine.start()
        gain_sends.append(mine)
        for i, peer in enumerate(others):
            item = push(gains_own, gains_in.at[s], ss_g.at[i], rs_g.at[i], shard=peer)
            item.start()
            gain_sends.append(item)

    def small_plane():
        for item in small + gain_sends:
            item.wait()
        gains_mid[...] = gains_in[0]
        for i in range(1, n_shard):
            gains_mid[...] += gains_in[i]
        router_mid[...] = router[s].astype(F32)
        for i in range(n_shard - 1):
            router_mid[...] += router_in[i].astype(F32)
        for i, layer in enumerate(layers):
            push(gains_mid, gains_far.at[c], ss_h.at[i], rs_h.at[i], ctx=layer).start()
            push(router_mid, router_far.at[c], ss_t.at[i], rs_t.at[i], ctx=layer).start()
        pltpu.make_async_copy(gains_mid, gains_far.at[c], local.at[1]).start()
        pltpu.make_async_copy(router_mid, router_far.at[c], local.at[2]).start()

    def small_all():
        pltpu.make_async_copy(gains_mid, gains_far.at[c], local.at[1]).wait()
        pltpu.make_async_copy(router_mid, router_far.at[c], local.at[2]).wait()
        for i, layer in enumerate(layers):
            push(gains_mid, gains_far.at[c], ss_h.at[i], rs_h.at[i], ctx=layer).wait()
            push(router_mid, router_far.at[c], ss_t.at[i], rs_t.at[i], ctx=layer).wait()
        gains_out[...] = gains_far[0]
        router_out[...] = router_far[0]
        for i in range(1, n_ctx):
            gains_out[...] += gains_far[i]
            router_out[...] += router_far[i]

    lag, ahead = 2, 6
    for which, j in steps[:ahead]:
        which.outermost(j)
    for d in list(range(1, chips)) + [0]:
        product(d)
    side = [functools.partial(chip_sum, d) for d in range(1, chips)] + [last_sum, small_plane]
    for n in range(len(steps) + lag):
        if n + ahead < len(steps):
            steps[n + ahead][0].outermost(steps[n + ahead][1])
        if n < len(steps):
            steps[n][0].first_half(steps[n][1])
        if n >= lag:
            steps[n - lag][0].second_half(steps[n - lag][1])
        if n >= 2 and side:
            side.pop(0)()
    for job in side:
        job()
    small_all()
    for which, j in steps:
        which.drain(j)


def finish(n_ctx, n_shard, q_cols, weights, wide, router, gains, left, right, tokens, gain, ident):
    n, rows, cols = weights.shape
    router_shape = router.shape[1:]
    count, width = tokens.shape
    chips = n // 2
    tile = 512
    wides = wide.shape[0]
    return call(
        functools.partial(finish_body, n_ctx, n, q_cols, tile),
        [
            jax.ShapeDtypeStruct((rows, n * q_cols), BF), jax.ShapeDtypeStruct((n, rows, 128), BF),
            jax.ShapeDtypeStruct(wide.shape, BF),
            jax.ShapeDtypeStruct(router_shape, F32), jax.ShapeDtypeStruct(gains.shape, F32),
            jax.ShapeDtypeStruct((count, width), F32),
        ],
        [VMEM] * 8,
        [
            pltpu.VMEM((2,) + wide.shape, BF), pltpu.VMEM(wide.shape, BF), pltpu.VMEM(wide.shape, BF),
            DMA((wides,)), DMA((2, wides)), DMA((wides,)), DMA((wides,)),
            pltpu.VMEM((n, rows, cols), BF), pltpu.VMEM((2, n, rows, cols), BF),
            pltpu.VMEM((n, rows, cols), BF), pltpu.VMEM((n, rows, cols), BF),
            pltpu.VMEM((n - 1,) + router_shape, BF), pltpu.VMEM(router_shape, F32),
            pltpu.VMEM((n_ctx,) + router_shape, F32),
            pltpu.VMEM(gains.shape, F32), pltpu.VMEM((n,) + gains.shape, F32),
            pltpu.VMEM(gains.shape, F32), pltpu.VMEM((n_ctx,) + gains.shape, F32),
            pltpu.VMEM((2, count, tile), F32), pltpu.VMEM((chips, count, width), F32),
            pltpu.VMEM((chips, count, width), BF), pltpu.VMEM((chips, count, width), BF),
            pltpu.VMEM((chips - 1, count, width), BF), pltpu.VMEM((chips - 1, count, width), BF),
            DMA((3,)), DMA((n - 1,)), DMA((n - 1,)), DMA((n,)), DMA((2, n)), DMA((n,)),
            DMA((n,)), DMA((n,)), DMA((n - 1,)), DMA((n - 1,)), DMA((n - 1,)), DMA((n - 1,)),
            DMA((n_ctx - 1,)), DMA((n_ctx - 1,)), DMA((n_ctx - 1,)), DMA((n_ctx - 1,)),
            DMA((chips,)), DMA((chips,)), DMA((chips - 1,)), DMA((chips - 1,)),
        ],
        ident, (weights, wide, router, gains, left, right, tokens, gain), mib=60,
        out_specs=[ANY, ANY, ANY, VMEM, VMEM, VMEM],
    )


def back_body(n_ctx, n_shard, group, heads, wides,
              grad_out, q_in, kv_in, attn_in, qpre_in, kvpre_in, w_out_in, rows_in, w_all_in, cosine, sine, bias, q_gain, k_gain,
              tokens, gain, gains, router, mix_near, mix_part, code,
              q_out, kv_out, wide_out, router_out, gains_out, rows_out, mix_out, mix_land,
              q, kv, attn, qpre, kvpre, w_out, w_all, loads, grads, attn_t, grad_heads, ds_all, p_all, parts, pre, q_sum, k_sum, wide, weights,
              sibk, zsend, zrecv, wide_landing, pieces, landing,
              own_part, pair, to_sib, sib, to_chip, got, router_in, router_mid, router_far,
              gains_own, gains_in, gains_mid, gains_far, mix_rows, mix_sent, mix_recv, local,
              ss_row, rs_row, ss_fwd, rs_fwd, ss_sk, rs_sk, ss_zk, rs_zk,
              ss_wi, rs_wi, ss_wo, ss_wc, ss_w, rs_w, ss_i, rs_i, ss_o, ss_q, ss_k,
              ss_r, rs_r, ss_g, rs_g, ss_h, rs_h, ss_t, rs_t, ss_s, rs_s, ss_c, rs_c, ss_m, rs_m, ss_f, rs_f, ss_v, rs_v):
    c, s, parity, sibling, others, layers = here(n_ctx, n_shard)
    half = n_ctx // 2
    chips = n_shard // 2
    chip = lax.div(s, 2)
    mates = [lax.rem(s + 2 * d, n_shard) for d in range(1, chips)]
    left_side = c < half
    depth = jnp.where(left_side, c, n_ctx - 1 - c)
    inner = jnp.where(left_side, c + 1, c - 1)
    outer = jnp.clip(jnp.where(left_side, c - 1, c + 1), 0, n_ctx - 1)
    middle = depth == half - 1
    inside = depth > 0
    count, width = tokens.shape
    wr = w_all.shape[1]
    cols = heads * HEAD_DIM
    keys = n_ctx * count
    scaling = HEAD_DIM ** -0.5
    own_copies = [
        pltpu.make_async_copy(grad_out, grads.at[s], local.at[0]),
        pltpu.make_async_copy(rows_in, grads, local.at[1]),
    ]
    own_copies[0].start()
    load = [
        pltpu.make_async_copy(a, b, loads.at[n])
        for n, (a, b) in enumerate(((q_in, q), (kv_in, kv), (w_out_in, w_out), (qpre_in, qpre), (attn_in, attn),
                                    (kvpre_in, kvpre), (w_all_in, w_all)))
    ]
    greet(others, layers)

    first, forwards = {}, {}
    for d in range(1, chips):
        first[d] = push(grad_out, grads.at[s], ss_row.at[d], rs_row.at[d], shard=mates[d - 1])
        first[d].start()
    forwards[0] = push(grad_out, grads.at[s], ss_fwd.at[0], rs_fwd.at[0], shard=sibling)
    forwards[0].start()
    for item in load:
        item.start()
    small = []
    for i, peer in enumerate(others):
        item = push(router.at[peer], router_in.at[i], ss_r.at[i], rs_r.at[i], shard=peer)
        item.start()
        small.append(item)
    q_sum[...] = jnp.zeros_like(q_sum)
    k_sum[...] = jnp.zeros_like(k_sum)

    def norm_back(grad, value, norm_gain, total):
        unit, scale = unit_rows(value)
        grad = grad * cosine[...] + pltpu.roll(grad * sine[...], HEAD_DIM // 2, 1)
        total[...] += jnp.sum(grad * unit, axis=0, keepdims=True)
        scaled = grad * norm_gain[...]
        return scale * (scaled - unit * jnp.mean(scaled * unit, axis=-1, keepdims=True))

    slots = mix_near.shape[1]
    mix_fold = Fold(c, mix_sent, mix_recv, ss_f, rs_f)
    tile = mix_rows.shape[2]

    def mix_sums(k, ref):
        table = slot_table(code[flip_bits(lax.div(c, group), k)], slots).T

        @pl.loop(0, width // tile)
        def _(j):
            part = pl.ds(pl.multiple_of(j * tile, tile), tile)
            item = pltpu.make_async_copy(ref.at[:, :, part], mix_rows, local.at[5])
            item.start()
            item.wait()
            value = jnp.dot(table, mix_rows[...].reshape(n_shard * slots, tile), preferred_element_type=F32)
            own_part[:, :, part] = value.reshape(2, count, tile)

    def near_part(d):
        return own_part[lax.rem(flip_bits(c, d), group)]

    def mix_send():
        for i, peer in enumerate(others):
            push(mix_near.at[by_core(peer, n_shard)], mix_land.at[s], ss_m.at[i], rs_m.at[i], shard=peer).start()
        pltpu.make_async_copy(mix_near.at[by_core(s, n_shard)], mix_land.at[s], local.at[6]).start()

    def mix_last():
        for i, peer in enumerate(others):
            push(mix_near.at[by_core(peer, n_shard)], mix_land.at[s], ss_m.at[i], rs_m.at[i], shard=peer).wait()
        pltpu.make_async_copy(mix_near.at[by_core(s, n_shard)], mix_land.at[s], local.at[6]).wait()
        mix_sums(0, mix_land)
        mix_fold.give(1, near_part(1))
        mix_out[...] = near_part(0)

    mix_fold.give_as_is(3, mix_part.at[1])
    near, far = {}, {}

    def seqs_of(d):
        return 2 * lax.rem(chip + chips - d, chips)

    def attention_back(d):
        fs = seqs_of(d)
        grad = lax.dot_general(grads[pl.ds(fs, 2)].reshape(2 * count, width), w_out[...],
                               (((1,), (1,)), ((), ())), preferred_element_type=F32)
        grad_heads[...] = grad.reshape(2, count, cols).astype(BF)

        @pl.loop(0, 2)
        def _(i):
            b = fs + i
            k_all = kv[0, b].reshape(keys, HEAD_DIM)
            v_all = kv[1, b].reshape(keys, HEAD_DIM)
            for h in range(heads):
                hs = slice(h * HEAD_DIM, (h + 1) * HEAD_DIM)
                rs = slice(h * count, (h + 1) * count)
                scores = lax.dot_general(q[b, :, hs], k_all, (((1,), (1,)), ((), ())), preferred_element_type=F32)
                scores = scores * scaling + bias[...]
                raised = jnp.exp(scores - jnp.max(scores, axis=-1, keepdims=True))
                probs = raised / jnp.sum(raised, axis=-1, keepdims=True)
                grad_p = lax.dot_general(grad_heads[i, :, hs], v_all, (((1,), (1,)), ((), ())),
                                         preferred_element_type=F32)
                delta = jnp.sum(probs * grad_p, axis=-1, keepdims=True)
                ds = (probs * (grad_p - delta)).astype(BF)
                ds_all[rs, :] = ds
                p_all[rs, :] = probs.astype(BF)
                grad_q = jnp.dot(ds, k_all, preferred_element_type=F32) * scaling
                pre[b, :, hs] = norm_back(grad_q, qpre[b, :, hs], q_gain, q_sum).astype(BF)
            grad_k, grad_v = jnp.zeros((keys, HEAD_DIM), F32), jnp.zeros((keys, HEAD_DIM), F32)
            stacked_q = jnp.concatenate([q[b, :, h * HEAD_DIM : (h + 1) * HEAD_DIM] for h in range(heads)], axis=0)
            stacked_g = jnp.concatenate(
                [grad_heads[i, :, h * HEAD_DIM : (h + 1) * HEAD_DIM] for h in range(heads)], axis=0
            )
            grad_k = lax.dot_general(ds_all[...], stacked_q, (((0,), (0,)), ((), ())), preferred_element_type=F32)
            grad_v = lax.dot_general(p_all[...], stacked_g, (((0,), (0,)), ((), ())), preferred_element_type=F32)
            parts[0, b] = (grad_k * scaling).astype(BF).reshape(n_ctx, count, HEAD_DIM)
            parts[1, b] = grad_v.astype(BF).reshape(n_ctx, count, HEAD_DIM)

        near[d] = push(parts.at[1 - parity, pl.ds(fs, 2)], sibk.at[d], ss_sk.at[d], rs_sk.at[d], shard=sibling)
        near[d].start()

    def key_sum(d):
        fs = seqs_of(d)
        near[d].wait()
        for i, layer in enumerate(layers):
            zsend[d, i] = (
                parts[parity, pl.ds(fs, 2), layer].astype(F32) + sibk[d, :, layer].astype(F32)
            ).astype(BF)
            far[d, i] = push(zsend.at[d, i], zrecv.at[d, i], ss_zk.at[d, i], rs_zk.at[d, i], ctx=layer)
            far[d, i].start()

    def half_rows(j):
        return pl.ds((j % 2) * (wr // 2), wr // 2)

    def out_copies(j, ref):
        source = lax.rem(s + n_shard - j // 2, n_shard)
        to = pl.ds(pl.multiple_of(source * cols, cols), cols)
        return (
            pltpu.make_async_copy(ref.at[:, pl.ds(0, cols)], q_out.at[half_rows(j), to], ss_q.at[j]),
            pltpu.make_async_copy(ref.at[:, pl.ds(cols, HEAD_DIM)], kv_out.at[source, half_rows(j)], ss_k.at[j]),
        )

    def wide_copies(j, ref):
        step = wide.shape[2]
        return (pltpu.make_async_copy(ref, wide_out.at[:, pl.ds(j * step, step)], ss_wc.at[j]),)

    class Line:
        def __init__(self, ready, own, landing, ss_i, rs_i, ss_o, copies):
            self.ready, self.own, self.landing = ready, own, landing
            self.ss_i, self.rs_i, self.ss_o, self.copies = ss_i, rs_i, ss_o, copies

        def inward(self, j, ref):
            at = jnp.where(middle, 1, 0)
            return push(ref, self.landing.at[at, j], self.ss_i.at[j], self.rs_i.at[at, j], ctx=inner)

        def outward(self, j):
            return push(self.landing.at[1, j], self.landing.at[1, j], self.ss_o.at[j], self.rs_i.at[1, j], ctx=outer)

        def arrived(self, which, j):
            push(self.landing.at[0, j], self.landing.at[which, j], self.ss_i.at[j], self.rs_i.at[which, j],
                 ctx=inner).wait_recv()

        def outermost(self, j):
            @pl.when(jnp.logical_not(inside))
            def _():
                self.ready(j)
                self.inward(j, self.own(j)).start()

        def first_half(self, j):
            @pl.when(inside)
            def _():
                self.ready(j)
                self.arrived(0, j)
                self.landing[0, j] = (self.own(j)[...].astype(F32) + self.landing[0, j].astype(F32)).astype(BF)
                self.inward(j, self.landing.at[0, j]).start()

        def second_half(self, j):
            self.arrived(1, j)

            @pl.when(middle)
            def _():
                self.landing[1, j] = (self.landing[0, j].astype(F32) + self.landing[1, j].astype(F32)).astype(BF)

            @pl.when(inside)
            def _():
                self.outward(j).start()

            for item in self.copies(j, self.landing.at[1, j]):
                item.start()

        def drain(self, j):
            self.inward(j, self.landing.at[0, j]).wait_send()

            @pl.when(inside)
            def _():
                self.outward(j).wait_send()

            for item in self.copies(j, self.landing.at[1, j]):
                item.wait()

    sends = [[] for j in range(n_shard)]
    line = Line(lambda j: [item.wait() for item in sends[j // 2]] if j % 2 == 0 else None,
                lambda j: pieces.at[j // 2, half_rows(j)] if j >= 2 else weights.at[s, half_rows(j)],
                landing, ss_i, rs_i, ss_o, out_copies)
    wide_line = Line(lambda j: None, lambda j: wide.at[j], wide_landing, ss_wi, rs_wi, ss_wo, wide_copies)
    steps = [(wide_line, j) for j in range(wides)] + [(line, j) for j in range(2 * n_shard)]
    lag, ahead = 2, 6

    def advance(n):
        if n + ahead < len(steps):
            steps[n + ahead][0].outermost(steps[n + ahead][1])
        if n < len(steps):
            steps[n][0].first_half(steps[n][1])
        if n >= lag:
            steps[n - lag][0].second_half(steps[n - lag][1])

    step = width // wides
    for item in load[:4]:
        item.wait()
    for d in range(chips):
        if d:
            first[d].wait()
            origin = lax.rem(s + n_shard - 2 * d, n_shard)
            forwards[d] = push(grads.at[origin], grads.at[origin], ss_fwd.at[d], rs_fwd.at[d], shard=sibling)
            forwards[d].start()
        else:
            own_copies[0].wait()
        forwards[d].wait()
        if d + 1 == chips:
            mix_send()
            for item in load[4:]:
                item.wait()
            attn_t[...] = attn[...].reshape(n_shard * count, cols).T
            for j in range(wides):
                block = grads[:, :, j * step : (j + 1) * step].reshape(n_shard * count, step)
                wide[j] = jnp.dot(attn_t[...], block, preferred_element_type=F32).astype(BF)
                if j < ahead:
                    wide_line.outermost(j)
        attention_back(d)
        if d == 0:
            mix_fold.give(2, mix_fold.take(2, mix_part[0].astype(F32)))
        if d:
            key_sum(d - 1)

    rows_all = grads
    own_copies[1].start()
    key_sum(chips - 1)
    advance(0)
    own_copies[1].wait()

    @pl.loop(0, n_shard)
    def _(e):
        block = rows_all[:, :, pl.ds(pl.multiple_of(e * wr, wr), wr)].reshape(n_shard * count, wr)
        right = pre[:, :, pl.ds(0, cols)].reshape(n_shard * count, cols)
        weights[e, :, pl.ds(0, cols)] = lax.dot_general(
            block, right, (((0,), (0,)), ((), ())), preferred_element_type=F32).astype(BF)

    for i, peer in enumerate(others):
        item = push(weights.at[peer, :, pl.ds(0, cols)], pieces.at[i + 1, :, pl.ds(0, cols)],
                    ss_w.at[i], rs_w.at[i], shard=peer)
        item.start()
        sends[i + 1].append(item)
    advance(1)
    for d in range(chips):
        fs = seqs_of(d)
        total = parts[parity, pl.ds(fs, 2), c].astype(F32) + sibk[d, :, c].astype(F32)
        for i in range(n_ctx - 1):
            far[d, i].wait()
            total = total + zrecv[d, i].astype(F32)
        for i in range(2):
            keyed = norm_back(total[i], kvpre[fs + i], k_gain, k_sum)
            pre[fs + i, :, pl.ds(cols, HEAD_DIM)] = jnp.where(parity == 0, keyed, total[i]).astype(BF)

    @pl.loop(0, n_shard)
    def _(e):
        block = rows_all[:, :, pl.ds(pl.multiple_of(e * wr, wr), wr)].reshape(n_shard * count, wr)
        right = pre[:, :, pl.ds(cols, HEAD_DIM)].reshape(n_shard * count, HEAD_DIM)
        weights[e, :, pl.ds(cols, HEAD_DIM)] = lax.dot_general(
            block, right, (((0,), (0,)), ((), ())), preferred_element_type=F32).astype(BF)

    for i, peer in enumerate(others):
        item = push(weights.at[peer, :, pl.ds(cols, HEAD_DIM)], pieces.at[i + 1, :, pl.ds(cols, HEAD_DIM)],
                    ss_v.at[i], rs_v.at[i], shard=peer)
        item.start()
        sends[i + 1].append(item)
    advance(2)

    order = list(range(1, chips)) + [0]
    to_sibling, to_mate = {}, {}

    def product(at):
        fs = 2 * lax.rem(chip + order[at], chips)
        left = pre[pl.ds(fs, 2)].reshape(2 * count, cols + HEAD_DIM)

        @pl.loop(0, n_shard)
        def _(j):
            part = pl.ds(pl.multiple_of(j * wr, wr), wr)
            value = lax.dot_general(left, w_all[j], (((1,), (1,)), ((), ())), preferred_element_type=F32)
            pair[...] = value.reshape(2, count, wr)
            own_part[at % 2, :, part] = pair[parity]
            to_sib[at, :, part] = pair[1 - parity].astype(BF)

        to_sibling[at] = push(to_sib.at[at], sib.at[at], ss_s.at[at], rs_s.at[at], shard=sibling)
        to_sibling[at].start()

    def chip_sum(at):
        to_sibling[at].wait()
        to_chip[at] = (own_part[at % 2] + sib[at].astype(F32)).astype(BF)
        to_mate[at] = push(to_chip.at[at], got.at[at], ss_c.at[at], rs_c.at[at], shard=mates[order[at] - 1])
        to_mate[at].start()

    gain_sends = []

    def last_sum():
        to_sibling[chips - 1].wait()
        grad = own_part[(chips - 1) % 2] + sib[chips - 1].astype(F32)
        for at in range(chips - 1):
            to_mate[at].wait()
            grad = grad + got[at].astype(F32)
        unit, scale = unit_rows(tokens[...].astype(F32))
        scaled = grad * gain[...]
        rows_out[...] = scale * (scaled - unit * jnp.mean(scaled * unit, axis=-1, keepdims=True))
        gains_own[...] = gains[...]
        summed = jnp.sum(grad * unit, axis=0, keepdims=True)
        lanes = gains.shape[1]
        for n in range(width // lanes):
            gains_own[n : n + 1] = summed[:, n * lanes : (n + 1) * lanes]
        n = 2 * width // lanes
        gains_own[n : n + 1] = q_sum[...]
        gains_own[n + 1 : n + 2] = jnp.where(parity == 0, k_sum[...], jnp.zeros_like(k_sum))
        mine = pltpu.make_async_copy(gains_own, gains_in.at[s], local.at[2])
        mine.start()
        gain_sends.append(mine)
        for i, peer in enumerate(others):
            item = push(gains_own, gains_in.at[s], ss_g.at[i], rs_g.at[i], shard=peer)
            item.start()
            gain_sends.append(item)

    def small_plane():
        for item in small + gain_sends:
            item.wait()
        gains_mid[...] = gains_in[0]
        for i in range(1, n_shard):
            gains_mid[...] += gains_in[i]
        total = router[s].astype(F32)
        for i in range(n_shard - 1):
            total = total + router_in[i].astype(F32)
        router_mid[...] = total.astype(BF)
        for i, layer in enumerate(layers):
            push(gains_mid, gains_far.at[c], ss_h.at[i], rs_h.at[i], ctx=layer).start()
            push(router_mid, router_far.at[c], ss_t.at[i], rs_t.at[i], ctx=layer).start()
        pltpu.make_async_copy(gains_mid, gains_far.at[c], local.at[3]).start()
        pltpu.make_async_copy(router_mid, router_far.at[c], local.at[4]).start()

    def small_all():
        pltpu.make_async_copy(gains_mid, gains_far.at[c], local.at[3]).wait()
        pltpu.make_async_copy(router_mid, router_far.at[c], local.at[4]).wait()
        for i, layer in enumerate(layers):
            push(gains_mid, gains_far.at[c], ss_h.at[i], rs_h.at[i], ctx=layer).wait()
            push(router_mid, router_far.at[c], ss_t.at[i], rs_t.at[i], ctx=layer).wait()
        gains_out[...] = gains_far[0]
        router_out[...] = router_far[0].astype(F32)
        for i in range(1, n_ctx):
            gains_out[...] += gains_far[i]
            router_out[...] += router_far[i].astype(F32)

    side = []
    for at in range(chips):
        side.append(functools.partial(product, at))
        if at:
            side.append(functools.partial(chip_sum, at - 1))
    count_steps = len(steps) + lag
    late = {21: last_sum, 23: mix_last, 26: small_plane}
    for n in range(3, count_steps):
        advance(n)
        if side:
            side.pop(0)()
        if n in late:
            late[n]()
    for job in side:
        job()
    small_all()
    mix_out[...] = mix_fold.take(0, mix_out[...])
    mix_fold.drain()
    for which, j in steps:
        which.drain(j)


def back(n_ctx, n_shard, group, heads, args, ident):
    count, width = args[0].shape
    rows_in, w_all, router, gains, mix_near = args[7], args[8], args[17], args[16], args[18]
    n, z, chips, wides = n_shard, n_ctx, n_shard // 2, 16
    wr, cols = w_all.shape[1], heads * HEAD_DIM
    keys = z * count
    sds, scratch = jax.ShapeDtypeStruct, pltpu.VMEM
    router_shape = router.shape[1:]
    dma = lambda *shape: DMA(shape)
    wide_block, block = (cols, width // wides), (wr, cols + HEAD_DIM)
    return call(
        functools.partial(back_body, z, n, group, heads, wides),
        [
            sds((wr, n * cols), BF), sds((n, wr, HEAD_DIM), BF), sds((cols, width), BF), sds(router_shape, F32),
            sds(gains.shape, F32), sds((count, width), F32), sds((count, width), F32), sds(mix_near.shape, BF),
        ],
        [VMEM] + [ANY] * 8 + [VMEM] * 9 + [ANY, VMEM, VMEM],
        [scratch(item.shape, item.dtype) for item in args[1:7] + args[8:9]] + [dma(7)] + [
            scratch((n, count, width), BF), scratch((cols, n * count), BF),
            scratch((2, count, cols), BF), scratch((heads * count, keys), BF), scratch((heads * count, keys), BF),
            scratch((2, n, z, count, HEAD_DIM), BF), scratch((n, count, cols + HEAD_DIM), BF),
            scratch((1, HEAD_DIM), F32), scratch((1, HEAD_DIM), F32),
            scratch((wides,) + wide_block, BF), scratch((n,) + block, BF),
            scratch((chips, 2, z, count, HEAD_DIM), BF), scratch((chips, z - 1, 2, count, HEAD_DIM), BF),
            scratch((chips, z - 1, 2, count, HEAD_DIM), BF), scratch((2, wides) + wide_block, BF),
            scratch((n,) + block, BF), scratch((2, 2 * n, wr // 2, cols + HEAD_DIM), BF),
            scratch((2, count, width), F32), scratch((2, count, wr), F32), scratch((chips, count, width), BF),
            scratch((chips, count, width), BF), scratch((chips - 1, count, width), BF),
            scratch((chips - 1, count, width), BF),
            scratch((n - 1,) + router_shape, BF), scratch(router_shape, BF), scratch((z,) + router_shape, BF),
            scratch(gains.shape, F32), scratch((n,) + gains.shape, F32), scratch(gains.shape, F32),
            scratch((z,) + gains.shape, F32), scratch((n, mix_near.shape[1], 512), BF),
            scratch((z - 1, count, width), BF), scratch((z - 1, count, width), BF), dma(7),
            dma(chips), dma(chips), dma(chips), dma(chips), dma(chips), dma(chips), dma(chips, z - 1), dma(chips, z - 1),
            dma(wides), dma(2, wides), dma(wides), dma(wides), dma(n - 1), dma(n - 1), dma(2 * n), dma(2, 2 * n), dma(2 * n),
            dma(2 * n), dma(2 * n), dma(n - 1), dma(n - 1), dma(n - 1), dma(n - 1), dma(z - 1), dma(z - 1), dma(z - 1), dma(z - 1),
            dma(chips), dma(chips), dma(chips - 1), dma(chips - 1), dma(n - 1), dma(n - 1), dma(z), dma(z), dma(n - 1), dma(n - 1),
        ],
        ident, args, mib=62, out_specs=[ANY, ANY, ANY, VMEM, VMEM, VMEM, VMEM, ANY],
    )


def dispatch_body(n_ctx, n_shard, group, tile, rows, tail, code, recv, tail_recv,
                  zrows, ztail, ready, tail_ready, local, ss_z, rs_z, ss_t, rs_t, ss_x, rs_x, ss_y, rs_y):
    c, s, parity, sibling, others, layers = here(n_ctx, n_shard)
    greet(others, layers)
    count, width = rows.shape
    groups = n_ctx // group
    slots = recv.shape[2]
    own = [pltpu.make_async_copy(rows, zrows.at[c], local.at[0]), pltpu.make_async_copy(tail, ztail.at[c], local.at[1])]
    fans = [
        Fan(n_ctx, c, lambda d: ztail.at[flip_bits(c, d)], ss_t, rs_t, True),
        Fan(n_ctx, c, lambda d: zrows.at[flip_bits(c, d)], ss_z, rs_z, True),
    ]
    fans[0].send(0, tail)
    fans[1].send(0, rows)
    for item in own:
        item.start()
    waits = []
    seen = set()
    for k in range(groups):
        at = flip_bits(lax.div(c, group), k)
        if k == 0:
            for item in own:
                item.wait()
        table = slot_table(code[at], slots)
        for d in fans[0].order():
            if d < (k + 1) * group and d not in seen:
                fans[0].arrival(d)
                fans[1].arrival(d)
                seen.add(d)
        first = pl.multiple_of(at * group, group)
        block = ztail[pl.ds(first, group)].reshape(group * count, -1)
        tail_ready[k] = jnp.dot(table, block, preferred_element_type=F32).astype(BF).reshape(n_shard, slots, -1)

        @pl.loop(0, width // tile)
        def _(j):
            cols = pl.ds(pl.multiple_of(j * tile, tile), tile)
            block = zrows[pl.ds(first, group), :, cols].reshape(group * count, tile)
            value = jnp.dot(table, block, preferred_element_type=F32).astype(BF)
            ready[k, :, :, cols] = value.reshape(n_shard, slots, tile)

        for i, peer in enumerate(others):
            item = push(ready.at[k, peer], recv.at[s, at], ss_x.at[k, i], rs_x.at[k, i], shard=peer)
            item.start()
            waits.append(item)
            item = push(tail_ready.at[k, peer], tail_recv.at[s, at], ss_y.at[k, i], rs_y.at[k, i], shard=peer)
            item.start()
            waits.append(item)
        item = pltpu.make_async_copy(ready.at[k, s], recv.at[s, at], local.at[2 * k + 2])
        item.start()
        waits.append(item)
        item = pltpu.make_async_copy(tail_ready.at[k, s], tail_recv.at[s, at], local.at[2 * k + 3])
        item.start()
        waits.append(item)
    for fan in fans:
        fan.drain()
    for item in waits:
        item.wait()


def dispatch_rows(n_ctx, n_shard, group, capacity, rows, tail, code, ident):
    groups, slots = code.shape[0], group * capacity
    count, width = rows.shape
    few = tail.shape[1]
    return call(
        functools.partial(dispatch_body, n_ctx, n_shard, group, 512),
        [
            jax.ShapeDtypeStruct((n_shard, groups, slots, width), BF),
            jax.ShapeDtypeStruct((n_shard, groups, slots, few), BF),
        ],
        [VMEM, VMEM, VMEM],
        [
            pltpu.VMEM((n_ctx, count, width), BF), pltpu.VMEM((n_ctx, count, few), BF),
            pltpu.VMEM((groups, n_shard, slots, width), BF), pltpu.VMEM((groups, n_shard, slots, few), BF),
            DMA((2 * groups + 2,)), DMA((n_ctx,)), DMA((n_ctx,)), DMA((n_ctx,)), DMA((n_ctx,)),
        ] + [DMA((groups, n_shard - 1))] * 4,
        ident, (rows, tail, code), mib=56,
    )


def combine_body(n_ctx, n_shard, group, tile, rows, tail, mix, code, out, tail_out, mix_out,
                 land, tail_land, value, tail_value, zsend, zrecv, tsend, trecv, msend, mrecv, mix_kept, table, local,
                 ss_x, rs_x, ss_y, rs_y, ss_z, rs_z, ss_t, rs_t, ss_m, rs_m):
    c, s, parity, sibling, others, layers = here(n_ctx, n_shard)
    greet(others, layers)
    count, width = out.shape
    groups = n_ctx // group
    slots = rows.shape[2]
    near = {}
    for k in reversed(range(groups)):
        at = flip_bits(lax.div(c, group), k)
        near[k] = []
        for i, peer in enumerate(others):
            item = push(rows.at[peer, at], land.at[k, s], ss_x.at[k, i], rs_x.at[k, i], shard=peer)
            item.start()
            near[k].append(item)
            item = push(tail.at[peer, at], tail_land.at[k, s], ss_y.at[k, i], rs_y.at[k, i], shard=peer)
            item.start()
            near[k].append(item)
        item = pltpu.make_async_copy(rows.at[s, at], land.at[k, s], local.at[k, 0])
        item.start()
        near[k].append(item)
        item = pltpu.make_async_copy(tail.at[s, at], tail_land.at[k, s], local.at[k, 1])
        item.start()
        near[k].append(item)
    for k in range(groups):
        table[k] = slot_table(code[flip_bits(lax.div(c, group), k)], slots).T

    def local_sums(k, block_of):
        @pl.loop(0, width // tile)
        def _(j):
            cols = pl.ds(pl.multiple_of(j * tile, tile), tile)
            value[:, cols] = jnp.dot(table[k], block_of(cols), preferred_element_type=F32)

    def part(ref, d):
        place = lax.rem(flip_bits(c, d), group)
        return ref[pl.ds(pl.multiple_of(place * count, count), count), :]

    def in_group(k):
        return sorted(range(k * group, (k + 1) * group), key=lambda d: (lowest(d) or n_ctx, d))

    mix_fold = Fold(c, msend, mrecv, ss_m, rs_m)
    for k in reversed(range(groups)):
        at = flip_bits(lax.div(c, group), k)
        local_sums(k, lambda cols: mix[:, at, :, cols].reshape(n_shard * slots, tile))
        for d in in_group(k):
            if lowest(d) == 1:
                mix_fold.give(d, part(value, d))
            else:
                mix_kept[d // 2] = part(value, d)
    fold = Fold(c, zsend, zrecv, ss_z, rs_z)
    tail_fold = Fold(c, tsend, trecv, ss_t, rs_t)
    for k in reversed(range(groups)):
        for item in near[k]:
            item.wait()
        local_sums(k, lambda cols: land[k, :, :, cols].reshape(n_shard * slots, tile))
        tail_value[...] = jnp.dot(
            table[k], tail_land[k].reshape(n_shard * slots, -1), preferred_element_type=F32
        )
        for d in in_group(k):
            if lowest(d) == 1:
                fold.give(d, part(value, d))
                tail_fold.give(d, part(tail_value, d))
        for d in in_group(k):
            if lowest(d) != 1:
                if d:
                    mix_fold.give(d, mix_fold.take(d, mix_kept[d // 2]))
                    fold.give(d, fold.take(d, part(value, d)))
                    tail_fold.give(d, tail_fold.take(d, part(tail_value, d)))
                else:
                    mix_out[...] = mix_fold.take(0, mix_kept[0])
                    out[...] = fold.take(0, part(value, 0))
                    tail_out[...] = tail_fold.take(0, part(tail_value, 0))
    for item in (mix_fold, fold, tail_fold):
        item.drain()


def combine_rows(n_ctx, n_shard, group, rows, tail, mix, code, ident):
    groups, slots, width = rows.shape[1:]
    few = tail.shape[3]
    count = code.shape[2] // group
    sds = jax.ShapeDtypeStruct
    return call(
        functools.partial(combine_body, n_ctx, n_shard, group, 512),
        [sds((count, width), F32), sds((count, few), F32), sds((count, width), F32)],
        [VMEM] * 4,
        [
            pltpu.VMEM((groups, n_shard, slots, width), BF), pltpu.VMEM((groups, n_shard, slots, few), BF),
            pltpu.VMEM((group * count, width), F32), pltpu.VMEM((group * count, few), F32),
            pltpu.VMEM((n_ctx - 1, count, width), BF), pltpu.VMEM((n_ctx - 1, count, width), BF),
            pltpu.VMEM((n_ctx - 1, count, few), BF), pltpu.VMEM((n_ctx - 1, count, few), BF),
            pltpu.VMEM((n_ctx - 1, count, width), BF), pltpu.VMEM((n_ctx - 1, count, width), BF),
            pltpu.VMEM((n_ctx // 2, count, width), F32), pltpu.VMEM((groups, group * count, n_shard * slots), BF),
            DMA((groups, 2)),
        ] + [DMA((groups, n_shard - 1))] * 4 + [DMA((n_ctx,))] * 6,
        ident, (rows, tail, mix, code), mib=60, out_specs=[VMEM] * 3,
    )


def expert_body(n_ctx, n_shard, group, half, tile,
                rows, tail, code, gate_in, up_in, down_in, cot_in,
                out, tail_out, mix_near, mix_far, mix_part, g_gate, g_up, g_down,
                w_gate, w_up, w_down, loaded, zrows, ztail, ready, tail_ready, recv, tail_recv, cot, back_rows, back_tail, land, tail_land,
                hidden, grad_gate, grad_up, work, slot_dot, table, tail_value,
                zrecv, tsend, trecv, stage, stage_d, local, ss_a, rs_a,
                ss_z, rs_z, ss_t, rs_t, ss_x, rs_x, ss_y, rs_y, ss_d, rs_d, ss_e, rs_e, ss_m, rs_m,
                ss_fz, rs_fz, ss_ft, rs_ft, ss_st, ss_sd):
    c, s, parity, sibling, others, layers = here(n_ctx, n_shard)
    count, width = rows.shape
    few = tail.shape[1]
    inner = w_gate.shape[1]
    groups = n_ctx // group
    slots = recv.shape[2]
    chunk = half * slots
    experts = n_ctx * n_shard
    expert = c * n_shard + s
    mine = by_core(s, n_shard)
    loads = [
        pltpu.make_async_copy(rows, zrows.at[c], local.at[0]),
        pltpu.make_async_copy(tail, ztail.at[c], local.at[1]),
    ] + [
        pltpu.make_async_copy(cot_in.at[flip_bits(lax.div(c, group), k)], cot.at[k], local.at[2 + 2 * groups + k])
        for k in range(groups)
    ]
    greet(others, layers)
    fan = Fan(n_ctx, c, lambda d: ztail.at[flip_bits(c, d)], ss_t, rs_t, True)
    fan.send(0, tail)
    near_layer, far_layer = flip_bits(c, 1), flip_bits(c, 2)
    sides = [slice(0, width // 2), slice(width // 2, width)]
    near = push(rows, zrows.at[c], ss_z.at[0], rs_z.at[0], ctx=near_layer)
    near.start()
    edge = jnp.logical_or(c == 0, c == n_ctx - 1)
    away = [push(rows.at[:, side], zrows.at[c, :, side], ss_z.at[1 + n], rs_z.at[1 + n], ctx=far_layer)
            for n, side in enumerate(sides)]
    passed = [push(zrows.at[far_layer, :, side], zrows.at[far_layer, :, side], ss_z.at[3 + n], rs_z.at[3 + n],
                   ctx=near_layer) for n, side in enumerate(sides)]

    @pl.when(jnp.logical_not(edge))
    def _():
        for item in away:
            item.start()

    loads += [
        pltpu.make_async_copy(a, b, loaded.at[n])
        for n, (a, b) in enumerate(((gate_in, w_gate), (up_in, w_up), (down_in, w_down)))
    ]
    loads[0].start()
    loads[1].start()

    sent = {0: [], 1: []}
    early = (slots // group) // 16 * 16
    place = lax.rem(c, group)
    early_at = pl.multiple_of(place * (slots - early), 16)
    late_at = pl.multiple_of((1 - place) * early, 16)

    def some_slots(rows_code, first, amount):
        places = (lax.broadcasted_iota(jnp.int32, (amount, rows_code.shape[1]), 0) + first).astype(F32)
        return jnp.concatenate(
            [(places == rows_code[e : e + 1, :]).astype(BF) for e in range(n_shard)], axis=0
        )

    own_code = code[lax.div(c, group), :, pl.ds(pl.multiple_of(place * count, count), count)]
    early_picks = some_slots(own_code, early_at, early)

    @pl.loop(0, width // tile)
    def _(j):
        cols = pl.ds(pl.multiple_of(j * tile, tile), tile)
        moved = jnp.dot(early_picks, rows[:, cols], preferred_element_type=F32).astype(BF)
        ready[0, :, pl.ds(early_at, early), cols] = moved.reshape(n_shard, early, tile)

    for i, peer in enumerate(others):
        sent[0].append(push(ready.at[0, peer, pl.ds(early_at, early)], recv.at[0, mine, pl.ds(early_at, early)],
                            ss_a.at[i], rs_a.at[i], shard=peer))
        sent[0][-1].start()
    for item in loads[2:]:
        item.start()
    loads[0].wait()
    loads[1].wait()
    near.wait_send()

    @pl.when(edge)
    def _():
        for item in away:
            item.start()

    near.wait_recv()
    for k in range(groups):
        at = flip_bits(lax.div(c, group), k)
        whole = slot_table(code[at], slots)
        table[k] = whole.T
        for d in (2, 3) if k else (1,):
            fan.arrival(d)
        first = pl.multiple_of(at * group, group)
        block = ztail[pl.ds(first, group)].reshape(group * count, few)
        tail_ready[k] = jnp.dot(whole, block, preferred_element_type=F32).astype(BF).reshape(n_shard, slots, few)
        amount = slots if k else slots - early
        begin = 0 if k else late_at
        span = pl.ds(begin, amount)
        picks = some_slots(code[at], begin, amount)
        for n, side in enumerate(sides if k else [slice(0, width)]):
            if k:
                if n == 0:
                    for m in range(2):
                        away[m].wait_recv()
                        passed[m].start()
                passed[n].wait_recv()

            @pl.loop(side.start // tile, side.stop // tile)
            def _(j):
                cols = pl.ds(pl.multiple_of(j * tile, tile), tile)
                block = zrows[pl.ds(first, group), :, cols].reshape(group * count, tile)
                moved = jnp.dot(picks, block, preferred_element_type=F32).astype(BF)
                ready[k, :, span, cols] = moved.reshape(n_shard, amount, tile)

            fresh = []
            for i, peer in enumerate(others):
                fresh.append(push(ready.at[k, peer, span, side], recv.at[k, mine, span, side],
                                  ss_x.at[k + n, i], rs_x.at[k + n, i], shard=peer))
            if n == 0:
                for i, peer in enumerate(others):
                    fresh.append(push(tail_ready.at[k, peer], tail_recv.at[k, mine], ss_y.at[k, i], rs_y.at[k, i], shard=peer))
                fresh.append(pltpu.make_async_copy(tail_ready.at[k, s], tail_recv.at[k, mine], local.at[3 + 2 * k]))
            if n == k:
                fresh.append(pltpu.make_async_copy(ready.at[k, s], recv.at[k, mine], local.at[2 + 2 * k]))
            for item in fresh:
                item.start()
            sent[k] += fresh
    fan.drain()
    for item in away + passed:
        item.wait_send()
    for item in loads[2:]:
        item.wait()

    gate_pre, up_pre = work.at[0:chunk, 0:inner], work.at[0:chunk, inner : 2 * inner]
    value = work.at[0 : group * count, 0:width]
    column = lax.broadcasted_iota(jnp.int32, (1, few), 1)
    is_coarse, is_fine = column == expert, column == experts + expert

    def send_back(src, dst, p, ss, rs):
        e = from_core(p, n_shard)

        @pl.when(s != e)
        def _():
            push(src.at[p], dst.at[s], ss.at[e], rs.at[s], shard=e).start()

        @pl.when(s == e)
        def _():
            pltpu.make_async_copy(src.at[p], dst.at[e], rs.at[e]).start()

    def wait_back(src, dst, ss, rs):
        for p in range(n_shard):
            e = from_core(p, n_shard)

            @pl.when(s != e)
            def _():
                push(src.at[p], dst.at[e], ss.at[e], rs.at[e], shard=e).wait()

            @pl.when(s == e)
            def _():
                pltpu.make_async_copy(src.at[p], dst.at[e], rs.at[e]).wait()

    def experts_part(k, h):
        of = slice(h * half, (h + 1) * half)
        r = pl.ds((k * n_shard + h * half) * slots, chunk)
        gates = jnp.sum(
            jnp.where(is_coarse | is_fine, tail_recv[k, of].reshape(chunk, few).astype(F32), 0.0), axis=1, keepdims=True
        )

        @pl.loop(0, inner // 256)
        def _(j):
            cols = pl.ds(pl.multiple_of(j * 256, 256), 256)
            x = recv[k, of].reshape(chunk, width)
            g = jnp.dot(x, w_gate[:, cols], preferred_element_type=F32)
            u = jnp.dot(x, w_up[:, cols], preferred_element_type=F32)
            gate_pre[:, cols] = g
            up_pre[:, cols] = u
            hidden[r, cols] = (g * jax.nn.sigmoid(g) * u).astype(BF)

        slot_dot[...] = jnp.zeros_like(slot_dot)

        @pl.loop(0, width // tile)
        def _(j):
            cols = pl.ds(pl.multiple_of(j * tile, tile), tile)
            o = jnp.dot(hidden[r, :], w_down[:, cols], preferred_element_type=F32).astype(BF).astype(F32)
            up_row = cot[k, of, :, cols].reshape(chunk, tile).astype(F32)
            slot_dot[...] += jnp.sum(o * up_row, axis=1, keepdims=True)
            ready[k, of, :, cols] = (gates * o).astype(BF).reshape(half, slots, tile)
            cot[k, of, :, cols] = (gates * up_row).astype(BF).reshape(half, slots, tile)

        coarse = slot_dot[...].astype(BF).astype(F32)
        fine = slot_dot[...] - coarse
        back_tail[k, of] = jnp.where(is_coarse, coarse, jnp.where(is_fine, fine, 0.0)).astype(BF).reshape(half, slots, few)

        @pl.loop(0, inner // 256)
        def _(j):
            cols = pl.ds(pl.multiple_of(j * 256, 256), 256)
            gh = lax.dot_general(cot[k, of].reshape(chunk, width), w_down[cols, :], (((1,), (1,)), ((), ())),
                                 preferred_element_type=F32)
            g, u = gate_pre[:, cols], up_pre[:, cols]
            sig = jax.nn.sigmoid(g)
            grad_gate[r, cols] = (gh * u * (sig * (1.0 + g * (1.0 - sig)))).astype(BF)
            grad_up[r, cols] = (gh * (g * sig)).astype(BF)

        @pl.loop(0, width // tile)
        def _(j):
            cols = pl.ds(pl.multiple_of(j * tile, tile), tile)
            gx = lax.dot_general(grad_gate[r, :], w_gate[cols, :], (((1,), (1,)), ((), ())), preferred_element_type=F32)
            gx += lax.dot_general(grad_up[r, :], w_up[cols, :], (((1,), (1,)), ((), ())), preferred_element_type=F32)
            back_rows[k, of, :, cols] = gx.astype(BF).reshape(half, slots, tile)

    def send_part(k, h):
        for p in range(h * half, (h + 1) * half):
            send_back(back_rows.at[k], land.at[k], p, ss_d.at[k], rs_d.at[k])
            send_back(back_tail.at[k], tail_land.at[k], p, ss_e.at[k], rs_e.at[k])

    halves = n_shard // half
    for k in range(groups):
        for item in sent[k]:
            item.wait()
        for h in range(halves):
            experts_part(k, h)
            if k or h + 1 < halves:
                send_part(k, h)
    send_part(0, halves - 1)
    for p in range(n_shard):
        send_back(ready.at[groups - 1], mix_far, p, ss_m, rs_m)
    keep = pltpu.make_async_copy(ready.at[0], mix_near, local.at[0])
    keep.start()

    everything = groups * n_shard * slots

    def stage_out(j, which):
        at = pl.ds(pl.multiple_of(j * 256, 256), 256)
        return pltpu.make_async_copy(stage.at[which], (g_gate, g_up)[which].at[at], ss_st.at[which])

    @pl.loop(0, width // 256)
    def _(j):
        x = recv[:, :, :, pl.ds(pl.multiple_of(j * 256, 256), 256)].reshape(everything, 256)
        for which, grad in enumerate((grad_gate, grad_up)):
            total = lax.dot_general(x, grad[...], (((0,), (0,)), ((), ())), preferred_element_type=F32).astype(BF)

            @pl.when(j >= 1)
            def _():
                stage_out(j - 1, which).wait()

            stage[which] = total
            stage_out(j, which).start()

    def down_out(j):
        return pltpu.make_async_copy(stage_d, g_down.at[:, pl.ds(pl.multiple_of(j * 256, 256), 256)], ss_sd)

    @pl.loop(0, width // 256)
    def _(j):
        grad = cot[:, :, :, pl.ds(pl.multiple_of(j * 256, 256), 256)].reshape(everything, 256)
        total = lax.dot_general(
            hidden[...], grad, (((0,), (0,)), ((), ())), preferred_element_type=F32).astype(BF)

        @pl.when(j >= 1)
        def _():
            down_out(j - 1).wait()

        stage_d[...] = total
        down_out(j).start()

    last = width // 256 - 1
    stage_out(last, 0).wait()
    stage_out(last, 1).wait()
    down_out(last).wait()

    def local_sums(k, ref):
        @pl.loop(0, width // tile)
        def _(j):
            cols = pl.ds(pl.multiple_of(j * tile, tile), tile)
            block = ref[k, :, :, cols].reshape(n_shard * slots, tile)
            value[:, cols] = jnp.dot(table[k], block, preferred_element_type=F32)

    def part(ref, d):
        place = lax.rem(flip_bits(c, d), group)
        return ref[pl.ds(pl.multiple_of(place * count, count), count), :]

    folds = [Fold(c, zrows.at[:, :, side], zrecv.at[:, :, side], ss_fz.at[n], rs_fz.at[n]) for n, side in enumerate(sides)]
    tail_fold = Fold(c, tsend, trecv, ss_ft, rs_ft)
    for k in reversed(range(groups)):
        wait_back(back_rows.at[k], land.at[k], ss_d.at[k], rs_d.at[k])
        wait_back(back_tail.at[k], tail_land.at[k], ss_e.at[k], rs_e.at[k])
        local_sums(k, land)
        tail_value[...] = jnp.dot(table[k], tail_land[k].reshape(n_shard * slots, few), preferred_element_type=F32)
        if k:
            tail_fold.give(3, part(tail_value, 3))
            folds[0].give(3, part(value, 3)[:, sides[0]])
            folds[0].items[3].wait_send()
            folds[0].left.add(3)
            folds[1].give(3, part(value, 3)[:, sides[1]])
            for fold, side in zip(folds, sides):
                fold.give(2, fold.take(2, part(value, 2)[:, side]))
            tail_fold.give(2, tail_fold.take(2, part(tail_value, 2)))
        else:
            tail_fold.give(1, part(tail_value, 1))
            for fold, side in zip(folds, sides):
                fold.give(1, part(value, 1)[:, side])
    out[...] = part(value, 0)
    wait_back(ready.at[groups - 1], mix_far, ss_m, rs_m)
    keep.wait()
    again = pltpu.make_async_copy(mix_far, ready.at[0], local.at[0])
    again.start()
    again.wait()

    @pl.loop(0, width // tile)
    def _(j):
        cols = pl.ds(pl.multiple_of(j * tile, tile), tile)
        block = ready[0, :, :, cols].reshape(n_shard * slots, tile)
        value[:, cols] = jnp.dot(table[1], block, preferred_element_type=F32)

    for d in (2, 3):
        mix_part[d - 2] = part(value, d).astype(BF)
    for fold, side in zip(folds, sides):
        out[:, side] = fold.take(0, out[:, side])
    tail_out[...] = tail_fold.take(0, part(tail_value, 0))
    for fold in folds + [tail_fold]:
        fold.drain()


def run_experts(n_ctx, n_shard, group, capacity, rows, tail, code, w_gate, w_up, w_down, cot_rows, ident):
    n, z, groups, slots = n_shard, n_ctx, code.shape[0], group * capacity
    count, width = rows.shape
    few, inner, half = tail.shape[1], w_gate.shape[1], n_shard // 2
    everything, chunk = groups * n * slots, half * slots
    sds, scratch = jax.ShapeDtypeStruct, pltpu.VMEM
    dma = lambda *shape: DMA(shape)
    wide, thin = (groups, n, slots, width), (groups, n, slots, few)
    return call(
        functools.partial(expert_body, z, n, group, half, 512),
        [
            sds((count, width), F32), sds((count, few), F32), sds((n, slots, width), BF), sds((n, slots, width), BF),
            sds((2, count, width), BF), sds((width, inner), BF), sds((width, inner), BF), sds((inner, width), BF),
        ],
        [VMEM] * 3 + [ANY] * 4,
        [scratch(item.shape, BF) for item in (w_gate, w_up, w_down)] + [
            dma(3),
            scratch((z, count, width), BF), scratch((z, count, few), BF), scratch(wide, BF), scratch(thin, BF),
            scratch(wide, BF), scratch(thin, BF), scratch(wide, BF), scratch(wide, BF), scratch(thin, BF),
            scratch(wide, BF), scratch(thin, BF),
            scratch((everything, inner), BF), scratch((everything, inner), BF), scratch((everything, inner), BF),
            scratch((max(chunk, group * count), max(2 * inner, width)), F32), scratch((chunk, 1), F32),
            scratch((groups, group * count, n * slots), BF),
            scratch((group * count, few), F32), scratch((z - 1, count, width), BF),
            scratch((z - 1, count, few), BF), scratch((z - 1, count, few), BF),
            scratch((2, 256, inner), BF), scratch((inner, 256), BF), dma(2 + 3 * groups), dma(n - 1), dma(n - 1),
        ] + [dma(5)] * 2 + [dma(z)] * 2 + [dma(groups + 1, n - 1)] * 2 + [dma(groups, n - 1)] * 2 + [dma(groups, n)] * 4
        + [dma(n)] * 2 + [dma(2, z)] * 2 + [dma(z)] * 2 + [dma(2), DMA],
        ident, (rows, tail, code, w_gate, w_up, w_down, cot_rows), mib=62, out_specs=[VMEM] * 2 + [ANY] * 2 + [VMEM] + [ANY] * 3,
    )


def finish_types_body(q, o, g, u, d, kv, tokens, part, mid, mix, gains, router,
                      q_out, o_out, g_out, u_out, d_out, k_out, v_out, tokens_out, mixed_out,
                      attn_gain, ffn_gain, q_gain, k_gain, router_out):
    for source, target in ((q, q_out), (o, o_out), (g, g_out), (u, u_out), (d, d_out)):
        target[...] = source[...].astype(F32)
    for head in range(kv.shape[0] // 2):
        lanes = slice(head * HEAD_DIM, (head + 1) * HEAD_DIM)
        k_out[:, lanes] = kv[2 * head].astype(F32)
        v_out[:, lanes] = kv[2 * head + 1].astype(F32)
    tokens_out[...] = tokens[...] + part[...]
    mixed_out[...] = (mid[...] + mix[...]).astype(BF)
    n = attn_gain.shape[0]
    attn_gain[...] = gains[0:n]
    ffn_gain[...] = gains[n : 2 * n]
    q_gain[...] = gains[2 * n : 2 * n + 1]
    k_gain[...] = gains[2 * n + 1 : 2 * n + 2]
    router_out[...] = router[...].T


def finish_types(q, o, g, u, d, kv, tokens, part, mid, mix, gains, router):
    steps = 8
    sds = jax.ShapeDtypeStruct
    heads, wr, lanes = kv.shape
    width = tokens.shape[1]
    by_rows = lambda shape: pl.BlockSpec((shape[0] // steps,) + shape[1:], lambda i: (i, 0))
    whole = lambda shape: pl.BlockSpec(shape, lambda i: (0, 0))
    kv_shape, gain_shape, one = (wr, heads // 2 * lanes), (width // lanes, lanes), (1, lanes)
    ins = [q, o, g, u, d, kv, tokens, part, mid, mix, gains, router]
    in_specs = [by_rows(item.shape) for item in (q, o, g, u, d)]
    in_specs += [pl.BlockSpec((heads, wr // steps, lanes), lambda i: (0, i, 0))]
    in_specs += [by_rows(tokens.shape)] * 4 + [whole(gains.shape), whole(router.shape)]
    outs = [sds(item.shape, F32) for item in (q, o, g, u, d)] + [sds(kv_shape, F32)] * 2
    outs += [sds(tokens.shape, F32), sds(tokens.shape, BF)]
    out_specs = [by_rows(item.shape) for item in outs]
    small = [gain_shape, gain_shape, one, one, router.shape[::-1]]
    return pl.pallas_call(
        finish_types_body,
        grid=(steps,),
        out_shape=outs + [sds(shape, F32) for shape in small],
        in_specs=in_specs,
        out_specs=out_specs + [whole(shape) for shape in small],
        compiler_params=pltpu.CompilerParams(vmem_limit_bytes=62 * 2**20),
    )(*ins)


def rms_scale(hidden, gain):
    return hidden * lax.rsqrt(jnp.mean(hidden * hidden, axis=-1, keepdims=True) + epsilon) * gain


def rotate(headwise, places):
    half_size = headwise.shape[-1] // 2
    frequency = rope_base ** (-jnp.arange(half_size, dtype=F32) * 2.0 / headwise.shape[-1])
    angles = places.astype(F32)[:, None] * frequency[None, :]
    cosine = jnp.cos(angles)[:, None, :]
    sine = jnp.sin(angles)[:, None, :]
    former = headwise[..., :half_size]
    latter = headwise[..., half_size:]
    return jnp.concatenate(
        [former * cosine - latter * sine, latter * cosine + former * sine], axis=-1
    )


def place_of(row_ids, order, block_rows):
    block_ids = jnp.arange(order.shape[0], dtype=jnp.int32)
    owner_block = row_ids // block_rows
    picked_block = jnp.sum(
        jnp.where(owner_block[:, None] == block_ids[None, :], order[None, :], 0), axis=1
    )
    return picked_block * block_rows + row_ids % block_rows


def dot(left, right):
    return jnp.dot(left, right, preferred_element_type=F32)


def contract_rows(left, right):
    return lax.dot_general(left, right, (((0,), (0,)), ((), ())), preferred_element_type=F32)


def contract_cols(left, right):
    return lax.dot_general(left, right, (((1,), (1,)), ((), ())), preferred_element_type=F32)


def exchange_shard(x):
    return lax.all_to_all(x, "shard", split_axis=0, concat_axis=0, tiled=True)


def gather_ctx(x):
    return lax.all_gather(x, "ctx", axis=0, tiled=False)


def shards(
    tokens,
    cotangent,
    block_order,
    routes,
    attn_gain,
    w_query,
    key_weight,
    value_weight,
    query_gain,
    key_gain,
    w_out,
    ffn_gain,
    w_router,
    w_gate,
    w_up,
    w_down,
):
    rows = tokens.shape[1]
    width = tokens.shape[2]
    ctx_count = lax.axis_size("ctx")
    shard_count = lax.axis_size("shard")
    my_ctx = lax.axis_index("ctx")
    my_shard = lax.axis_index("shard")
    experts = ctx_count * shard_count
    block_rows = rows // 2
    heads = QUERY_HEADS // shard_count
    head_cols = heads * HEAD_DIM
    sharers = shard_count // KEY_VALUE_HEADS
    score_scale = HEAD_DIM ** (-0.5)
    top_count = routes.shape[2]
    capacity = rows * top_count // experts + max(rows * top_count // (4 * experts), 1)
    sequence = rows * ctx_count
    plane = rows * shard_count
    wrows = width // shard_count

    inputs = tokens[0].astype(F32)
    upstream_b = cotangent[0]
    upstream = upstream_b.astype(F32)

    group = 1
    while group * capacity % 16:
        group *= 2
    groups = ctx_count // group
    small = plane * width <= 2**21 and ctx_count == 4 and group == 2
    slot_rows = shard_count * ctx_count * capacity
    block_shape = (shard_count, groups, group * capacity)
    row_ids = my_ctx * rows + jnp.arange(rows, dtype=jnp.int32)
    q_places = place_of(row_ids, block_order, block_rows)
    k_places = place_of(jnp.arange(sequence, dtype=jnp.int32), block_order, block_rows)
    bias = jnp.where(k_places[None, :] <= q_places[:, None], 0.0, -1e30).astype(F32)
    frequency = rope_base ** (-jnp.arange(HEAD_DIM // 2, dtype=F32) * 2.0 / HEAD_DIM)
    angles = q_places.astype(F32)[:, None] * frequency[None, :]
    cosine = jnp.concatenate([jnp.cos(angles)] * 2, axis=1)
    sine = jnp.concatenate([-jnp.sin(angles), jnp.sin(angles)], axis=1)
    (
        normed_all, w_mine, router_all, code, upstream_rows, query_pre, kv_pre, queries, kv_all, attn_rows, middle,
    ) = front(
        ctx_count, shard_count, group, capacity, KEY_VALUE_HEADS, small,
        (
            tokens[0], attn_gain[None], w_query, key_weight, value_weight, routes[0].T, w_router.T, upstream_b,
            cosine, sine, bias, query_gain[None], key_gain[None], w_out,
        ),
        0,
    )
    is_key = lax.rem(my_shard, 2) == 0
    part_count = sharers // 2

    def prep(pre, gain):
        shape = pre.shape
        flat = pre.reshape(-1, rows, shape[-2], HEAD_DIM)
        return jax.vmap(lambda v: rotate(rms_scale(v, gain), q_places))(flat).reshape(shape)

    normed_two = rms_scale(middle, ffn_gain)
    second_b = normed_two.astype(BF)
    logits = contract_cols(second_b, router_all)
    chosen = jnp.sum(
        (routes[0][:, :, None] == jnp.arange(experts, dtype=jnp.int32)).astype(F32), axis=1
    )

    def gates_of(log, mask):
        masked = jnp.where(mask > 0, log, -1e30)
        peak = jnp.max(masked, axis=-1, keepdims=True)
        risen = jnp.exp(masked - peak) * mask
        return risen / jnp.maximum(jnp.sum(risen, axis=-1, keepdims=True), 1e-30)

    gates = gates_of(logits, chosen)

    tail_cols = -(-2 * experts // 128) * 128

    def two_parts(value):
        coarse = value.astype(BF).astype(F32)
        return coarse.astype(BF), (value - coarse).astype(BF)

    gates_two = jnp.concatenate(two_parts(gates), axis=1)
    gates_two = jnp.pad(gates_two, ((0, 0), (0, tail_cols - 2 * experts)))
    if small:
        grad_second, back_tail, mix_near, unused, mix_part, grad_w_gate, grad_w_up, grad_w_down = run_experts(
            ctx_count, shard_count, group, capacity, second_b, gates_two, code, w_gate[0], w_up[0], w_down[0],
            upstream_rows, 3,
        )
    else:
        received, gate_tail = dispatch_rows(ctx_count, shard_count, group, capacity, second_b, gates_two, code, 3)
        received = received.reshape(slot_rows, width)
        my_expert = my_ctx * shard_count + my_shard
        upstream_rows = jnp.swapaxes(upstream_rows, 0, 1).reshape(slot_rows, width)
        column = jnp.arange(tail_cols, dtype=jnp.int32)[None, :]
        mine_column = (column == my_expert) | (column == experts + my_expert)
        gate_tail = gate_tail.reshape(slot_rows, tail_cols).astype(F32)
        slot_gates = jnp.sum(jnp.where(mine_column, gate_tail, 0.0), axis=1, keepdims=True)
        gate_pre = dot(received, w_gate[0])
        up_pre = dot(received, w_up[0])
        activated = jax.nn.silu(gate_pre)
        hidden_b = (activated * up_pre).astype(BF)
        expert_out = dot(hidden_b, w_down[0]).astype(BF)
        expert_out_f = expert_out.astype(F32)
        mix_sent = (slot_gates * expert_out_f).astype(BF)
        mix_sent, upstream_rows, expert_out = lax.optimization_barrier((mix_sent, upstream_rows, expert_out))
        expert_out_f = expert_out.astype(F32)
        mix_back = exchange_shard(mix_sent.reshape(block_shape + (width,)))
        upstream_rows = upstream_rows.astype(F32)
        slot_dot = jnp.sum(expert_out_f * upstream_rows, axis=1, keepdims=True)
        grad_expert = (slot_gates * upstream_rows).astype(BF)
        grad_w_down = contract_rows(hidden_b, grad_expert)
        grad_hidden = contract_cols(grad_expert, w_down[0])
        sigmoid_g = jax.nn.sigmoid(gate_pre)
        silu_slope = sigmoid_g * (1.0 + gate_pre * (1.0 - sigmoid_g))
        grad_gate_pre = (grad_hidden * up_pre * silu_slope).astype(BF)
        grad_up_pre = (grad_hidden * activated).astype(BF)
        grad_w_gate = contract_rows(received, grad_gate_pre)
        grad_w_up = contract_rows(received, grad_up_pre)
        grad_received = contract_cols(grad_gate_pre, w_gate[0]) + contract_cols(grad_up_pre, w_up[0])

        coarse, fine = two_parts(slot_dot)
        tail = jnp.where(column == my_expert, coarse, jnp.where(column == experts + my_expert, fine, jnp.zeros((), BF)))
        grad_second, back_tail, mixture = combine_rows(
            ctx_count, shard_count, group, grad_received.astype(BF).reshape(block_shape + (width,)),
            tail.reshape(block_shape + (tail_cols,)), mix_back, code, 4,
        )
    grad_gates = back_tail[:, :experts] + back_tail[:, experts : 2 * experts]
    grad_logits_b = (
        gates * (grad_gates - jnp.sum(gates * grad_gates, axis=-1, keepdims=True))
    ).astype(BF)
    router_part = contract_rows(grad_logits_b, second_b).astype(BF)
    grad_second = grad_second + dot(grad_logits_b, router_all)
    unused, norm_two_back = jax.vjp(rms_scale, middle, ffn_gain)
    grad_middle_part, grad_ffn_gain = norm_two_back(grad_second)
    grad_middle = upstream + grad_middle_part
    grad_proj_b = grad_middle.astype(BF)

    router_parts = jnp.swapaxes(router_part.reshape(experts, shard_count, wrows), 0, 1)
    if small:
        gains = jnp.concatenate([jnp.zeros((width,), F32), grad_ffn_gain, jnp.zeros((8 * HEAD_DIM,), F32)])
        gains = gains.reshape(-1, HEAD_DIM)
        q_sum, kv_sum, out_sum, router_sum, gains, grad_input_part, mixture, unused = back(
            ctx_count, shard_count, group, heads,
            (
                grad_proj_b, queries, kv_all, attn_rows, query_pre, kv_pre, w_out, normed_all, w_mine,
                cosine, sine, bias, query_gain[None], key_gain[None], tokens[0], attn_gain[None], gains, router_parts,
                mix_near, mix_part, code,
            ),
            5,
        )
        (
            grad_w_query, grad_w_out, grad_w_gate, grad_w_up, grad_w_down, grad_w_key, grad_w_value, grad_tokens, mixed,
            grad_attn_gain, grad_ffn_gain, grad_query_gain, grad_key_gain, grad_w_router,
        ) = finish_types(
            q_sum, out_sum, grad_w_gate, grad_w_up, grad_w_down, kv_sum, grad_middle, grad_input_part, middle, mixture,
            gains, router_sum,
        )
        grad_attn_gain, grad_ffn_gain = grad_attn_gain.reshape(-1), grad_ffn_gain.reshape(-1)
        grad_query_gain, grad_key_gain = grad_query_gain.reshape(-1), grad_key_gain.reshape(-1)
    else:
        normed_all = normed_all.reshape(plane, width)
        w_mine = w_mine.reshape(width, head_cols + HEAD_DIM)
        query_pre = query_pre.reshape(shard_count, rows, heads, HEAD_DIM)
        kv_pre = kv_pre.reshape(plane, HEAD_DIM)
        queries = queries.reshape(shard_count, rows, heads, HEAD_DIM)
        kv_all = kv_all.reshape(2, shard_count, sequence, HEAD_DIM)
        keys, values = kv_all[0], kv_all[1]
        attn_rows = attn_rows.reshape(plane, head_cols)
        grad_proj_all = spread(shard_count, grad_proj_b, 5).reshape(plane, width)
        out_part = contract_rows(attn_rows, grad_proj_all).astype(BF)
        out_part, grad_proj_all = lax.optimization_barrier((out_part, grad_proj_all))
        grad_attn = contract_cols(grad_proj_all, w_out).astype(BF)
        grad_heads = grad_attn.reshape(shard_count, rows, heads, HEAD_DIM)
        scores = (
            jnp.einsum("sthd,spd->shtp", queries, keys, preferred_element_type=F32) * score_scale
        )
        scores = scores + bias
        raised = jnp.exp(scores - jnp.max(scores, axis=-1, keepdims=True))
        probs = raised / jnp.sum(raised, axis=-1, keepdims=True)
        probs_b = probs.astype(BF)
        grad_probs = jnp.einsum("sthd,spd->shtp", grad_heads, values, preferred_element_type=F32)
        delta = jnp.sum(probs * grad_probs, axis=-1, keepdims=True)
        grad_scores = (probs * (grad_probs - delta)).astype(BF)
        grad_query = score_scale * jnp.einsum(
            "shtp,spd->sthd", grad_scores, keys, preferred_element_type=F32
        )
        grad_keys = score_scale * jnp.einsum(
            "shtp,sthd->spd", grad_scores, queries, preferred_element_type=F32
        )
        grad_values = jnp.einsum("shtp,sthd->spd", probs_b, grad_heads, preferred_element_type=F32)
        grad_kv = jnp.stack([grad_keys, grad_values]).astype(BF)
        grad_kv = key_back(
            ctx_count, shard_count, grad_kv.reshape(2, shard_count, ctx_count, rows, HEAD_DIM), 6
        )
        unused, query_back = jax.vjp(prep, query_pre, query_gain)
        grad_query_pre, grad_query_gain = query_back(grad_query)
        kv_shape = (shard_count, rows, 1, HEAD_DIM)
        unused, key_prep_back = jax.vjp(prep, kv_pre.reshape(kv_shape), key_gain)
        grad_key_pre, grad_key_gain = key_prep_back(grad_kv.reshape(kv_shape))
        grad_key_gain = jnp.where(is_key, grad_key_gain, 0.0)
        grad_kv_full = jnp.where(
            is_key, grad_key_pre.reshape(plane, HEAD_DIM), grad_kv.reshape(plane, HEAD_DIM)
        ).astype(BF)
        grad_pre = jnp.concatenate(
            [grad_query_pre.reshape(plane, head_cols).astype(BF), grad_kv_full], axis=1
        )
        gains = jnp.concatenate(
            [
                jnp.zeros((1, width), F32),
                grad_ffn_gain[None],
                jnp.pad(
                    jnp.concatenate([grad_query_gain, grad_key_gain])[None],
                    ((0, 6 - 1), (0, width - 2 * HEAD_DIM)),
                ),
            ]
        )
        grad_w = contract_rows(normed_all, grad_pre).astype(BF).reshape(shard_count, wrows, -1)
        q_sum, kv_sum, out_sum, router_sum, gains, grad_input_part = finish(
            ctx_count, shard_count, head_cols, grad_w, out_part.reshape(8, -1, width), router_parts, gains, grad_pre, w_mine,
            tokens[0], attn_gain[None], 8,
        )
        mixed = (middle + mixture).astype(BF)
        grad_tokens = grad_middle + grad_input_part
        gains = gains.reshape(-1)
        grad_attn_gain, grad_ffn_gain = gains[:width], gains[width : 2 * width]
        grad_query_gain = gains[2 * width : 2 * width + HEAD_DIM]
        grad_key_gain = gains[2 * width + HEAD_DIM : 2 * width + 2 * HEAD_DIM]
        grad_w_query = q_sum.astype(F32)
        grad_w_out = out_sum.reshape(head_cols, width).astype(F32)
        kinds = kv_sum.astype(F32).reshape(KEY_VALUE_HEADS, part_count, 2, wrows, HEAD_DIM)
        kinds = jnp.transpose(jnp.sum(kinds, axis=1), (1, 2, 0, 3)).reshape(2, wrows, -1)
        grad_w_key, grad_w_value = kinds[0], kinds[1]
        grad_w_router = router_sum.T
    return (
        mixed[None],
        grad_tokens[None],
        grad_attn_gain,
        grad_w_query,
        grad_w_key,
        grad_w_value,
        grad_query_gain,
        grad_key_gain,
        grad_w_out,
        grad_ffn_gain,
        grad_w_router,
        grad_w_gate[None],
        grad_w_up[None],
        grad_w_down[None],
    )


def solution(mesh):
    rows = P("shard", "ctx", None)
    matrix = P("shard", None)
    expert = P(("ctx", "shard"), None, None)
    return jax.shard_map(
        shards,
        mesh=mesh,
        in_specs=(
            rows, rows, P(), rows, P(), matrix, matrix, matrix, P(), P(), matrix, P(), matrix,
            expert, expert, expert,
        ),
        out_specs=(
            rows, rows, P(), matrix, matrix, matrix, P(), P(), matrix, P(), matrix,
            expert, expert, expert,
        ),
        check_vma=False,
    )
```

```python
import functools

import jax
import jax.numpy as jnp
from jax import lax
from jax.experimental import pallas as pl
from jax.experimental.pallas import tpu as pltpu
from jax.sharding import PartitionSpec as P

BF = jnp.bfloat16
F32 = jnp.float32
MESH = pl.DeviceIdType.MESH
ANY = pl.BlockSpec(memory_space=pl.ANY)
VMEM = pl.BlockSpec(memory_space=pltpu.VMEM)
DMA = pltpu.SemaphoreType.DMA
epsilon = 1e-06
rope_base = 1000000.0
QUERY_HEADS = 32
KEY_VALUE_HEADS = 4
HEAD_DIM = 128


def push(src, dst, send_sem, recv_sem, **where):
    return pltpu.make_async_remote_copy(
        src_ref=src, dst_ref=dst, send_sem=send_sem, recv_sem=recv_sem,
        device_id=where, device_id_type=MESH,
    )


def greet(shard_peers, ctx_peers):
    barrier = pltpu.get_barrier_semaphore()
    for peer in shard_peers:
        pl.semaphore_signal(barrier, inc=1, device_id={"shard": peer}, device_id_type=MESH)
    for peer in ctx_peers:
        pl.semaphore_signal(barrier, inc=1, device_id={"ctx": peer}, device_id_type=MESH)
    pl.semaphore_wait(barrier, len(shard_peers) + len(ctx_peers))


def here(ctx_count, shard_count):
    c, s = lax.axis_index("ctx"), lax.axis_index("shard")
    parity = lax.rem(s, 2)
    sibling = s + 1 - 2 * parity
    others = [lax.rem(s + d, shard_count) for d in range(1, shard_count)]
    layers = [lax.rem(c + d, ctx_count) for d in range(1, ctx_count)]
    return c, s, parity, sibling, others, layers


def flip_bits(index, mask):
    result = index
    bit = 1
    while bit <= mask:
        if mask & bit:
            result = result + bit - 2 * bit * lax.rem(lax.div(index, bit), 2)
        bit *= 2
    return result


def lowest(d):
    return d & -d


class Fan:
    def __init__(self, n_ctx, c, block, ss, rs, near_first):
        self.n_ctx, self.c, self.block, self.ss, self.rs, self.near_first = n_ctx, c, block, ss, rs, near_first
        self.items = {}

    def send(self, d, src):
        bits = [b for b in (1, 2, 4, 8, 16) if b < (lowest(d) or self.n_ctx)]
        for b in bits if self.near_first else reversed(bits):
            item = push(src, self.block(d), self.ss.at[d | b], self.rs.at[d | b], ctx=flip_bits(self.c, b))
            item.start()
            self.items[d | b] = item

    def arrival(self, d):
        self.items[d].wait_recv()
        if lowest(d) > 1:
            self.send(d, self.block(d))

    def order(self):
        return sorted(range(1, self.n_ctx), key=lambda d: (bin(d).count("1"), d if self.near_first else -d))

    def drain(self):
        for d in range(1, self.n_ctx):
            self.items[d].wait_send()


class Fold:
    def __init__(self, c, sent, received, ss, rs, slots=None, after=None):
        self.c, self.sent, self.received, self.ss, self.rs = c, sent, received, ss, rs
        self.slots, self.after = slots or {}, after or {}
        self.items, self.left = {}, set()

    def take(self, d, value):
        for b in (1, 2, 4, 8, 16):
            if b < lowest(d) or (d == 0 and b in self.items):
                self.items[d | b].wait_recv()
                value = value + self.received[(d | b) - 1].astype(F32)
        return value

    def give(self, d, value):
        slot = self.slots.get(d, d - 1)
        if d in self.after:
            other, which = self.after[d]
            other.items[which].wait_send()
            other.left.add(which)
        self.sent[slot] = value.astype(BF)
        item = push(self.sent.at[slot], self.received.at[d - 1], self.ss.at[d], self.rs.at[d],
                    ctx=flip_bits(self.c, lowest(d)))
        item.start()
        self.items[d] = item

    def give_as_is(self, d, ref):
        self.items[d] = push(ref, self.received.at[d - 1], self.ss.at[d], self.rs.at[d],
                             ctx=flip_bits(self.c, lowest(d)))
        self.items[d].start()

    def drain(self):
        for d, item in self.items.items():
            if d not in self.left:
                item.wait_send()


def call(body, outs, in_specs, scratch, ident, args, mib=48, out_specs=None):
    return pl.pallas_call(
        body,
        out_shape=outs,
        in_specs=in_specs,
        out_specs=out_specs if out_specs is not None else [ANY] * len(outs),
        scratch_shapes=scratch,
        compiler_params=pltpu.CompilerParams(
            collective_id=ident, has_side_effects=True, vmem_limit_bytes=mib * 2**20
        ),
    )(*args)


def by_core(s, n_shard):
    return lax.rem(s, 2) * (n_shard // 2) + lax.div(s, 2)


def from_core(place, n_shard):
    return place % (n_shard // 2) * 2 + place // (n_shard // 2)


def slot_table(code, slots):
    places = lax.broadcasted_iota(jnp.int32, (slots, code.shape[1]), 0).astype(F32)
    return jnp.concatenate(
        [(places == code[e : e + 1, :]).astype(BF) for e in range(code.shape[0])], axis=0
    )


def turn(value, cosine, sine):
    return value * cosine + pltpu.roll(value, HEAD_DIM // 2, 1) * sine


def unit_rows(value):
    scale = lax.rsqrt(jnp.mean(value * value, axis=-1, keepdims=True) + epsilon)
    return value * scale, scale


def front_body(n_ctx, n_shard, group, capacity, heads, kv_heads, paired, tile,
               tokens, gain, w_query, key_w, value_w, routes, router, cot, cosine, sine, bias, q_gain, k_gain, w_out, second_gain,
               rows_out, w_all_out, router_all, code, cot_rows, qpre_out, kvpre, q_out, kv_out, attn_out, mid, second,
               own_rows, rows_all, w_all, zroutes, zcot, ready, qpre, q, kv, attn,
               own_part, pair, to_sib, sib, to_chip, got,
               local, ss_row, rs_row, ss_fwd, rs_fwd, ss_w, rs_w, ss_k, rs_k, ss_rt, rs_rt, ss_ro, rs_ro, ss_z, rs_z,
               ss_x, rs_x, ss_kz, rs_kz, ss_kf, rs_kf, ss_s, rs_s, ss_c, rs_c, out_sem):
    c, s, parity, sibling, others, layers = here(n_ctx, n_shard)
    chips = n_shard // 2
    chip = lax.div(s, 2)
    count, width = tokens.shape
    wr = w_query.shape[0]
    cols = heads * HEAD_DIM
    sharers = n_shard // kv_heads
    groups = n_ctx // group
    slots = group * capacity
    keys = n_ctx * count
    mates = [lax.rem(s + 2 * d, n_shard) for d in range(1, chips)]
    x = tokens[...].astype(F32)
    unit, unused = unit_rows(x)
    own_rows[...] = (unit * gain[...]).astype(BF)
    greet(others, layers)

    route_fan = Fan(n_ctx, c, lambda d: zroutes.at[flip_bits(c, d)], ss_ro, rs_ro, False)
    route_fan.send(0, routes)
    cot_fan = Fan(n_ctx, c, lambda d: zcot.at[flip_bits(c, d)], ss_z, rs_z, False)
    cot_fan.send(0, cot)
    first, waits = [], []
    for d in range(1, chips):
        item = push(own_rows, rows_all.at[s], ss_row.at[d], rs_row.at[d], shard=mates[d - 1])
        item.start()
        first.append(item)
    item = push(own_rows, rows_all.at[s], ss_fwd.at[0], rs_fwd.at[0], shard=sibling)
    item.start()
    waits.append(item)
    w_waits = []
    for i, peer in enumerate(others):
        from_q = w_query.at[:, pl.ds(pl.multiple_of(peer * cols, cols), cols)]
        item = push(from_q, w_all.at[s, :, pl.ds(0, cols)], ss_w.at[i], rs_w.at[i], shard=peer)
        item.start()
        w_waits.append(item)
        head = pl.ds(pl.multiple_of(lax.div(peer, sharers) * HEAD_DIM, HEAD_DIM), HEAD_DIM)
        for kind, ref in enumerate((key_w, value_w)):
            item = push(ref.at[:, head], w_all.at[s, :, pl.ds(cols, HEAD_DIM)], ss_k.at[i], rs_k.at[i], shard=peer)

            @pl.when(lax.rem(peer, 2) == kind)
            def _(item=item):
                item.start()

        w_waits.append(item)
        item = push(router, router_all.at[:, pl.ds(pl.multiple_of(s * wr, wr), wr)], ss_rt.at[i], rs_rt.at[i], shard=peer)
        item.start()
        waits.append(item)
    copies = [
        pltpu.make_async_copy(own_rows, rows_all.at[s], local.at[0]),
        pltpu.make_async_copy(w_query.at[:, pl.ds(pl.multiple_of(s * cols, cols), cols)],
                              w_all.at[s, :, pl.ds(0, cols)], local.at[1]),
        pltpu.make_async_copy(routes, zroutes.at[c], local.at[2]),
        pltpu.make_async_copy(router, router_all.at[:, pl.ds(pl.multiple_of(s * wr, wr), wr)], local.at[3]),
        pltpu.make_async_copy(cot, zcot.at[c], local.at[4]),
    ]
    for item in copies:
        item.start()
    head = pl.ds(pl.multiple_of(lax.div(s, sharers) * HEAD_DIM, HEAD_DIM), HEAD_DIM)
    for kind, ref in enumerate((key_w, value_w)):
        own_head = pltpu.make_async_copy(ref.at[:, head], w_all.at[s, :, pl.ds(cols, HEAD_DIM)], local.at[5])

        @pl.when(parity == kind)
        def _(own_head=own_head):
            own_head.start()

    copies[2].wait()
    for d in route_fan.order():
        route_fan.arrival(d)
    before = (
        lax.broadcasted_iota(jnp.int32, (count, count), 0) < lax.broadcasted_iota(jnp.int32, (count, count), 1)
    ).astype(BF)
    for layer in range(n_ctx):
        named = zroutes[layer]
        mask = jnp.concatenate(
            [jnp.max((named == c * n_shard + e).astype(F32), axis=0, keepdims=True) for e in range(n_shard)], axis=0
        )
        rank = jnp.dot(mask.astype(BF), before, preferred_element_type=F32)
        at = layer % group
        code[layer // group, :, at * count : (at + 1) * count] = jnp.where(
            mask > 0, rank + float(at * capacity), -1.0
        )

    for d in range(1, chips):
        first[d - 1].wait()
        origin = lax.rem(s + n_shard - 2 * d, n_shard)
        item = push(rows_all.at[origin], rows_all.at[origin], ss_fwd.at[d], rs_fwd.at[d], shard=sibling)
        item.start()
        waits.append(item)
    for d in cot_fan.order():
        cot_fan.arrival(d)
    copies[4].wait()
    for k in range(groups):
        table = slot_table(code[k], slots)

        @pl.loop(0, width // tile)
        def _(j):
            part = pl.ds(pl.multiple_of(j * tile, tile), tile)
            block = zcot[k * group : (k + 1) * group, :, part].reshape(group * count, tile)
            value = jnp.dot(table, block, preferred_element_type=F32).astype(BF)
            ready[k, :, :, part] = value.reshape(n_shard, slots, tile)

    place = by_core(s, n_shard) if paired else s
    cot_waits = []
    for k in range(groups):
        for i, peer in enumerate(others):
            item = push(ready.at[k, peer], cot_rows.at[k, place], ss_x.at[k, i], rs_x.at[k, i], shard=peer)
            item.start()
            cot_waits.append(item)
        item = pltpu.make_async_copy(ready.at[k, s], cot_rows.at[k, place], local.at[6 + k])
        item.start()
        cot_waits.append(item)

    for item in waits + w_waits:
        item.wait()
    copies[0].wait()
    copies[1].wait()
    copies[3].wait()
    own_head.wait()
    outs = [
        pltpu.make_async_copy(rows_all, rows_out, out_sem.at[0]),
        pltpu.make_async_copy(w_all, w_all_out, out_sem.at[1]),
    ]
    outs[0].start()
    outs[1].start()

    right = w_all[:, :, pl.ds(cols, HEAD_DIM)].reshape(width, HEAD_DIM)

    @pl.loop(0, n_shard)
    def _(b):
        pre = jnp.dot(rows_all[b], right, preferred_element_type=F32)
        kvpre[b] = pre
        keyed, unused = unit_rows(pre)
        keyed = turn(keyed * k_gain[...], cosine[...], sine[...])
        kv[parity, b, c] = jnp.where(parity == 0, keyed, pre).astype(BF)

    fan = Fan(n_ctx, c, lambda d: kv.at[parity, :, flip_bits(c, d)], ss_kz, rs_kz, False)
    fan.send(0, kv.at[parity, :, c])
    kv_waits = []
    item = push(kv.at[parity, :, c], kv.at[parity, :, c], ss_kf.at[0], rs_kf.at[0], shard=sibling)
    item.start()
    kv_waits.append(item)

    @pl.loop(0, n_shard // 2)
    def _(b):
        left = rows_all[pl.ds(b * 2, 2)].reshape(2 * count, width)
        pre = jnp.dot(left, w_all[:, :, pl.ds(0, cols)].reshape(width, cols), preferred_element_type=F32)
        qpre[pl.ds(b * 2, 2)] = pre.reshape(2, count, cols)
        for i in range(2):
            for h in range(heads):
                part = pre[i * count : (i + 1) * count, h * HEAD_DIM : (h + 1) * HEAD_DIM]
                unit, unused = unit_rows(part)
                q[b * 2 + i, :, h * HEAD_DIM : (h + 1) * HEAD_DIM] = turn(
                    unit * q_gain[...], cosine[...], sine[...]
                ).astype(BF)

    for d in fan.order():
        fan.arrival(d)
        block = kv.at[parity, :, flip_bits(c, d)]
        item = push(block, block, ss_kf.at[d], rs_kf.at[d], shard=sibling)
        item.start()
        kv_waits.append(item)
    outs += [pltpu.make_async_copy(qpre, qpre_out, out_sem.at[2]), pltpu.make_async_copy(q, q_out, out_sem.at[3])]
    outs[2].start()
    outs[3].start()
    for item in kv_waits:
        item.wait()
    fan.drain()
    outs.append(pltpu.make_async_copy(kv, kv_out, out_sem.at[4]))
    outs[4].start()

    near, far = {}, {}
    order = list(range(1, chips)) + [0]

    def product(at):
        d = order[at]
        first_seq = 2 * lax.rem(chip + d, chips)

        @pl.loop(0, 2)
        def _(i):
            b = first_seq + i
            k_all = kv[0, b].reshape(keys, HEAD_DIM)
            v_all = kv[1, b].reshape(keys, HEAD_DIM)
            for h in range(heads):
                hs = slice(h * HEAD_DIM, (h + 1) * HEAD_DIM)
                scores = lax.dot_general(q[b, :, hs], k_all, (((1,), (1,)), ((), ())), preferred_element_type=F32)
                scores = scores * (HEAD_DIM ** -0.5) + bias[...]
                raised = jnp.exp(scores - jnp.max(scores, axis=-1, keepdims=True))
                probs = raised / jnp.sum(raised, axis=-1, keepdims=True)
                attn[b, :, hs] = jnp.dot(probs.astype(BF), v_all, preferred_element_type=F32).astype(BF)

        left = attn[pl.ds(first_seq, 2)].reshape(2 * count, cols)

        @pl.loop(0, width // tile)
        def _(j):
            part = pl.ds(pl.multiple_of(j * tile, tile), tile)
            value = jnp.dot(left, w_out[:, part], preferred_element_type=F32)
            pair[...] = value.reshape(2, count, tile)
            own_part[at % 2, :, part] = pair[parity]
            to_sib[at, :, part] = pair[1 - parity].astype(BF)

        near[at] = push(to_sib.at[at], sib.at[at], ss_s.at[at], rs_s.at[at], shard=sibling)
        near[at].start()

    def chip_sum(at):
        near[at].wait()
        to_chip[at] = (own_part[at % 2] + sib[at].astype(F32)).astype(BF)
        far[at] = push(to_chip.at[at], got.at[at], ss_c.at[at], rs_c.at[at], shard=mates[order[at] - 1])
        far[at].start()

    for at in range(chips):
        product(at)
        if at:
            chip_sum(at - 1)
    outs.append(pltpu.make_async_copy(attn, attn_out, out_sem.at[5]))
    outs[5].start()
    near[chips - 1].wait()
    mid[...] = tokens[...].astype(F32) + own_part[(chips - 1) % 2] + sib[chips - 1].astype(F32)
    for at in range(chips - 1):
        far[at].wait()
        mid[...] += got[at].astype(F32)
    unit, unused = unit_rows(mid[...])
    second[...] = (unit * second_gain[...]).astype(BF)
    cot_fan.drain()
    route_fan.drain()
    for item in cot_waits + outs:
        item.wait()


def front(n_ctx, n_shard, group, capacity, kv_heads, paired, args, ident):
    tokens, gain, w_query, key_w, value_w, routes, router, cot = args[:8]
    n, z = n_shard, n_ctx
    count, width = tokens.shape
    wr, chips, groups, slots = w_query.shape[0], n_shard // 2, n_ctx // group, group * capacity
    cols = w_query.shape[1] // n
    heads = cols // HEAD_DIM
    sds = jax.ShapeDtypeStruct
    dma = lambda *shape: DMA(shape)
    return call(
        functools.partial(front_body, z, n, group, capacity, heads, kv_heads, paired, 512),
        [
            sds((n, count, width), BF), sds((n, wr, cols + HEAD_DIM), BF), sds((router.shape[0], width), BF),
            sds((groups, n, group * count), F32), sds((groups, n, slots, width), BF), sds((n, count, cols), F32),
            sds((n, count, HEAD_DIM), F32), sds((n, count, cols), BF), sds((2, n, z, count, HEAD_DIM), BF),
            sds((n, count, cols), BF), sds((count, width), F32), sds((count, width), BF),
        ],
        [VMEM, VMEM, ANY, ANY, ANY, VMEM, ANY, ANY] + [VMEM] * 7,
        [
            pltpu.VMEM((count, width), BF), pltpu.VMEM((n, count, width), BF), pltpu.VMEM((n, wr, cols + HEAD_DIM), BF),
            pltpu.VMEM((z,) + routes.shape, jnp.int32), pltpu.VMEM((z, count, width), BF),
            pltpu.VMEM((groups, n, slots, width), BF), pltpu.VMEM((n, count, cols), F32),
            pltpu.VMEM((n, count, cols), BF), pltpu.VMEM((2, n, z, count, HEAD_DIM), BF),
            pltpu.VMEM((n, count, cols), BF), pltpu.VMEM((2, count, width), F32), pltpu.VMEM((2, count, 512), F32),
            pltpu.VMEM((chips, count, width), BF), pltpu.VMEM((chips, count, width), BF),
            pltpu.VMEM((chips - 1, count, width), BF), pltpu.VMEM((chips - 1, count, width), BF),
            dma(6 + groups), dma(chips), dma(chips), dma(chips), dma(chips), dma(n - 1), dma(n - 1), dma(n - 1), dma(n - 1),
            dma(n - 1), dma(n - 1), dma(z), dma(z), dma(z), dma(z), dma(groups, n - 1), dma(groups, n - 1),
            dma(z), dma(z), dma(z), dma(z), dma(chips), dma(chips), dma(chips - 1), dma(chips - 1), dma(6),
        ],
        ident, args, mib=60,
        out_specs=[ANY, ANY, ANY, VMEM, ANY, ANY, VMEM, ANY, ANY, ANY, VMEM, VMEM],
    )


def spread_body(n_shard, rows, rows_all, local, ss_row, rs_row, ss_fwd, rs_fwd):
    c, s, parity, sibling, others, layers = here(1, n_shard)
    chips = n_shard // 2
    mates = [lax.rem(s + 2 * d, n_shard) for d in range(1, chips)]
    greet(mates + [sibling], [])
    mine = pltpu.make_async_copy(rows, rows_all.at[s], local)
    mine.start()
    first, waits = [], []
    for d in range(1, chips):
        item = push(rows, rows_all.at[s], ss_row.at[d], rs_row.at[d], shard=mates[d - 1])
        item.start()
        first.append(item)
    item = push(rows, rows_all.at[s], ss_fwd.at[0], rs_fwd.at[0], shard=sibling)
    item.start()
    waits.append(item)
    for d in range(1, chips):
        first[d - 1].wait()
        origin = lax.rem(s + n_shard - 2 * d, n_shard)
        item = push(rows_all.at[origin], rows_all.at[origin], ss_fwd.at[d], rs_fwd.at[d], shard=sibling)
        item.start()
        waits.append(item)
    mine.wait()
    for item in waits:
        item.wait()


def spread(n_shard, rows, ident):
    return call(
        functools.partial(spread_body, n_shard),
        [jax.ShapeDtypeStruct((n_shard,) + rows.shape, rows.dtype)],
        [ANY], [DMA] + [DMA((n_shard // 2,))] * 4, ident, (rows,),
    )[0]


def key_back_body(n_ctx, n_shard, parts, out, sib, zsend, zrecv, ss_s, rs_s, ss_z, rs_z):
    c, s, parity, sibling, others, layers = here(n_ctx, n_shard)
    greet([sibling], layers)
    order = list(range(1, n_ctx)) + [0]
    near = {}
    for d in order:
        block = parts.at[1 - parity, :, lax.rem(c + d, n_ctx)]
        near[d] = push(block, sib.at[d], ss_s.at[d], rs_s.at[d], shard=sibling)
        near[d].start()
    far = {}
    for d in order:
        near[d].wait()
        layer = lax.rem(c + d, n_ctx)
        value = parts[parity, :, layer].astype(F32) + sib[d].astype(F32)
        if d:
            zsend[d - 1] = value.astype(BF)
            far[d] = push(zsend.at[d - 1], zrecv.at[d - 1], ss_z.at[d], rs_z.at[d], ctx=layer)
            far[d].start()
    for d in range(1, n_ctx):
        far[d].wait()
        value = value + zrecv[d - 1].astype(F32)
    out[...] = value


def key_back(n_ctx, n_shard, parts, ident):
    block = (parts.shape[1], parts.shape[3], parts.shape[4])
    return call(
        functools.partial(key_back_body, n_ctx, n_shard),
        [jax.ShapeDtypeStruct(block, F32)],
        [VMEM],
        [
            pltpu.VMEM((n_ctx,) + block, BF), pltpu.VMEM((n_ctx - 1,) + block, BF),
            pltpu.VMEM((n_ctx - 1,) + block, BF),
        ] + [DMA((n_ctx,))] * 4,
        ident, (parts,), out_specs=[VMEM],
    )[0]


def finish_body(n_ctx, n_shard, q_cols, tile,
                weights, wide, router, gains, left, right, tokens, gain,
                q_out, kv_out, wide_out, router_out, gains_out, rows_out,
                wide_landing, wide_acc, wide_total, ss_wi, rs_wi, ss_wo, ss_wc, pieces, landing, acc, total, router_in, router_mid, router_far,
                gains_own, gains_in, gains_mid, gains_far, pair, own_part, to_sib, sib, to_chip, got,
                local, ss_w, rs_w, ss_i, rs_i, ss_o, ss_q, ss_k, ss_r, rs_r, ss_g, rs_g, ss_h, rs_h,
                ss_t, rs_t, ss_s, rs_s, ss_c, rs_c):
    c, s, parity, sibling, others, layers = here(n_ctx, n_shard)
    half = n_ctx // 2
    chips = n_shard // 2
    chip = lax.div(s, 2)
    mates = [lax.rem(s + 2 * d, n_shard) for d in range(1, chips)]
    left_side = c < half
    depth = jnp.where(left_side, c, n_ctx - 1 - c)
    inner = jnp.where(left_side, c + 1, c - 1)
    outer = jnp.clip(jnp.where(left_side, c - 1, c + 1), 0, n_ctx - 1)
    middle = depth == half - 1
    inside = depth > 0
    rows, width = rows_out.shape
    greet(others, layers)
    sends, small = [None], []
    for i, peer in enumerate(others):
        item = push(weights.at[peer], pieces.at[i + 1], ss_w.at[i], rs_w.at[i], shard=peer)
        item.start()
        sends.append(item)
    for i, peer in enumerate(others):
        item = push(router.at[peer], router_in.at[i], ss_r.at[i], rs_r.at[i], shard=peer)
        item.start()
        small.append(item)

    def out_copies(j, ref):
        source = lax.rem(s + n_shard - j, n_shard)
        cols = pl.ds(pl.multiple_of(source * q_cols, q_cols), q_cols)
        return (
            pltpu.make_async_copy(ref.at[:, pl.ds(0, q_cols)], q_out.at[:, cols], ss_q.at[j]),
            pltpu.make_async_copy(ref.at[:, pl.ds(q_cols, 128)], kv_out.at[source], ss_k.at[j]),
        )

    def wide_copies(j, ref):
        return (pltpu.make_async_copy(ref, wide_out.at[j], ss_wc.at[j]),)

    class Line:
        def __init__(self, ready, own, acc, landing, total, ss_i, rs_i, ss_o, copies):
            self.ready, self.own, self.acc, self.landing, self.total = ready, own, acc, landing, total
            self.ss_i, self.rs_i, self.ss_o, self.copies = ss_i, rs_i, ss_o, copies

        def inward(self, j, ref):
            at = jnp.where(middle, 1, 0)
            return push(ref, self.landing.at[at, j], self.ss_i.at[j], self.rs_i.at[at, j], ctx=inner)

        def outward(self, j):
            return push(self.total.at[j], self.landing.at[1, j], self.ss_o.at[j], self.rs_i.at[1, j], ctx=outer)

        def arrived(self, which, j):
            push(self.acc.at[j], self.landing.at[which, j], self.ss_i.at[j], self.rs_i.at[which, j],
                 ctx=inner).wait_recv()

        def outermost(self, j):
            @pl.when(jnp.logical_not(inside))
            def _():
                self.ready(j)
                self.inward(j, self.own(j)).start()

        def first_half(self, j):
            @pl.when(inside)
            def _():
                self.ready(j)
                self.arrived(0, j)
                self.acc[j] = (self.own(j)[...].astype(F32) + self.landing[0, j].astype(F32)).astype(BF)
                self.inward(j, self.acc.at[j]).start()

        def second_half(self, j):
            self.arrived(1, j)

            @pl.when(middle)
            def _():
                self.total[j] = (self.acc[j].astype(F32) + self.landing[1, j].astype(F32)).astype(BF)

            @pl.when(jnp.logical_not(middle))
            def _():
                self.total[j] = self.landing[1, j]

            @pl.when(inside)
            def _():
                self.outward(j).start()

            for item in self.copies(j, self.total.at[j]):
                item.start()

        def drain(self, j):
            self.inward(j, self.acc.at[j]).wait_send()

            @pl.when(inside)
            def _():
                self.outward(j).wait_send()

            for item in self.copies(j, self.total.at[j]):
                item.wait()

    line = Line(lambda j: sends[j].wait() if j else None, lambda j: pieces.at[j] if j else weights.at[s],
                acc, landing, total, ss_i, rs_i, ss_o, out_copies)
    wide_line = Line(lambda j: None, lambda j: wide.at[j], wide_acc, wide_landing, wide_total,
                     ss_wi, rs_wi, ss_wo, wide_copies)
    wides = wide.shape[0]
    steps = [(wide_line, j) for j in range(wides)] + [(line, j) for j in range(n_shard)]

    near, far = {}, {}

    def product(d):
        first = pl.multiple_of(lax.rem(chip + d, chips) * (2 * rows), 2 * rows)

        @pl.loop(0, width // tile)
        def _(j):
            cols = pl.ds(pl.multiple_of(j * tile, tile), tile)
            value = lax.dot_general(left[pl.ds(first, 2 * rows), :], right[cols, :],
                                    (((1,), (1,)), ((), ())), preferred_element_type=F32)
            pair[...] = value.reshape(2, rows, tile)
            own_part[d, :, cols] = pair[parity]
            to_sib[d, :, cols] = pair[1 - parity].astype(BF)

        near[d] = push(to_sib.at[d], sib.at[d], ss_s.at[d], rs_s.at[d], shard=sibling)
        near[d].start()

    def chip_sum(d):
        near[d].wait()
        to_chip[d - 1] = (own_part[d] + sib[d].astype(F32)).astype(BF)
        far[d] = push(to_chip.at[d - 1], got.at[d - 1], ss_c.at[d - 1], rs_c.at[d - 1], shard=mates[d - 1])
        far[d].start()

    gain_sends = []

    def last_sum():
        near[0].wait()
        grad = own_part[0] + sib[0].astype(F32)
        for d in range(1, chips):
            far[d].wait()
            grad = grad + got[d - 1].astype(F32)
        x = tokens[...].astype(F32)
        scale = lax.rsqrt(jnp.mean(x * x, axis=-1, keepdims=True) + epsilon)
        unit = x * scale
        scaled = grad * gain[...]
        rows_out[...] = scale * (scaled - unit * jnp.mean(scaled * unit, axis=-1, keepdims=True))
        gains_own[...] = gains[...]
        gains_own[0:1] = jnp.sum(grad * unit, axis=0, keepdims=True)
        mine = pltpu.make_async_copy(gains_own, gains_in.at[s], local.at[0])
        mine.start()
        gain_sends.append(mine)
        for i, peer in enumerate(others):
            item = push(gains_own, gains_in.at[s], ss_g.at[i], rs_g.at[i], shard=peer)
            item.start()
            gain_sends.append(item)

    def small_plane():
        for item in small + gain_sends:
            item.wait()
        gains_mid[...] = gains_in[0]
        for i in range(1, n_shard):
            gains_mid[...] += gains_in[i]
        router_mid[...] = router[s].astype(F32)
        for i in range(n_shard - 1):
            router_mid[...] += router_in[i].astype(F32)
        for i, layer in enumerate(layers):
            push(gains_mid, gains_far.at[c], ss_h.at[i], rs_h.at[i], ctx=layer).start()
            push(router_mid, router_far.at[c], ss_t.at[i], rs_t.at[i], ctx=layer).start()
        pltpu.make_async_copy(gains_mid, gains_far.at[c], local.at[1]).start()
        pltpu.make_async_copy(router_mid, router_far.at[c], local.at[2]).start()

    def small_all():
        pltpu.make_async_copy(gains_mid, gains_far.at[c], local.at[1]).wait()
        pltpu.make_async_copy(router_mid, router_far.at[c], local.at[2]).wait()
        for i, layer in enumerate(layers):
            push(gains_mid, gains_far.at[c], ss_h.at[i], rs_h.at[i], ctx=layer).wait()
            push(router_mid, router_far.at[c], ss_t.at[i], rs_t.at[i], ctx=layer).wait()
        gains_out[...] = gains_far[0]
        router_out[...] = router_far[0]
        for i in range(1, n_ctx):
            gains_out[...] += gains_far[i]
            router_out[...] += router_far[i]

    lag, ahead = 2, 6
    for which, j in steps[:ahead]:
        which.outermost(j)
    for d in list(range(1, chips)) + [0]:
        product(d)
    side = [functools.partial(chip_sum, d) for d in range(1, chips)] + [last_sum, small_plane]
    for n in range(len(steps) + lag):
        if n + ahead < len(steps):
            steps[n + ahead][0].outermost(steps[n + ahead][1])
        if n < len(steps):
            steps[n][0].first_half(steps[n][1])
        if n >= lag:
            steps[n - lag][0].second_half(steps[n - lag][1])
        if n >= 2 and side:
            side.pop(0)()
    for job in side:
        job()
    small_all()
    for which, j in steps:
        which.drain(j)


def finish(n_ctx, n_shard, q_cols, weights, wide, router, gains, left, right, tokens, gain, ident):
    n, rows, cols = weights.shape
    router_shape = router.shape[1:]
    count, width = tokens.shape
    chips = n // 2
    tile = 512
    wides = wide.shape[0]
    return call(
        functools.partial(finish_body, n_ctx, n, q_cols, tile),
        [
            jax.ShapeDtypeStruct((rows, n * q_cols), BF), jax.ShapeDtypeStruct((n, rows, 128), BF),
            jax.ShapeDtypeStruct(wide.shape, BF),
            jax.ShapeDtypeStruct(router_shape, F32), jax.ShapeDtypeStruct(gains.shape, F32),
            jax.ShapeDtypeStruct((count, width), F32),
        ],
        [VMEM] * 8,
        [
            pltpu.VMEM((2,) + wide.shape, BF), pltpu.VMEM(wide.shape, BF), pltpu.VMEM(wide.shape, BF),
            DMA((wides,)), DMA((2, wides)), DMA((wides,)), DMA((wides,)),
            pltpu.VMEM((n, rows, cols), BF), pltpu.VMEM((2, n, rows, cols), BF),
            pltpu.VMEM((n, rows, cols), BF), pltpu.VMEM((n, rows, cols), BF),
            pltpu.VMEM((n - 1,) + router_shape, BF), pltpu.VMEM(router_shape, F32),
            pltpu.VMEM((n_ctx,) + router_shape, F32),
            pltpu.VMEM(gains.shape, F32), pltpu.VMEM((n,) + gains.shape, F32),
            pltpu.VMEM(gains.shape, F32), pltpu.VMEM((n_ctx,) + gains.shape, F32),
            pltpu.VMEM((2, count, tile), F32), pltpu.VMEM((chips, count, width), F32),
            pltpu.VMEM((chips, count, width), BF), pltpu.VMEM((chips, count, width), BF),
            pltpu.VMEM((chips - 1, count, width), BF), pltpu.VMEM((chips - 1, count, width), BF),
            DMA((3,)), DMA((n - 1,)), DMA((n - 1,)), DMA((n,)), DMA((2, n)), DMA((n,)),
            DMA((n,)), DMA((n,)), DMA((n - 1,)), DMA((n - 1,)), DMA((n - 1,)), DMA((n - 1,)),
            DMA((n_ctx - 1,)), DMA((n_ctx - 1,)), DMA((n_ctx - 1,)), DMA((n_ctx - 1,)),
            DMA((chips,)), DMA((chips,)), DMA((chips - 1,)), DMA((chips - 1,)),
        ],
        ident, (weights, wide, router, gains, left, right, tokens, gain), mib=60,
        out_specs=[ANY, ANY, ANY, VMEM, VMEM, VMEM],
    )


def back_body(n_ctx, n_shard, group, heads, wides,
              grad_out, q_in, kv_in, attn_in, qpre_in, kvpre_in, w_out_in, rows_in, w_all_in, cosine, sine, bias, q_gain, k_gain,
              tokens, gain, gains, router, mix_near, mix_part, code,
              q_out, kv_out, wide_out, router_out, gains_out, rows_out, mix_out, mix_land,
              q, kv, attn, qpre, kvpre, w_out, w_all, loads, grads, attn_t, grad_heads, ds_all, p_all, parts, pre, q_sum, k_sum, wide, weights,
              sibk, zsend, zrecv, wide_landing, pieces, landing,
              own_part, pair, to_sib, sib, to_chip, got, router_in, router_mid, router_far,
              gains_own, gains_in, gains_mid, gains_far, mix_rows, mix_sent, mix_recv, local,
              ss_row, rs_row, ss_fwd, rs_fwd, ss_sk, rs_sk, ss_zk, rs_zk,
              ss_wi, rs_wi, ss_wo, ss_wc, ss_w, rs_w, ss_i, rs_i, ss_o, ss_q, ss_k,
              ss_r, rs_r, ss_g, rs_g, ss_h, rs_h, ss_t, rs_t, ss_s, rs_s, ss_c, rs_c, ss_m, rs_m, ss_f, rs_f, ss_v, rs_v):
    c, s, parity, sibling, others, layers = here(n_ctx, n_shard)
    half = n_ctx // 2
    chips = n_shard // 2
    chip = lax.div(s, 2)
    mates = [lax.rem(s + 2 * d, n_shard) for d in range(1, chips)]
    left_side = c < half
    depth = jnp.where(left_side, c, n_ctx - 1 - c)
    inner = jnp.where(left_side, c + 1, c - 1)
    outer = jnp.clip(jnp.where(left_side, c - 1, c + 1), 0, n_ctx - 1)
    middle = depth == half - 1
    inside = depth > 0
    count, width = tokens.shape
    wr = w_all.shape[1]
    cols = heads * HEAD_DIM
    keys = n_ctx * count
    scaling = HEAD_DIM ** -0.5
    own_copies = [
        pltpu.make_async_copy(grad_out, grads.at[s], local.at[0]),
        pltpu.make_async_copy(rows_in, grads, local.at[1]),
    ]
    own_copies[0].start()
    load = [
        pltpu.make_async_copy(a, b, loads.at[n])
        for n, (a, b) in enumerate(((q_in, q), (kv_in, kv), (w_out_in, w_out), (qpre_in, qpre), (attn_in, attn),
                                    (kvpre_in, kvpre), (w_all_in, w_all)))
    ]
    greet(others, layers)

    first, forwards = {}, {}
    for d in range(1, chips):
        first[d] = push(grad_out, grads.at[s], ss_row.at[d], rs_row.at[d], shard=mates[d - 1])
        first[d].start()
    forwards[0] = push(grad_out, grads.at[s], ss_fwd.at[0], rs_fwd.at[0], shard=sibling)
    forwards[0].start()
    for item in load:
        item.start()
    small = []
    for i, peer in enumerate(others):
        item = push(router.at[peer], router_in.at[i], ss_r.at[i], rs_r.at[i], shard=peer)
        item.start()
        small.append(item)
    q_sum[...] = jnp.zeros_like(q_sum)
    k_sum[...] = jnp.zeros_like(k_sum)

    def norm_back(grad, value, norm_gain, total):
        unit, scale = unit_rows(value)
        grad = grad * cosine[...] + pltpu.roll(grad * sine[...], HEAD_DIM // 2, 1)
        total[...] += jnp.sum(grad * unit, axis=0, keepdims=True)
        scaled = grad * norm_gain[...]
        return scale * (scaled - unit * jnp.mean(scaled * unit, axis=-1, keepdims=True))

    slots = mix_near.shape[1]
    mix_fold = Fold(c, mix_sent, mix_recv, ss_f, rs_f)
    tile = mix_rows.shape[2]

    def mix_sums(k, ref):
        table = slot_table(code[flip_bits(lax.div(c, group), k)], slots).T

        @pl.loop(0, width // tile)
        def _(j):
            part = pl.ds(pl.multiple_of(j * tile, tile), tile)
            item = pltpu.make_async_copy(ref.at[:, :, part], mix_rows, local.at[5])
            item.start()
            item.wait()
            value = jnp.dot(table, mix_rows[...].reshape(n_shard * slots, tile), preferred_element_type=F32)
            own_part[:, :, part] = value.reshape(2, count, tile)

    def near_part(d):
        return own_part[lax.rem(flip_bits(c, d), group)]

    def mix_send():
        for i, peer in enumerate(others):
            push(mix_near.at[by_core(peer, n_shard)], mix_land.at[s], ss_m.at[i], rs_m.at[i], shard=peer).start()
        pltpu.make_async_copy(mix_near.at[by_core(s, n_shard)], mix_land.at[s], local.at[6]).start()

    def mix_last():
        for i, peer in enumerate(others):
            push(mix_near.at[by_core(peer, n_shard)], mix_land.at[s], ss_m.at[i], rs_m.at[i], shard=peer).wait()
        pltpu.make_async_copy(mix_near.at[by_core(s, n_shard)], mix_land.at[s], local.at[6]).wait()
        mix_sums(0, mix_land)
        mix_fold.give(1, near_part(1))
        mix_out[...] = near_part(0)

    mix_fold.give_as_is(3, mix_part.at[1])
    near, far = {}, {}

    def seqs_of(d):
        return 2 * lax.rem(chip + chips - d, chips)

    def attention_back(d):
        fs = seqs_of(d)
        grad = lax.dot_general(grads[pl.ds(fs, 2)].reshape(2 * count, width), w_out[...],
                               (((1,), (1,)), ((), ())), preferred_element_type=F32)
        grad_heads[...] = grad.reshape(2, count, cols).astype(BF)

        @pl.loop(0, 2)
        def _(i):
            b = fs + i
            k_all = kv[0, b].reshape(keys, HEAD_DIM)
            v_all = kv[1, b].reshape(keys, HEAD_DIM)
            for h in range(heads):
                hs = slice(h * HEAD_DIM, (h + 1) * HEAD_DIM)
                rs = slice(h * count, (h + 1) * count)
                scores = lax.dot_general(q[b, :, hs], k_all, (((1,), (1,)), ((), ())), preferred_element_type=F32)
                scores = scores * scaling + bias[...]
                raised = jnp.exp(scores - jnp.max(scores, axis=-1, keepdims=True))
                probs = raised / jnp.sum(raised, axis=-1, keepdims=True)
                grad_p = lax.dot_general(grad_heads[i, :, hs], v_all, (((1,), (1,)), ((), ())),
                                         preferred_element_type=F32)
                delta = jnp.sum(probs * grad_p, axis=-1, keepdims=True)
                ds = (probs * (grad_p - delta)).astype(BF)
                ds_all[rs, :] = ds
                p_all[rs, :] = probs.astype(BF)
                grad_q = jnp.dot(ds, k_all, preferred_element_type=F32) * scaling
                pre[b, :, hs] = norm_back(grad_q, qpre[b, :, hs], q_gain, q_sum).astype(BF)
            grad_k, grad_v = jnp.zeros((keys, HEAD_DIM), F32), jnp.zeros((keys, HEAD_DIM), F32)
            stacked_q = jnp.concatenate([q[b, :, h * HEAD_DIM : (h + 1) * HEAD_DIM] for h in range(heads)], axis=0)
            stacked_g = jnp.concatenate(
                [grad_heads[i, :, h * HEAD_DIM : (h + 1) * HEAD_DIM] for h in range(heads)], axis=0
            )
            grad_k = lax.dot_general(ds_all[...], stacked_q, (((0,), (0,)), ((), ())), preferred_element_type=F32)
            grad_v = lax.dot_general(p_all[...], stacked_g, (((0,), (0,)), ((), ())), preferred_element_type=F32)
            parts[0, b] = (grad_k * scaling).astype(BF).reshape(n_ctx, count, HEAD_DIM)
            parts[1, b] = grad_v.astype(BF).reshape(n_ctx, count, HEAD_DIM)

        near[d] = push(parts.at[1 - parity, pl.ds(fs, 2)], sibk.at[d], ss_sk.at[d], rs_sk.at[d], shard=sibling)
        near[d].start()

    def key_sum(d):
        fs = seqs_of(d)
        near[d].wait()
        for i, layer in enumerate(layers):
            zsend[d, i] = (
                parts[parity, pl.ds(fs, 2), layer].astype(F32) + sibk[d, :, layer].astype(F32)
            ).astype(BF)
            far[d, i] = push(zsend.at[d, i], zrecv.at[d, i], ss_zk.at[d, i], rs_zk.at[d, i], ctx=layer)
            far[d, i].start()

    def half_rows(j):
        return pl.ds((j % 2) * (wr // 2), wr // 2)

    def out_copies(j, ref):
        source = lax.rem(s + n_shard - j // 2, n_shard)
        to = pl.ds(pl.multiple_of(source * cols, cols), cols)
        return (
            pltpu.make_async_copy(ref.at[:, pl.ds(0, cols)], q_out.at[half_rows(j), to], ss_q.at[j]),
            pltpu.make_async_copy(ref.at[:, pl.ds(cols, HEAD_DIM)], kv_out.at[source, half_rows(j)], ss_k.at[j]),
        )

    def wide_copies(j, ref):
        step = wide.shape[2]
        return (pltpu.make_async_copy(ref, wide_out.at[:, pl.ds(j * step, step)], ss_wc.at[j]),)

    class Line:
        def __init__(self, ready, own, landing, ss_i, rs_i, ss_o, copies):
            self.ready, self.own, self.landing = ready, own, landing
            self.ss_i, self.rs_i, self.ss_o, self.copies = ss_i, rs_i, ss_o, copies

        def inward(self, j, ref):
            at = jnp.where(middle, 1, 0)
            return push(ref, self.landing.at[at, j], self.ss_i.at[j], self.rs_i.at[at, j], ctx=inner)

        def outward(self, j):
            return push(self.landing.at[1, j], self.landing.at[1, j], self.ss_o.at[j], self.rs_i.at[1, j], ctx=outer)

        def arrived(self, which, j):
            push(self.landing.at[0, j], self.landing.at[which, j], self.ss_i.at[j], self.rs_i.at[which, j],
                 ctx=inner).wait_recv()

        def outermost(self, j):
            @pl.when(jnp.logical_not(inside))
            def _():
                self.ready(j)
                self.inward(j, self.own(j)).start()

        def first_half(self, j):
            @pl.when(inside)
            def _():
                self.ready(j)
                self.arrived(0, j)
                self.landing[0, j] = (self.own(j)[...].astype(F32) + self.landing[0, j].astype(F32)).astype(BF)
                self.inward(j, self.landing.at[0, j]).start()

        def second_half(self, j):
            self.arrived(1, j)

            @pl.when(middle)
            def _():
                self.landing[1, j] = (self.landing[0, j].astype(F32) + self.landing[1, j].astype(F32)).astype(BF)

            @pl.when(inside)
            def _():
                self.outward(j).start()

            for item in self.copies(j, self.landing.at[1, j]):
                item.start()

        def drain(self, j):
            self.inward(j, self.landing.at[0, j]).wait_send()

            @pl.when(inside)
            def _():
                self.outward(j).wait_send()

            for item in self.copies(j, self.landing.at[1, j]):
                item.wait()

    sends = [[] for j in range(n_shard)]
    line = Line(lambda j: [item.wait() for item in sends[j // 2]] if j % 2 == 0 else None,
                lambda j: pieces.at[j // 2, half_rows(j)] if j >= 2 else weights.at[s, half_rows(j)],
                landing, ss_i, rs_i, ss_o, out_copies)
    wide_line = Line(lambda j: None, lambda j: wide.at[j], wide_landing, ss_wi, rs_wi, ss_wo, wide_copies)
    steps = [(wide_line, j) for j in range(wides)] + [(line, j) for j in range(2 * n_shard)]
    lag, ahead = 2, 6

    def advance(n):
        if n + ahead < len(steps):
            steps[n + ahead][0].outermost(steps[n + ahead][1])
        if n < len(steps):
            steps[n][0].first_half(steps[n][1])
        if n >= lag:
            steps[n - lag][0].second_half(steps[n - lag][1])

    step = width // wides
    for item in load[:4]:
        item.wait()
    for d in range(chips):
        if d:
            first[d].wait()
            origin = lax.rem(s + n_shard - 2 * d, n_shard)
            forwards[d] = push(grads.at[origin], grads.at[origin], ss_fwd.at[d], rs_fwd.at[d], shard=sibling)
            forwards[d].start()
        else:
            own_copies[0].wait()
        forwards[d].wait()
        if d + 1 == chips:
            mix_send()
            for item in load[4:]:
                item.wait()
            attn_t[...] = attn[...].reshape(n_shard * count, cols).T
            for j in range(wides):
                block = grads[:, :, j * step : (j + 1) * step].reshape(n_shard * count, step)
                wide[j] = jnp.dot(attn_t[...], block, preferred_element_type=F32).astype(BF)
                if j < ahead:
                    wide_line.outermost(j)
        attention_back(d)
        if d == 0:
            mix_fold.give(2, mix_fold.take(2, mix_part[0].astype(F32)))
        if d:
            key_sum(d - 1)

    rows_all = grads
    own_copies[1].start()
    key_sum(chips - 1)
    advance(0)
    own_copies[1].wait()

    @pl.loop(0, n_shard)
    def _(e):
        block = rows_all[:, :, pl.ds(pl.multiple_of(e * wr, wr), wr)].reshape(n_shard * count, wr)
        right = pre[:, :, pl.ds(0, cols)].reshape(n_shard * count, cols)
        weights[e, :, pl.ds(0, cols)] = lax.dot_general(
            block, right, (((0,), (0,)), ((), ())), preferred_element_type=F32).astype(BF)

    for i, peer in enumerate(others):
        item = push(weights.at[peer, :, pl.ds(0, cols)], pieces.at[i + 1, :, pl.ds(0, cols)],
                    ss_w.at[i], rs_w.at[i], shard=peer)
        item.start()
        sends[i + 1].append(item)
    advance(1)
    for d in range(chips):
        fs = seqs_of(d)
        total = parts[parity, pl.ds(fs, 2), c].astype(F32) + sibk[d, :, c].astype(F32)
        for i in range(n_ctx - 1):
            far[d, i].wait()
            total = total + zrecv[d, i].astype(F32)
        for i in range(2):
            keyed = norm_back(total[i], kvpre[fs + i], k_gain, k_sum)
            pre[fs + i, :, pl.ds(cols, HEAD_DIM)] = jnp.where(parity == 0, keyed, total[i]).astype(BF)

    @pl.loop(0, n_shard)
    def _(e):
        block = rows_all[:, :, pl.ds(pl.multiple_of(e * wr, wr), wr)].reshape(n_shard * count, wr)
        right = pre[:, :, pl.ds(cols, HEAD_DIM)].reshape(n_shard * count, HEAD_DIM)
        weights[e, :, pl.ds(cols, HEAD_DIM)] = lax.dot_general(
            block, right, (((0,), (0,)), ((), ())), preferred_element_type=F32).astype(BF)

    for i, peer in enumerate(others):
        item = push(weights.at[peer, :, pl.ds(cols, HEAD_DIM)], pieces.at[i + 1, :, pl.ds(cols, HEAD_DIM)],
                    ss_v.at[i], rs_v.at[i], shard=peer)
        item.start()
        sends[i + 1].append(item)
    advance(2)

    order = list(range(1, chips)) + [0]
    to_sibling, to_mate = {}, {}

    def product(at):
        fs = 2 * lax.rem(chip + order[at], chips)
        left = pre[pl.ds(fs, 2)].reshape(2 * count, cols + HEAD_DIM)

        @pl.loop(0, n_shard)
        def _(j):
            part = pl.ds(pl.multiple_of(j * wr, wr), wr)
            value = lax.dot_general(left, w_all[j], (((1,), (1,)), ((), ())), preferred_element_type=F32)
            pair[...] = value.reshape(2, count, wr)
            own_part[at % 2, :, part] = pair[parity]
            to_sib[at, :, part] = pair[1 - parity].astype(BF)

        to_sibling[at] = push(to_sib.at[at], sib.at[at], ss_s.at[at], rs_s.at[at], shard=sibling)
        to_sibling[at].start()

    def chip_sum(at):
        to_sibling[at].wait()
        to_chip[at] = (own_part[at % 2] + sib[at].astype(F32)).astype(BF)
        to_mate[at] = push(to_chip.at[at], got.at[at], ss_c.at[at], rs_c.at[at], shard=mates[order[at] - 1])
        to_mate[at].start()

    gain_sends = []

    def last_sum():
        to_sibling[chips - 1].wait()
        grad = own_part[(chips - 1) % 2] + sib[chips - 1].astype(F32)
        for at in range(chips - 1):
            to_mate[at].wait()
            grad = grad + got[at].astype(F32)
        unit, scale = unit_rows(tokens[...].astype(F32))
        scaled = grad * gain[...]
        rows_out[...] = scale * (scaled - unit * jnp.mean(scaled * unit, axis=-1, keepdims=True))
        gains_own[...] = gains[...]
        summed = jnp.sum(grad * unit, axis=0, keepdims=True)
        lanes = gains.shape[1]
        for n in range(width // lanes):
            gains_own[n : n + 1] = summed[:, n * lanes : (n + 1) * lanes]
        n = 2 * width // lanes
        gains_own[n : n + 1] = q_sum[...]
        gains_own[n + 1 : n + 2] = jnp.where(parity == 0, k_sum[...], jnp.zeros_like(k_sum))
        mine = pltpu.make_async_copy(gains_own, gains_in.at[s], local.at[2])
        mine.start()
        gain_sends.append(mine)
        for i, peer in enumerate(others):
            item = push(gains_own, gains_in.at[s], ss_g.at[i], rs_g.at[i], shard=peer)
            item.start()
            gain_sends.append(item)

    def small_plane():
        for item in small + gain_sends:
            item.wait()
        gains_mid[...] = gains_in[0]
        for i in range(1, n_shard):
            gains_mid[...] += gains_in[i]
        total = router[s].astype(F32)
        for i in range(n_shard - 1):
            total = total + router_in[i].astype(F32)
        router_mid[...] = total.astype(BF)
        for i, layer in enumerate(layers):
            push(gains_mid, gains_far.at[c], ss_h.at[i], rs_h.at[i], ctx=layer).start()
            push(router_mid, router_far.at[c], ss_t.at[i], rs_t.at[i], ctx=layer).start()
        pltpu.make_async_copy(gains_mid, gains_far.at[c], local.at[3]).start()
        pltpu.make_async_copy(router_mid, router_far.at[c], local.at[4]).start()

    def small_all():
        pltpu.make_async_copy(gains_mid, gains_far.at[c], local.at[3]).wait()
        pltpu.make_async_copy(router_mid, router_far.at[c], local.at[4]).wait()
        for i, layer in enumerate(layers):
            push(gains_mid, gains_far.at[c], ss_h.at[i], rs_h.at[i], ctx=layer).wait()
            push(router_mid, router_far.at[c], ss_t.at[i], rs_t.at[i], ctx=layer).wait()
        gains_out[...] = gains_far[0]
        router_out[...] = router_far[0].astype(F32)
        for i in range(1, n_ctx):
            gains_out[...] += gains_far[i]
            router_out[...] += router_far[i].astype(F32)

    side = []
    for at in range(chips):
        side.append(functools.partial(product, at))
        if at:
            side.append(functools.partial(chip_sum, at - 1))
    count_steps = len(steps) + lag
    late = {21: last_sum, 23: mix_last, 26: small_plane}
    for n in range(3, count_steps):
        advance(n)
        if side:
            side.pop(0)()
        if n in late:
            late[n]()
    for job in side:
        job()
    small_all()
    mix_out[...] = mix_fold.take(0, mix_out[...])
    mix_fold.drain()
    for which, j in steps:
        which.drain(j)


def back(n_ctx, n_shard, group, heads, args, ident):
    count, width = args[0].shape
    rows_in, w_all, router, gains, mix_near = args[7], args[8], args[17], args[16], args[18]
    n, z, chips, wides = n_shard, n_ctx, n_shard // 2, 16
    wr, cols = w_all.shape[1], heads * HEAD_DIM
    keys = z * count
    sds, scratch = jax.ShapeDtypeStruct, pltpu.VMEM
    router_shape = router.shape[1:]
    dma = lambda *shape: DMA(shape)
    wide_block, block = (cols, width // wides), (wr, cols + HEAD_DIM)
    return call(
        functools.partial(back_body, z, n, group, heads, wides),
        [
            sds((wr, n * cols), BF), sds((n, wr, HEAD_DIM), BF), sds((cols, width), BF), sds(router_shape, F32),
            sds(gains.shape, F32), sds((count, width), F32), sds((count, width), F32), sds(mix_near.shape, BF),
        ],
        [VMEM] + [ANY] * 8 + [VMEM] * 9 + [ANY, VMEM, VMEM],
        [scratch(item.shape, item.dtype) for item in args[1:7] + args[8:9]] + [dma(7)] + [
            scratch((n, count, width), BF), scratch((cols, n * count), BF),
            scratch((2, count, cols), BF), scratch((heads * count, keys), BF), scratch((heads * count, keys), BF),
            scratch((2, n, z, count, HEAD_DIM), BF), scratch((n, count, cols + HEAD_DIM), BF),
            scratch((1, HEAD_DIM), F32), scratch((1, HEAD_DIM), F32),
            scratch((wides,) + wide_block, BF), scratch((n,) + block, BF),
            scratch((chips, 2, z, count, HEAD_DIM), BF), scratch((chips, z - 1, 2, count, HEAD_DIM), BF),
            scratch((chips, z - 1, 2, count, HEAD_DIM), BF), scratch((2, wides) + wide_block, BF),
            scratch((n,) + block, BF), scratch((2, 2 * n, wr // 2, cols + HEAD_DIM), BF),
            scratch((2, count, width), F32), scratch((2, count, wr), F32), scratch((chips, count, width), BF),
            scratch((chips, count, width), BF), scratch((chips - 1, count, width), BF),
            scratch((chips - 1, count, width), BF),
            scratch((n - 1,) + router_shape, BF), scratch(router_shape, BF), scratch((z,) + router_shape, BF),
            scratch(gains.shape, F32), scratch((n,) + gains.shape, F32), scratch(gains.shape, F32),
            scratch((z,) + gains.shape, F32), scratch((n, mix_near.shape[1], 512), BF),
            scratch((z - 1, count, width), BF), scratch((z - 1, count, width), BF), dma(7),
            dma(chips), dma(chips), dma(chips), dma(chips), dma(chips), dma(chips), dma(chips, z - 1), dma(chips, z - 1),
            dma(wides), dma(2, wides), dma(wides), dma(wides), dma(n - 1), dma(n - 1), dma(2 * n), dma(2, 2 * n), dma(2 * n),
            dma(2 * n), dma(2 * n), dma(n - 1), dma(n - 1), dma(n - 1), dma(n - 1), dma(z - 1), dma(z - 1), dma(z - 1), dma(z - 1),
            dma(chips), dma(chips), dma(chips - 1), dma(chips - 1), dma(n - 1), dma(n - 1), dma(z), dma(z), dma(n - 1), dma(n - 1),
        ],
        ident, args, mib=62, out_specs=[ANY, ANY, ANY, VMEM, VMEM, VMEM, VMEM, ANY],
    )


def dispatch_body(n_ctx, n_shard, group, tile, rows, tail, code, recv, tail_recv,
                  zrows, ztail, ready, tail_ready, local, ss_z, rs_z, ss_t, rs_t, ss_x, rs_x, ss_y, rs_y):
    c, s, parity, sibling, others, layers = here(n_ctx, n_shard)
    greet(others, layers)
    count, width = rows.shape
    groups = n_ctx // group
    slots = recv.shape[2]
    own = [pltpu.make_async_copy(rows, zrows.at[c], local.at[0]), pltpu.make_async_copy(tail, ztail.at[c], local.at[1])]
    fans = [
        Fan(n_ctx, c, lambda d: ztail.at[flip_bits(c, d)], ss_t, rs_t, True),
        Fan(n_ctx, c, lambda d: zrows.at[flip_bits(c, d)], ss_z, rs_z, True),
    ]
    fans[0].send(0, tail)
    fans[1].send(0, rows)
    for item in own:
        item.start()
    waits = []
    seen = set()
    for k in range(groups):
        at = flip_bits(lax.div(c, group), k)
        if k == 0:
            for item in own:
                item.wait()
        table = slot_table(code[at], slots)
        for d in fans[0].order():
            if d < (k + 1) * group and d not in seen:
                fans[0].arrival(d)
                fans[1].arrival(d)
                seen.add(d)
        first = pl.multiple_of(at * group, group)
        block = ztail[pl.ds(first, group)].reshape(group * count, -1)
        tail_ready[k] = jnp.dot(table, block, preferred_element_type=F32).astype(BF).reshape(n_shard, slots, -1)

        @pl.loop(0, width // tile)
        def _(j):
            cols = pl.ds(pl.multiple_of(j * tile, tile), tile)
            block = zrows[pl.ds(first, group), :, cols].reshape(group * count, tile)
            value = jnp.dot(table, block, preferred_element_type=F32).astype(BF)
            ready[k, :, :, cols] = value.reshape(n_shard, slots, tile)

        for i, peer in enumerate(others):
            item = push(ready.at[k, peer], recv.at[s, at], ss_x.at[k, i], rs_x.at[k, i], shard=peer)
            item.start()
            waits.append(item)
            item = push(tail_ready.at[k, peer], tail_recv.at[s, at], ss_y.at[k, i], rs_y.at[k, i], shard=peer)
            item.start()
            waits.append(item)
        item = pltpu.make_async_copy(ready.at[k, s], recv.at[s, at], local.at[2 * k + 2])
        item.start()
        waits.append(item)
        item = pltpu.make_async_copy(tail_ready.at[k, s], tail_recv.at[s, at], local.at[2 * k + 3])
        item.start()
        waits.append(item)
    for fan in fans:
        fan.drain()
    for item in waits:
        item.wait()


def dispatch_rows(n_ctx, n_shard, group, capacity, rows, tail, code, ident):
    groups, slots = code.shape[0], group * capacity
    count, width = rows.shape
    few = tail.shape[1]
    return call(
        functools.partial(dispatch_body, n_ctx, n_shard, group, 512),
        [
            jax.ShapeDtypeStruct((n_shard, groups, slots, width), BF),
            jax.ShapeDtypeStruct((n_shard, groups, slots, few), BF),
        ],
        [VMEM, VMEM, VMEM],
        [
            pltpu.VMEM((n_ctx, count, width), BF), pltpu.VMEM((n_ctx, count, few), BF),
            pltpu.VMEM((groups, n_shard, slots, width), BF), pltpu.VMEM((groups, n_shard, slots, few), BF),
            DMA((2 * groups + 2,)), DMA((n_ctx,)), DMA((n_ctx,)), DMA((n_ctx,)), DMA((n_ctx,)),
        ] + [DMA((groups, n_shard - 1))] * 4,
        ident, (rows, tail, code), mib=56,
    )


def combine_body(n_ctx, n_shard, group, tile, rows, tail, mix, code, out, tail_out, mix_out,
                 land, tail_land, value, tail_value, zsend, zrecv, tsend, trecv, msend, mrecv, mix_kept, table, local,
                 ss_x, rs_x, ss_y, rs_y, ss_z, rs_z, ss_t, rs_t, ss_m, rs_m):
    c, s, parity, sibling, others, layers = here(n_ctx, n_shard)
    greet(others, layers)
    count, width = out.shape
    groups = n_ctx // group
    slots = rows.shape[2]
    near = {}
    for k in reversed(range(groups)):
        at = flip_bits(lax.div(c, group), k)
        near[k] = []
        for i, peer in enumerate(others):
            item = push(rows.at[peer, at], land.at[k, s], ss_x.at[k, i], rs_x.at[k, i], shard=peer)
            item.start()
            near[k].append(item)
            item = push(tail.at[peer, at], tail_land.at[k, s], ss_y.at[k, i], rs_y.at[k, i], shard=peer)
            item.start()
            near[k].append(item)
        item = pltpu.make_async_copy(rows.at[s, at], land.at[k, s], local.at[k, 0])
        item.start()
        near[k].append(item)
        item = pltpu.make_async_copy(tail.at[s, at], tail_land.at[k, s], local.at[k, 1])
        item.start()
        near[k].append(item)
    for k in range(groups):
        table[k] = slot_table(code[flip_bits(lax.div(c, group), k)], slots).T

    def local_sums(k, block_of):
        @pl.loop(0, width // tile)
        def _(j):
            cols = pl.ds(pl.multiple_of(j * tile, tile), tile)
            value[:, cols] = jnp.dot(table[k], block_of(cols), preferred_element_type=F32)

    def part(ref, d):
        place = lax.rem(flip_bits(c, d), group)
        return ref[pl.ds(pl.multiple_of(place * count, count), count), :]

    def in_group(k):
        return sorted(range(k * group, (k + 1) * group), key=lambda d: (lowest(d) or n_ctx, d))

    mix_fold = Fold(c, msend, mrecv, ss_m, rs_m)
    for k in reversed(range(groups)):
        at = flip_bits(lax.div(c, group), k)
        local_sums(k, lambda cols: mix[:, at, :, cols].reshape(n_shard * slots, tile))
        for d in in_group(k):
            if lowest(d) == 1:
                mix_fold.give(d, part(value, d))
            else:
                mix_kept[d // 2] = part(value, d)
    fold = Fold(c, zsend, zrecv, ss_z, rs_z)
    tail_fold = Fold(c, tsend, trecv, ss_t, rs_t)
    for k in reversed(range(groups)):
        for item in near[k]:
            item.wait()
        local_sums(k, lambda cols: land[k, :, :, cols].reshape(n_shard * slots, tile))
        tail_value[...] = jnp.dot(
            table[k], tail_land[k].reshape(n_shard * slots, -1), preferred_element_type=F32
        )
        for d in in_group(k):
            if lowest(d) == 1:
                fold.give(d, part(value, d))
                tail_fold.give(d, part(tail_value, d))
        for d in in_group(k):
            if lowest(d) != 1:
                if d:
                    mix_fold.give(d, mix_fold.take(d, mix_kept[d // 2]))
                    fold.give(d, fold.take(d, part(value, d)))
                    tail_fold.give(d, tail_fold.take(d, part(tail_value, d)))
                else:
                    mix_out[...] = mix_fold.take(0, mix_kept[0])
                    out[...] = fold.take(0, part(value, 0))
                    tail_out[...] = tail_fold.take(0, part(tail_value, 0))
    for item in (mix_fold, fold, tail_fold):
        item.drain()


def combine_rows(n_ctx, n_shard, group, rows, tail, mix, code, ident):
    groups, slots, width = rows.shape[1:]
    few = tail.shape[3]
    count = code.shape[2] // group
    sds = jax.ShapeDtypeStruct
    return call(
        functools.partial(combine_body, n_ctx, n_shard, group, 512),
        [sds((count, width), F32), sds((count, few), F32), sds((count, width), F32)],
        [VMEM] * 4,
        [
            pltpu.VMEM((groups, n_shard, slots, width), BF), pltpu.VMEM((groups, n_shard, slots, few), BF),
            pltpu.VMEM((group * count, width), F32), pltpu.VMEM((group * count, few), F32),
            pltpu.VMEM((n_ctx - 1, count, width), BF), pltpu.VMEM((n_ctx - 1, count, width), BF),
            pltpu.VMEM((n_ctx - 1, count, few), BF), pltpu.VMEM((n_ctx - 1, count, few), BF),
            pltpu.VMEM((n_ctx - 1, count, width), BF), pltpu.VMEM((n_ctx - 1, count, width), BF),
            pltpu.VMEM((n_ctx // 2, count, width), F32), pltpu.VMEM((groups, group * count, n_shard * slots), BF),
            DMA((groups, 2)),
        ] + [DMA((groups, n_shard - 1))] * 4 + [DMA((n_ctx,))] * 6,
        ident, (rows, tail, mix, code), mib=60, out_specs=[VMEM] * 3,
    )


def expert_body(n_ctx, n_shard, group, half, tile,
                rows, tail, code, gate_in, up_in, down_in, cot_in,
                out, tail_out, mix_near, mix_far, mix_part, g_gate, g_up, g_down,
                w_gate, w_up, w_down, loaded, zrows, ztail, ready, tail_ready, recv, tail_recv, cot, back_rows, back_tail, land, tail_land,
                hidden, grad_gate, grad_up, work, slot_dot, table, tail_value,
                zrecv, tsend, trecv, stage, stage_d, local, ss_a, rs_a,
                ss_z, rs_z, ss_t, rs_t, ss_x, rs_x, ss_y, rs_y, ss_d, rs_d, ss_e, rs_e, ss_m, rs_m,
                ss_fz, rs_fz, ss_ft, rs_ft, ss_st, ss_sd):
    c, s, parity, sibling, others, layers = here(n_ctx, n_shard)
    count, width = rows.shape
    few = tail.shape[1]
    inner = w_gate.shape[1]
    groups = n_ctx // group
    slots = recv.shape[2]
    chunk = half * slots
    experts = n_ctx * n_shard
    expert = c * n_shard + s
    mine = by_core(s, n_shard)
    loads = [
        pltpu.make_async_copy(rows, zrows.at[c], local.at[0]),
        pltpu.make_async_copy(tail, ztail.at[c], local.at[1]),
    ] + [
        pltpu.make_async_copy(cot_in.at[flip_bits(lax.div(c, group), k)], cot.at[k], local.at[2 + 2 * groups + k])
        for k in range(groups)
    ]
    greet(others, layers)
    fan = Fan(n_ctx, c, lambda d: ztail.at[flip_bits(c, d)], ss_t, rs_t, True)
    fan.send(0, tail)
    near_layer, far_layer = flip_bits(c, 1), flip_bits(c, 2)
    sides = [slice(0, width // 2), slice(width // 2, width)]
    near = push(rows, zrows.at[c], ss_z.at[0], rs_z.at[0], ctx=near_layer)
    near.start()
    edge = jnp.logical_or(c == 0, c == n_ctx - 1)
    away = [push(rows.at[:, side], zrows.at[c, :, side], ss_z.at[1 + n], rs_z.at[1 + n], ctx=far_layer)
            for n, side in enumerate(sides)]
    passed = [push(zrows.at[far_layer, :, side], zrows.at[far_layer, :, side], ss_z.at[3 + n], rs_z.at[3 + n],
                   ctx=near_layer) for n, side in enumerate(sides)]

    @pl.when(jnp.logical_not(edge))
    def _():
        for item in away:
            item.start()

    loads += [
        pltpu.make_async_copy(a, b, loaded.at[n])
        for n, (a, b) in enumerate(((gate_in, w_gate), (up_in, w_up), (down_in, w_down)))
    ]
    loads[0].start()
    loads[1].start()

    sent = {0: [], 1: []}
    early = (slots // group) // 16 * 16
    place = lax.rem(c, group)
    early_at = pl.multiple_of(place * (slots - early), 16)
    late_at = pl.multiple_of((1 - place) * early, 16)

    def some_slots(rows_code, first, amount):
        places = (lax.broadcasted_iota(jnp.int32, (amount, rows_code.shape[1]), 0) + first).astype(F32)
        return jnp.concatenate(
            [(places == rows_code[e : e + 1, :]).astype(BF) for e in range(n_shard)], axis=0
        )

    own_code = code[lax.div(c, group), :, pl.ds(pl.multiple_of(place * count, count), count)]
    early_picks = some_slots(own_code, early_at, early)

    @pl.loop(0, width // tile)
    def _(j):
        cols = pl.ds(pl.multiple_of(j * tile, tile), tile)
        moved = jnp.dot(early_picks, rows[:, cols], preferred_element_type=F32).astype(BF)
        ready[0, :, pl.ds(early_at, early), cols] = moved.reshape(n_shard, early, tile)

    for i, peer in enumerate(others):
        sent[0].append(push(ready.at[0, peer, pl.ds(early_at, early)], recv.at[0, mine, pl.ds(early_at, early)],
                            ss_a.at[i], rs_a.at[i], shard=peer))
        sent[0][-1].start()
    for item in loads[2:]:
        item.start()
    loads[0].wait()
    loads[1].wait()
    near.wait_send()

    @pl.when(edge)
    def _():
        for item in away:
            item.start()

    near.wait_recv()
    for k in range(groups):
        at = flip_bits(lax.div(c, group), k)
        whole = slot_table(code[at], slots)
        table[k] = whole.T
        for d in (2, 3) if k else (1,):
            fan.arrival(d)
        first = pl.multiple_of(at * group, group)
        block = ztail[pl.ds(first, group)].reshape(group * count, few)
        tail_ready[k] = jnp.dot(whole, block, preferred_element_type=F32).astype(BF).reshape(n_shard, slots, few)
        amount = slots if k else slots - early
        begin = 0 if k else late_at
        span = pl.ds(begin, amount)
        picks = some_slots(code[at], begin, amount)
        for n, side in enumerate(sides if k else [slice(0, width)]):
            if k:
                if n == 0:
                    for m in range(2):
                        away[m].wait_recv()
                        passed[m].start()
                passed[n].wait_recv()

            @pl.loop(side.start // tile, side.stop // tile)
            def _(j):
                cols = pl.ds(pl.multiple_of(j * tile, tile), tile)
                block = zrows[pl.ds(first, group), :, cols].reshape(group * count, tile)
                moved = jnp.dot(picks, block, preferred_element_type=F32).astype(BF)
                ready[k, :, span, cols] = moved.reshape(n_shard, amount, tile)

            fresh = []
            for i, peer in enumerate(others):
                fresh.append(push(ready.at[k, peer, span, side], recv.at[k, mine, span, side],
                                  ss_x.at[k + n, i], rs_x.at[k + n, i], shard=peer))
            if n == 0:
                for i, peer in enumerate(others):
                    fresh.append(push(tail_ready.at[k, peer], tail_recv.at[k, mine], ss_y.at[k, i], rs_y.at[k, i], shard=peer))
                fresh.append(pltpu.make_async_copy(tail_ready.at[k, s], tail_recv.at[k, mine], local.at[3 + 2 * k]))
            if n == k:
                fresh.append(pltpu.make_async_copy(ready.at[k, s], recv.at[k, mine], local.at[2 + 2 * k]))
            for item in fresh:
                item.start()
            sent[k] += fresh
    fan.drain()
    for item in away + passed:
        item.wait_send()
    for item in loads[2:]:
        item.wait()

    gate_pre, up_pre = work.at[0:chunk, 0:inner], work.at[0:chunk, inner : 2 * inner]
    value = work.at[0 : group * count, 0:width]
    column = lax.broadcasted_iota(jnp.int32, (1, few), 1)
    is_coarse, is_fine = column == expert, column == experts + expert

    def send_back(src, dst, p, ss, rs):
        e = from_core(p, n_shard)

        @pl.when(s != e)
        def _():
            push(src.at[p], dst.at[s], ss.at[e], rs.at[s], shard=e).start()

        @pl.when(s == e)
        def _():
            pltpu.make_async_copy(src.at[p], dst.at[e], rs.at[e]).start()

    def wait_back(src, dst, ss, rs):
        for p in range(n_shard):
            e = from_core(p, n_shard)

            @pl.when(s != e)
            def _():
                push(src.at[p], dst.at[e], ss.at[e], rs.at[e], shard=e).wait()

            @pl.when(s == e)
            def _():
                pltpu.make_async_copy(src.at[p], dst.at[e], rs.at[e]).wait()

    def experts_part(k, h):
        of = slice(h * half, (h + 1) * half)
        r = pl.ds((k * n_shard + h * half) * slots, chunk)
        gates = jnp.sum(
            jnp.where(is_coarse | is_fine, tail_recv[k, of].reshape(chunk, few).astype(F32), 0.0), axis=1, keepdims=True
        )

        @pl.loop(0, inner // 256)
        def _(j):
            cols = pl.ds(pl.multiple_of(j * 256, 256), 256)
            x = recv[k, of].reshape(chunk, width)
            g = jnp.dot(x, w_gate[:, cols], preferred_element_type=F32)
            u = jnp.dot(x, w_up[:, cols], preferred_element_type=F32)
            gate_pre[:, cols] = g
            up_pre[:, cols] = u
            hidden[r, cols] = (g * jax.nn.sigmoid(g) * u).astype(BF)

        slot_dot[...] = jnp.zeros_like(slot_dot)

        @pl.loop(0, width // tile)
        def _(j):
            cols = pl.ds(pl.multiple_of(j * tile, tile), tile)
            o = jnp.dot(hidden[r, :], w_down[:, cols], preferred_element_type=F32).astype(BF).astype(F32)
            up_row = cot[k, of, :, cols].reshape(chunk, tile).astype(F32)
            slot_dot[...] += jnp.sum(o * up_row, axis=1, keepdims=True)
            ready[k, of, :, cols] = (gates * o).astype(BF).reshape(half, slots, tile)
            cot[k, of, :, cols] = (gates * up_row).astype(BF).reshape(half, slots, tile)

        coarse = slot_dot[...].astype(BF).astype(F32)
        fine = slot_dot[...] - coarse
        back_tail[k, of] = jnp.where(is_coarse, coarse, jnp.where(is_fine, fine, 0.0)).astype(BF).reshape(half, slots, few)

        @pl.loop(0, inner // 256)
        def _(j):
            cols = pl.ds(pl.multiple_of(j * 256, 256), 256)
            gh = lax.dot_general(cot[k, of].reshape(chunk, width), w_down[cols, :], (((1,), (1,)), ((), ())),
                                 preferred_element_type=F32)
            g, u = gate_pre[:, cols], up_pre[:, cols]
            sig = jax.nn.sigmoid(g)
            grad_gate[r, cols] = (gh * u * (sig * (1.0 + g * (1.0 - sig)))).astype(BF)
            grad_up[r, cols] = (gh * (g * sig)).astype(BF)

        @pl.loop(0, width // tile)
        def _(j):
            cols = pl.ds(pl.multiple_of(j * tile, tile), tile)
            gx = lax.dot_general(grad_gate[r, :], w_gate[cols, :], (((1,), (1,)), ((), ())), preferred_element_type=F32)
            gx += lax.dot_general(grad_up[r, :], w_up[cols, :], (((1,), (1,)), ((), ())), preferred_element_type=F32)
            back_rows[k, of, :, cols] = gx.astype(BF).reshape(half, slots, tile)

    def send_part(k, h):
        for p in range(h * half, (h + 1) * half):
            send_back(back_rows.at[k], land.at[k], p, ss_d.at[k], rs_d.at[k])
            send_back(back_tail.at[k], tail_land.at[k], p, ss_e.at[k], rs_e.at[k])

    halves = n_shard // half
    for k in range(groups):
        for item in sent[k]:
            item.wait()
        for h in range(halves):
            experts_part(k, h)
            if k or h + 1 < halves:
                send_part(k, h)
    send_part(0, halves - 1)
    for p in range(n_shard):
        send_back(ready.at[groups - 1], mix_far, p, ss_m, rs_m)
    keep = pltpu.make_async_copy(ready.at[0], mix_near, local.at[0])
    keep.start()

    everything = groups * n_shard * slots

    def stage_out(j, which):
        at = pl.ds(pl.multiple_of(j * 256, 256), 256)
        return pltpu.make_async_copy(stage.at[which], (g_gate, g_up)[which].at[at], ss_st.at[which])

    @pl.loop(0, width // 256)
    def _(j):
        x = recv[:, :, :, pl.ds(pl.multiple_of(j * 256, 256), 256)].reshape(everything, 256)
        for which, grad in enumerate((grad_gate, grad_up)):
            total = lax.dot_general(x, grad[...], (((0,), (0,)), ((), ())), preferred_element_type=F32).astype(BF)

            @pl.when(j >= 1)
            def _():
                stage_out(j - 1, which).wait()

            stage[which] = total
            stage_out(j, which).start()

    def down_out(j):
        return pltpu.make_async_copy(stage_d, g_down.at[:, pl.ds(pl.multiple_of(j * 256, 256), 256)], ss_sd)

    @pl.loop(0, width // 256)
    def _(j):
        grad = cot[:, :, :, pl.ds(pl.multiple_of(j * 256, 256), 256)].reshape(everything, 256)
        total = lax.dot_general(
            hidden[...], grad, (((0,), (0,)), ((), ())), preferred_element_type=F32).astype(BF)

        @pl.when(j >= 1)
        def _():
            down_out(j - 1).wait()

        stage_d[...] = total
        down_out(j).start()

    last = width // 256 - 1
    stage_out(last, 0).wait()
    stage_out(last, 1).wait()
    down_out(last).wait()

    def local_sums(k, ref):
        @pl.loop(0, width // tile)
        def _(j):
            cols = pl.ds(pl.multiple_of(j * tile, tile), tile)
            block = ref[k, :, :, cols].reshape(n_shard * slots, tile)
            value[:, cols] = jnp.dot(table[k], block, preferred_element_type=F32)

    def part(ref, d):
        place = lax.rem(flip_bits(c, d), group)
        return ref[pl.ds(pl.multiple_of(place * count, count), count), :]

    folds = [Fold(c, zrows.at[:, :, side], zrecv.at[:, :, side], ss_fz.at[n], rs_fz.at[n]) for n, side in enumerate(sides)]
    tail_fold = Fold(c, tsend, trecv, ss_ft, rs_ft)
    for k in reversed(range(groups)):
        wait_back(back_rows.at[k], land.at[k], ss_d.at[k], rs_d.at[k])
        wait_back(back_tail.at[k], tail_land.at[k], ss_e.at[k], rs_e.at[k])
        local_sums(k, land)
        tail_value[...] = jnp.dot(table[k], tail_land[k].reshape(n_shard * slots, few), preferred_element_type=F32)
        if k:
            tail_fold.give(3, part(tail_value, 3))
            folds[0].give(3, part(value, 3)[:, sides[0]])
            folds[0].items[3].wait_send()
            folds[0].left.add(3)
            folds[1].give(3, part(value, 3)[:, sides[1]])
            for fold, side in zip(folds, sides):
                fold.give(2, fold.take(2, part(value, 2)[:, side]))
            tail_fold.give(2, tail_fold.take(2, part(tail_value, 2)))
        else:
            tail_fold.give(1, part(tail_value, 1))
            for fold, side in zip(folds, sides):
                fold.give(1, part(value, 1)[:, side])
    out[...] = part(value, 0)
    wait_back(ready.at[groups - 1], mix_far, ss_m, rs_m)
    keep.wait()
    again = pltpu.make_async_copy(mix_far, ready.at[0], local.at[0])
    again.start()
    again.wait()

    @pl.loop(0, width // tile)
    def _(j):
        cols = pl.ds(pl.multiple_of(j * tile, tile), tile)
        block = ready[0, :, :, cols].reshape(n_shard * slots, tile)
        value[:, cols] = jnp.dot(table[1], block, preferred_element_type=F32)

    for d in (2, 3):
        mix_part[d - 2] = part(value, d).astype(BF)
    for fold, side in zip(folds, sides):
        out[:, side] = fold.take(0, out[:, side])
    tail_out[...] = tail_fold.take(0, part(tail_value, 0))
    for fold in folds + [tail_fold]:
        fold.drain()


def run_experts(n_ctx, n_shard, group, capacity, rows, tail, code, w_gate, w_up, w_down, cot_rows, ident):
    n, z, groups, slots = n_shard, n_ctx, code.shape[0], group * capacity
    count, width = rows.shape
    few, inner, half = tail.shape[1], w_gate.shape[1], n_shard // 2
    everything, chunk = groups * n * slots, half * slots
    sds, scratch = jax.ShapeDtypeStruct, pltpu.VMEM
    dma = lambda *shape: DMA(shape)
    wide, thin = (groups, n, slots, width), (groups, n, slots, few)
    return call(
        functools.partial(expert_body, z, n, group, half, 512),
        [
            sds((count, width), F32), sds((count, few), F32), sds((n, slots, width), BF), sds((n, slots, width), BF),
            sds((2, count, width), BF), sds((width, inner), BF), sds((width, inner), BF), sds((inner, width), BF),
        ],
        [VMEM] * 3 + [ANY] * 4,
        [scratch(item.shape, BF) for item in (w_gate, w_up, w_down)] + [
            dma(3),
            scratch((z, count, width), BF), scratch((z, count, few), BF), scratch(wide, BF), scratch(thin, BF),
            scratch(wide, BF), scratch(thin, BF), scratch(wide, BF), scratch(wide, BF), scratch(thin, BF),
            scratch(wide, BF), scratch(thin, BF),
            scratch((everything, inner), BF), scratch((everything, inner), BF), scratch((everything, inner), BF),
            scratch((max(chunk, group * count), max(2 * inner, width)), F32), scratch((chunk, 1), F32),
            scratch((groups, group * count, n * slots), BF),
            scratch((group * count, few), F32), scratch((z - 1, count, width), BF),
            scratch((z - 1, count, few), BF), scratch((z - 1, count, few), BF),
            scratch((2, 256, inner), BF), scratch((inner, 256), BF), dma(2 + 3 * groups), dma(n - 1), dma(n - 1),
        ] + [dma(5)] * 2 + [dma(z)] * 2 + [dma(groups + 1, n - 1)] * 2 + [dma(groups, n - 1)] * 2 + [dma(groups, n)] * 4
        + [dma(n)] * 2 + [dma(2, z)] * 2 + [dma(z)] * 2 + [dma(2), DMA],
        ident, (rows, tail, code, w_gate, w_up, w_down, cot_rows), mib=62, out_specs=[VMEM] * 2 + [ANY] * 2 + [VMEM] + [ANY] * 3,
    )


def finish_types_body(q, o, g, u, d, kv, tokens, part, mid, mix, gains, router,
                      q_out, o_out, g_out, u_out, d_out, k_out, v_out, tokens_out, mixed_out,
                      attn_gain, ffn_gain, q_gain, k_gain, router_out):
    for source, target in ((q, q_out), (o, o_out), (g, g_out), (u, u_out), (d, d_out)):
        target[...] = source[...].astype(F32)
    for head in range(kv.shape[0] // 2):
        lanes = slice(head * HEAD_DIM, (head + 1) * HEAD_DIM)
        k_out[:, lanes] = kv[2 * head].astype(F32)
        v_out[:, lanes] = kv[2 * head + 1].astype(F32)
    tokens_out[...] = tokens[...] + part[...]
    mixed_out[...] = (mid[...] + mix[...]).astype(BF)
    n = attn_gain.shape[0]
    attn_gain[...] = gains[0:n]
    ffn_gain[...] = gains[n : 2 * n]
    q_gain[...] = gains[2 * n : 2 * n + 1]
    k_gain[...] = gains[2 * n + 1 : 2 * n + 2]
    router_out[...] = router[...]


def finish_types(q, o, g, u, d, kv, tokens, part, mid, mix, gains, router):
    steps = 8
    sds = jax.ShapeDtypeStruct
    heads, wr, lanes = kv.shape
    width = tokens.shape[1]
    by_rows = lambda shape: pl.BlockSpec((shape[0] // steps,) + shape[1:], lambda i: (i, 0))
    whole = lambda shape: pl.BlockSpec(shape, lambda i: (0, 0))
    kv_shape, gain_shape, one = (wr, heads // 2 * lanes), (width // lanes, lanes), (1, lanes)
    ins = [q, o, g, u, d, kv, tokens, part, mid, mix, gains, router]
    in_specs = [by_rows(item.shape) for item in (q, o, g, u, d)]
    in_specs += [pl.BlockSpec((heads, wr // steps, lanes), lambda i: (0, i, 0))]
    in_specs += [by_rows(tokens.shape)] * 4 + [whole(gains.shape), whole(router.shape)]
    outs = [sds(item.shape, F32) for item in (q, o, g, u, d)] + [sds(kv_shape, F32)] * 2
    outs += [sds(tokens.shape, F32), sds(tokens.shape, BF)]
    out_specs = [by_rows(item.shape) for item in outs]
    small = [gain_shape, gain_shape, one, one, router.shape]
    return pl.pallas_call(
        finish_types_body,
        grid=(steps,),
        out_shape=outs + [sds(shape, F32) for shape in small],
        in_specs=in_specs,
        out_specs=out_specs + [whole(shape) for shape in small],
        compiler_params=pltpu.CompilerParams(vmem_limit_bytes=62 * 2**20),
    )(*ins)


def rms_scale(hidden, gain):
    return hidden * lax.rsqrt(jnp.mean(hidden * hidden, axis=-1, keepdims=True) + epsilon) * gain


def rotate(headwise, places):
    half_size = headwise.shape[-1] // 2
    frequency = rope_base ** (-jnp.arange(half_size, dtype=F32) * 2.0 / headwise.shape[-1])
    angles = places.astype(F32)[:, None] * frequency[None, :]
    cosine = jnp.cos(angles)[:, None, :]
    sine = jnp.sin(angles)[:, None, :]
    former = headwise[..., :half_size]
    latter = headwise[..., half_size:]
    return jnp.concatenate(
        [former * cosine - latter * sine, latter * cosine + former * sine], axis=-1
    )


def place_of(row_ids, order, block_rows):
    block_ids = jnp.arange(order.shape[0], dtype=jnp.int32)
    owner_block = row_ids // block_rows
    picked_block = jnp.sum(
        jnp.where(owner_block[:, None] == block_ids[None, :], order[None, :], 0), axis=1
    )
    return picked_block * block_rows + row_ids % block_rows


def dot(left, right):
    return jnp.dot(left, right, preferred_element_type=F32)


def contract_rows(left, right):
    return lax.dot_general(left, right, (((0,), (0,)), ((), ())), preferred_element_type=F32)


def contract_cols(left, right):
    return lax.dot_general(left, right, (((1,), (1,)), ((), ())), preferred_element_type=F32)


def exchange_shard(x):
    return lax.all_to_all(x, "shard", split_axis=0, concat_axis=0, tiled=True)


def gather_ctx(x):
    return lax.all_gather(x, "ctx", axis=0, tiled=False)


def shards(
    tokens,
    cotangent,
    block_order,
    routes,
    attn_gain,
    w_query,
    key_weight,
    value_weight,
    query_gain,
    key_gain,
    w_out,
    ffn_gain,
    w_router,
    w_gate,
    w_up,
    w_down,
):
    rows = tokens.shape[1]
    width = tokens.shape[2]
    ctx_count = lax.axis_size("ctx")
    shard_count = lax.axis_size("shard")
    my_ctx = lax.axis_index("ctx")
    my_shard = lax.axis_index("shard")
    experts = ctx_count * shard_count
    block_rows = rows // 2
    heads = QUERY_HEADS // shard_count
    head_cols = heads * HEAD_DIM
    sharers = shard_count // KEY_VALUE_HEADS
    score_scale = HEAD_DIM ** (-0.5)
    top_count = routes.shape[2]
    capacity = rows * top_count // experts + max(rows * top_count // (4 * experts), 1)
    sequence = rows * ctx_count
    plane = rows * shard_count
    wrows = width // shard_count

    inputs = tokens[0].astype(F32)
    upstream_b = cotangent[0]
    upstream = upstream_b.astype(F32)

    group = 1
    while group * capacity % 16:
        group *= 2
    groups = ctx_count // group
    small = plane * width <= 2**21 and ctx_count == 4 and group == 2
    slot_rows = shard_count * ctx_count * capacity
    block_shape = (shard_count, groups, group * capacity)
    row_ids = my_ctx * rows + jnp.arange(rows, dtype=jnp.int32)
    q_places = place_of(row_ids, block_order, block_rows)
    k_places = place_of(jnp.arange(sequence, dtype=jnp.int32), block_order, block_rows)
    bias = jnp.where(k_places[None, :] <= q_places[:, None], 0.0, -1e30).astype(F32)
    frequency = rope_base ** (-jnp.arange(HEAD_DIM // 2, dtype=F32) * 2.0 / HEAD_DIM)
    angles = q_places.astype(F32)[:, None] * frequency[None, :]
    cosine = jnp.concatenate([jnp.cos(angles)] * 2, axis=1)
    sine = jnp.concatenate([-jnp.sin(angles), jnp.sin(angles)], axis=1)
    (
        normed_all, w_mine, router_all, code, upstream_rows, query_pre, kv_pre, queries, kv_all, attn_rows, middle,
        second_b,
    ) = front(
        ctx_count, shard_count, group, capacity, KEY_VALUE_HEADS, small,
        (
            tokens[0], attn_gain[None], w_query, key_weight, value_weight, routes[0].T, w_router.T, upstream_b,
            cosine, sine, bias, query_gain[None], key_gain[None], w_out, ffn_gain[None],
        ),
        0,
    )
    is_key = lax.rem(my_shard, 2) == 0
    part_count = sharers // 2

    def prep(pre, gain):
        shape = pre.shape
        flat = pre.reshape(-1, rows, shape[-2], HEAD_DIM)
        return jax.vmap(lambda v: rotate(rms_scale(v, gain), q_places))(flat).reshape(shape)

    logits = contract_cols(second_b, router_all)
    chosen = jnp.sum(
        (routes[0][:, :, None] == jnp.arange(experts, dtype=jnp.int32)).astype(F32), axis=1
    )

    def gates_of(log, mask):
        masked = jnp.where(mask > 0, log, -1e30)
        peak = jnp.max(masked, axis=-1, keepdims=True)
        risen = jnp.exp(masked - peak) * mask
        return risen / jnp.maximum(jnp.sum(risen, axis=-1, keepdims=True), 1e-30)

    gates = gates_of(logits, chosen)

    tail_cols = -(-2 * experts // 128) * 128

    def two_parts(value):
        coarse = value.astype(BF).astype(F32)
        return coarse.astype(BF), (value - coarse).astype(BF)

    gates_two = jnp.concatenate(two_parts(gates), axis=1)
    gates_two = jnp.pad(gates_two, ((0, 0), (0, tail_cols - 2 * experts)))
    if small:
        grad_second, back_tail, mix_near, unused, mix_part, grad_w_gate, grad_w_up, grad_w_down = run_experts(
            ctx_count, shard_count, group, capacity, second_b, gates_two, code, w_gate[0], w_up[0], w_down[0],
            upstream_rows, 3,
        )
    else:
        received, gate_tail = dispatch_rows(ctx_count, shard_count, group, capacity, second_b, gates_two, code, 3)
        received = received.reshape(slot_rows, width)
        my_expert = my_ctx * shard_count + my_shard
        upstream_rows = jnp.swapaxes(upstream_rows, 0, 1).reshape(slot_rows, width)
        column = jnp.arange(tail_cols, dtype=jnp.int32)[None, :]
        mine_column = (column == my_expert) | (column == experts + my_expert)
        gate_tail = gate_tail.reshape(slot_rows, tail_cols).astype(F32)
        slot_gates = jnp.sum(jnp.where(mine_column, gate_tail, 0.0), axis=1, keepdims=True)
        gate_pre = dot(received, w_gate[0])
        up_pre = dot(received, w_up[0])
        activated = jax.nn.silu(gate_pre)
        hidden_b = (activated * up_pre).astype(BF)
        expert_out = dot(hidden_b, w_down[0]).astype(BF)
        expert_out_f = expert_out.astype(F32)
        mix_sent = (slot_gates * expert_out_f).astype(BF)
        mix_sent, upstream_rows, expert_out = lax.optimization_barrier((mix_sent, upstream_rows, expert_out))
        expert_out_f = expert_out.astype(F32)
        mix_back = exchange_shard(mix_sent.reshape(block_shape + (width,)))
        upstream_rows = upstream_rows.astype(F32)
        slot_dot = jnp.sum(expert_out_f * upstream_rows, axis=1, keepdims=True)
        grad_expert = (slot_gates * upstream_rows).astype(BF)
        grad_w_down = contract_rows(hidden_b, grad_expert)
        grad_hidden = contract_cols(grad_expert, w_down[0])
        sigmoid_g = jax.nn.sigmoid(gate_pre)
        silu_slope = sigmoid_g * (1.0 + gate_pre * (1.0 - sigmoid_g))
        grad_gate_pre = (grad_hidden * up_pre * silu_slope).astype(BF)
        grad_up_pre = (grad_hidden * activated).astype(BF)
        grad_w_gate = contract_rows(received, grad_gate_pre)
        grad_w_up = contract_rows(received, grad_up_pre)
        grad_received = contract_cols(grad_gate_pre, w_gate[0]) + contract_cols(grad_up_pre, w_up[0])

        coarse, fine = two_parts(slot_dot)
        tail = jnp.where(column == my_expert, coarse, jnp.where(column == experts + my_expert, fine, jnp.zeros((), BF)))
        grad_second, back_tail, mixture = combine_rows(
            ctx_count, shard_count, group, grad_received.astype(BF).reshape(block_shape + (width,)),
            tail.reshape(block_shape + (tail_cols,)), mix_back, code, 4,
        )
    grad_gates = back_tail[:, :experts] + back_tail[:, experts : 2 * experts]
    grad_logits_b = (
        gates * (grad_gates - jnp.sum(gates * grad_gates, axis=-1, keepdims=True))
    ).astype(BF)
    router_part = contract_rows(grad_logits_b, second_b).astype(BF)
    grad_second = grad_second + dot(grad_logits_b, router_all)
    unused, norm_two_back = jax.vjp(rms_scale, middle, ffn_gain)
    grad_middle_part, grad_ffn_gain = norm_two_back(grad_second)
    grad_middle = upstream + grad_middle_part
    grad_proj_b = grad_middle.astype(BF)

    router_parts = jnp.swapaxes(router_part.reshape(experts, shard_count, wrows), 0, 1)
    if small:
        gains = jnp.concatenate([jnp.zeros((width,), F32), grad_ffn_gain, jnp.zeros((8 * HEAD_DIM,), F32)])
        gains = gains.reshape(-1, HEAD_DIM)
        q_sum, kv_sum, out_sum, router_sum, gains, grad_input_part, mixture, unused = back(
            ctx_count, shard_count, group, heads,
            (
                grad_proj_b, queries, kv_all, attn_rows, query_pre, kv_pre, w_out, normed_all, w_mine,
                cosine, sine, bias, query_gain[None], key_gain[None], tokens[0], attn_gain[None], gains, router_parts,
                mix_near, mix_part, code,
            ),
            5,
        )
        (
            grad_w_query, grad_w_out, grad_w_gate, grad_w_up, grad_w_down, grad_w_key, grad_w_value, grad_tokens, mixed,
            grad_attn_gain, grad_ffn_gain, grad_query_gain, grad_key_gain, grad_w_router,
        ) = finish_types(
            q_sum, out_sum, grad_w_gate, grad_w_up, grad_w_down, kv_sum, grad_middle, grad_input_part, middle, mixture,
            gains, router_sum,
        )
        grad_attn_gain, grad_ffn_gain = grad_attn_gain.reshape(-1), grad_ffn_gain.reshape(-1)
        grad_query_gain, grad_key_gain = grad_query_gain.reshape(-1), grad_key_gain.reshape(-1)
        grad_w_router = grad_w_router.T
    else:
        normed_all = normed_all.reshape(plane, width)
        w_mine = w_mine.reshape(width, head_cols + HEAD_DIM)
        query_pre = query_pre.reshape(shard_count, rows, heads, HEAD_DIM)
        kv_pre = kv_pre.reshape(plane, HEAD_DIM)
        queries = queries.reshape(shard_count, rows, heads, HEAD_DIM)
        kv_all = kv_all.reshape(2, shard_count, sequence, HEAD_DIM)
        keys, values = kv_all[0], kv_all[1]
        attn_rows = attn_rows.reshape(plane, head_cols)
        grad_proj_all = spread(shard_count, grad_proj_b, 5).reshape(plane, width)
        out_part = contract_rows(attn_rows, grad_proj_all).astype(BF)
        out_part, grad_proj_all = lax.optimization_barrier((out_part, grad_proj_all))
        grad_attn = contract_cols(grad_proj_all, w_out).astype(BF)
        grad_heads = grad_attn.reshape(shard_count, rows, heads, HEAD_DIM)
        scores = (
            jnp.einsum("sthd,spd->shtp", queries, keys, preferred_element_type=F32) * score_scale
        )
        scores = scores + bias
        raised = jnp.exp(scores - jnp.max(scores, axis=-1, keepdims=True))
        probs = raised / jnp.sum(raised, axis=-1, keepdims=True)
        probs_b = probs.astype(BF)
        grad_probs = jnp.einsum("sthd,spd->shtp", grad_heads, values, preferred_element_type=F32)
        delta = jnp.sum(probs * grad_probs, axis=-1, keepdims=True)
        grad_scores = (probs * (grad_probs - delta)).astype(BF)
        grad_query = score_scale * jnp.einsum(
            "shtp,spd->sthd", grad_scores, keys, preferred_element_type=F32
        )
        grad_keys = score_scale * jnp.einsum(
            "shtp,sthd->spd", grad_scores, queries, preferred_element_type=F32
        )
        grad_values = jnp.einsum("shtp,sthd->spd", probs_b, grad_heads, preferred_element_type=F32)
        grad_kv = jnp.stack([grad_keys, grad_values]).astype(BF)
        grad_kv = key_back(
            ctx_count, shard_count, grad_kv.reshape(2, shard_count, ctx_count, rows, HEAD_DIM), 6
        )
        unused, query_back = jax.vjp(prep, query_pre, query_gain)
        grad_query_pre, grad_query_gain = query_back(grad_query)
        kv_shape = (shard_count, rows, 1, HEAD_DIM)
        unused, key_prep_back = jax.vjp(prep, kv_pre.reshape(kv_shape), key_gain)
        grad_key_pre, grad_key_gain = key_prep_back(grad_kv.reshape(kv_shape))
        grad_key_gain = jnp.where(is_key, grad_key_gain, 0.0)
        grad_kv_full = jnp.where(
            is_key, grad_key_pre.reshape(plane, HEAD_DIM), grad_kv.reshape(plane, HEAD_DIM)
        ).astype(BF)
        grad_pre = jnp.concatenate(
            [grad_query_pre.reshape(plane, head_cols).astype(BF), grad_kv_full], axis=1
        )
        gains = jnp.concatenate(
            [
                jnp.zeros((1, width), F32),
                grad_ffn_gain[None],
                jnp.pad(
                    jnp.concatenate([grad_query_gain, grad_key_gain])[None],
                    ((0, 6 - 1), (0, width - 2 * HEAD_DIM)),
                ),
            ]
        )
        grad_w = contract_rows(normed_all, grad_pre).astype(BF).reshape(shard_count, wrows, -1)
        q_sum, kv_sum, out_sum, router_sum, gains, grad_input_part = finish(
            ctx_count, shard_count, head_cols, grad_w, out_part.reshape(8, -1, width), router_parts, gains, grad_pre, w_mine,
            tokens[0], attn_gain[None], 8,
        )
        mixed = (middle + mixture).astype(BF)
        grad_tokens = grad_middle + grad_input_part
        gains = gains.reshape(-1)
        grad_attn_gain, grad_ffn_gain = gains[:width], gains[width : 2 * width]
        grad_query_gain = gains[2 * width : 2 * width + HEAD_DIM]
        grad_key_gain = gains[2 * width + HEAD_DIM : 2 * width + 2 * HEAD_DIM]
        grad_w_query = q_sum.astype(F32)
        grad_w_out = out_sum.reshape(head_cols, width).astype(F32)
        kinds = kv_sum.astype(F32).reshape(KEY_VALUE_HEADS, part_count, 2, wrows, HEAD_DIM)
        kinds = jnp.transpose(jnp.sum(kinds, axis=1), (1, 2, 0, 3)).reshape(2, wrows, -1)
        grad_w_key, grad_w_value = kinds[0], kinds[1]
        grad_w_router = router_sum.T
    return (
        mixed[None],
        grad_tokens[None],
        grad_attn_gain,
        grad_w_query,
        grad_w_key,
        grad_w_value,
        grad_query_gain,
        grad_key_gain,
        grad_w_out,
        grad_ffn_gain,
        grad_w_router,
        grad_w_gate[None],
        grad_w_up[None],
        grad_w_down[None],
    )


def solution(mesh):
    rows = P("shard", "ctx", None)
    matrix = P("shard", None)
    expert = P(("ctx", "shard"), None, None)
    return jax.shard_map(
        shards,
        mesh=mesh,
        in_specs=(
            rows, rows, P(), rows, P(), matrix, matrix, matrix, P(), P(), matrix, P(), matrix,
            expert, expert, expert,
        ),
        out_specs=(
            rows, rows, P(), matrix, matrix, matrix, P(), P(), matrix, P(), matrix,
            expert, expert, expert,
        ),
        check_vma=False,
    )
```

```python
import functools

import jax
import jax.numpy as jnp
from jax import lax
from jax.experimental import pallas as pl
from jax.experimental.pallas import tpu as pltpu
from jax.sharding import PartitionSpec as P

BF = jnp.bfloat16
F32 = jnp.float32
MESH = pl.DeviceIdType.MESH
ANY = pl.BlockSpec(memory_space=pl.ANY)
VMEM = pl.BlockSpec(memory_space=pltpu.VMEM)
DMA = pltpu.SemaphoreType.DMA
epsilon = 1e-06
rope_base = 1000000.0
QUERY_HEADS = 32
KEY_VALUE_HEADS = 4
HEAD_DIM = 128


def push(src, dst, send_sem, recv_sem, **where):
    return pltpu.make_async_remote_copy(
        src_ref=src, dst_ref=dst, send_sem=send_sem, recv_sem=recv_sem,
        device_id=where, device_id_type=MESH,
    )


def greet(shard_peers, ctx_peers):
    barrier = pltpu.get_barrier_semaphore()
    for peer in shard_peers:
        pl.semaphore_signal(barrier, inc=1, device_id={"shard": peer}, device_id_type=MESH)
    for peer in ctx_peers:
        pl.semaphore_signal(barrier, inc=1, device_id={"ctx": peer}, device_id_type=MESH)
    pl.semaphore_wait(barrier, len(shard_peers) + len(ctx_peers))


def here(ctx_count, shard_count):
    c, s = lax.axis_index("ctx"), lax.axis_index("shard")
    parity = lax.rem(s, 2)
    sibling = s + 1 - 2 * parity
    others = [lax.rem(s + d, shard_count) for d in range(1, shard_count)]
    layers = [lax.rem(c + d, ctx_count) for d in range(1, ctx_count)]
    return c, s, parity, sibling, others, layers


def flip_bits(index, mask):
    result = index
    bit = 1
    while bit <= mask:
        if mask & bit:
            result = result + bit - 2 * bit * lax.rem(lax.div(index, bit), 2)
        bit *= 2
    return result


def lowest(d):
    return d & -d


class Fan:
    def __init__(self, n_ctx, c, block, ss, rs, near_first):
        self.n_ctx, self.c, self.block, self.ss, self.rs, self.near_first = n_ctx, c, block, ss, rs, near_first
        self.items = {}

    def send(self, d, src):
        bits = [b for b in (1, 2, 4, 8, 16) if b < (lowest(d) or self.n_ctx)]
        for b in bits if self.near_first else reversed(bits):
            item = push(src, self.block(d), self.ss.at[d | b], self.rs.at[d | b], ctx=flip_bits(self.c, b))
            item.start()
            self.items[d | b] = item

    def arrival(self, d):
        self.items[d].wait_recv()
        if lowest(d) > 1:
            self.send(d, self.block(d))

    def order(self):
        return sorted(range(1, self.n_ctx), key=lambda d: (bin(d).count("1"), d if self.near_first else -d))

    def drain(self):
        for d in range(1, self.n_ctx):
            self.items[d].wait_send()


class Fold:
    def __init__(self, c, sent, received, ss, rs, slots=None, after=None):
        self.c, self.sent, self.received, self.ss, self.rs = c, sent, received, ss, rs
        self.slots, self.after = slots or {}, after or {}
        self.items, self.left = {}, set()

    def take(self, d, value):
        for b in (1, 2, 4, 8, 16):
            if b < lowest(d) or (d == 0 and b in self.items):
                self.items[d | b].wait_recv()
                value = value + self.received[(d | b) - 1].astype(F32)
        return value

    def give(self, d, value):
        slot = self.slots.get(d, d - 1)
        if d in self.after:
            other, which = self.after[d]
            other.items[which].wait_send()
            other.left.add(which)
        self.sent[slot] = value.astype(BF)
        item = push(self.sent.at[slot], self.received.at[d - 1], self.ss.at[d], self.rs.at[d],
                    ctx=flip_bits(self.c, lowest(d)))
        item.start()
        self.items[d] = item

    def give_as_is(self, d, ref):
        self.items[d] = push(ref, self.received.at[d - 1], self.ss.at[d], self.rs.at[d],
                             ctx=flip_bits(self.c, lowest(d)))
        self.items[d].start()

    def drain(self):
        for d, item in self.items.items():
            if d not in self.left:
                item.wait_send()


def call(body, outs, in_specs, scratch, ident, args, mib=48, out_specs=None):
    return pl.pallas_call(
        body,
        out_shape=outs,
        in_specs=in_specs,
        out_specs=out_specs if out_specs is not None else [ANY] * len(outs),
        scratch_shapes=scratch,
        compiler_params=pltpu.CompilerParams(
            collective_id=ident, has_side_effects=True, vmem_limit_bytes=mib * 2**20
        ),
    )(*args)


def by_core(s, n_shard):
    return lax.rem(s, 2) * (n_shard // 2) + lax.div(s, 2)


def from_core(place, n_shard):
    return place % (n_shard // 2) * 2 + place // (n_shard // 2)


def slot_table(code, slots):
    places = lax.broadcasted_iota(jnp.int32, (slots, code.shape[1]), 0).astype(F32)
    return jnp.concatenate(
        [(places == code[e : e + 1, :]).astype(BF) for e in range(code.shape[0])], axis=0
    )


def turn(value, cosine, sine):
    return value * cosine + pltpu.roll(value, HEAD_DIM // 2, 1) * sine


def unit_rows(value):
    scale = lax.rsqrt(jnp.mean(value * value, axis=-1, keepdims=True) + epsilon)
    return value * scale, scale


def front_body(n_ctx, n_shard, group, capacity, heads, kv_heads, paired, tile,
               tokens, gain, w_query, key_w, value_w, routes, router, cot, cosine, sine, bias, q_gain, k_gain, w_out, second_gain,
               rows_out, w_all_out, router_all, code, cot_rows, qpre_out, kvpre, q_out, kv_out, attn_out, mid, second,
               own_rows, rows_all, w_all, zroutes, zcot, ready, qpre, q, kv, attn,
               own_part, pair, to_sib, sib, to_chip, got,
               local, ss_row, rs_row, ss_fwd, rs_fwd, ss_w, rs_w, ss_k, rs_k, ss_rt, rs_rt, ss_ro, rs_ro, ss_z, rs_z,
               ss_x, rs_x, ss_kz, rs_kz, ss_kf, rs_kf, ss_s, rs_s, ss_c, rs_c, out_sem):
    c, s, parity, sibling, others, layers = here(n_ctx, n_shard)
    chips = n_shard // 2
    chip = lax.div(s, 2)
    count, width = tokens.shape
    wr = w_query.shape[0]
    cols = heads * HEAD_DIM
    sharers = n_shard // kv_heads
    groups = n_ctx // group
    slots = group * capacity
    keys = n_ctx * count
    mates = [lax.rem(s + 2 * d, n_shard) for d in range(1, chips)]
    x = tokens[...].astype(F32)
    unit, unused = unit_rows(x)
    own_rows[...] = (unit * gain[...]).astype(BF)
    greet(others, layers)

    route_fan = Fan(n_ctx, c, lambda d: zroutes.at[flip_bits(c, d)], ss_ro, rs_ro, False)
    route_fan.send(0, routes)
    cot_fan = Fan(n_ctx, c, lambda d: zcot.at[flip_bits(c, d)], ss_z, rs_z, False)
    cot_fan.send(0, cot)
    first, waits = [], []
    for d in range(1, chips):
        item = push(own_rows, rows_all.at[s], ss_row.at[d], rs_row.at[d], shard=mates[d - 1])
        item.start()
        first.append(item)
    item = push(own_rows, rows_all.at[s], ss_fwd.at[0], rs_fwd.at[0], shard=sibling)
    item.start()
    waits.append(item)
    w_waits = []
    for i, peer in enumerate(others):
        from_q = w_query.at[:, pl.ds(pl.multiple_of(peer * cols, cols), cols)]
        item = push(from_q, w_all.at[s, :, pl.ds(0, cols)], ss_w.at[i], rs_w.at[i], shard=peer)
        item.start()
        w_waits.append(item)
        head = pl.ds(pl.multiple_of(lax.div(peer, sharers) * HEAD_DIM, HEAD_DIM), HEAD_DIM)
        for kind, ref in enumerate((key_w, value_w)):
            item = push(ref.at[:, head], w_all.at[s, :, pl.ds(cols, HEAD_DIM)], ss_k.at[i], rs_k.at[i], shard=peer)

            @pl.when(lax.rem(peer, 2) == kind)
            def _(item=item):
                item.start()

        w_waits.append(item)
        item = push(router, router_all.at[:, pl.ds(pl.multiple_of(s * wr, wr), wr)], ss_rt.at[i], rs_rt.at[i], shard=peer)
        item.start()
        waits.append(item)
    copies = [
        pltpu.make_async_copy(own_rows, rows_all.at[s], local.at[0]),
        pltpu.make_async_copy(w_query.at[:, pl.ds(pl.multiple_of(s * cols, cols), cols)],
                              w_all.at[s, :, pl.ds(0, cols)], local.at[1]),
        pltpu.make_async_copy(routes, zroutes.at[c], local.at[2]),
        pltpu.make_async_copy(router, router_all.at[:, pl.ds(pl.multiple_of(s * wr, wr), wr)], local.at[3]),
        pltpu.make_async_copy(cot, zcot.at[c], local.at[4]),
    ]
    for item in copies:
        item.start()
    head = pl.ds(pl.multiple_of(lax.div(s, sharers) * HEAD_DIM, HEAD_DIM), HEAD_DIM)
    for kind, ref in enumerate((key_w, value_w)):
        own_head = pltpu.make_async_copy(ref.at[:, head], w_all.at[s, :, pl.ds(cols, HEAD_DIM)], local.at[5])

        @pl.when(parity == kind)
        def _(own_head=own_head):
            own_head.start()

    copies[2].wait()
    for d in route_fan.order():
        route_fan.arrival(d)
    before = (
        lax.broadcasted_iota(jnp.int32, (count, count), 0) < lax.broadcasted_iota(jnp.int32, (count, count), 1)
    ).astype(BF)
    for layer in range(n_ctx):
        named = zroutes[layer]
        mask = jnp.concatenate(
            [jnp.max((named == c * n_shard + e).astype(F32), axis=0, keepdims=True) for e in range(n_shard)], axis=0
        )
        rank = jnp.dot(mask.astype(BF), before, preferred_element_type=F32)
        at = layer % group
        code[layer // group, :, at * count : (at + 1) * count] = jnp.where(
            mask > 0, rank + float(at * capacity), -1.0
        )

    for d in range(1, chips):
        first[d - 1].wait()
        origin = lax.rem(s + n_shard - 2 * d, n_shard)
        item = push(rows_all.at[origin], rows_all.at[origin], ss_fwd.at[d], rs_fwd.at[d], shard=sibling)
        item.start()
        waits.append(item)
    for d in cot_fan.order():
        cot_fan.arrival(d)
    copies[4].wait()
    for k in range(groups):
        table = slot_table(code[k], slots)

        @pl.loop(0, width // tile)
        def _(j):
            part = pl.ds(pl.multiple_of(j * tile, tile), tile)
            block = zcot[k * group : (k + 1) * group, :, part].reshape(group * count, tile)
            value = jnp.dot(table, block, preferred_element_type=F32).astype(BF)
            ready[k, :, :, part] = value.reshape(n_shard, slots, tile)

    place = by_core(s, n_shard) if paired else s
    cot_waits = []
    for k in range(groups):
        for i, peer in enumerate(others):
            item = push(ready.at[k, peer], cot_rows.at[k, place], ss_x.at[k, i], rs_x.at[k, i], shard=peer)
            item.start()
            cot_waits.append(item)
        item = pltpu.make_async_copy(ready.at[k, s], cot_rows.at[k, place], local.at[6 + k])
        item.start()
        cot_waits.append(item)

    for item in waits + w_waits:
        item.wait()
    copies[0].wait()
    copies[1].wait()
    copies[3].wait()
    own_head.wait()
    outs = [
        pltpu.make_async_copy(rows_all, rows_out, out_sem.at[0]),
        pltpu.make_async_copy(w_all, w_all_out, out_sem.at[1]),
    ]
    outs[0].start()
    outs[1].start()

    right = w_all[:, :, pl.ds(cols, HEAD_DIM)].reshape(width, HEAD_DIM)

    @pl.loop(0, n_shard)
    def _(b):
        pre = jnp.dot(rows_all[b], right, preferred_element_type=F32)
        kvpre[b] = pre
        keyed, unused = unit_rows(pre)
        keyed = turn(keyed * k_gain[...], cosine[...], sine[...])
        kv[parity, b, c] = jnp.where(parity == 0, keyed, pre).astype(BF)

    fan = Fan(n_ctx, c, lambda d: kv.at[parity, :, flip_bits(c, d)], ss_kz, rs_kz, False)
    fan.send(0, kv.at[parity, :, c])
    kv_waits = []
    item = push(kv.at[parity, :, c], kv.at[parity, :, c], ss_kf.at[0], rs_kf.at[0], shard=sibling)
    item.start()
    kv_waits.append(item)

    @pl.loop(0, n_shard // 2)
    def _(b):
        left = rows_all[pl.ds(b * 2, 2)].reshape(2 * count, width)
        pre = jnp.dot(left, w_all[:, :, pl.ds(0, cols)].reshape(width, cols), preferred_element_type=F32)
        qpre[pl.ds(b * 2, 2)] = pre.reshape(2, count, cols)
        for i in range(2):
            for h in range(heads):
                part = pre[i * count : (i + 1) * count, h * HEAD_DIM : (h + 1) * HEAD_DIM]
                unit, unused = unit_rows(part)
                q[b * 2 + i, :, h * HEAD_DIM : (h + 1) * HEAD_DIM] = turn(
                    unit * q_gain[...], cosine[...], sine[...]
                ).astype(BF)

    for d in fan.order():
        fan.arrival(d)
        block = kv.at[parity, :, flip_bits(c, d)]
        item = push(block, block, ss_kf.at[d], rs_kf.at[d], shard=sibling)
        item.start()
        kv_waits.append(item)
    outs += [pltpu.make_async_copy(qpre, qpre_out, out_sem.at[2]), pltpu.make_async_copy(q, q_out, out_sem.at[3])]
    outs[2].start()
    outs[3].start()
    for item in kv_waits:
        item.wait()
    fan.drain()
    outs.append(pltpu.make_async_copy(kv, kv_out, out_sem.at[4]))
    outs[4].start()

    near, far = {}, {}
    order = list(range(1, chips)) + [0]

    def product(at):
        d = order[at]
        first_seq = 2 * lax.rem(chip + d, chips)

        @pl.loop(0, 2)
        def _(i):
            b = first_seq + i
            k_all = kv[0, b].reshape(keys, HEAD_DIM)
            v_all = kv[1, b].reshape(keys, HEAD_DIM)
            for h in range(heads):
                hs = slice(h * HEAD_DIM, (h + 1) * HEAD_DIM)
                scores = lax.dot_general(q[b, :, hs], k_all, (((1,), (1,)), ((), ())), preferred_element_type=F32)
                scores = scores * (HEAD_DIM ** -0.5) + bias[...]
                raised = jnp.exp(scores - jnp.max(scores, axis=-1, keepdims=True))
                probs = raised / jnp.sum(raised, axis=-1, keepdims=True)
                attn[b, :, hs] = jnp.dot(probs.astype(BF), v_all, preferred_element_type=F32).astype(BF)

        left = attn[pl.ds(first_seq, 2)].reshape(2 * count, cols)

        @pl.loop(0, width // tile)
        def _(j):
            part = pl.ds(pl.multiple_of(j * tile, tile), tile)
            value = jnp.dot(left, w_out[:, part], preferred_element_type=F32)
            pair[...] = value.reshape(2, count, tile)
            own_part[at % 2, :, part] = pair[parity]
            to_sib[at, :, part] = pair[1 - parity].astype(BF)

        near[at] = push(to_sib.at[at], sib.at[at], ss_s.at[at], rs_s.at[at], shard=sibling)
        near[at].start()

    def chip_sum(at):
        near[at].wait()
        to_chip[at] = (own_part[at % 2] + sib[at].astype(F32)).astype(BF)
        far[at] = push(to_chip.at[at], got.at[at], ss_c.at[at], rs_c.at[at], shard=mates[order[at] - 1])
        far[at].start()

    for at in range(chips):
        product(at)
        if at:
            chip_sum(at - 1)
    outs.append(pltpu.make_async_copy(attn, attn_out, out_sem.at[5]))
    outs[5].start()
    near[chips - 1].wait()
    mid[...] = tokens[...].astype(F32) + own_part[(chips - 1) % 2] + sib[chips - 1].astype(F32)
    for at in range(chips - 1):
        far[at].wait()
        mid[...] += got[at].astype(F32)
    unit, unused = unit_rows(mid[...])
    second[...] = (unit * second_gain[...]).astype(BF)
    cot_fan.drain()
    route_fan.drain()
    for item in cot_waits + outs:
        item.wait()


def front(n_ctx, n_shard, group, capacity, kv_heads, paired, args, ident):
    tokens, gain, w_query, key_w, value_w, routes, router, cot = args[:8]
    n, z = n_shard, n_ctx
    count, width = tokens.shape
    wr, chips, groups, slots = w_query.shape[0], n_shard // 2, n_ctx // group, group * capacity
    cols = w_query.shape[1] // n
    heads = cols // HEAD_DIM
    sds = jax.ShapeDtypeStruct
    dma = lambda *shape: DMA(shape)
    return call(
        functools.partial(front_body, z, n, group, capacity, heads, kv_heads, paired, 512),
        [
            sds((n, count, width), BF), sds((n, wr, cols + HEAD_DIM), BF), sds((router.shape[0], width), BF),
            sds((groups, n, group * count), F32), sds((groups, n, slots, width), BF), sds((n, count, cols), F32),
            sds((n, count, HEAD_DIM), F32), sds((n, count, cols), BF), sds((2, n, z, count, HEAD_DIM), BF),
            sds((n, count, cols), BF), sds((count, width), F32), sds((count, width), BF),
        ],
        [VMEM, VMEM, ANY, ANY, ANY, VMEM, ANY, ANY] + [VMEM] * 7,
        [
            pltpu.VMEM((count, width), BF), pltpu.VMEM((n, count, width), BF), pltpu.VMEM((n, wr, cols + HEAD_DIM), BF),
            pltpu.VMEM((z,) + routes.shape, jnp.int32), pltpu.VMEM((z, count, width), BF),
            pltpu.VMEM((groups, n, slots, width), BF), pltpu.VMEM((n, count, cols), F32),
            pltpu.VMEM((n, count, cols), BF), pltpu.VMEM((2, n, z, count, HEAD_DIM), BF),
            pltpu.VMEM((n, count, cols), BF), pltpu.VMEM((2, count, width), F32), pltpu.VMEM((2, count, 512), F32),
            pltpu.VMEM((chips, count, width), BF), pltpu.VMEM((chips, count, width), BF),
            pltpu.VMEM((chips - 1, count, width), BF), pltpu.VMEM((chips - 1, count, width), BF),
            dma(6 + groups), dma(chips), dma(chips), dma(chips), dma(chips), dma(n - 1), dma(n - 1), dma(n - 1), dma(n - 1),
            dma(n - 1), dma(n - 1), dma(z), dma(z), dma(z), dma(z), dma(groups, n - 1), dma(groups, n - 1),
            dma(z), dma(z), dma(z), dma(z), dma(chips), dma(chips), dma(chips - 1), dma(chips - 1), dma(6),
        ],
        ident, args, mib=60,
        out_specs=[ANY, ANY, ANY, VMEM, ANY, ANY, VMEM, ANY, ANY, ANY, VMEM, VMEM],
    )


def spread_body(n_shard, rows, rows_all, local, ss_row, rs_row, ss_fwd, rs_fwd):
    c, s, parity, sibling, others, layers = here(1, n_shard)
    chips = n_shard // 2
    mates = [lax.rem(s + 2 * d, n_shard) for d in range(1, chips)]
    greet(mates + [sibling], [])
    mine = pltpu.make_async_copy(rows, rows_all.at[s], local)
    mine.start()
    first, waits = [], []
    for d in range(1, chips):
        item = push(rows, rows_all.at[s], ss_row.at[d], rs_row.at[d], shard=mates[d - 1])
        item.start()
        first.append(item)
    item = push(rows, rows_all.at[s], ss_fwd.at[0], rs_fwd.at[0], shard=sibling)
    item.start()
    waits.append(item)
    for d in range(1, chips):
        first[d - 1].wait()
        origin = lax.rem(s + n_shard - 2 * d, n_shard)
        item = push(rows_all.at[origin], rows_all.at[origin], ss_fwd.at[d], rs_fwd.at[d], shard=sibling)
        item.start()
        waits.append(item)
    mine.wait()
    for item in waits:
        item.wait()


def spread(n_shard, rows, ident):
    return call(
        functools.partial(spread_body, n_shard),
        [jax.ShapeDtypeStruct((n_shard,) + rows.shape, rows.dtype)],
        [ANY], [DMA] + [DMA((n_shard // 2,))] * 4, ident, (rows,),
    )[0]


def key_back_body(n_ctx, n_shard, parts, out, sib, zsend, zrecv, ss_s, rs_s, ss_z, rs_z):
    c, s, parity, sibling, others, layers = here(n_ctx, n_shard)
    greet([sibling], layers)
    order = list(range(1, n_ctx)) + [0]
    near = {}
    for d in order:
        block = parts.at[1 - parity, :, lax.rem(c + d, n_ctx)]
        near[d] = push(block, sib.at[d], ss_s.at[d], rs_s.at[d], shard=sibling)
        near[d].start()
    far = {}
    for d in order:
        near[d].wait()
        layer = lax.rem(c + d, n_ctx)
        value = parts[parity, :, layer].astype(F32) + sib[d].astype(F32)
        if d:
            zsend[d - 1] = value.astype(BF)
            far[d] = push(zsend.at[d - 1], zrecv.at[d - 1], ss_z.at[d], rs_z.at[d], ctx=layer)
            far[d].start()
    for d in range(1, n_ctx):
        far[d].wait()
        value = value + zrecv[d - 1].astype(F32)
    out[...] = value


def key_back(n_ctx, n_shard, parts, ident):
    block = (parts.shape[1], parts.shape[3], parts.shape[4])
    return call(
        functools.partial(key_back_body, n_ctx, n_shard),
        [jax.ShapeDtypeStruct(block, F32)],
        [VMEM],
        [
            pltpu.VMEM((n_ctx,) + block, BF), pltpu.VMEM((n_ctx - 1,) + block, BF),
            pltpu.VMEM((n_ctx - 1,) + block, BF),
        ] + [DMA((n_ctx,))] * 4,
        ident, (parts,), out_specs=[VMEM],
    )[0]


def finish_body(n_ctx, n_shard, q_cols, tile,
                weights, wide, router, gains, left, right, tokens, gain,
                q_out, kv_out, wide_out, router_out, gains_out, rows_out,
                wide_landing, wide_acc, wide_total, ss_wi, rs_wi, ss_wo, ss_wc, pieces, landing, acc, total, router_in, router_mid, router_far,
                gains_own, gains_in, gains_mid, gains_far, pair, own_part, to_sib, sib, to_chip, got,
                local, ss_w, rs_w, ss_i, rs_i, ss_o, ss_q, ss_k, ss_r, rs_r, ss_g, rs_g, ss_h, rs_h,
                ss_t, rs_t, ss_s, rs_s, ss_c, rs_c):
    c, s, parity, sibling, others, layers = here(n_ctx, n_shard)
    half = n_ctx // 2
    chips = n_shard // 2
    chip = lax.div(s, 2)
    mates = [lax.rem(s + 2 * d, n_shard) for d in range(1, chips)]
    left_side = c < half
    depth = jnp.where(left_side, c, n_ctx - 1 - c)
    inner = jnp.where(left_side, c + 1, c - 1)
    outer = jnp.clip(jnp.where(left_side, c - 1, c + 1), 0, n_ctx - 1)
    middle = depth == half - 1
    inside = depth > 0
    rows, width = rows_out.shape
    greet(others, layers)
    sends, small = [None], []
    for i, peer in enumerate(others):
        item = push(weights.at[peer], pieces.at[i + 1], ss_w.at[i], rs_w.at[i], shard=peer)
        item.start()
        sends.append(item)
    for i, peer in enumerate(others):
        item = push(router.at[peer], router_in.at[i], ss_r.at[i], rs_r.at[i], shard=peer)
        item.start()
        small.append(item)

    def out_copies(j, ref):
        source = lax.rem(s + n_shard - j, n_shard)
        cols = pl.ds(pl.multiple_of(source * q_cols, q_cols), q_cols)
        return (
            pltpu.make_async_copy(ref.at[:, pl.ds(0, q_cols)], q_out.at[:, cols], ss_q.at[j]),
            pltpu.make_async_copy(ref.at[:, pl.ds(q_cols, 128)], kv_out.at[source], ss_k.at[j]),
        )

    def wide_copies(j, ref):
        return (pltpu.make_async_copy(ref, wide_out.at[j], ss_wc.at[j]),)

    class Line:
        def __init__(self, ready, own, acc, landing, total, ss_i, rs_i, ss_o, copies):
            self.ready, self.own, self.acc, self.landing, self.total = ready, own, acc, landing, total
            self.ss_i, self.rs_i, self.ss_o, self.copies = ss_i, rs_i, ss_o, copies

        def inward(self, j, ref):
            at = jnp.where(middle, 1, 0)
            return push(ref, self.landing.at[at, j], self.ss_i.at[j], self.rs_i.at[at, j], ctx=inner)

        def outward(self, j):
            return push(self.total.at[j], self.landing.at[1, j], self.ss_o.at[j], self.rs_i.at[1, j], ctx=outer)

        def arrived(self, which, j):
            push(self.acc.at[j], self.landing.at[which, j], self.ss_i.at[j], self.rs_i.at[which, j],
                 ctx=inner).wait_recv()

        def outermost(self, j):
            @pl.when(jnp.logical_not(inside))
            def _():
                self.ready(j)
                self.inward(j, self.own(j)).start()

        def first_half(self, j):
            @pl.when(inside)
            def _():
                self.ready(j)
                self.arrived(0, j)
                self.acc[j] = (self.own(j)[...].astype(F32) + self.landing[0, j].astype(F32)).astype(BF)
                self.inward(j, self.acc.at[j]).start()

        def second_half(self, j):
            self.arrived(1, j)

            @pl.when(middle)
            def _():
                self.total[j] = (self.acc[j].astype(F32) + self.landing[1, j].astype(F32)).astype(BF)

            @pl.when(jnp.logical_not(middle))
            def _():
                self.total[j] = self.landing[1, j]

            @pl.when(inside)
            def _():
                self.outward(j).start()

            for item in self.copies(j, self.total.at[j]):
                item.start()

        def drain(self, j):
            self.inward(j, self.acc.at[j]).wait_send()

            @pl.when(inside)
            def _():
                self.outward(j).wait_send()

            for item in self.copies(j, self.total.at[j]):
                item.wait()

    line = Line(lambda j: sends[j].wait() if j else None, lambda j: pieces.at[j] if j else weights.at[s],
                acc, landing, total, ss_i, rs_i, ss_o, out_copies)
    wide_line = Line(lambda j: None, lambda j: wide.at[j], wide_acc, wide_landing, wide_total,
                     ss_wi, rs_wi, ss_wo, wide_copies)
    wides = wide.shape[0]
    steps = [(wide_line, j) for j in range(wides)] + [(line, j) for j in range(n_shard)]

    near, far = {}, {}

    def product(d):
        first = pl.multiple_of(lax.rem(chip + d, chips) * (2 * rows), 2 * rows)

        @pl.loop(0, width // tile)
        def _(j):
            cols = pl.ds(pl.multiple_of(j * tile, tile), tile)
            value = lax.dot_general(left[pl.ds(first, 2 * rows), :], right[cols, :],
                                    (((1,), (1,)), ((), ())), preferred_element_type=F32)
            pair[...] = value.reshape(2, rows, tile)
            own_part[d, :, cols] = pair[parity]
            to_sib[d, :, cols] = pair[1 - parity].astype(BF)

        near[d] = push(to_sib.at[d], sib.at[d], ss_s.at[d], rs_s.at[d], shard=sibling)
        near[d].start()

    def chip_sum(d):
        near[d].wait()
        to_chip[d - 1] = (own_part[d] + sib[d].astype(F32)).astype(BF)
        far[d] = push(to_chip.at[d - 1], got.at[d - 1], ss_c.at[d - 1], rs_c.at[d - 1], shard=mates[d - 1])
        far[d].start()

    gain_sends = []

    def last_sum():
        near[0].wait()
        grad = own_part[0] + sib[0].astype(F32)
        for d in range(1, chips):
            far[d].wait()
            grad = grad + got[d - 1].astype(F32)
        x = tokens[...].astype(F32)
        scale = lax.rsqrt(jnp.mean(x * x, axis=-1, keepdims=True) + epsilon)
        unit = x * scale
        scaled = grad * gain[...]
        rows_out[...] = scale * (scaled - unit * jnp.mean(scaled * unit, axis=-1, keepdims=True))
        gains_own[...] = gains[...]
        gains_own[0:1] = jnp.sum(grad * unit, axis=0, keepdims=True)
        mine = pltpu.make_async_copy(gains_own, gains_in.at[s], local.at[0])
        mine.start()
        gain_sends.append(mine)
        for i, peer in enumerate(others):
            item = push(gains_own, gains_in.at[s], ss_g.at[i], rs_g.at[i], shard=peer)
            item.start()
            gain_sends.append(item)

    def small_plane():
        for item in small + gain_sends:
            item.wait()
        gains_mid[...] = gains_in[0]
        for i in range(1, n_shard):
            gains_mid[...] += gains_in[i]
        router_mid[...] = router[s].astype(F32)
        for i in range(n_shard - 1):
            router_mid[...] += router_in[i].astype(F32)
        for i, layer in enumerate(layers):
            push(gains_mid, gains_far.at[c], ss_h.at[i], rs_h.at[i], ctx=layer).start()
            push(router_mid, router_far.at[c], ss_t.at[i], rs_t.at[i], ctx=layer).start()
        pltpu.make_async_copy(gains_mid, gains_far.at[c], local.at[1]).start()
        pltpu.make_async_copy(router_mid, router_far.at[c], local.at[2]).start()

    def small_all():
        pltpu.make_async_copy(gains_mid, gains_far.at[c], local.at[1]).wait()
        pltpu.make_async_copy(router_mid, router_far.at[c], local.at[2]).wait()
        for i, layer in enumerate(layers):
            push(gains_mid, gains_far.at[c], ss_h.at[i], rs_h.at[i], ctx=layer).wait()
            push(router_mid, router_far.at[c], ss_t.at[i], rs_t.at[i], ctx=layer).wait()
        gains_out[...] = gains_far[0]
        router_out[...] = router_far[0]
        for i in range(1, n_ctx):
            gains_out[...] += gains_far[i]
            router_out[...] += router_far[i]

    lag, ahead = 2, 6
    for which, j in steps[:ahead]:
        which.outermost(j)
    for d in list(range(1, chips)) + [0]:
        product(d)
    side = [functools.partial(chip_sum, d) for d in range(1, chips)] + [last_sum, small_plane]
    for n in range(len(steps) + lag):
        if n + ahead < len(steps):
            steps[n + ahead][0].outermost(steps[n + ahead][1])
        if n < len(steps):
            steps[n][0].first_half(steps[n][1])
        if n >= lag:
            steps[n - lag][0].second_half(steps[n - lag][1])
        if n >= 2 and side:
            side.pop(0)()
    for job in side:
        job()
    small_all()
    for which, j in steps:
        which.drain(j)


def finish(n_ctx, n_shard, q_cols, weights, wide, router, gains, left, right, tokens, gain, ident):
    n, rows, cols = weights.shape
    router_shape = router.shape[1:]
    count, width = tokens.shape
    chips = n // 2
    tile = 512
    wides = wide.shape[0]
    return call(
        functools.partial(finish_body, n_ctx, n, q_cols, tile),
        [
            jax.ShapeDtypeStruct((rows, n * q_cols), BF), jax.ShapeDtypeStruct((n, rows, 128), BF),
            jax.ShapeDtypeStruct(wide.shape, BF),
            jax.ShapeDtypeStruct(router_shape, F32), jax.ShapeDtypeStruct(gains.shape, F32),
            jax.ShapeDtypeStruct((count, width), F32),
        ],
        [VMEM] * 8,
        [
            pltpu.VMEM((2,) + wide.shape, BF), pltpu.VMEM(wide.shape, BF), pltpu.VMEM(wide.shape, BF),
            DMA((wides,)), DMA((2, wides)), DMA((wides,)), DMA((wides,)),
            pltpu.VMEM((n, rows, cols), BF), pltpu.VMEM((2, n, rows, cols), BF),
            pltpu.VMEM((n, rows, cols), BF), pltpu.VMEM((n, rows, cols), BF),
            pltpu.VMEM((n - 1,) + router_shape, BF), pltpu.VMEM(router_shape, F32),
            pltpu.VMEM((n_ctx,) + router_shape, F32),
            pltpu.VMEM(gains.shape, F32), pltpu.VMEM((n,) + gains.shape, F32),
            pltpu.VMEM(gains.shape, F32), pltpu.VMEM((n_ctx,) + gains.shape, F32),
            pltpu.VMEM((2, count, tile), F32), pltpu.VMEM((chips, count, width), F32),
            pltpu.VMEM((chips, count, width), BF), pltpu.VMEM((chips, count, width), BF),
            pltpu.VMEM((chips - 1, count, width), BF), pltpu.VMEM((chips - 1, count, width), BF),
            DMA((3,)), DMA((n - 1,)), DMA((n - 1,)), DMA((n,)), DMA((2, n)), DMA((n,)),
            DMA((n,)), DMA((n,)), DMA((n - 1,)), DMA((n - 1,)), DMA((n - 1,)), DMA((n - 1,)),
            DMA((n_ctx - 1,)), DMA((n_ctx - 1,)), DMA((n_ctx - 1,)), DMA((n_ctx - 1,)),
            DMA((chips,)), DMA((chips,)), DMA((chips - 1,)), DMA((chips - 1,)),
        ],
        ident, (weights, wide, router, gains, left, right, tokens, gain), mib=60,
        out_specs=[ANY, ANY, ANY, VMEM, VMEM, VMEM],
    )


def back_body(n_ctx, n_shard, group, heads, wides,
              grad_out, q_in, kv_in, attn_in, qpre_in, kvpre_in, w_out_in, rows_in, w_all_in, cosine, sine, bias, q_gain, k_gain,
              tokens, gain, gains, router, mix_near, mix_part, code,
              q_out, kv_out, wide_out, router_out, gains_out, rows_out, mix_out, mix_land,
              q, kv, attn, qpre, kvpre, w_out, w_all, loads, grads, attn_t, grad_heads, ds_all, p_all, parts, pre, q_sum, k_sum, wide, weights,
              sibk, zsend, zrecv, wide_landing, pieces, landing,
              own_part, pair, to_sib, sib, to_chip, got, router_in, router_mid, router_far,
              gains_own, gains_in, gains_mid, gains_far, mix_rows, mix_sent, mix_recv, local,
              ss_row, rs_row, ss_fwd, rs_fwd, ss_sk, rs_sk, ss_zk, rs_zk,
              ss_wi, rs_wi, ss_wo, ss_wc, ss_w, rs_w, ss_i, rs_i, ss_o, ss_q, ss_k,
              ss_r, rs_r, ss_g, rs_g, ss_h, rs_h, ss_t, rs_t, ss_s, rs_s, ss_c, rs_c, ss_m, rs_m, ss_f, rs_f, ss_v, rs_v):
    c, s, parity, sibling, others, layers = here(n_ctx, n_shard)
    half = n_ctx // 2
    chips = n_shard // 2
    chip = lax.div(s, 2)
    mates = [lax.rem(s + 2 * d, n_shard) for d in range(1, chips)]
    left_side = c < half
    depth = jnp.where(left_side, c, n_ctx - 1 - c)
    inner = jnp.where(left_side, c + 1, c - 1)
    outer = jnp.clip(jnp.where(left_side, c - 1, c + 1), 0, n_ctx - 1)
    middle = depth == half - 1
    inside = depth > 0
    count, width = tokens.shape
    wr = w_all.shape[1]
    cols = heads * HEAD_DIM
    keys = n_ctx * count
    scaling = HEAD_DIM ** -0.5
    own_copies = [
        pltpu.make_async_copy(grad_out, grads.at[s], local.at[0]),
        pltpu.make_async_copy(rows_in, grads, local.at[1]),
    ]
    own_copies[0].start()
    load = [
        pltpu.make_async_copy(a, b, loads.at[n])
        for n, (a, b) in enumerate(((q_in, q), (kv_in, kv), (w_out_in, w_out), (qpre_in, qpre), (attn_in, attn),
                                    (kvpre_in, kvpre), (w_all_in, w_all)))
    ]
    greet(others, layers)

    first, forwards = {}, {}
    for d in range(1, chips):
        first[d] = push(grad_out, grads.at[s], ss_row.at[d], rs_row.at[d], shard=mates[d - 1])
        first[d].start()
    forwards[0] = push(grad_out, grads.at[s], ss_fwd.at[0], rs_fwd.at[0], shard=sibling)
    forwards[0].start()
    for item in load:
        item.start()
    small = []
    for i, peer in enumerate(others):
        item = push(router.at[peer], router_in.at[i], ss_r.at[i], rs_r.at[i], shard=peer)
        item.start()
        small.append(item)
    q_sum[...] = jnp.zeros_like(q_sum)
    k_sum[...] = jnp.zeros_like(k_sum)

    def norm_back(grad, value, norm_gain, total):
        unit, scale = unit_rows(value)
        grad = grad * cosine[...] + pltpu.roll(grad * sine[...], HEAD_DIM // 2, 1)
        total[...] += jnp.sum(grad * unit, axis=0, keepdims=True)
        scaled = grad * norm_gain[...]
        return scale * (scaled - unit * jnp.mean(scaled * unit, axis=-1, keepdims=True))

    slots = mix_near.shape[1]
    mix_fold = Fold(c, mix_sent, mix_recv, ss_f, rs_f)
    tile = mix_rows.shape[2]

    def mix_sums(k, ref):
        table = slot_table(code[flip_bits(lax.div(c, group), k)], slots).T

        @pl.loop(0, width // tile)
        def _(j):
            part = pl.ds(pl.multiple_of(j * tile, tile), tile)
            item = pltpu.make_async_copy(ref.at[:, :, part], mix_rows, local.at[5])
            item.start()
            item.wait()
            value = jnp.dot(table, mix_rows[...].reshape(n_shard * slots, tile), preferred_element_type=F32)
            own_part[:, :, part] = value.reshape(2, count, tile)

    def near_part(d):
        return own_part[lax.rem(flip_bits(c, d), group)]

    def mix_send():
        for i, peer in enumerate(others):
            push(mix_near.at[by_core(peer, n_shard)], mix_land.at[s], ss_m.at[i], rs_m.at[i], shard=peer).start()
        pltpu.make_async_copy(mix_near.at[by_core(s, n_shard)], mix_land.at[s], local.at[6]).start()

    def mix_last():
        for i, peer in enumerate(others):
            push(mix_near.at[by_core(peer, n_shard)], mix_land.at[s], ss_m.at[i], rs_m.at[i], shard=peer).wait()
        pltpu.make_async_copy(mix_near.at[by_core(s, n_shard)], mix_land.at[s], local.at[6]).wait()
        mix_sums(0, mix_land)
        mix_fold.give(1, near_part(1))
        mix_out[...] = near_part(0)

    mix_fold.give_as_is(3, mix_part.at[1])
    near, far = {}, {}

    def seqs_of(d):
        return 2 * lax.rem(chip + chips - d, chips)

    def attention_back(d):
        fs = seqs_of(d)
        grad = lax.dot_general(grads[pl.ds(fs, 2)].reshape(2 * count, width), w_out[...],
                               (((1,), (1,)), ((), ())), preferred_element_type=F32)
        grad_heads[...] = grad.reshape(2, count, cols).astype(BF)

        @pl.loop(0, 2)
        def _(i):
            b = fs + i
            k_all = kv[0, b].reshape(keys, HEAD_DIM)
            v_all = kv[1, b].reshape(keys, HEAD_DIM)
            for h in range(heads):
                hs = slice(h * HEAD_DIM, (h + 1) * HEAD_DIM)
                rs = slice(h * count, (h + 1) * count)
                scores = lax.dot_general(q[b, :, hs], k_all, (((1,), (1,)), ((), ())), preferred_element_type=F32)
                scores = scores * scaling + bias[...]
                raised = jnp.exp(scores - jnp.max(scores, axis=-1, keepdims=True))
                probs = raised / jnp.sum(raised, axis=-1, keepdims=True)
                grad_p = lax.dot_general(grad_heads[i, :, hs], v_all, (((1,), (1,)), ((), ())),
                                         preferred_element_type=F32)
                delta = jnp.sum(probs * grad_p, axis=-1, keepdims=True)
                ds = (probs * (grad_p - delta)).astype(BF)
                ds_all[rs, :] = ds
                p_all[rs, :] = probs.astype(BF)
                grad_q = jnp.dot(ds, k_all, preferred_element_type=F32) * scaling
                pre[b, :, hs] = norm_back(grad_q, qpre[b, :, hs], q_gain, q_sum).astype(BF)
            grad_k, grad_v = jnp.zeros((keys, HEAD_DIM), F32), jnp.zeros((keys, HEAD_DIM), F32)
            stacked_q = jnp.concatenate([q[b, :, h * HEAD_DIM : (h + 1) * HEAD_DIM] for h in range(heads)], axis=0)
            stacked_g = jnp.concatenate(
                [grad_heads[i, :, h * HEAD_DIM : (h + 1) * HEAD_DIM] for h in range(heads)], axis=0
            )
            grad_k = lax.dot_general(ds_all[...], stacked_q, (((0,), (0,)), ((), ())), preferred_element_type=F32)
            grad_v = lax.dot_general(p_all[...], stacked_g, (((0,), (0,)), ((), ())), preferred_element_type=F32)
            parts[0, b] = (grad_k * scaling).astype(BF).reshape(n_ctx, count, HEAD_DIM)
            parts[1, b] = grad_v.astype(BF).reshape(n_ctx, count, HEAD_DIM)

        near[d] = push(parts.at[1 - parity, pl.ds(fs, 2)], sibk.at[d], ss_sk.at[d], rs_sk.at[d], shard=sibling)
        near[d].start()

    def key_sum(d):
        fs = seqs_of(d)
        near[d].wait()
        for i, layer in enumerate(layers):
            zsend[d, i] = (
                parts[parity, pl.ds(fs, 2), layer].astype(F32) + sibk[d, :, layer].astype(F32)
            ).astype(BF)
            far[d, i] = push(zsend.at[d, i], zrecv.at[d, i], ss_zk.at[d, i], rs_zk.at[d, i], ctx=layer)
            far[d, i].start()

    def half_rows(j):
        return pl.ds((j % 2) * (wr // 2), wr // 2)

    def out_copies(j, ref):
        source = lax.rem(s + n_shard - j // 2, n_shard)
        to = pl.ds(pl.multiple_of(source * cols, cols), cols)
        return (
            pltpu.make_async_copy(ref.at[:, pl.ds(0, cols)], q_out.at[half_rows(j), to], ss_q.at[j]),
            pltpu.make_async_copy(ref.at[:, pl.ds(cols, HEAD_DIM)], kv_out.at[source, half_rows(j)], ss_k.at[j]),
        )

    def wide_copies(j, ref):
        step = wide.shape[2]
        return (pltpu.make_async_copy(ref, wide_out.at[:, pl.ds(j * step, step)], ss_wc.at[j]),)

    class Line:
        def __init__(self, ready, own, landing, ss_i, rs_i, ss_o, copies):
            self.ready, self.own, self.landing = ready, own, landing
            self.ss_i, self.rs_i, self.ss_o, self.copies = ss_i, rs_i, ss_o, copies

        def inward(self, j, ref):
            at = jnp.where(middle, 1, 0)
            return push(ref, self.landing.at[at, j], self.ss_i.at[j], self.rs_i.at[at, j], ctx=inner)

        def outward(self, j):
            return push(self.landing.at[1, j], self.landing.at[1, j], self.ss_o.at[j], self.rs_i.at[1, j], ctx=outer)

        def arrived(self, which, j):
            push(self.landing.at[0, j], self.landing.at[which, j], self.ss_i.at[j], self.rs_i.at[which, j],
                 ctx=inner).wait_recv()

        def outermost(self, j):
            @pl.when(jnp.logical_not(inside))
            def _():
                self.ready(j)
                self.inward(j, self.own(j)).start()

        def first_half(self, j):
            @pl.when(inside)
            def _():
                self.ready(j)
                self.arrived(0, j)
                self.landing[0, j] = (self.own(j)[...].astype(F32) + self.landing[0, j].astype(F32)).astype(BF)
                self.inward(j, self.landing.at[0, j]).start()

        def second_half(self, j):
            self.arrived(1, j)

            @pl.when(middle)
            def _():
                self.landing[1, j] = (self.landing[0, j].astype(F32) + self.landing[1, j].astype(F32)).astype(BF)

            @pl.when(inside)
            def _():
                self.outward(j).start()

            for item in self.copies(j, self.landing.at[1, j]):
                item.start()

        def drain(self, j):
            self.inward(j, self.landing.at[0, j]).wait_send()

            @pl.when(inside)
            def _():
                self.outward(j).wait_send()

            for item in self.copies(j, self.landing.at[1, j]):
                item.wait()

    sends = [[] for j in range(n_shard)]
    line = Line(lambda j: [item.wait() for item in sends[j // 2]] if j % 2 == 0 else None,
                lambda j: pieces.at[j // 2, half_rows(j)] if j >= 2 else weights.at[s, half_rows(j)],
                landing, ss_i, rs_i, ss_o, out_copies)
    wide_line = Line(lambda j: None, lambda j: wide.at[j], wide_landing, ss_wi, rs_wi, ss_wo, wide_copies)
    steps = [(wide_line, j) for j in range(wides)] + [(line, j) for j in range(2 * n_shard)]
    lag, ahead = 2, 4

    def advance(n):
        if n + ahead < len(steps):
            steps[n + ahead][0].outermost(steps[n + ahead][1])
        if n < len(steps):
            steps[n][0].first_half(steps[n][1])
        if n >= lag:
            steps[n - lag][0].second_half(steps[n - lag][1])

    step = width // wides
    for item in load[:4]:
        item.wait()
    for d in range(chips):
        if d:
            first[d].wait()
            origin = lax.rem(s + n_shard - 2 * d, n_shard)
            forwards[d] = push(grads.at[origin], grads.at[origin], ss_fwd.at[d], rs_fwd.at[d], shard=sibling)
            forwards[d].start()
        else:
            own_copies[0].wait()
        forwards[d].wait()
        if d + 1 == chips:
            mix_send()
            for item in load[4:]:
                item.wait()
            attn_t[...] = attn[...].reshape(n_shard * count, cols).T
            for j in range(wides):
                block = grads[:, :, j * step : (j + 1) * step].reshape(n_shard * count, step)
                wide[j] = jnp.dot(attn_t[...], block, preferred_element_type=F32).astype(BF)
                if j < ahead:
                    wide_line.outermost(j)
        attention_back(d)
        if d == 0:
            mix_fold.give(2, mix_fold.take(2, mix_part[0].astype(F32)))
        if d:
            key_sum(d - 1)

    rows_all = grads
    own_copies[1].start()
    key_sum(chips - 1)
    advance(0)
    own_copies[1].wait()

    @pl.loop(0, n_shard)
    def _(e):
        block = rows_all[:, :, pl.ds(pl.multiple_of(e * wr, wr), wr)].reshape(n_shard * count, wr)
        right = pre[:, :, pl.ds(0, cols)].reshape(n_shard * count, cols)
        weights[e, :, pl.ds(0, cols)] = lax.dot_general(
            block, right, (((0,), (0,)), ((), ())), preferred_element_type=F32).astype(BF)

    for i, peer in enumerate(others):
        item = push(weights.at[peer, :, pl.ds(0, cols)], pieces.at[i + 1, :, pl.ds(0, cols)],
                    ss_w.at[i], rs_w.at[i], shard=peer)
        item.start()
        sends[i + 1].append(item)
    advance(1)
    for d in range(chips):
        fs = seqs_of(d)
        total = parts[parity, pl.ds(fs, 2), c].astype(F32) + sibk[d, :, c].astype(F32)
        for i in range(n_ctx - 1):
            far[d, i].wait()
            total = total + zrecv[d, i].astype(F32)
        for i in range(2):
            keyed = norm_back(total[i], kvpre[fs + i], k_gain, k_sum)
            pre[fs + i, :, pl.ds(cols, HEAD_DIM)] = jnp.where(parity == 0, keyed, total[i]).astype(BF)

    @pl.loop(0, n_shard)
    def _(e):
        block = rows_all[:, :, pl.ds(pl.multiple_of(e * wr, wr), wr)].reshape(n_shard * count, wr)
        right = pre[:, :, pl.ds(cols, HEAD_DIM)].reshape(n_shard * count, HEAD_DIM)
        weights[e, :, pl.ds(cols, HEAD_DIM)] = lax.dot_general(
            block, right, (((0,), (0,)), ((), ())), preferred_element_type=F32).astype(BF)

    for i, peer in enumerate(others):
        item = push(weights.at[peer, :, pl.ds(cols, HEAD_DIM)], pieces.at[i + 1, :, pl.ds(cols, HEAD_DIM)],
                    ss_v.at[i], rs_v.at[i], shard=peer)
        item.start()
        sends[i + 1].append(item)
    advance(2)

    order = list(range(1, chips)) + [0]
    to_sibling, to_mate = {}, {}

    def product(at):
        fs = 2 * lax.rem(chip + order[at], chips)
        left = pre[pl.ds(fs, 2)].reshape(2 * count, cols + HEAD_DIM)

        @pl.loop(0, n_shard)
        def _(j):
            part = pl.ds(pl.multiple_of(j * wr, wr), wr)
            value = lax.dot_general(left, w_all[j], (((1,), (1,)), ((), ())), preferred_element_type=F32)
            pair[...] = value.reshape(2, count, wr)
            own_part[at % 2, :, part] = pair[parity]
            to_sib[at, :, part] = pair[1 - parity].astype(BF)

        to_sibling[at] = push(to_sib.at[at], sib.at[at], ss_s.at[at], rs_s.at[at], shard=sibling)
        to_sibling[at].start()

    def chip_sum(at):
        to_sibling[at].wait()
        to_chip[at] = (own_part[at % 2] + sib[at].astype(F32)).astype(BF)
        to_mate[at] = push(to_chip.at[at], got.at[at], ss_c.at[at], rs_c.at[at], shard=mates[order[at] - 1])
        to_mate[at].start()

    gain_sends = []

    def last_sum():
        to_sibling[chips - 1].wait()
        grad = own_part[(chips - 1) % 2] + sib[chips - 1].astype(F32)
        for at in range(chips - 1):
            to_mate[at].wait()
            grad = grad + got[at].astype(F32)
        unit, scale = unit_rows(tokens[...].astype(F32))
        scaled = grad * gain[...]
        rows_out[...] = scale * (scaled - unit * jnp.mean(scaled * unit, axis=-1, keepdims=True))
        gains_own[...] = gains[...]
        summed = jnp.sum(grad * unit, axis=0, keepdims=True)
        lanes = gains.shape[1]
        for n in range(width // lanes):
            gains_own[n : n + 1] = summed[:, n * lanes : (n + 1) * lanes]
        n = 2 * width // lanes
        gains_own[n : n + 1] = q_sum[...]
        gains_own[n + 1 : n + 2] = jnp.where(parity == 0, k_sum[...], jnp.zeros_like(k_sum))
        mine = pltpu.make_async_copy(gains_own, gains_in.at[s], local.at[2])
        mine.start()
        gain_sends.append(mine)
        for i, peer in enumerate(others):
            item = push(gains_own, gains_in.at[s], ss_g.at[i], rs_g.at[i], shard=peer)
            item.start()
            gain_sends.append(item)

    def small_plane():
        for item in small + gain_sends:
            item.wait()
        gains_mid[...] = gains_in[0]
        for i in range(1, n_shard):
            gains_mid[...] += gains_in[i]
        total = router[s].astype(F32)
        for i in range(n_shard - 1):
            total = total + router_in[i].astype(F32)
        router_mid[...] = total.astype(BF)
        for i, layer in enumerate(layers):
            push(gains_mid, gains_far.at[c], ss_h.at[i], rs_h.at[i], ctx=layer).start()
            push(router_mid, router_far.at[c], ss_t.at[i], rs_t.at[i], ctx=layer).start()
        pltpu.make_async_copy(gains_mid, gains_far.at[c], local.at[3]).start()
        pltpu.make_async_copy(router_mid, router_far.at[c], local.at[4]).start()

    def small_all():
        pltpu.make_async_copy(gains_mid, gains_far.at[c], local.at[3]).wait()
        pltpu.make_async_copy(router_mid, router_far.at[c], local.at[4]).wait()
        for i, layer in enumerate(layers):
            push(gains_mid, gains_far.at[c], ss_h.at[i], rs_h.at[i], ctx=layer).wait()
            push(router_mid, router_far.at[c], ss_t.at[i], rs_t.at[i], ctx=layer).wait()
        gains_out[...] = gains_far[0]
        router_out[...] = router_far[0].astype(F32)
        for i in range(1, n_ctx):
            gains_out[...] += gains_far[i]
            router_out[...] += router_far[i].astype(F32)

    side = []
    for at in range(chips):
        side.append(functools.partial(product, at))
        if at:
            side.append(functools.partial(chip_sum, at - 1))
    count_steps = len(steps) + lag
    late = {24: last_sum, 26: mix_last, 29: small_plane}
    for n in range(3, count_steps):
        advance(n)
        if side:
            side.pop(0)()
        if n in late:
            late[n]()
    for job in side:
        job()
    small_all()
    mix_out[...] = mix_fold.take(0, mix_out[...])
    mix_fold.drain()
    for which, j in steps:
        which.drain(j)


def back(n_ctx, n_shard, group, heads, args, ident):
    count, width = args[0].shape
    rows_in, w_all, router, gains, mix_near = args[7], args[8], args[17], args[16], args[18]
    n, z, chips, wides = n_shard, n_ctx, n_shard // 2, 16
    wr, cols = w_all.shape[1], heads * HEAD_DIM
    keys = z * count
    sds, scratch = jax.ShapeDtypeStruct, pltpu.VMEM
    router_shape = router.shape[1:]
    dma = lambda *shape: DMA(shape)
    wide_block, block = (cols, width // wides), (wr, cols + HEAD_DIM)
    return call(
        functools.partial(back_body, z, n, group, heads, wides),
        [
            sds((wr, n * cols), BF), sds((n, wr, HEAD_DIM), BF), sds((cols, width), BF), sds(router_shape, F32),
            sds(gains.shape, F32), sds((count, width), F32), sds((count, width), F32), sds(mix_near.shape, BF),
        ],
        [VMEM] + [ANY] * 8 + [VMEM] * 9 + [ANY, VMEM, VMEM],
        [scratch(item.shape, item.dtype) for item in args[1:7] + args[8:9]] + [dma(7)] + [
            scratch((n, count, width), BF), scratch((cols, n * count), BF),
            scratch((2, count, cols), BF), scratch((heads * count, keys), BF), scratch((heads * count, keys), BF),
            scratch((2, n, z, count, HEAD_DIM), BF), scratch((n, count, cols + HEAD_DIM), BF),
            scratch((1, HEAD_DIM), F32), scratch((1, HEAD_DIM), F32),
            scratch((wides,) + wide_block, BF), scratch((n,) + block, BF),
            scratch((chips, 2, z, count, HEAD_DIM), BF), scratch((chips, z - 1, 2, count, HEAD_DIM), BF),
            scratch((chips, z - 1, 2, count, HEAD_DIM), BF), scratch((2, wides) + wide_block, BF),
            scratch((n,) + block, BF), scratch((2, 2 * n, wr // 2, cols + HEAD_DIM), BF),
            scratch((2, count, width), F32), scratch((2, count, wr), F32), scratch((chips, count, width), BF),
            scratch((chips, count, width), BF), scratch((chips - 1, count, width), BF),
            scratch((chips - 1, count, width), BF),
            scratch((n - 1,) + router_shape, BF), scratch(router_shape, BF), scratch((z,) + router_shape, BF),
            scratch(gains.shape, F32), scratch((n,) + gains.shape, F32), scratch(gains.shape, F32),
            scratch((z,) + gains.shape, F32), scratch((n, mix_near.shape[1], 512), BF),
            scratch((z - 1, count, width), BF), scratch((z - 1, count, width), BF), dma(7),
            dma(chips), dma(chips), dma(chips), dma(chips), dma(chips), dma(chips), dma(chips, z - 1), dma(chips, z - 1),
            dma(wides), dma(2, wides), dma(wides), dma(wides), dma(n - 1), dma(n - 1), dma(2 * n), dma(2, 2 * n), dma(2 * n),
            dma(2 * n), dma(2 * n), dma(n - 1), dma(n - 1), dma(n - 1), dma(n - 1), dma(z - 1), dma(z - 1), dma(z - 1), dma(z - 1),
            dma(chips), dma(chips), dma(chips - 1), dma(chips - 1), dma(n - 1), dma(n - 1), dma(z), dma(z), dma(n - 1), dma(n - 1),
        ],
        ident, args, mib=62, out_specs=[ANY, ANY, ANY, VMEM, VMEM, VMEM, VMEM, ANY],
    )


def dispatch_body(n_ctx, n_shard, group, tile, rows, tail, code, recv, tail_recv,
                  zrows, ztail, ready, tail_ready, local, ss_z, rs_z, ss_t, rs_t, ss_x, rs_x, ss_y, rs_y):
    c, s, parity, sibling, others, layers = here(n_ctx, n_shard)
    greet(others, layers)
    count, width = rows.shape
    groups = n_ctx // group
    slots = recv.shape[2]
    own = [pltpu.make_async_copy(rows, zrows.at[c], local.at[0]), pltpu.make_async_copy(tail, ztail.at[c], local.at[1])]
    fans = [
        Fan(n_ctx, c, lambda d: ztail.at[flip_bits(c, d)], ss_t, rs_t, True),
        Fan(n_ctx, c, lambda d: zrows.at[flip_bits(c, d)], ss_z, rs_z, True),
    ]
    fans[0].send(0, tail)
    fans[1].send(0, rows)
    for item in own:
        item.start()
    waits = []
    seen = set()
    for k in range(groups):
        at = flip_bits(lax.div(c, group), k)
        if k == 0:
            for item in own:
                item.wait()
        table = slot_table(code[at], slots)
        for d in fans[0].order():
            if d < (k + 1) * group and d not in seen:
                fans[0].arrival(d)
                fans[1].arrival(d)
                seen.add(d)
        first = pl.multiple_of(at * group, group)
        block = ztail[pl.ds(first, group)].reshape(group * count, -1)
        tail_ready[k] = jnp.dot(table, block, preferred_element_type=F32).astype(BF).reshape(n_shard, slots, -1)

        @pl.loop(0, width // tile)
        def _(j):
            cols = pl.ds(pl.multiple_of(j * tile, tile), tile)
            block = zrows[pl.ds(first, group), :, cols].reshape(group * count, tile)
            value = jnp.dot(table, block, preferred_element_type=F32).astype(BF)
            ready[k, :, :, cols] = value.reshape(n_shard, slots, tile)

        for i, peer in enumerate(others):
            item = push(ready.at[k, peer], recv.at[s, at], ss_x.at[k, i], rs_x.at[k, i], shard=peer)
            item.start()
            waits.append(item)
            item = push(tail_ready.at[k, peer], tail_recv.at[s, at], ss_y.at[k, i], rs_y.at[k, i], shard=peer)
            item.start()
            waits.append(item)
        item = pltpu.make_async_copy(ready.at[k, s], recv.at[s, at], local.at[2 * k + 2])
        item.start()
        waits.append(item)
        item = pltpu.make_async_copy(tail_ready.at[k, s], tail_recv.at[s, at], local.at[2 * k + 3])
        item.start()
        waits.append(item)
    for fan in fans:
        fan.drain()
    for item in waits:
        item.wait()


def dispatch_rows(n_ctx, n_shard, group, capacity, rows, tail, code, ident):
    groups, slots = code.shape[0], group * capacity
    count, width = rows.shape
    few = tail.shape[1]
    return call(
        functools.partial(dispatch_body, n_ctx, n_shard, group, 512),
        [
            jax.ShapeDtypeStruct((n_shard, groups, slots, width), BF),
            jax.ShapeDtypeStruct((n_shard, groups, slots, few), BF),
        ],
        [VMEM, VMEM, VMEM],
        [
            pltpu.VMEM((n_ctx, count, width), BF), pltpu.VMEM((n_ctx, count, few), BF),
            pltpu.VMEM((groups, n_shard, slots, width), BF), pltpu.VMEM((groups, n_shard, slots, few), BF),
            DMA((2 * groups + 2,)), DMA((n_ctx,)), DMA((n_ctx,)), DMA((n_ctx,)), DMA((n_ctx,)),
        ] + [DMA((groups, n_shard - 1))] * 4,
        ident, (rows, tail, code), mib=56,
    )


def combine_body(n_ctx, n_shard, group, tile, rows, tail, mix, code, out, tail_out, mix_out,
                 land, tail_land, value, tail_value, zsend, zrecv, tsend, trecv, msend, mrecv, mix_kept, table, local,
                 ss_x, rs_x, ss_y, rs_y, ss_z, rs_z, ss_t, rs_t, ss_m, rs_m):
    c, s, parity, sibling, others, layers = here(n_ctx, n_shard)
    greet(others, layers)
    count, width = out.shape
    groups = n_ctx // group
    slots = rows.shape[2]
    near = {}
    for k in reversed(range(groups)):
        at = flip_bits(lax.div(c, group), k)
        near[k] = []
        for i, peer in enumerate(others):
            item = push(rows.at[peer, at], land.at[k, s], ss_x.at[k, i], rs_x.at[k, i], shard=peer)
            item.start()
            near[k].append(item)
            item = push(tail.at[peer, at], tail_land.at[k, s], ss_y.at[k, i], rs_y.at[k, i], shard=peer)
            item.start()
            near[k].append(item)
        item = pltpu.make_async_copy(rows.at[s, at], land.at[k, s], local.at[k, 0])
        item.start()
        near[k].append(item)
        item = pltpu.make_async_copy(tail.at[s, at], tail_land.at[k, s], local.at[k, 1])
        item.start()
        near[k].append(item)
    for k in range(groups):
        table[k] = slot_table(code[flip_bits(lax.div(c, group), k)], slots).T

    def local_sums(k, block_of):
        @pl.loop(0, width // tile)
        def _(j):
            cols = pl.ds(pl.multiple_of(j * tile, tile), tile)
            value[:, cols] = jnp.dot(table[k], block_of(cols), preferred_element_type=F32)

    def part(ref, d):
        place = lax.rem(flip_bits(c, d), group)
        return ref[pl.ds(pl.multiple_of(place * count, count), count), :]

    def in_group(k):
        return sorted(range(k * group, (k + 1) * group), key=lambda d: (lowest(d) or n_ctx, d))

    mix_fold = Fold(c, msend, mrecv, ss_m, rs_m)
    for k in reversed(range(groups)):
        at = flip_bits(lax.div(c, group), k)
        local_sums(k, lambda cols: mix[:, at, :, cols].reshape(n_shard * slots, tile))
        for d in in_group(k):
            if lowest(d) == 1:
                mix_fold.give(d, part(value, d))
            else:
                mix_kept[d // 2] = part(value, d)
    fold = Fold(c, zsend, zrecv, ss_z, rs_z)
    tail_fold = Fold(c, tsend, trecv, ss_t, rs_t)
    for k in reversed(range(groups)):
        for item in near[k]:
            item.wait()
        local_sums(k, lambda cols: land[k, :, :, cols].reshape(n_shard * slots, tile))
        tail_value[...] = jnp.dot(
            table[k], tail_land[k].reshape(n_shard * slots, -1), preferred_element_type=F32
        )
        for d in in_group(k):
            if lowest(d) == 1:
                fold.give(d, part(value, d))
                tail_fold.give(d, part(tail_value, d))
        for d in in_group(k):
            if lowest(d) != 1:
                if d:
                    mix_fold.give(d, mix_fold.take(d, mix_kept[d // 2]))
                    fold.give(d, fold.take(d, part(value, d)))
                    tail_fold.give(d, tail_fold.take(d, part(tail_value, d)))
                else:
                    mix_out[...] = mix_fold.take(0, mix_kept[0])
                    out[...] = fold.take(0, part(value, 0))
                    tail_out[...] = tail_fold.take(0, part(tail_value, 0))
    for item in (mix_fold, fold, tail_fold):
        item.drain()


def combine_rows(n_ctx, n_shard, group, rows, tail, mix, code, ident):
    groups, slots, width = rows.shape[1:]
    few = tail.shape[3]
    count = code.shape[2] // group
    sds = jax.ShapeDtypeStruct
    return call(
        functools.partial(combine_body, n_ctx, n_shard, group, 512),
        [sds((count, width), F32), sds((count, few), F32), sds((count, width), F32)],
        [VMEM] * 4,
        [
            pltpu.VMEM((groups, n_shard, slots, width), BF), pltpu.VMEM((groups, n_shard, slots, few), BF),
            pltpu.VMEM((group * count, width), F32), pltpu.VMEM((group * count, few), F32),
            pltpu.VMEM((n_ctx - 1, count, width), BF), pltpu.VMEM((n_ctx - 1, count, width), BF),
            pltpu.VMEM((n_ctx - 1, count, few), BF), pltpu.VMEM((n_ctx - 1, count, few), BF),
            pltpu.VMEM((n_ctx - 1, count, width), BF), pltpu.VMEM((n_ctx - 1, count, width), BF),
            pltpu.VMEM((n_ctx // 2, count, width), F32), pltpu.VMEM((groups, group * count, n_shard * slots), BF),
            DMA((groups, 2)),
        ] + [DMA((groups, n_shard - 1))] * 4 + [DMA((n_ctx,))] * 6,
        ident, (rows, tail, mix, code), mib=60, out_specs=[VMEM] * 3,
    )


def expert_body(n_ctx, n_shard, group, half, tile,
                rows, tail, code, gate_in, up_in, down_in, cot_in,
                out, tail_out, mix_near, mix_far, mix_part, g_gate, g_up, g_down,
                w_gate, w_up, w_down, loaded, zrows, ztail, ready, tail_ready, recv, tail_recv, cot, back_rows, back_tail, land, tail_land,
                hidden, grad_gate, grad_up, work, slot_dot, table, tail_value,
                zrecv, tsend, trecv, stage, stage_d, local, ss_a, rs_a,
                ss_z, rs_z, ss_t, rs_t, ss_x, rs_x, ss_y, rs_y, ss_d, rs_d, ss_e, rs_e, ss_m, rs_m,
                ss_fz, rs_fz, ss_ft, rs_ft, ss_st, ss_sd):
    c, s, parity, sibling, others, layers = here(n_ctx, n_shard)
    count, width = rows.shape
    few = tail.shape[1]
    inner = w_gate.shape[1]
    groups = n_ctx // group
    slots = recv.shape[2]
    chunk = half * slots
    experts = n_ctx * n_shard
    expert = c * n_shard + s
    mine = by_core(s, n_shard)
    loads = [
        pltpu.make_async_copy(rows, zrows.at[c], local.at[0]),
        pltpu.make_async_copy(tail, ztail.at[c], local.at[1]),
    ] + [
        pltpu.make_async_copy(cot_in.at[flip_bits(lax.div(c, group), k)], cot.at[k], local.at[2 + 2 * groups + k])
        for k in range(groups)
    ]
    greet(others, layers)
    fan = Fan(n_ctx, c, lambda d: ztail.at[flip_bits(c, d)], ss_t, rs_t, True)
    fan.send(0, tail)
    near_layer, far_layer = flip_bits(c, 1), flip_bits(c, 2)
    sides = [slice(0, width // 2), slice(width // 2, width)]
    near = push(rows, zrows.at[c], ss_z.at[0], rs_z.at[0], ctx=near_layer)
    near.start()
    edge = jnp.logical_or(c == 0, c == n_ctx - 1)
    away = [push(rows.at[:, side], zrows.at[c, :, side], ss_z.at[1 + n], rs_z.at[1 + n], ctx=far_layer)
            for n, side in enumerate(sides)]
    passed = [push(zrows.at[far_layer, :, side], zrows.at[far_layer, :, side], ss_z.at[3 + n], rs_z.at[3 + n],
                   ctx=near_layer) for n, side in enumerate(sides)]

    @pl.when(jnp.logical_not(edge))
    def _():
        for item in away:
            item.start()

    loads += [
        pltpu.make_async_copy(a, b, loaded.at[n])
        for n, (a, b) in enumerate(((gate_in, w_gate), (up_in, w_up), (down_in, w_down)))
    ]
    loads[0].start()
    loads[1].start()

    sent = {0: [], 1: []}
    early = (slots // group) // 16 * 16
    place = lax.rem(c, group)
    early_at = pl.multiple_of(place * (slots - early), 16)
    late_at = pl.multiple_of((1 - place) * early, 16)

    def some_slots(rows_code, first, amount):
        places = (lax.broadcasted_iota(jnp.int32, (amount, rows_code.shape[1]), 0) + first).astype(F32)
        return jnp.concatenate(
            [(places == rows_code[e : e + 1, :]).astype(BF) for e in range(n_shard)], axis=0
        )

    own_code = code[lax.div(c, group), :, pl.ds(pl.multiple_of(place * count, count), count)]
    early_picks = some_slots(own_code, early_at, early)

    @pl.loop(0, width // tile)
    def _(j):
        cols = pl.ds(pl.multiple_of(j * tile, tile), tile)
        moved = jnp.dot(early_picks, rows[:, cols], preferred_element_type=F32).astype(BF)
        ready[0, :, pl.ds(early_at, early), cols] = moved.reshape(n_shard, early, tile)

    for i, peer in enumerate(others):
        sent[0].append(push(ready.at[0, peer, pl.ds(early_at, early)], recv.at[0, mine, pl.ds(early_at, early)],
                            ss_a.at[i], rs_a.at[i], shard=peer))
        sent[0][-1].start()
    for item in loads[2:]:
        item.start()
    loads[0].wait()
    loads[1].wait()
    near.wait_send()

    @pl.when(edge)
    def _():
        for item in away:
            item.start()

    near.wait_recv()
    for k in range(groups):
        at = flip_bits(lax.div(c, group), k)
        whole = slot_table(code[at], slots)
        table[k] = whole.T
        for d in (2, 3) if k else (1,):
            fan.arrival(d)
        first = pl.multiple_of(at * group, group)
        block = ztail[pl.ds(first, group)].reshape(group * count, few)
        tail_ready[k] = jnp.dot(whole, block, preferred_element_type=F32).astype(BF).reshape(n_shard, slots, few)
        amount = slots if k else slots - early
        begin = 0 if k else late_at
        span = pl.ds(begin, amount)
        picks = some_slots(code[at], begin, amount)
        for n, side in enumerate(sides if k else [slice(0, width)]):
            if k:
                if n == 0:
                    for m in range(2):
                        away[m].wait_recv()
                        passed[m].start()
                passed[n].wait_recv()

            @pl.loop(side.start // tile, side.stop // tile)
            def _(j):
                cols = pl.ds(pl.multiple_of(j * tile, tile), tile)
                block = zrows[pl.ds(first, group), :, cols].reshape(group * count, tile)
                moved = jnp.dot(picks, block, preferred_element_type=F32).astype(BF)
                ready[k, :, span, cols] = moved.reshape(n_shard, amount, tile)

            fresh = []
            for i, peer in enumerate(others):
                fresh.append(push(ready.at[k, peer, span, side], recv.at[k, mine, span, side],
                                  ss_x.at[k + n, i], rs_x.at[k + n, i], shard=peer))
            if n == 0:
                for i, peer in enumerate(others):
                    fresh.append(push(tail_ready.at[k, peer], tail_recv.at[k, mine], ss_y.at[k, i], rs_y.at[k, i], shard=peer))
                fresh.append(pltpu.make_async_copy(tail_ready.at[k, s], tail_recv.at[k, mine], local.at[3 + 2 * k]))
            if n == k:
                fresh.append(pltpu.make_async_copy(ready.at[k, s], recv.at[k, mine], local.at[2 + 2 * k]))
            for item in fresh:
                item.start()
            sent[k] += fresh
    fan.drain()
    for item in away + passed:
        item.wait_send()
    for item in loads[2:]:
        item.wait()

    gate_pre, up_pre = work.at[0:chunk, 0:inner], work.at[0:chunk, inner : 2 * inner]
    value = work.at[0 : group * count, 0:width]
    column = lax.broadcasted_iota(jnp.int32, (1, few), 1)
    is_coarse, is_fine = column == expert, column == experts + expert

    def send_back(src, dst, p, ss, rs):
        e = from_core(p, n_shard)

        @pl.when(s != e)
        def _():
            push(src.at[p], dst.at[s], ss.at[e], rs.at[s], shard=e).start()

        @pl.when(s == e)
        def _():
            pltpu.make_async_copy(src.at[p], dst.at[e], rs.at[e]).start()

    def wait_back(src, dst, ss, rs):
        for p in range(n_shard):
            e = from_core(p, n_shard)

            @pl.when(s != e)
            def _():
                push(src.at[p], dst.at[e], ss.at[e], rs.at[e], shard=e).wait()

            @pl.when(s == e)
            def _():
                pltpu.make_async_copy(src.at[p], dst.at[e], rs.at[e]).wait()

    def experts_part(k, h):
        of = slice(h * half, (h + 1) * half)
        r = pl.ds((k * n_shard + h * half) * slots, chunk)
        gates = jnp.sum(
            jnp.where(is_coarse | is_fine, tail_recv[k, of].reshape(chunk, few).astype(F32), 0.0), axis=1, keepdims=True
        )

        @pl.loop(0, inner // 256)
        def _(j):
            cols = pl.ds(pl.multiple_of(j * 256, 256), 256)
            x = recv[k, of].reshape(chunk, width)
            g = jnp.dot(x, w_gate[:, cols], preferred_element_type=F32)
            u = jnp.dot(x, w_up[:, cols], preferred_element_type=F32)
            gate_pre[:, cols] = g
            up_pre[:, cols] = u
            hidden[r, cols] = (g * jax.nn.sigmoid(g) * u).astype(BF)

        slot_dot[...] = jnp.zeros_like(slot_dot)

        @pl.loop(0, width // tile)
        def _(j):
            cols = pl.ds(pl.multiple_of(j * tile, tile), tile)
            o = jnp.dot(hidden[r, :], w_down[:, cols], preferred_element_type=F32).astype(BF).astype(F32)
            up_row = cot[k, of, :, cols].reshape(chunk, tile).astype(F32)
            slot_dot[...] += jnp.sum(o * up_row, axis=1, keepdims=True)
            ready[k, of, :, cols] = (gates * o).astype(BF).reshape(half, slots, tile)
            cot[k, of, :, cols] = (gates * up_row).astype(BF).reshape(half, slots, tile)

        coarse = slot_dot[...].astype(BF).astype(F32)
        fine = slot_dot[...] - coarse
        back_tail[k, of] = jnp.where(is_coarse, coarse, jnp.where(is_fine, fine, 0.0)).astype(BF).reshape(half, slots, few)

        @pl.loop(0, inner // 256)
        def _(j):
            cols = pl.ds(pl.multiple_of(j * 256, 256), 256)
            gh = lax.dot_general(cot[k, of].reshape(chunk, width), w_down[cols, :], (((1,), (1,)), ((), ())),
                                 preferred_element_type=F32)
            g, u = gate_pre[:, cols], up_pre[:, cols]
            sig = jax.nn.sigmoid(g)
            grad_gate[r, cols] = (gh * u * (sig * (1.0 + g * (1.0 - sig)))).astype(BF)
            grad_up[r, cols] = (gh * (g * sig)).astype(BF)

        @pl.loop(0, width // tile)
        def _(j):
            cols = pl.ds(pl.multiple_of(j * tile, tile), tile)
            gx = lax.dot_general(grad_gate[r, :], w_gate[cols, :], (((1,), (1,)), ((), ())), preferred_element_type=F32)
            gx += lax.dot_general(grad_up[r, :], w_up[cols, :], (((1,), (1,)), ((), ())), preferred_element_type=F32)
            back_rows[k, of, :, cols] = gx.astype(BF).reshape(half, slots, tile)

    def send_part(k, h):
        for p in range(h * half, (h + 1) * half):
            send_back(back_rows.at[k], land.at[k], p, ss_d.at[k], rs_d.at[k])
            send_back(back_tail.at[k], tail_land.at[k], p, ss_e.at[k], rs_e.at[k])

    halves = n_shard // half
    for k in range(groups):
        for item in sent[k]:
            item.wait()
        for h in range(halves):
            experts_part(k, h)
            if k or h + 1 < halves:
                send_part(k, h)
    send_part(0, halves - 1)
    for p in range(n_shard):
        send_back(ready.at[groups - 1], mix_far, p, ss_m, rs_m)
    keep = pltpu.make_async_copy(ready.at[0], mix_near, local.at[0])
    keep.start()

    everything = groups * n_shard * slots

    def stage_out(j, which):
        at = pl.ds(pl.multiple_of(j * 256, 256), 256)
        return pltpu.make_async_copy(stage.at[which], (g_gate, g_up)[which].at[at], ss_st.at[which])

    @pl.loop(0, width // 256)
    def _(j):
        x = recv[:, :, :, pl.ds(pl.multiple_of(j * 256, 256), 256)].reshape(everything, 256)
        for which, grad in enumerate((grad_gate, grad_up)):
            total = lax.dot_general(x, grad[...], (((0,), (0,)), ((), ())), preferred_element_type=F32).astype(BF)

            @pl.when(j >= 1)
            def _():
                stage_out(j - 1, which).wait()

            stage[which] = total
            stage_out(j, which).start()

    def down_out(j):
        return pltpu.make_async_copy(stage_d, g_down.at[:, pl.ds(pl.multiple_of(j * 256, 256), 256)], ss_sd)

    @pl.loop(0, width // 256)
    def _(j):
        grad = cot[:, :, :, pl.ds(pl.multiple_of(j * 256, 256), 256)].reshape(everything, 256)
        total = lax.dot_general(
            hidden[...], grad, (((0,), (0,)), ((), ())), preferred_element_type=F32).astype(BF)

        @pl.when(j >= 1)
        def _():
            down_out(j - 1).wait()

        stage_d[...] = total
        down_out(j).start()

    last = width // 256 - 1
    stage_out(last, 0).wait()
    stage_out(last, 1).wait()
    down_out(last).wait()

    def local_sums(k, ref):
        @pl.loop(0, width // tile)
        def _(j):
            cols = pl.ds(pl.multiple_of(j * tile, tile), tile)
            block = ref[k, :, :, cols].reshape(n_shard * slots, tile)
            value[:, cols] = jnp.dot(table[k], block, preferred_element_type=F32)

    def part(ref, d):
        place = lax.rem(flip_bits(c, d), group)
        return ref[pl.ds(pl.multiple_of(place * count, count), count), :]

    folds = [Fold(c, zrows.at[:, :, side], zrecv.at[:, :, side], ss_fz.at[n], rs_fz.at[n]) for n, side in enumerate(sides)]
    tail_fold = Fold(c, tsend, trecv, ss_ft, rs_ft)
    for k in reversed(range(groups)):
        wait_back(back_rows.at[k], land.at[k], ss_d.at[k], rs_d.at[k])
        wait_back(back_tail.at[k], tail_land.at[k], ss_e.at[k], rs_e.at[k])
        local_sums(k, land)
        tail_value[...] = jnp.dot(table[k], tail_land[k].reshape(n_shard * slots, few), preferred_element_type=F32)
        if k:
            tail_fold.give(3, part(tail_value, 3))
            folds[0].give(3, part(value, 3)[:, sides[0]])
            folds[0].items[3].wait_send()
            folds[0].left.add(3)
            folds[1].give(3, part(value, 3)[:, sides[1]])
            for fold, side in zip(folds, sides):
                fold.give(2, fold.take(2, part(value, 2)[:, side]))
            tail_fold.give(2, tail_fold.take(2, part(tail_value, 2)))
        else:
            tail_fold.give(1, part(tail_value, 1))
            for fold, side in zip(folds, sides):
                fold.give(1, part(value, 1)[:, side])
    out[...] = part(value, 0)
    wait_back(ready.at[groups - 1], mix_far, ss_m, rs_m)
    keep.wait()
    again = pltpu.make_async_copy(mix_far, ready.at[0], local.at[0])
    again.start()
    again.wait()

    @pl.loop(0, width // tile)
    def _(j):
        cols = pl.ds(pl.multiple_of(j * tile, tile), tile)
        block = ready[0, :, :, cols].reshape(n_shard * slots, tile)
        value[:, cols] = jnp.dot(table[1], block, preferred_element_type=F32)

    for d in (2, 3):
        mix_part[d - 2] = part(value, d).astype(BF)
    for fold, side in zip(folds, sides):
        out[:, side] = fold.take(0, out[:, side])
    tail_out[...] = tail_fold.take(0, part(tail_value, 0))
    for fold in folds + [tail_fold]:
        fold.drain()


def run_experts(n_ctx, n_shard, group, capacity, rows, tail, code, w_gate, w_up, w_down, cot_rows, ident):
    n, z, groups, slots = n_shard, n_ctx, code.shape[0], group * capacity
    count, width = rows.shape
    few, inner, half = tail.shape[1], w_gate.shape[1], n_shard // 2
    everything, chunk = groups * n * slots, half * slots
    sds, scratch = jax.ShapeDtypeStruct, pltpu.VMEM
    dma = lambda *shape: DMA(shape)
    wide, thin = (groups, n, slots, width), (groups, n, slots, few)
    return call(
        functools.partial(expert_body, z, n, group, half, 512),
        [
            sds((count, width), F32), sds((count, few), F32), sds((n, slots, width), BF), sds((n, slots, width), BF),
            sds((2, count, width), BF), sds((width, inner), BF), sds((width, inner), BF), sds((inner, width), BF),
        ],
        [VMEM] * 3 + [ANY] * 4,
        [scratch(item.shape, BF) for item in (w_gate, w_up, w_down)] + [
            dma(3),
            scratch((z, count, width), BF), scratch((z, count, few), BF), scratch(wide, BF), scratch(thin, BF),
            scratch(wide, BF), scratch(thin, BF), scratch(wide, BF), scratch(wide, BF), scratch(thin, BF),
            scratch(wide, BF), scratch(thin, BF),
            scratch((everything, inner), BF), scratch((everything, inner), BF), scratch((everything, inner), BF),
            scratch((max(chunk, group * count), max(2 * inner, width)), F32), scratch((chunk, 1), F32),
            scratch((groups, group * count, n * slots), BF),
            scratch((group * count, few), F32), scratch((z - 1, count, width), BF),
            scratch((z - 1, count, few), BF), scratch((z - 1, count, few), BF),
            scratch((2, 256, inner), BF), scratch((inner, 256), BF), dma(2 + 3 * groups), dma(n - 1), dma(n - 1),
        ] + [dma(5)] * 2 + [dma(z)] * 2 + [dma(groups + 1, n - 1)] * 2 + [dma(groups, n - 1)] * 2 + [dma(groups, n)] * 4
        + [dma(n)] * 2 + [dma(2, z)] * 2 + [dma(z)] * 2 + [dma(2), DMA],
        ident, (rows, tail, code, w_gate, w_up, w_down, cot_rows), mib=62, out_specs=[VMEM] * 2 + [ANY] * 2 + [VMEM] + [ANY] * 3,
    )


def finish_types_body(q, o, g, u, d, kv, tokens, part, mid, mix, gains, router,
                      q_out, o_out, g_out, u_out, d_out, k_out, v_out, tokens_out, mixed_out,
                      attn_gain, ffn_gain, q_gain, k_gain, router_out):
    for source, target in ((q, q_out), (o, o_out), (g, g_out), (u, u_out), (d, d_out)):
        target[...] = source[...].astype(F32)
    for head in range(kv.shape[0] // 2):
        lanes = slice(head * HEAD_DIM, (head + 1) * HEAD_DIM)
        k_out[:, lanes] = kv[2 * head].astype(F32)
        v_out[:, lanes] = kv[2 * head + 1].astype(F32)
    tokens_out[...] = tokens[...] + part[...]
    mixed_out[...] = (mid[...] + mix[...]).astype(BF)
    n = attn_gain.shape[0]
    attn_gain[...] = gains[0:n]
    ffn_gain[...] = gains[n : 2 * n]
    q_gain[...] = gains[2 * n : 2 * n + 1]
    k_gain[...] = gains[2 * n + 1 : 2 * n + 2]
    router_out[...] = router[...]


def finish_types(q, o, g, u, d, kv, tokens, part, mid, mix, gains, router):
    steps = 8
    sds = jax.ShapeDtypeStruct
    heads, wr, lanes = kv.shape
    width = tokens.shape[1]
    by_rows = lambda shape: pl.BlockSpec((shape[0] // steps,) + shape[1:], lambda i: (i, 0))
    whole = lambda shape: pl.BlockSpec(shape, lambda i: (0, 0))
    kv_shape, gain_shape, one = (wr, heads // 2 * lanes), (width // lanes, lanes), (1, lanes)
    ins = [q, o, g, u, d, kv, tokens, part, mid, mix, gains, router]
    in_specs = [by_rows(item.shape) for item in (q, o, g, u, d)]
    in_specs += [pl.BlockSpec((heads, wr // steps, lanes), lambda i: (0, i, 0))]
    in_specs += [by_rows(tokens.shape)] * 4 + [whole(gains.shape), whole(router.shape)]
    outs = [sds(item.shape, F32) for item in (q, o, g, u, d)] + [sds(kv_shape, F32)] * 2
    outs += [sds(tokens.shape, F32), sds(tokens.shape, BF)]
    out_specs = [by_rows(item.shape) for item in outs]
    small = [gain_shape, gain_shape, one, one, router.shape]
    return pl.pallas_call(
        finish_types_body,
        grid=(steps,),
        out_shape=outs + [sds(shape, F32) for shape in small],
        in_specs=in_specs,
        out_specs=out_specs + [whole(shape) for shape in small],
        compiler_params=pltpu.CompilerParams(vmem_limit_bytes=62 * 2**20),
    )(*ins)


def rms_scale(hidden, gain):
    return hidden * lax.rsqrt(jnp.mean(hidden * hidden, axis=-1, keepdims=True) + epsilon) * gain


def rotate(headwise, places):
    half_size = headwise.shape[-1] // 2
    frequency = rope_base ** (-jnp.arange(half_size, dtype=F32) * 2.0 / headwise.shape[-1])
    angles = places.astype(F32)[:, None] * frequency[None, :]
    cosine = jnp.cos(angles)[:, None, :]
    sine = jnp.sin(angles)[:, None, :]
    former = headwise[..., :half_size]
    latter = headwise[..., half_size:]
    return jnp.concatenate(
        [former * cosine - latter * sine, latter * cosine + former * sine], axis=-1
    )


def place_of(row_ids, order, block_rows):
    block_ids = jnp.arange(order.shape[0], dtype=jnp.int32)
    owner_block = row_ids // block_rows
    picked_block = jnp.sum(
        jnp.where(owner_block[:, None] == block_ids[None, :], order[None, :], 0), axis=1
    )
    return picked_block * block_rows + row_ids % block_rows


def dot(left, right):
    return jnp.dot(left, right, preferred_element_type=F32)


def contract_rows(left, right):
    return lax.dot_general(left, right, (((0,), (0,)), ((), ())), preferred_element_type=F32)


def contract_cols(left, right):
    return lax.dot_general(left, right, (((1,), (1,)), ((), ())), preferred_element_type=F32)


def exchange_shard(x):
    return lax.all_to_all(x, "shard", split_axis=0, concat_axis=0, tiled=True)


def gather_ctx(x):
    return lax.all_gather(x, "ctx", axis=0, tiled=False)


def shards(
    tokens,
    cotangent,
    block_order,
    routes,
    attn_gain,
    w_query,
    key_weight,
    value_weight,
    query_gain,
    key_gain,
    w_out,
    ffn_gain,
    w_router,
    w_gate,
    w_up,
    w_down,
):
    rows = tokens.shape[1]
    width = tokens.shape[2]
    ctx_count = lax.axis_size("ctx")
    shard_count = lax.axis_size("shard")
    my_ctx = lax.axis_index("ctx")
    my_shard = lax.axis_index("shard")
    experts = ctx_count * shard_count
    block_rows = rows // 2
    heads = QUERY_HEADS // shard_count
    head_cols = heads * HEAD_DIM
    sharers = shard_count // KEY_VALUE_HEADS
    score_scale = HEAD_DIM ** (-0.5)
    top_count = routes.shape[2]
    capacity = rows * top_count // experts + max(rows * top_count // (4 * experts), 1)
    sequence = rows * ctx_count
    plane = rows * shard_count
    wrows = width // shard_count

    inputs = tokens[0].astype(F32)
    upstream_b = cotangent[0]
    upstream = upstream_b.astype(F32)

    group = 1
    while group * capacity % 16:
        group *= 2
    groups = ctx_count // group
    small = plane * width <= 2**21 and ctx_count == 4 and group == 2
    slot_rows = shard_count * ctx_count * capacity
    block_shape = (shard_count, groups, group * capacity)
    row_ids = my_ctx * rows + jnp.arange(rows, dtype=jnp.int32)
    q_places = place_of(row_ids, block_order, block_rows)
    k_places = place_of(jnp.arange(sequence, dtype=jnp.int32), block_order, block_rows)
    bias = jnp.where(k_places[None, :] <= q_places[:, None], 0.0, -1e30).astype(F32)
    frequency = rope_base ** (-jnp.arange(HEAD_DIM // 2, dtype=F32) * 2.0 / HEAD_DIM)
    angles = q_places.astype(F32)[:, None] * frequency[None, :]
    cosine = jnp.concatenate([jnp.cos(angles)] * 2, axis=1)
    sine = jnp.concatenate([-jnp.sin(angles), jnp.sin(angles)], axis=1)
    (
        normed_all, w_mine, router_all, code, upstream_rows, query_pre, kv_pre, queries, kv_all, attn_rows, middle,
        second_b,
    ) = front(
        ctx_count, shard_count, group, capacity, KEY_VALUE_HEADS, small,
        (
            tokens[0], attn_gain[None], w_query, key_weight, value_weight, routes[0].T, w_router.T, upstream_b,
            cosine, sine, bias, query_gain[None], key_gain[None], w_out, ffn_gain[None],
        ),
        0,
    )
    is_key = lax.rem(my_shard, 2) == 0
    part_count = sharers // 2

    def prep(pre, gain):
        shape = pre.shape
        flat = pre.reshape(-1, rows, shape[-2], HEAD_DIM)
        return jax.vmap(lambda v: rotate(rms_scale(v, gain), q_places))(flat).reshape(shape)

    logits = contract_cols(second_b, router_all)
    chosen = jnp.sum(
        (routes[0][:, :, None] == jnp.arange(experts, dtype=jnp.int32)).astype(F32), axis=1
    )

    def gates_of(log, mask):
        masked = jnp.where(mask > 0, log, -1e30)
        peak = jnp.max(masked, axis=-1, keepdims=True)
        risen = jnp.exp(masked - peak) * mask
        return risen / jnp.maximum(jnp.sum(risen, axis=-1, keepdims=True), 1e-30)

    gates = gates_of(logits, chosen)

    tail_cols = -(-2 * experts // 128) * 128

    def two_parts(value):
        coarse = value.astype(BF).astype(F32)
        return coarse.astype(BF), (value - coarse).astype(BF)

    gates_two = jnp.concatenate(two_parts(gates), axis=1)
    gates_two = jnp.pad(gates_two, ((0, 0), (0, tail_cols - 2 * experts)))
    if small:
        grad_second, back_tail, mix_near, unused, mix_part, grad_w_gate, grad_w_up, grad_w_down = run_experts(
            ctx_count, shard_count, group, capacity, second_b, gates_two, code, w_gate[0], w_up[0], w_down[0],
            upstream_rows, 3,
        )
    else:
        received, gate_tail = dispatch_rows(ctx_count, shard_count, group, capacity, second_b, gates_two, code, 3)
        received = received.reshape(slot_rows, width)
        my_expert = my_ctx * shard_count + my_shard
        upstream_rows = jnp.swapaxes(upstream_rows, 0, 1).reshape(slot_rows, width)
        column = jnp.arange(tail_cols, dtype=jnp.int32)[None, :]
        mine_column = (column == my_expert) | (column == experts + my_expert)
        gate_tail = gate_tail.reshape(slot_rows, tail_cols).astype(F32)
        slot_gates = jnp.sum(jnp.where(mine_column, gate_tail, 0.0), axis=1, keepdims=True)
        gate_pre = dot(received, w_gate[0])
        up_pre = dot(received, w_up[0])
        activated = jax.nn.silu(gate_pre)
        hidden_b = (activated * up_pre).astype(BF)
        expert_out = dot(hidden_b, w_down[0]).astype(BF)
        expert_out_f = expert_out.astype(F32)
        mix_sent = (slot_gates * expert_out_f).astype(BF)
        mix_sent, upstream_rows, expert_out = lax.optimization_barrier((mix_sent, upstream_rows, expert_out))
        expert_out_f = expert_out.astype(F32)
        mix_back = exchange_shard(mix_sent.reshape(block_shape + (width,)))
        upstream_rows = upstream_rows.astype(F32)
        slot_dot = jnp.sum(expert_out_f * upstream_rows, axis=1, keepdims=True)
        grad_expert = (slot_gates * upstream_rows).astype(BF)
        grad_w_down = contract_rows(hidden_b, grad_expert)
        grad_hidden = contract_cols(grad_expert, w_down[0])
        sigmoid_g = jax.nn.sigmoid(gate_pre)
        silu_slope = sigmoid_g * (1.0 + gate_pre * (1.0 - sigmoid_g))
        grad_gate_pre = (grad_hidden * up_pre * silu_slope).astype(BF)
        grad_up_pre = (grad_hidden * activated).astype(BF)
        grad_w_gate = contract_rows(received, grad_gate_pre)
        grad_w_up = contract_rows(received, grad_up_pre)
        grad_received = contract_cols(grad_gate_pre, w_gate[0]) + contract_cols(grad_up_pre, w_up[0])

        coarse, fine = two_parts(slot_dot)
        tail = jnp.where(column == my_expert, coarse, jnp.where(column == experts + my_expert, fine, jnp.zeros((), BF)))
        grad_second, back_tail, mixture = combine_rows(
            ctx_count, shard_count, group, grad_received.astype(BF).reshape(block_shape + (width,)),
            tail.reshape(block_shape + (tail_cols,)), mix_back, code, 4,
        )
    grad_gates = back_tail[:, :experts] + back_tail[:, experts : 2 * experts]
    grad_logits_b = (
        gates * (grad_gates - jnp.sum(gates * grad_gates, axis=-1, keepdims=True))
    ).astype(BF)
    router_part = contract_rows(grad_logits_b, second_b).astype(BF)
    grad_second = grad_second + dot(grad_logits_b, router_all)
    unused, norm_two_back = jax.vjp(rms_scale, middle, ffn_gain)
    grad_middle_part, grad_ffn_gain = norm_two_back(grad_second)
    grad_middle = upstream + grad_middle_part
    grad_proj_b = grad_middle.astype(BF)

    router_parts = jnp.swapaxes(router_part.reshape(experts, shard_count, wrows), 0, 1)
    if small:
        gains = jnp.concatenate([jnp.zeros((width,), F32), grad_ffn_gain, jnp.zeros((8 * HEAD_DIM,), F32)])
        gains = gains.reshape(-1, HEAD_DIM)
        q_sum, kv_sum, out_sum, router_sum, gains, grad_input_part, mixture, unused = back(
            ctx_count, shard_count, group, heads,
            (
                grad_proj_b, queries, kv_all, attn_rows, query_pre, kv_pre, w_out, normed_all, w_mine,
                cosine, sine, bias, query_gain[None], key_gain[None], tokens[0], attn_gain[None], gains, router_parts,
                mix_near, mix_part, code,
            ),
            5,
        )
        (
            grad_w_query, grad_w_out, grad_w_gate, grad_w_up, grad_w_down, grad_w_key, grad_w_value, grad_tokens, mixed,
            grad_attn_gain, grad_ffn_gain, grad_query_gain, grad_key_gain, grad_w_router,
        ) = finish_types(
            q_sum, out_sum, grad_w_gate, grad_w_up, grad_w_down, kv_sum, grad_middle, grad_input_part, middle, mixture,
            gains, router_sum,
        )
        grad_attn_gain, grad_ffn_gain = grad_attn_gain.reshape(-1), grad_ffn_gain.reshape(-1)
        grad_query_gain, grad_key_gain = grad_query_gain.reshape(-1), grad_key_gain.reshape(-1)
        grad_w_router = grad_w_router.T
    else:
        normed_all = normed_all.reshape(plane, width)
        w_mine = w_mine.reshape(width, head_cols + HEAD_DIM)
        query_pre = query_pre.reshape(shard_count, rows, heads, HEAD_DIM)
        kv_pre = kv_pre.reshape(plane, HEAD_DIM)
        queries = queries.reshape(shard_count, rows, heads, HEAD_DIM)
        kv_all = kv_all.reshape(2, shard_count, sequence, HEAD_DIM)
        keys, values = kv_all[0], kv_all[1]
        attn_rows = attn_rows.reshape(plane, head_cols)
        grad_proj_all = spread(shard_count, grad_proj_b, 5).reshape(plane, width)
        out_part = contract_rows(attn_rows, grad_proj_all).astype(BF)
        out_part, grad_proj_all = lax.optimization_barrier((out_part, grad_proj_all))
        grad_attn = contract_cols(grad_proj_all, w_out).astype(BF)
        grad_heads = grad_attn.reshape(shard_count, rows, heads, HEAD_DIM)
        scores = (
            jnp.einsum("sthd,spd->shtp", queries, keys, preferred_element_type=F32) * score_scale
        )
        scores = scores + bias
        raised = jnp.exp(scores - jnp.max(scores, axis=-1, keepdims=True))
        probs = raised / jnp.sum(raised, axis=-1, keepdims=True)
        probs_b = probs.astype(BF)
        grad_probs = jnp.einsum("sthd,spd->shtp", grad_heads, values, preferred_element_type=F32)
        delta = jnp.sum(probs * grad_probs, axis=-1, keepdims=True)
        grad_scores = (probs * (grad_probs - delta)).astype(BF)
        grad_query = score_scale * jnp.einsum(
            "shtp,spd->sthd", grad_scores, keys, preferred_element_type=F32
        )
        grad_keys = score_scale * jnp.einsum(
            "shtp,sthd->spd", grad_scores, queries, preferred_element_type=F32
        )
        grad_values = jnp.einsum("shtp,sthd->spd", probs_b, grad_heads, preferred_element_type=F32)
        grad_kv = jnp.stack([grad_keys, grad_values]).astype(BF)
        grad_kv = key_back(
            ctx_count, shard_count, grad_kv.reshape(2, shard_count, ctx_count, rows, HEAD_DIM), 6
        )
        unused, query_back = jax.vjp(prep, query_pre, query_gain)
        grad_query_pre, grad_query_gain = query_back(grad_query)
        kv_shape = (shard_count, rows, 1, HEAD_DIM)
        unused, key_prep_back = jax.vjp(prep, kv_pre.reshape(kv_shape), key_gain)
        grad_key_pre, grad_key_gain = key_prep_back(grad_kv.reshape(kv_shape))
        grad_key_gain = jnp.where(is_key, grad_key_gain, 0.0)
        grad_kv_full = jnp.where(
            is_key, grad_key_pre.reshape(plane, HEAD_DIM), grad_kv.reshape(plane, HEAD_DIM)
        ).astype(BF)
        grad_pre = jnp.concatenate(
            [grad_query_pre.reshape(plane, head_cols).astype(BF), grad_kv_full], axis=1
        )
        gains = jnp.concatenate(
            [
                jnp.zeros((1, width), F32),
                grad_ffn_gain[None],
                jnp.pad(
                    jnp.concatenate([grad_query_gain, grad_key_gain])[None],
                    ((0, 6 - 1), (0, width - 2 * HEAD_DIM)),
                ),
            ]
        )
        grad_w = contract_rows(normed_all, grad_pre).astype(BF).reshape(shard_count, wrows, -1)
        q_sum, kv_sum, out_sum, router_sum, gains, grad_input_part = finish(
            ctx_count, shard_count, head_cols, grad_w, out_part.reshape(8, -1, width), router_parts, gains, grad_pre, w_mine,
            tokens[0], attn_gain[None], 8,
        )
        mixed = (middle + mixture).astype(BF)
        grad_tokens = grad_middle + grad_input_part
        gains = gains.reshape(-1)
        grad_attn_gain, grad_ffn_gain = gains[:width], gains[width : 2 * width]
        grad_query_gain = gains[2 * width : 2 * width + HEAD_DIM]
        grad_key_gain = gains[2 * width + HEAD_DIM : 2 * width + 2 * HEAD_DIM]
        grad_w_query = q_sum.astype(F32)
        grad_w_out = out_sum.reshape(head_cols, width).astype(F32)
        kinds = kv_sum.astype(F32).reshape(KEY_VALUE_HEADS, part_count, 2, wrows, HEAD_DIM)
        kinds = jnp.transpose(jnp.sum(kinds, axis=1), (1, 2, 0, 3)).reshape(2, wrows, -1)
        grad_w_key, grad_w_value = kinds[0], kinds[1]
        grad_w_router = router_sum.T
    return (
        mixed[None],
        grad_tokens[None],
        grad_attn_gain,
        grad_w_query,
        grad_w_key,
        grad_w_value,
        grad_query_gain,
        grad_key_gain,
        grad_w_out,
        grad_ffn_gain,
        grad_w_router,
        grad_w_gate[None],
        grad_w_up[None],
        grad_w_down[None],
    )


def solution(mesh):
    rows = P("shard", "ctx", None)
    matrix = P("shard", None)
    expert = P(("ctx", "shard"), None, None)
    return jax.shard_map(
        shards,
        mesh=mesh,
        in_specs=(
            rows, rows, P(), rows, P(), matrix, matrix, matrix, P(), P(), matrix, P(), matrix,
            expert, expert, expert,
        ),
        out_specs=(
            rows, rows, P(), matrix, matrix, matrix, P(), P(), matrix, P(), matrix,
            expert, expert, expert,
        ),
        check_vma=False,
    )
```
